32 devices in a mesh: seq: 16 (over z, y, core), col: 2 (over x).
Axes of the slice: x: 2, y: 2, z: 4, core: 2. Of those that a mesh axis runs over, the one named last changes fastest.
Arguments:
- tokens: int32 [2, 16, 512], P(None, 'seq', 'col'), may hold values from 4 to 28
- targets: int32 [2, 16, 512], P(None, 'seq', 'col'), may hold values from 4 to 28
- masked: int32 [2, 16, 512], P(None, 'seq', 'col'), may hold values from 0 to 1, as said below
- contact_pairs: int32 [2, 2048, 2], P(None, ('seq', 'col')), may hold values from 0 to 511, as said below
- labels: int32 [2, 2048], P(None, ('seq', 'col')), may hold values from -1 to 1, as said below
- attention_in_master: float32 [2, 768, 2304], P(None, ('seq', 'col')), may hold values from -0.21875 to 0.21875
- attention_in_first: float32 [2, 768, 2304], P(None, ('seq', 'col')), may hold values from -2.0861626e-07 to 2.0861626e-07
- attention_in_second: float32 [2, 768, 2304], P(None, ('seq', 'col')), may hold values from 5.2805643e-15 to 2.1122257e-14
- attention_out_master: float32 [2, 768, 768], P(None, ('seq', 'col')), may hold values from -1.75 to 1.75
- attention_out_first: float32 [2, 768, 768], P(None, ('seq', 'col')), may hold values from -2.0861626e-07 to 2.0861626e-07
- attention_out_second: float32 [2, 768, 768], P(None, ('seq', 'col')), may hold values from 5.2805643e-15 to 2.1122257e-14
- feed_up_master: float32 [768, 3072], P(('seq', 'col')), may hold values from -0.21875 to 0.21875
- feed_up_first: float32 [768, 3072], P(('seq', 'col')), may hold values from -2.0861626e-07 to 2.0861626e-07
- feed_up_second: float32 [768, 3072], P(('seq', 'col')), may hold values from 5.2805643e-15 to 2.1122257e-14
- feed_down_master: float32 [3072, 768], P(None, ('seq', 'col')), may hold values from -0.109375 to 0.109375
- feed_down_first: float32 [3072, 768], P(None, ('seq', 'col')), may hold values from -2.0861626e-07 to 2.0861626e-07
- feed_down_second: float32 [3072, 768], P(None, ('seq', 'col')), may hold values from 5.2805643e-15 to 2.1122257e-14
- embedding_master: float32 [33, 768], P(None, ('seq', 'col')), may hold values from -6 to 6
- embedding_first: float32 [33, 768], P(None, ('seq', 'col')), may hold values from -8.34465e-07 to 8.34465e-07
- embedding_second: float32 [33, 768], P(None, ('seq', 'col')), may hold values from 8.448903e-14 to 3.3795612e-13
- norm_params_master: float32 [8, 768], P(None, ('seq', 'col'))
- norm_params_first: float32 [8, 768], P(None, ('seq', 'col')), may hold values from -8.34465e-07 to 8.34465e-07
- norm_params_second: float32 [8, 768], P(None, ('seq', 'col')), may hold values from 8.448903e-14 to 3.3795612e-13
- contact_head_master: float32 [13], replicated, may hold values from -6 to 6
- contact_head_first: float32 [13], replicated, may hold values from -2.2888184e-05 to 2.2888184e-05
- contact_head_second: float32 [13], replicated, may hold values from 3.1683386e-12 to 1.26733546e-11
Outputs:
- attention_in_new: float32 [2, 768, 2304], P(None, ('seq', 'col'))
- attention_in_moment: float32 [2, 768, 2304], P(None, ('seq', 'col'))
- attention_in_square: float32 [2, 768, 2304], P(None, ('seq', 'col'))
- attention_out_new: float32 [2, 768, 768], P(None, ('seq', 'col'))
- attention_out_moment: float32 [2, 768, 768], P(None, ('seq', 'col'))
- attention_out_square: float32 [2, 768, 768], P(None, ('seq', 'col'))
- feed_up_new: float32 [768, 3072], P(('seq', 'col'))
- feed_up_moment: float32 [768, 3072], P(('seq', 'col'))
- feed_up_square: float32 [768, 3072], P(('seq', 'col'))
- feed_down_new: float32 [3072, 768], P(None, ('seq', 'col'))
- feed_down_moment: float32 [3072, 768], P(None, ('seq', 'col'))
- feed_down_square: float32 [3072, 768], P(None, ('seq', 'col'))
- embedding_new: float32 [33, 768], P(None, ('seq', 'col'))
- embedding_moment: float32 [33, 768], P(None, ('seq', 'col'))
- embedding_square: float32 [33, 768], P(None, ('seq', 'col'))
- norm_params_new: float32 [8, 768], P(None, ('seq', 'col'))
- norm_params_moment: float32 [8, 768], P(None, ('seq', 'col'))
- norm_params_square: float32 [8, 768], P(None, ('seq', 'col'))
- contact_head_new: float32 [13], replicated
- contact_head_moment: float32 [13], replicated
- contact_head_square: float32 [13], replicated
- attention_in_copy: bfloat16 [2, 768, 2304], P(None, ('seq', 'col'))
- attention_out_copy: bfloat16 [2, 768, 768], P(None, ('seq', 'col'))
- feed_up_copy: bfloat16 [768, 3072], P(('seq', 'col'))
- feed_down_copy: bfloat16 [3072, 768], P(None, ('seq', 'col'))
- embedding_copy: bfloat16 [33, 768], P(None, ('seq', 'col'))
- loss_parts: float32 [4], replicated
- grad_norm: float32 [], replicated
The draws below stay inside these ranges and needn't reach their ends.
Inputs may be any that keep to these rules, and one draw needn't show every extreme that they name: 1 marks a masked residue. `contact_pairs`: pairs are laid out in blocks of 64, one block for each shard of the seq+col axes; the first column of a pair lies among the 256 columns of its shard's col index. `labels`: -1: pair ignored; 1: contact; 0: no contact.
All inputs are finite; a program needn't handle non-finite values.
Results may differ from the reference program's by a relative error of at most 0.0081.
The reference program's roundings to bfloat16 on the way count: a program that leaves them out, or rounds other values in their place, can miss the bound.
Values may be sent and summed in bfloat16 or wider, within the bound.
A program may use at most 320 MiB of HBM per device.

```python
import math
import jax
import jax.numpy as jnp
from jax import lax

D = 768
HEADS = 12
HD = 64
FF = 3072
VOCAB = 33
C = 512
MB = 2
PAIRS_DEV = 64
STEP = 10
R = 16
PARAMS = 9468685
N_COL = 2
DEVICES = 32


def draw_masked(key, part):
    key = jax.random.fold_in(key, 5)
    row_index = jnp.arange(R, dtype=jnp.int32)[:, None]
    col_index = jnp.arange(C, dtype=jnp.int32)[None, :]
    border = 400 * (R + 2 * row_index) // R * (C + 2 * col_index) // C
    forced = (row_index * 7 + col_index) % 61 == 0
    drawn = jax.random.randint(key, (MB, R, C), 0, 10000)
    return jnp.where((drawn < border[None]) | forced[None], 1, 0).astype(jnp.int32)


def draw_contact_pairs(key, part):
    key = jax.random.fold_in(key, 7)
    first_key, second_key = jax.random.split(key)
    total = PAIRS_DEV * DEVICES
    block = jnp.arange(total, dtype=jnp.int32) // PAIRS_DEV
    group = block % N_COL
    first = group[None, :] * (C // N_COL) + jax.random.randint(first_key, (MB, total), 0, C // N_COL)
    second = jax.random.randint(second_key, (MB, total), 0, C)
    return jnp.stack([first, second], -1).astype(jnp.int32)


def draw_labels(key, part):
    key = jax.random.fold_in(key, 9)
    total = PAIRS_DEV * DEVICES
    slot = jnp.arange(total, dtype=jnp.int32)
    block = slot // PAIRS_DEV
    border = 2500 + 5000 * block // max(DEVICES - 1, 1)
    border = jnp.where(slot % PAIRS_DEV == 0, 10000, border)
    drawn = jax.random.randint(key, (MB, total), 0, 10000)
    return jnp.where(drawn < border[None, :], jnp.where(drawn % 10 < 3, 1, 0), -1).astype(jnp.int32)


def draw_norm_params_master(key, part):
    key = jax.random.fold_in(key, 11)
    gain_key, bias_key = jax.random.split(key)
    ramp = jnp.arange(D, dtype=jnp.float32) / D
    gains = (0.5 + ramp) * jax.random.uniform(gain_key, (4, D), jnp.float32, 0.8, 1.2)
    biases = 0.3 * jax.random.normal(bias_key, (4, D), jnp.float32)
    return jnp.concatenate([gains, biases], 0)


def plant(values, stream_key, least, largest):
    longest = values.shape.index(max(values.shape))
    spots = []
    for shift in (0, 1):
        where = [jax.random.randint(jax.random.fold_in(stream_key, axis), (), 0, length) for axis, length in enumerate(values.shape)]
        where[longest] = (where[longest] + shift) % values.shape[longest]
        spots.append(tuple(where))
    return values.at[spots[0]].set(least).at[spots[1]].set(largest)


def block_levels(stream_key, dims, shards, low, high):
    factor_of, own = 1.0, jax.random.fold_in(stream_key, 6)
    for axis_at, parts in shards:
        draws = jnp.exp(jax.random.uniform(jax.random.fold_in(own, axis_at), (parts,), jnp.float32, low / len(shards), high / len(shards)))
        factor_of = factor_of * jnp.repeat(draws, dims[axis_at] // parts).reshape([-1 if axis == axis_at else 1 for axis in range(len(dims))])
    return factor_of


def scatter_about(stream_key, dims, deviation, most, shards=(), held_as=jnp.bfloat16):
    gain = block_levels(stream_key, dims, shards, -0.22, 0.18) if shards else 1.0
    values = jax.random.normal(stream_key, dims, jnp.float32) * deviation * gain
    return jnp.minimum(jnp.maximum(values, -most), most).astype(held_as)


def setup_inputs(seed: int = 0) -> dict:
    key_of = jax.random.split(jax.random.key(seed), 27)
    return {
        "tokens": plant(jax.random.randint(key_of[0], (MB, R, C), 4, 29), jax.random.fold_in(key_of[0], 1), 4, 28).astype(jnp.int32),
        "targets": plant(jax.random.randint(key_of[1], (MB, R, C), 4, 29), jax.random.fold_in(key_of[1], 1), 4, 28).astype(jnp.int32),
        "masked": draw_masked(jax.random.fold_in(key_of[26], 71), 0),
        "contact_pairs": draw_contact_pairs(jax.random.fold_in(key_of[26], 71), 0),
        "labels": draw_labels(jax.random.fold_in(key_of[26], 71), 0),
        "attention_in_master": scatter_about(key_of[5], (2, D, 3 * D), D ** -0.5, 0.21875, ((1, 32),), jnp.float32),
        "attention_in_first": scatter_about(key_of[6], (2, D, 3 * D), (0.00011 / PARAMS ** 0.5), 2.086162567138672e-07, ((1, 32),), jnp.float32),
        "attention_in_second": jnp.clip(jnp.exp(math.log(2.1122257317773147e-14) - 1.3862944 * jax.random.uniform(key_of[7], (2, D, 3 * D), jnp.float32) ** block_levels(key_of[7], (2, D, 3 * D), ((1, 32),), -0.2, 0.2)), 5.280564329443287e-15, 2.1122257317773147e-14),
        "attention_out_master": scatter_about(key_of[8], (2, D, D), 12 ** -0.5, 1.75, ((1, 32),), jnp.float32),
        "attention_out_first": scatter_about(key_of[9], (2, D, D), (0.00011 / PARAMS ** 0.5), 2.086162567138672e-07, ((1, 32),), jnp.float32),
        "attention_out_second": jnp.clip(jnp.exp(math.log(2.1122257317773147e-14) - 1.3862944 * jax.random.uniform(key_of[10], (2, D, D), jnp.float32) ** block_levels(key_of[10], (2, D, D), ((1, 32),), -0.2, 0.2)), 5.280564329443287e-15, 2.1122257317773147e-14),
        "feed_up_master": scatter_about(key_of[11], (D, FF), D ** -0.5, 0.21875, ((0, 32),), jnp.float32),
        "feed_up_first": scatter_about(key_of[12], (D, FF), (0.00011 / PARAMS ** 0.5), 2.086162567138672e-07, ((0, 32),), jnp.float32),
        "feed_up_second": jnp.clip(jnp.exp(math.log(2.1122257317773147e-14) - 1.3862944 * jax.random.uniform(key_of[13], (D, FF), jnp.float32) ** block_levels(key_of[13], (D, FF), ((0, 32),), -0.2, 0.2)), 5.280564329443287e-15, 2.1122257317773147e-14),
        "feed_down_master": scatter_about(key_of[14], (FF, D), FF ** -0.5, 0.109375, ((1, 32),), jnp.float32),
        "feed_down_first": scatter_about(key_of[15], (FF, D), (0.00011 / PARAMS ** 0.5), 2.086162567138672e-07, ((1, 32),), jnp.float32),
        "feed_down_second": jnp.clip(jnp.exp(math.log(2.1122257317773147e-14) - 1.3862944 * jax.random.uniform(key_of[16], (FF, D), jnp.float32) ** block_levels(key_of[16], (FF, D), ((1, 32),), -0.2, 0.2)), 5.280564329443287e-15, 2.1122257317773147e-14),
        "embedding_master": scatter_about(key_of[17], (VOCAB, D), 1.0, 6.0, ((1, 32),), jnp.float32),
        "embedding_first": scatter_about(key_of[18], (VOCAB, D), (0.00044 / PARAMS ** 0.5), 8.344650268554688e-07, ((1, 32),), jnp.float32),
        "embedding_second": jnp.clip(jnp.exp(math.log(3.3795611708437034e-13) - 1.3862944 * jax.random.uniform(key_of[19], (VOCAB, D), jnp.float32) ** block_levels(key_of[19], (VOCAB, D), ((1, 32),), -0.2, 0.2)), 8.448902927109259e-14, 3.3795611708437034e-13),
        "norm_params_master": draw_norm_params_master(jax.random.fold_in(key_of[26], 71), 0),
        "norm_params_first": scatter_about(key_of[21], (8, D), (0.00044 / PARAMS ** 0.5), 8.344650268554688e-07, ((1, 32),), jnp.float32),
        "norm_params_second": jnp.clip(jnp.exp(math.log(3.3795611708437034e-13) - 1.3862944 * jax.random.uniform(key_of[22], (8, D), jnp.float32) ** block_levels(key_of[22], (8, D), ((1, 32),), -0.2, 0.2)), 8.448902927109259e-14, 3.3795611708437034e-13),
        "contact_head_master": scatter_about(key_of[23], (HEADS + 1,), 1.0, 6.0, (), jnp.float32),
        "contact_head_first": scatter_about(key_of[24], (HEADS + 1,), (0.011 / PARAMS ** 0.5), 2.288818359375e-05, (), jnp.float32),
        "contact_head_second": jnp.clip(jnp.exp(jax.random.uniform(key_of[25], (HEADS + 1,), jnp.float32, math.log(3.1683386383235534e-12), math.log(1.2673354553294214e-11))), 3.1683386383235534e-12, 1.2673354553294214e-11),
    }


@jax.custom_vjp
def low(v):
    return lax.optimization_barrier(v.astype(jnp.bfloat16)).astype(jnp.float32)

@jax.custom_vjp
def low_back(v):
    return v

def low_keep(v):
    return (low(v), None)

def low_pass(kept, grad):
    return (grad,)

def back_keep(v):
    return (v, None)

def back_low(kept, grad):
    return (low(grad),)
low.defvjp(low_keep, low_pass)
low_back.defvjp(back_keep, back_low)
PRECISE = lax.Precision.HIGHEST
NORM_EPS = 1e-05
MASK_ID = 32
MAX_NORM = 0.001
LEARN_RATE = 0.05
VECTOR_RATE = 0.5
BETA_ONE = 0.9
BETA_TWO = 0.95
ADAM_EPS = 1e-08
WEIGHT_DECAY = 0.01

def layer_norm(values, scale_vec, shift_vec):
    centre = values - lax.optimization_barrier(jnp.mean(values, -1, keepdims=True))
    spread = lax.optimization_barrier(jnp.mean(centre * centre, -1, keepdims=True))
    return centre * lax.rsqrt(spread + NORM_EPS) * scale_vec + shift_vec

def project(normed, matrix):
    return jnp.einsum('rcd,de->rce', low(normed), matrix, precision=PRECISE)

def split_heads(block):
    return block.reshape(block.shape[0], block.shape[1], HEADS, HD)

def micro_loss(params, inputs, targets, masked, contact_pairs, labels, mlm_count, pair_count):
    attention_in, attention_out, feed_up, feed_down, embedding, norm_params, contact_head = params
    attention_in = low(attention_in)
    attention_out = low(attention_out)
    feed_up = low(feed_up)
    feed_down = low(feed_down)
    table = low(embedding)
    norms = low(norm_params)
    stream = table[inputs]
    row_proj = low_back(low(project(layer_norm(stream, norms[0], norms[4]), attention_in[0])))
    row_query = split_heads(row_proj[..., :D])
    row_key = split_heads(row_proj[..., D:2 * D])
    row_value = split_heads(row_proj[..., 2 * D:])
    row_score = low_back(jnp.einsum('rihe,rjhe->ihj', row_query, row_key, precision=PRECISE) * (HD * R) ** (-0.5))
    row_prob = low(jax.nn.softmax(row_score, axis=-1))
    row_mixed = low_back(low(jnp.einsum('ihj,rjhe->rihe', row_prob, row_value, precision=PRECISE).reshape(R, C, D)))
    stream = stream + low_back(jnp.einsum('rcd,de->rce', row_mixed, attention_out[0], precision=PRECISE))
    col_proj = low_back(low(project(layer_norm(stream, norms[1], norms[5]), attention_in[1])))
    col_query = split_heads(col_proj[..., :D])
    col_key = split_heads(col_proj[..., D:2 * D])
    col_value = split_heads(col_proj[..., 2 * D:])
    col_score = low_back(jnp.einsum('rche,sche->chrs', col_query, col_key, precision=PRECISE) * HD ** (-0.5))
    col_prob = low(jax.nn.softmax(col_score, axis=-1))
    col_mixed = low_back(low(jnp.einsum('chrs,sche->rche', col_prob, col_value, precision=PRECISE).reshape(R, C, D)))
    stream = stream + low_back(jnp.einsum('rcd,de->rce', col_mixed, attention_out[1], precision=PRECISE))
    hidden_up = low_back(project(layer_norm(stream, norms[2], norms[6]), feed_up))
    active = low(jax.nn.gelu(hidden_up))
    stream = stream + low_back(jnp.einsum('rcf,fd->rcd', active, feed_down, precision=PRECISE))
    normed = low(layer_norm(stream, norms[3], norms[7]))
    logits = low_back(jnp.einsum('rcd,vd->rcv', normed, table, precision=PRECISE)) * D ** (-0.5)
    log_probs = jax.nn.log_softmax(logits, axis=-1)
    picked = jnp.take_along_axis(log_probs, targets[..., None], axis=-1)[..., 0]
    mlm_sum = -jnp.sum(jnp.where(masked > 0, picked, 0.0))
    features = row_prob[contact_pairs[:, 0], :, contact_pairs[:, 1]]
    contact_logit = jnp.dot(features, contact_head[:HEADS], precision=PRECISE) * C + contact_head[HEADS]
    positive = (labels == 1).astype(jnp.float32)
    bce_sum = jnp.sum(jnp.where(labels >= 0, jax.nn.softplus(contact_logit) - positive * contact_logit, 0.0))
    return (mlm_sum / mlm_count + bce_sum / pair_count, (mlm_sum, bce_sum))

def adam_update(master, first, second, grad_part, rate):
    first = BETA_ONE * first + (1.0 - BETA_ONE) * grad_part
    second = BETA_TWO * second + (1.0 - BETA_TWO) * grad_part * grad_part
    moved = first / (1.0 - BETA_ONE ** STEP) / (jnp.sqrt(second / (1.0 - BETA_TWO ** STEP)) + ADAM_EPS)
    return (master - rate * (moved + WEIGHT_DECAY * master), first, second)

def reference(tokens, targets, masked, contact_pairs, labels, attention_in_master, attention_in_first, attention_in_second, attention_out_master, attention_out_first, attention_out_second, feed_up_master, feed_up_first, feed_up_second, feed_down_master, feed_down_first, feed_down_second, embedding_master, embedding_first, embedding_second, norm_params_master, norm_params_first, norm_params_second, contact_head_master, contact_head_first, contact_head_second):
    masters = (attention_in_master, attention_out_master, feed_up_master, feed_down_master, embedding_master, norm_params_master, contact_head_master)
    mlm_count = jnp.sum(masked).astype(jnp.float32)
    pair_count = jnp.sum(labels >= 0).astype(jnp.float32)
    inputs = jnp.where(masked > 0, MASK_ID, tokens)
    totals = tuple((jnp.zeros_like(master) for master in masters))
    mlm_total = jnp.zeros((), jnp.float32)
    bce_total = jnp.zeros((), jnp.float32)
    for micro_index in range(MB):

        def loss_of(params):
            return micro_loss(params, inputs[micro_index], targets[micro_index], masked[micro_index], contact_pairs[micro_index], labels[micro_index], mlm_count, pair_count)
        value, pullback, sums = jax.vjp(loss_of, masters, has_aux=True)
        grads, = pullback(jnp.ones((), jnp.float32))
        totals = tuple((summed + grad_part for summed, grad_part in zip(totals, grads)))
        mlm_total = mlm_total + sums[0]
        bce_total = bce_total + sums[1]
    grad_norm = jnp.sqrt(sum((jnp.sum(summed * summed) for summed in totals)))
    factor = jnp.minimum(1.0, MAX_NORM / grad_norm)
    in_new, in_moment, in_square = adam_update(attention_in_master, attention_in_first, attention_in_second, totals[0] * factor, LEARN_RATE)
    out_new, out_moment, out_square = adam_update(attention_out_master, attention_out_first, attention_out_second, totals[1] * factor, LEARN_RATE)
    up_new, up_moment, up_square = adam_update(feed_up_master, feed_up_first, feed_up_second, totals[2] * factor, LEARN_RATE)
    down_new, down_moment, down_square = adam_update(feed_down_master, feed_down_first, feed_down_second, totals[3] * factor, LEARN_RATE)
    table_new, table_moment, table_square = adam_update(embedding_master, embedding_first, embedding_second, totals[4] * factor, VECTOR_RATE)
    norm_new, norm_moment, norm_square = adam_update(norm_params_master, norm_params_first, norm_params_second, totals[5] * factor, VECTOR_RATE)
    head_new, head_moment, head_square = adam_update(contact_head_master, contact_head_first, contact_head_second, totals[6] * factor, VECTOR_RATE)
    loss_parts = jnp.stack([mlm_total, mlm_count, bce_total, pair_count])
    return (in_new, in_moment, in_square, out_new, out_moment, out_square, up_new, up_moment, up_square, down_new, down_moment, down_square, table_new, table_moment, table_square, norm_new, norm_moment, norm_square, head_new, head_moment, head_square, in_new.astype(jnp.bfloat16), out_new.astype(jnp.bfloat16), up_new.astype(jnp.bfloat16), down_new.astype(jnp.bfloat16), table_new.astype(jnp.bfloat16), loss_parts, grad_norm)
```

```python
import jax
import jax.numpy as jnp
from jax import lax
from jax.sharding import PartitionSpec as P

D = 768
HEADS = 12
HD = 64
FF = 3072
VOCAB = 33
VP = 64
STEP = 10

NORM_EPS = 1e-05
MASK_ID = 32
MAX_NORM = 0.001
LEARN_RATE = 0.05
VECTOR_RATE = 0.5
BETA_ONE = 0.9
BETA_TWO = 0.95
ADAM_EPS = 1e-08
WEIGHT_DECAY = 0.01
PRECISE = lax.Precision.HIGHEST
F32 = jnp.float32
BF16 = jnp.bfloat16


def nn(left, right):
    return lax.dot_general(left, right, (((1,), (0,)), ((), ())), preferred_element_type=F32)


def tn(left, right):
    return lax.dot_general(left, right, (((0,), (0,)), ((), ())), preferred_element_type=F32)


def nt(left, right):
    return lax.dot_general(left, right, (((1,), (1,)), ((), ())), preferred_element_type=F32)


def split_two(values):
    high = values.astype(BF16)
    return high, (values - high.astype(F32)).astype(BF16)


def norm_stats(values):
    centre = values - jnp.mean(values, -1, keepdims=True)
    rstd = lax.rsqrt(jnp.mean(centre * centre, -1, keepdims=True) + NORM_EPS)
    return centre * rstd, rstd


def norm_back(unit, rstd, scale_vec, upstream):
    inner = upstream * scale_vec
    grad = rstd * (
        inner - jnp.mean(inner, -1, keepdims=True) - unit * jnp.mean(inner * unit, -1, keepdims=True)
    )
    return grad, jnp.sum(upstream * unit, 0), jnp.sum(upstream, 0)


GELU_K = 0.7978845608028654
GELU_C = 0.044715


def gelu_parts(up):
    square = up * up
    bent = jnp.tanh(GELU_K * up * (1.0 + GELU_C * square))
    half = 0.5 * (1.0 + bent)
    slope = half + 0.5 * up * (1.0 - bent * bent) * GELU_K * (1.0 + 3.0 * GELU_C * square)
    return up * half, slope


def heads_of(block, head):
    return block[:, head * HD : (head + 1) * HD]


def step(big, table, norms, contact_head, ids_all, ids_ri, ids_ir, targets_ir, pair_first, pair_second, labels, counts, cw):
    in_row, in_col, out_row, out_col, up_w, down_t = big
    rows, cols = ids_all.shape
    here = rows * cw
    row_scale = (HD * rows) ** (-0.5)
    vocab = jnp.arange(VP)[:, None]
    hot_all = (ids_all[:, None, :] == vocab[None]).astype(BF16).reshape(rows * VP, cols)
    hot_ri = (ids_ri[None, :] == vocab).astype(BF16)
    hot_ir = (ids_ir[None, :] == vocab).astype(BF16)
    spot = jnp.arange(here)
    perm = (
        ((spot // rows)[:, None] == (spot % cw)[None, :])
        & ((spot % rows)[:, None] == (spot // cw)[None, :])
    ).astype(BF16)

    def to_heads(block):
        return block.reshape(rows, cw, HEADS, VP).transpose(2, 1, 0, 3).reshape(HEADS * cw, rows * VP)

    def to_tokens(block):
        return block.reshape(HEADS, cw, rows, VP).transpose(2, 1, 0, 3).reshape(here, HEADS * VP)

    def per_head(block, other, how):
        return jnp.concatenate(
            [how(heads_of(block, h), heads_of(other, h)) for h in range(HEADS)], -1
        )

    table_f = table.astype(F32)
    unit_t, rstd_t = norm_stats(table_f)
    normed_t = (unit_t * norms[0] + norms[4]).astype(BF16)
    proj_t = nn(normed_t, in_row).astype(BF16)
    query_t, key_t, value_t = proj_t[:, :D], proj_t[:, D : 2 * D], proj_t[:, 2 * D :]

    pair_t = per_head(query_t, key_t, nt)
    pair_hi, pair_lo = split_two(pair_t)
    left_hi = to_heads(tn(hot_ri, pair_hi).astype(BF16))
    left_lo = to_heads(tn(hot_ri, pair_lo).astype(BF16))
    score = (nn(left_hi, hot_all) + nn(left_lo, hot_all)) * row_scale
    prob = jax.nn.softmax(score, axis=-1)
    prob_low = prob.astype(BF16)
    weight_t = to_tokens(nt(prob_low, hot_all))
    weight_hi, weight_lo = split_two(weight_t)
    row_mixed_ri = (
        per_head(weight_hi, value_t, nn) + per_head(weight_lo, value_t, nn)
    ).astype(BF16)
    row_mixed = nn(perm, row_mixed_ri).astype(BF16)
    embedded = tn(hot_ir, table)
    after_row = embedded + nn(row_mixed, out_row)

    prob_cube = prob_low.astype(F32).reshape(HEADS, cw, cols)
    head_sum = jnp.sum(prob_cube * contact_head[:HEADS, None, None], 0)
    first_hot = (pair_first[None, :] == jnp.arange(cw)[:, None]).astype(F32)
    second_hot = (pair_second[None, :] == jnp.arange(cols)[:, None]).astype(BF16)
    sum_hi, sum_lo = split_two(head_sum)
    sum_last = (head_sum - sum_hi.astype(F32) - sum_lo.astype(F32)).astype(BF16)
    picked = nn(sum_hi, second_hot) + nn(sum_lo, second_hot) + nn(sum_last, second_hot)
    contact_logit = jnp.sum(picked * first_hot, 0) * cols + contact_head[HEADS]
    owned = jnp.sum(first_hot, 0) > 0
    valid = (labels >= 0) & owned
    positive = (labels == 1).astype(F32)
    bce_sum = jnp.sum(
        jnp.where(valid, jax.nn.softplus(contact_logit) - positive * contact_logit, 0.0)
    )
    coef = jnp.where(valid, jax.nn.sigmoid(contact_logit) - positive, 0.0) / counts[1]
    coef_hi, coef_lo = split_two(coef)
    first_low = first_hot.astype(BF16)
    touch = nt(first_low * coef_hi[None], second_hot) + nt(first_low * coef_lo[None], second_hot)
    grad_contact = jnp.concatenate(
        [jnp.sum(prob_cube * touch[None], (1, 2)) * cols, jnp.sum(coef)[None]]
    )

    unit_1, rstd_1 = norm_stats(after_row)
    col_normed = (unit_1 * norms[1] + norms[5]).astype(BF16)
    col_proj = nn(col_normed, in_col).astype(BF16)
    group = 128 if here % 128 == 0 and 128 % rows == 0 else here
    groups = here // group
    lane = jnp.arange(group)
    same = (lane[:, None] // rows) == (lane[None, :] // rows)

    def cut(block):
        return block.reshape(groups, group, HEADS, HD)

    col_query, col_key, col_value = (cut(col_proj[:, k * D : (k + 1) * D]) for k in range(3))
    col_score = jnp.einsum("gqhe,gkhe->ghqk", col_query, col_key, preferred_element_type=F32) * HD ** (-0.5)
    col_prob = jax.nn.softmax(jnp.where(same, col_score, -1e30), axis=-1)
    col_prob_low = col_prob.astype(BF16)
    col_mixed = (
        jnp.einsum("ghqk,gkhe->gqhe", col_prob_low, col_value, preferred_element_type=F32)
        .astype(BF16)
        .reshape(here, D)
    )
    after_col = after_row + nn(col_mixed, out_col)

    unit_2, rstd_2 = norm_stats(after_col)
    feed_normed = (unit_2 * norms[2] + norms[6]).astype(BF16)
    hidden_up = nn(feed_normed, up_w)
    active, slope = gelu_parts(hidden_up)
    active = active.astype(BF16)
    after_feed = after_col + nt(active, down_t)
    unit_3, rstd_3 = norm_stats(after_feed)
    head_normed = (unit_3 * norms[3] + norms[7]).astype(BF16)
    logits = nt(table, head_normed) * D ** (-0.5)
    logits = jnp.where(vocab < VOCAB, logits, -1e30)
    top = jnp.max(logits, 0, keepdims=True)
    shifted = logits - top
    log_probs = shifted - jnp.log(jnp.sum(jnp.exp(shifted), 0, keepdims=True))
    target_hot = (targets_ir[None, :] == vocab).astype(F32)
    keep = ids_ir[None, :] == MASK_ID
    mlm_sum = -jnp.sum(jnp.where(keep & (target_hot > 0), log_probs, 0.0))
    logit_grad = jnp.where(keep, jnp.exp(log_probs) - target_hot, 0.0) / counts[0]
    logit_low = (logit_grad * D ** (-0.5)).astype(BF16)

    grad_head = nn(logit_low, head_normed)
    stream, scale_3, shift_3 = norm_back(unit_3, rstd_3, norms[3], tn(logit_low, table))
    branch = stream.astype(BF16)
    grad_down = tn(branch, active)
    up_low = (nn(branch, down_t) * slope).astype(BF16)
    grad_up = tn(feed_normed, up_low)
    inner, scale_2, shift_2 = norm_back(unit_2, rstd_2, norms[2], nt(up_low, up_w))
    stream = stream + inner
    branch = stream.astype(BF16)
    grad_out_col = tn(col_mixed, branch)
    mixed_low = nt(branch, out_col).astype(BF16)
    mixed_cut = cut(mixed_low)
    prob_grad = jnp.einsum("gqhe,gkhe->ghqk", mixed_cut, col_value, preferred_element_type=F32)
    score_grad = col_prob * (prob_grad - jnp.sum(col_prob * prob_grad, -1, keepdims=True))
    score_low = score_grad.astype(BF16)
    grad_q = jnp.einsum("ghqk,gkhe->gqhe", score_low, col_key, preferred_element_type=F32)
    grad_k = jnp.einsum("ghqk,gqhe->gkhe", score_low, col_query, preferred_element_type=F32)
    grad_v = jnp.einsum("ghqk,gqhe->gkhe", col_prob_low, mixed_cut, preferred_element_type=F32)
    proj_low = jnp.concatenate(
        [
            (grad_q * HD ** (-0.5)).reshape(here, D),
            (grad_k * HD ** (-0.5)).reshape(here, D),
            grad_v.reshape(here, D),
        ],
        -1,
    ).astype(BF16)
    grad_in_col = tn(col_normed, proj_low)
    inner, scale_1, shift_1 = norm_back(unit_1, rstd_1, norms[1], nt(proj_low, in_col))
    stream = stream + inner
    branch = stream.astype(BF16)
    grad_out_row = tn(row_mixed, branch)
    mixed_low = nt(branch, out_row).astype(BF16)
    mixed_ri = tn(perm, mixed_low).astype(BF16)
    drive_hi, drive_lo = split_two(per_head(mixed_ri, value_t, nt))
    prob_grad = nn(to_heads(drive_hi), hot_all) + nn(to_heads(drive_lo), hot_all)
    prob_grad = prob_grad + (
        touch[None] * (contact_head[:HEADS, None, None] * cols)
    ).reshape(HEADS * cw, cols)
    score_grad = prob * (prob_grad - jnp.sum(prob * prob_grad, -1, keepdims=True))
    score_low = score_grad.astype(BF16)
    spread = to_tokens(nt(score_low, hot_all)).astype(BF16)
    table_pair = nn(hot_ri, spread)
    value_grad = per_head(weight_hi, mixed_ri, tn)
    stream_hi, stream_lo = split_two(stream)
    lookup_grad = nn(hot_ir, stream_hi) + nn(hot_ir, stream_lo)
    vectors = jnp.stack([scale_1, scale_2, scale_3, shift_1, shift_2, shift_3])
    return (
        (grad_in_col, grad_out_row, grad_out_col, grad_up, grad_down),
        (table_pair, value_grad, grad_head + lookup_grad, vectors),
        grad_contact,
        mlm_sum,
        bce_sum,
        (unit_t, rstd_t, normed_t, query_t, key_t),
    )


def adam_update(master, first, second, grad_part, rate):
    first = BETA_ONE * first + (1.0 - BETA_ONE) * grad_part
    second = BETA_TWO * second + (1.0 - BETA_TWO) * grad_part * grad_part
    moved = first / (1.0 - BETA_ONE**STEP) / (jnp.sqrt(second / (1.0 - BETA_TWO**STEP)) + ADAM_EPS)
    return (master - rate * (moved + WEIGHT_DECAY * master), first, second)


def shards(
    tokens,
    targets,
    masked,
    contact_pairs,
    labels,
    attention_in_master,
    attention_in_first,
    attention_in_second,
    attention_out_master,
    attention_out_first,
    attention_out_second,
    feed_up_master,
    feed_up_first,
    feed_up_second,
    feed_down_master,
    feed_down_first,
    feed_down_second,
    embedding_master,
    embedding_first,
    embedding_second,
    norm_params_master,
    norm_params_first,
    norm_params_second,
    contact_head_master,
    contact_head_first,
    contact_head_second,
):
    both = ("seq", "col")
    micro, rows_here, cols_here = tokens.shape
    ncol = lax.axis_size("col")
    ndev = lax.axis_size("seq") * ncol
    cols = cols_here * ncol
    me = lax.axis_index("seq") * ncol + lax.axis_index("col")
    per = ndev // micro
    cw = cols // per
    mine = me // per
    base = (me % per) * cw
    shard = D // ndev

    inputs = jnp.where(masked > 0, MASK_ID, tokens)
    whole = jnp.stack([inputs, targets])
    whole = lax.all_gather(lax.all_gather(whole, "col", axis=3, tiled=True), "seq", axis=2, tiled=True)
    pairs_all = lax.all_gather(
        jnp.concatenate([contact_pairs, labels[:, :, None]], -1), both, axis=1, tiled=True
    )
    counts = (
        jnp.sum(whole[0] == MASK_ID).astype(F32),
        jnp.sum(pairs_all[..., 2] >= 0).astype(F32),
    )
    ids_all = lax.dynamic_index_in_dim(whole[0], mine, 0, False)
    ids_local = lax.dynamic_slice_in_dim(ids_all, base, cw, 1)
    targets_local = lax.dynamic_slice_in_dim(
        lax.dynamic_index_in_dim(whole[1], mine, 0, False), base, cw, 1
    )
    pairs = lax.dynamic_index_in_dim(pairs_all, mine, 0, False)

    flat = jnp.concatenate(
        [
            attention_in_master[0],
            attention_in_master[1],
            attention_out_master[0],
            attention_out_master[1],
            feed_up_master,
            feed_down_master.T,
            jnp.pad(embedding_master.T, ((0, 0), (0, VP - VOCAB))),
            jnp.pad(norm_params_master.T, ((0, 0), (0, VP - 8))),
        ],
        1,
    ).astype(BF16)
    full = lax.all_gather(flat, both, axis=0, tiled=True)
    edges = [0, 3 * D, 6 * D, 7 * D, 8 * D, 8 * D + FF, 8 * D + 2 * FF]
    big = [full[:, a:b] for a, b in zip(edges[:-1], edges[1:])]
    in_row = big[0]
    table = full[:, edges[-1] : edges[-1] + VP].T
    norms = full[:, edges[-1] + VP : edges[-1] + VP + 8].T.astype(F32)

    grads, tables, contact_total, mlm_total, bce_total, kept = step(
        big,
        table,
        norms,
        contact_head_master,
        ids_all,
        ids_local.reshape(-1),
        ids_local.T.reshape(-1),
        targets_local.T.reshape(-1),
        pairs[:, 0] - base,
        pairs[:, 1],
        pairs[:, 2],
        counts,
        cw,
    )
    flat_grad = jnp.concatenate([g.astype(BF16) for g in grads], 1)
    reduced = lax.psum_scatter(flat_grad, both, scatter_dimension=0, tiled=True).astype(F32)
    table_pair, value_grad, table_grad, vectors, contact_grad, mlm_total, bce_total = lax.psum(
        (*tables, contact_total, mlm_total, bce_total), both
    )
    unit_t, rstd_t, normed_t, query_t, key_t = kept
    row_scale = (HD * ids_all.shape[0]) ** (-0.5)
    query_grad = []
    key_grad = []
    for h in range(HEADS):
        pair = heads_of(table_pair, h)
        query_grad.append(jnp.dot(pair, heads_of(key_t, h).astype(F32), precision=PRECISE))
        key_grad.append(jnp.dot(pair.T, heads_of(query_t, h).astype(F32), precision=PRECISE))
    proj_grad = jnp.concatenate(
        [
            jnp.concatenate(query_grad, 1) * row_scale,
            jnp.concatenate(key_grad, 1) * row_scale,
            value_grad,
        ],
        1,
    )
    proj_hi, proj_lo = split_two(proj_grad)
    normed_grad = nt(proj_hi, in_row) + nt(proj_lo, in_row)
    back_t, scale_0, shift_0 = norm_back(unit_t, rstd_t, norms[0], normed_grad)
    table_grad = table_grad + back_t
    low = me * shard
    normed_mine = lax.dynamic_slice_in_dim(normed_t, low, shard, 1)
    grad_in_row = tn(normed_mine, proj_hi) + tn(normed_mine, proj_lo)
    norm_grad = jnp.concatenate([scale_0[None], vectors[:3], shift_0[None], vectors[3:]])
    table_mine = lax.dynamic_slice_in_dim(table_grad[:VOCAB], low, shard, 1)
    norm_mine = lax.dynamic_slice_in_dim(norm_grad, low, shard, 1)
    cuts = [3 * D, 4 * D, 5 * D, 5 * D + FF]
    g_in_col, g_out_row, g_out_col, g_up, g_down = jnp.split(reduced, cuts, 1)

    local_square = (
        jnp.sum(reduced * reduced)
        + jnp.sum(grad_in_row * grad_in_row)
        + jnp.sum(table_mine * table_mine)
        + jnp.sum(norm_mine * norm_mine)
    )
    square = lax.psum(local_square, both) + jnp.sum(contact_grad * contact_grad)
    grad_norm = jnp.sqrt(square)
    factor = jnp.minimum(1.0, MAX_NORM / grad_norm)
    in_new, in_moment, in_square = adam_update(
        attention_in_master, attention_in_first, attention_in_second, jnp.stack([grad_in_row, g_in_col]) * factor, LEARN_RATE
    )
    out_new, out_moment, out_square = adam_update(
        attention_out_master, attention_out_first, attention_out_second, jnp.stack([g_out_row, g_out_col]) * factor, LEARN_RATE
    )
    up_new, up_moment, up_square = adam_update(
        feed_up_master, feed_up_first, feed_up_second, g_up * factor, LEARN_RATE
    )
    down_new, down_moment, down_square = adam_update(
        feed_down_master, feed_down_first, feed_down_second, g_down.T * factor, LEARN_RATE
    )
    table_new, table_moment, table_square = adam_update(
        embedding_master, embedding_first, embedding_second, table_mine * factor, VECTOR_RATE
    )
    norm_new, norm_moment, norm_square = adam_update(
        norm_params_master, norm_params_first, norm_params_second, norm_mine * factor, VECTOR_RATE
    )
    head_new, head_moment, head_square = adam_update(
        contact_head_master, contact_head_first, contact_head_second, contact_grad * factor, VECTOR_RATE
    )
    loss_parts = jnp.stack([mlm_total, counts[0], bce_total, counts[1]])
    return (
        in_new, in_moment, in_square,
        out_new, out_moment, out_square,
        up_new, up_moment, up_square,
        down_new, down_moment, down_square,
        table_new, table_moment, table_square,
        norm_new, norm_moment, norm_square,
        head_new, head_moment, head_square,
        in_new.astype(BF16), out_new.astype(BF16), up_new.astype(BF16), down_new.astype(BF16), table_new.astype(BF16),
        loss_parts, grad_norm,
    )


def solution(mesh):
    both = ("seq", "col")
    cells = P(None, "seq", "col")
    stack = P(None, both, None)
    row_split = P(both, None)
    col_split = P(None, both)
    weights = [stack] * 6 + [row_split] * 3 + [col_split] * 9 + [P()] * 3
    return jax.shard_map(
        shards,
        mesh=mesh,
        in_specs=(cells, cells, cells, stack, col_split, *weights),
        out_specs=(*weights, stack, stack, row_split, col_split, col_split, P(), P()),
        check_vma=False,
    )
```

```python
import functools

import jax
import jax.numpy as jnp
from jax import lax
from jax.experimental import pallas as pl
from jax.experimental.pallas import tpu as pltpu
from jax.sharding import PartitionSpec as P

D = 768
HEADS = 12
HD = 64
FF = 3072
VOCAB = 33
VP = 64
STEP = 10

NORM_EPS = 1e-05
MASK_ID = 32
MAX_NORM = 0.001
LEARN_RATE = 0.05
VECTOR_RATE = 0.5
BETA_ONE = 0.9
BETA_TWO = 0.95
ADAM_EPS = 1e-08
WEIGHT_DECAY = 0.01
PRECISE = lax.Precision.HIGHEST
F32 = jnp.float32
BF16 = jnp.bfloat16


def nn(left, right):
    return lax.dot_general(left, right, (((1,), (0,)), ((), ())), preferred_element_type=F32)


def tn(left, right):
    return lax.dot_general(left, right, (((0,), (0,)), ((), ())), preferred_element_type=F32)


def nt(left, right):
    return lax.dot_general(left, right, (((1,), (1,)), ((), ())), preferred_element_type=F32)


def split_two(values):
    high = values.astype(BF16)
    return high, (values - high.astype(F32)).astype(BF16)


def norm_stats(values):
    centre = values - jnp.mean(values, -1, keepdims=True)
    rstd = lax.rsqrt(jnp.mean(centre * centre, -1, keepdims=True) + NORM_EPS)
    return centre * rstd, rstd


def norm_back(unit, rstd, scale_vec, upstream):
    inner = upstream * scale_vec
    grad = rstd * (
        inner - jnp.mean(inner, -1, keepdims=True) - unit * jnp.mean(inner * unit, -1, keepdims=True)
    )
    return grad, jnp.sum(upstream * unit, 0), jnp.sum(upstream, 0)


GELU_K = 0.7978845608028654
GELU_C = 0.044715


def gelu_parts(up):
    square = up * up
    bent = jnp.tanh(GELU_K * up * (1.0 + GELU_C * square))
    half = 0.5 * (1.0 + bent)
    slope = half + 0.5 * up * (1.0 - bent * bent) * GELU_K * (1.0 + 3.0 * GELU_C * square)
    return up * half, slope


def heads_of(block, head):
    return block[:, head * HD : (head + 1) * HD]


def step(big, table, norms, contact_head, ids_all, ids_ri, ids_ir, targets_ir, pair_first, pair_second, labels, counts, cw):
    in_row, in_col, out_row, out_col, up_w, down_t = big
    rows, cols = ids_all.shape
    here = rows * cw
    row_scale = (HD * rows) ** (-0.5)
    vocab = jnp.arange(VP)[:, None]
    hot_all = (ids_all[:, None, :] == vocab[None]).astype(BF16).reshape(rows * VP, cols)
    hot_ri = (ids_ri[None, :] == vocab).astype(BF16)
    hot_ir = (ids_ir[None, :] == vocab).astype(BF16)
    spot = jnp.arange(here)
    perm = (
        ((spot // rows)[:, None] == (spot % cw)[None, :])
        & ((spot % rows)[:, None] == (spot // cw)[None, :])
    ).astype(BF16)

    def to_heads(block):
        return block.reshape(rows, cw, HEADS, VP).transpose(2, 1, 0, 3).reshape(HEADS * cw, rows * VP)

    def to_tokens(block):
        return block.reshape(HEADS, cw, rows, VP).transpose(2, 1, 0, 3).reshape(here, HEADS * VP)

    def per_head(block, other, how):
        return jnp.concatenate(
            [how(heads_of(block, h), heads_of(other, h)) for h in range(HEADS)], -1
        )

    table_f = table.astype(F32)
    unit_t, rstd_t = norm_stats(table_f)
    normed_t = (unit_t * norms[0] + norms[4]).astype(BF16)
    proj_t = nn(normed_t, in_row).astype(BF16)
    query_t, key_t, value_t = proj_t[:, :D], proj_t[:, D : 2 * D], proj_t[:, 2 * D :]

    pair_t = per_head(query_t, key_t, nt)
    pair_hi, pair_lo = split_two(pair_t)
    left_hi = to_heads(tn(hot_ri, pair_hi).astype(BF16))
    left_lo = to_heads(tn(hot_ri, pair_lo).astype(BF16))
    score = (nn(left_hi, hot_all) + nn(left_lo, hot_all)) * row_scale
    prob = jax.nn.softmax(score, axis=-1)
    prob_low = prob.astype(BF16)
    weight_t = to_tokens(nt(prob_low, hot_all))
    weight_hi, weight_lo = split_two(weight_t)
    row_mixed_ri = (
        per_head(weight_hi, value_t, nn) + per_head(weight_lo, value_t, nn)
    ).astype(BF16)
    row_mixed = nn(perm, row_mixed_ri).astype(BF16)
    embedded = tn(hot_ir, table)
    after_row = embedded + nn(row_mixed, out_row)

    prob_cube = prob_low.astype(F32).reshape(HEADS, cw, cols)
    head_sum = jnp.sum(prob_cube * contact_head[:HEADS, None, None], 0)
    first_hot = (pair_first[None, :] == jnp.arange(cw)[:, None]).astype(F32)
    second_hot = (pair_second[None, :] == jnp.arange(cols)[:, None]).astype(BF16)
    sum_hi, sum_lo = split_two(head_sum)
    sum_last = (head_sum - sum_hi.astype(F32) - sum_lo.astype(F32)).astype(BF16)
    picked = nn(sum_hi, second_hot) + nn(sum_lo, second_hot) + nn(sum_last, second_hot)
    contact_logit = jnp.sum(picked * first_hot, 0) * cols + contact_head[HEADS]
    owned = jnp.sum(first_hot, 0) > 0
    valid = (labels >= 0) & owned
    positive = (labels == 1).astype(F32)
    bce_sum = jnp.sum(
        jnp.where(valid, jax.nn.softplus(contact_logit) - positive * contact_logit, 0.0)
    )
    coef = jnp.where(valid, jax.nn.sigmoid(contact_logit) - positive, 0.0) / counts[1]
    coef_hi, coef_lo = split_two(coef)
    first_low = first_hot.astype(BF16)
    touch = nt(first_low * coef_hi[None], second_hot) + nt(first_low * coef_lo[None], second_hot)
    grad_contact = jnp.concatenate(
        [jnp.sum(prob_cube * touch[None], (1, 2)) * cols, jnp.sum(coef)[None]]
    )

    unit_1, rstd_1 = norm_stats(after_row)
    col_normed = (unit_1 * norms[1] + norms[5]).astype(BF16)
    col_proj = nn(col_normed, in_col).astype(BF16)
    group = 128 if here % 128 == 0 and 128 % rows == 0 else here
    groups = here // group
    lane = jnp.arange(group)
    same = (lane[:, None] // rows) == (lane[None, :] // rows)

    def cut(block):
        return block.reshape(groups, group, HEADS, HD)

    col_query, col_key, col_value = (cut(col_proj[:, k * D : (k + 1) * D]) for k in range(3))
    col_score = jnp.einsum("gqhe,gkhe->ghqk", col_query, col_key, preferred_element_type=F32) * HD ** (-0.5)
    col_prob = jax.nn.softmax(jnp.where(same, col_score, -1e30), axis=-1)
    col_prob_low = col_prob.astype(BF16)
    col_mixed = (
        jnp.einsum("ghqk,gkhe->gqhe", col_prob_low, col_value, preferred_element_type=F32)
        .astype(BF16)
        .reshape(here, D)
    )
    after_col = after_row + nn(col_mixed, out_col)

    unit_2, rstd_2 = norm_stats(after_col)
    feed_normed = (unit_2 * norms[2] + norms[6]).astype(BF16)
    hidden_up = nn(feed_normed, up_w)
    active, slope = gelu_parts(hidden_up)
    active = active.astype(BF16)
    after_feed = after_col + nt(active, down_t)
    unit_3, rstd_3 = norm_stats(after_feed)
    head_normed = (unit_3 * norms[3] + norms[7]).astype(BF16)
    logits = nt(table, head_normed) * D ** (-0.5)
    logits = jnp.where(vocab < VOCAB, logits, -1e30)
    top = jnp.max(logits, 0, keepdims=True)
    shifted = logits - top
    log_probs = shifted - jnp.log(jnp.sum(jnp.exp(shifted), 0, keepdims=True))
    target_hot = (targets_ir[None, :] == vocab).astype(F32)
    keep = ids_ir[None, :] == MASK_ID
    mlm_sum = -jnp.sum(jnp.where(keep & (target_hot > 0), log_probs, 0.0))
    logit_grad = jnp.where(keep, jnp.exp(log_probs) - target_hot, 0.0) / counts[0]
    logit_low = (logit_grad * D ** (-0.5)).astype(BF16)

    grad_head = nn(logit_low, head_normed)
    stream, scale_3, shift_3 = norm_back(unit_3, rstd_3, norms[3], tn(logit_low, table))
    branch = stream.astype(BF16)
    grad_down = tn(branch, active)
    up_low = (nn(branch, down_t) * slope).astype(BF16)
    grad_up = tn(feed_normed, up_low)
    inner, scale_2, shift_2 = norm_back(unit_2, rstd_2, norms[2], nt(up_low, up_w))
    stream = stream + inner
    branch = stream.astype(BF16)
    grad_out_col = tn(col_mixed, branch)
    mixed_low = nt(branch, out_col).astype(BF16)
    mixed_cut = cut(mixed_low)
    prob_grad = jnp.einsum("gqhe,gkhe->ghqk", mixed_cut, col_value, preferred_element_type=F32)
    score_grad = col_prob * (prob_grad - jnp.sum(col_prob * prob_grad, -1, keepdims=True))
    score_low = score_grad.astype(BF16)
    grad_q = jnp.einsum("ghqk,gkhe->gqhe", score_low, col_key, preferred_element_type=F32)
    grad_k = jnp.einsum("ghqk,gqhe->gkhe", score_low, col_query, preferred_element_type=F32)
    grad_v = jnp.einsum("ghqk,gqhe->gkhe", col_prob_low, mixed_cut, preferred_element_type=F32)
    proj_low = jnp.concatenate(
        [
            (grad_q * HD ** (-0.5)).reshape(here, D),
            (grad_k * HD ** (-0.5)).reshape(here, D),
            grad_v.reshape(here, D),
        ],
        -1,
    ).astype(BF16)
    grad_in_col = tn(col_normed, proj_low)
    inner, scale_1, shift_1 = norm_back(unit_1, rstd_1, norms[1], nt(proj_low, in_col))
    stream = stream + inner
    branch = stream.astype(BF16)
    grad_out_row = tn(row_mixed, branch)
    mixed_low = nt(branch, out_row).astype(BF16)
    mixed_ri = tn(perm, mixed_low).astype(BF16)
    drive_hi, drive_lo = split_two(per_head(mixed_ri, value_t, nt))
    prob_grad = nn(to_heads(drive_hi), hot_all) + nn(to_heads(drive_lo), hot_all)
    prob_grad = prob_grad + (
        touch[None] * (contact_head[:HEADS, None, None] * cols)
    ).reshape(HEADS * cw, cols)
    score_grad = prob * (prob_grad - jnp.sum(prob * prob_grad, -1, keepdims=True))
    score_low = score_grad.astype(BF16)
    spread = to_tokens(nt(score_low, hot_all)).astype(BF16)
    table_pair = nn(hot_ri, spread)
    value_grad = per_head(weight_hi, mixed_ri, tn)
    stream_hi, stream_lo = split_two(stream)
    lookup_grad = nn(hot_ir, stream_hi) + nn(hot_ir, stream_lo)
    vectors = jnp.stack([scale_1, scale_2, scale_3, shift_1, shift_2, shift_3])
    return (
        (grad_in_col, grad_out_row, grad_out_col, grad_up, grad_down),
        (table_pair, value_grad, grad_head + lookup_grad, vectors),
        grad_contact,
        mlm_sum,
        bce_sum,
        (unit_t, rstd_t, normed_t, query_t, key_t),
    )


MESH = pl.DeviceIdType.MESH
NZ, NY = 4, 2


def place():
    s, c = lax.axis_index("seq"), lax.axis_index("col")
    z, y, k = s // 4, lax.rem(s // 2, 2), lax.rem(s, 2)
    return z, y, k, c


def device(z, y, k, c):
    return (z * 4 + y * 2 + k, c)


def greet_all():
    z, y, k, c = place()
    me = (z * 4 + y * 2 + k) * 2 + c
    barrier = pltpu.get_barrier_semaphore()

    def signal(step, carry):
        other = lax.rem(me + step, 32)
        pl.semaphore_signal(
            barrier, inc=1, device_id=(other // 2, lax.rem(other, 2)), device_id_type=MESH
        )
        return carry

    lax.fori_loop(1, 32, signal, 0)
    return barrier


def remote(src, dst, send, recv, target):
    return pltpu.make_async_remote_copy(
        src_ref=src, dst_ref=dst, send_sem=send, recv_sem=recv, device_id=target, device_id_type=MESH
    )


def gather_kernel(widths, *refs):
    count = len(widths)
    small = refs[0]
    masters = refs[1 : 1 + count]
    small_out = refs[1 + count]
    outs = refs[2 + count : 2 + 2 * count]
    at = 2 + 2 * count
    outgoing = refs[at : at + count]
    incoming = refs[at + count : at + 2 * count]
    piece = refs[at + 2 * count : at + 3 * count]
    small_send, small_recv, send, recv, local = refs[at + 3 * count :]
    z, y, k, c = place()
    me = (z * 4 + y * 2 + k) * 2 + c
    barrier = greet_all()
    for m in range(count):
        n = widths[m]
        left, right = masters[m][:, :n], masters[m][:, n:]
        other = jnp.where(c == 0, right, left)
        outgoing[m][...] = jnp.concatenate([other, jnp.zeros((8, n), F32)], 0).astype(BF16)
    pl.semaphore_wait(barrier, 31)

    def small_copy(step):
        other = lax.rem(me + step, 32)
        return remote(
            small, small_out.at[me], small_send.at[step], small_recv.at[step], (other // 2, lax.rem(other, 2))
        )

    def spread(step, carry):
        small_copy(step).start()
        return carry

    across, beside, twin = device(z, y, k, 1 - c), device(z, 1 - y, k, c), device(z, y, 1 - k, c)

    def copy(m, at, src, dst, target):
        return remote(src, dst, send.at[m, at], recv.at[m, at], target)

    def pair_copy(m):
        return copy(m, 0, outgoing[m], incoming[m], across)

    def own_copy(m):
        return pltpu.make_async_copy(piece[m], outs[m].at[c, z, y, k], local.at[m])

    def line_copy(m, step):
        return copy(m, step, piece[m], outs[m].at[c, z, y, k], device(lax.rem(z + step, 4), y, k, c))

    def same(m, at, where, target):
        view = outs[m].at[where]
        return copy(m, at, view, view, target)

    low, high = pl.ds(0, 2), pl.ds(2, 2)

    def second(m):
        return [same(m, 4, (c, low, y, k), across), same(m, 5, (c, high, y, k), beside)]

    def third_own(m):
        return [same(m, 6, (c, low, y, k), beside), same(m, 7, (c, high, y, k), across)]

    def third_far(m):
        return [same(m, 8, (1 - c, low, y, k), beside), same(m, 9, (c, high, 1 - y, k), across)]

    def twin_own(m):
        return [same(m, 10, (c, slice(None), y, k), twin)]

    def twin_second(m):
        return [same(m, 11, (1 - c, low, y, k), twin), same(m, 12, (c, high, 1 - y, k), twin)]

    def twin_third(m):
        return [
            same(m, 13, (c, low, 1 - y, k), twin),
            same(m, 14, (1 - c, high, y, k), twin),
            same(m, 15, (1 - c, low, 1 - y, k), twin),
            same(m, 16, (1 - c, high, 1 - y, k), twin),
        ]

    for m in range(count):
        pair_copy(m).start()
    lax.fori_loop(1, 32, spread, 0)
    small_out[me] = small[...]

    def stage_line(m):
        n = widths[m]
        pair_copy(m).wait_recv()
        mine = jnp.where(c == 0, masters[m][:, :n], masters[m][:, n:])
        theirs = incoming[m][...].astype(F32)[:24]
        top = jnp.where(c == 0, mine, theirs)
        bottom = jnp.where(c == 0, theirs, mine)
        piece[m][...] = jnp.concatenate([top, bottom], 0).astype(BF16)
        own_copy(m).start()
        for step in (1, 3, 2):
            line_copy(m, step).start()

    def stage_second(m):
        own_copy(m).wait()
        for step in (1, 3, 2):
            line_copy(m, step).wait_recv()
        for item in second(m) + third_own(m) + twin_own(m):
            item.start()

    def stage_third(m):
        for item in second(m):
            item.wait_recv()
        for item in third_far(m) + twin_second(m):
            item.start()

    def stage_twin(m):
        for item in third_own(m) + third_far(m):
            item.wait_recv()
        for item in twin_third(m):
            item.start()

    def stage_end(m):
        for item in twin_own(m) + twin_second(m) + twin_third(m):
            item.wait_recv()

    stages = (stage_line, stage_second, stage_third, stage_twin, stage_end)
    for tick in range(count + len(stages) - 1):
        for number, stage in enumerate(stages):
            if 0 <= tick - number < count:
                stage(tick - number)
    for m in range(count):
        pair_copy(m).wait_send()
        for step in (1, 2, 3):
            line_copy(m, step).wait_send()
        for item in second(m) + third_own(m) + third_far(m) + twin_own(m) + twin_second(m) + twin_third(m):
            item.wait_send()

    def finish(step, carry):
        small_copy(step).wait()
        return carry

    lax.fori_loop(1, 32, finish, 0)


def gather_all(small, masters):
    widths = tuple(m.shape[1] // 2 for m in masters)
    count = len(widths)
    anywhere = pl.BlockSpec(memory_space=pl.ANY)
    inside = pl.BlockSpec(memory_space=pltpu.VMEM)
    outs = pl.pallas_call(
        functools.partial(gather_kernel, widths),
        out_shape=[jax.ShapeDtypeStruct((32, *small.shape), small.dtype)]
        + [jax.ShapeDtypeStruct((2, NZ, NY, 2, 48, n), BF16) for n in widths],
        in_specs=[inside] * (1 + count),
        out_specs=[inside] + [anywhere] * count,
        scratch_shapes=[pltpu.VMEM((32, n), BF16) for n in widths] * 2
        + [pltpu.VMEM((48, n), BF16) for n in widths]
        + [
            pltpu.SemaphoreType.DMA((32,)),
            pltpu.SemaphoreType.DMA((32,)),
            pltpu.SemaphoreType.DMA((count, 17)),
            pltpu.SemaphoreType.DMA((count, 17)),
            pltpu.SemaphoreType.DMA((count,)),
        ],
        compiler_params=pltpu.CompilerParams(
            collective_id=0, has_side_effects=True, vmem_limit_bytes=48 * 2**20
        ),
    )(small, *masters)
    return outs[0], outs[1:]


def scatter_kernel(widths, *refs):
    count = len(widths)
    table = refs[0]
    grads = refs[1 : 1 + count]
    table_out = refs[1 + count]
    outs = refs[2 + count : 2 + 2 * count]
    scratch = refs[2 + 2 * count :]
    acc, got_0, got_1a, got_1b, got_2a, got_2b, got_3, total, got_4 = (
        scratch[i * count : (i + 1) * count] for i in range(9)
    )
    table_got, table_send, table_recv, send, recv, local = scratch[9 * count :]
    z, y, k, c = place()
    me = (z * 4 + y * 2 + k) * 2 + c
    across, beside, twin = device(z, y, k, 1 - c), device(z, 1 - y, k, c), device(z, y, 1 - k, c)
    barrier = greet_all()

    def own_copy(m):
        return pltpu.make_async_copy(grads[m].at[:, :, :, k], acc[m], local.at[m])

    for m in range(count):
        own_copy(m).start()
    pl.semaphore_wait(barrier, 31)

    def copy(m, at, src, dst, target):
        return remote(src, dst, send.at[m, at], recv.at[m, at], target)

    def twin_copy(m):
        return copy(m, 0, grads[m].at[:, :, :, 1 - k], got_0[m], twin)

    low, high = pl.ds(0, 2), pl.ds(2, 2)

    def first(m):
        return [
            copy(m, 1, acc[m].at[:, low, 1 - y], got_1a[m], beside),
            copy(m, 2, acc[m].at[1 - c, high], got_1b[m], across),
        ]

    def second(m):
        return [
            copy(m, 3, acc[m].at[1 - c, low, y], got_2a[m], across),
            copy(m, 4, acc[m].at[c, high, 1 - y], got_2b[m], beside),
        ]

    def line(m):
        return [
            copy(m, 4 + step, acc[m].at[c, lax.rem(z + step, 4), y], got_3[m].at[step - 1], device(lax.rem(z + step, 4), y, k, c))
            for step in (1, 2, 3)
        ]

    def pair(m):
        return [copy(m, 8, total[m].at[1 - c], got_4[m], across)]

    def table_copy(step, back):
        other = lax.rem(me + step, 32)
        target = (other // 2, lax.rem(other, 2))
        if back:
            return remote(
                table_out.at[me], table_out.at[me], table_send.at[1, step], table_recv.at[1, step], target
            )
        return remote(
            table.at[other], table_got.at[me], table_send.at[0, step], table_recv.at[0, step], target
        )

    def each(action):
        def body(step, carry):
            action(step)
            return carry

        lax.fori_loop(1, 32, body, 0)

    def plus(left, right):
        return (left.astype(F32) + right.astype(F32)).astype(BF16)

    for m in range(count):
        twin_copy(m).start()
    each(lambda step: table_copy(step, False).start())

    def stage_first(m):
        own_copy(m).wait()
        twin_copy(m).wait_recv()

        def body(at, carry):
            zz = at // 2
            yy = lax.rem(at, 2)
            for cc in range(2):
                acc[m][cc, zz, yy] = plus(acc[m][cc, zz, yy], got_0[m][cc, zz, yy])
            return carry

        lax.fori_loop(0, NZ * NY, body, 0)
        for item in first(m):
            item.start()

    def stage_second(m):
        for item in first(m):
            item.wait_recv()
        for a in range(2):
            for b in range(2):
                acc[m][a, b, y] = plus(acc[m][a, b, y], got_1a[m][a, b])
                acc[m][c, 2 + a, b] = plus(acc[m][c, 2 + a, b], got_1b[m][a, b])
        for item in second(m):
            item.start()

    def stage_line(m):
        for item in second(m):
            item.wait_recv()
        for a in range(2):
            acc[m][c, a, y] = plus(acc[m][c, a, y], got_2a[m][a])
            acc[m][c, 2 + a, y] = plus(acc[m][c, 2 + a, y], got_2b[m][a])
        for item in line(m):
            item.start()

    def stage_pair(m):
        for item in line(m):
            item.wait_recv()
        full = acc[m][c, z, y].astype(F32)
        for step in range(3):
            full = full + got_3[m][step].astype(F32)
        total[m][0] = full[:24]
        total[m][1] = full[24:]
        for item in pair(m):
            item.start()

    def stage_end(m):
        outs[m][c] = total[m][c]
        for item in pair(m):
            item.wait_recv()
        outs[m][1 - c] = got_4[m][...]

    def table_sum():
        table_got[me] = table[me]
        each(lambda step: table_copy(step, False).wait_recv())

        def body(at, held):
            return held + table_got[at]

        table_out[me] = lax.fori_loop(1, 32, body, table_got[0])
        each(lambda step: table_copy(step, True).start())

    stages = (stage_first, stage_second, stage_line, stage_pair, stage_end)
    for tick in range(count + len(stages) - 1):
        for number, stage in enumerate(stages):
            if 0 <= tick - number < count:
                stage(tick - number)
        if tick == count - 1:
            table_sum()
    each(lambda step: table_copy(step, True).wait())
    each(lambda step: table_copy(step, False).wait_send())
    for m in range(count):
        for item in [twin_copy(m)] + first(m) + second(m) + line(m) + pair(m):
            item.wait_send()


def scatter_all(table, grads):
    widths = tuple(g.shape[-1] for g in grads)
    count = len(widths)
    anywhere = pl.BlockSpec(memory_space=pl.ANY)
    inside = pl.BlockSpec(memory_space=pltpu.VMEM)

    def shapes(lead, dtype):
        return [pltpu.VMEM((*lead, n), dtype) for n in widths]

    outs = pl.pallas_call(
        functools.partial(scatter_kernel, widths),
        out_shape=[jax.ShapeDtypeStruct(table.shape, F32)]
        + [jax.ShapeDtypeStruct((2, 24, n), F32) for n in widths],
        in_specs=[inside] + [anywhere] * count,
        out_specs=[inside] * (1 + count),
        scratch_shapes=shapes((2, NZ, NY, 48), BF16)
        + shapes((2, NZ, NY, 48), BF16)
        + shapes((2, 2, 48), BF16)
        + shapes((2, 2, 48), BF16)
        + shapes((2, 48), BF16)
        + shapes((2, 48), BF16)
        + shapes((3, 48), BF16)
        + shapes((2, 24), F32)
        + shapes((24,), F32)
        + [
            pltpu.VMEM(table.shape, F32),
            pltpu.SemaphoreType.DMA((2, 32)),
            pltpu.SemaphoreType.DMA((2, 32)),
            pltpu.SemaphoreType.DMA((count, 9)),
            pltpu.SemaphoreType.DMA((count, 9)),
            pltpu.SemaphoreType.DMA((count,)),
        ],
        compiler_params=pltpu.CompilerParams(
            collective_id=1, has_side_effects=True, vmem_limit_bytes=56 * 2**20
        ),
    )(table, *grads)
    return outs[0], outs[1:]


def adam_update(master, first, second, grad_part, rate):
    first = BETA_ONE * first + (1.0 - BETA_ONE) * grad_part
    second = BETA_TWO * second + (1.0 - BETA_TWO) * grad_part * grad_part
    moved = first / (1.0 - BETA_ONE**STEP) / (jnp.sqrt(second / (1.0 - BETA_TWO**STEP)) + ADAM_EPS)
    return (master - rate * (moved + WEIGHT_DECAY * master), first, second)


def shards(
    tokens,
    targets,
    masked,
    contact_pairs,
    labels,
    attention_in_master,
    attention_in_first,
    attention_in_second,
    attention_out_master,
    attention_out_first,
    attention_out_second,
    feed_up_master,
    feed_up_first,
    feed_up_second,
    feed_down_master,
    feed_down_first,
    feed_down_second,
    embedding_master,
    embedding_first,
    embedding_second,
    norm_params_master,
    norm_params_first,
    norm_params_second,
    contact_head_master,
    contact_head_first,
    contact_head_second,
):
    both = ("seq", "col")
    micro, rows_here, cols_here = tokens.shape
    ncol = lax.axis_size("col")
    ndev = lax.axis_size("seq") * ncol
    cols = cols_here * ncol
    me = lax.axis_index("seq") * ncol + lax.axis_index("col")
    per = ndev // micro
    cw = cols // per
    mine = me // per
    base = (me % per) * cw
    shard = D // ndev

    tiled = lax.axis_size("seq") == 16 and ncol == 2
    inputs = jnp.where(masked > 0, MASK_ID, tokens)
    masters = [
        jnp.concatenate(
            [
                jnp.pad(embedding_master.T, ((0, 0), (0, 128 - VOCAB))),
                jnp.pad(norm_params_master.T, ((0, 0), (0, 120))),
            ],
            1,
        ),
        attention_in_master[0],
        attention_out_master[0],
        attention_in_master[1],
        attention_out_master[1],
        feed_up_master,
        feed_down_master.T,
    ]
    if tiled:
        small = jnp.concatenate(
            [
                inputs.reshape(4, 128),
                targets.reshape(4, 128),
                contact_pairs[..., 0].reshape(1, 128),
                contact_pairs[..., 1].reshape(1, 128),
                labels.reshape(1, 128),
                jnp.zeros((5, 128), jnp.int32),
            ]
        )
        small_all, gathered = gather_all(small, masters)
        small_all = small_all.reshape(16, 2, 16, 128)
        whole = small_all[:, :, :8].reshape(16, 2, 2, 2, 2, 128).transpose(2, 3, 0, 1, 4, 5).reshape(2, 2, 16, 512)
        pairs_all = small_all[:, :, 8:11].reshape(32, 3, 2, 64).transpose(2, 0, 3, 1).reshape(2, 2048, 3)
        gathered = [g.reshape(2, D, g.shape[-1]) for g in gathered]
    else:
        whole = jnp.stack([inputs, targets])
        whole = lax.all_gather(lax.all_gather(whole, "col", axis=3, tiled=True), "seq", axis=2, tiled=True)
        pairs_all = lax.all_gather(
            jnp.concatenate([contact_pairs, labels[:, :, None]], -1), both, axis=1, tiled=True
        )
        gathered = []
        for master in masters:
            full = lax.all_gather(master.astype(BF16), both, axis=0, tiled=True)
            gathered.append(full.reshape(D, 2, -1).transpose(1, 0, 2))
    counts = (
        jnp.sum(whole[0] == MASK_ID).astype(F32),
        jnp.sum(pairs_all[..., 2] >= 0).astype(F32),
    )
    ids_all = lax.dynamic_index_in_dim(whole[0], mine, 0, False)
    ids_local = lax.dynamic_slice_in_dim(ids_all, base, cw, 1)
    targets_local = lax.dynamic_slice_in_dim(
        lax.dynamic_index_in_dim(whole[1], mine, 0, False), base, cw, 1
    )
    pairs = lax.dynamic_index_in_dim(pairs_all, mine, 0, False)

    table = gathered[0][0][:, :VP].T
    norms = gathered[0][1][:, :8].T.astype(F32)
    in_row, out_row, in_col, out_col, up_w, down_t = (
        jnp.concatenate([g[0], g[1]], 1) for g in gathered[1:]
    )
    big = (in_row, in_col, out_row, out_col, up_w, down_t)

    grads, tables, contact_total, mlm_total, bce_total, kept = step(
        big,
        table,
        norms,
        contact_head_master,
        ids_all,
        ids_local.reshape(-1),
        ids_local.T.reshape(-1),
        targets_local.T.reshape(-1),
        pairs[:, 0] - base,
        pairs[:, 1],
        pairs[:, 2],
        counts,
        cw,
    )
    table_pair, value_grad, table_grad, vectors = tables
    extras = jnp.zeros((2, D), F32).at[0, : HEADS + 3].set(
        jnp.concatenate([contact_total, mlm_total[None], bce_total[None]])
    )
    sums = jnp.concatenate([table_pair[:40], value_grad[:40], table_grad[:40], vectors, extras])
    if tiled:
        sums = sums.reshape(16, 8, 2, 384).transpose(0, 2, 1, 3).reshape(32, 8, 384)
        blocks = []
        for g in (grads[4], grads[3], grads[2], grads[0], grads[1]):
            n = g.shape[1] // 2
            blocks.append(jnp.stack([g[:, :n], g[:, n:]]).astype(BF16).reshape(2, NZ, NY, 2, 48, n))
        sums, reduced = scatter_all(sums, blocks)
        sums = sums.reshape(16, 2, 8, 384).transpose(0, 2, 1, 3).reshape(128, D)
        g_down, g_up, g_out_col, g_in_col, g_out_row = (jnp.concatenate([r[0], r[1]], 1) for r in reduced)
    else:
        flat_grad = jnp.concatenate([g.astype(BF16) for g in grads], 1)
        reduced = lax.psum_scatter(flat_grad, both, scatter_dimension=0, tiled=True).astype(F32)
        g_in_col, g_out_row, g_out_col, g_up, g_down = jnp.split(
            reduced, [3 * D, 4 * D, 5 * D, 5 * D + FF], 1
        )
        sums = lax.psum(sums, both)
    spare = ((0, VP - 40), (0, 0))
    table_pair, value_grad, table_grad = (
        jnp.pad(sums[a : a + 40], spare) for a in (0, 40, 80)
    )
    vectors = sums[120:126]
    contact_grad, mlm_total, bce_total = (
        sums[126, : HEADS + 1], sums[126, HEADS + 1], sums[126, HEADS + 2]
    )
    unit_t, rstd_t, normed_t, query_t, key_t = kept
    row_scale = (HD * ids_all.shape[0]) ** (-0.5)
    query_grad = []
    key_grad = []
    for h in range(HEADS):
        pair = heads_of(table_pair, h)
        query_grad.append(jnp.dot(pair, heads_of(key_t, h).astype(F32), precision=PRECISE))
        key_grad.append(jnp.dot(pair.T, heads_of(query_t, h).astype(F32), precision=PRECISE))
    proj_grad = jnp.concatenate(
        [
            jnp.concatenate(query_grad, 1) * row_scale,
            jnp.concatenate(key_grad, 1) * row_scale,
            value_grad,
        ],
        1,
    )
    proj_hi, proj_lo = split_two(proj_grad)
    normed_grad = nt(proj_hi, in_row) + nt(proj_lo, in_row)
    back_t, scale_0, shift_0 = norm_back(unit_t, rstd_t, norms[0], normed_grad)
    table_grad = table_grad + back_t
    low = me * shard
    normed_mine = lax.dynamic_slice_in_dim(normed_t, low, shard, 1)
    grad_in_row = tn(normed_mine, proj_hi) + tn(normed_mine, proj_lo)
    norm_grad = jnp.concatenate([scale_0[None], vectors[:3], shift_0[None], vectors[3:]])
    table_mine = lax.dynamic_slice_in_dim(table_grad[:VOCAB], low, shard, 1)
    norm_mine = lax.dynamic_slice_in_dim(norm_grad, low, shard, 1)
    reduced_all = (g_in_col, g_out_row, g_out_col, g_up, g_down)

    local_square = (
        sum(jnp.sum(g * g) for g in reduced_all)
        + jnp.sum(grad_in_row * grad_in_row)
        + jnp.sum(table_mine * table_mine)
        + jnp.sum(norm_mine * norm_mine)
    )
    square = lax.psum(local_square, both) + jnp.sum(contact_grad * contact_grad)
    grad_norm = jnp.sqrt(square)
    factor = jnp.minimum(1.0, MAX_NORM / grad_norm)
    in_new, in_moment, in_square = adam_update(
        attention_in_master, attention_in_first, attention_in_second, jnp.stack([grad_in_row, g_in_col]) * factor, LEARN_RATE
    )
    out_new, out_moment, out_square = adam_update(
        attention_out_master, attention_out_first, attention_out_second, jnp.stack([g_out_row, g_out_col]) * factor, LEARN_RATE
    )
    up_new, up_moment, up_square = adam_update(
        feed_up_master, feed_up_first, feed_up_second, g_up * factor, LEARN_RATE
    )
    down_new, down_moment, down_square = adam_update(
        feed_down_master, feed_down_first, feed_down_second, g_down.T * factor, LEARN_RATE
    )
    table_new, table_moment, table_square = adam_update(
        embedding_master, embedding_first, embedding_second, table_mine * factor, VECTOR_RATE
    )
    norm_new, norm_moment, norm_square = adam_update(
        norm_params_master, norm_params_first, norm_params_second, norm_mine * factor, VECTOR_RATE
    )
    head_new, head_moment, head_square = adam_update(
        contact_head_master, contact_head_first, contact_head_second, contact_grad * factor, VECTOR_RATE
    )
    loss_parts = jnp.stack([mlm_total, counts[0], bce_total, counts[1]])
    return (
        in_new, in_moment, in_square,
        out_new, out_moment, out_square,
        up_new, up_moment, up_square,
        down_new, down_moment, down_square,
        table_new, table_moment, table_square,
        norm_new, norm_moment, norm_square,
        head_new, head_moment, head_square,
        in_new.astype(BF16), out_new.astype(BF16), up_new.astype(BF16), down_new.astype(BF16), table_new.astype(BF16),
        loss_parts, grad_norm,
    )


def solution(mesh):
    both = ("seq", "col")
    cells = P(None, "seq", "col")
    stack = P(None, both, None)
    row_split = P(both, None)
    col_split = P(None, both)
    weights = [stack] * 6 + [row_split] * 3 + [col_split] * 9 + [P()] * 3
    return jax.shard_map(
        shards,
        mesh=mesh,
        in_specs=(cells, cells, cells, stack, col_split, *weights),
        out_specs=(*weights, stack, stack, row_split, col_split, col_split, P(), P()),
        check_vma=False,
    )
```

```python
import functools

import jax
import jax.numpy as jnp
from jax import lax
from jax.experimental import pallas as pl
from jax.experimental.pallas import tpu as pltpu
from jax.sharding import PartitionSpec as P

D = 768
HEADS = 12
HD = 64
FF = 3072
VOCAB = 33
VP = 64
STEP = 10

NORM_EPS = 1e-05
MASK_ID = 32
MAX_NORM = 0.001
LEARN_RATE = 0.05
VECTOR_RATE = 0.5
BETA_ONE = 0.9
BETA_TWO = 0.95
ADAM_EPS = 1e-08
WEIGHT_DECAY = 0.01
PRECISE = lax.Precision.HIGHEST
F32 = jnp.float32
BF16 = jnp.bfloat16


def nn(left, right):
    return lax.dot_general(left, right, (((1,), (0,)), ((), ())), preferred_element_type=F32)


def tn(left, right):
    return lax.dot_general(left, right, (((0,), (0,)), ((), ())), preferred_element_type=F32)


def nt(left, right):
    return lax.dot_general(left, right, (((1,), (1,)), ((), ())), preferred_element_type=F32)


def split_two(values):
    high = values.astype(BF16)
    return high, (values - high.astype(F32)).astype(BF16)


def norm_stats(values):
    centre = values - jnp.mean(values, -1, keepdims=True)
    rstd = lax.rsqrt(jnp.mean(centre * centre, -1, keepdims=True) + NORM_EPS)
    return centre * rstd, rstd


def norm_back(unit, rstd, scale_vec, upstream):
    inner = upstream * scale_vec
    grad = rstd * (
        inner - jnp.mean(inner, -1, keepdims=True) - unit * jnp.mean(inner * unit, -1, keepdims=True)
    )
    return grad, jnp.sum(upstream * unit, 0), jnp.sum(upstream, 0)


GELU_K = 0.7978845608028654
GELU_C = 0.044715


def gelu_parts(up):
    square = up * up
    bent = jnp.tanh(GELU_K * up * (1.0 + GELU_C * square))
    half = 0.5 * (1.0 + bent)
    slope = half + 0.5 * up * (1.0 - bent * bent) * GELU_K * (1.0 + 3.0 * GELU_C * square)
    return up * half, slope


def heads_of(block, head):
    return block[:, head * HD : (head + 1) * HD]


def step(big, table, norms, contact_head, ids_all, ids_ri, ids_ir, targets_ir, pair_first, pair_second, labels, counts, cw):
    in_row, in_col, out_row, out_col, up_w, down_t = big
    rows, cols = ids_all.shape
    here = rows * cw
    row_scale = (HD * rows) ** (-0.5)
    vocab = jnp.arange(VP)[:, None]
    hot_all = (ids_all[:, None, :] == vocab[None]).astype(BF16).reshape(rows * VP, cols)
    hot_ri = (ids_ri[None, :] == vocab).astype(BF16)
    hot_ir = (ids_ir[None, :] == vocab).astype(BF16)
    spot = jnp.arange(here)
    perm = (
        ((spot // rows)[:, None] == (spot % cw)[None, :])
        & ((spot % rows)[:, None] == (spot // cw)[None, :])
    ).astype(BF16)

    def to_heads(block):
        return block.reshape(rows, cw, HEADS, VP).transpose(2, 1, 0, 3).reshape(HEADS * cw, rows * VP)

    def to_tokens(block):
        return block.reshape(HEADS, cw, rows, VP).transpose(2, 1, 0, 3).reshape(here, HEADS * VP)

    def per_head(block, other, how):
        return jnp.concatenate(
            [how(heads_of(block, h), heads_of(other, h)) for h in range(HEADS)], -1
        )

    table_f = table.astype(F32)
    unit_t, rstd_t = norm_stats(table_f)
    normed_t = (unit_t * norms[0] + norms[4]).astype(BF16)
    proj_t = nn(normed_t, in_row).astype(BF16)
    query_t, key_t, value_t = proj_t[:, :D], proj_t[:, D : 2 * D], proj_t[:, 2 * D :]

    pair_t = per_head(query_t, key_t, nt)
    pair_hi, pair_lo = split_two(pair_t)
    left_hi = to_heads(tn(hot_ri, pair_hi).astype(BF16))
    left_lo = to_heads(tn(hot_ri, pair_lo).astype(BF16))
    score = (nn(left_hi, hot_all) + nn(left_lo, hot_all)) * row_scale
    prob = jax.nn.softmax(score, axis=-1)
    prob_low = prob.astype(BF16)
    weight_t = to_tokens(nt(prob_low, hot_all))
    weight_hi, weight_lo = split_two(weight_t)
    row_mixed_ri = (
        per_head(weight_hi, value_t, nn) + per_head(weight_lo, value_t, nn)
    ).astype(BF16)
    row_mixed = nn(perm, row_mixed_ri).astype(BF16)
    embedded = tn(hot_ir, table)
    after_row = embedded + nn(row_mixed, out_row)

    prob_cube = prob_low.astype(F32).reshape(HEADS, cw, cols)
    head_sum = jnp.sum(prob_cube * contact_head[:HEADS, None, None], 0)
    first_hot = (pair_first[None, :] == jnp.arange(cw)[:, None]).astype(F32)
    second_hot = (pair_second[None, :] == jnp.arange(cols)[:, None]).astype(BF16)
    sum_hi, sum_lo = split_two(head_sum)
    sum_last = (head_sum - sum_hi.astype(F32) - sum_lo.astype(F32)).astype(BF16)
    picked = nn(sum_hi, second_hot) + nn(sum_lo, second_hot) + nn(sum_last, second_hot)
    contact_logit = jnp.sum(picked * first_hot, 0) * cols + contact_head[HEADS]
    owned = jnp.sum(first_hot, 0) > 0
    valid = (labels >= 0) & owned
    positive = (labels == 1).astype(F32)
    bce_sum = jnp.sum(
        jnp.where(valid, jax.nn.softplus(contact_logit) - positive * contact_logit, 0.0)
    )
    coef = jnp.where(valid, jax.nn.sigmoid(contact_logit) - positive, 0.0) / counts[1]
    coef_hi, coef_lo = split_two(coef)
    first_low = first_hot.astype(BF16)
    touch = nt(first_low * coef_hi[None], second_hot) + nt(first_low * coef_lo[None], second_hot)
    grad_contact = jnp.concatenate(
        [jnp.sum(prob_cube * touch[None], (1, 2)) * cols, jnp.sum(coef)[None]]
    )

    unit_1, rstd_1 = norm_stats(after_row)
    col_normed = (unit_1 * norms[1] + norms[5]).astype(BF16)
    col_proj = nn(col_normed, in_col).astype(BF16)
    group = 128 if here % 128 == 0 and 128 % rows == 0 else here
    groups = here // group
    lane = jnp.arange(group)
    same = (lane[:, None] // rows) == (lane[None, :] // rows)

    def cut(block):
        return block.reshape(groups, group, HEADS, HD)

    col_query, col_key, col_value = (cut(col_proj[:, k * D : (k + 1) * D]) for k in range(3))
    col_score = jnp.einsum("gqhe,gkhe->ghqk", col_query, col_key, preferred_element_type=F32) * HD ** (-0.5)
    col_prob = jax.nn.softmax(jnp.where(same, col_score, -1e30), axis=-1)
    col_prob_low = col_prob.astype(BF16)
    col_mixed = (
        jnp.einsum("ghqk,gkhe->gqhe", col_prob_low, col_value, preferred_element_type=F32)
        .astype(BF16)
        .reshape(here, D)
    )
    after_col = after_row + nn(col_mixed, out_col)

    unit_2, rstd_2 = norm_stats(after_col)
    feed_normed = (unit_2 * norms[2] + norms[6]).astype(BF16)
    hidden_up = nn(feed_normed, up_w)
    active, slope = gelu_parts(hidden_up)
    active = active.astype(BF16)
    after_feed = after_col + nt(active, down_t)
    unit_3, rstd_3 = norm_stats(after_feed)
    head_normed = (unit_3 * norms[3] + norms[7]).astype(BF16)
    logits = nt(table, head_normed) * D ** (-0.5)
    logits = jnp.where(vocab < VOCAB, logits, -1e30)
    top = jnp.max(logits, 0, keepdims=True)
    shifted = logits - top
    log_probs = shifted - jnp.log(jnp.sum(jnp.exp(shifted), 0, keepdims=True))
    target_hot = (targets_ir[None, :] == vocab).astype(F32)
    keep = ids_ir[None, :] == MASK_ID
    mlm_sum = -jnp.sum(jnp.where(keep & (target_hot > 0), log_probs, 0.0))
    logit_grad = jnp.where(keep, jnp.exp(log_probs) - target_hot, 0.0) / counts[0]
    logit_low = (logit_grad * D ** (-0.5)).astype(BF16)

    grad_head = nn(logit_low, head_normed)
    stream, scale_3, shift_3 = norm_back(unit_3, rstd_3, norms[3], tn(logit_low, table))
    branch = stream.astype(BF16)
    grad_down = tn(branch, active)
    up_low = (nn(branch, down_t) * slope).astype(BF16)
    grad_up = tn(feed_normed, up_low)
    inner, scale_2, shift_2 = norm_back(unit_2, rstd_2, norms[2], nt(up_low, up_w))
    stream = stream + inner
    branch = stream.astype(BF16)
    grad_out_col = tn(col_mixed, branch)
    mixed_low = nt(branch, out_col).astype(BF16)
    mixed_cut = cut(mixed_low)
    prob_grad = jnp.einsum("gqhe,gkhe->ghqk", mixed_cut, col_value, preferred_element_type=F32)
    score_grad = col_prob * (prob_grad - jnp.sum(col_prob * prob_grad, -1, keepdims=True))
    score_low = score_grad.astype(BF16)
    grad_q = jnp.einsum("ghqk,gkhe->gqhe", score_low, col_key, preferred_element_type=F32)
    grad_k = jnp.einsum("ghqk,gqhe->gkhe", score_low, col_query, preferred_element_type=F32)
    grad_v = jnp.einsum("ghqk,gqhe->gkhe", col_prob_low, mixed_cut, preferred_element_type=F32)
    proj_low = jnp.concatenate(
        [
            (grad_q * HD ** (-0.5)).reshape(here, D),
            (grad_k * HD ** (-0.5)).reshape(here, D),
            grad_v.reshape(here, D),
        ],
        -1,
    ).astype(BF16)
    grad_in_col = tn(col_normed, proj_low)
    inner, scale_1, shift_1 = norm_back(unit_1, rstd_1, norms[1], nt(proj_low, in_col))
    stream = stream + inner
    branch = stream.astype(BF16)
    grad_out_row = tn(row_mixed, branch)
    mixed_low = nt(branch, out_row).astype(BF16)
    mixed_ri = tn(perm, mixed_low).astype(BF16)
    drive_hi, drive_lo = split_two(per_head(mixed_ri, value_t, nt))
    prob_grad = nn(to_heads(drive_hi), hot_all) + nn(to_heads(drive_lo), hot_all)
    prob_grad = prob_grad + (
        touch[None] * (contact_head[:HEADS, None, None] * cols)
    ).reshape(HEADS * cw, cols)
    score_grad = prob * (prob_grad - jnp.sum(prob * prob_grad, -1, keepdims=True))
    score_low = score_grad.astype(BF16)
    spread = to_tokens(nt(score_low, hot_all)).astype(BF16)
    table_pair = nn(hot_ri, spread)
    value_grad = per_head(weight_hi, mixed_ri, tn)
    stream_hi, stream_lo = split_two(stream)
    lookup_grad = nn(hot_ir, stream_hi) + nn(hot_ir, stream_lo)
    vectors = jnp.stack([scale_1, scale_2, scale_3, shift_1, shift_2, shift_3])
    return (
        (grad_in_col, grad_out_row, grad_out_col, grad_up, grad_down),
        (table_pair, value_grad, grad_head + lookup_grad, vectors),
        grad_contact,
        mlm_sum,
        bce_sum,
        (unit_t, rstd_t, normed_t, query_t, key_t),
    )


MESH = pl.DeviceIdType.MESH
NZ, NY = 4, 2


def place():
    s, c = lax.axis_index("seq"), lax.axis_index("col")
    z, y, k = s // 4, lax.rem(s // 2, 2), lax.rem(s, 2)
    return z, y, k, c


def device(z, y, k, c):
    return (z * 4 + y * 2 + k, c)


def greet_all():
    z, y, k, c = place()
    me = (z * 4 + y * 2 + k) * 2 + c
    barrier = pltpu.get_barrier_semaphore()

    def signal(step, carry):
        other = lax.rem(me + step, 32)
        pl.semaphore_signal(
            barrier, inc=1, device_id=(other // 2, lax.rem(other, 2)), device_id_type=MESH
        )
        return carry

    lax.fori_loop(1, 32, signal, 0)
    return barrier


def remote(src, dst, send, recv, target):
    return pltpu.make_async_remote_copy(
        src_ref=src, dst_ref=dst, send_sem=send, recv_sem=recv, device_id=target, device_id_type=MESH
    )


def gather_kernel(widths, *refs):
    count = len(widths)
    small = refs[0]
    masters = refs[1 : 1 + count]
    small_out = refs[1 + count]
    outs = refs[2 + count : 2 + 2 * count]
    at = 2 + 2 * count
    outgoing = refs[at : at + count]
    incoming = refs[at + count : at + 2 * count]
    piece = refs[at + 2 * count : at + 3 * count]
    small_send, small_recv, send, recv, local = refs[at + 3 * count :]
    z, y, k, c = place()
    me = (z * 4 + y * 2 + k) * 2 + c
    barrier = greet_all()
    for m in range(count):
        n = widths[m]
        left, right = masters[m][:, :n], masters[m][:, n:]
        other = jnp.where(c == 0, right, left)
        outgoing[m][...] = jnp.concatenate([other, jnp.zeros((8, n), F32)], 0).astype(BF16)
    pl.semaphore_wait(barrier, 31)

    def small_copy(step):
        other = lax.rem(me + step, 32)
        return remote(
            small, small_out.at[me], small_send.at[step], small_recv.at[step], (other // 2, lax.rem(other, 2))
        )

    def spread(step, carry):
        small_copy(step).start()
        return carry

    across, beside, twin = device(z, y, k, 1 - c), device(z, 1 - y, k, c), device(z, y, 1 - k, c)

    def copy(m, at, src, dst, target):
        return remote(src, dst, send.at[m, at], recv.at[m, at], target)

    def pair_copy(m):
        return copy(m, 0, outgoing[m], incoming[m], across)

    def own_copy(m):
        return pltpu.make_async_copy(piece[m], outs[m].at[c, z, y, k], local.at[m])

    def line_copy(m, step):
        return copy(m, step, piece[m], outs[m].at[c, z, y, k], device(lax.rem(z + step, 4), y, k, c))

    def same(m, at, where, target):
        view = outs[m].at[where]
        return copy(m, at, view, view, target)

    low, high = pl.ds(0, 2), pl.ds(2, 2)

    def second(m):
        return [same(m, 4, (c, low, y, k), across), same(m, 5, (c, high, y, k), beside)]

    def third_own(m):
        return [same(m, 6, (c, low, y, k), beside), same(m, 7, (c, high, y, k), across)]

    def third_far(m):
        return [same(m, 8, (1 - c, low, y, k), beside), same(m, 9, (c, high, 1 - y, k), across)]

    def twin_own(m):
        return [same(m, 10, (c, slice(None), y, k), twin)]

    def twin_second(m):
        return [same(m, 11, (1 - c, low, y, k), twin), same(m, 12, (c, high, 1 - y, k), twin)]

    def twin_third(m):
        return [
            same(m, 13, (c, low, 1 - y, k), twin),
            same(m, 14, (1 - c, high, y, k), twin),
            same(m, 15, (1 - c, low, 1 - y, k), twin),
            same(m, 16, (1 - c, high, 1 - y, k), twin),
        ]

    for m in range(count):
        pair_copy(m).start()
    lax.fori_loop(1, 32, spread, 0)
    small_out[me] = small[...]

    def stage_line(m):
        n = widths[m]
        pair_copy(m).wait_recv()
        mine = jnp.where(c == 0, masters[m][:, :n], masters[m][:, n:])
        theirs = incoming[m][...].astype(F32)[:24]
        top = jnp.where(c == 0, mine, theirs)
        bottom = jnp.where(c == 0, theirs, mine)
        piece[m][...] = jnp.concatenate([top, bottom], 0).astype(BF16)
        own_copy(m).start()
        for step in (1, 3, 2):
            line_copy(m, step).start()

    def stage_second(m):
        own_copy(m).wait()
        for step in (1, 3, 2):
            line_copy(m, step).wait_recv()
        for item in second(m) + third_own(m) + twin_own(m):
            item.start()

    def stage_third(m):
        for item in second(m):
            item.wait_recv()
        for item in third_far(m) + twin_second(m):
            item.start()

    def stage_twin(m):
        for item in third_own(m) + third_far(m):
            item.wait_recv()
        for item in twin_third(m):
            item.start()

    def stage_end(m):
        for item in twin_own(m) + twin_second(m) + twin_third(m):
            item.wait_recv()

    stages = (stage_line, stage_second, stage_third, stage_twin, stage_end)
    for tick in range(count + len(stages) - 1):
        for number, stage in enumerate(stages):
            if 0 <= tick - number < count:
                stage(tick - number)
    for m in range(count):
        pair_copy(m).wait_send()
        for step in (1, 2, 3):
            line_copy(m, step).wait_send()
        for item in second(m) + third_own(m) + third_far(m) + twin_own(m) + twin_second(m) + twin_third(m):
            item.wait_send()

    def finish(step, carry):
        small_copy(step).wait()
        return carry

    lax.fori_loop(1, 32, finish, 0)


def gather_all(small, masters):
    widths = tuple(m.shape[1] // 2 for m in masters)
    count = len(widths)
    anywhere = pl.BlockSpec(memory_space=pl.ANY)
    inside = pl.BlockSpec(memory_space=pltpu.VMEM)
    outs = pl.pallas_call(
        functools.partial(gather_kernel, widths),
        out_shape=[jax.ShapeDtypeStruct((32, *small.shape), small.dtype)]
        + [jax.ShapeDtypeStruct((2, NZ, NY, 2, 48, n), BF16) for n in widths],
        in_specs=[inside] * (1 + count),
        out_specs=[inside] + [anywhere] * count,
        scratch_shapes=[pltpu.VMEM((32, n), BF16) for n in widths] * 2
        + [pltpu.VMEM((48, n), BF16) for n in widths]
        + [
            pltpu.SemaphoreType.DMA((32,)),
            pltpu.SemaphoreType.DMA((32,)),
            pltpu.SemaphoreType.DMA((count, 17)),
            pltpu.SemaphoreType.DMA((count, 17)),
            pltpu.SemaphoreType.DMA((count,)),
        ],
        compiler_params=pltpu.CompilerParams(
            collective_id=0, has_side_effects=True, vmem_limit_bytes=48 * 2**20
        ),
    )(small, *masters)
    return outs[0], outs[1:]


def scatter_kernel(widths, *refs):
    count = len(widths)
    table, lookup, norms, proj_t, extras, in_row_far = refs[:6]
    grads = refs[6 : 6 + count]
    outs = refs[6 + count : 6 + 2 * count]
    g_in, g_emb, g_norm, stats = refs[6 + 2 * count : 10 + 2 * count]
    scratch = refs[10 + 2 * count :]
    acc, got_0, got_1a, got_1b, got_2a, got_2b, got_3, total, got_4 = (
        scratch[i * count : (i + 1) * count] for i in range(9)
    )
    table_out, table_got, in_row, square, square_got = scratch[9 * count : 9 * count + 5]
    table_send, table_recv, send, recv, local = scratch[9 * count + 5 :]
    z, y, k, c = place()
    me = (z * 4 + y * 2 + k) * 2 + c
    across, beside, twin = device(z, y, k, 1 - c), device(z, 1 - y, k, c), device(z, y, 1 - k, c)
    barrier = greet_all()

    def own_copy(m):
        return pltpu.make_async_copy(grads[m].at[:, :, :, k], acc[m], local.at[m])

    for m in range(count):
        own_copy(m).start()
    in_row_copy = pltpu.make_async_copy(in_row_far, in_row, local.at[count])
    in_row_copy.start()
    pl.semaphore_wait(barrier, 31)

    def copy(m, at, src, dst, target):
        return remote(src, dst, send.at[m, at], recv.at[m, at], target)

    def twin_copy(m):
        return copy(m, 0, grads[m].at[:, :, :, 1 - k], got_0[m], twin)

    low, high = pl.ds(0, 2), pl.ds(2, 2)

    def first(m):
        return [
            copy(m, 1, acc[m].at[:, low, 1 - y], got_1a[m], beside),
            copy(m, 2, acc[m].at[1 - c, high], got_1b[m], across),
        ]

    def second(m):
        return [
            copy(m, 3, acc[m].at[1 - c, low, y], got_2a[m], across),
            copy(m, 4, acc[m].at[c, high, 1 - y], got_2b[m], beside),
        ]

    def line(m):
        return [
            copy(m, 4 + step, acc[m].at[c, lax.rem(z + step, 4), y], got_3[m].at[step - 1], device(lax.rem(z + step, 4), y, k, c))
            for step in (1, 2, 3)
        ]

    def pair(m):
        return [copy(m, 8, total[m].at[1 - c], got_4[m], across)]

    def table_copy(step, back):
        other = lax.rem(me + step, 32)
        target = (other // 2, lax.rem(other, 2))
        if back:
            return remote(
                table_out.at[me], table_out.at[me], table_send.at[1, step], table_recv.at[1, step], target
            )
        return remote(
            table.at[other], table_got.at[me], table_send.at[0, step], table_recv.at[0, step], target
        )

    def each(action):
        def body(step, carry):
            action(step)
            return carry

        lax.fori_loop(1, 32, body, 0)

    def plus(left, right):
        return (left.astype(F32) + right.astype(F32)).astype(BF16)

    for m in range(count):
        twin_copy(m).start()
    each(lambda step: table_copy(step, False).start())

    def stage_first(m):
        own_copy(m).wait()
        twin_copy(m).wait_recv()

        def body(at, carry):
            zz = at // 2
            yy = lax.rem(at, 2)
            for cc in range(2):
                acc[m][cc, zz, yy] = plus(acc[m][cc, zz, yy], got_0[m][cc, zz, yy])
            return carry

        lax.fori_loop(0, NZ * NY, body, 0)
        for item in first(m):
            item.start()

    def stage_second(m):
        for item in first(m):
            item.wait_recv()
        for a in range(2):
            for b in range(2):
                acc[m][a, b, y] = plus(acc[m][a, b, y], got_1a[m][a, b])
                acc[m][c, 2 + a, b] = plus(acc[m][c, 2 + a, b], got_1b[m][a, b])
        for item in second(m):
            item.start()

    def stage_line(m):
        for item in second(m):
            item.wait_recv()
        for a in range(2):
            acc[m][c, a, y] = plus(acc[m][c, a, y], got_2a[m][a])
            acc[m][c, 2 + a, y] = plus(acc[m][c, 2 + a, y], got_2b[m][a])
        for item in line(m):
            item.start()

    def stage_pair(m):
        for item in line(m):
            item.wait_recv()
        full = acc[m][c, z, y].astype(F32)
        for step in range(3):
            full = full + got_3[m][step].astype(F32)
        total[m][0] = full[:24]
        total[m][1] = full[24:]
        for item in pair(m):
            item.start()

    def stage_end(m):
        outs[m][c] = total[m][c]
        for item in pair(m):
            item.wait_recv()
        outs[m][1 - c] = got_4[m][...]

    def table_sum():
        table_got[me] = table[me]
        each(lambda step: table_copy(step, False).wait_recv())

        def body(at, held):
            return held + table_got[at]

        table_out[me] = lax.fori_loop(1, 32, body, table_got[0])
        each(lambda step: table_copy(step, True).start())

    stages = (stage_first, stage_second, stage_line, stage_pair, stage_end)
    for tick in range(count + len(stages) - 1):
        for number, stage in enumerate(stages):
            if 0 <= tick - number < count:
                stage(tick - number)
        if tick == 1:
            table_sum()
        if tick == count:
            each(lambda step: table_copy(step, True).wait_recv())
            in_row_copy.wait()
            local_square = table_finish(table_out, lookup, norms, proj_t, in_row, g_in, g_emb, g_norm)
    for m in range(count):
        for half in range(2):
            local_square = local_square + total_of(outs[m][half] * outs[m][half])

    def square_copy(step):
        other = lax.rem(me + step, 32)
        return remote(
            square, square_got.at[me], table_send.at[2, step], table_recv.at[2, step], (other // 2, lax.rem(other, 2))
        )

    square[...] = jnp.broadcast_to(local_square, (8, 128))
    each(lambda step: square_copy(step).start())
    square_got[me] = square[...]
    each(lambda step: square_copy(step).wait())
    total_square = lax.fori_loop(1, 32, lambda at, held: held + square_got[at], square_got[0])[0:1]
    vector = table_out[30, 6:7, :128]
    counted = extras[1:2, :]
    column = iota((1, 128), 1)
    contact = jnp.where(column <= HEADS, vector, 0.0)
    total_square = total_square + total_of(contact * contact)
    grad_norm = jnp.sqrt(total_square)
    factor = jnp.minimum(1.0, MAX_NORM / grad_norm)
    losses = (
        (0, vector[:, HEADS + 1 : HEADS + 2]),
        (1, counted[:, 0:1]),
        (2, vector[:, HEADS + 2 : HEADS + 3]),
        (3, counted[:, 1:2]),
    )
    loss_row = jnp.zeros((1, 128), F32)
    for at, value in losses:
        loss_row = jnp.where(column == at, value, loss_row)
    number = iota((8, 128), 0)
    result = jnp.zeros((8, 128), F32)
    for at, row in enumerate((contact, counted, factor, grad_norm, loss_row)):
        result = jnp.where(number == at, row, result)
    stats[...] = result
    each(lambda step: table_copy(step, True).wait_send())
    each(lambda step: table_copy(step, False).wait_send())
    for m in range(count):
        for item in [twin_copy(m)] + first(m) + second(m) + line(m) + pair(m):
            item.wait_send()


def scatter_all(table, lookup, norms, proj_t, extras, in_row, grads):
    widths = tuple(g.shape[-1] for g in grads)
    count = len(widths)
    anywhere = pl.BlockSpec(memory_space=pl.ANY)
    inside = pl.BlockSpec(memory_space=pltpu.VMEM)

    def shapes(lead, dtype):
        return [pltpu.VMEM((*lead, n), dtype) for n in widths]

    outs = pl.pallas_call(
        functools.partial(scatter_kernel, widths),
        out_shape=[jax.ShapeDtypeStruct((2, 24, n), F32) for n in widths]
        + [
            jax.ShapeDtypeStruct((24, 3 * D), F32),
            jax.ShapeDtypeStruct((24, VP), F32),
            jax.ShapeDtypeStruct((8, 24), F32),
            jax.ShapeDtypeStruct((8, 128), F32),
        ],
        in_specs=[inside] * 5 + [anywhere] * (1 + count),
        out_specs=[inside] * (4 + count),
        scratch_shapes=shapes((2, NZ, NY, 48), BF16)
        + shapes((2, NZ, NY, 48), BF16)
        + shapes((2, 2, 48), BF16)
        + shapes((2, 2, 48), BF16)
        + shapes((2, 48), BF16)
        + shapes((2, 48), BF16)
        + shapes((3, 48), BF16)
        + shapes((2, 24), F32)
        + shapes((24,), F32)
        + [
            pltpu.VMEM(table.shape, F32),
            pltpu.VMEM(table.shape, F32),
            pltpu.VMEM(in_row.shape, BF16),
            pltpu.VMEM((8, 128), F32),
            pltpu.VMEM((32, 8, 128), F32),
            pltpu.SemaphoreType.DMA((3, 32)),
            pltpu.SemaphoreType.DMA((3, 32)),
            pltpu.SemaphoreType.DMA((count, 9)),
            pltpu.SemaphoreType.DMA((count, 9)),
            pltpu.SemaphoreType.DMA((count + 1,)),
        ],
        compiler_params=pltpu.CompilerParams(
            collective_id=1, has_side_effects=True, vmem_limit_bytes=56 * 2**20
        ),
    )(table, lookup, norms, proj_t, extras, in_row, *grads)
    return outs[:count], outs[count:]


ROWS, COLS, WIDE, HERE = 16, 512, 32, 512
PAIRS = 6
SLOTS = 1024
UP_TILE = 384


def iota(shape, dim):
    return lax.broadcasted_iota(jnp.int32, shape, dim)


def one_zero(test):
    return jnp.where(test, 1.0, 0.0)


def total_of(values):
    return jnp.sum(jnp.sum(values, 0, keepdims=True), 1, keepdims=True)


def half_lanes(values, side):
    lane = iota(values.shape, len(values.shape) - 1)
    keep = (lane < 64) if side == 0 else (lane >= 64)
    return jnp.where(keep, values.astype(F32), 0.0).astype(BF16)


def stacked(values):
    return jnp.concatenate([half_lanes(values, 0), half_lanes(values, 1)], 0)


def unstacked(values, count):
    lane = iota((count, 128), 1)
    return jnp.where(lane < 64, values[:count], values[count:])


def swap_blocks(first, second):
    lane = iota(first.shape, 1)
    low = jnp.where(lane < 64, first, pltpu.roll(second, 64, 1))
    high = jnp.where(lane < 64, pltpu.roll(first, 64, 1), second)
    return low, high


def split_heads_to(source, high_ref, low_ref):
    for rp in range(ROWS // 2):
        for hp in range(PAIRS):
            lanes = slice(hp * 128, hp * 128 + 128)
            first = source[rp * 64 : rp * 64 + 32, lanes]
            second = source[rp * 64 + 32 : rp * 64 + 64, lanes]
            for side, block in enumerate(swap_blocks(first, second)):
                top, rest = split_two(block)
                rows = slice((2 * hp + side) * 32, (2 * hp + side) * 32 + 32)
                high_ref[rows, rp * 128 : rp * 128 + 128] = top
                low_ref[rows, rp * 128 : rp * 128 + 128] = rest


def merge_heads(probs, hot_all, high_ref, low_ref):
    for rp in range(ROWS // 2):
        block = nt(probs, hot_all[rp * 128 : rp * 128 + 128, :])
        for hp in range(PAIRS):
            first = block[hp * 64 : hp * 64 + 32]
            second = block[hp * 64 + 32 : hp * 64 + 64]
            for side, part in enumerate(swap_blocks(first, second)):
                top, rest = split_two(part)
                rows = slice(rp * 64 + side * 32, rp * 64 + side * 32 + 32)
                high_ref[rows, hp * 128 : hp * 128 + 128] = top
                if low_ref is not None:
                    low_ref[rows, hp * 128 : hp * 128 + 128] = rest


def norm_rows(source, gain, bias, unit_ref, rstd_ref, normed_ref):
    def body(at, carry):
        rows = pl.ds(pl.multiple_of(at * 32, 32), 32)
        values = source[rows, :]
        centre = values - jnp.sum(values, -1, keepdims=True) * (1.0 / D)
        rstd = lax.rsqrt(jnp.sum(centre * centre, -1, keepdims=True) * (1.0 / D) + NORM_EPS)
        unit = centre * rstd
        unit_ref[rows, :] = unit
        rstd_ref[rows, :] = jnp.broadcast_to(rstd, (32, 128))
        normed_ref[rows, :] = (unit * gain + bias).astype(BF16)
        return carry

    lax.fori_loop(0, HERE // 32, body, 0)


def transpose_into(source, target):
    def body(at, carry):
        rows = pl.ds(pl.multiple_of(at * 128, 128), 128)
        target[:, rows] = source[rows, :].astype(F32).T.astype(BF16)
        return carry

    lax.fori_loop(0, HERE // 128, body, 0)


def over_tiles(width, tile, body):
    for half in range(2):

        def step(at, carry, half=half):
            body(half, pl.multiple_of(at * tile, tile))
            return carry

        lax.fori_loop(0, width // tile, step, 0)


def column_mask():
    rows, lanes = iota((256, 128), 0), iota((256, 128), 1)
    return ((rows & 127) >> 4) == (lanes >> 4)


SAVED = (
    ("unit_1", (HERE, D), F32),
    ("unit_2", (HERE, D), F32),
    ("unit_3", (HERE, D), F32),
    ("rstd_1", (HERE, 128), F32),
    ("rstd_2", (HERE, 128), F32),
    ("rstd_3", (HERE, 128), F32),
    ("row_mixed_t", (D, HERE), BF16),
    ("col_normed_t", (D, HERE), BF16),
    ("col_mixed_t", (D, HERE), BF16),
    ("feed_normed_t", (D, HERE), BF16),
    ("col_proj", (HERE, 3 * D), BF16),
    ("col_prob", (4 * PAIRS, 256, 128), F32),
    ("active", (HERE, FF), BF16),
    ("slope", (HERE, FF), BF16),
    ("logit_low", (VP, HERE), BF16),
    ("grad_head", (VP, D), F32),
    ("hot_all", (ROWS * VP, COLS), BF16),
    ("hot_ri", (VP, HERE), BF16),
    ("hot_ir", (VP, HERE), BF16),
    ("prob", (HEADS * WIDE, COLS), F32),
    ("weight_hi", (HERE, D), BF16),
    ("value_two", (PAIRS, 128, 128), BF16),
    ("touch", (WIDE, COLS), F32),
    ("table", (VP, D), F32),
    ("norms", (8, D), F32),
    ("proj_t", (VP, 3 * D), BF16),
    ("extras", (8, 128), F32),
)
FORWARD_SCRATCH = (
    ("ids", (ROWS, COLS), jnp.int32),
    ("targets", (ROWS, 128), jnp.int32),
    ("slots", (8, SLOTS), jnp.int32),
    ("stream", (HERE, D), F32),
    ("normed", (HERE, D), BF16),
    ("mixed", (HERE, D), BF16),
    ("weight_lo", (HERE, D), BF16),
    ("left_hi", (HEADS * WIDE, ROWS * VP), BF16),
    ("left_lo", (HEADS * WIDE, ROWS * VP), BF16),
    ("lookup", (HERE, D), F32),
    ("prob_low", (HEADS * WIDE, COLS), BF16),
)


class Named:
    def __init__(self, names, refs):
        for (name, _, _), ref in zip(names, refs):
            setattr(self, name, ref)


def position():
    z, y, k, c = place()
    me = (z * 4 + y * 2 + k) * 2 + c
    return z // 2, lax.rem(me, 16)


def read_tokens(small, f):
    alignment, block = position()
    side, part = block // 8, lax.rem(block // 4, 2)
    for r in range(ROWS):
        for cc in range(2):
            for q in range(2):
                lanes = slice(cc * 256 + q * 128, cc * 256 + q * 128 + 128)
                f.ids[r : r + 1, lanes] = small[r * 2 + cc, pl.ds(2 * alignment + q, 1), :]
        f.targets[r : r + 1, :] = small[r * 2 + side, pl.ds(4 + 2 * alignment + part, 1), :]
    lane = iota((1, 128), 1)
    turn = alignment * 64
    for number in range(SLOTS // 128):
        for which in range(3):
            first = small[number * 4 + side, 8 + which : 9 + which, :]
            second = small[number * 4 + 2 + side, 8 + which : 9 + which, :]
            first = pltpu.roll(first, lax.rem(128 - turn, 128), 1)
            second = pltpu.roll(second, 64 - turn, 1)
            f.slots[which : which + 1, number * 128 : number * 128 + 128] = jnp.where(
                lane < 64, first, second
            )


def local_hot(values, shift):
    values = pltpu.roll(values, shift, 1)
    turned = [values] + [pltpu.roll(values, 32 * n, 1) for n in (1, 2, 3)]
    lane = iota((1, 128), 1)
    tiles = []
    for tile in range(4):
        row = turned[3][4 * tile + 3 : 4 * tile + 4]
        for n in (2, 1, 0):
            row = jnp.where(lane < 32 * n + 32, turned[n][4 * tile + n : 4 * tile + n + 1], row)
        tiles.append(row)
    row = jnp.concatenate(tiles, 1)
    return one_zero(row == iota((VP, HERE), 0)).astype(BF16)


def contact_part(contact_head, f, s, pair_count):
    _, block = position()
    base = block * WIDE
    head_sum = jnp.zeros((WIDE, COLS), F32)
    for h in range(HEADS):
        head_sum = head_sum + contact_head[h] * f.prob_low[h * 32 : h * 32 + 32, :].astype(F32)
    top, rest = split_two(head_sum)
    last = (head_sum - top.astype(F32) - rest.astype(F32)).astype(BF16)
    parts = jnp.concatenate([top, rest, last], 0)
    touch = jnp.zeros((WIDE, COLS), F32)
    bce = jnp.zeros((1, 1), F32)
    coef_sum = jnp.zeros((1, 1), F32)
    for number in range(SLOTS // 512):
        lanes = slice(number * 512, number * 512 + 512)
        first, second, label = (f.slots[n : n + 1, lanes] for n in range(3))
        second_hot = one_zero(second == iota((COLS, 512), 0)).astype(BF16)
        picked = nn(parts, second_hot)
        picked = picked[:32] + picked[32:64] + picked[64:]
        first_hot = one_zero((first - base) == iota((WIDE, 512), 0))
        logit = jnp.sum(picked * first_hot, 0, keepdims=True) * COLS + contact_head[HEADS]
        owned = jnp.sum(first_hot, 0, keepdims=True) > 0.5
        valid = (label >= 0) & owned
        positive = one_zero(label == 1)
        small = jnp.exp(-jnp.abs(logit))
        soft = jnp.maximum(logit, 0.0) + jnp.log(1.0 + small)
        bce = bce + total_of(jnp.where(valid, soft - positive * logit, 0.0))
        sigmoid = jnp.where(logit >= 0.0, 1.0, small) / (1.0 + small)
        coef = jnp.where(valid, sigmoid - positive, 0.0) / pair_count
        coef_sum = coef_sum + total_of(coef)
        coef_top, coef_rest = split_two(first_hot * coef)
        touch = touch + nt(coef_top, second_hot) + nt(coef_rest, second_hot)
    s.touch[...] = touch
    column = iota((1, 128), 1)
    row = jnp.where(column == HEADS, coef_sum, 0.0)
    for h in range(HEADS):
        part = total_of(touch * f.prob_low[h * 32 : h * 32 + 32, :].astype(F32)) * COLS
        row = row + jnp.where(column == h, part, 0.0)
    return row, bce


def forward_body(small, contact_head, weights, s, f, ready, emit):
    emb, in_row, out_row, in_col, out_col, up_w, down_t = weights
    ready(-1)
    read_tokens(small, f)
    _, block = position()
    shift = lax.rem(128 - lax.rem(block, 4) * 32, 128)
    window = pl.ds(pl.multiple_of((block // 4) * 128, 128), 128)
    hot_ri = local_hot(f.ids[:, window], shift)
    goal_ri = local_hot(f.targets[...], shift)
    s.hot_ri[...] = hot_ri
    for r in range(ROWS):
        row = f.ids[r : r + 1, :]
        s.hot_all[r * VP : r * VP + VP, :] = one_zero(row == iota((VP, COLS), 0)).astype(BF16)
    shape = (HERE, HERE)
    back = (
        ((iota(shape, 1) >> 4) == (iota(shape, 0) & 31))
        & ((iota(shape, 1) & 15) == (iota(shape, 0) >> 5))
    )
    back = one_zero(back).astype(BF16)
    hot_ir = nn(hot_ri, back).astype(BF16)
    s.hot_ir[...] = hot_ir
    goal = nn(goal_ri, back)
    entries = jnp.zeros((4, 128), F32)
    labelled = jnp.zeros((1, 128), F32)
    for d in range(32):
        entries = entries + one_zero(small[d, 0:4, :] == MASK_ID)
        labelled = labelled + one_zero(small[d, 10:11, :] >= 0)
    entries, labelled = total_of(entries), total_of(labelled)

    ready(0)
    table = emb[0].astype(F32).T[:VP]
    norms = emb[1].astype(F32).T[:8]
    s.table[...] = table
    s.norms[...] = norms
    table_low = table.astype(BF16)

    def vector(number):
        return norms[number : number + 1, :]

    unit_t, _ = norm_stats(table)
    normed_t = (unit_t * vector(0) + vector(4)).astype(BF16)
    ready(1)
    for half in range(2):
        s.proj_t[:, half * 1152 : half * 1152 + 1152] = nn(normed_t, in_row[half]).astype(BF16)
    pair_parts = []
    for hp in range(PAIRS):
        lanes = slice(hp * 128, hp * 128 + 128)
        key = s.proj_t[:, D + hp * 128 : D + hp * 128 + 128]
        value = s.proj_t[:, 2 * D + hp * 128 : 2 * D + hp * 128 + 128]
        s.value_two[hp] = stacked(value)
        pair_parts.append(nt(s.proj_t[:, lanes], stacked(key)))
    pair_hi, pair_lo = split_two(jnp.concatenate(pair_parts, 1))
    f.lookup[...] = tn(hot_ri, pair_hi) + tn(hot_ri, pair_lo)
    split_heads_to(f.lookup, f.left_hi, f.left_lo)
    hot_all = s.hot_all[...]
    score = (nn(f.left_hi[...], hot_all) + nn(f.left_lo[...], hot_all)) * (HD * ROWS) ** (-0.5)
    score = jnp.exp(score - jnp.max(score, -1, keepdims=True))
    prob = score / jnp.sum(score, -1, keepdims=True)
    s.prob[...] = prob
    f.prob_low[...] = prob.astype(BF16)
    merge_heads(f.prob_low[...], s.hot_all, s.weight_hi, f.weight_lo)
    for hp in range(PAIRS):
        lanes = slice(hp * 128, hp * 128 + 128)
        value = s.value_two[hp]
        f.mixed[:, lanes] = (nn(s.weight_hi[:, lanes], value) + nn(f.weight_lo[:, lanes], value)).astype(BF16)
    ahead = (
        ((iota(shape, 0) >> 4) == (iota(shape, 1) & 31))
        & ((iota(shape, 0) & 15) == (iota(shape, 1) >> 5))
    )
    f.mixed[...] = nn(one_zero(ahead).astype(BF16), f.mixed[...]).astype(BF16)
    transpose_into(f.mixed, s.row_mixed_t)
    f.stream[...] = tn(hot_ir, table_low)
    contact_row, bce = contact_part(contact_head, f, s, labelled)
    emit("hot_all", "hot_ri", "hot_ir", "table", "norms", "proj_t", "value_two", "prob", "weight_hi", "row_mixed_t", "touch")

    ready(2)
    for half in range(2):
        lanes = slice(half * 384, half * 384 + 384)
        f.stream[:, lanes] += nn(f.mixed[...], out_row[half])
    norm_rows(f.stream, vector(1), vector(5), s.unit_1, s.rstd_1, f.normed)
    transpose_into(f.normed, s.col_normed_t)
    emit("unit_1", "rstd_1", "col_normed_t")
    ready(3)

    def project(half, at):
        s.col_proj[:, pl.ds(pl.multiple_of(half * 1152 + at, 128), 384)] = nn(
            f.normed[...], in_col[half, :, pl.ds(at, 384)]
        ).astype(BF16)

    over_tiles(1152, 384, project)
    emit("col_proj")

    def attend(at, carry):
        rows = pl.ds(pl.multiple_of((at // PAIRS) * 128, 128), 128)
        lane = lax.rem(at, PAIRS) * 128

        def lanes(part):
            return pl.ds(pl.multiple_of(part * D + lane, 128), 128)

        query = stacked(s.col_proj[rows, lanes(0)])
        score = nt(query, s.col_proj[rows, lanes(1)]) * HD ** (-0.5)
        score = jnp.where(column_mask(), score, -1e30)
        score = jnp.exp(score - jnp.max(score, -1, keepdims=True))
        prob = score / jnp.sum(score, -1, keepdims=True)
        s.col_prob[at] = prob
        mixed = nn(prob.astype(BF16), s.col_proj[rows, lanes(2)])
        f.mixed[rows, lanes(0)] = unstacked(mixed, 128).astype(BF16)
        return carry

    lax.fori_loop(0, 4 * PAIRS, attend, 0, unroll=2)
    transpose_into(f.mixed, s.col_mixed_t)
    emit("col_prob", "col_mixed_t")
    ready(4)
    for half in range(2):
        lanes = slice(half * 384, half * 384 + 384)
        f.stream[:, lanes] += nn(f.mixed[...], out_col[half])
    norm_rows(f.stream, vector(2), vector(6), s.unit_2, s.rstd_2, f.normed)
    transpose_into(f.normed, s.feed_normed_t)
    emit("unit_2", "rstd_2", "feed_normed_t")
    ready(5)

    def widen(half, at):
        lanes = pl.ds(pl.multiple_of(half * 1536 + at, 128), UP_TILE)
        up = nn(f.normed[...], up_w[half, :, pl.ds(at, UP_TILE)])
        active, slope = gelu_parts(up)
        s.active[:, lanes] = active.astype(BF16)
        s.slope[:, lanes] = slope.astype(BF16)

    over_tiles(1536, UP_TILE, widen)
    emit("active", "slope")
    ready(6)

    def narrow(half, at):
        lanes = pl.ds(pl.multiple_of(half * 1536 + at, 128), 768)
        f.stream[...] += nt(s.active[:, lanes], down_t[half, :, pl.ds(at, 768)])

    over_tiles(1536, 768, narrow)
    norm_rows(f.stream, vector(3), vector(7), s.unit_3, s.rstd_3, f.normed)
    emit("unit_3", "rstd_3")
    logits = nt(table_low, f.normed[...]) * D ** (-0.5)
    vocab = iota((VP, HERE), 0)
    logits = jnp.where(vocab < VOCAB, logits, -1e30)
    shifted = logits - jnp.max(logits, 0, keepdims=True)
    log_probs = shifted - jnp.log(jnp.sum(jnp.exp(shifted), 0, keepdims=True))
    keep = hot_ir[MASK_ID : MASK_ID + 1].astype(F32) > 0.5
    mlm = -total_of(jnp.where(keep & (goal > 0.5), log_probs, 0.0))
    logit_grad = jnp.where(keep, jnp.exp(log_probs) - goal, 0.0) / entries
    logit_low = (logit_grad * D ** (-0.5)).astype(BF16)
    s.logit_low[...] = logit_low
    s.grad_head[...] = nn(logit_low, f.normed[...])
    column = iota((1, 128), 1)
    row = contact_row + jnp.where(column == HEADS + 1, mlm, 0.0) + jnp.where(column == HEADS + 2, bce, 0.0)
    counted = jnp.where(column == 0, entries, 0.0) + jnp.where(column == 1, labelled, 0.0)
    line = iota((8, 128), 0)
    s.extras[...] = jnp.where(line == 0, row, jnp.where(line == 1, counted, 0.0))
    emit("logit_low", "grad_head", "extras")


def back_rows(unit_ref, rstd_ref, gain, upstream_ref, stream_ref, low_ref, first):
    def body(at, carry):
        scale, move = carry
        rows = pl.ds(pl.multiple_of(at * 32, 32), 32)
        upstream = upstream_ref[rows, :]
        unit = unit_ref[rows, :]
        inner = upstream * gain
        mean = jnp.sum(inner, -1, keepdims=True) * (1.0 / D)
        along = jnp.sum(inner * unit, -1, keepdims=True) * (1.0 / D)
        grad = rstd_ref[rows, 0:1] * (inner - mean - unit * along)
        if not first:
            grad = grad + stream_ref[rows, :]
        stream_ref[rows, :] = grad
        low_ref[rows, :] = grad.astype(BF16)
        touched = upstream * unit
        for n in range(4):
            scale = scale + touched[n * 8 : n * 8 + 8]
            move = move + upstream[n * 8 : n * 8 + 8]
        return scale, move

    zero = jnp.zeros((8, D), F32)
    scale, move = lax.fori_loop(0, HERE // 32, body, (zero, zero))
    return jnp.sum(scale, 0, keepdims=True), jnp.sum(move, 0, keepdims=True)


BACKWARD_SCRATCH = (
    ("stream", (HERE, D), F32),
    ("upstream", (HERE, D), F32),
    ("branch", (HERE, D), BF16),
    ("branch_t", (D, HERE), BF16),
    ("mixed", (HERE, D), BF16),
    ("proj", (HERE, 3 * D), BF16),
    ("left_hi", (HEADS * WIDE, ROWS * VP), BF16),
    ("left_lo", (HEADS * WIDE, ROWS * VP), BF16),
)


def backward_body(contact_head, weights, s, b, grads, sums, need, done):
    out_row, in_col, out_col, up_w, down_t = weights
    g_down, g_up, g_out_col, g_in_col, g_out_row = grads
    need("norms", "table", "logit_low", "unit_3", "rstd_3")
    norms = s.norms[...]

    def gain(number):
        return norms[number : number + 1, :]

    table_low = s.table[...].astype(BF16)
    b.upstream[...] = tn(s.logit_low[...], table_low)
    scale_3, shift_3 = back_rows(s.unit_3, s.rstd_3, gain(3), b.upstream, b.stream, b.branch, True)
    transpose_into(b.branch, b.branch_t)

    def down_grad(half, at):
        lanes = pl.ds(pl.multiple_of(half * 1536 + at, 128), 384)
        g_down[half, :, pl.ds(at, 384)] = nn(b.branch_t[...], s.active[:, lanes]).astype(BF16)

    def down_back(half, at):
        lanes = pl.ds(pl.multiple_of(half * 1536 + at, 128), 384)
        back = nn(b.branch[...], down_t[half, :, pl.ds(at, 384)])
        s.slope[:, lanes] = (back * s.slope[:, lanes].astype(F32)).astype(BF16)

    need("slope", "down_t")
    over_tiles(1536, 384, down_back)
    need("active")
    over_tiles(1536, 384, down_grad)
    done(0)

    def up_grad(half, at):
        lanes = pl.ds(pl.multiple_of(half * 1536 + at, 128), 384)
        g_up[half, :, pl.ds(at, 384)] = nn(s.feed_normed_t[...], s.slope[:, lanes]).astype(BF16)

    b.upstream[...] = jnp.zeros((HERE, D), F32)

    def up_back(half, at):
        lanes = pl.ds(pl.multiple_of(half * 1536 + at, 128), 768)
        b.upstream[...] += nt(s.slope[:, lanes], up_w[half, :, pl.ds(at, 768)])

    need("up_w")
    over_tiles(1536, 768, up_back)
    need("feed_normed_t")
    over_tiles(1536, 384, up_grad)
    done(1)
    need("unit_2", "rstd_2")
    scale_2, shift_2 = back_rows(s.unit_2, s.rstd_2, gain(2), b.upstream, b.stream, b.branch, False)
    need("out_col", "col_mixed_t")
    first, second = slice(0, 384), slice(384, 768)
    b.mixed[...] = (
        nt(b.branch[:, first], out_col[0]) + nt(b.branch[:, second], out_col[1])
    ).astype(BF16)
    g_out_col[0] = nn(s.col_mixed_t[...], b.branch[:, first]).astype(BF16)
    g_out_col[1] = nn(s.col_mixed_t[...], b.branch[:, second]).astype(BF16)
    done(2)

    def attend(at, carry):
        rows = pl.ds(pl.multiple_of((at // PAIRS) * 128, 128), 128)
        lane = lax.rem(at, PAIRS) * 128

        def lanes(part):
            return pl.ds(pl.multiple_of(part * D + lane, 128), 128)

        query = stacked(s.col_proj[rows, lanes(0)])
        key = s.col_proj[rows, lanes(1)]
        value = s.col_proj[rows, lanes(2)]
        upstream = stacked(b.mixed[rows, lanes(0)])
        prob = s.col_prob[at]
        grad = nt(upstream, value)
        grad = prob * (grad - jnp.sum(prob * grad, -1, keepdims=True))
        low = grad.astype(BF16)
        scale = HD ** (-0.5)
        b.proj[rows, lanes(0)] = (unstacked(nn(low, key), 128) * scale).astype(BF16)
        b.proj[rows, lanes(1)] = (tn(low, query) * scale).astype(BF16)
        b.proj[rows, lanes(2)] = tn(prob.astype(BF16), upstream).astype(BF16)
        return carry

    need("col_proj", "col_prob")
    lax.fori_loop(0, 4 * PAIRS, attend, 0, unroll=2)
    need("in_col")
    for half in range(2):
        lanes = slice(half * 1152, half * 1152 + 1152)
        part = nt(b.proj[:, lanes], in_col[half])
        b.upstream[...] = part if half == 0 else b.upstream[...] + part

    def in_grad(half, at):
        lanes = pl.ds(pl.multiple_of(half * 1152 + at, 128), 384)
        g_in_col[half, :, pl.ds(at, 384)] = nn(s.col_normed_t[...], b.proj[:, lanes]).astype(BF16)

    need("col_normed_t")
    over_tiles(1152, 384, in_grad)
    done(3)
    need("unit_1", "rstd_1")
    scale_1, shift_1 = back_rows(s.unit_1, s.rstd_1, gain(1), b.upstream, b.stream, b.branch, False)
    need("out_row", "row_mixed_t")
    b.mixed[...] = (
        nt(b.branch[:, first], out_row[0]) + nt(b.branch[:, second], out_row[1])
    ).astype(BF16)
    g_out_row[0] = nn(s.row_mixed_t[...], b.branch[:, first]).astype(BF16)
    g_out_row[1] = nn(s.row_mixed_t[...], b.branch[:, second]).astype(BF16)
    done(4)
    shape = (HERE, HERE)
    back = (
        ((iota(shape, 1) >> 4) == (iota(shape, 0) & 31))
        & ((iota(shape, 1) & 15) == (iota(shape, 0) >> 5))
    )
    b.mixed[...] = nn(one_zero(back).astype(BF16), b.mixed[...]).astype(BF16)
    need("value_two", "weight_hi", "hot_all", "hot_ri", "hot_ir", "prob", "touch", "grad_head", "extras")
    value_rows = []
    for hp in range(PAIRS):
        lanes = slice(hp * 128, hp * 128 + 128)
        mixed = b.mixed[:, lanes]
        b.upstream[:, lanes] = nt(mixed, s.value_two[hp])
        value_rows.append(unstacked(tn(s.weight_hi[:, lanes], mixed), 64))
    split_heads_to(b.upstream, b.left_hi, b.left_lo)
    hot_all = s.hot_all[...]
    grad = nn(b.left_hi[...], hot_all) + nn(b.left_lo[...], hot_all)
    extra = jnp.concatenate([s.touch[...] * (contact_head[h] * COLS) for h in range(HEADS)], 0)
    grad = grad + extra
    prob = s.prob[...]
    grad = prob * (grad - jnp.sum(prob * grad, -1, keepdims=True))
    merge_heads(grad.astype(BF16), s.hot_all, b.branch, None)
    table_pair = nn(s.hot_ri[...], b.branch[...])
    stream_hi, stream_lo = split_two(b.stream[...])
    hot_ir = s.hot_ir[...]
    table_grad = s.grad_head[...] + nn(hot_ir, stream_hi) + nn(hot_ir, stream_lo)
    value_grad = jnp.concatenate(value_rows, 1)
    line = iota((8, D), 0)
    vectors = jnp.zeros((8, D), F32)
    for number, row in enumerate((scale_1, scale_2, scale_3, shift_1, shift_2, shift_3)):
        vectors = jnp.where(line == number, row, vectors)
    extras = jnp.concatenate([s.extras[0:1, :], jnp.zeros((1, D - 128), F32)], 1)
    vectors = jnp.where(line == 6, extras, vectors)
    for start, block in ((0, table_pair), (5, value_grad), (10, table_grad), (15, vectors)):
        for group in range(min(5, block.shape[0] // 8)):
            for half in range(2):
                sums[2 * (start + group) + half] = block[
                    group * 8 : group * 8 + 8, half * 384 : half * 384 + 384
                ]


def shapes_of(names):
    return [jax.ShapeDtypeStruct(shape, dtype) for _, shape, dtype in names]


def scratch_of(names):
    return [pltpu.VMEM(shape, dtype) for _, shape, dtype in names]


def nothing(*names):
    pass


def forward_kernel(*refs):
    count = len(SAVED)
    outs, held = refs[9 : 9 + count], refs[9 + count : 9 + 2 * count]
    scratch, sems = refs[9 + 2 * count : -1], refs[-1]
    number_of = {name: at for at, (name, _, _) in enumerate(SAVED)}

    def out_copy(at):
        return pltpu.make_async_copy(held[at], outs[at], sems.at[at])

    def emit(*names):
        for name in names:
            out_copy(number_of[name]).start()

    forward_body(
        refs[0], refs[1], refs[2:9], Named(SAVED, held), Named(FORWARD_SCRATCH, scratch), nothing, emit
    )
    for at in range(count):
        out_copy(at).wait()


def forward_call(small, contact_head, weights):
    inside = pl.BlockSpec(memory_space=pltpu.VMEM)
    anywhere = pl.BlockSpec(memory_space=pl.ANY)
    return pl.pallas_call(
        forward_kernel,
        out_shape=shapes_of(SAVED),
        in_specs=[inside, pl.BlockSpec(memory_space=pltpu.SMEM)] + [inside] * 7,
        out_specs=[anywhere] * len(SAVED),
        scratch_shapes=scratch_of(SAVED)
        + scratch_of(FORWARD_SCRATCH)
        + [pltpu.SemaphoreType.DMA((len(SAVED),))],
        compiler_params=pltpu.CompilerParams(vmem_limit_bytes=62 * 2**20),
    )(small, contact_head, *weights)


GRADS = tuple(
    (name, (2, D, n), BF16)
    for name, n in (("down_t", 1536), ("up_w", 1536), ("out_col", 384), ("in_col", 1152), ("out_row", 384))
)
LOADED = tuple(item for item in SAVED if item[0] != "proj_t") + GRADS


def backward_kernel(*refs):
    count = len(LOADED)
    head, given = refs[0], refs[1 : 1 + count]
    outs, sums = refs[1 + count : 6 + count], refs[6 + count]
    held = refs[7 + count : 7 + 2 * count]
    scratch, sems = refs[7 + 2 * count : -1], refs[-1]
    number_of = {name: at for at, (name, _, _) in enumerate(LOADED)}
    s = Named(LOADED, held)

    def in_copy(at):
        return pltpu.make_async_copy(given[at], held[at], sems.at[at])

    def out_copy(m):
        return pltpu.make_async_copy(held[count - 5 + m], outs[m], sems.at[count + m])

    for name in (
        ("norms", "table", "logit_low", "unit_3", "rstd_3", "slope", "down_t", "active", "up_w")
        + ("feed_normed_t", "unit_2", "rstd_2", "out_col", "col_mixed_t", "col_proj", "col_prob")
        + ("in_col", "col_normed_t", "unit_1", "rstd_1", "out_row", "row_mixed_t", "value_two")
        + ("weight_hi", "hot_all", "hot_ri", "hot_ir", "prob", "touch", "grad_head", "extras")
    ):
        in_copy(number_of[name]).start()

    def need(*names):
        for name in names:
            in_copy(number_of[name]).wait()

    def done(m):
        out_copy(m).start()

    blocks = held[count - 5 :]
    backward_body(
        head,
        (blocks[4], blocks[3], blocks[2], blocks[1], blocks[0]),
        s,
        Named(BACKWARD_SCRATCH, scratch),
        blocks,
        sums,
        need,
        done,
    )
    for m in range(5):
        out_copy(m).wait()


def backward_call(contact_head, loaded):
    inside = pl.BlockSpec(memory_space=pltpu.VMEM)
    anywhere = pl.BlockSpec(memory_space=pl.ANY)
    outs = pl.pallas_call(
        backward_kernel,
        out_shape=shapes_of(GRADS) + [jax.ShapeDtypeStruct((32, 8, 384), F32)],
        in_specs=[pl.BlockSpec(memory_space=pltpu.SMEM)] + [anywhere] * len(LOADED),
        out_specs=[anywhere] * 5 + [inside],
        scratch_shapes=scratch_of(LOADED)
        + scratch_of(BACKWARD_SCRATCH)
        + [pltpu.SemaphoreType.DMA((len(LOADED) + 5,))],
        compiler_params=pltpu.CompilerParams(vmem_limit_bytes=62 * 2**20),
    )(contact_head, *loaded)
    return outs[:5], outs[5]


def summed_rows(sums, start, groups, rows):
    parts = [
        jnp.concatenate([sums[2 * (start + g)], sums[2 * (start + g) + 1]], 1) for g in range(groups)
    ]
    if rows > 8 * groups:
        parts.append(jnp.zeros((rows - 8 * groups, D), F32))
    return jnp.concatenate(parts, 0) if len(parts) > 1 else parts[0]


def table_finish(sums, table_ref, norms_ref, proj_t, in_row, g_in, g_emb, g_norm):
    z, y, k, c = place()
    me = (z * 4 + y * 2 + k) * 2 + c
    pair = summed_rows(sums, 0, 5, VP)
    value_grad = summed_rows(sums, 5, 5, VP)
    table_grad = summed_rows(sums, 10, 5, VP)
    vectors = summed_rows(sums, 15, 1, 8)
    pair_hi, pair_lo = split_two(pair)
    scale = (HD * ROWS) ** (-0.5)
    query_grad, key_grad = [], []
    for hp in range(PAIRS):
        lanes = slice(hp * 128, hp * 128 + 128)
        query = proj_t[:, lanes]
        key = stacked(proj_t[:, D + hp * 128 : D + hp * 128 + 128])
        high, low = pair_hi[:, lanes], pair_lo[:, lanes]
        query_grad.append((nn(high, key) + nn(low, key)) * scale)
        key_grad.append(unstacked(tn(high, query) + tn(low, query), VP) * scale)
    proj_hi, proj_lo = split_two(jnp.concatenate(query_grad + key_grad + [value_grad], 1))
    normed_grad = jnp.zeros((VP, D), F32)
    for half in range(2):
        lanes = slice(half * 1152, half * 1152 + 1152)
        matrix = in_row[half]
        normed_grad = normed_grad + nt(proj_hi[:, lanes], matrix) + nt(proj_lo[:, lanes], matrix)
    unit, rstd = norm_stats(table_ref[...])
    gain = norms_ref[0:1, :]
    back, scale_0, shift_0 = norm_back(unit, rstd, gain, normed_grad)
    table_grad = table_grad + back
    line = iota((16, D), 0)
    norm_grad = jnp.zeros((16, D), F32)
    rows = [scale_0[None]] + [vectors[n : n + 1] for n in range(3)]
    rows += [shift_0[None]] + [vectors[n : n + 1] for n in range(3, 6)]
    for number, row in enumerate(rows):
        norm_grad = jnp.where(line == number, row, norm_grad)
    shard = D // 32
    pick = one_zero(iota((shard, D), 1) == iota((shard, D), 0) + me * shard).astype(BF16)
    normed = (unit * gain + norms_ref[4:5, :]).astype(BF16)
    mine = nt(pick, normed).astype(BF16)
    in_grad = nn(mine, proj_hi) + nn(mine, proj_lo)
    g_in[...] = in_grad

    def three(values):
        top, rest = split_two(values)
        return top, rest, (values - top.astype(F32) - rest.astype(F32)).astype(BF16)

    emb_grad = sum(nt(pick, part) for part in three(table_grad))
    g_emb[...] = emb_grad
    own_norm = sum(nt(part, pick) for part in three(norm_grad))[:8]
    g_norm[...] = own_norm
    return total_of(in_grad * in_grad) + total_of(emb_grad * emb_grad) + total_of(own_norm * own_norm)


UPDATE_RATES = (LEARN_RATE,) * 4 + (VECTOR_RATE,) * 3


def update_kernel(*refs):
    reduced, g_in, g_emb, g_norm, stats = refs[:5], refs[5], refs[6], refs[7], refs[8]
    states = [refs[9 + 3 * n : 12 + 3 * n] for n in range(7)]
    outs = [refs[30 + 3 * n : 33 + 3 * n] for n in range(7)]
    copies = refs[51:56]
    loss_ref, norm_ref = refs[56:58]
    g_down, g_up, g_out_col, g_in_col, g_out_row = reduced
    factor = stats[2:3, 0:1]
    loss_ref[...] = stats[4:5, 0:4]
    norm_ref[...] = stats[3:4, 0:1]

    def update(number, where, grad):
        master, first, second = (ref[where] for ref in states[number])
        new, first, second = adam_update(master, first, second, grad * factor, UPDATE_RATES[number])
        for ref, value in zip(outs[number], (new, first, second)):
            ref[where] = value
        if number < 5:
            copies[number][where] = new.astype(BF16)

    every = slice(None)
    for half in range(2):
        lanes = slice(half * 1152, half * 1152 + 1152)
        update(0, (0, every, lanes), g_in[:, lanes])
        update(0, (1, every, lanes), g_in_col[half])
        lanes = slice(half * 384, half * 384 + 384)
        update(1, (0, every, lanes), g_out_row[half])
        update(1, (1, every, lanes), g_out_col[half])
        lanes = slice(half * 1536, half * 1536 + 1536)
        update(2, (every, lanes), g_up[half])
        update(3, (every, lanes), g_down[half])
    update(4, (every, every), g_emb[:, :VOCAB])
    update(5, (every, every), g_norm[...])
    update(6, (every, every), stats[0:1, : HEADS + 1])


def update_call(reduced, g_in, g_emb, g_norm, stats, states):
    inside = pl.BlockSpec(memory_space=pltpu.VMEM)
    flat = [item for state in states for item in state]
    shapes = [jax.ShapeDtypeStruct(item.shape, F32) for item in flat]
    shapes += [jax.ShapeDtypeStruct(states[n][0].shape, BF16) for n in range(5)]
    shapes += [jax.ShapeDtypeStruct((1, 4), F32), jax.ShapeDtypeStruct((1, 1), F32)]
    return pl.pallas_call(
        update_kernel,
        out_shape=shapes,
        in_specs=[inside] * (9 + len(flat)),
        out_specs=[inside] * len(shapes),
        compiler_params=pltpu.CompilerParams(vmem_limit_bytes=48 * 2**20),
    )(*reduced, g_in, g_emb, g_norm, stats, *flat)


def adam_update(master, first, second, grad_part, rate):
    first = BETA_ONE * first + (1.0 - BETA_ONE) * grad_part
    second = BETA_TWO * second + (1.0 - BETA_TWO) * grad_part * grad_part
    moved = first / (1.0 - BETA_ONE**STEP) / (jnp.sqrt(second / (1.0 - BETA_TWO**STEP)) + ADAM_EPS)
    return (master - rate * (moved + WEIGHT_DECAY * master), first, second)


def shards(
    tokens,
    targets,
    masked,
    contact_pairs,
    labels,
    attention_in_master,
    attention_in_first,
    attention_in_second,
    attention_out_master,
    attention_out_first,
    attention_out_second,
    feed_up_master,
    feed_up_first,
    feed_up_second,
    feed_down_master,
    feed_down_first,
    feed_down_second,
    embedding_master,
    embedding_first,
    embedding_second,
    norm_params_master,
    norm_params_first,
    norm_params_second,
    contact_head_master,
    contact_head_first,
    contact_head_second,
):
    both = ("seq", "col")
    micro, rows_here, cols_here = tokens.shape
    ncol = lax.axis_size("col")
    ndev = lax.axis_size("seq") * ncol
    cols = cols_here * ncol
    me = lax.axis_index("seq") * ncol + lax.axis_index("col")
    per = ndev // micro
    cw = cols // per
    mine = me // per
    base = (me % per) * cw
    shard = D // ndev

    tiled = lax.axis_size("seq") == 16 and ncol == 2
    inputs = jnp.where(masked > 0, MASK_ID, tokens)
    masters = [
        jnp.concatenate(
            [
                jnp.pad(embedding_master.T, ((0, 0), (0, 128 - VOCAB))),
                jnp.pad(norm_params_master.T, ((0, 0), (0, 120))),
            ],
            1,
        ),
        attention_in_master[0],
        attention_out_master[0],
        attention_in_master[1],
        attention_out_master[1],
        feed_up_master,
        feed_down_master.T,
    ]
    if tiled:
        small = jnp.concatenate(
            [
                inputs.reshape(4, 128),
                targets.reshape(4, 128),
                contact_pairs[..., 0].reshape(1, 128),
                contact_pairs[..., 1].reshape(1, 128),
                labels.reshape(1, 128),
                jnp.zeros((5, 128), jnp.int32),
            ]
        )
        small_all, gathered = gather_all(small, masters)
        gathered = [g.reshape(2, D, g.shape[-1]) for g in gathered]
        saved = forward_call(small_all, contact_head_master, gathered)
        by_name = {name: value for (name, _, _), value in zip(SAVED, saved)}
        by_name.update(zip(("out_row", "in_col", "out_col", "up_w", "down_t"), gathered[2:]))
        blocks, sums = backward_call(contact_head_master, [by_name[name] for name, _, _ in LOADED])
        blocks = [g.reshape(2, NZ, NY, 2, 48, g.shape[-1]) for g in blocks]
        reduced, (g_in, g_emb, g_norm, stats) = scatter_all(
            sums, by_name["table"], by_name["norms"], by_name["proj_t"], by_name["extras"], gathered[1], blocks
        )
        states = (
            (attention_in_master, attention_in_first, attention_in_second),
            (attention_out_master, attention_out_first, attention_out_second),
            (feed_up_master, feed_up_first, feed_up_second),
            (feed_down_master.T, feed_down_first.T, feed_down_second.T),
            (embedding_master.T, embedding_first.T, embedding_second.T),
            (norm_params_master, norm_params_first, norm_params_second),
            (contact_head_master[None], contact_head_first[None], contact_head_second[None]),
        )
        outs = update_call(reduced, g_in, g_emb, g_norm, stats, states)
        return (
            *outs[:9],
            *(item.T for item in outs[9:15]),
            *outs[15:18],
            *(item[0] for item in outs[18:21]),
            *outs[21:24],
            *(item.T for item in outs[24:26]),
            outs[26][0],
            outs[27][0, 0],
        )
    whole = jnp.stack([inputs, targets])
    whole = lax.all_gather(lax.all_gather(whole, "col", axis=3, tiled=True), "seq", axis=2, tiled=True)
    pairs_all = lax.all_gather(
        jnp.concatenate([contact_pairs, labels[:, :, None]], -1), both, axis=1, tiled=True
    )
    gathered = []
    for master in masters:
        full = lax.all_gather(master.astype(BF16), both, axis=0, tiled=True)
        gathered.append(full.reshape(D, 2, -1).transpose(1, 0, 2))
    counts = (
        jnp.sum(whole[0] == MASK_ID).astype(F32),
        jnp.sum(pairs_all[..., 2] >= 0).astype(F32),
    )
    ids_all = lax.dynamic_index_in_dim(whole[0], mine, 0, False)
    ids_local = lax.dynamic_slice_in_dim(ids_all, base, cw, 1)
    targets_local = lax.dynamic_slice_in_dim(
        lax.dynamic_index_in_dim(whole[1], mine, 0, False), base, cw, 1
    )
    pairs = lax.dynamic_index_in_dim(pairs_all, mine, 0, False)

    table = gathered[0][0][:, :VP].T
    norms = gathered[0][1][:, :8].T.astype(F32)
    in_row, out_row, in_col, out_col, up_w, down_t = (
        jnp.concatenate([g[0], g[1]], 1) for g in gathered[1:]
    )
    big = (in_row, in_col, out_row, out_col, up_w, down_t)

    grads, tables, contact_total, mlm_total, bce_total, kept = step(
        big,
        table,
        norms,
        contact_head_master,
        ids_all,
        ids_local.reshape(-1),
        ids_local.T.reshape(-1),
        targets_local.T.reshape(-1),
        pairs[:, 0] - base,
        pairs[:, 1],
        pairs[:, 2],
        counts,
        cw,
    )
    table_pair, value_grad, table_grad, vectors = tables
    extras = jnp.zeros((2, D), F32).at[0, : HEADS + 3].set(
        jnp.concatenate([contact_total, mlm_total[None], bce_total[None]])
    )
    sums = jnp.concatenate([table_pair[:40], value_grad[:40], table_grad[:40], vectors, extras])
    flat_grad = jnp.concatenate([g.astype(BF16) for g in grads], 1)
    reduced = lax.psum_scatter(flat_grad, both, scatter_dimension=0, tiled=True).astype(F32)
    g_in_col, g_out_row, g_out_col, g_up, g_down = jnp.split(
        reduced, [3 * D, 4 * D, 5 * D, 5 * D + FF], 1
    )
    sums = lax.psum(sums, both)
    unit_t, rstd_t, normed_t, query_t, key_t = kept
    rows_all = ids_all.shape[0]
    spare = ((0, VP - 40), (0, 0))
    table_pair, value_grad, table_grad = (
        jnp.pad(sums[a : a + 40], spare) for a in (0, 40, 80)
    )
    vectors = sums[120:126]
    contact_grad, mlm_total, bce_total = (
        sums[126, : HEADS + 1], sums[126, HEADS + 1], sums[126, HEADS + 2]
    )
    row_scale = (HD * rows_all) ** (-0.5)
    query_grad = []
    key_grad = []
    for h in range(HEADS):
        pair = heads_of(table_pair, h)
        query_grad.append(jnp.dot(pair, heads_of(key_t, h).astype(F32), precision=PRECISE))
        key_grad.append(jnp.dot(pair.T, heads_of(query_t, h).astype(F32), precision=PRECISE))
    proj_grad = jnp.concatenate(
        [
            jnp.concatenate(query_grad, 1) * row_scale,
            jnp.concatenate(key_grad, 1) * row_scale,
            value_grad,
        ],
        1,
    )
    proj_hi, proj_lo = split_two(proj_grad)
    normed_grad = nt(proj_hi, in_row) + nt(proj_lo, in_row)
    back_t, scale_0, shift_0 = norm_back(unit_t, rstd_t, norms[0], normed_grad)
    table_grad = table_grad + back_t
    low = me * shard
    normed_mine = lax.dynamic_slice_in_dim(normed_t, low, shard, 1)
    grad_in_row = tn(normed_mine, proj_hi) + tn(normed_mine, proj_lo)
    norm_grad = jnp.concatenate([scale_0[None], vectors[:3], shift_0[None], vectors[3:]])
    table_mine = lax.dynamic_slice_in_dim(table_grad[:VOCAB], low, shard, 1)
    norm_mine = lax.dynamic_slice_in_dim(norm_grad, low, shard, 1)
    reduced_all = (g_in_col, g_out_row, g_out_col, g_up, g_down)

    local_square = (
        sum(jnp.sum(g * g) for g in reduced_all)
        + jnp.sum(grad_in_row * grad_in_row)
        + jnp.sum(table_mine * table_mine)
        + jnp.sum(norm_mine * norm_mine)
    )
    square = lax.psum(local_square, both) + jnp.sum(contact_grad * contact_grad)
    grad_norm = jnp.sqrt(square)
    factor = jnp.minimum(1.0, MAX_NORM / grad_norm)
    in_new, in_moment, in_square = adam_update(
        attention_in_master, attention_in_first, attention_in_second, jnp.stack([grad_in_row, g_in_col]) * factor, LEARN_RATE
    )
    out_new, out_moment, out_square = adam_update(
        attention_out_master, attention_out_first, attention_out_second, jnp.stack([g_out_row, g_out_col]) * factor, LEARN_RATE
    )
    up_new, up_moment, up_square = adam_update(
        feed_up_master, feed_up_first, feed_up_second, g_up * factor, LEARN_RATE
    )
    down_new, down_moment, down_square = adam_update(
        feed_down_master, feed_down_first, feed_down_second, g_down.T * factor, LEARN_RATE
    )
    table_new, table_moment, table_square = adam_update(
        embedding_master, embedding_first, embedding_second, table_mine * factor, VECTOR_RATE
    )
    norm_new, norm_moment, norm_square = adam_update(
        norm_params_master, norm_params_first, norm_params_second, norm_mine * factor, VECTOR_RATE
    )
    head_new, head_moment, head_square = adam_update(
        contact_head_master, contact_head_first, contact_head_second, contact_grad * factor, VECTOR_RATE
    )
    loss_parts = jnp.stack([mlm_total, counts[0], bce_total, counts[1]])
    return (
        in_new, in_moment, in_square,
        out_new, out_moment, out_square,
        up_new, up_moment, up_square,
        down_new, down_moment, down_square,
        table_new, table_moment, table_square,
        norm_new, norm_moment, norm_square,
        head_new, head_moment, head_square,
        in_new.astype(BF16), out_new.astype(BF16), up_new.astype(BF16), down_new.astype(BF16), table_new.astype(BF16),
        loss_parts, grad_norm,
    )


def solution(mesh):
    both = ("seq", "col")
    cells = P(None, "seq", "col")
    stack = P(None, both, None)
    row_split = P(both, None)
    col_split = P(None, both)
    weights = [stack] * 6 + [row_split] * 3 + [col_split] * 9 + [P()] * 3
    return jax.shard_map(
        shards,
        mesh=mesh,
        in_specs=(cells, cells, cells, stack, col_split, *weights),
        out_specs=(*weights, stack, stack, row_split, col_split, col_split, P(), P()),
        check_vma=False,
    )
```

```python
import typing

import jax
import jax.numpy as jnp
from jax import lax
from jax.experimental import pallas as pl
from jax.experimental.pallas import tpu as pltpu
from jax.sharding import PartitionSpec as P

D = 768
HEADS = 12
HD = 64
FF = 3072
VOCAB = 33
VP = 64
STEP = 10

NORM_EPS = 1e-05
MASK_ID = 32
MAX_NORM = 0.001
LEARN_RATE = 0.05
VECTOR_RATE = 0.5
BETA_ONE = 0.9
BETA_TWO = 0.95
ADAM_EPS = 1e-08
WEIGHT_DECAY = 0.01
PRECISE = lax.Precision.HIGHEST
F32 = jnp.float32
BF16 = jnp.bfloat16


def nn(left, right):
    return lax.dot_general(left, right, (((1,), (0,)), ((), ())), preferred_element_type=F32)


def tn(left, right):
    return lax.dot_general(left, right, (((0,), (0,)), ((), ())), preferred_element_type=F32)


def nt(left, right):
    return lax.dot_general(left, right, (((1,), (1,)), ((), ())), preferred_element_type=F32)


def split_two(values):
    high = values.astype(BF16)
    return high, (values - high.astype(F32)).astype(BF16)


def norm_stats(values):
    centre = values - jnp.mean(values, -1, keepdims=True)
    rstd = lax.rsqrt(jnp.mean(centre * centre, -1, keepdims=True) + NORM_EPS)
    return centre * rstd, rstd


def norm_back(unit, rstd, scale_vec, upstream):
    inner = upstream * scale_vec
    grad = rstd * (
        inner - jnp.mean(inner, -1, keepdims=True) - unit * jnp.mean(inner * unit, -1, keepdims=True)
    )
    return grad, jnp.sum(upstream * unit, 0), jnp.sum(upstream, 0)


GELU_K = 0.7978845608028654
GELU_C = 0.044715


def gelu_parts(up):
    square = up * up
    bent = jnp.tanh(GELU_K * up * (1.0 + GELU_C * square))
    half = 0.5 * (1.0 + bent)
    slope = half + 0.5 * up * (1.0 - bent * bent) * GELU_K * (1.0 + 3.0 * GELU_C * square)
    return up * half, slope


def heads_of(block, head):
    return block[:, head * HD : (head + 1) * HD]


def step(big, table, norms, contact_head, ids_all, ids_ri, ids_ir, targets_ir, pair_first, pair_second, labels, counts, cw):
    in_row, in_col, out_row, out_col, up_w, down_t = big
    rows, cols = ids_all.shape
    here = rows * cw
    row_scale = (HD * rows) ** (-0.5)
    vocab = jnp.arange(VP)[:, None]
    hot_all = (ids_all[:, None, :] == vocab[None]).astype(BF16).reshape(rows * VP, cols)
    hot_ri = (ids_ri[None, :] == vocab).astype(BF16)
    hot_ir = (ids_ir[None, :] == vocab).astype(BF16)
    spot = jnp.arange(here)
    perm = (
        ((spot // rows)[:, None] == (spot % cw)[None, :])
        & ((spot % rows)[:, None] == (spot // cw)[None, :])
    ).astype(BF16)

    def to_heads(block):
        return block.reshape(rows, cw, HEADS, VP).transpose(2, 1, 0, 3).reshape(HEADS * cw, rows * VP)

    def to_tokens(block):
        return block.reshape(HEADS, cw, rows, VP).transpose(2, 1, 0, 3).reshape(here, HEADS * VP)

    def per_head(block, other, how):
        return jnp.concatenate(
            [how(heads_of(block, h), heads_of(other, h)) for h in range(HEADS)], -1
        )

    table_f = table.astype(F32)
    unit_t, rstd_t = norm_stats(table_f)
    normed_t = (unit_t * norms[0] + norms[4]).astype(BF16)
    proj_t = nn(normed_t, in_row).astype(BF16)
    query_t, key_t, value_t = proj_t[:, :D], proj_t[:, D : 2 * D], proj_t[:, 2 * D :]

    pair_t = per_head(query_t, key_t, nt)
    pair_hi, pair_lo = split_two(pair_t)
    left_hi = to_heads(tn(hot_ri, pair_hi).astype(BF16))
    left_lo = to_heads(tn(hot_ri, pair_lo).astype(BF16))
    score = (nn(left_hi, hot_all) + nn(left_lo, hot_all)) * row_scale
    prob = jax.nn.softmax(score, axis=-1)
    prob_low = prob.astype(BF16)
    weight_t = to_tokens(nt(prob_low, hot_all))
    weight_hi, weight_lo = split_two(weight_t)
    row_mixed_ri = (
        per_head(weight_hi, value_t, nn) + per_head(weight_lo, value_t, nn)
    ).astype(BF16)
    row_mixed = nn(perm, row_mixed_ri).astype(BF16)
    embedded = tn(hot_ir, table)
    after_row = embedded + nn(row_mixed, out_row)

    prob_cube = prob_low.astype(F32).reshape(HEADS, cw, cols)
    head_sum = jnp.sum(prob_cube * contact_head[:HEADS, None, None], 0)
    first_hot = (pair_first[None, :] == jnp.arange(cw)[:, None]).astype(F32)
    second_hot = (pair_second[None, :] == jnp.arange(cols)[:, None]).astype(BF16)
    sum_hi, sum_lo = split_two(head_sum)
    sum_last = (head_sum - sum_hi.astype(F32) - sum_lo.astype(F32)).astype(BF16)
    picked = nn(sum_hi, second_hot) + nn(sum_lo, second_hot) + nn(sum_last, second_hot)
    contact_logit = jnp.sum(picked * first_hot, 0) * cols + contact_head[HEADS]
    owned = jnp.sum(first_hot, 0) > 0
    valid = (labels >= 0) & owned
    positive = (labels == 1).astype(F32)
    bce_sum = jnp.sum(
        jnp.where(valid, jax.nn.softplus(contact_logit) - positive * contact_logit, 0.0)
    )
    coef = jnp.where(valid, jax.nn.sigmoid(contact_logit) - positive, 0.0) / counts[1]
    coef_hi, coef_lo = split_two(coef)
    first_low = first_hot.astype(BF16)
    touch = nt(first_low * coef_hi[None], second_hot) + nt(first_low * coef_lo[None], second_hot)
    grad_contact = jnp.concatenate(
        [jnp.sum(prob_cube * touch[None], (1, 2)) * cols, jnp.sum(coef)[None]]
    )

    unit_1, rstd_1 = norm_stats(after_row)
    col_normed = (unit_1 * norms[1] + norms[5]).astype(BF16)
    col_proj = nn(col_normed, in_col).astype(BF16)
    group = 128 if here % 128 == 0 and 128 % rows == 0 else here
    groups = here // group
    lane = jnp.arange(group)
    same = (lane[:, None] // rows) == (lane[None, :] // rows)

    def cut(block):
        return block.reshape(groups, group, HEADS, HD)

    col_query, col_key, col_value = (cut(col_proj[:, k * D : (k + 1) * D]) for k in range(3))
    col_score = jnp.einsum("gqhe,gkhe->ghqk", col_query, col_key, preferred_element_type=F32) * HD ** (-0.5)
    col_prob = jax.nn.softmax(jnp.where(same, col_score, -1e30), axis=-1)
    col_prob_low = col_prob.astype(BF16)
    col_mixed = (
        jnp.einsum("ghqk,gkhe->gqhe", col_prob_low, col_value, preferred_element_type=F32)
        .astype(BF16)
        .reshape(here, D)
    )
    after_col = after_row + nn(col_mixed, out_col)

    unit_2, rstd_2 = norm_stats(after_col)
    feed_normed = (unit_2 * norms[2] + norms[6]).astype(BF16)
    hidden_up = nn(feed_normed, up_w)
    active, slope = gelu_parts(hidden_up)
    active = active.astype(BF16)
    after_feed = after_col + nt(active, down_t)
    unit_3, rstd_3 = norm_stats(after_feed)
    head_normed = (unit_3 * norms[3] + norms[7]).astype(BF16)
    logits = nt(table, head_normed) * D ** (-0.5)
    logits = jnp.where(vocab < VOCAB, logits, -1e30)
    top = jnp.max(logits, 0, keepdims=True)
    shifted = logits - top
    log_probs = shifted - jnp.log(jnp.sum(jnp.exp(shifted), 0, keepdims=True))
    target_hot = (targets_ir[None, :] == vocab).astype(F32)
    keep = ids_ir[None, :] == MASK_ID
    mlm_sum = -jnp.sum(jnp.where(keep & (target_hot > 0), log_probs, 0.0))
    logit_grad = jnp.where(keep, jnp.exp(log_probs) - target_hot, 0.0) / counts[0]
    logit_low = (logit_grad * D ** (-0.5)).astype(BF16)

    grad_head = nn(logit_low, head_normed)
    stream, scale_3, shift_3 = norm_back(unit_3, rstd_3, norms[3], tn(logit_low, table))
    branch = stream.astype(BF16)
    grad_down = tn(branch, active)
    up_low = (nn(branch, down_t) * slope).astype(BF16)
    grad_up = tn(feed_normed, up_low)
    inner, scale_2, shift_2 = norm_back(unit_2, rstd_2, norms[2], nt(up_low, up_w))
    stream = stream + inner
    branch = stream.astype(BF16)
    grad_out_col = tn(col_mixed, branch)
    mixed_low = nt(branch, out_col).astype(BF16)
    mixed_cut = cut(mixed_low)
    prob_grad = jnp.einsum("gqhe,gkhe->ghqk", mixed_cut, col_value, preferred_element_type=F32)
    score_grad = col_prob * (prob_grad - jnp.sum(col_prob * prob_grad, -1, keepdims=True))
    score_low = score_grad.astype(BF16)
    grad_q = jnp.einsum("ghqk,gkhe->gqhe", score_low, col_key, preferred_element_type=F32)
    grad_k = jnp.einsum("ghqk,gqhe->gkhe", score_low, col_query, preferred_element_type=F32)
    grad_v = jnp.einsum("ghqk,gqhe->gkhe", col_prob_low, mixed_cut, preferred_element_type=F32)
    proj_low = jnp.concatenate(
        [
            (grad_q * HD ** (-0.5)).reshape(here, D),
            (grad_k * HD ** (-0.5)).reshape(here, D),
            grad_v.reshape(here, D),
        ],
        -1,
    ).astype(BF16)
    grad_in_col = tn(col_normed, proj_low)
    inner, scale_1, shift_1 = norm_back(unit_1, rstd_1, norms[1], nt(proj_low, in_col))
    stream = stream + inner
    branch = stream.astype(BF16)
    grad_out_row = tn(row_mixed, branch)
    mixed_low = nt(branch, out_row).astype(BF16)
    mixed_ri = tn(perm, mixed_low).astype(BF16)
    drive_hi, drive_lo = split_two(per_head(mixed_ri, value_t, nt))
    prob_grad = nn(to_heads(drive_hi), hot_all) + nn(to_heads(drive_lo), hot_all)
    prob_grad = prob_grad + (
        touch[None] * (contact_head[:HEADS, None, None] * cols)
    ).reshape(HEADS * cw, cols)
    score_grad = prob * (prob_grad - jnp.sum(prob * prob_grad, -1, keepdims=True))
    score_low = score_grad.astype(BF16)
    spread = to_tokens(nt(score_low, hot_all)).astype(BF16)
    table_pair = nn(hot_ri, spread)
    value_grad = per_head(weight_hi, mixed_ri, tn)
    stream_hi, stream_lo = split_two(stream)
    lookup_grad = nn(hot_ir, stream_hi) + nn(hot_ir, stream_lo)
    vectors = jnp.stack([scale_1, scale_2, scale_3, shift_1, shift_2, shift_3])
    return (
        (grad_in_col, grad_out_row, grad_out_col, grad_up, grad_down),
        (table_pair, value_grad, grad_head + lookup_grad, vectors),
        grad_contact,
        mlm_sum,
        bce_sum,
        (unit_t, rstd_t, normed_t, query_t, key_t),
    )


MESH = pl.DeviceIdType.MESH
NZ, NY = 4, 2


def place():
    s, c = lax.axis_index("seq"), lax.axis_index("col")
    z, y, k = s // 4, lax.rem(s // 2, 2), lax.rem(s, 2)
    return z, y, k, c


def device(z, y, k, c):
    return (z * 4 + y * 2 + k, c)


def greet_all():
    z, y, k, c = place()
    me = (z * 4 + y * 2 + k) * 2 + c
    barrier = pltpu.get_barrier_semaphore()

    def signal(step, carry):
        other = lax.rem(me + step, 32)
        pl.semaphore_signal(
            barrier, inc=1, device_id=(other // 2, lax.rem(other, 2)), device_id_type=MESH
        )
        return carry

    lax.fori_loop(1, 32, signal, 0)
    return barrier


def remote(src, dst, send, recv, target):
    return pltpu.make_async_remote_copy(
        src_ref=src, dst_ref=dst, send_sem=send, recv_sem=recv, device_id=target, device_id_type=MESH
    )


ROWS, COLS, WIDE, HERE = 16, 512, 32, 512
PAIRS = 6
SLOTS = 1024
UP_TILE = 384


def iota(shape, dim):
    return lax.broadcasted_iota(jnp.int32, shape, dim)


def one_zero(test):
    return jnp.where(test, 1.0, 0.0)


def total_of(values):
    return jnp.sum(jnp.sum(values, 0, keepdims=True), 1, keepdims=True)


def half_lanes(values, side):
    lane = iota(values.shape, len(values.shape) - 1)
    keep = (lane < 64) if side == 0 else (lane >= 64)
    return jnp.where(keep, values.astype(F32), 0.0).astype(BF16)


def stacked(values):
    return jnp.concatenate([half_lanes(values, 0), half_lanes(values, 1)], 0)


def unstacked(values, count):
    lane = iota((count, 128), 1)
    return jnp.where(lane < 64, values[:count], values[count:])


def swap_blocks(first, second):
    lane = iota(first.shape, 1)
    low = jnp.where(lane < 64, first, pltpu.roll(second, 64, 1))
    high = jnp.where(lane < 64, pltpu.roll(first, 64, 1), second)
    return low, high


def split_heads_to(source, high_ref, low_ref):
    for rp in range(ROWS // 2):
        for hp in range(PAIRS):
            lanes = slice(hp * 128, hp * 128 + 128)
            first = source[rp * 64 : rp * 64 + 32, lanes]
            second = source[rp * 64 + 32 : rp * 64 + 64, lanes]
            for side, block in enumerate(swap_blocks(first, second)):
                top, rest = split_two(block)
                rows = slice((2 * hp + side) * 32, (2 * hp + side) * 32 + 32)
                high_ref[rows, rp * 128 : rp * 128 + 128] = top
                low_ref[rows, rp * 128 : rp * 128 + 128] = rest


def merge_heads(probs, hot_all, high_ref, low_ref):
    for rp in range(ROWS // 2):
        block = nt(probs, hot_all[rp * 128 : rp * 128 + 128, :])
        for hp in range(PAIRS):
            first = block[hp * 64 : hp * 64 + 32]
            second = block[hp * 64 + 32 : hp * 64 + 64]
            for side, part in enumerate(swap_blocks(first, second)):
                top, rest = split_two(part)
                rows = slice(rp * 64 + side * 32, rp * 64 + side * 32 + 32)
                high_ref[rows, hp * 128 : hp * 128 + 128] = top
                if low_ref is not None:
                    low_ref[rows, hp * 128 : hp * 128 + 128] = rest


def norm_rows(source, gain, bias, unit_ref, rstd_ref, normed_ref):
    def body(at, carry):
        rows = pl.ds(pl.multiple_of(at * 32, 32), 32)
        values = source[rows, :]
        centre = values - jnp.sum(values, -1, keepdims=True) * (1.0 / D)
        rstd = lax.rsqrt(jnp.sum(centre * centre, -1, keepdims=True) * (1.0 / D) + NORM_EPS)
        unit = centre * rstd
        unit_ref[rows, :] = unit
        rstd_ref[rows, :] = jnp.broadcast_to(rstd, (32, 128))
        normed_ref[rows, :] = (unit * gain + bias).astype(BF16)
        return carry

    lax.fori_loop(0, HERE // 32, body, 0)


def transpose_into(source, target):
    def body(at, carry):
        rows = pl.ds(pl.multiple_of(at * 128, 128), 128)
        target[:, rows] = source[rows, :].astype(F32).T.astype(BF16)
        return carry

    lax.fori_loop(0, HERE // 128, body, 0)


def over_tiles(width, tile, body):
    for half in range(2):

        def step(at, carry, half=half):
            body(half, pl.multiple_of(at * tile, tile))
            return carry

        lax.fori_loop(0, width // tile, step, 0)


def column_mask():
    rows, lanes = iota((256, 128), 0), iota((256, 128), 1)
    return ((rows & 127) >> 4) == (lanes >> 4)


class Saved(typing.NamedTuple):
    stream: typing.Any
    unit_1: typing.Any
    unit_2: typing.Any
    rstd_1: typing.Any
    rstd_2: typing.Any
    row_mixed_t: typing.Any
    col_normed_t: typing.Any
    col_mixed_t: typing.Any
    feed_normed_t: typing.Any
    col_proj: typing.Any
    col_prob: typing.Any
    active: typing.Any
    slope: typing.Any
    grad_head: typing.Any
    hot_all: typing.Any
    hot_ri: typing.Any
    hot_ir: typing.Any
    prob: typing.Any
    weight_hi: typing.Any
    value_two: typing.Any
    touch: typing.Any
    table: typing.Any
    norms: typing.Any
    proj_t: typing.Any
    extras: typing.Any
    moved: typing.Any


AT = Saved(*range(len(Saved._fields)))
SAVED = Saved(
    stream=((HERE, D), F32),
    unit_1=((HERE, D), F32),
    unit_2=((HERE, D), F32),
    rstd_1=((HERE, 128), F32),
    rstd_2=((HERE, 128), F32),
    row_mixed_t=((D, HERE), BF16),
    col_normed_t=((D, HERE), BF16),
    col_mixed_t=((D, HERE), BF16),
    feed_normed_t=((D, HERE), BF16),
    col_proj=((HERE, 3 * D), BF16),
    col_prob=((4 * PAIRS, 256, 128), F32),
    active=((HERE, FF), BF16),
    slope=((HERE, FF), BF16),
    grad_head=((VP, D), F32),
    hot_all=((ROWS * VP, COLS), BF16),
    hot_ri=((VP, HERE), BF16),
    hot_ir=((VP, HERE), BF16),
    prob=((HEADS * WIDE, COLS), F32),
    weight_hi=((HERE, D), BF16),
    value_two=((PAIRS, 128, 128), BF16),
    touch=((WIDE, COLS), F32),
    table=((VP, D), F32),
    norms=((8, D), F32),
    proj_t=((VP, 3 * D), BF16),
    extras=((8, 128), F32),
    moved=((8, D), F32),
)


class Forward(typing.NamedTuple):
    ids: typing.Any
    targets: typing.Any
    slots: typing.Any
    normed: typing.Any
    mixed: typing.Any
    weight_lo: typing.Any
    left_hi: typing.Any
    left_lo: typing.Any
    lookup: typing.Any
    prob_low: typing.Any
    unit: typing.Any
    rstd: typing.Any


FORWARD = Forward(
    ids=((ROWS, COLS), jnp.int32),
    targets=((ROWS, 128), jnp.int32),
    slots=((8, SLOTS), jnp.int32),
    normed=((HERE, D), BF16),
    mixed=((HERE, D), BF16),
    weight_lo=((HERE, D), BF16),
    left_hi=((HEADS * WIDE, ROWS * VP), BF16),
    left_lo=((HEADS * WIDE, ROWS * VP), BF16),
    lookup=((HERE, D), F32),
    prob_low=((HEADS * WIDE, COLS), BF16),
    unit=((HERE, D), F32),
    rstd=((HERE, 128), F32),
)


def position():
    z, y, k, c = place()
    me = (z * 4 + y * 2 + k) * 2 + c
    return z // 2, lax.rem(me, 16)


def read_tokens(small, f):
    alignment, block = position()
    side, part = block // 8, lax.rem(block // 4, 2)
    for r in range(ROWS):
        for cc in range(2):
            for q in range(2):
                lanes = slice(cc * 256 + q * 128, cc * 256 + q * 128 + 128)
                f.ids[r : r + 1, lanes] = small[r * 2 + cc, pl.ds(2 * alignment + q, 1), :]
        f.targets[r : r + 1, :] = small[r * 2 + side, pl.ds(4 + 2 * alignment + part, 1), :]
    lane = iota((1, 128), 1)
    turn = alignment * 64
    for number in range(SLOTS // 128):
        for which in range(3):
            first = small[number * 4 + side, 8 + which : 9 + which, :]
            second = small[number * 4 + 2 + side, 8 + which : 9 + which, :]
            first = pltpu.roll(first, lax.rem(128 - turn, 128), 1)
            second = pltpu.roll(second, 64 - turn, 1)
            f.slots[which : which + 1, number * 128 : number * 128 + 128] = jnp.where(
                lane < 64, first, second
            )


def local_hot(values, shift):
    values = pltpu.roll(values, shift, 1)
    turned = [values] + [pltpu.roll(values, 32 * n, 1) for n in (1, 2, 3)]
    lane = iota((1, 128), 1)
    tiles = []
    for tile in range(4):
        row = turned[3][4 * tile + 3 : 4 * tile + 4]
        for n in (2, 1, 0):
            row = jnp.where(lane < 32 * n + 32, turned[n][4 * tile + n : 4 * tile + n + 1], row)
        tiles.append(row)
    row = jnp.concatenate(tiles, 1)
    return one_zero(row == iota((VP, HERE), 0)).astype(BF16)


def contact_part(contact_head, f, s, pair_count):
    _, block = position()
    base = block * WIDE
    head_sum = jnp.zeros((WIDE, COLS), F32)
    for h in range(HEADS):
        head_sum = head_sum + contact_head[h] * f.prob_low[h * 32 : h * 32 + 32, :].astype(F32)
    top, rest = split_two(head_sum)
    last = (head_sum - top.astype(F32) - rest.astype(F32)).astype(BF16)
    parts = jnp.concatenate([top, rest, last], 0)
    touch = jnp.zeros((WIDE, COLS), F32)
    bce = jnp.zeros((1, 1), F32)
    coef_sum = jnp.zeros((1, 1), F32)
    for number in range(SLOTS // 512):
        lanes = slice(number * 512, number * 512 + 512)
        first, second, label = (f.slots[n : n + 1, lanes] for n in range(3))
        second_hot = one_zero(second == iota((COLS, 512), 0)).astype(BF16)
        picked = nn(parts, second_hot)
        picked = picked[:32] + picked[32:64] + picked[64:]
        first_hot = one_zero((first - base) == iota((WIDE, 512), 0))
        logit = jnp.sum(picked * first_hot, 0, keepdims=True) * COLS + contact_head[HEADS]
        owned = jnp.sum(first_hot, 0, keepdims=True) > 0.5
        valid = (label >= 0) & owned
        positive = one_zero(label == 1)
        small = jnp.exp(-jnp.abs(logit))
        soft = jnp.maximum(logit, 0.0) + jnp.log(1.0 + small)
        bce = bce + total_of(jnp.where(valid, soft - positive * logit, 0.0))
        sigmoid = jnp.where(logit >= 0.0, 1.0, small) / (1.0 + small)
        coef = jnp.where(valid, sigmoid - positive, 0.0) / pair_count
        coef_sum = coef_sum + total_of(coef)
        coef_top, coef_rest = split_two(first_hot * coef)
        touch = touch + nt(coef_top, second_hot) + nt(coef_rest, second_hot)
    s.touch[...] = touch
    column = iota((1, 128), 1)
    row = jnp.where(column == HEADS, coef_sum, 0.0)
    for h in range(HEADS):
        part = total_of(touch * f.prob_low[h * 32 : h * 32 + 32, :].astype(F32)) * COLS
        row = row + jnp.where(column == h, part, 0.0)
    return row, bce


def forward_body(small, contact_head, weights, s, f, ready, tick, emit):
    emb, in_row, out_row, in_col, out_col = weights[:5]
    up_parts, down_parts = weights[5:7], weights[7:9]
    ready(-1)
    read_tokens(small, f)
    _, block = position()
    shift = lax.rem(128 - lax.rem(block, 4) * 32, 128)
    window = pl.ds(pl.multiple_of((block // 4) * 128, 128), 128)
    hot_ri = local_hot(f.ids[:, window], shift)
    goal_ri = local_hot(f.targets[...], shift)
    s.hot_ri[...] = hot_ri
    for r in range(ROWS):
        row = f.ids[r : r + 1, :]
        s.hot_all[r * VP : r * VP + VP, :] = one_zero(row == iota((VP, COLS), 0)).astype(BF16)
    shape = (HERE, HERE)
    back = (
        ((iota(shape, 1) >> 4) == (iota(shape, 0) & 31))
        & ((iota(shape, 1) & 15) == (iota(shape, 0) >> 5))
    )
    back = one_zero(back).astype(BF16)
    hot_ir = nn(hot_ri, back).astype(BF16)
    s.hot_ir[...] = hot_ir
    goal = nn(goal_ri, back)
    entries = jnp.zeros((4, 128), F32)
    labelled = jnp.zeros((1, 128), F32)
    for d in range(32):
        entries = entries + one_zero(small[d, 0:4, :] == MASK_ID)
        labelled = labelled + one_zero(small[d, 10:11, :] >= 0)
    entries, labelled = total_of(entries), total_of(labelled)

    ready(0)
    table = emb[0].astype(F32).T[:VP]
    norms = emb[1].astype(F32).T[:8]
    s.table[...] = table
    s.norms[...] = norms
    table_low = table.astype(BF16)

    def vector(number):
        return norms[number : number + 1, :]

    unit_t, _ = norm_stats(table)
    normed_t = (unit_t * vector(0) + vector(4)).astype(BF16)
    ready(1)
    for half in range(2):
        s.proj_t[:, half * 1152 : half * 1152 + 1152] = nn(normed_t, in_row[half]).astype(BF16)
    pair_parts = []
    for hp in range(PAIRS):
        lanes = slice(hp * 128, hp * 128 + 128)
        key = s.proj_t[:, D + hp * 128 : D + hp * 128 + 128]
        value = s.proj_t[:, 2 * D + hp * 128 : 2 * D + hp * 128 + 128]
        s.value_two[hp] = stacked(value)
        pair_parts.append(nt(s.proj_t[:, lanes], stacked(key)))
    pair_hi, pair_lo = split_two(jnp.concatenate(pair_parts, 1))
    f.lookup[...] = tn(hot_ri, pair_hi) + tn(hot_ri, pair_lo)
    split_heads_to(f.lookup, f.left_hi, f.left_lo)
    tick(6)
    hot_all = s.hot_all[...]
    score = (nn(f.left_hi[...], hot_all) + nn(f.left_lo[...], hot_all)) * (HD * ROWS) ** (-0.5)
    score = jnp.exp(score - jnp.max(score, -1, keepdims=True))
    prob = score / jnp.sum(score, -1, keepdims=True)
    s.prob[...] = prob
    f.prob_low[...] = prob.astype(BF16)
    merge_heads(f.prob_low[...], s.hot_all, s.weight_hi, f.weight_lo)
    for hp in range(PAIRS):
        lanes = slice(hp * 128, hp * 128 + 128)
        value = s.value_two[hp]
        f.mixed[:, lanes] = (nn(s.weight_hi[:, lanes], value) + nn(f.weight_lo[:, lanes], value)).astype(BF16)
    ahead = (
        ((iota(shape, 0) >> 4) == (iota(shape, 1) & 31))
        & ((iota(shape, 0) & 15) == (iota(shape, 1) >> 5))
    )
    f.mixed[...] = nn(one_zero(ahead).astype(BF16), f.mixed[...]).astype(BF16)
    transpose_into(f.mixed, s.row_mixed_t)
    s.stream[...] = tn(hot_ir, table_low)
    tick(7)
    contact_row, bce = contact_part(contact_head, f, s, labelled)
    emit(AT.hot_all, AT.hot_ri, AT.hot_ir, AT.table, AT.norms, AT.proj_t, AT.value_two, AT.prob, AT.weight_hi, AT.row_mixed_t, AT.touch)

    ready(2)
    for half in range(2):
        lanes = slice(half * 384, half * 384 + 384)
        s.stream[:, lanes] += nn(f.mixed[...], out_row[half])
    norm_rows(s.stream, vector(1), vector(5), s.unit_1, s.rstd_1, f.normed)
    transpose_into(f.normed, s.col_normed_t)
    emit(AT.unit_1, AT.rstd_1, AT.col_normed_t)
    ready(3)

    def project(half, at):
        s.col_proj[:, pl.ds(pl.multiple_of(half * 1152 + at, 128), 384)] = nn(
            f.normed[...], in_col[half, :, pl.ds(at, 384)]
        ).astype(BF16)

    over_tiles(1152, 384, project)
    emit(AT.col_proj)

    def attend(at, carry):
        rows = pl.ds(pl.multiple_of((at // PAIRS) * 128, 128), 128)
        lane = lax.rem(at, PAIRS) * 128

        def lanes(part):
            return pl.ds(pl.multiple_of(part * D + lane, 128), 128)

        query = stacked(s.col_proj[rows, lanes(0)])
        score = nt(query, s.col_proj[rows, lanes(1)]) * HD ** (-0.5)
        score = jnp.where(column_mask(), score, -1e30)
        score = jnp.exp(score - jnp.max(score, -1, keepdims=True))
        prob = score / jnp.sum(score, -1, keepdims=True)
        s.col_prob[at] = prob
        mixed = nn(prob.astype(BF16), s.col_proj[rows, lanes(2)])
        f.mixed[rows, lanes(0)] = unstacked(mixed, 128).astype(BF16)
        return carry

    lax.fori_loop(0, 2 * PAIRS, attend, 0, unroll=2)
    tick(8)
    lax.fori_loop(2 * PAIRS, 4 * PAIRS, attend, 0, unroll=2)
    transpose_into(f.mixed, s.col_mixed_t)
    emit(AT.col_prob, AT.col_mixed_t)
    ready(4)
    for half in range(2):
        lanes = slice(half * 384, half * 384 + 384)
        s.stream[:, lanes] += nn(f.mixed[...], out_col[half])
    norm_rows(s.stream, vector(2), vector(6), s.unit_2, s.rstd_2, f.normed)
    transpose_into(f.normed, s.feed_normed_t)
    emit(AT.unit_2, AT.rstd_2, AT.feed_normed_t)
    for part in range(2):
        ready(5 + part)

        def widen(half, at, part=part):
            lanes = pl.ds(pl.multiple_of(part * 1536 + half * 768 + at, 128), UP_TILE)
            up = nn(f.normed[...], up_parts[part][half, :, pl.ds(at, UP_TILE)])
            active, slope = gelu_parts(up)
            s.active[:, lanes] = active.astype(BF16)
            s.slope[:, lanes] = slope.astype(BF16)

        over_tiles(768, UP_TILE, widen)
    emit(AT.active, AT.slope)
    for part in range(2):
        ready(7 + part)
        for half in range(2):
            start = part * 1536 + half * 768
            s.stream[...] += nt(s.active[:, start : start + 768], down_parts[part][half])
    norm_rows(s.stream, vector(3), vector(7), f.unit, f.rstd, f.normed)
    logits = nt(table_low, f.normed[...]) * D ** (-0.5)
    vocab = iota((VP, HERE), 0)
    logits = jnp.where(vocab < VOCAB, logits, -1e30)
    shifted = logits - jnp.max(logits, 0, keepdims=True)
    log_probs = shifted - jnp.log(jnp.sum(jnp.exp(shifted), 0, keepdims=True))
    keep = hot_ir[MASK_ID : MASK_ID + 1].astype(F32) > 0.5
    mlm = -total_of(jnp.where(keep & (goal > 0.5), log_probs, 0.0))
    logit_grad = jnp.where(keep, jnp.exp(log_probs) - goal, 0.0) / entries
    logit_low = (logit_grad * D ** (-0.5)).astype(BF16)
    s.grad_head[...] = nn(logit_low, f.normed[...])
    f.lookup[...] = tn(logit_low, table_low)
    scale_3, shift_3 = back_rows(f.unit, f.rstd, vector(3), f.lookup, s.stream, f.normed, True)
    emit(AT.stream)
    line = iota((8, D), 0)
    s.moved[...] = jnp.where(line == 0, scale_3, jnp.where(line == 1, shift_3, 0.0))
    column = iota((1, 128), 1)
    row = contact_row + jnp.where(column == HEADS + 1, mlm, 0.0) + jnp.where(column == HEADS + 2, bce, 0.0)
    counted = jnp.where(column == 0, entries, 0.0) + jnp.where(column == 1, labelled, 0.0)
    line = iota((8, 128), 0)
    s.extras[...] = jnp.where(line == 0, row, jnp.where(line == 1, counted, 0.0))
    emit(AT.grad_head, AT.extras, AT.moved)


def back_rows(unit_ref, rstd_ref, gain, upstream_ref, stream_ref, low_ref, first):
    def body(at, carry):
        scale, move = carry
        rows = pl.ds(pl.multiple_of(at * 32, 32), 32)
        upstream = upstream_ref[rows, :]
        unit = unit_ref[rows, :]
        inner = upstream * gain
        mean = jnp.sum(inner, -1, keepdims=True) * (1.0 / D)
        along = jnp.sum(inner * unit, -1, keepdims=True) * (1.0 / D)
        grad = rstd_ref[rows, 0:1] * (inner - mean - unit * along)
        if not first:
            grad = grad + stream_ref[rows, :]
        stream_ref[rows, :] = grad
        low_ref[rows, :] = grad.astype(BF16)
        touched = upstream * unit
        for n in range(4):
            scale = scale + touched[n * 8 : n * 8 + 8]
            move = move + upstream[n * 8 : n * 8 + 8]
        return scale, move

    zero = jnp.zeros((8, D), F32)
    scale, move = lax.fori_loop(0, HERE // 32, body, (zero, zero))
    return jnp.sum(scale, 0, keepdims=True), jnp.sum(move, 0, keepdims=True)


WIDTHS = (128, 1152, 384, 1152, 384, 768, 768, 768, 768)


def forward_kernel(*refs):
    widths = WIDTHS
    count = len(widths)
    small, contact_head, emb, in_w, out_w, up_w, down_w = refs[:7]
    given = (
        (emb, None, 0), (in_w, 0, 0), (out_w, 0, 0), (in_w, 1, 0), (out_w, 1, 0),
        (up_w, None, 0), (up_w, None, 1536), (down_w, None, 0), (down_w, None, 1536),
    )

    def master(m, side):
        ref, number, start = given[m]
        lanes = slice(start + side * widths[m], start + side * widths[m] + widths[m])
        return ref[:, lanes] if number is None else ref[number, :, lanes]

    at = 7
    far = refs[at : at + count]
    saved_far = refs[at + count : at + count + len(SAVED)]
    at += count + len(SAVED)
    outs = refs[at : at + count]
    outgoing = refs[at + count : at + 2 * count]
    incoming = refs[at + 2 * count : at + 3 * count]
    piece = refs[at + 3 * count : at + 4 * count]
    at += 4 * count
    saved = Saved(*refs[at : at + len(SAVED)])
    at += len(SAVED)
    scratch = Forward(*refs[at : at + len(FORWARD)])
    small_out, small_send, small_recv, send, recv, local, out_sem = refs[at + len(FORWARD) :]
    z, y, k, c = place()
    me = (z * 4 + y * 2 + k) * 2 + c
    barrier = greet_all()
    for m in range(count):
        n = widths[m]
        other = jnp.where(c == 0, master(m, 1), master(m, 0))
        outgoing[m][...] = jnp.concatenate([other, jnp.zeros((8, n), F32)], 0).astype(BF16)
    pl.semaphore_wait(barrier, 31)

    def small_copy(step):
        other = lax.rem(me + step, 32)
        return remote(
            small, small_out.at[me], small_send.at[step], small_recv.at[step], (other // 2, lax.rem(other, 2))
        )

    def spread(step, carry):
        small_copy(step).start()
        return carry

    across, beside, twin = device(z, y, k, 1 - c), device(z, 1 - y, k, c), device(z, y, 1 - k, c)

    def copy(m, at, src, dst, target):
        return remote(src, dst, send.at[m, at], recv.at[m, at], target)

    def pair_copy(m):
        return copy(m, 0, outgoing[m], incoming[m], across)

    def own_copy(m):
        return pltpu.make_async_copy(piece[m], outs[m].at[c, z, y, k], local.at[m])

    def line_copy(m, step):
        return copy(m, step, piece[m], outs[m].at[c, z, y, k], device(lax.rem(z + step, 4), y, k, c))

    def same(m, at, where, target):
        view = outs[m].at[where]
        return copy(m, at, view, view, target)

    low, high = pl.ds(0, 2), pl.ds(2, 2)

    def second(m):
        return [same(m, 4, (c, low, y, k), across), same(m, 5, (c, high, y, k), beside)]

    def third_own(m):
        return [same(m, 6, (c, low, y, k), beside), same(m, 7, (c, high, y, k), across)]

    def third_far(m):
        return [same(m, 8, (1 - c, low, y, k), beside), same(m, 9, (c, high, 1 - y, k), across)]

    def twin_own(m):
        return [same(m, 10, (c, slice(None), y, k), twin)]

    def twin_second(m):
        return [same(m, 11, (1 - c, low, y, k), twin), same(m, 12, (c, high, 1 - y, k), twin)]

    def twin_third(m):
        return [
            same(m, 13, (c, low, 1 - y, k), twin),
            same(m, 14, (1 - c, high, y, k), twin),
            same(m, 15, (1 - c, low, 1 - y, k), twin),
            same(m, 16, (1 - c, high, 1 - y, k), twin),
        ]

    for m in range(count):
        pair_copy(m).start()
    lax.fori_loop(1, 32, spread, 0)
    small_out[me] = small[...]

    def stage_line(m):
        pair_copy(m).wait_recv()
        mine = jnp.where(c == 0, master(m, 0), master(m, 1))
        theirs = incoming[m][...].astype(F32)[:24]
        top = jnp.where(c == 0, mine, theirs)
        bottom = jnp.where(c == 0, theirs, mine)
        piece[m][...] = jnp.concatenate([top, bottom], 0).astype(BF16)
        own_copy(m).start()
        for step in (1, 3, 2):
            line_copy(m, step).start()

    def stage_second(m):
        own_copy(m).wait()
        for step in (1, 3, 2):
            line_copy(m, step).wait_recv()
        for item in second(m) + third_own(m) + twin_own(m):
            item.start()

    def stage_third(m):
        for item in second(m):
            item.wait_recv()
        for item in third_far(m) + twin_second(m):
            item.start()

    def stage_twin(m):
        for item in third_own(m) + third_far(m):
            item.wait_recv()
        for item in twin_third(m):
            item.start()

    def stage_end(m):
        for item in twin_own(m) + twin_second(m) + twin_third(m):
            item.wait_recv()

    stages = (stage_line, stage_end, stage_twin, stage_third, stage_second)
    late = (-1, 4, 3, 2, 1)
    pending = []
    for number in range(count + 4):
        todo = [(stage_line, 0)] if number == 0 else []
        for stage, behind in zip(stages, late):
            if 0 <= number - behind < count:
                todo.append((stage, number - behind))
        pending.append(todo)

    def tick(last):
        while len(pending) > count + 3 - last:
            for stage, m in pending.pop(0):
                stage(m)

    def far_copy(m):
        return pltpu.make_async_copy(outs[m], far[m], local.at[m])

    def ready(m):
        if m < 0:
            lax.fori_loop(1, 32, finish, 0)
            return
        tick(m + 4)
        far_copy(m).start()

    def out_copy(at):
        return pltpu.make_async_copy(saved[at], saved_far[at], out_sem.at[at])

    def emit(*numbers):
        for number in numbers:
            out_copy(number).start()

    def finish(step, carry):
        small_copy(step).wait()
        return carry

    tick(1)
    views = [w.reshape(2, D, n) for w, n in zip(outs, widths)]
    forward_body(small_out, contact_head, views, saved, scratch, ready, tick, emit)
    for m in range(count):
        pair_copy(m).wait_send()
        for step in (1, 2, 3):
            line_copy(m, step).wait_send()
        for item in second(m) + third_own(m) + third_far(m) + twin_own(m) + twin_second(m) + twin_third(m):
            item.wait_send()

    for m in range(count):
        far_copy(m).wait()
    for at in range(len(SAVED)):
        out_copy(at).wait()


def forward_call(small, contact_head, masters):
    count = len(WIDTHS)
    inside = pl.BlockSpec(memory_space=pltpu.VMEM)
    anywhere = pl.BlockSpec(memory_space=pl.ANY)
    shapes = [(2, NZ, NY, 2, 48, n) for n in WIDTHS]
    outs = pl.pallas_call(
        forward_kernel,
        out_shape=[jax.ShapeDtypeStruct(shape, BF16) for shape in shapes]
        + [jax.ShapeDtypeStruct(*item) for item in SAVED],
        in_specs=[inside, pl.BlockSpec(memory_space=pltpu.SMEM)] + [inside] * 5,
        out_specs=[anywhere] * (count + len(SAVED)),
        scratch_shapes=[pltpu.VMEM(shape, BF16) for shape in shapes]
        + [pltpu.VMEM((32, n), BF16) for n in WIDTHS] * 2
        + [pltpu.VMEM((48, n), BF16) for n in WIDTHS]
        + [pltpu.VMEM(*item) for item in SAVED]
        + [pltpu.VMEM(*item) for item in FORWARD]
        + [
            pltpu.VMEM((32, *small.shape), jnp.int32),
            pltpu.SemaphoreType.DMA((32,)),
            pltpu.SemaphoreType.DMA((32,)),
            pltpu.SemaphoreType.DMA((count, 17)),
            pltpu.SemaphoreType.DMA((count, 17)),
            pltpu.SemaphoreType.DMA((count,)),
            pltpu.SemaphoreType.DMA((len(SAVED),)),
        ],
        compiler_params=pltpu.CompilerParams(
            collective_id=0, has_side_effects=True, vmem_limit_bytes=62 * 2**20
        ),
    )(small, contact_head, *masters)
    return outs[:count], Saved(*outs[count:])


def summed_rows(sums, start, groups, rows):
    parts = [
        jnp.concatenate([sums[2 * (start + g)], sums[2 * (start + g) + 1]], 1) for g in range(groups)
    ]
    if rows > 8 * groups:
        parts.append(jnp.zeros((rows - 8 * groups, D), F32))
    return jnp.concatenate(parts, 0) if len(parts) > 1 else parts[0]


def table_finish(sums, table_ref, norms_ref, proj_t, in_row, g_in, g_emb, g_norm):
    z, y, k, c = place()
    me = (z * 4 + y * 2 + k) * 2 + c
    pair = summed_rows(sums, 0, 5, VP)
    value_grad = summed_rows(sums, 5, 5, VP)
    table_grad = summed_rows(sums, 10, 5, VP)
    vectors = summed_rows(sums, 15, 1, 8)
    pair_hi, pair_lo = split_two(pair)
    scale = (HD * ROWS) ** (-0.5)
    query_grad, key_grad = [], []
    for hp in range(PAIRS):
        lanes = slice(hp * 128, hp * 128 + 128)
        query = proj_t[:, lanes]
        key = stacked(proj_t[:, D + hp * 128 : D + hp * 128 + 128])
        high, low = pair_hi[:, lanes], pair_lo[:, lanes]
        query_grad.append((nn(high, key) + nn(low, key)) * scale)
        key_grad.append(unstacked(tn(high, query) + tn(low, query), VP) * scale)
    proj_hi, proj_lo = split_two(jnp.concatenate(query_grad + key_grad + [value_grad], 1))
    normed_grad = jnp.zeros((VP, D), F32)
    for half in range(2):
        lanes = slice(half * 1152, half * 1152 + 1152)
        matrix = in_row[half]
        normed_grad = normed_grad + nt(proj_hi[:, lanes], matrix) + nt(proj_lo[:, lanes], matrix)
    unit, rstd = norm_stats(table_ref[...])
    gain = norms_ref[0:1, :]
    back, scale_0, shift_0 = norm_back(unit, rstd, gain, normed_grad)
    table_grad = table_grad + back
    line = iota((16, D), 0)
    norm_grad = jnp.zeros((16, D), F32)
    rows = [scale_0[None]] + [vectors[n : n + 1] for n in range(3)]
    rows += [shift_0[None]] + [vectors[n : n + 1] for n in range(3, 6)]
    for number, row in enumerate(rows):
        norm_grad = jnp.where(line == number, row, norm_grad)
    shard = D // 32
    pick = one_zero(iota((shard, D), 1) == iota((shard, D), 0) + me * shard).astype(BF16)
    normed = (unit * gain + norms_ref[4:5, :]).astype(BF16)
    mine = nt(pick, normed).astype(BF16)
    in_grad = nn(mine, proj_hi) + nn(mine, proj_lo)
    g_in[...] = in_grad

    def three(values):
        top, rest = split_two(values)
        return top, rest, (values - top.astype(F32) - rest.astype(F32)).astype(BF16)

    emb_grad = sum(nt(pick, part) for part in three(table_grad))
    g_emb[...] = emb_grad
    own_norm = sum(nt(part, pick) for part in three(norm_grad))[:8]
    g_norm[...] = own_norm
    return total_of(in_grad * in_grad) + total_of(emb_grad * emb_grad) + total_of(own_norm * own_norm)


GRAD_WIDTHS = (768, 768, 768, 768, 384, 1152, 384)


class Kept(typing.NamedTuple):
    stream: typing.Any
    norms: typing.Any
    table: typing.Any
    proj_t: typing.Any
    extras: typing.Any
    moved: typing.Any
    grad_head: typing.Any
    touch: typing.Any
    value_two: typing.Any


class Early(typing.NamedTuple):
    slope: typing.Any
    active: typing.Any
    feed_normed_t: typing.Any
    unit_2: typing.Any
    rstd_2: typing.Any
    col_mixed_t: typing.Any
    col_proj: typing.Any
    col_prob: typing.Any
    col_normed_t: typing.Any
    unit_1: typing.Any
    rstd_1: typing.Any


class Late(typing.NamedTuple):
    row_mixed_t: typing.Any
    hot_all: typing.Any
    weight_hi: typing.Any
    prob: typing.Any
    hot_ri: typing.Any
    hot_ir: typing.Any


def pick_items(group, source):
    return [getattr(source, name) for name in group._fields]


def backward_kernel(*refs):
    widths = GRAD_WIDTHS
    count = len(widths)
    contact_head = refs[0]
    far = refs[1 : 1 + count]
    in_row_far = refs[1 + count]
    saved = Saved(*refs[2 + count : 2 + count + len(SAVED)])
    at = 2 + count + len(SAVED)
    outs = refs[at : at + count]
    g_in, g_emb, g_norm, stats = refs[at + count : at + count + 4]
    at += count + 4
    grads = refs[at : at + count]
    kept = Kept(*refs[at + count : at + count + len(Kept._fields)])
    at += count + len(Kept._fields)
    upstream, branch, branch_t, mixed = refs[at : at + 4]
    scratch = refs[at + 4 :]
    got_0, got_1a, got_1b, got_2a, got_2b, got_3, total, got_4 = (
        scratch[i * count : (i + 1) * count] for i in range(8)
    )
    table, table_out, table_got, square, square_got = scratch[8 * count : 8 * count + 5]
    table_send, table_recv, send, recv, local = scratch[8 * count + 5 :]
    z, y, k, c = place()
    me = (z * 4 + y * 2 + k) * 2 + c
    across, beside, twin = device(z, y, k, 1 - c), device(z, 1 - y, k, c), device(z, y, 1 - k, c)
    barrier = greet_all()
    stream = kept.stream

    copies = {}

    def load(number, source, target):
        copies[number] = pltpu.make_async_copy(source, target, local.at[number])
        copies[number].start()

    def need(*numbers):
        for number in numbers:
            copies[number].wait()

    def weight(m):
        return len(SAVED) + m

    def copy(m, at, src, dst, target):
        return remote(src, dst, send.at[m, at], recv.at[m, at], target)

    def twin_copy(m):
        return copy(m, 0, grads[m].at[:, :, :, 1 - k], got_0[m], twin)

    low, high = pl.ds(0, 2), pl.ds(2, 2)
    every = slice(None)

    def first(m):
        return [
            copy(m, 1, grads[m].at[:, low, 1 - y, k], got_1a[m], beside),
            copy(m, 2, grads[m].at[1 - c, high, :, k], got_1b[m], across),
        ]

    def second(m):
        return [
            copy(m, 3, grads[m].at[1 - c, low, y, k], got_2a[m], across),
            copy(m, 4, grads[m].at[c, high, 1 - y, k], got_2b[m], beside),
        ]

    def along(m):
        return [
            copy(
                m,
                4 + step,
                grads[m].at[c, lax.rem(z + step, 4), y, k],
                got_3[m].at[step - 1],
                device(lax.rem(z + step, 4), y, k, c),
            )
            for step in (1, 3, 2)
        ]

    def pair(m):
        return [copy(m, 8, total[m].at[1 - c], got_4[m], across)]

    def table_copy(step, back):
        other = lax.rem(me + step, 32)
        target = (other // 2, lax.rem(other, 2))
        if back:
            return remote(
                table_out.at[me], table_out.at[me], table_send.at[1, step], table_recv.at[1, step], target
            )
        return remote(
            table.at[other], table_got.at[me], table_send.at[0, step], table_recv.at[0, step], target
        )

    def each(action):
        def body(step, carry):
            action(step)
            return carry

        lax.fori_loop(1, 32, body, 0)

    def plus(left, right):
        return (left.astype(F32) + right.astype(F32)).astype(BF16)

    def add_into(m, where, value):
        grads[m][where] = plus(grads[m][where], value)

    def stage_first(m):
        twin_copy(m).wait_recv()

        def body(at, carry):
            zz, yy = at // 2, lax.rem(at, 2)
            for cc in range(2):
                add_into(m, (cc, zz, yy, k), got_0[m][cc, zz, yy])
            return carry

        lax.fori_loop(0, NZ * NY, body, 0)
        for item in first(m):
            item.start()

    def stage_second(m):
        for item in first(m):
            item.wait_recv()
        for a in range(2):
            for b in range(2):
                add_into(m, (a, b, y, k), got_1a[m][a, b])
                add_into(m, (c, 2 + a, b, k), got_1b[m][a, b])
        for item in second(m):
            item.start()

    def stage_along(m):
        for item in second(m):
            item.wait_recv()
        for a in range(2):
            add_into(m, (c, a, y, k), got_2a[m][a])
            add_into(m, (c, 2 + a, y, k), got_2b[m][a])
        for item in along(m):
            item.start()

    def stage_pair(m):
        for item in along(m):
            item.wait_recv()
        full = grads[m][c, z, y, k].astype(F32)
        for step in range(3):
            full = full + got_3[m][step].astype(F32)
        total[m][0] = full[:24]
        total[m][1] = full[24:]
        for item in pair(m):
            item.start()

    def stage_end(m):
        outs[m][c] = total[m][c]
        for item in pair(m):
            item.wait_recv()
        outs[m][1 - c] = got_4[m][...]

    stages = (stage_first, stage_second, stage_along, stage_pair, stage_end)
    reached = {}

    def tick():
        for m in sorted(reached):
            if reached[m] < len(stages):
                stages[reached[m]](m)
                reached[m] += 1

    def done(m):
        if m == 0:
            pl.semaphore_wait(barrier, 31)
        tick()
        twin_copy(m).start()
        reached[m] = 0

    names = Kept._fields
    for name in names:
        load(getattr(AT, name), getattr(saved, name), getattr(kept, name))

    def phase_one(*early_refs):
        e = Early(*early_refs)
        load(weight(0), far[0], grads[0])
        load(AT.slope, saved.slope, e.slope)
        load(AT.active, saved.active, e.active)
        for m in (1, 2, 3):
            load(weight(m), far[m], grads[m])
        for name in Early._fields[2:6]:
            load(getattr(AT, name), getattr(saved, name), getattr(e, name))
        load(weight(4), far[4], grads[4])
        for name in Early._fields[6:8]:
            load(getattr(AT, name), getattr(saved, name), getattr(e, name))
        load(weight(5), far[5], grads[5])
        for name in Early._fields[8:]:
            load(getattr(AT, name), getattr(saved, name), getattr(e, name))
        load(weight(6), far[6], grads[6])
        view = [g.reshape(2, D, n) for g, n in zip(grads, widths)]
        need(*(getattr(AT, name) for name in names))
        norms = kept.norms[...]

        def gain(number):
            return norms[number : number + 1, :]

        def narrow(at, carry):
            rows = pl.ds(pl.multiple_of(at * 32, 32), 32)
            branch[rows, :] = stream[rows, :].astype(BF16)
            return carry

        lax.fori_loop(0, HERE // 32, narrow, 0)
        transpose_into(branch, branch_t)

        def grad_tiles(m, start, left_t, right):
            def body(half, at):
                lanes = pl.ds(pl.multiple_of(start + half * widths[m] + at, 128), 384)
                view[m][half, :, pl.ds(at, 384)] = nn(left_t[...], right[:, lanes]).astype(BF16)

            over_tiles(widths[m], 384, body)

        for part in range(2):
            need(weight(part))
            if part == 0:
                need(AT.slope)

            def down_back(half, at, part=part):
                lanes = pl.ds(pl.multiple_of(part * 1536 + half * 768 + at, 128), 384)
                back = nn(branch[...], view[part][half, :, pl.ds(at, 384)])
                e.slope[:, lanes] = (back * e.slope[:, lanes].astype(F32)).astype(BF16)

            over_tiles(768, 384, down_back)
            if part == 0:
                need(AT.active)
            grad_tiles(part, part * 1536, branch_t, e.active)
            done(part)
        for part in range(2):
            need(weight(2 + part))
            for half in range(2):
                start = part * 1536 + half * 768
                back = nt(e.slope[:, start : start + 768], view[2 + part][half])
                upstream[...] = back if start == 0 else upstream[...] + back
            if part == 0:
                need(AT.feed_normed_t)
            grad_tiles(2 + part, part * 1536, e.feed_normed_t, e.slope)
            done(2 + part)
        need(AT.unit_2, AT.rstd_2)
        scale_2, shift_2 = back_rows(e.unit_2, e.rstd_2, gain(2), upstream, stream, branch, False)
        need(weight(4), AT.col_mixed_t)
        mixed[...] = (nt(branch[:, :384], view[4][0]) + nt(branch[:, 384:], view[4][1])).astype(BF16)
        grad_tiles(4, 0, e.col_mixed_t, branch)
        done(4)
        need(AT.col_proj, AT.col_prob)
        proj = e.active

        def attend(at, carry):
            rows = pl.ds(pl.multiple_of((at // PAIRS) * 128, 128), 128)
            lane = lax.rem(at, PAIRS) * 128

            def lanes(part):
                return pl.ds(pl.multiple_of(part * D + lane, 128), 128)

            query = stacked(e.col_proj[rows, lanes(0)])
            key = e.col_proj[rows, lanes(1)]
            value = e.col_proj[rows, lanes(2)]
            above = stacked(mixed[rows, lanes(0)])
            prob = e.col_prob[at]
            grad = nt(above, value)
            grad = prob * (grad - jnp.sum(prob * grad, -1, keepdims=True))
            small = grad.astype(BF16)
            scale = HD ** (-0.5)
            proj[rows, lanes(0)] = (unstacked(nn(small, key), 128) * scale).astype(BF16)
            proj[rows, lanes(1)] = (tn(small, query) * scale).astype(BF16)
            proj[rows, lanes(2)] = tn(prob.astype(BF16), above).astype(BF16)
            return carry

        for part in range(3):
            lax.fori_loop(8 * part, 8 * part + 8, attend, 0, unroll=2)
            if part < 2:
                tick()
        need(weight(5))
        for half in range(2):
            back = nt(proj[:, half * 1152 : half * 1152 + 1152], view[5][half])
            upstream[...] = back if half == 0 else upstream[...] + back
        need(AT.col_normed_t)
        grad_tiles(5, 0, e.col_normed_t, proj)
        done(5)
        need(AT.unit_1, AT.rstd_1)
        scale_1, shift_1 = back_rows(e.unit_1, e.rstd_1, gain(1), upstream, stream, branch, False)
        need(weight(6))
        mixed[...] = (nt(branch[:, :384], view[6][0]) + nt(branch[:, 384:], view[6][1])).astype(BF16)
        line = iota((8, D), 0)
        vectors = jnp.zeros((8, D), F32)
        moved = kept.moved[...]
        rows = (scale_1, scale_2, moved[0:1], shift_1, shift_2, moved[1:2])
        for number, row in enumerate(rows):
            vectors = jnp.where(line == number, row, vectors)
        extras = jnp.concatenate([kept.extras[0:1, :], jnp.zeros((1, D - 128), F32)], 1)
        kept.moved[...] = jnp.where(line == 6, extras, vectors)

    pl.run_scoped(phase_one, *(pltpu.VMEM(*item) for item in pick_items(Early, SAVED)))

    def phase_two(*late_refs):
        e = Late(*late_refs[:-3])
        in_row, left_hi, left_lo = late_refs[-3:]
        for name in Late._fields:
            load(getattr(AT, name), getattr(saved, name), getattr(e, name))
        load(weight(count), in_row_far, in_row)
        view = grads[6].reshape(2, D, widths[6])
        tick()
        need(AT.row_mixed_t)
        for half in range(2):
            lanes = slice(half * 384, half * 384 + 384)
            view[half] = nn(e.row_mixed_t[...], branch[:, lanes]).astype(BF16)
        done(6)
        need(AT.hot_all, AT.weight_hi, AT.prob, AT.hot_ri, AT.hot_ir)
        shape = (HERE, HERE)
        back = (
            ((iota(shape, 1) >> 4) == (iota(shape, 0) & 31))
            & ((iota(shape, 1) & 15) == (iota(shape, 0) >> 5))
        )
        mixed[...] = nn(one_zero(back).astype(BF16), mixed[...]).astype(BF16)
        value_rows = []
        for hp in range(PAIRS):
            lanes = slice(hp * 128, hp * 128 + 128)
            part = mixed[:, lanes]
            upstream[:, lanes] = nt(part, kept.value_two[hp])
            value_rows.append(unstacked(tn(e.weight_hi[:, lanes], part), 64))
        split_heads_to(upstream, left_hi, left_lo)
        hot_all = e.hot_all[...]
        grad = nn(left_hi[...], hot_all) + nn(left_lo[...], hot_all)
        extra = jnp.concatenate(
            [kept.touch[...] * (contact_head[h] * COLS) for h in range(HEADS)], 0
        )
        grad = grad + extra
        prob = e.prob[...]
        grad = prob * (grad - jnp.sum(prob * grad, -1, keepdims=True))
        tick()
        merge_heads(grad.astype(BF16), e.hot_all, branch, None)
        table_pair = nn(e.hot_ri[...], branch[...])
        stream_hi, stream_lo = split_two(stream[...])
        hot_ir = e.hot_ir[...]
        table_grad = kept.grad_head[...] + nn(hot_ir, stream_hi) + nn(hot_ir, stream_lo)
        value_grad = jnp.concatenate(value_rows, 1)
        blocks = ((0, table_pair), (5, value_grad), (10, table_grad), (15, kept.moved[...]))
        for start, block in blocks:
            for group in range(min(5, block.shape[0] // 8)):
                for half in range(2):
                    table[2 * (start + group) + half] = block[
                        group * 8 : group * 8 + 8, half * 384 : half * 384 + 384
                    ]
        each(lambda step: table_copy(step, False).start())
        tick()
        table_got[me] = table[me]
        each(lambda step: table_copy(step, False).wait_recv())
        table_out[me] = lax.fori_loop(1, 32, lambda at, held: held + table_got[at], table_got[0])
        each(lambda step: table_copy(step, True).start())
        tick()
        each(lambda step: table_copy(step, True).wait_recv())
        need(weight(count))
        square[...] = jnp.broadcast_to(
            table_finish(
                table_out, kept.table, kept.norms, kept.proj_t, in_row.reshape(2, D, 1152), g_in, g_emb, g_norm
            ),
            (8, 128),
        )

    pl.run_scoped(
        phase_two,
        *(pltpu.VMEM(*item) for item in pick_items(Late, SAVED)),
        pltpu.VMEM((2, NZ, NY, 2, 48, 1152), BF16),
        pltpu.VMEM((HEADS * WIDE, ROWS * VP), BF16),
        pltpu.VMEM((HEADS * WIDE, ROWS * VP), BF16),
    )
    while any(at < len(stages) for at in reached.values()):
        tick()
    local_square = jnp.zeros((1, 1), F32)
    for m in range(count):
        for half in range(2):
            local_square = local_square + total_of(outs[m][half] * outs[m][half])

    def square_copy(step):
        other = lax.rem(me + step, 32)
        return remote(
            square, square_got.at[me], table_send.at[2, step], table_recv.at[2, step], (other // 2, lax.rem(other, 2))
        )

    square[...] = square[...] + local_square
    each(lambda step: square_copy(step).start())
    square_got[me] = square[...]
    each(lambda step: square_copy(step).wait())
    total_square = lax.fori_loop(1, 32, lambda at, held: held + square_got[at], square_got[0])[0:1]
    vector = table_out[30, 6:7, :128]
    counted = kept.extras[1:2, :]
    column = iota((1, 128), 1)
    contact = jnp.where(column <= HEADS, vector, 0.0)
    total_square = total_square + total_of(contact * contact)
    grad_norm = jnp.sqrt(total_square)
    factor = jnp.minimum(1.0, MAX_NORM / grad_norm)
    losses = (
        (0, vector[:, HEADS + 1 : HEADS + 2]),
        (1, counted[:, 0:1]),
        (2, vector[:, HEADS + 2 : HEADS + 3]),
        (3, counted[:, 1:2]),
    )
    loss_row = jnp.zeros((1, 128), F32)
    for at, value in losses:
        loss_row = jnp.where(column == at, value, loss_row)
    number = iota((8, 128), 0)
    result = jnp.zeros((8, 128), F32)
    for at, row in enumerate((contact, counted, factor, grad_norm, loss_row)):
        result = jnp.where(number == at, row, result)
    stats[...] = result
    each(lambda step: table_copy(step, True).wait_send())
    each(lambda step: table_copy(step, False).wait_send())
    for m in range(count):
        for item in [twin_copy(m)] + first(m) + second(m) + along(m) + pair(m):
            item.wait_send()


def backward_call(contact_head, weights, in_row, saved):
    widths = GRAD_WIDTHS
    count = len(widths)
    inside = pl.BlockSpec(memory_space=pltpu.VMEM)
    anywhere = pl.BlockSpec(memory_space=pl.ANY)

    def shapes(lead, dtype):
        return [pltpu.VMEM((*lead, n), dtype) for n in widths]

    outs = pl.pallas_call(
        backward_kernel,
        out_shape=[jax.ShapeDtypeStruct((2, 24, n), F32) for n in widths]
        + [
            jax.ShapeDtypeStruct((24, 3 * D), F32),
            jax.ShapeDtypeStruct((24, VP), F32),
            jax.ShapeDtypeStruct((8, 24), F32),
            jax.ShapeDtypeStruct((8, 128), F32),
        ],
        in_specs=[pl.BlockSpec(memory_space=pltpu.SMEM)] + [anywhere] * (1 + count + len(SAVED)),
        out_specs=[inside] * (4 + count),
        scratch_shapes=shapes((2, NZ, NY, 2, 48), BF16)
        + [pltpu.VMEM(*item) for item in pick_items(Kept, SAVED)]
        + [
            pltpu.VMEM((HERE, D), F32),
            pltpu.VMEM((HERE, D), BF16),
            pltpu.VMEM((D, HERE), BF16),
            pltpu.VMEM((HERE, D), BF16),
        ]
        + shapes((2, NZ, NY, 48), BF16)
        + shapes((2, 2, 48), BF16)
        + shapes((2, 2, 48), BF16)
        + shapes((2, 48), BF16)
        + shapes((2, 48), BF16)
        + shapes((3, 48), BF16)
        + shapes((2, 24), F32)
        + shapes((24,), F32)
        + [
            pltpu.VMEM((32, 8, 384), F32),
            pltpu.VMEM((32, 8, 384), F32),
            pltpu.VMEM((32, 8, 384), F32),
            pltpu.VMEM((8, 128), F32),
            pltpu.VMEM((32, 8, 128), F32),
            pltpu.SemaphoreType.DMA((3, 32)),
            pltpu.SemaphoreType.DMA((3, 32)),
            pltpu.SemaphoreType.DMA((count, 9)),
            pltpu.SemaphoreType.DMA((count, 9)),
            pltpu.SemaphoreType.DMA((len(SAVED) + count + 1,)),
        ],
        compiler_params=pltpu.CompilerParams(
            collective_id=1, has_side_effects=True, vmem_limit_bytes=63 * 2**20
        ),
    )(contact_head, *weights, in_row, *saved)
    return outs[:count], outs[count:]


UPDATE_RATES = (LEARN_RATE,) * 4 + (VECTOR_RATE,) * 3


def update_kernel(*refs):
    reduced, g_in, g_emb, g_norm, stats = refs[:7], refs[7], refs[8], refs[9], refs[10]
    states = [refs[11 + 3 * n : 14 + 3 * n] for n in range(7)]
    outs = [refs[32 + 3 * n : 35 + 3 * n] for n in range(7)]
    copies = refs[53:58]
    loss_ref, norm_ref = refs[58:60]
    g_out_col, g_in_col, g_out_row = reduced[4:]
    factor = stats[2:3, 0:1]
    loss_ref[...] = stats[4:5, 0:4]
    norm_ref[...] = stats[3:4, 0:1]

    def update(number, where, grad):
        master, first, second = (ref[where] for ref in states[number])
        new, first, second = adam_update(master, first, second, grad * factor, UPDATE_RATES[number])
        for ref, value in zip(outs[number], (new, first, second)):
            ref[where] = value
        if number < 5:
            copies[number][where] = new.astype(BF16)

    every = slice(None)
    for half in range(2):
        lanes = slice(half * 1152, half * 1152 + 1152)
        update(0, (0, every, lanes), g_in[:, lanes])
        update(0, (1, every, lanes), g_in_col[half])
        lanes = slice(half * 384, half * 384 + 384)
        update(1, (0, every, lanes), g_out_row[half])
        update(1, (1, every, lanes), g_out_col[half])
        for part in range(2):
            start = part * 1536 + half * 768
            lanes = slice(start, start + 768)
            update(2, (every, lanes), reduced[2 + part][half])
            update(3, (every, lanes), reduced[part][half])
    update(4, (every, every), g_emb[:, :VOCAB])
    update(5, (every, every), g_norm[...])
    update(6, (every, every), stats[0:1, : HEADS + 1])


def update_call(reduced, g_in, g_emb, g_norm, stats, states):
    inside = pl.BlockSpec(memory_space=pltpu.VMEM)
    flat = [item for state in states for item in state]
    shapes = [jax.ShapeDtypeStruct(item.shape, F32) for item in flat]
    shapes += [jax.ShapeDtypeStruct(states[n][0].shape, BF16) for n in range(5)]
    shapes += [jax.ShapeDtypeStruct((1, 4), F32), jax.ShapeDtypeStruct((1, 1), F32)]
    return pl.pallas_call(
        update_kernel,
        out_shape=shapes,
        in_specs=[inside] * (11 + len(flat)),
        out_specs=[inside] * len(shapes),
        compiler_params=pltpu.CompilerParams(vmem_limit_bytes=48 * 2**20),
    )(*reduced, g_in, g_emb, g_norm, stats, *flat)


def adam_update(master, first, second, grad_part, rate):
    first = BETA_ONE * first + (1.0 - BETA_ONE) * grad_part
    second = BETA_TWO * second + (1.0 - BETA_TWO) * grad_part * grad_part
    moved = first / (1.0 - BETA_ONE**STEP) / (jnp.sqrt(second / (1.0 - BETA_TWO**STEP)) + ADAM_EPS)
    return (master - rate * (moved + WEIGHT_DECAY * master), first, second)


def shards(
    tokens,
    targets,
    masked,
    contact_pairs,
    labels,
    attention_in_master,
    attention_in_first,
    attention_in_second,
    attention_out_master,
    attention_out_first,
    attention_out_second,
    feed_up_master,
    feed_up_first,
    feed_up_second,
    feed_down_master,
    feed_down_first,
    feed_down_second,
    embedding_master,
    embedding_first,
    embedding_second,
    norm_params_master,
    norm_params_first,
    norm_params_second,
    contact_head_master,
    contact_head_first,
    contact_head_second,
):
    both = ("seq", "col")
    micro, rows_here, cols_here = tokens.shape
    ncol = lax.axis_size("col")
    ndev = lax.axis_size("seq") * ncol
    cols = cols_here * ncol
    me = lax.axis_index("seq") * ncol + lax.axis_index("col")
    per = ndev // micro
    cw = cols // per
    mine = me // per
    base = (me % per) * cw
    shard = D // ndev

    tiled = lax.axis_size("seq") == 16 and ncol == 2
    inputs = jnp.where(masked > 0, MASK_ID, tokens)
    masters = [
        jnp.concatenate(
            [
                jnp.pad(embedding_master.T, ((0, 0), (0, 128 - VOCAB))),
                jnp.pad(norm_params_master.T, ((0, 0), (0, 120))),
            ],
            1,
        ),
        attention_in_master[0],
        attention_out_master[0],
        attention_in_master[1],
        attention_out_master[1],
        feed_up_master,
        feed_down_master.T,
    ]
    if tiled:
        small = jnp.concatenate(
            [
                inputs.reshape(4, 128),
                targets.reshape(4, 128),
                contact_pairs[..., 0].reshape(1, 128),
                contact_pairs[..., 1].reshape(1, 128),
                labels.reshape(1, 128),
                jnp.zeros((5, 128), jnp.int32),
            ]
        )
        weights, saved = forward_call(
            small,
            contact_head_master,
            (masters[0], attention_in_master, attention_out_master, feed_up_master, feed_down_master.T),
        )
        reduced, (g_in, g_emb, g_norm, stats) = backward_call(
            contact_head_master, [weights[n] for n in (7, 8, 5, 6, 4, 3, 2)], weights[1], saved
        )
        states = (
            (attention_in_master, attention_in_first, attention_in_second),
            (attention_out_master, attention_out_first, attention_out_second),
            (feed_up_master, feed_up_first, feed_up_second),
            (feed_down_master.T, feed_down_first.T, feed_down_second.T),
            (embedding_master.T, embedding_first.T, embedding_second.T),
            (norm_params_master, norm_params_first, norm_params_second),
            (contact_head_master[None], contact_head_first[None], contact_head_second[None]),
        )
        outs = update_call(reduced, g_in, g_emb, g_norm, stats, states)
        return (
            *outs[:9],
            *(item.T for item in outs[9:15]),
            *outs[15:18],
            *(item[0] for item in outs[18:21]),
            *outs[21:24],
            *(item.T for item in outs[24:26]),
            outs[26][0],
            outs[27][0, 0],
        )
    whole = jnp.stack([inputs, targets])
    whole = lax.all_gather(lax.all_gather(whole, "col", axis=3, tiled=True), "seq", axis=2, tiled=True)
    pairs_all = lax.all_gather(
        jnp.concatenate([contact_pairs, labels[:, :, None]], -1), both, axis=1, tiled=True
    )
    gathered = []
    for master in masters:
        full = lax.all_gather(master.astype(BF16), both, axis=0, tiled=True)
        gathered.append(full.reshape(D, 2, -1).transpose(1, 0, 2))
    counts = (
        jnp.sum(whole[0] == MASK_ID).astype(F32),
        jnp.sum(pairs_all[..., 2] >= 0).astype(F32),
    )
    ids_all = lax.dynamic_index_in_dim(whole[0], mine, 0, False)
    ids_local = lax.dynamic_slice_in_dim(ids_all, base, cw, 1)
    targets_local = lax.dynamic_slice_in_dim(
        lax.dynamic_index_in_dim(whole[1], mine, 0, False), base, cw, 1
    )
    pairs = lax.dynamic_index_in_dim(pairs_all, mine, 0, False)

    table = gathered[0][0][:, :VP].T
    norms = gathered[0][1][:, :8].T.astype(F32)
    in_row, out_row, in_col, out_col, up_w, down_t = (
        jnp.concatenate([g[0], g[1]], 1) for g in gathered[1:]
    )
    big = (in_row, in_col, out_row, out_col, up_w, down_t)

    grads, tables, contact_total, mlm_total, bce_total, kept = step(
        big,
        table,
        norms,
        contact_head_master,
        ids_all,
        ids_local.reshape(-1),
        ids_local.T.reshape(-1),
        targets_local.T.reshape(-1),
        pairs[:, 0] - base,
        pairs[:, 1],
        pairs[:, 2],
        counts,
        cw,
    )
    table_pair, value_grad, table_grad, vectors = tables
    extras = jnp.zeros((2, D), F32).at[0, : HEADS + 3].set(
        jnp.concatenate([contact_total, mlm_total[None], bce_total[None]])
    )
    sums = jnp.concatenate([table_pair[:40], value_grad[:40], table_grad[:40], vectors, extras])
    flat_grad = jnp.concatenate([g.astype(BF16) for g in grads], 1)
    reduced = lax.psum_scatter(flat_grad, both, scatter_dimension=0, tiled=True).astype(F32)
    g_in_col, g_out_row, g_out_col, g_up, g_down = jnp.split(
        reduced, [3 * D, 4 * D, 5 * D, 5 * D + FF], 1
    )
    sums = lax.psum(sums, both)
    unit_t, rstd_t, normed_t, query_t, key_t = kept
    rows_all = ids_all.shape[0]
    spare = ((0, VP - 40), (0, 0))
    table_pair, value_grad, table_grad = (
        jnp.pad(sums[a : a + 40], spare) for a in (0, 40, 80)
    )
    vectors = sums[120:126]
    contact_grad, mlm_total, bce_total = (
        sums[126, : HEADS + 1], sums[126, HEADS + 1], sums[126, HEADS + 2]
    )
    row_scale = (HD * rows_all) ** (-0.5)
    query_grad = []
    key_grad = []
    for h in range(HEADS):
        pair = heads_of(table_pair, h)
        query_grad.append(jnp.dot(pair, heads_of(key_t, h).astype(F32), precision=PRECISE))
        key_grad.append(jnp.dot(pair.T, heads_of(query_t, h).astype(F32), precision=PRECISE))
    proj_grad = jnp.concatenate(
        [
            jnp.concatenate(query_grad, 1) * row_scale,
            jnp.concatenate(key_grad, 1) * row_scale,
            value_grad,
        ],
        1,
    )
    proj_hi, proj_lo = split_two(proj_grad)
    normed_grad = nt(proj_hi, in_row) + nt(proj_lo, in_row)
    back_t, scale_0, shift_0 = norm_back(unit_t, rstd_t, norms[0], normed_grad)
    table_grad = table_grad + back_t
    low = me * shard
    normed_mine = lax.dynamic_slice_in_dim(normed_t, low, shard, 1)
    grad_in_row = tn(normed_mine, proj_hi) + tn(normed_mine, proj_lo)
    norm_grad = jnp.concatenate([scale_0[None], vectors[:3], shift_0[None], vectors[3:]])
    table_mine = lax.dynamic_slice_in_dim(table_grad[:VOCAB], low, shard, 1)
    norm_mine = lax.dynamic_slice_in_dim(norm_grad, low, shard, 1)
    reduced_all = (g_in_col, g_out_row, g_out_col, g_up, g_down)

    local_square = (
        sum(jnp.sum(g * g) for g in reduced_all)
        + jnp.sum(grad_in_row * grad_in_row)
        + jnp.sum(table_mine * table_mine)
        + jnp.sum(norm_mine * norm_mine)
    )
    square = lax.psum(local_square, both) + jnp.sum(contact_grad * contact_grad)
    grad_norm = jnp.sqrt(square)
    factor = jnp.minimum(1.0, MAX_NORM / grad_norm)
    in_new, in_moment, in_square = adam_update(
        attention_in_master, attention_in_first, attention_in_second, jnp.stack([grad_in_row, g_in_col]) * factor, LEARN_RATE
    )
    out_new, out_moment, out_square = adam_update(
        attention_out_master, attention_out_first, attention_out_second, jnp.stack([g_out_row, g_out_col]) * factor, LEARN_RATE
    )
    up_new, up_moment, up_square = adam_update(
        feed_up_master, feed_up_first, feed_up_second, g_up * factor, LEARN_RATE
    )
    down_new, down_moment, down_square = adam_update(
        feed_down_master, feed_down_first, feed_down_second, g_down.T * factor, LEARN_RATE
    )
    table_new, table_moment, table_square = adam_update(
        embedding_master, embedding_first, embedding_second, table_mine * factor, VECTOR_RATE
    )
    norm_new, norm_moment, norm_square = adam_update(
        norm_params_master, norm_params_first, norm_params_second, norm_mine * factor, VECTOR_RATE
    )
    head_new, head_moment, head_square = adam_update(
        contact_head_master, contact_head_first, contact_head_second, contact_grad * factor, VECTOR_RATE
    )
    loss_parts = jnp.stack([mlm_total, counts[0], bce_total, counts[1]])
    return (
        in_new, in_moment, in_square,
        out_new, out_moment, out_square,
        up_new, up_moment, up_square,
        down_new, down_moment, down_square,
        table_new, table_moment, table_square,
        norm_new, norm_moment, norm_square,
        head_new, head_moment, head_square,
        in_new.astype(BF16), out_new.astype(BF16), up_new.astype(BF16), down_new.astype(BF16), table_new.astype(BF16),
        loss_parts, grad_norm,
    )


def solution(mesh):
    both = ("seq", "col")
    cells = P(None, "seq", "col")
    stack = P(None, both, None)
    row_split = P(both, None)
    col_split = P(None, both)
    weights = [stack] * 6 + [row_split] * 3 + [col_split] * 9 + [P()] * 3
    return jax.shard_map(
        shards,
        mesh=mesh,
        in_specs=(cells, cells, cells, stack, col_split, *weights),
        out_specs=(*weights, stack, stack, row_split, col_split, col_split, P(), P()),
        check_vma=False,
    )
```

```python
import typing

import jax
import jax.numpy as jnp
from jax import lax
from jax.experimental import pallas as pl
from jax.experimental.pallas import tpu as pltpu
from jax.sharding import PartitionSpec as P

D = 768
HEADS = 12
HD = 64
FF = 3072
VOCAB = 33
VP = 64
STEP = 10

NORM_EPS = 1e-05
MASK_ID = 32
MAX_NORM = 0.001
LEARN_RATE = 0.05
VECTOR_RATE = 0.5
BETA_ONE = 0.9
BETA_TWO = 0.95
ADAM_EPS = 1e-08
WEIGHT_DECAY = 0.01
PRECISE = lax.Precision.HIGHEST
F32 = jnp.float32
BF16 = jnp.bfloat16


def nn(left, right):
    return lax.dot_general(left, right, (((1,), (0,)), ((), ())), preferred_element_type=F32)


def tn(left, right):
    return lax.dot_general(left, right, (((0,), (0,)), ((), ())), preferred_element_type=F32)


def nt(left, right):
    return lax.dot_general(left, right, (((1,), (1,)), ((), ())), preferred_element_type=F32)


def split_two(values):
    high = values.astype(BF16)
    return high, (values - high.astype(F32)).astype(BF16)


def norm_stats(values):
    centre = values - jnp.mean(values, -1, keepdims=True)
    rstd = lax.rsqrt(jnp.mean(centre * centre, -1, keepdims=True) + NORM_EPS)
    return centre * rstd, rstd


def norm_back(unit, rstd, scale_vec, upstream):
    inner = upstream * scale_vec
    grad = rstd * (
        inner - jnp.mean(inner, -1, keepdims=True) - unit * jnp.mean(inner * unit, -1, keepdims=True)
    )
    return grad, jnp.sum(upstream * unit, 0), jnp.sum(upstream, 0)


GELU_K = 0.7978845608028654
GELU_C = 0.044715


def gelu_parts(up):
    square = up * up
    bent = jnp.tanh(GELU_K * up * (1.0 + GELU_C * square))
    half = 0.5 * (1.0 + bent)
    slope = half + 0.5 * up * (1.0 - bent * bent) * GELU_K * (1.0 + 3.0 * GELU_C * square)
    return up * half, slope


def heads_of(block, head):
    return block[:, head * HD : (head + 1) * HD]


def step(big, table, norms, contact_head, ids_all, ids_ri, ids_ir, targets_ir, pair_first, pair_second, labels, counts, cw):
    in_row, in_col, out_row, out_col, up_w, down_t = big
    rows, cols = ids_all.shape
    here = rows * cw
    row_scale = (HD * rows) ** (-0.5)
    vocab = jnp.arange(VP)[:, None]
    hot_all = (ids_all[:, None, :] == vocab[None]).astype(BF16).reshape(rows * VP, cols)
    hot_ri = (ids_ri[None, :] == vocab).astype(BF16)
    hot_ir = (ids_ir[None, :] == vocab).astype(BF16)
    spot = jnp.arange(here)
    perm = (
        ((spot // rows)[:, None] == (spot % cw)[None, :])
        & ((spot % rows)[:, None] == (spot // cw)[None, :])
    ).astype(BF16)

    def to_heads(block):
        return block.reshape(rows, cw, HEADS, VP).transpose(2, 1, 0, 3).reshape(HEADS * cw, rows * VP)

    def to_tokens(block):
        return block.reshape(HEADS, cw, rows, VP).transpose(2, 1, 0, 3).reshape(here, HEADS * VP)

    def per_head(block, other, how):
        return jnp.concatenate(
            [how(heads_of(block, h), heads_of(other, h)) for h in range(HEADS)], -1
        )

    table_f = table.astype(F32)
    unit_t, rstd_t = norm_stats(table_f)
    normed_t = (unit_t * norms[0] + norms[4]).astype(BF16)
    proj_t = nn(normed_t, in_row).astype(BF16)
    query_t, key_t, value_t = proj_t[:, :D], proj_t[:, D : 2 * D], proj_t[:, 2 * D :]

    pair_t = per_head(query_t, key_t, nt)
    pair_hi, pair_lo = split_two(pair_t)
    left_hi = to_heads(tn(hot_ri, pair_hi).astype(BF16))
    left_lo = to_heads(tn(hot_ri, pair_lo).astype(BF16))
    score = (nn(left_hi, hot_all) + nn(left_lo, hot_all)) * row_scale
    prob = jax.nn.softmax(score, axis=-1)
    prob_low = prob.astype(BF16)
    weight_t = to_tokens(nt(prob_low, hot_all))
    weight_hi, weight_lo = split_two(weight_t)
    row_mixed_ri = (
        per_head(weight_hi, value_t, nn) + per_head(weight_lo, value_t, nn)
    ).astype(BF16)
    row_mixed = nn(perm, row_mixed_ri).astype(BF16)
    embedded = tn(hot_ir, table)
    after_row = embedded + nn(row_mixed, out_row)

    prob_cube = prob_low.astype(F32).reshape(HEADS, cw, cols)
    head_sum = jnp.sum(prob_cube * contact_head[:HEADS, None, None], 0)
    first_hot = (pair_first[None, :] == jnp.arange(cw)[:, None]).astype(F32)
    second_hot = (pair_second[None, :] == jnp.arange(cols)[:, None]).astype(BF16)
    sum_hi, sum_lo = split_two(head_sum)
    sum_last = (head_sum - sum_hi.astype(F32) - sum_lo.astype(F32)).astype(BF16)
    picked = nn(sum_hi, second_hot) + nn(sum_lo, second_hot) + nn(sum_last, second_hot)
    contact_logit = jnp.sum(picked * first_hot, 0) * cols + contact_head[HEADS]
    owned = jnp.sum(first_hot, 0) > 0
    valid = (labels >= 0) & owned
    positive = (labels == 1).astype(F32)
    bce_sum = jnp.sum(
        jnp.where(valid, jax.nn.softplus(contact_logit) - positive * contact_logit, 0.0)
    )
    coef = jnp.where(valid, jax.nn.sigmoid(contact_logit) - positive, 0.0) / counts[1]
    coef_hi, coef_lo = split_two(coef)
    first_low = first_hot.astype(BF16)
    touch = nt(first_low * coef_hi[None], second_hot) + nt(first_low * coef_lo[None], second_hot)
    grad_contact = jnp.concatenate(
        [jnp.sum(prob_cube * touch[None], (1, 2)) * cols, jnp.sum(coef)[None]]
    )

    unit_1, rstd_1 = norm_stats(after_row)
    col_normed = (unit_1 * norms[1] + norms[5]).astype(BF16)
    col_proj = nn(col_normed, in_col).astype(BF16)
    group = 128 if here % 128 == 0 and 128 % rows == 0 else here
    groups = here // group
    lane = jnp.arange(group)
    same = (lane[:, None] // rows) == (lane[None, :] // rows)

    def cut(block):
        return block.reshape(groups, group, HEADS, HD)

    col_query, col_key, col_value = (cut(col_proj[:, k * D : (k + 1) * D]) for k in range(3))
    col_score = jnp.einsum("gqhe,gkhe->ghqk", col_query, col_key, preferred_element_type=F32) * HD ** (-0.5)
    col_prob = jax.nn.softmax(jnp.where(same, col_score, -1e30), axis=-1)
    col_prob_low = col_prob.astype(BF16)
    col_mixed = (
        jnp.einsum("ghqk,gkhe->gqhe", col_prob_low, col_value, preferred_element_type=F32)
        .astype(BF16)
        .reshape(here, D)
    )
    after_col = after_row + nn(col_mixed, out_col)

    unit_2, rstd_2 = norm_stats(after_col)
    feed_normed = (unit_2 * norms[2] + norms[6]).astype(BF16)
    hidden_up = nn(feed_normed, up_w)
    active, slope = gelu_parts(hidden_up)
    active = active.astype(BF16)
    after_feed = after_col + nt(active, down_t)
    unit_3, rstd_3 = norm_stats(after_feed)
    head_normed = (unit_3 * norms[3] + norms[7]).astype(BF16)
    logits = nt(table, head_normed) * D ** (-0.5)
    logits = jnp.where(vocab < VOCAB, logits, -1e30)
    top = jnp.max(logits, 0, keepdims=True)
    shifted = logits - top
    log_probs = shifted - jnp.log(jnp.sum(jnp.exp(shifted), 0, keepdims=True))
    target_hot = (targets_ir[None, :] == vocab).astype(F32)
    keep = ids_ir[None, :] == MASK_ID
    mlm_sum = -jnp.sum(jnp.where(keep & (target_hot > 0), log_probs, 0.0))
    logit_grad = jnp.where(keep, jnp.exp(log_probs) - target_hot, 0.0) / counts[0]
    logit_low = (logit_grad * D ** (-0.5)).astype(BF16)

    grad_head = nn(logit_low, head_normed)
    stream, scale_3, shift_3 = norm_back(unit_3, rstd_3, norms[3], tn(logit_low, table))
    branch = stream.astype(BF16)
    grad_down = tn(branch, active)
    up_low = (nn(branch, down_t) * slope).astype(BF16)
    grad_up = tn(feed_normed, up_low)
    inner, scale_2, shift_2 = norm_back(unit_2, rstd_2, norms[2], nt(up_low, up_w))
    stream = stream + inner
    branch = stream.astype(BF16)
    grad_out_col = tn(col_mixed, branch)
    mixed_low = nt(branch, out_col).astype(BF16)
    mixed_cut = cut(mixed_low)
    prob_grad = jnp.einsum("gqhe,gkhe->ghqk", mixed_cut, col_value, preferred_element_type=F32)
    score_grad = col_prob * (prob_grad - jnp.sum(col_prob * prob_grad, -1, keepdims=True))
    score_low = score_grad.astype(BF16)
    grad_q = jnp.einsum("ghqk,gkhe->gqhe", score_low, col_key, preferred_element_type=F32)
    grad_k = jnp.einsum("ghqk,gqhe->gkhe", score_low, col_query, preferred_element_type=F32)
    grad_v = jnp.einsum("ghqk,gqhe->gkhe", col_prob_low, mixed_cut, preferred_element_type=F32)
    proj_low = jnp.concatenate(
        [
            (grad_q * HD ** (-0.5)).reshape(here, D),
            (grad_k * HD ** (-0.5)).reshape(here, D),
            grad_v.reshape(here, D),
        ],
        -1,
    ).astype(BF16)
    grad_in_col = tn(col_normed, proj_low)
    inner, scale_1, shift_1 = norm_back(unit_1, rstd_1, norms[1], nt(proj_low, in_col))
    stream = stream + inner
    branch = stream.astype(BF16)
    grad_out_row = tn(row_mixed, branch)
    mixed_low = nt(branch, out_row).astype(BF16)
    mixed_ri = tn(perm, mixed_low).astype(BF16)
    drive_hi, drive_lo = split_two(per_head(mixed_ri, value_t, nt))
    prob_grad = nn(to_heads(drive_hi), hot_all) + nn(to_heads(drive_lo), hot_all)
    prob_grad = prob_grad + (
        touch[None] * (contact_head[:HEADS, None, None] * cols)
    ).reshape(HEADS * cw, cols)
    score_grad = prob * (prob_grad - jnp.sum(prob * prob_grad, -1, keepdims=True))
    score_low = score_grad.astype(BF16)
    spread = to_tokens(nt(score_low, hot_all)).astype(BF16)
    table_pair = nn(hot_ri, spread)
    value_grad = per_head(weight_hi, mixed_ri, tn)
    stream_hi, stream_lo = split_two(stream)
    lookup_grad = nn(hot_ir, stream_hi) + nn(hot_ir, stream_lo)
    vectors = jnp.stack([scale_1, scale_2, scale_3, shift_1, shift_2, shift_3])
    return (
        (grad_in_col, grad_out_row, grad_out_col, grad_up, grad_down),
        (table_pair, value_grad, grad_head + lookup_grad, vectors),
        grad_contact,
        mlm_sum,
        bce_sum,
        (unit_t, rstd_t, normed_t, query_t, key_t),
    )


MESH = pl.DeviceIdType.MESH
NZ, NY = 4, 2


def place():
    s, c = lax.axis_index("seq"), lax.axis_index("col")
    z, y, k = s // 4, lax.rem(s // 2, 2), lax.rem(s, 2)
    return z, y, k, c


def device(z, y, k, c):
    return (z * 4 + y * 2 + k, c)


def greet_all():
    z, y, k, c = place()
    me = (z * 4 + y * 2 + k) * 2 + c
    barrier = pltpu.get_barrier_semaphore()

    def signal(step, carry):
        other = lax.rem(me + step, 32)
        pl.semaphore_signal(
            barrier, inc=1, device_id=(other // 2, lax.rem(other, 2)), device_id_type=MESH
        )
        return carry

    lax.fori_loop(1, 32, signal, 0)
    return barrier


def remote(src, dst, send, recv, target):
    return pltpu.make_async_remote_copy(
        src_ref=src, dst_ref=dst, send_sem=send, recv_sem=recv, device_id=target, device_id_type=MESH
    )


ROWS, COLS, WIDE, HERE = 16, 512, 32, 512
PAIRS = 6
SLOTS = 1024
UP_TILE = 384


def iota(shape, dim):
    return lax.broadcasted_iota(jnp.int32, shape, dim)


def one_zero(test):
    return jnp.where(test, 1.0, 0.0)


def total_of(values):
    return jnp.sum(jnp.sum(values, 0, keepdims=True), 1, keepdims=True)


def half_lanes(values, side):
    lane = iota(values.shape, len(values.shape) - 1)
    keep = (lane < 64) if side == 0 else (lane >= 64)
    return jnp.where(keep, values.astype(F32), 0.0).astype(BF16)


def stacked(values):
    return jnp.concatenate([half_lanes(values, 0), half_lanes(values, 1)], 0)


def unstacked(values, count):
    lane = iota((count, 128), 1)
    return jnp.where(lane < 64, values[:count], values[count:])


def swap_blocks(first, second):
    lane = iota(first.shape, 1)
    low = jnp.where(lane < 64, first, pltpu.roll(second, 64, 1))
    high = jnp.where(lane < 64, pltpu.roll(first, 64, 1), second)
    return low, high


def split_heads_to(source, high_ref, low_ref):
    for rp in range(ROWS // 2):
        for hp in range(PAIRS):
            lanes = slice(hp * 128, hp * 128 + 128)
            first = source[rp * 64 : rp * 64 + 32, lanes]
            second = source[rp * 64 + 32 : rp * 64 + 64, lanes]
            for side, block in enumerate(swap_blocks(first, second)):
                top, rest = split_two(block)
                rows = slice((2 * hp + side) * 32, (2 * hp + side) * 32 + 32)
                high_ref[rows, rp * 128 : rp * 128 + 128] = top
                low_ref[rows, rp * 128 : rp * 128 + 128] = rest


def merge_heads(probs, hot_all, high_ref, low_ref):
    for rp in range(ROWS // 2):
        block = nt(probs, hot_all[rp * 128 : rp * 128 + 128, :])
        for hp in range(PAIRS):
            first = block[hp * 64 : hp * 64 + 32]
            second = block[hp * 64 + 32 : hp * 64 + 64]
            for side, part in enumerate(swap_blocks(first, second)):
                top, rest = split_two(part)
                rows = slice(rp * 64 + side * 32, rp * 64 + side * 32 + 32)
                high_ref[rows, hp * 128 : hp * 128 + 128] = top
                if low_ref is not None:
                    low_ref[rows, hp * 128 : hp * 128 + 128] = rest


def norm_rows(source, gain, bias, unit_ref, rstd_ref, normed_ref):
    def body(at, carry):
        rows = pl.ds(pl.multiple_of(at * 32, 32), 32)
        values = source[rows, :]
        centre = values - jnp.sum(values, -1, keepdims=True) * (1.0 / D)
        rstd = lax.rsqrt(jnp.sum(centre * centre, -1, keepdims=True) * (1.0 / D) + NORM_EPS)
        unit = centre * rstd
        unit_ref[rows, :] = unit
        rstd_ref[rows, :] = jnp.broadcast_to(rstd, (32, 128))
        normed_ref[rows, :] = (unit * gain + bias).astype(BF16)
        return carry

    lax.fori_loop(0, HERE // 32, body, 0)


def transpose_into(source, target):
    def body(at, carry):
        rows = pl.ds(pl.multiple_of(at * 128, 128), 128)
        target[:, rows] = source[rows, :].astype(F32).T.astype(BF16)
        return carry

    lax.fori_loop(0, HERE // 128, body, 0)


def over_tiles(width, tile, body):
    for half in range(2):

        def step(at, carry, half=half):
            body(half, pl.multiple_of(at * tile, tile))
            return carry

        lax.fori_loop(0, width // tile, step, 0)


def column_mask():
    rows, lanes = iota((256, 128), 0), iota((256, 128), 1)
    return ((rows & 127) >> 4) == (lanes >> 4)


class Saved(typing.NamedTuple):
    stream: typing.Any
    unit_1: typing.Any
    unit_2: typing.Any
    rstd_1: typing.Any
    rstd_2: typing.Any
    row_mixed_t: typing.Any
    col_normed_t: typing.Any
    col_mixed_t: typing.Any
    feed_normed_t: typing.Any
    col_proj: typing.Any
    col_prob: typing.Any
    active: typing.Any
    slope: typing.Any
    grad_head: typing.Any
    hot_all: typing.Any
    hot_ri: typing.Any
    hot_ir: typing.Any
    prob: typing.Any
    weight_hi: typing.Any
    value_two: typing.Any
    touch: typing.Any
    table: typing.Any
    norms: typing.Any
    proj_t: typing.Any
    extras: typing.Any
    moved: typing.Any


AT = Saved(*range(len(Saved._fields)))
SAVED = Saved(
    stream=((HERE, D), F32),
    unit_1=((HERE, D), F32),
    unit_2=((HERE, D), F32),
    rstd_1=((HERE, 128), F32),
    rstd_2=((HERE, 128), F32),
    row_mixed_t=((D, HERE), BF16),
    col_normed_t=((D, HERE), BF16),
    col_mixed_t=((D, HERE), BF16),
    feed_normed_t=((D, HERE), BF16),
    col_proj=((HERE, 3 * D), BF16),
    col_prob=((4 * PAIRS, 256, 128), F32),
    active=((HERE, FF), BF16),
    slope=((HERE, FF), BF16),
    grad_head=((VP, D), F32),
    hot_all=((ROWS * VP, COLS), BF16),
    hot_ri=((VP, HERE), BF16),
    hot_ir=((VP, HERE), BF16),
    prob=((HEADS * WIDE, COLS), F32),
    weight_hi=((HERE, D), BF16),
    value_two=((PAIRS, 128, 128), BF16),
    touch=((WIDE, COLS), F32),
    table=((VP, D), F32),
    norms=((8, D), F32),
    proj_t=((VP, 3 * D), BF16),
    extras=((8, 128), F32),
    moved=((8, D), F32),
)


class Forward(typing.NamedTuple):
    ids: typing.Any
    targets: typing.Any
    slots: typing.Any
    normed: typing.Any
    mixed: typing.Any
    weight_lo: typing.Any
    left_hi: typing.Any
    left_lo: typing.Any
    lookup: typing.Any
    prob_low: typing.Any
    unit: typing.Any
    rstd: typing.Any


FORWARD = Forward(
    ids=((ROWS, COLS), jnp.int32),
    targets=((ROWS, 128), jnp.int32),
    slots=((8, SLOTS), jnp.int32),
    normed=((HERE, D), BF16),
    mixed=((HERE, D), BF16),
    weight_lo=((HERE, D), BF16),
    left_hi=((HEADS * WIDE, ROWS * VP), BF16),
    left_lo=((HEADS * WIDE, ROWS * VP), BF16),
    lookup=((HERE, D), F32),
    prob_low=((HEADS * WIDE, COLS), BF16),
    unit=((HERE, D), F32),
    rstd=((HERE, 128), F32),
)


def position():
    z, y, k, c = place()
    me = (z * 4 + y * 2 + k) * 2 + c
    return z // 2, lax.rem(me, 16)


def read_tokens(small, f):
    alignment, block = position()
    side, part = block // 8, lax.rem(block // 4, 2)
    for r in range(ROWS):
        for cc in range(2):
            for q in range(2):
                lanes = slice(cc * 256 + q * 128, cc * 256 + q * 128 + 128)
                f.ids[r : r + 1, lanes] = small[r * 2 + cc, pl.ds(2 * alignment + q, 1), :]
        f.targets[r : r + 1, :] = small[r * 2 + side, pl.ds(4 + 2 * alignment + part, 1), :]
    lane = iota((1, 128), 1)
    for number in range(SLOTS // 128):
        for which in range(3):
            row = pl.ds(8 + 3 * alignment + which, 1)
            first = small[number * 4 + side, row, :]
            second = pltpu.roll(small[number * 4 + 2 + side, row, :], 64, 1)
            f.slots[which : which + 1, number * 128 : number * 128 + 128] = jnp.where(
                lane < 64, first, second
            )


def local_hot(values, shift):
    values = pltpu.roll(values, shift, 1)
    turned = [values] + [pltpu.roll(values, 32 * n, 1) for n in (1, 2, 3)]
    lane = iota((1, 128), 1)
    tiles = []
    for tile in range(4):
        row = turned[3][4 * tile + 3 : 4 * tile + 4]
        for n in (2, 1, 0):
            row = jnp.where(lane < 32 * n + 32, turned[n][4 * tile + n : 4 * tile + n + 1], row)
        tiles.append(row)
    row = jnp.concatenate(tiles, 1)
    return one_zero(row == iota((VP, HERE), 0)).astype(BF16)


def contact_part(contact_head, f, s, pair_count):
    _, block = position()
    base = block * WIDE
    head_sum = jnp.zeros((WIDE, COLS), F32)
    for h in range(HEADS):
        head_sum = head_sum + contact_head[h] * f.prob_low[h * 32 : h * 32 + 32, :].astype(F32)
    top, rest = split_two(head_sum)
    last = (head_sum - top.astype(F32) - rest.astype(F32)).astype(BF16)
    parts = jnp.concatenate([top, rest, last], 0)
    touch = jnp.zeros((WIDE, COLS), F32)
    bce = jnp.zeros((1, 1), F32)
    coef_sum = jnp.zeros((1, 1), F32)
    for number in range(SLOTS // 512):
        lanes = slice(number * 512, number * 512 + 512)
        first, second, label = (f.slots[n : n + 1, lanes] for n in range(3))
        second_hot = one_zero(second == iota((COLS, 512), 0)).astype(BF16)
        picked = nn(parts, second_hot)
        picked = picked[:32] + picked[32:64] + picked[64:]
        first_hot = one_zero((first - base) == iota((WIDE, 512), 0))
        logit = jnp.sum(picked * first_hot, 0, keepdims=True) * COLS + contact_head[HEADS]
        owned = jnp.sum(first_hot, 0, keepdims=True) > 0.5
        valid = (label >= 0) & owned
        positive = one_zero(label == 1)
        small = jnp.exp(-jnp.abs(logit))
        soft = jnp.maximum(logit, 0.0) + jnp.log(1.0 + small)
        bce = bce + total_of(jnp.where(valid, soft - positive * logit, 0.0))
        sigmoid = jnp.where(logit >= 0.0, 1.0, small) / (1.0 + small)
        coef = jnp.where(valid, sigmoid - positive, 0.0) / pair_count
        coef_sum = coef_sum + total_of(coef)
        coef_top, coef_rest = split_two(first_hot * coef)
        touch = touch + nt(coef_top, second_hot) + nt(coef_rest, second_hot)
    s.touch[...] = touch
    column = iota((1, 128), 1)
    row = jnp.where(column == HEADS, coef_sum, 0.0)
    for h in range(HEADS):
        part = total_of(touch * f.prob_low[h * 32 : h * 32 + 32, :].astype(F32)) * COLS
        row = row + jnp.where(column == h, part, 0.0)
    return row, bce


def feature_order():
    shape = (384, 384)
    spot = iota(shape, 0)
    block = (spot * 2731) >> 16
    swapped = (block & 28) | ((block & 1) << 1) | ((block >> 1) & 1)
    return one_zero(spot + (swapped - block) * 24 == iota(shape, 1)).astype(BF16)


def forward_body(small, contact_head, weights, s, f, ready, hook, emit):
    emb, in_row, out_row, in_col, out_col = weights[:5]
    up_parts, down_parts = weights[5:7], weights[7:9]
    ready(-1)
    hook()
    read_tokens(small, f)
    _, block = position()
    shift = lax.rem(128 - lax.rem(block, 4) * 32, 128)
    window = pl.ds(pl.multiple_of((block // 4) * 128, 128), 128)
    hot_ri = local_hot(f.ids[:, window], shift)
    goal_ri = local_hot(f.targets[...], shift)
    s.hot_ri[...] = hot_ri
    for r in range(ROWS):
        row = f.ids[r : r + 1, :]
        s.hot_all[r * VP : r * VP + VP, :] = one_zero(row == iota((VP, COLS), 0)).astype(BF16)
    shape = (HERE, HERE)
    back = (
        ((iota(shape, 1) >> 4) == (iota(shape, 0) & 31))
        & ((iota(shape, 1) & 15) == (iota(shape, 0) >> 5))
    )
    back = one_zero(back).astype(BF16)
    hot_ir = nn(hot_ri, back).astype(BF16)
    s.hot_ir[...] = hot_ir
    goal = nn(goal_ri, back)
    entries = jnp.zeros((4, 128), F32)
    labelled = jnp.zeros((1, 128), F32)
    for d in range(32):
        entries = entries + one_zero(small[d, 0:4, :] == MASK_ID)
        labelled = labelled + one_zero(small[d, 10:11, :] >= 0) + one_zero(small[d, 13:14, :] >= 0)
    entries, labelled = total_of(entries), total_of(labelled)

    hook()
    table = emb[0].astype(F32).T[:VP]
    norms = emb[1].astype(F32).T[:8]
    s.table[...] = table
    s.norms[...] = norms
    table_low = table.astype(BF16)

    def vector(number):
        return norms[number : number + 1, :]

    unit_t, _ = norm_stats(table)
    normed_t = (unit_t * vector(0) + vector(4)).astype(BF16)
    hook()
    for half in range(2):
        s.proj_t[:, half * 1152 : half * 1152 + 1152] = nn(normed_t, in_row[half]).astype(BF16)
    pair_parts = []
    for hp in range(PAIRS):
        lanes = slice(hp * 128, hp * 128 + 128)
        key = s.proj_t[:, D + hp * 128 : D + hp * 128 + 128]
        value = s.proj_t[:, 2 * D + hp * 128 : 2 * D + hp * 128 + 128]
        s.value_two[hp] = stacked(value)
        pair_parts.append(nt(s.proj_t[:, lanes], stacked(key)))
    pair_hi, pair_lo = split_two(jnp.concatenate(pair_parts, 1))
    hook()
    f.lookup[...] = tn(hot_ri, pair_hi) + tn(hot_ri, pair_lo)
    split_heads_to(f.lookup, f.left_hi, f.left_lo)
    hook()
    hot_all = s.hot_all[...]
    score = (nn(f.left_hi[...], hot_all) + nn(f.left_lo[...], hot_all)) * (HD * ROWS) ** (-0.5)
    score = jnp.exp(score - jnp.max(score, -1, keepdims=True))
    prob = score / jnp.sum(score, -1, keepdims=True)
    s.prob[...] = prob
    f.prob_low[...] = prob.astype(BF16)
    hook()
    merge_heads(f.prob_low[...], s.hot_all, s.weight_hi, f.weight_lo)
    hook()
    for hp in range(PAIRS):
        lanes = slice(hp * 128, hp * 128 + 128)
        value = s.value_two[hp]
        f.mixed[:, lanes] = (nn(s.weight_hi[:, lanes], value) + nn(f.weight_lo[:, lanes], value)).astype(BF16)
    ahead = (
        ((iota(shape, 0) >> 4) == (iota(shape, 1) & 31))
        & ((iota(shape, 0) & 15) == (iota(shape, 1) >> 5))
    )
    f.mixed[...] = nn(one_zero(ahead).astype(BF16), f.mixed[...]).astype(BF16)
    transpose_into(f.mixed, s.row_mixed_t)
    s.stream[...] = tn(hot_ir, table_low)
    hook()
    contact_row, bce = contact_part(contact_head, f, s, labelled)
    emit(AT.hot_all, AT.hot_ri, AT.hot_ir, AT.table, AT.norms, AT.proj_t, AT.value_two, AT.prob, AT.weight_hi, AT.row_mixed_t, AT.touch)

    hook()
    for half in range(2):
        lanes = slice(half * 384, half * 384 + 384)
        s.stream[:, lanes] += nn(f.mixed[...], out_row[half])
    norm_rows(s.stream, vector(1), vector(5), s.unit_1, s.rstd_1, f.normed)
    transpose_into(f.normed, s.col_normed_t)
    emit(AT.unit_1, AT.rstd_1, AT.col_normed_t)
    def project(half, at):
        s.col_proj[:, half * 1152 + at : half * 1152 + at + 384] = nn(
            f.normed[...], in_col[half, :, at : at + 384]
        ).astype(BF16)

    for third in range(3):
        hook()
        for half in range(2):
            project(half, third * 384)
    emit(AT.col_proj)

    def attend(at, carry):
        rows = pl.ds(pl.multiple_of((at // PAIRS) * 128, 128), 128)
        lane = lax.rem(at, PAIRS) * 128

        def lanes(part):
            return pl.ds(pl.multiple_of(part * D + lane, 128), 128)

        query = stacked(s.col_proj[rows, lanes(0)])
        score = nt(query, s.col_proj[rows, lanes(1)]) * HD ** (-0.5)
        score = jnp.where(column_mask(), score, -1e30)
        score = jnp.exp(score - jnp.max(score, -1, keepdims=True))
        prob = score / jnp.sum(score, -1, keepdims=True)
        s.col_prob[at] = prob
        mixed = nn(prob.astype(BF16), s.col_proj[rows, lanes(2)])
        f.mixed[rows, lanes(0)] = unstacked(mixed, 128).astype(BF16)
        return carry

    for part in range(4):
        hook()
        lax.fori_loop(part * PAIRS, part * PAIRS + PAIRS, attend, 0, unroll=2)
    hook()
    transpose_into(f.mixed, s.col_mixed_t)
    emit(AT.col_prob, AT.col_mixed_t)
    for half in range(2):
        lanes = slice(half * 384, half * 384 + 384)
        s.stream[:, lanes] += nn(f.mixed[...], out_col[half])
    norm_rows(s.stream, vector(2), vector(6), s.unit_2, s.rstd_2, f.normed)
    transpose_into(f.normed, s.feed_normed_t)
    emit(AT.unit_2, AT.rstd_2, AT.feed_normed_t)
    for part in range(2):

        def widen(half, at, part=part):
            lanes = slice(part * 1536 + half * 768 + at, part * 1536 + half * 768 + at + UP_TILE)
            up = nn(f.normed[...], up_parts[part][half, :, at : at + UP_TILE])
            active, slope = gelu_parts(up)
            s.active[:, lanes] = active.astype(BF16)
            s.slope[:, lanes] = slope.astype(BF16)

        for half in range(2):
            hook()
            for at in range(0, 768, UP_TILE):
                widen(half, at)

    emit(AT.active, AT.slope)
    for part in range(2):
        hook()
        for half in range(2):
            start = part * 1536 + half * 768
            s.stream[...] += nt(s.active[:, start : start + 768], down_parts[part][half])
    hook()
    norm_rows(s.stream, vector(3), vector(7), f.unit, f.rstd, f.normed)
    logits = nt(table_low, f.normed[...]) * D ** (-0.5)
    vocab = iota((VP, HERE), 0)
    logits = jnp.where(vocab < VOCAB, logits, -1e30)
    shifted = logits - jnp.max(logits, 0, keepdims=True)
    log_probs = shifted - jnp.log(jnp.sum(jnp.exp(shifted), 0, keepdims=True))
    keep = hot_ir[MASK_ID : MASK_ID + 1].astype(F32) > 0.5
    mlm = -total_of(jnp.where(keep & (goal > 0.5), log_probs, 0.0))
    logit_grad = jnp.where(keep, jnp.exp(log_probs) - goal, 0.0) / entries
    logit_low = (logit_grad * D ** (-0.5)).astype(BF16)
    s.grad_head[...] = nn(logit_low, f.normed[...])
    hook()
    f.lookup[...] = tn(logit_low, table_low)
    scale_3, shift_3 = back_rows(f.unit, f.rstd, vector(3), f.lookup, s.stream, f.normed, True)
    emit(AT.stream)
    line = iota((8, D), 0)
    s.moved[...] = jnp.where(line == 0, scale_3, jnp.where(line == 1, shift_3, 0.0))
    column = iota((1, 128), 1)
    row = contact_row + jnp.where(column == HEADS + 1, mlm, 0.0) + jnp.where(column == HEADS + 2, bce, 0.0)
    counted = jnp.where(column == 0, entries, 0.0) + jnp.where(column == 1, labelled, 0.0)
    line = iota((8, 128), 0)
    s.extras[...] = jnp.where(line == 0, row, jnp.where(line == 1, counted, 0.0))
    emit(AT.grad_head, AT.extras, AT.moved)
    hook()


def back_rows(unit_ref, rstd_ref, gain, upstream_ref, stream_ref, low_ref, first):
    def body(at, carry):
        scale, move = carry
        rows = pl.ds(pl.multiple_of(at * 32, 32), 32)
        upstream = upstream_ref[rows, :]
        unit = unit_ref[rows, :]
        inner = upstream * gain
        mean = jnp.sum(inner, -1, keepdims=True) * (1.0 / D)
        along = jnp.sum(inner * unit, -1, keepdims=True) * (1.0 / D)
        grad = rstd_ref[rows, 0:1] * (inner - mean - unit * along)
        if not first:
            grad = grad + stream_ref[rows, :]
        stream_ref[rows, :] = grad
        low_ref[rows, :] = grad.astype(BF16)
        touched = upstream * unit
        for n in range(4):
            scale = scale + touched[n * 8 : n * 8 + 8]
            move = move + upstream[n * 8 : n * 8 + 8]
        return scale, move

    zero = jnp.zeros((8, D), F32)
    scale, move = lax.fori_loop(0, HERE // 32, body, (zero, zero))
    return jnp.sum(scale, 0, keepdims=True), jnp.sum(move, 0, keepdims=True)


MATRICES = (128, 1152, 384, 1152, 384, 768, 768, 768, 768)
UNITS = (
    (0, 0, 128, True),
    (1, 0, 384, True),
    (1, 384, 384, True),
    (1, 768, 384, True),
    (2, 0, 384, False),
    (3, 0, 384, True),
    (3, 384, 384, True),
    (3, 768, 384, True),
    (4, 0, 384, False),
    (5, 0, 768, True),
    (6, 0, 768, True),
    (7, 0, 768, True),
    (8, 0, 768, True),
)
FORWARD_ORDER = (
    (),
    ((0, 0), (0, 1), (0, 2), (0, 3), (0, 4), (0, 5), (0, 6), (0, 7), (0, 8), (1, 0), (0, 9), (0, 10), (0, 11), (0, 12), (2, 0), (1, 1), (3, 0), (1, 2), (2, 1), (4, 0),),
    ((1, 3), (2, 2), (1, 4), (3, 1), (2, 3), (1, 5), (4, 1), (3, 2), (1, 6), (2, 4), (4, 2), (1, 7), (3, 3), (2, 5), (1, 8), (4, 3),),
    (),
    ((2, 6),),
    ((3, 4), (1, 9),),
    ((4, 4), (2, 7),),
    ((3, 5),),
    ((2, 8), (1, 10), (4, 5),),
    ((3, 6), (2, 9), (1, 11), (4, 6), (3, 7), (3, 8), (1, 12), (4, 7),),
    (),
    ((4, 8), (2, 10),),
    (),
    (),
    (),
    ((3, 9),),
    ((2, 11),),
    ((4, 9),),
    (),
    ((2, 12), (3, 10), (3, 11), (4, 10),),
    (),
    ((3, 12), (4, 11),),
    ((4, 12),),
    (),
    (),
    (),
)


def spot(paired, cc, zz, yy, k):
    return (k, zz, yy, cc) if paired else (cc, zz, yy, k)


def forward_kernel(*refs):
    count, parts = len(UNITS), len(MATRICES)
    raw = refs[:11]
    contact_head = refs[11]
    at = 12
    far = refs[at : at + parts]
    saved_far = refs[at + parts : at + parts + len(SAVED)]
    at += parts + len(SAVED)
    outs = refs[at : at + parts]
    at += parts
    outgoing = refs[at : at + count]
    incoming = refs[at + count : at + 2 * count]
    piece = refs[at + 2 * count : at + 3 * count]
    at += 3 * count
    saved = Saved(*refs[at : at + len(SAVED)])
    at += len(SAVED)
    scratch = Forward(*refs[at : at + len(FORWARD)])
    at += len(FORWARD)
    near = refs[at : at + 11]
    at += 11
    small, small_out, sides, corner = refs[at : at + 4]
    small_send, small_recv, send, recv, local, out_sem, raw_sem = refs[at + 4 :]
    tokens, targets, masked, pairs, labels, table, norms, in_w, out_w, up_w, down_w = near
    z, y, k, c = place()
    me = (z * 4 + y * 2 + k) * 2 + c
    barrier = greet_all()
    raw_copies = [pltpu.make_async_copy(a, b, raw_sem.at[n]) for n, (a, b) in enumerate(zip(raw, near))]
    for item in raw_copies:
        item.start()
    for item in raw_copies[:7]:
        item.wait()
    small[...] = jnp.full(small.shape, -1, jnp.int32)
    for micro in range(2):
        for half in range(2):
            lanes = slice(half * 128, half * 128 + 128)
            row = 2 * micro + half
            small[row : row + 1, :] = jnp.where(
                masked[micro, :, lanes] > 0, MASK_ID, tokens[micro, :, lanes]
            )
            small[4 + row : 5 + row, :] = targets[micro, :, lanes]
        row = 8 + 3 * micro
        for which in range(2):
            small[row + which : row + which + 1, 0:64] = pairs[micro, which : which + 1, :]
        small[row + 2 : row + 3, 0:64] = labels[micro : micro + 1, :]
    sides[...] = jnp.zeros(sides.shape, F32)
    sides[0, :, 0:VOCAB] = table[...]
    corner[...] = jnp.zeros(corner.shape, F32)
    corner[0:8, 0:24] = norms[...]
    sides[1] = corner[...].T[:24]
    for item in raw_copies[7:]:
        item.wait()
    order = feature_order()

    def master(u, side):
        matrix, start, n, _ = UNITS[u]
        width = MATRICES[matrix]
        if matrix == 0:
            return sides[side]
        if matrix in (1, 3):
            return in_w[matrix // 2, :, side * 1152 + start : side * 1152 + start + n]
        if matrix in (2, 4):
            rows = out_w[matrix // 2 - 1, :, side * 384 : side * 384 + 384].astype(BF16)
            return nn(rows, order)
        begin = ((matrix - 5) % 2) * 1536 + side * width
        return (up_w if matrix < 7 else down_w)[:, begin : begin + n]

    def mine(u):
        return k if UNITS[u][3] else c

    for u in range(count):
        n = UNITS[u][2]
        other = jnp.where(mine(u) == 0, master(u, 1), master(u, 0))
        outgoing[u][...] = jnp.concatenate([other, jnp.zeros((8, n), F32)], 0).astype(BF16)
    pl.semaphore_wait(barrier, 31)

    def small_copy(step):
        other = lax.rem(me + step, 32)
        return remote(
            small, small_out.at[me], small_send.at[step], small_recv.at[step], (other // 2, lax.rem(other, 2))
        )

    def spread(step, carry):
        small_copy(step).start()
        return carry

    across, beside, twin = device(z, y, k, 1 - c), device(z, 1 - y, k, c), device(z, y, 1 - k, c)

    def block(u, cc, zz, yy):
        matrix, start, n, paired = UNITS[u]
        where = spot(paired, cc, zz, yy, k)
        if n == MATRICES[matrix]:
            return outs[matrix].at[where]
        return outs[matrix].at[(*where, slice(None), pl.ds(start, n))]

    def copy(u, at, src, dst, target):
        return remote(src, dst, send.at[u, at], recv.at[u, at], target)

    def pair_copy(u):
        return copy(u, 0, outgoing[u], incoming[u], twin if UNITS[u][3] else across)

    def own_copy(u):
        return pltpu.make_async_copy(piece[u], block(u, c, z, y), local.at[u])

    def line_copy(u, step):
        return copy(u, step, piece[u], block(u, c, z, y), device(lax.rem(z + step, 4), y, k, c))

    def same(u, at, cc, zz, yy, target):
        view = block(u, cc, zz, yy)
        return copy(u, at, view, view, target)

    low, high, every = pl.ds(0, 2), pl.ds(2, 2), slice(None)

    def second(u):
        return [same(u, 4, c, low, y, across), same(u, 5, c, high, y, beside)]

    def third_own(u):
        return [same(u, 6, c, low, y, beside), same(u, 7, c, high, y, across)]

    def third_far(u):
        return [same(u, 8, 1 - c, low, y, beside), same(u, 9, c, high, 1 - y, across)]

    def twin_own(u):
        return [same(u, 10, c, every, y, twin)]

    def twin_second(u):
        return [same(u, 11, 1 - c, low, y, twin), same(u, 12, c, high, 1 - y, twin)]

    def twin_third(u):
        return [
            same(u, 13, c, low, 1 - y, twin),
            same(u, 14, 1 - c, high, y, twin),
            same(u, 15, 1 - c, low, 1 - y, twin),
            same(u, 16, 1 - c, high, 1 - y, twin),
        ]

    for u in range(count):
        pair_copy(u).start()
    lax.fori_loop(1, 32, spread, 0)
    small_out[me] = small[...]

    def stage_line(u):
        pair_copy(u).wait_recv()
        side = mine(u)
        own = jnp.where(side == 0, master(u, 0), master(u, 1))
        theirs = incoming[u][...].astype(F32)[:24]
        top = jnp.where(side == 0, own, theirs)
        bottom = jnp.where(side == 0, theirs, own)
        piece[u][...] = jnp.concatenate([top, bottom], 0).astype(BF16)
        own_copy(u).start()
        for step in (1, 3, 2):
            line_copy(u, step).start()

    def stage_second(u):
        own_copy(u).wait()
        for step in (1, 3, 2):
            line_copy(u, step).wait_recv()
        for item in second(u) + third_own(u) + twin_own(u):
            item.start()

    def stage_third(u):
        for item in second(u):
            item.wait_recv()
        for item in third_far(u) + twin_second(u):
            item.start()

    def stage_twin(u):
        for item in third_own(u) + third_far(u):
            item.wait_recv()
        for item in twin_third(u):
            item.start()

    def far_copy(matrix):
        return pltpu.make_async_copy(outs[matrix], far[matrix], local.at[count + matrix])

    def stage_end(u):
        for item in twin_own(u) + twin_second(u) + twin_third(u):
            item.wait_recv()
        if u + 1 == count or UNITS[u + 1][0] != UNITS[u][0]:
            far_copy(UNITS[u][0]).start()

    stages = (stage_line, stage_second, stage_third, stage_twin, stage_end)
    pending = list(FORWARD_ORDER)

    def hook():
        for stage, u in pending.pop(0):
            stages[stage](u)

    def ready(number):
        lax.fori_loop(1, 32, finish, 0)

    def out_copy(at):
        return pltpu.make_async_copy(saved[at], saved_far[at], out_sem.at[at])

    def emit(*numbers):
        for number in numbers:
            out_copy(number).start()

    def finish(step, carry):
        small_copy(step).wait()
        return carry

    views = [w.reshape(2, D, n) for w, n in zip(outs, MATRICES)]
    forward_body(small_out, contact_head, views, saved, scratch, ready, hook, emit)
    assert not pending
    for u in range(count):
        pair_copy(u).wait_send()
        for step in (1, 2, 3):
            line_copy(u, step).wait_send()
        sent = second(u) + third_own(u) + third_far(u) + twin_own(u) + twin_second(u) + twin_third(u)
        for item in sent:
            item.wait_send()
    for matrix in range(parts):
        far_copy(matrix).wait()
    for at in range(len(SAVED)):
        out_copy(at).wait()


def forward_call(raw, contact_head):
    count, parts = len(UNITS), len(MATRICES)
    anywhere = pl.BlockSpec(memory_space=pl.ANY)
    shapes = [(2, NZ, NY, 2, 48, n) for n in MATRICES]
    widths = [n for _, _, n, _ in UNITS]
    outs = pl.pallas_call(
        forward_kernel,
        out_shape=[jax.ShapeDtypeStruct(shape, BF16) for shape in shapes]
        + [jax.ShapeDtypeStruct(*item) for item in SAVED],
        in_specs=[anywhere] * 11 + [pl.BlockSpec(memory_space=pltpu.SMEM)],
        out_specs=[anywhere] * (parts + len(SAVED)),
        scratch_shapes=[pltpu.VMEM(shape, BF16) for shape in shapes]
        + [pltpu.VMEM((32, n), BF16) for n in widths] * 2
        + [pltpu.VMEM((48, n), BF16) for n in widths]
        + [pltpu.VMEM(*item) for item in SAVED]
        + [pltpu.VMEM(*item) for item in FORWARD]
        + [pltpu.VMEM(item.shape, item.dtype) for item in raw]
        + [
            pltpu.VMEM((16, 128), jnp.int32),
            pltpu.VMEM((32, 16, 128), jnp.int32),
            pltpu.VMEM((2, 24, 128), F32),
            pltpu.VMEM((128, 128), F32),
            pltpu.SemaphoreType.DMA((32,)),
            pltpu.SemaphoreType.DMA((32,)),
            pltpu.SemaphoreType.DMA((count, 17)),
            pltpu.SemaphoreType.DMA((count, 17)),
            pltpu.SemaphoreType.DMA((count + parts,)),
            pltpu.SemaphoreType.DMA((len(SAVED),)),
            pltpu.SemaphoreType.DMA((len(raw),)),
        ],
        compiler_params=pltpu.CompilerParams(
            collective_id=0, has_side_effects=True, vmem_limit_bytes=62 * 2**20
        ),
    )(*raw, contact_head)
    return outs[:parts], Saved(*outs[parts:])


def summed_rows(sums, start, groups, rows):
    parts = [
        jnp.concatenate([sums[2 * (start + g)], sums[2 * (start + g) + 1]], 1) for g in range(groups)
    ]
    if rows > 8 * groups:
        parts.append(jnp.zeros((rows - 8 * groups, D), F32))
    return jnp.concatenate(parts, 0) if len(parts) > 1 else parts[0]


def table_finish(sums, table_ref, norms_ref, proj_t, in_row, g_in, g_emb, g_norm):
    z, y, k, c = place()
    me = ((z * 2 + y) * 2 + c) * 2 + k
    pair = summed_rows(sums, 0, 5, VP)
    value_grad = summed_rows(sums, 5, 5, VP)
    table_grad = summed_rows(sums, 10, 5, VP)
    vectors = summed_rows(sums, 15, 1, 8)
    pair_hi, pair_lo = split_two(pair)
    scale = (HD * ROWS) ** (-0.5)
    query_grad, key_grad = [], []
    for hp in range(PAIRS):
        lanes = slice(hp * 128, hp * 128 + 128)
        query = proj_t[:, lanes]
        key = stacked(proj_t[:, D + hp * 128 : D + hp * 128 + 128])
        high, low = pair_hi[:, lanes], pair_lo[:, lanes]
        query_grad.append((nn(high, key) + nn(low, key)) * scale)
        key_grad.append(unstacked(tn(high, query) + tn(low, query), VP) * scale)
    proj_hi, proj_lo = split_two(jnp.concatenate(query_grad + key_grad + [value_grad], 1))
    normed_grad = jnp.zeros((VP, D), F32)
    for half in range(2):
        lanes = slice(half * 1152, half * 1152 + 1152)
        matrix = in_row[half]
        normed_grad = normed_grad + nt(proj_hi[:, lanes], matrix) + nt(proj_lo[:, lanes], matrix)
    unit, rstd = norm_stats(table_ref[...])
    gain = norms_ref[0:1, :]
    back, scale_0, shift_0 = norm_back(unit, rstd, gain, normed_grad)
    table_grad = table_grad + back
    line = iota((16, D), 0)
    norm_grad = jnp.zeros((16, D), F32)
    rows = [scale_0[None]] + [vectors[n : n + 1] for n in range(3)]
    rows += [shift_0[None]] + [vectors[n : n + 1] for n in range(3, 6)]
    for number, row in enumerate(rows):
        norm_grad = jnp.where(line == number, row, norm_grad)
    shard = D // 32
    pick = one_zero(iota((shard, D), 1) == iota((shard, D), 0) + me * shard).astype(BF16)
    normed = (unit * gain + norms_ref[4:5, :]).astype(BF16)
    mine = nt(pick, normed).astype(BF16)
    in_grad = nn(mine, proj_hi) + nn(mine, proj_lo)
    g_in[...] = in_grad

    def three(values):
        top, rest = split_two(values)
        return top, rest, (values - top.astype(F32) - rest.astype(F32)).astype(BF16)

    emb_grad = sum(nt(pick, part) for part in three(table_grad))
    g_emb[...] = emb_grad
    own_norm = sum(nt(part, pick) for part in three(norm_grad))[:8]
    g_norm[...] = own_norm
    return total_of(in_grad * in_grad) + total_of(emb_grad * emb_grad) + total_of(own_norm * own_norm)


GRAD_WIDTHS = (768, 768, 768, 768, 384, 1152, 384)
GRAD_UNITS = (
    (0, 0, 768, True),
    (1, 0, 768, True),
    (2, 0, 768, True),
    (3, 0, 768, True),
    (4, 0, 384, False),
    (5, 0, 384, True),
    (5, 384, 384, True),
    (5, 768, 384, True),
    (6, 0, 384, False),
)
BACKWARD_ORDER = (
    (),
    (),
    (),
    (),
    (),
    (),
    (),
    (),
    (),
    ((0, 0),),
    (),
    (),
    ((0, 1),),
    (),
    (),
    (),
    ((0, 2), (1, 0),),
    (),
    (),
    ((0, 3),),
    ((1, 1),),
    ((0, 4),),
    (),
    ((1, 2),),
    ((2, 0),),
    (),
    (),
    (),
    (),
    ((1, 3),),
    (),
    ((3, 0), (2, 1), (0, 5), (0, 6), (1, 4), (4, 0), (0, 7),),
    (),
    ((2, 2),),
    (),
    ((2, 3), (3, 1), (0, 8),),
    ((4, 1), (1, 5),),
    ((1, 6), (3, 2), (2, 4),),
    ((4, 2), (1, 7),),
    ((3, 3), (1, 8), (2, 5), (4, 3), (3, 4), (2, 6), (5, 0), (2, 7), (3, 5), (2, 8), (4, 4), (4, 5), (3, 6), (4, 6), (6, 0), (3, 7), (4, 7), (3, 8), (4, 8),),
)


class Kept(typing.NamedTuple):
    stream: typing.Any
    norms: typing.Any
    table: typing.Any
    proj_t: typing.Any
    extras: typing.Any
    moved: typing.Any
    grad_head: typing.Any
    touch: typing.Any
    value_two: typing.Any


class Early(typing.NamedTuple):
    slope: typing.Any
    active: typing.Any
    feed_normed_t: typing.Any
    unit_2: typing.Any
    rstd_2: typing.Any
    col_mixed_t: typing.Any
    col_proj: typing.Any
    col_prob: typing.Any
    col_normed_t: typing.Any
    unit_1: typing.Any
    rstd_1: typing.Any


class Late(typing.NamedTuple):
    row_mixed_t: typing.Any
    hot_all: typing.Any
    weight_hi: typing.Any
    prob: typing.Any
    hot_ri: typing.Any
    hot_ir: typing.Any


def pick_items(group, source):
    return [getattr(source, name) for name in group._fields]


def backward_kernel(*refs):
    widths = GRAD_WIDTHS
    count = len(widths)
    contact_head = refs[0]
    far = refs[1 : 1 + count]
    in_row_far = refs[1 + count]
    saved = Saved(*refs[2 + count : 2 + count + len(SAVED)])
    at = 2 + count + len(SAVED)
    outs = refs[at : at + count]
    g_in, g_emb, g_norm, stats = refs[at + count : at + count + 4]
    at += count + 4
    grads = refs[at : at + count]
    kept = Kept(*refs[at + count : at + count + len(Kept._fields)])
    at += count + len(Kept._fields)
    upstream, branch, branch_t, mixed = refs[at : at + 4]
    scratch = refs[at + 4 :]
    units = len(GRAD_UNITS)
    got_0, got_1a, got_1b, got_2a, got_2b, got_3, total, got_4 = (
        scratch[i * units : (i + 1) * units] for i in range(8)
    )
    table, table_out, table_got, square, square_got = scratch[8 * units : 8 * units + 5]
    table_send, table_recv, send, recv, local = scratch[8 * units + 5 :]
    z, y, k, c = place()
    me = (z * 4 + y * 2 + k) * 2 + c
    across, beside, twin = device(z, y, k, 1 - c), device(z, 1 - y, k, c), device(z, y, 1 - k, c)
    barrier = greet_all()
    stream = kept.stream

    copies = {}

    def load(number, source, target):
        copies[number] = pltpu.make_async_copy(source, target, local.at[number])
        copies[number].start()

    def need(*numbers):
        for number in numbers:
            copies[number].wait()

    def weight(m):
        return len(SAVED) + m

    def copy(m, at, src, dst, target):
        return remote(src, dst, send.at[m, at], recv.at[m, at], target)

    low, high = pl.ds(0, 2), pl.ds(2, 2)
    every = slice(None)

    def where(u, cc, zz, yy):
        matrix, start, n, paired = GRAD_UNITS[u]
        index = spot(paired, cc, zz, yy, k)
        return index if n == widths[matrix] else (*index, every, pl.ds(start, n))

    def block(u, cc, zz, yy):
        return grads[GRAD_UNITS[u][0]].at[where(u, cc, zz, yy)]

    def ordered(u, cc, rest):
        return (*rest, cc) if GRAD_UNITS[u][3] else (cc, *rest)

    def twin_copy(u):
        matrix, start, n, paired = GRAD_UNITS[u]
        index = (1 - k,) if paired else (every, every, every, 1 - k)
        if n != widths[matrix]:
            index = (*index, *(every,) * (5 - len(index)), pl.ds(start, n))
        return copy(u, 0, grads[matrix].at[index], got_0[u], twin)

    def first(u):
        return [
            copy(u, 1, block(u, every, low, 1 - y), got_1a[u], beside),
            copy(u, 2, block(u, 1 - c, high, every), got_1b[u], across),
        ]

    def second(u):
        return [
            copy(u, 3, block(u, 1 - c, low, y), got_2a[u], across),
            copy(u, 4, block(u, c, high, 1 - y), got_2b[u], beside),
        ]

    def along(u):
        return [
            copy(
                u,
                4 + step,
                block(u, c, lax.rem(z + step, 4), y),
                got_3[u].at[step - 1],
                device(lax.rem(z + step, 4), y, k, c),
            )
            for step in (1, 3, 2)
        ]

    def mine(u):
        return k if GRAD_UNITS[u][3] else c

    def pair(u):
        return [copy(u, 8, total[u].at[1 - mine(u)], got_4[u], twin if GRAD_UNITS[u][3] else across)]

    def table_copy(step, back):
        other = lax.rem(me + step, 32)
        target = (other // 2, lax.rem(other, 2))
        if back:
            return remote(
                table_out.at[me], table_out.at[me], table_send.at[1, step], table_recv.at[1, step], target
            )
        return remote(
            table.at[other], table_got.at[me], table_send.at[0, step], table_recv.at[0, step], target
        )

    def each(action):
        def body(step, carry):
            action(step)
            return carry

        lax.fori_loop(1, 32, body, 0)

    def gather_into(u, cc, zz, yy, *others):
        matrix = GRAD_UNITS[u][0]
        index = where(u, cc, zz, yy)
        value = grads[matrix][index].astype(F32) + got_0[u][ordered(u, cc, (zz, yy))].astype(F32)
        for other in others:
            value = value + other.astype(F32)
        grads[matrix][index] = value.astype(BF16)

    def stage_first(u):
        twin_copy(u).wait_recv()
        for a in range(2):
            for b in range(2):
                gather_into(u, a, b, 1 - y)
                gather_into(u, 1 - c, 2 + a, b)
        for item in first(u):
            item.start()

    def from_beside(u, cc, a):
        return got_1a[u][ordered(u, cc, (a,))]

    def stage_second(u):
        for item in first(u):
            item.wait_recv()
        for a in range(2):
            gather_into(u, 1 - c, a, y, from_beside(u, 1 - c, a))
            gather_into(u, c, 2 + a, 1 - y, got_1b[u][a, 1 - y])
        for item in second(u):
            item.start()

    def stage_along(u):
        for item in second(u):
            item.wait_recv()
        for a in range(2):
            gather_into(u, c, a, y, from_beside(u, c, a), got_2a[u][a])
            gather_into(u, c, 2 + a, y, got_1b[u][a, y], got_2b[u][a])
        for item in along(u):
            item.start()

    def stage_pair(u):
        for item in along(u):
            item.wait_recv()
        full = grads[GRAD_UNITS[u][0]][where(u, c, z, y)].astype(F32)
        for step in range(3):
            full = full + got_3[u][step].astype(F32)
        total[u][0] = full[:24]
        total[u][1] = full[24:]
        for item in pair(u):
            item.start()

    def stage_end(u):
        matrix, start, n, _ = GRAD_UNITS[u]
        lanes = slice(start, start + n)
        side = mine(u)
        outs[matrix][side, :, lanes] = total[u][side]
        for item in pair(u):
            item.wait_recv()
        outs[matrix][1 - side, :, lanes] = got_4[u][...]

    def table_sum(u):
        table_got[me] = table[me]
        each(lambda step: table_copy(step, False).wait_recv())
        table_out[me] = lax.fori_loop(1, 32, lambda at, held: held + table_got[at], table_got[0])
        each(lambda step: table_copy(step, True).start())

    late_parts = []

    def table_end(u):
        each(lambda step: table_copy(step, True).wait_recv())
        need(weight(count))
        found = table_finish(
            table_out, kept.table, kept.norms, kept.proj_t, late_parts[0].reshape(2, D, 1152), g_in, g_emb, g_norm
        )
        square[...] = jnp.broadcast_to(found, (8, 128))

    stages = (stage_first, stage_second, stage_along, stage_pair, stage_end, table_sum, table_end)
    pending = list(BACKWARD_ORDER)

    def hook():
        for stage, u in pending.pop(0):
            stages[stage](u)

    def done(u):
        if u == 0:
            pl.semaphore_wait(barrier, 31)
        twin_copy(u).start()
        hook()

    names = Kept._fields
    for name in names:
        load(getattr(AT, name), getattr(saved, name), getattr(kept, name))

    def phase_one(*early_refs):
        e = Early(*early_refs)
        load(weight(0), far[0], grads[0])
        load(AT.slope, saved.slope, e.slope)
        load(AT.active, saved.active, e.active)
        for m in (1, 2, 3):
            load(weight(m), far[m], grads[m])
        for name in Early._fields[2:6]:
            load(getattr(AT, name), getattr(saved, name), getattr(e, name))
        load(weight(4), far[4], grads[4])
        for name in Early._fields[6:8]:
            load(getattr(AT, name), getattr(saved, name), getattr(e, name))
        load(weight(5), far[5], grads[5])
        for name in Early._fields[8:]:
            load(getattr(AT, name), getattr(saved, name), getattr(e, name))
        load(weight(6), far[6], grads[6])
        view = [g.reshape(2, D, n) for g, n in zip(grads, widths)]
        need(*(getattr(AT, name) for name in names))
        norms = kept.norms[...]

        def gain(number):
            return norms[number : number + 1, :]

        def narrow(at, carry):
            rows = pl.ds(pl.multiple_of(at * 32, 32), 32)
            branch[rows, :] = stream[rows, :].astype(BF16)
            return carry

        lax.fori_loop(0, HERE // 32, narrow, 0)
        transpose_into(branch, branch_t)
        hook()

        def grad_tile(m, start, left_t, right, half, at):
            lanes = slice(start + half * widths[m] + at, start + half * widths[m] + at + 384)
            view[m][half, :, at : at + 384] = nn(left_t[...], right[:, lanes]).astype(BF16)

        def grad_half(m, start, left_t, right, half):
            for at in range(0, widths[m], 384):
                grad_tile(m, start, left_t, right, half, at)

        for part in range(2):
            need(weight(part))
            if part == 0:
                need(AT.slope)

            for half in range(2):
                for at in (0, 384):
                    lanes = slice(part * 1536 + half * 768 + at, part * 1536 + half * 768 + at + 384)
                    back = nn(branch[...], view[part][half, :, at : at + 384])
                    e.slope[:, lanes] = (back * e.slope[:, lanes].astype(F32)).astype(BF16)
                hook()
            if part == 0:
                need(AT.active)
            grad_half(part, part * 1536, branch_t, e.active, 0)
            hook()
            grad_half(part, part * 1536, branch_t, e.active, 1)
            done(part)
        for part in range(2):
            need(weight(2 + part))
            for half in range(2):
                start = part * 1536 + half * 768
                back = nt(e.slope[:, start : start + 768], view[2 + part][half])
                upstream[...] = back if start == 0 else upstream[...] + back
                hook()
            if part == 0:
                need(AT.feed_normed_t)
            grad_half(2 + part, part * 1536, e.feed_normed_t, e.slope, 0)
            hook()
            grad_half(2 + part, part * 1536, e.feed_normed_t, e.slope, 1)
            done(2 + part)
        need(AT.unit_2, AT.rstd_2)
        scale_2, shift_2 = back_rows(e.unit_2, e.rstd_2, gain(2), upstream, stream, branch, False)
        hook()
        need(weight(4), AT.col_mixed_t)
        mixed[...] = (nt(branch[:, :384], view[4][0]) + nt(branch[:, 384:], view[4][1])).astype(BF16)
        hook()
        for half in range(2):
            grad_half(4, 0, e.col_mixed_t, branch, half)
        done(4)
        need(AT.col_proj, AT.col_prob)
        proj = e.active

        def attend(at, carry):
            rows = pl.ds(pl.multiple_of((at // PAIRS) * 128, 128), 128)
            lane = lax.rem(at, PAIRS) * 128

            def lanes(part):
                return pl.ds(pl.multiple_of(part * D + lane, 128), 128)

            query = stacked(e.col_proj[rows, lanes(0)])
            key = e.col_proj[rows, lanes(1)]
            value = e.col_proj[rows, lanes(2)]
            above = stacked(mixed[rows, lanes(0)])
            prob = e.col_prob[at]
            grad = nt(above, value)
            grad = prob * (grad - jnp.sum(prob * grad, -1, keepdims=True))
            small = grad.astype(BF16)
            scale = HD ** (-0.5)
            proj[rows, lanes(0)] = (unstacked(nn(small, key), 128) * scale).astype(BF16)
            proj[rows, lanes(1)] = (tn(small, query) * scale).astype(BF16)
            proj[rows, lanes(2)] = tn(prob.astype(BF16), above).astype(BF16)
            return carry

        for part in range(6):
            lax.fori_loop(4 * part, 4 * part + 4, attend, 0, unroll=2)
            hook()
        need(weight(5))
        for half in range(2):
            back = nt(proj[:, half * 1152 : half * 1152 + 1152], view[5][half])
            upstream[...] = back if half == 0 else upstream[...] + back
            hook()
        need(AT.col_normed_t)
        for third in range(3):
            for half in range(2):
                grad_tile(5, 0, e.col_normed_t, proj, half, third * 384)
            done(5 + third)
        need(AT.unit_1, AT.rstd_1)
        scale_1, shift_1 = back_rows(e.unit_1, e.rstd_1, gain(1), upstream, stream, branch, False)
        hook()
        need(weight(6))
        mixed[...] = (nt(branch[:, :384], view[6][0]) + nt(branch[:, 384:], view[6][1])).astype(BF16)
        line = iota((8, D), 0)
        vectors = jnp.zeros((8, D), F32)
        moved = kept.moved[...]
        rows = (scale_1, scale_2, moved[0:1], shift_1, shift_2, moved[1:2])
        for number, row in enumerate(rows):
            vectors = jnp.where(line == number, row, vectors)
        extras = jnp.concatenate([kept.extras[0:1, :], jnp.zeros((1, D - 128), F32)], 1)
        kept.moved[...] = jnp.where(line == 6, extras, vectors)
        hook()

    pl.run_scoped(phase_one, *(pltpu.VMEM(*item) for item in pick_items(Early, SAVED)))

    def phase_two(*late_refs):
        e = Late(*late_refs[:-3])
        in_row, left_hi, left_lo = late_refs[-3:]
        for name in Late._fields:
            load(getattr(AT, name), getattr(saved, name), getattr(e, name))
        load(weight(count), in_row_far, in_row)
        view = grads[6].reshape(2, D, widths[6])
        late_parts.append(in_row)
        need(AT.row_mixed_t)
        for half in range(2):
            lanes = slice(half * 384, half * 384 + 384)
            view[half] = nn(e.row_mixed_t[...], branch[:, lanes]).astype(BF16)
        done(8)
        need(AT.hot_all, AT.weight_hi, AT.prob, AT.hot_ri, AT.hot_ir)
        shape = (HERE, HERE)
        back = (
            ((iota(shape, 1) >> 4) == (iota(shape, 0) & 31))
            & ((iota(shape, 1) & 15) == (iota(shape, 0) >> 5))
        )
        mixed[...] = nn(one_zero(back).astype(BF16), mixed[...]).astype(BF16)
        value_rows = []
        for hp in range(PAIRS):
            lanes = slice(hp * 128, hp * 128 + 128)
            part = mixed[:, lanes]
            upstream[:, lanes] = nt(part, kept.value_two[hp])
            value_rows.append(unstacked(tn(e.weight_hi[:, lanes], part), 64))
        hook()
        split_heads_to(upstream, left_hi, left_lo)
        hook()
        hot_all = e.hot_all[...]
        grad = nn(left_hi[...], hot_all) + nn(left_lo[...], hot_all)
        extra = jnp.concatenate(
            [kept.touch[...] * (contact_head[h] * COLS) for h in range(HEADS)], 0
        )
        grad = grad + extra
        prob = e.prob[...]
        grad = prob * (grad - jnp.sum(prob * grad, -1, keepdims=True))
        low_grad = grad.astype(BF16)
        hook()
        merge_heads(low_grad, e.hot_all, branch, None)
        hook()
        table_pair = nn(e.hot_ri[...], branch[...])
        stream_hi, stream_lo = split_two(stream[...])
        hot_ir = e.hot_ir[...]
        table_grad = kept.grad_head[...] + nn(hot_ir, stream_hi) + nn(hot_ir, stream_lo)
        value_grad = jnp.concatenate(value_rows, 1)
        blocks = ((0, table_pair), (5, value_grad), (10, table_grad), (15, kept.moved[...]))
        for start, block in blocks:
            for group in range(min(5, block.shape[0] // 8)):
                for half in range(2):
                    table[2 * (start + group) + half] = block[
                        group * 8 : group * 8 + 8, half * 384 : half * 384 + 384
                    ]
        each(lambda step: table_copy(step, False).start())
        hook()
        hook()

    pl.run_scoped(
        phase_two,
        *(pltpu.VMEM(*item) for item in pick_items(Late, SAVED)),
        pltpu.VMEM((2, NZ, NY, 2, 48, 1152), BF16),
        pltpu.VMEM((HEADS * WIDE, ROWS * VP), BF16),
        pltpu.VMEM((HEADS * WIDE, ROWS * VP), BF16),
    )
    assert not pending
    local_square = jnp.zeros((1, 1), F32)
    for m in range(count):
        for half in range(2):
            local_square = local_square + total_of(outs[m][half] * outs[m][half])

    def square_copy(step):
        other = lax.rem(me + step, 32)
        return remote(
            square, square_got.at[me], table_send.at[2, step], table_recv.at[2, step], (other // 2, lax.rem(other, 2))
        )

    square[...] = square[...] + local_square
    each(lambda step: square_copy(step).start())
    square_got[me] = square[...]
    each(lambda step: square_copy(step).wait())
    total_square = lax.fori_loop(1, 32, lambda at, held: held + square_got[at], square_got[0])[0:1]
    vector = table_out[30, 6:7, :128]
    counted = kept.extras[1:2, :]
    column = iota((1, 128), 1)
    contact = jnp.where(column <= HEADS, vector, 0.0)
    total_square = total_square + total_of(contact * contact)
    grad_norm = jnp.sqrt(total_square)
    factor = jnp.minimum(1.0, MAX_NORM / grad_norm)
    losses = (
        (0, vector[:, HEADS + 1 : HEADS + 2]),
        (1, counted[:, 0:1]),
        (2, vector[:, HEADS + 2 : HEADS + 3]),
        (3, counted[:, 1:2]),
    )
    loss_row = jnp.zeros((1, 128), F32)
    for at, value in losses:
        loss_row = jnp.where(column == at, value, loss_row)
    number = iota((8, 128), 0)
    result = jnp.zeros((8, 128), F32)
    for at, row in enumerate((contact, counted, factor, grad_norm, loss_row)):
        result = jnp.where(number == at, row, result)
    stats[...] = result
    each(lambda step: table_copy(step, True).wait_send())
    each(lambda step: table_copy(step, False).wait_send())
    for u in range(units):
        for item in [twin_copy(u)] + first(u) + second(u) + along(u) + pair(u):
            item.wait_send()


def backward_call(contact_head, weights, in_row, saved):
    widths = GRAD_WIDTHS
    count = len(widths)
    inside = pl.BlockSpec(memory_space=pltpu.VMEM)
    anywhere = pl.BlockSpec(memory_space=pl.ANY)

    units = len(GRAD_UNITS)

    def shapes(lead, dtype):
        return [pltpu.VMEM((*lead, n), dtype) for _, _, n, _ in GRAD_UNITS]

    outs = pl.pallas_call(
        backward_kernel,
        out_shape=[jax.ShapeDtypeStruct((2, 24, n), F32) for n in widths]
        + [
            jax.ShapeDtypeStruct((24, 3 * D), F32),
            jax.ShapeDtypeStruct((24, VP), F32),
            jax.ShapeDtypeStruct((8, 24), F32),
            jax.ShapeDtypeStruct((8, 128), F32),
        ],
        in_specs=[pl.BlockSpec(memory_space=pltpu.SMEM)] + [anywhere] * (1 + count + len(SAVED)),
        out_specs=[inside] * (4 + count),
        scratch_shapes=[pltpu.VMEM((2, NZ, NY, 2, 48, n), BF16) for n in widths]
        + [pltpu.VMEM(*item) for item in pick_items(Kept, SAVED)]
        + [
            pltpu.VMEM((HERE, D), F32),
            pltpu.VMEM((HERE, D), BF16),
            pltpu.VMEM((D, HERE), BF16),
            pltpu.VMEM((HERE, D), BF16),
        ]
        + [
            pltpu.VMEM((NZ, NY, 2, 48, n) if paired else (2, NZ, NY, 48, n), BF16)
            for _, _, n, paired in GRAD_UNITS
        ]
        + shapes((2, 2, 48), BF16)
        + shapes((2, 2, 48), BF16)
        + shapes((2, 48), BF16)
        + shapes((2, 48), BF16)
        + shapes((3, 48), BF16)
        + shapes((2, 24), F32)
        + shapes((24,), F32)
        + [
            pltpu.VMEM((32, 8, 384), F32),
            pltpu.VMEM((32, 8, 384), F32),
            pltpu.VMEM((32, 8, 384), F32),
            pltpu.VMEM((8, 128), F32),
            pltpu.VMEM((32, 8, 128), F32),
            pltpu.SemaphoreType.DMA((3, 32)),
            pltpu.SemaphoreType.DMA((3, 32)),
            pltpu.SemaphoreType.DMA((units, 9)),
            pltpu.SemaphoreType.DMA((units, 9)),
            pltpu.SemaphoreType.DMA((len(SAVED) + count + 1,)),
        ],
        compiler_params=pltpu.CompilerParams(
            collective_id=1, has_side_effects=True, vmem_limit_bytes=63 * 2**20
        ),
    )(contact_head, *weights, in_row, *saved)
    return outs[:count], outs[count:]


UPDATE_RATES = (LEARN_RATE,) * 4 + (VECTOR_RATE,) * 3


def update_kernel(*refs):
    given, outs, copies = refs[:32], refs[32:53], refs[53:58]
    loss_ref, norm_ref = refs[58:60]
    held, sems = refs[60:92], refs[92]
    moves = [pltpu.make_async_copy(a, b, sems.at[n]) for n, (a, b) in enumerate(zip(given, held))]
    for item in moves:
        item.start()
    reduced, g_in, g_emb, g_norm, stats = held[:7], held[7], held[8], held[9], held[10]
    states = [held[11 + 3 * n : 14 + 3 * n] for n in range(7)]
    outs = [outs[3 * n : 3 * n + 3] for n in range(7)]
    order = feature_order()
    for item in moves[4:11]:
        item.wait()
    factor = stats[2:3, 0:1]
    loss_ref[...] = stats[4:5, 0:4]
    norm_ref[...] = stats[3:4, 0:1]

    def natural(values):
        top, rest = split_two(values)
        last = (values - top.astype(F32) - rest.astype(F32)).astype(BF16)
        return nt(top, order) + nt(rest, order) + nt(last, order)

    def update(number, where, grad):
        master, first, second = (ref[where] for ref in states[number])
        new, first, second = adam_update(master, first, second, grad * factor, UPDATE_RATES[number])
        for ref, value in zip(outs[number], (new, first, second)):
            ref[where] = value
        if number < 5:
            copies[number][where] = new.astype(BF16)

    every = slice(None)
    g_out_col, g_in_col, g_out_row = reduced[4:]
    for item in moves[11:17]:
        item.wait()
    for half in range(2):
        lanes = slice(half * 1152, half * 1152 + 1152)
        update(0, (0, every, lanes), g_in[:, lanes])
        update(0, (1, every, lanes), g_in_col[half])
        lanes = slice(half * 384, half * 384 + 384)
        update(1, (0, every, lanes), natural(g_out_row[half]))
        update(1, (1, every, lanes), natural(g_out_col[half]))
    for item in moves[:4] + moves[17:]:
        item.wait()
    for half in range(2):
        for part in range(2):
            start = part * 1536 + half * 768
            lanes = slice(start, start + 768)
            update(2, (every, lanes), reduced[2 + part][half])
            update(3, (every, lanes), reduced[part][half])
    update(4, (every, every), g_emb[:, :VOCAB])
    update(5, (every, every), g_norm[...])
    update(6, (every, every), stats[0:1, : HEADS + 1])


def update_call(reduced, g_in, g_emb, g_norm, stats, states):
    inside = pl.BlockSpec(memory_space=pltpu.VMEM)
    anywhere = pl.BlockSpec(memory_space=pl.ANY)
    flat = [item for state in states for item in state]
    shapes = [jax.ShapeDtypeStruct(item.shape, F32) for item in flat]
    shapes += [jax.ShapeDtypeStruct(states[n][0].shape, BF16) for n in range(5)]
    shapes += [jax.ShapeDtypeStruct((1, 4), F32), jax.ShapeDtypeStruct((1, 1), F32)]
    given = (*reduced, g_in, g_emb, g_norm, stats, *flat)
    return pl.pallas_call(
        update_kernel,
        out_shape=shapes,
        in_specs=[anywhere] * len(given),
        out_specs=[inside] * len(shapes),
        scratch_shapes=[pltpu.VMEM(item.shape, F32) for item in given]
        + [pltpu.SemaphoreType.DMA((len(given),))],
        compiler_params=pltpu.CompilerParams(vmem_limit_bytes=48 * 2**20),
    )(*given)


def adam_update(master, first, second, grad_part, rate):
    first = BETA_ONE * first + (1.0 - BETA_ONE) * grad_part
    second = BETA_TWO * second + (1.0 - BETA_TWO) * grad_part * grad_part
    moved = first / (1.0 - BETA_ONE**STEP) / (jnp.sqrt(second / (1.0 - BETA_TWO**STEP)) + ADAM_EPS)
    return (master - rate * (moved + WEIGHT_DECAY * master), first, second)


def shards(
    tokens,
    targets,
    masked,
    contact_pairs,
    labels,
    attention_in_master,
    attention_in_first,
    attention_in_second,
    attention_out_master,
    attention_out_first,
    attention_out_second,
    feed_up_master,
    feed_up_first,
    feed_up_second,
    feed_down_master,
    feed_down_first,
    feed_down_second,
    embedding_master,
    embedding_first,
    embedding_second,
    norm_params_master,
    norm_params_first,
    norm_params_second,
    contact_head_master,
    contact_head_first,
    contact_head_second,
):
    both = ("seq", "col")
    micro, rows_here, cols_here = tokens.shape
    ncol = lax.axis_size("col")
    ndev = lax.axis_size("seq") * ncol
    cols = cols_here * ncol
    me = lax.axis_index("seq") * ncol + lax.axis_index("col")
    per = ndev // micro
    cw = cols // per
    mine = me // per
    base = (me % per) * cw
    shard = D // ndev

    tiled = lax.axis_size("seq") == 16 and ncol == 2
    if tiled:
        raw = (
            tokens,
            targets,
            masked,
            contact_pairs.transpose(0, 2, 1),
            labels,
            embedding_master.T,
            norm_params_master,
            attention_in_master,
            attention_out_master,
            feed_up_master,
            feed_down_master.T,
        )
        weights, saved = forward_call(raw, contact_head_master)
        reduced, (g_in, g_emb, g_norm, stats) = backward_call(
            contact_head_master, [weights[n] for n in (7, 8, 5, 6, 4, 3, 2)], weights[1], saved
        )
        states = (
            (attention_in_master, attention_in_first, attention_in_second),
            (attention_out_master, attention_out_first, attention_out_second),
            (feed_up_master, feed_up_first, feed_up_second),
            (feed_down_master.T, feed_down_first.T, feed_down_second.T),
            (embedding_master.T, embedding_first.T, embedding_second.T),
            (norm_params_master, norm_params_first, norm_params_second),
            (contact_head_master[None], contact_head_first[None], contact_head_second[None]),
        )
        outs = update_call(reduced, g_in, g_emb, g_norm, stats, states)
        return (
            *outs[:9],
            *(item.T for item in outs[9:15]),
            *outs[15:18],
            *(item[0] for item in outs[18:21]),
            *outs[21:24],
            *(item.T for item in outs[24:26]),
            outs[26][0],
            outs[27][0, 0],
        )
    inputs = jnp.where(masked > 0, MASK_ID, tokens)
    masters = [
        jnp.concatenate(
            [
                jnp.pad(embedding_master.T, ((0, 0), (0, 128 - VOCAB))),
                jnp.pad(norm_params_master.T, ((0, 0), (0, 120))),
            ],
            1,
        ),
        attention_in_master[0],
        attention_out_master[0],
        attention_in_master[1],
        attention_out_master[1],
        feed_up_master,
        feed_down_master.T,
    ]
    whole = jnp.stack([inputs, targets])
    whole = lax.all_gather(lax.all_gather(whole, "col", axis=3, tiled=True), "seq", axis=2, tiled=True)
    pairs_all = lax.all_gather(
        jnp.concatenate([contact_pairs, labels[:, :, None]], -1), both, axis=1, tiled=True
    )
    gathered = []
    for master in masters:
        full = lax.all_gather(master.astype(BF16), both, axis=0, tiled=True)
        gathered.append(full.reshape(D, 2, -1).transpose(1, 0, 2))
    counts = (
        jnp.sum(whole[0] == MASK_ID).astype(F32),
        jnp.sum(pairs_all[..., 2] >= 0).astype(F32),
    )
    ids_all = lax.dynamic_index_in_dim(whole[0], mine, 0, False)
    ids_local = lax.dynamic_slice_in_dim(ids_all, base, cw, 1)
    targets_local = lax.dynamic_slice_in_dim(
        lax.dynamic_index_in_dim(whole[1], mine, 0, False), base, cw, 1
    )
    pairs = lax.dynamic_index_in_dim(pairs_all, mine, 0, False)

    table = gathered[0][0][:, :VP].T
    norms = gathered[0][1][:, :8].T.astype(F32)
    in_row, out_row, in_col, out_col, up_w, down_t = (
        jnp.concatenate([g[0], g[1]], 1) for g in gathered[1:]
    )
    big = (in_row, in_col, out_row, out_col, up_w, down_t)

    grads, tables, contact_total, mlm_total, bce_total, kept = step(
        big,
        table,
        norms,
        contact_head_master,
        ids_all,
        ids_local.reshape(-1),
        ids_local.T.reshape(-1),
        targets_local.T.reshape(-1),
        pairs[:, 0] - base,
        pairs[:, 1],
        pairs[:, 2],
        counts,
        cw,
    )
    table_pair, value_grad, table_grad, vectors = tables
    extras = jnp.zeros((2, D), F32).at[0, : HEADS + 3].set(
        jnp.concatenate([contact_total, mlm_total[None], bce_total[None]])
    )
    sums = jnp.concatenate([table_pair[:40], value_grad[:40], table_grad[:40], vectors, extras])
    flat_grad = jnp.concatenate([g.astype(BF16) for g in grads], 1)
    reduced = lax.psum_scatter(flat_grad, both, scatter_dimension=0, tiled=True).astype(F32)
    g_in_col, g_out_row, g_out_col, g_up, g_down = jnp.split(
        reduced, [3 * D, 4 * D, 5 * D, 5 * D + FF], 1
    )
    sums = lax.psum(sums, both)
    unit_t, rstd_t, normed_t, query_t, key_t = kept
    rows_all = ids_all.shape[0]
    spare = ((0, VP - 40), (0, 0))
    table_pair, value_grad, table_grad = (
        jnp.pad(sums[a : a + 40], spare) for a in (0, 40, 80)
    )
    vectors = sums[120:126]
    contact_grad, mlm_total, bce_total = (
        sums[126, : HEADS + 1], sums[126, HEADS + 1], sums[126, HEADS + 2]
    )
    row_scale = (HD * rows_all) ** (-0.5)
    query_grad = []
    key_grad = []
    for h in range(HEADS):
        pair = heads_of(table_pair, h)
        query_grad.append(jnp.dot(pair, heads_of(key_t, h).astype(F32), precision=PRECISE))
        key_grad.append(jnp.dot(pair.T, heads_of(query_t, h).astype(F32), precision=PRECISE))
    proj_grad = jnp.concatenate(
        [
            jnp.concatenate(query_grad, 1) * row_scale,
            jnp.concatenate(key_grad, 1) * row_scale,
            value_grad,
        ],
        1,
    )
    proj_hi, proj_lo = split_two(proj_grad)
    normed_grad = nt(proj_hi, in_row) + nt(proj_lo, in_row)
    back_t, scale_0, shift_0 = norm_back(unit_t, rstd_t, norms[0], normed_grad)
    table_grad = table_grad + back_t
    low = me * shard
    normed_mine = lax.dynamic_slice_in_dim(normed_t, low, shard, 1)
    grad_in_row = tn(normed_mine, proj_hi) + tn(normed_mine, proj_lo)
    norm_grad = jnp.concatenate([scale_0[None], vectors[:3], shift_0[None], vectors[3:]])
    table_mine = lax.dynamic_slice_in_dim(table_grad[:VOCAB], low, shard, 1)
    norm_mine = lax.dynamic_slice_in_dim(norm_grad, low, shard, 1)
    reduced_all = (g_in_col, g_out_row, g_out_col, g_up, g_down)

    local_square = (
        sum(jnp.sum(g * g) for g in reduced_all)
        + jnp.sum(grad_in_row * grad_in_row)
        + jnp.sum(table_mine * table_mine)
        + jnp.sum(norm_mine * norm_mine)
    )
    square = lax.psum(local_square, both) + jnp.sum(contact_grad * contact_grad)
    grad_norm = jnp.sqrt(square)
    factor = jnp.minimum(1.0, MAX_NORM / grad_norm)
    in_new, in_moment, in_square = adam_update(
        attention_in_master, attention_in_first, attention_in_second, jnp.stack([grad_in_row, g_in_col]) * factor, LEARN_RATE
    )
    out_new, out_moment, out_square = adam_update(
        attention_out_master, attention_out_first, attention_out_second, jnp.stack([g_out_row, g_out_col]) * factor, LEARN_RATE
    )
    up_new, up_moment, up_square = adam_update(
        feed_up_master, feed_up_first, feed_up_second, g_up * factor, LEARN_RATE
    )
    down_new, down_moment, down_square = adam_update(
        feed_down_master, feed_down_first, feed_down_second, g_down.T * factor, LEARN_RATE
    )
    table_new, table_moment, table_square = adam_update(
        embedding_master, embedding_first, embedding_second, table_mine * factor, VECTOR_RATE
    )
    norm_new, norm_moment, norm_square = adam_update(
        norm_params_master, norm_params_first, norm_params_second, norm_mine * factor, VECTOR_RATE
    )
    head_new, head_moment, head_square = adam_update(
        contact_head_master, contact_head_first, contact_head_second, contact_grad * factor, VECTOR_RATE
    )
    loss_parts = jnp.stack([mlm_total, counts[0], bce_total, counts[1]])
    return (
        in_new, in_moment, in_square,
        out_new, out_moment, out_square,
        up_new, up_moment, up_square,
        down_new, down_moment, down_square,
        table_new, table_moment, table_square,
        norm_new, norm_moment, norm_square,
        head_new, head_moment, head_square,
        in_new.astype(BF16), out_new.astype(BF16), up_new.astype(BF16), down_new.astype(BF16), table_new.astype(BF16),
        loss_parts, grad_norm,
    )


def solution(mesh):
    both = ("seq", "col")
    cells = P(None, "seq", "col")
    stack = P(None, both, None)
    row_split = P(both, None)
    col_split = P(None, both)
    weights = [stack] * 6 + [row_split] * 3 + [col_split] * 9 + [P()] * 3
    return jax.shard_map(
        shards,
        mesh=mesh,
        in_specs=(cells, cells, cells, stack, col_split, *weights),
        out_specs=(*weights, stack, stack, row_split, col_split, col_split, P(), P()),
        check_vma=False,
    )
```

```python
import typing

import jax
import jax.numpy as jnp
from jax import lax
from jax.experimental import pallas as pl
from jax.experimental.pallas import tpu as pltpu
from jax.sharding import PartitionSpec as P

D = 768
HEADS = 12
HD = 64
FF = 3072
VOCAB = 33
VP = 64
STEP = 10

NORM_EPS = 1e-05
MASK_ID = 32
MAX_NORM = 0.001
LEARN_RATE = 0.05
VECTOR_RATE = 0.5
BETA_ONE = 0.9
BETA_TWO = 0.95
ADAM_EPS = 1e-08
WEIGHT_DECAY = 0.01
PRECISE = lax.Precision.HIGHEST
F32 = jnp.float32
BF16 = jnp.bfloat16


def nn(left, right):
    return lax.dot_general(left, right, (((1,), (0,)), ((), ())), preferred_element_type=F32)


def tn(left, right):
    return lax.dot_general(left, right, (((0,), (0,)), ((), ())), preferred_element_type=F32)


def nt(left, right):
    return lax.dot_general(left, right, (((1,), (1,)), ((), ())), preferred_element_type=F32)


def split_two(values):
    high = values.astype(BF16)
    return high, (values - high.astype(F32)).astype(BF16)


def norm_stats(values):
    centre = values - jnp.mean(values, -1, keepdims=True)
    rstd = lax.rsqrt(jnp.mean(centre * centre, -1, keepdims=True) + NORM_EPS)
    return centre * rstd, rstd


def norm_back(unit, rstd, scale_vec, upstream):
    inner = upstream * scale_vec
    grad = rstd * (
        inner - jnp.mean(inner, -1, keepdims=True) - unit * jnp.mean(inner * unit, -1, keepdims=True)
    )
    return grad, jnp.sum(upstream * unit, 0), jnp.sum(upstream, 0)


GELU_K = 0.7978845608028654
GELU_C = 0.044715


def gelu_parts(up):
    square = up * up
    bent = jnp.tanh(GELU_K * up * (1.0 + GELU_C * square))
    half = 0.5 * (1.0 + bent)
    slope = half + 0.5 * up * (1.0 - bent * bent) * GELU_K * (1.0 + 3.0 * GELU_C * square)
    return up * half, slope


def heads_of(block, head):
    return block[:, head * HD : (head + 1) * HD]


def step(big, table, norms, contact_head, ids_all, ids_ri, ids_ir, targets_ir, pair_first, pair_second, labels, counts, cw):
    in_row, in_col, out_row, out_col, up_w, down_t = big
    rows, cols = ids_all.shape
    here = rows * cw
    row_scale = (HD * rows) ** (-0.5)
    vocab = jnp.arange(VP)[:, None]
    hot_all = (ids_all[:, None, :] == vocab[None]).astype(BF16).reshape(rows * VP, cols)
    hot_ri = (ids_ri[None, :] == vocab).astype(BF16)
    hot_ir = (ids_ir[None, :] == vocab).astype(BF16)
    spot = jnp.arange(here)
    perm = (
        ((spot // rows)[:, None] == (spot % cw)[None, :])
        & ((spot % rows)[:, None] == (spot // cw)[None, :])
    ).astype(BF16)

    def to_heads(block):
        return block.reshape(rows, cw, HEADS, VP).transpose(2, 1, 0, 3).reshape(HEADS * cw, rows * VP)

    def to_tokens(block):
        return block.reshape(HEADS, cw, rows, VP).transpose(2, 1, 0, 3).reshape(here, HEADS * VP)

    def per_head(block, other, how):
        return jnp.concatenate(
            [how(heads_of(block, h), heads_of(other, h)) for h in range(HEADS)], -1
        )

    table_f = table.astype(F32)
    unit_t, rstd_t = norm_stats(table_f)
    normed_t = (unit_t * norms[0] + norms[4]).astype(BF16)
    proj_t = nn(normed_t, in_row).astype(BF16)
    query_t, key_t, value_t = proj_t[:, :D], proj_t[:, D : 2 * D], proj_t[:, 2 * D :]

    pair_t = per_head(query_t, key_t, nt)
    pair_hi, pair_lo = split_two(pair_t)
    left_hi = to_heads(tn(hot_ri, pair_hi).astype(BF16))
    left_lo = to_heads(tn(hot_ri, pair_lo).astype(BF16))
    score = (nn(left_hi, hot_all) + nn(left_lo, hot_all)) * row_scale
    prob = jax.nn.softmax(score, axis=-1)
    prob_low = prob.astype(BF16)
    weight_t = to_tokens(nt(prob_low, hot_all))
    weight_hi, weight_lo = split_two(weight_t)
    row_mixed_ri = (
        per_head(weight_hi, value_t, nn) + per_head(weight_lo, value_t, nn)
    ).astype(BF16)
    row_mixed = nn(perm, row_mixed_ri).astype(BF16)
    embedded = tn(hot_ir, table)
    after_row = embedded + nn(row_mixed, out_row)

    prob_cube = prob_low.astype(F32).reshape(HEADS, cw, cols)
    head_sum = jnp.sum(prob_cube * contact_head[:HEADS, None, None], 0)
    first_hot = (pair_first[None, :] == jnp.arange(cw)[:, None]).astype(F32)
    second_hot = (pair_second[None, :] == jnp.arange(cols)[:, None]).astype(BF16)
    sum_hi, sum_lo = split_two(head_sum)
    sum_last = (head_sum - sum_hi.astype(F32) - sum_lo.astype(F32)).astype(BF16)
    picked = nn(sum_hi, second_hot) + nn(sum_lo, second_hot) + nn(sum_last, second_hot)
    contact_logit = jnp.sum(picked * first_hot, 0) * cols + contact_head[HEADS]
    owned = jnp.sum(first_hot, 0) > 0
    valid = (labels >= 0) & owned
    positive = (labels == 1).astype(F32)
    bce_sum = jnp.sum(
        jnp.where(valid, jax.nn.softplus(contact_logit) - positive * contact_logit, 0.0)
    )
    coef = jnp.where(valid, jax.nn.sigmoid(contact_logit) - positive, 0.0) / counts[1]
    coef_hi, coef_lo = split_two(coef)
    first_low = first_hot.astype(BF16)
    touch = nt(first_low * coef_hi[None], second_hot) + nt(first_low * coef_lo[None], second_hot)
    grad_contact = jnp.concatenate(
        [jnp.sum(prob_cube * touch[None], (1, 2)) * cols, jnp.sum(coef)[None]]
    )

    unit_1, rstd_1 = norm_stats(after_row)
    col_normed = (unit_1 * norms[1] + norms[5]).astype(BF16)
    col_proj = nn(col_normed, in_col).astype(BF16)
    group = 128 if here % 128 == 0 and 128 % rows == 0 else here
    groups = here // group
    lane = jnp.arange(group)
    same = (lane[:, None] // rows) == (lane[None, :] // rows)

    def cut(block):
        return block.reshape(groups, group, HEADS, HD)

    col_query, col_key, col_value = (cut(col_proj[:, k * D : (k + 1) * D]) for k in range(3))
    col_score = jnp.einsum("gqhe,gkhe->ghqk", col_query, col_key, preferred_element_type=F32) * HD ** (-0.5)
    col_prob = jax.nn.softmax(jnp.where(same, col_score, -1e30), axis=-1)
    col_prob_low = col_prob.astype(BF16)
    col_mixed = (
        jnp.einsum("ghqk,gkhe->gqhe", col_prob_low, col_value, preferred_element_type=F32)
        .astype(BF16)
        .reshape(here, D)
    )
    after_col = after_row + nn(col_mixed, out_col)

    unit_2, rstd_2 = norm_stats(after_col)
    feed_normed = (unit_2 * norms[2] + norms[6]).astype(BF16)
    hidden_up = nn(feed_normed, up_w)
    active, slope = gelu_parts(hidden_up)
    active = active.astype(BF16)
    after_feed = after_col + nt(active, down_t)
    unit_3, rstd_3 = norm_stats(after_feed)
    head_normed = (unit_3 * norms[3] + norms[7]).astype(BF16)
    logits = nt(table, head_normed) * D ** (-0.5)
    logits = jnp.where(vocab < VOCAB, logits, -1e30)
    top = jnp.max(logits, 0, keepdims=True)
    shifted = logits - top
    log_probs = shifted - jnp.log(jnp.sum(jnp.exp(shifted), 0, keepdims=True))
    target_hot = (targets_ir[None, :] == vocab).astype(F32)
    keep = ids_ir[None, :] == MASK_ID
    mlm_sum = -jnp.sum(jnp.where(keep & (target_hot > 0), log_probs, 0.0))
    logit_grad = jnp.where(keep, jnp.exp(log_probs) - target_hot, 0.0) / counts[0]
    logit_low = (logit_grad * D ** (-0.5)).astype(BF16)

    grad_head = nn(logit_low, head_normed)
    stream, scale_3, shift_3 = norm_back(unit_3, rstd_3, norms[3], tn(logit_low, table))
    branch = stream.astype(BF16)
    grad_down = tn(branch, active)
    up_low = (nn(branch, down_t) * slope).astype(BF16)
    grad_up = tn(feed_normed, up_low)
    inner, scale_2, shift_2 = norm_back(unit_2, rstd_2, norms[2], nt(up_low, up_w))
    stream = stream + inner
    branch = stream.astype(BF16)
    grad_out_col = tn(col_mixed, branch)
    mixed_low = nt(branch, out_col).astype(BF16)
    mixed_cut = cut(mixed_low)
    prob_grad = jnp.einsum("gqhe,gkhe->ghqk", mixed_cut, col_value, preferred_element_type=F32)
    score_grad = col_prob * (prob_grad - jnp.sum(col_prob * prob_grad, -1, keepdims=True))
    score_low = score_grad.astype(BF16)
    grad_q = jnp.einsum("ghqk,gkhe->gqhe", score_low, col_key, preferred_element_type=F32)
    grad_k = jnp.einsum("ghqk,gqhe->gkhe", score_low, col_query, preferred_element_type=F32)
    grad_v = jnp.einsum("ghqk,gqhe->gkhe", col_prob_low, mixed_cut, preferred_element_type=F32)
    proj_low = jnp.concatenate(
        [
            (grad_q * HD ** (-0.5)).reshape(here, D),
            (grad_k * HD ** (-0.5)).reshape(here, D),
            grad_v.reshape(here, D),
        ],
        -1,
    ).astype(BF16)
    grad_in_col = tn(col_normed, proj_low)
    inner, scale_1, shift_1 = norm_back(unit_1, rstd_1, norms[1], nt(proj_low, in_col))
    stream = stream + inner
    branch = stream.astype(BF16)
    grad_out_row = tn(row_mixed, branch)
    mixed_low = nt(branch, out_row).astype(BF16)
    mixed_ri = tn(perm, mixed_low).astype(BF16)
    drive_hi, drive_lo = split_two(per_head(mixed_ri, value_t, nt))
    prob_grad = nn(to_heads(drive_hi), hot_all) + nn(to_heads(drive_lo), hot_all)
    prob_grad = prob_grad + (
        touch[None] * (contact_head[:HEADS, None, None] * cols)
    ).reshape(HEADS * cw, cols)
    score_grad = prob * (prob_grad - jnp.sum(prob * prob_grad, -1, keepdims=True))
    score_low = score_grad.astype(BF16)
    spread = to_tokens(nt(score_low, hot_all)).astype(BF16)
    table_pair = nn(hot_ri, spread)
    value_grad = per_head(weight_hi, mixed_ri, tn)
    stream_hi, stream_lo = split_two(stream)
    lookup_grad = nn(hot_ir, stream_hi) + nn(hot_ir, stream_lo)
    vectors = jnp.stack([scale_1, scale_2, scale_3, shift_1, shift_2, shift_3])
    return (
        (grad_in_col, grad_out_row, grad_out_col, grad_up, grad_down),
        (table_pair, value_grad, grad_head + lookup_grad, vectors),
        grad_contact,
        mlm_sum,
        bce_sum,
        (unit_t, rstd_t, normed_t, query_t, key_t),
    )


MESH = pl.DeviceIdType.MESH
NZ, NY = 4, 2


def place():
    s, c = lax.axis_index("seq"), lax.axis_index("col")
    z, y, k = s // 4, lax.rem(s // 2, 2), lax.rem(s, 2)
    return z, y, k, c


def device(z, y, k, c):
    return (z * 4 + y * 2 + k, c)


def greet_all():
    z, y, k, c = place()
    me = (z * 4 + y * 2 + k) * 2 + c
    barrier = pltpu.get_barrier_semaphore()

    def signal(step, carry):
        other = lax.rem(me + step, 32)
        pl.semaphore_signal(
            barrier, inc=1, device_id=(other // 2, lax.rem(other, 2)), device_id_type=MESH
        )
        return carry

    lax.fori_loop(1, 32, signal, 0)
    return barrier


def remote(src, dst, send, recv, target):
    return pltpu.make_async_remote_copy(
        src_ref=src, dst_ref=dst, send_sem=send, recv_sem=recv, device_id=target, device_id_type=MESH
    )


ROWS, COLS, WIDE, HERE = 16, 512, 32, 512
PAIRS = 6
SLOTS = 1024
UP_TILE = 384


def iota(shape, dim):
    return lax.broadcasted_iota(jnp.int32, shape, dim)


def one_zero(test):
    return jnp.where(test, 1.0, 0.0)


def total_of(values):
    return jnp.sum(jnp.sum(values, 0, keepdims=True), 1, keepdims=True)


def half_lanes(values, side):
    lane = iota(values.shape, len(values.shape) - 1)
    keep = (lane < 64) if side == 0 else (lane >= 64)
    return jnp.where(keep, values.astype(F32), 0.0).astype(BF16)


def stacked(values):
    return jnp.concatenate([half_lanes(values, 0), half_lanes(values, 1)], 0)


def unstacked(values, count):
    lane = iota((count, 128), 1)
    return jnp.where(lane < 64, values[:count], values[count:])


def swap_blocks(first, second):
    lane = iota(first.shape, 1)
    low = jnp.where(lane < 64, first, pltpu.roll(second, 64, 1))
    high = jnp.where(lane < 64, pltpu.roll(first, 64, 1), second)
    return low, high


def split_heads_to(source, high_ref, low_ref):
    for rp in range(ROWS // 2):
        for hp in range(PAIRS):
            lanes = slice(hp * 128, hp * 128 + 128)
            first = source[rp * 64 : rp * 64 + 32, lanes]
            second = source[rp * 64 + 32 : rp * 64 + 64, lanes]
            for side, block in enumerate(swap_blocks(first, second)):
                top, rest = split_two(block)
                rows = slice((2 * hp + side) * 32, (2 * hp + side) * 32 + 32)
                high_ref[rows, rp * 128 : rp * 128 + 128] = top
                low_ref[rows, rp * 128 : rp * 128 + 128] = rest


def merge_heads(probs, hot_all, high_ref, low_ref):
    for rp in range(ROWS // 2):
        block = nt(probs, hot_all[rp * 128 : rp * 128 + 128, :])
        for hp in range(PAIRS):
            first = block[hp * 64 : hp * 64 + 32]
            second = block[hp * 64 + 32 : hp * 64 + 64]
            for side, part in enumerate(swap_blocks(first, second)):
                top, rest = split_two(part)
                rows = slice(rp * 64 + side * 32, rp * 64 + side * 32 + 32)
                high_ref[rows, hp * 128 : hp * 128 + 128] = top
                if low_ref is not None:
                    low_ref[rows, hp * 128 : hp * 128 + 128] = rest


def norm_rows(source, gain, bias, unit_ref, rstd_ref, normed_ref):
    def body(at, carry):
        rows = pl.ds(pl.multiple_of(at * 64, 64), 64)
        values = source[rows, :]
        centre = values - jnp.sum(values, -1, keepdims=True) * (1.0 / D)
        rstd = lax.rsqrt(jnp.sum(centre * centre, -1, keepdims=True) * (1.0 / D) + NORM_EPS)
        unit = centre * rstd
        unit_ref[rows, :] = unit
        rstd_ref[rows, :] = jnp.broadcast_to(rstd, (64, 128))
        normed_ref[rows, :] = (unit * gain + bias).astype(BF16)
        return carry

    lax.fori_loop(0, HERE // 64, body, 0)


def transpose_into(source, target):
    def body(at, carry):
        rows = pl.ds(pl.multiple_of(at * 128, 128), 128)
        target[:, rows] = source[rows, :].astype(F32).T.astype(BF16)
        return carry

    lax.fori_loop(0, HERE // 128, body, 0)


def over_tiles(width, tile, body):
    for half in range(2):

        def step(at, carry, half=half):
            body(half, pl.multiple_of(at * tile, tile))
            return carry

        lax.fori_loop(0, width // tile, step, 0)


def column_mask():
    rows, lanes = iota((256, 128), 0), iota((256, 128), 1)
    return ((rows & 127) >> 4) == (lanes >> 4)


class Saved(typing.NamedTuple):
    stream: typing.Any
    branch: typing.Any
    unit_1: typing.Any
    unit_2: typing.Any
    rstd_1: typing.Any
    rstd_2: typing.Any
    row_mixed_t: typing.Any
    col_normed_t: typing.Any
    col_mixed_t: typing.Any
    feed_normed_t: typing.Any
    col_proj: typing.Any
    col_prob: typing.Any
    active: typing.Any
    slope: typing.Any
    grad_head: typing.Any
    hot_all: typing.Any
    hot_ri: typing.Any
    hot_ir: typing.Any
    prob: typing.Any
    weight_hi: typing.Any
    value_two: typing.Any
    touch: typing.Any
    table: typing.Any
    norms: typing.Any
    proj_t: typing.Any
    extras: typing.Any
    moved: typing.Any


AT = Saved(*range(len(Saved._fields)))
SAVED = Saved(
    stream=((HERE, D), F32),
    branch=((HERE, D), BF16),
    unit_1=((HERE, D), F32),
    unit_2=((HERE, D), F32),
    rstd_1=((HERE, 128), F32),
    rstd_2=((HERE, 128), F32),
    row_mixed_t=((D, HERE), BF16),
    col_normed_t=((D, HERE), BF16),
    col_mixed_t=((D, HERE), BF16),
    feed_normed_t=((D, HERE), BF16),
    col_proj=((HERE, 3 * D), BF16),
    col_prob=((4 * PAIRS, 256, 128), F32),
    active=((HERE, FF), BF16),
    slope=((HERE, FF), BF16),
    grad_head=((VP, D), F32),
    hot_all=((ROWS * VP, COLS), BF16),
    hot_ri=((VP, HERE), BF16),
    hot_ir=((VP, HERE), BF16),
    prob=((HEADS * WIDE, COLS), F32),
    weight_hi=((HERE, D), BF16),
    value_two=((PAIRS, 128, 128), BF16),
    touch=((WIDE, COLS), F32),
    table=((VP, D), F32),
    norms=((8, D), F32),
    proj_t=((VP, 3 * D), BF16),
    extras=((8, 128), F32),
    moved=((8, D), F32),
)


class Forward(typing.NamedTuple):
    ids: typing.Any
    targets: typing.Any
    slots: typing.Any
    normed: typing.Any
    mixed: typing.Any
    weight_lo: typing.Any
    left_hi: typing.Any
    left_lo: typing.Any
    lookup: typing.Any
    prob_low: typing.Any
    unit: typing.Any
    rstd: typing.Any


FORWARD = Forward(
    ids=((ROWS, COLS), jnp.int32),
    targets=((ROWS, 128), jnp.int32),
    slots=((8, SLOTS), jnp.int32),
    normed=((HERE, D), BF16),
    mixed=((HERE, D), BF16),
    weight_lo=((HERE, D), BF16),
    left_hi=((HEADS * WIDE, ROWS * VP), BF16),
    left_lo=((HEADS * WIDE, ROWS * VP), BF16),
    lookup=((HERE, D), F32),
    prob_low=((HEADS * WIDE, COLS), BF16),
    unit=((HERE, D), F32),
    rstd=((HERE, 128), F32),
)


def position():
    z, y, k, c = place()
    me = (z * 4 + y * 2 + k) * 2 + c
    return z // 2, lax.rem(me, 16)


def read_tokens(small, f):
    alignment, block = position()
    side, part = block // 8, lax.rem(block // 4, 2)
    for r in range(ROWS):
        for cc in range(2):
            for q in range(2):
                lanes = slice(cc * 256 + q * 128, cc * 256 + q * 128 + 128)
                f.ids[r : r + 1, lanes] = small[r * 2 + cc, pl.ds(2 * alignment + q, 1), :]
        f.targets[r : r + 1, :] = small[r * 2 + side, pl.ds(4 + 2 * alignment + part, 1), :]
    lane = iota((1, 128), 1)
    for number in range(SLOTS // 128):
        for which in range(3):
            row = pl.ds(8 + 3 * alignment + which, 1)
            first = small[number * 4 + side, row, :]
            second = pltpu.roll(small[number * 4 + 2 + side, row, :], 64, 1)
            f.slots[which : which + 1, number * 128 : number * 128 + 128] = jnp.where(
                lane < 64, first, second
            )


def local_hot(values, shift):
    values = pltpu.roll(values, shift, 1)
    turned = [values] + [pltpu.roll(values, 32 * n, 1) for n in (1, 2, 3)]
    lane = iota((1, 128), 1)
    tiles = []
    for tile in range(4):
        row = turned[3][4 * tile + 3 : 4 * tile + 4]
        for n in (2, 1, 0):
            row = jnp.where(lane < 32 * n + 32, turned[n][4 * tile + n : 4 * tile + n + 1], row)
        tiles.append(row)
    row = jnp.concatenate(tiles, 1)
    return one_zero(row == iota((VP, HERE), 0)).astype(BF16)


def contact_part(contact_head, f, s, pair_count):
    _, block = position()
    base = block * WIDE
    head_sum = jnp.zeros((WIDE, COLS), F32)
    for h in range(HEADS):
        head_sum = head_sum + contact_head[h] * f.prob_low[h * 32 : h * 32 + 32, :].astype(F32)
    top, rest = split_two(head_sum)
    last = (head_sum - top.astype(F32) - rest.astype(F32)).astype(BF16)
    parts = jnp.concatenate([top, rest, last], 0)
    touch = jnp.zeros((WIDE, COLS), F32)
    bce = jnp.zeros((1, 1), F32)
    coef_sum = jnp.zeros((1, 1), F32)
    for number in range(SLOTS // 512):
        lanes = slice(number * 512, number * 512 + 512)
        first, second, label = (f.slots[n : n + 1, lanes] for n in range(3))
        second_hot = one_zero(second == iota((COLS, 512), 0)).astype(BF16)
        picked = nn(parts, second_hot)
        picked = picked[:32] + picked[32:64] + picked[64:]
        first_hot = one_zero((first - base) == iota((WIDE, 512), 0))
        logit = jnp.sum(picked * first_hot, 0, keepdims=True) * COLS + contact_head[HEADS]
        owned = jnp.sum(first_hot, 0, keepdims=True) > 0.5
        valid = (label >= 0) & owned
        positive = one_zero(label == 1)
        small = jnp.exp(-jnp.abs(logit))
        soft = jnp.maximum(logit, 0.0) + jnp.log(1.0 + small)
        bce = bce + total_of(jnp.where(valid, soft - positive * logit, 0.0))
        sigmoid = jnp.where(logit >= 0.0, 1.0, small) / (1.0 + small)
        coef = jnp.where(valid, sigmoid - positive, 0.0) / pair_count
        coef_sum = coef_sum + total_of(coef)
        coef_top, coef_rest = split_two(first_hot * coef)
        touch = touch + nt(coef_top, second_hot) + nt(coef_rest, second_hot)
    s.touch[...] = touch
    column = iota((1, 128), 1)
    row = jnp.where(column == HEADS, coef_sum, 0.0)
    for h in range(HEADS):
        part = total_of(touch * f.prob_low[h * 32 : h * 32 + 32, :].astype(F32)) * COLS
        row = row + jnp.where(column == h, part, 0.0)
    return row, bce


def feature_order():
    shape = (384, 384)
    spot = iota(shape, 0)
    block = (spot * 2731) >> 16
    swapped = (block & 28) | ((block & 1) << 1) | ((block >> 1) & 1)
    return one_zero(spot + (swapped - block) * 24 == iota(shape, 1)).astype(BF16)


def forward_body(small, contact_head, weights, s, f, ready, hook, emit):
    emb, in_row, out_row, in_col, out_col = weights[:5]
    up_parts, down_parts = weights[5:7], weights[7:9]
    ready(-1)
    hook()
    read_tokens(small, f)
    _, block = position()
    shift = lax.rem(128 - lax.rem(block, 4) * 32, 128)
    window = pl.ds(pl.multiple_of((block // 4) * 128, 128), 128)
    hot_ri = local_hot(f.ids[:, window], shift)
    goal_ri = local_hot(f.targets[...], shift)
    s.hot_ri[...] = hot_ri
    for r in range(ROWS):
        row = f.ids[r : r + 1, :]
        s.hot_all[r * VP : r * VP + VP, :] = one_zero(row == iota((VP, COLS), 0)).astype(BF16)
    shape = (HERE, HERE)
    back = (
        ((iota(shape, 1) >> 4) == (iota(shape, 0) & 31))
        & ((iota(shape, 1) & 15) == (iota(shape, 0) >> 5))
    )
    back = one_zero(back).astype(BF16)
    hot_ir = nn(hot_ri, back).astype(BF16)
    s.hot_ir[...] = hot_ir
    goal = nn(goal_ri, back)
    entries = jnp.zeros((4, 128), F32)
    labelled = jnp.zeros((1, 128), F32)
    for d in range(32):
        entries = entries + one_zero(small[d, 0:4, :] == MASK_ID)
        labelled = labelled + one_zero(small[d, 10:11, :] >= 0) + one_zero(small[d, 13:14, :] >= 0)
    entries, labelled = total_of(entries), total_of(labelled)

    hook()
    table = emb[0].astype(F32).T[:VP]
    norms = emb[1].astype(F32).T[:8]
    s.table[...] = table
    s.norms[...] = norms
    table_low = table.astype(BF16)

    def vector(number):
        return norms[number : number + 1, :]

    unit_t, _ = norm_stats(table)
    normed_t = (unit_t * vector(0) + vector(4)).astype(BF16)
    hook()
    for half in range(2):
        s.proj_t[:, half * 1152 : half * 1152 + 1152] = nn(normed_t, in_row[half]).astype(BF16)
    pair_parts = []
    for hp in range(PAIRS):
        lanes = slice(hp * 128, hp * 128 + 128)
        key = s.proj_t[:, D + hp * 128 : D + hp * 128 + 128]
        value = s.proj_t[:, 2 * D + hp * 128 : 2 * D + hp * 128 + 128]
        s.value_two[hp] = stacked(value)
        pair_parts.append(nt(s.proj_t[:, lanes], stacked(key)))
    pair_hi, pair_lo = split_two(jnp.concatenate(pair_parts, 1))
    hook()
    f.lookup[...] = tn(hot_ri, pair_hi) + tn(hot_ri, pair_lo)
    split_heads_to(f.lookup, f.left_hi, f.left_lo)
    hook()
    hot_all = s.hot_all[...]
    score = (nn(f.left_hi[...], hot_all) + nn(f.left_lo[...], hot_all)) * (HD * ROWS) ** (-0.5)
    score = jnp.exp(score - jnp.max(score, -1, keepdims=True))
    prob = score / jnp.sum(score, -1, keepdims=True)
    s.prob[...] = prob
    f.prob_low[...] = prob.astype(BF16)
    hook()
    merge_heads(f.prob_low[...], s.hot_all, s.weight_hi, f.weight_lo)
    hook()
    for hp in range(PAIRS):
        lanes = slice(hp * 128, hp * 128 + 128)
        value = s.value_two[hp]
        f.mixed[:, lanes] = (nn(s.weight_hi[:, lanes], value) + nn(f.weight_lo[:, lanes], value)).astype(BF16)
    ahead = (
        ((iota(shape, 0) >> 4) == (iota(shape, 1) & 31))
        & ((iota(shape, 0) & 15) == (iota(shape, 1) >> 5))
    )
    f.mixed[...] = nn(one_zero(ahead).astype(BF16), f.mixed[...]).astype(BF16)
    transpose_into(f.mixed, s.row_mixed_t)
    s.stream[...] = tn(hot_ir, table_low)
    hook()
    contact_row, bce = contact_part(contact_head, f, s, labelled)
    emit(AT.hot_all, AT.hot_ri, AT.hot_ir, AT.table, AT.norms, AT.proj_t, AT.value_two, AT.prob, AT.weight_hi, AT.row_mixed_t, AT.touch)

    hook()
    for half in range(2):
        lanes = slice(half * 384, half * 384 + 384)
        s.stream[:, lanes] += nn(f.mixed[...], out_row[half])
    norm_rows(s.stream, vector(1), vector(5), s.unit_1, s.rstd_1, f.normed)
    transpose_into(f.normed, s.col_normed_t)
    emit(AT.unit_1, AT.rstd_1, AT.col_normed_t)
    def project(half, at):
        s.col_proj[:, half * 1152 + at : half * 1152 + at + 384] = nn(
            f.normed[...], in_col[half, :, at : at + 384]
        ).astype(BF16)

    for third in range(3):
        hook()
        for half in range(2):
            project(half, third * 384)
    emit(AT.col_proj)

    def attend(at, carry):
        rows = pl.ds(pl.multiple_of((at // PAIRS) * 128, 128), 128)
        lane = lax.rem(at, PAIRS) * 128

        def lanes(part):
            return pl.ds(pl.multiple_of(part * D + lane, 128), 128)

        query = stacked(s.col_proj[rows, lanes(0)])
        score = nt(query, s.col_proj[rows, lanes(1)]) * HD ** (-0.5)
        score = jnp.where(column_mask(), score, -1e30)
        score = jnp.exp(score - jnp.max(score, -1, keepdims=True))
        prob = score / jnp.sum(score, -1, keepdims=True)
        s.col_prob[at] = prob
        mixed = nn(prob.astype(BF16), s.col_proj[rows, lanes(2)])
        f.mixed[rows, lanes(0)] = unstacked(mixed, 128).astype(BF16)
        return carry

    for part in range(4):
        hook()
        lax.fori_loop(part * PAIRS, part * PAIRS + PAIRS, attend, 0, unroll=3)
    hook()
    transpose_into(f.mixed, s.col_mixed_t)
    emit(AT.col_prob, AT.col_mixed_t)
    for half in range(2):
        lanes = slice(half * 384, half * 384 + 384)
        s.stream[:, lanes] += nn(f.mixed[...], out_col[half])
    norm_rows(s.stream, vector(2), vector(6), s.unit_2, s.rstd_2, f.normed)
    transpose_into(f.normed, s.feed_normed_t)
    emit(AT.unit_2, AT.rstd_2, AT.feed_normed_t)
    for part in range(2):

        def widen(half, at, part=part):
            lanes = slice(part * 1536 + half * 768 + at, part * 1536 + half * 768 + at + UP_TILE)
            up = nn(f.normed[...], up_parts[part][half, :, at : at + UP_TILE])
            active, slope = gelu_parts(up)
            s.active[:, lanes] = active.astype(BF16)
            s.slope[:, lanes] = slope.astype(BF16)

        for half in range(2):
            hook()
            for at in range(0, 768, UP_TILE):
                widen(half, at)

    emit(AT.active, AT.slope)
    for part, at, size in ((0, 0, 768), (1, 0, 384), (1, 384, 384)):
        hook()
        for half in range(2):
            start = part * 1536 + half * 768 + at
            s.stream[...] += nt(
                s.active[:, start : start + size], down_parts[part][half, :, at : at + size]
            )
    hook()
    norm_rows(s.stream, vector(3), vector(7), f.unit, f.rstd, f.normed)
    logits = nt(table_low, f.normed[...]) * D ** (-0.5)
    vocab = iota((VP, HERE), 0)
    logits = jnp.where(vocab < VOCAB, logits, -1e30)
    shifted = logits - jnp.max(logits, 0, keepdims=True)
    log_probs = shifted - jnp.log(jnp.sum(jnp.exp(shifted), 0, keepdims=True))
    keep = hot_ir[MASK_ID : MASK_ID + 1].astype(F32) > 0.5
    mlm = -total_of(jnp.where(keep & (goal > 0.5), log_probs, 0.0))
    logit_grad = jnp.where(keep, jnp.exp(log_probs) - goal, 0.0) / entries
    logit_low = (logit_grad * D ** (-0.5)).astype(BF16)
    s.grad_head[...] = nn(logit_low, f.normed[...])
    hook()
    f.lookup[...] = tn(logit_low, table_low)
    scale_3, shift_3 = back_rows(f.unit, f.rstd, vector(3), f.lookup, s.stream, s.branch, True)
    emit(AT.stream, AT.branch)
    line = iota((8, D), 0)
    s.moved[...] = jnp.where(line == 0, scale_3, jnp.where(line == 1, shift_3, 0.0))
    column = iota((1, 128), 1)
    row = contact_row + jnp.where(column == HEADS + 1, mlm, 0.0) + jnp.where(column == HEADS + 2, bce, 0.0)
    counted = jnp.where(column == 0, entries, 0.0) + jnp.where(column == 1, labelled, 0.0)
    line = iota((8, 128), 0)
    s.extras[...] = jnp.where(line == 0, row, jnp.where(line == 1, counted, 0.0))
    emit(AT.grad_head, AT.extras, AT.moved)
    hook()


def back_rows(unit_ref, rstd_ref, gain, upstream_ref, stream_ref, low_ref, first):
    def body(at, carry):
        scale, move = carry
        rows = pl.ds(pl.multiple_of(at * 64, 64), 64)
        upstream = upstream_ref[rows, :]
        unit = unit_ref[rows, :]
        inner = upstream * gain
        mean = jnp.sum(inner, -1, keepdims=True) * (1.0 / D)
        along = jnp.sum(inner * unit, -1, keepdims=True) * (1.0 / D)
        grad = rstd_ref[rows, 0:1] * (inner - mean - unit * along)
        if not first:
            grad = grad + stream_ref[rows, :]
        stream_ref[rows, :] = grad
        low_ref[rows, :] = grad.astype(BF16)
        touched = upstream * unit
        for n in range(8):
            scale = scale + touched[n * 8 : n * 8 + 8]
            move = move + upstream[n * 8 : n * 8 + 8]
        return scale, move

    zero = jnp.zeros((8, D), F32)
    scale, move = lax.fori_loop(0, HERE // 64, body, (zero, zero))
    return jnp.sum(scale, 0, keepdims=True), jnp.sum(move, 0, keepdims=True)


MATRICES = (128, 1152, 384, 1152, 384, 768, 768, 768, 768)
UNITS = (
    (0, 0, 128, True),
    (1, 0, 384, True),
    (1, 384, 384, True),
    (1, 768, 384, True),
    (2, 0, 384, False),
    (3, 0, 384, True),
    (3, 384, 384, True),
    (3, 768, 384, True),
    (4, 0, 384, False),
    (5, 0, 768, True),
    (6, 0, 768, True),
    (7, 0, 768, True),
    (8, 0, 384, True),
    (8, 384, 384, True),
)
FORWARD_ORDER = (
    (),
    ((0, 0), (0, 1), (0, 2), (0, 3), (0, 4), (0, 5), (0, 6), (0, 7), (0, 8), (1, 0), (0, 9), (0, 10), (0, 11), (0, 12), (2, 0), (1, 1), (0, 13), (3, 0), (1, 2), (2, 1), (4, 0),),
    ((1, 3), (2, 2), (1, 4), (3, 1), (2, 3), (1, 5), (4, 1), (3, 2), (1, 6), (2, 4), (4, 2), (1, 7), (3, 3), (2, 5), (1, 8), (4, 3),),
    (),
    ((2, 6),),
    ((3, 4), (1, 9),),
    ((4, 4), (2, 7),),
    ((3, 5),),
    ((2, 8), (1, 10), (4, 5),),
    ((3, 6), (2, 9), (1, 11), (4, 6), (1, 12), (3, 7), (3, 8), (1, 13), (4, 7),),
    (),
    ((4, 8), (2, 10),),
    (),
    (),
    (),
    ((3, 9),),
    ((2, 11),),
    ((4, 9),),
    ((2, 12),),
    ((2, 13), (3, 10), (3, 11), (4, 10),),
    (),
    ((3, 12), (3, 13), (4, 11),),
    ((4, 12),),
    ((4, 13),),
    (),
    (),
    (),
)


def spot(paired, cc, zz, yy, k):
    return (k, zz, yy, cc) if paired else (cc, zz, yy, k)


def forward_kernel(*refs):
    count, parts = len(UNITS), len(MATRICES)
    raw = refs[:11]
    contact_head = refs[11]
    at = 12
    far = refs[at : at + parts]
    saved_far = refs[at + parts : at + parts + len(SAVED)]
    at += parts + len(SAVED)
    outs = refs[at : at + parts]
    at += parts
    outgoing = refs[at : at + count]
    incoming = refs[at + count : at + 2 * count]
    piece = refs[at + 2 * count : at + 3 * count]
    at += 3 * count
    saved = Saved(*refs[at : at + len(SAVED)])
    at += len(SAVED)
    scratch = Forward(*refs[at : at + len(FORWARD)])
    at += len(FORWARD)
    near = refs[at : at + 11]
    at += 11
    small, small_out, sides, corner = refs[at : at + 4]
    small_send, small_recv, send, recv, local, out_sem, raw_sem = refs[at + 4 :]
    tokens, targets, masked, pairs, labels, table, norms, in_w, out_w, up_w, down_w = near
    z, y, k, c = place()
    me = (z * 4 + y * 2 + k) * 2 + c
    barrier = greet_all()
    raw_copies = [pltpu.make_async_copy(a, b, raw_sem.at[n]) for n, (a, b) in enumerate(zip(raw, near))]
    for item in raw_copies:
        item.start()
    for item in raw_copies[:7]:
        item.wait()
    small[...] = jnp.full(small.shape, -1, jnp.int32)
    for micro in range(2):
        for half in range(2):
            lanes = slice(half * 128, half * 128 + 128)
            row = 2 * micro + half
            small[row : row + 1, :] = jnp.where(
                masked[micro, :, lanes] > 0, MASK_ID, tokens[micro, :, lanes]
            )
            small[4 + row : 5 + row, :] = targets[micro, :, lanes]
        row = 8 + 3 * micro
        for which in range(2):
            small[row + which : row + which + 1, 0:64] = pairs[micro, which : which + 1, :]
        small[row + 2 : row + 3, 0:64] = labels[micro : micro + 1, :]
    sides[...] = jnp.zeros(sides.shape, F32)
    sides[0, :, 0:VOCAB] = table[...]
    corner[...] = jnp.zeros(corner.shape, F32)
    corner[0:8, 0:24] = norms[...]
    sides[1] = corner[...].T[:24]
    for item in raw_copies[7:]:
        item.wait()
    order = feature_order()

    def master(u, side):
        matrix, start, n, _ = UNITS[u]
        width = MATRICES[matrix]
        if matrix == 0:
            return sides[side]
        if matrix in (1, 3):
            return in_w[matrix // 2, :, side * 1152 + start : side * 1152 + start + n]
        if matrix in (2, 4):
            rows = out_w[matrix // 2 - 1, :, side * 384 : side * 384 + 384].astype(BF16)
            return nn(rows, order)
        begin = ((matrix - 5) % 2) * 1536 + side * width + start
        return (up_w if matrix < 7 else down_w)[:, begin : begin + n]

    def mine(u):
        return k if UNITS[u][3] else c

    for u in range(count):
        n = UNITS[u][2]
        other = jnp.where(mine(u) == 0, master(u, 1), master(u, 0))
        outgoing[u][...] = jnp.concatenate([other, jnp.zeros((8, n), F32)], 0).astype(BF16)
    pl.semaphore_wait(barrier, 31)

    def small_copy(step):
        other = lax.rem(me + step, 32)
        return remote(
            small, small_out.at[me], small_send.at[step], small_recv.at[step], (other // 2, lax.rem(other, 2))
        )

    def spread(step, carry):
        small_copy(step).start()
        return carry

    across, beside, twin = device(z, y, k, 1 - c), device(z, 1 - y, k, c), device(z, y, 1 - k, c)

    def block(u, cc, zz, yy):
        matrix, start, n, paired = UNITS[u]
        where = spot(paired, cc, zz, yy, k)
        if n == MATRICES[matrix]:
            return outs[matrix].at[where]
        return outs[matrix].at[(*where, slice(None), pl.ds(start, n))]

    def copy(u, at, src, dst, target):
        return remote(src, dst, send.at[u, at], recv.at[u, at], target)

    def pair_copy(u):
        return copy(u, 0, outgoing[u], incoming[u], twin if UNITS[u][3] else across)

    def own_copy(u):
        return pltpu.make_async_copy(piece[u], block(u, c, z, y), local.at[u])

    def line_copy(u, step):
        return copy(u, step, piece[u], block(u, c, z, y), device(lax.rem(z + step, 4), y, k, c))

    def same(u, at, cc, zz, yy, target):
        view = block(u, cc, zz, yy)
        return copy(u, at, view, view, target)

    low, high, every = pl.ds(0, 2), pl.ds(2, 2), slice(None)

    def second(u):
        return [same(u, 4, c, low, y, across), same(u, 5, c, high, y, beside)]

    def third_own(u):
        return [same(u, 6, c, low, y, beside), same(u, 7, c, high, y, across)]

    def third_far(u):
        return [same(u, 8, 1 - c, low, y, beside), same(u, 9, c, high, 1 - y, across)]

    def twin_own(u):
        return [same(u, 10, c, every, y, twin)]

    def twin_second(u):
        return [same(u, 11, 1 - c, low, y, twin), same(u, 12, c, high, 1 - y, twin)]

    def twin_third(u):
        return [
            same(u, 13, c, low, 1 - y, twin),
            same(u, 14, 1 - c, high, y, twin),
            same(u, 15, 1 - c, low, 1 - y, twin),
            same(u, 16, 1 - c, high, 1 - y, twin),
        ]

    for u in range(count):
        pair_copy(u).start()
    lax.fori_loop(1, 32, spread, 0)
    small_out[me] = small[...]

    def stage_line(u):
        pair_copy(u).wait_recv()
        side = mine(u)
        own = jnp.where(side == 0, master(u, 0), master(u, 1))
        theirs = incoming[u][...].astype(F32)[:24]
        top = jnp.where(side == 0, own, theirs)
        bottom = jnp.where(side == 0, theirs, own)
        piece[u][...] = jnp.concatenate([top, bottom], 0).astype(BF16)
        own_copy(u).start()
        for step in (1, 3, 2):
            line_copy(u, step).start()

    def stage_second(u):
        own_copy(u).wait()
        for step in (1, 3, 2):
            line_copy(u, step).wait_recv()
        for item in second(u) + third_own(u) + twin_own(u):
            item.start()

    def stage_third(u):
        for item in second(u):
            item.wait_recv()
        for item in third_far(u) + twin_second(u):
            item.start()

    def stage_twin(u):
        for item in third_own(u) + third_far(u):
            item.wait_recv()
        for item in twin_third(u):
            item.start()

    def far_copy(matrix):
        return pltpu.make_async_copy(outs[matrix], far[matrix], local.at[count + matrix])

    def stage_end(u):
        for item in twin_own(u) + twin_second(u) + twin_third(u):
            item.wait_recv()
        if u + 1 == count or UNITS[u + 1][0] != UNITS[u][0]:
            far_copy(UNITS[u][0]).start()

    stages = (stage_line, stage_second, stage_third, stage_twin, stage_end)
    pending = list(FORWARD_ORDER)

    def hook():
        for stage, u in pending.pop(0):
            stages[stage](u)

    def ready(number):
        lax.fori_loop(1, 32, finish, 0)

    def out_copy(at):
        return pltpu.make_async_copy(saved[at], saved_far[at], out_sem.at[at])

    def emit(*numbers):
        for number in numbers:
            out_copy(number).start()

    def finish(step, carry):
        small_copy(step).wait()
        return carry

    views = [w.reshape(2, D, n) for w, n in zip(outs, MATRICES)]
    forward_body(small_out, contact_head, views, saved, scratch, ready, hook, emit)
    assert not pending
    for u in range(count):
        pair_copy(u).wait_send()
        for step in (1, 2, 3):
            line_copy(u, step).wait_send()
        sent = second(u) + third_own(u) + third_far(u) + twin_own(u) + twin_second(u) + twin_third(u)
        for item in sent:
            item.wait_send()
    for matrix in range(parts):
        far_copy(matrix).wait()
    for at in range(len(SAVED)):
        out_copy(at).wait()


def forward_call(raw, contact_head):
    count, parts = len(UNITS), len(MATRICES)
    anywhere = pl.BlockSpec(memory_space=pl.ANY)
    shapes = [(2, NZ, NY, 2, 48, n) for n in MATRICES]
    widths = [n for _, _, n, _ in UNITS]
    outs = pl.pallas_call(
        forward_kernel,
        out_shape=[jax.ShapeDtypeStruct(shape, BF16) for shape in shapes]
        + [jax.ShapeDtypeStruct(*item) for item in SAVED],
        in_specs=[anywhere] * 11 + [pl.BlockSpec(memory_space=pltpu.SMEM)],
        out_specs=[anywhere] * (parts + len(SAVED)),
        scratch_shapes=[pltpu.VMEM(shape, BF16) for shape in shapes]
        + [pltpu.VMEM((32, n), BF16) for n in widths] * 2
        + [pltpu.VMEM((48, n), BF16) for n in widths]
        + [pltpu.VMEM(*item) for item in SAVED]
        + [pltpu.VMEM(*item) for item in FORWARD]
        + [pltpu.VMEM(item.shape, item.dtype) for item in raw]
        + [
            pltpu.VMEM((16, 128), jnp.int32),
            pltpu.VMEM((32, 16, 128), jnp.int32),
            pltpu.VMEM((2, 24, 128), F32),
            pltpu.VMEM((128, 128), F32),
            pltpu.SemaphoreType.DMA((32,)),
            pltpu.SemaphoreType.DMA((32,)),
            pltpu.SemaphoreType.DMA((count, 17)),
            pltpu.SemaphoreType.DMA((count, 17)),
            pltpu.SemaphoreType.DMA((count + parts,)),
            pltpu.SemaphoreType.DMA((len(SAVED),)),
            pltpu.SemaphoreType.DMA((len(raw),)),
        ],
        compiler_params=pltpu.CompilerParams(
            collective_id=0, has_side_effects=True, vmem_limit_bytes=62 * 2**20
        ),
    )(*raw, contact_head)
    return outs[:parts], Saved(*outs[parts:])


def summed_rows(sums, start, groups, rows):
    parts = [
        jnp.concatenate([sums[2 * (start + g)], sums[2 * (start + g) + 1]], 1) for g in range(groups)
    ]
    if rows > 8 * groups:
        parts.append(jnp.zeros((rows - 8 * groups, D), F32))
    return jnp.concatenate(parts, 0) if len(parts) > 1 else parts[0]


def table_finish(sums, table_ref, norms_ref, proj_t, in_row, g_in, g_emb, g_norm):
    z, y, k, c = place()
    me = ((z * 2 + y) * 2 + c) * 2 + k
    pair = summed_rows(sums, 0, 5, VP)
    value_grad = summed_rows(sums, 5, 5, VP)
    table_grad = summed_rows(sums, 10, 5, VP)
    vectors = summed_rows(sums, 15, 1, 8)
    pair_hi, pair_lo = split_two(pair)
    scale = (HD * ROWS) ** (-0.5)
    query_grad, key_grad = [], []
    for hp in range(PAIRS):
        lanes = slice(hp * 128, hp * 128 + 128)
        query = proj_t[:, lanes]
        key = stacked(proj_t[:, D + hp * 128 : D + hp * 128 + 128])
        high, low = pair_hi[:, lanes], pair_lo[:, lanes]
        query_grad.append((nn(high, key) + nn(low, key)) * scale)
        key_grad.append(unstacked(tn(high, query) + tn(low, query), VP) * scale)
    proj_hi, proj_lo = split_two(jnp.concatenate(query_grad + key_grad + [value_grad], 1))
    normed_grad = jnp.zeros((VP, D), F32)
    for half in range(2):
        lanes = slice(half * 1152, half * 1152 + 1152)
        matrix = in_row[half]
        normed_grad = normed_grad + nt(proj_hi[:, lanes], matrix) + nt(proj_lo[:, lanes], matrix)
    unit, rstd = norm_stats(table_ref[...])
    gain = norms_ref[0:1, :]
    back, scale_0, shift_0 = norm_back(unit, rstd, gain, normed_grad)
    table_grad = table_grad + back
    line = iota((16, D), 0)
    norm_grad = jnp.zeros((16, D), F32)
    rows = [scale_0[None]] + [vectors[n : n + 1] for n in range(3)]
    rows += [shift_0[None]] + [vectors[n : n + 1] for n in range(3, 6)]
    for number, row in enumerate(rows):
        norm_grad = jnp.where(line == number, row, norm_grad)
    shard = D // 32
    pick = one_zero(iota((shard, D), 1) == iota((shard, D), 0) + me * shard).astype(BF16)
    normed = (unit * gain + norms_ref[4:5, :]).astype(BF16)
    mine = nt(pick, normed).astype(BF16)
    in_grad = nn(mine, proj_hi) + nn(mine, proj_lo)
    g_in[...] = in_grad

    def three(values):
        top, rest = split_two(values)
        return top, rest, (values - top.astype(F32) - rest.astype(F32)).astype(BF16)

    emb_grad = sum(nt(pick, part) for part in three(table_grad))
    g_emb[...] = emb_grad
    own_norm = sum(nt(part, pick) for part in three(norm_grad))[:8]
    g_norm[...] = own_norm
    return total_of(in_grad * in_grad) + total_of(emb_grad * emb_grad) + total_of(own_norm * own_norm)


GRAD_WIDTHS = (768, 768, 768, 768, 384, 1152, 384)
GRAD_UNITS = (
    (0, 0, 384, True),
    (0, 384, 384, True),
    (1, 0, 768, True),
    (2, 0, 768, True),
    (3, 0, 768, True),
    (4, 0, 384, False),
    (5, 0, 384, True),
    (5, 384, 384, True),
    (5, 768, 384, True),
    (6, 0, 384, False),
)
BACKWARD_ORDER = (
    (),
    (),
    (),
    (),
    (),
    (),
    ((0, 0),),
    ((0, 1),),
    (),
    (),
    (),
    ((1, 0),),
    (),
    ((0, 2), (1, 1),),
    ((2, 0),),
    ((0, 3),),
    (),
    (),
    ((3, 0),),
    ((1, 2), (0, 4), (4, 0), (2, 1),),
    ((0, 5),),
    (),
    ((3, 1), (1, 3),),
    ((4, 1),),
    ((2, 2),),
    (),
    (),
    ((1, 4),),
    (),
    (),
    ((1, 5),),
    ((3, 2), (2, 3), (0, 6), (0, 7), (0, 8), (4, 2),),
    ((2, 4),),
    ((2, 5),),
    (),
    ((1, 6), (3, 3), (0, 9),),
    ((4, 3), (1, 7),),
    ((1, 8), (3, 4), (2, 6),),
    ((4, 4), (3, 5), (1, 9),),
    ((2, 7), (3, 6), (2, 8), (4, 6), (5, 0), (4, 5), (2, 9), (3, 7), (4, 7), (3, 8), (4, 8), (6, 0), (3, 9), (4, 9),),
)


class Kept(typing.NamedTuple):
    stream: typing.Any
    norms: typing.Any
    table: typing.Any
    proj_t: typing.Any
    extras: typing.Any
    moved: typing.Any
    grad_head: typing.Any
    touch: typing.Any
    value_two: typing.Any


class Early(typing.NamedTuple):
    slope: typing.Any
    active: typing.Any
    feed_normed_t: typing.Any
    unit_2: typing.Any
    rstd_2: typing.Any
    col_mixed_t: typing.Any
    col_proj: typing.Any
    col_prob: typing.Any
    col_normed_t: typing.Any
    unit_1: typing.Any
    rstd_1: typing.Any


class Late(typing.NamedTuple):
    row_mixed_t: typing.Any
    hot_all: typing.Any
    weight_hi: typing.Any
    prob: typing.Any
    hot_ri: typing.Any
    hot_ir: typing.Any


def pick_items(group, source):
    return [getattr(source, name) for name in group._fields]


def backward_kernel(*refs):
    widths = GRAD_WIDTHS
    count = len(widths)
    contact_head = refs[0]
    far = refs[1 : 1 + count]
    in_row_far = refs[1 + count]
    saved = Saved(*refs[2 + count : 2 + count + len(SAVED)])
    at = 2 + count + len(SAVED)
    outs = refs[at : at + count]
    g_in, g_emb, g_norm, stats = refs[at + count : at + count + 4]
    at += count + 4
    grads = refs[at : at + count]
    kept = Kept(*refs[at + count : at + count + len(Kept._fields)])
    at += count + len(Kept._fields)
    upstream, branch, branch_t, mixed = refs[at : at + 4]
    scratch = refs[at + 4 :]
    units = len(GRAD_UNITS)
    got_0, got_1a, got_1b, got_2a, got_2b, got_3, total, got_4 = (
        scratch[i * units : (i + 1) * units] for i in range(8)
    )
    table, table_out, table_got, square, square_got = scratch[8 * units : 8 * units + 5]
    table_send, table_recv, send, recv, local = scratch[8 * units + 5 :]
    z, y, k, c = place()
    me = (z * 4 + y * 2 + k) * 2 + c
    across, beside, twin = device(z, y, k, 1 - c), device(z, 1 - y, k, c), device(z, y, 1 - k, c)
    barrier = greet_all()
    stream = kept.stream

    copies = {}

    def load(number, source, target):
        copies[number] = pltpu.make_async_copy(source, target, local.at[number])
        copies[number].start()

    def need(*numbers):
        for number in numbers:
            copies[number].wait()

    def weight(m):
        return len(SAVED) + m

    def copy(m, at, src, dst, target):
        return remote(src, dst, send.at[m, at], recv.at[m, at], target)

    low, high = pl.ds(0, 2), pl.ds(2, 2)
    every = slice(None)

    def where(u, cc, zz, yy):
        matrix, start, n, paired = GRAD_UNITS[u]
        index = spot(paired, cc, zz, yy, k)
        return index if n == widths[matrix] else (*index, every, pl.ds(start, n))

    def block(u, cc, zz, yy):
        return grads[GRAD_UNITS[u][0]].at[where(u, cc, zz, yy)]

    def ordered(u, cc, rest):
        return (*rest, cc) if GRAD_UNITS[u][3] else (cc, *rest)

    def twin_copy(u):
        matrix, start, n, paired = GRAD_UNITS[u]
        index = (1 - k,) if paired else (every, every, every, 1 - k)
        if n != widths[matrix]:
            index = (*index, *(every,) * (5 - len(index)), pl.ds(start, n))
        return copy(u, 0, grads[matrix].at[index], got_0[u], twin)

    def first(u):
        return [
            copy(u, 1, block(u, every, low, 1 - y), got_1a[u], beside),
            copy(u, 2, block(u, 1 - c, high, every), got_1b[u], across),
        ]

    def second(u):
        return [
            copy(u, 3, block(u, 1 - c, low, y), got_2a[u], across),
            copy(u, 4, block(u, c, high, 1 - y), got_2b[u], beside),
        ]

    def along(u):
        return [
            copy(
                u,
                4 + step,
                block(u, c, lax.rem(z + step, 4), y),
                got_3[u].at[step - 1],
                device(lax.rem(z + step, 4), y, k, c),
            )
            for step in (1, 3, 2)
        ]

    def mine(u):
        return k if GRAD_UNITS[u][3] else c

    def pair(u):
        return [copy(u, 8, total[u].at[1 - mine(u)], got_4[u], twin if GRAD_UNITS[u][3] else across)]

    def table_copy(step, back):
        other = lax.rem(me + step, 32)
        target = (other // 2, lax.rem(other, 2))
        if back:
            return remote(
                table_out.at[me], table_out.at[me], table_send.at[1, step], table_recv.at[1, step], target
            )
        return remote(
            table.at[other], table_got.at[me], table_send.at[0, step], table_recv.at[0, step], target
        )

    def each(action):
        def body(step, carry):
            action(step)
            return carry

        lax.fori_loop(1, 32, body, 0)

    def gather_into(u, cc, zz, yy, *others):
        matrix = GRAD_UNITS[u][0]
        index = where(u, cc, zz, yy)
        value = grads[matrix][index].astype(F32) + got_0[u][ordered(u, cc, (zz, yy))].astype(F32)
        for other in others:
            value = value + other.astype(F32)
        grads[matrix][index] = value.astype(BF16)

    def stage_first(u):
        twin_copy(u).wait_recv()
        for a in range(2):
            for b in range(2):
                gather_into(u, a, b, 1 - y)
                gather_into(u, 1 - c, 2 + a, b)
        for item in first(u):
            item.start()

    def from_beside(u, cc, a):
        return got_1a[u][ordered(u, cc, (a,))]

    def stage_second(u):
        for item in first(u):
            item.wait_recv()
        for a in range(2):
            gather_into(u, 1 - c, a, y, from_beside(u, 1 - c, a))
            gather_into(u, c, 2 + a, 1 - y, got_1b[u][a, 1 - y])
        for item in second(u):
            item.start()

    def stage_along(u):
        for item in second(u):
            item.wait_recv()
        for a in range(2):
            gather_into(u, c, a, y, from_beside(u, c, a), got_2a[u][a])
            gather_into(u, c, 2 + a, y, got_1b[u][a, y], got_2b[u][a])
        for item in along(u):
            item.start()

    def stage_pair(u):
        for item in along(u):
            item.wait_recv()
        full = grads[GRAD_UNITS[u][0]][where(u, c, z, y)].astype(F32)
        for step in range(3):
            full = full + got_3[u][step].astype(F32)
        total[u][0] = full[:24]
        total[u][1] = full[24:]
        for item in pair(u):
            item.start()

    def stage_end(u):
        matrix, start, n, _ = GRAD_UNITS[u]
        lanes = slice(start, start + n)
        side = mine(u)
        outs[matrix][side, :, lanes] = total[u][side]
        for item in pair(u):
            item.wait_recv()
        outs[matrix][1 - side, :, lanes] = got_4[u][...]

    def table_sum(u):
        table_got[me] = table[me]
        each(lambda step: table_copy(step, False).wait_recv())
        table_out[me] = lax.fori_loop(1, 32, lambda at, held: held + table_got[at], table_got[0])
        each(lambda step: table_copy(step, True).start())

    late_parts = []

    def table_end(u):
        each(lambda step: table_copy(step, True).wait_recv())
        need(weight(count))
        found = table_finish(
            table_out, kept.table, kept.norms, kept.proj_t, late_parts[0].reshape(2, D, 1152), g_in, g_emb, g_norm
        )
        square[...] = jnp.broadcast_to(found, (8, 128))

    stages = (stage_first, stage_second, stage_along, stage_pair, stage_end, table_sum, table_end)
    pending = list(BACKWARD_ORDER)

    def hook():
        for stage, u in pending.pop(0):
            stages[stage](u)

    def done(u):
        if u == 0:
            pl.semaphore_wait(barrier, 31)
        twin_copy(u).start()
        hook()

    names = Kept._fields
    for name in names:
        load(getattr(AT, name), getattr(saved, name), getattr(kept, name))

    load(AT.branch, saved.branch, branch)

    def phase_one(*early_refs):
        e = Early(*early_refs)
        load(weight(0), far[0], grads[0])
        load(AT.slope, saved.slope, e.slope)
        load(AT.active, saved.active, e.active)
        for m in (1, 2, 3):
            load(weight(m), far[m], grads[m])
        for name in Early._fields[2:6]:
            load(getattr(AT, name), getattr(saved, name), getattr(e, name))
        load(weight(4), far[4], grads[4])
        for name in Early._fields[6:8]:
            load(getattr(AT, name), getattr(saved, name), getattr(e, name))
        load(weight(5), far[5], grads[5])
        for name in Early._fields[8:]:
            load(getattr(AT, name), getattr(saved, name), getattr(e, name))
        load(weight(6), far[6], grads[6])
        view = [g.reshape(2, D, n) for g, n in zip(grads, widths)]
        need(*(getattr(AT, name) for name in names))
        norms = kept.norms[...]

        def gain(number):
            return norms[number : number + 1, :]

        need(AT.branch)
        transpose_into(branch, branch_t)
        hook()

        def grad_tile(m, start, left_t, right, half, at):
            lanes = slice(start + half * widths[m] + at, start + half * widths[m] + at + 384)
            view[m][half, :, at : at + 384] = nn(left_t[...], right[:, lanes]).astype(BF16)

        def grad_half(m, start, left_t, right, half):
            for at in range(0, widths[m], 384):
                grad_tile(m, start, left_t, right, half, at)

        for part in range(2):
            need(weight(part))
            if part == 0:
                need(AT.slope)

            def down_back(half, at, part=part):
                lanes = slice(part * 1536 + half * 768 + at, part * 1536 + half * 768 + at + 384)
                back = nn(branch[...], view[part][half, :, at : at + 384])
                e.slope[:, lanes] = (back * e.slope[:, lanes].astype(F32)).astype(BF16)

            if part == 0:
                for at in (0, 384):
                    for half in range(2):
                        down_back(half, at)
                    hook()
                    if at == 0:
                        need(AT.active)
                    for half in range(2):
                        grad_tile(part, 0, branch_t, e.active, half, at)
                    done(at // 384)
            else:
                for half in range(2):
                    for at in (0, 384):
                        down_back(half, at)
                    hook()
                grad_half(part, part * 1536, branch_t, e.active, 0)
                hook()
                grad_half(part, part * 1536, branch_t, e.active, 1)
                done(2)
        for part in range(2):
            need(weight(2 + part))
            for half in range(2):
                start = part * 1536 + half * 768
                back = nt(e.slope[:, start : start + 768], view[2 + part][half])
                upstream[...] = back if start == 0 else upstream[...] + back
                hook()
            if part == 0:
                need(AT.feed_normed_t)
            grad_half(2 + part, part * 1536, e.feed_normed_t, e.slope, 0)
            hook()
            grad_half(2 + part, part * 1536, e.feed_normed_t, e.slope, 1)
            done(3 + part)
        need(AT.unit_2, AT.rstd_2)
        scale_2, shift_2 = back_rows(e.unit_2, e.rstd_2, gain(2), upstream, stream, branch, False)
        hook()
        need(weight(4), AT.col_mixed_t)
        mixed[...] = (nt(branch[:, :384], view[4][0]) + nt(branch[:, 384:], view[4][1])).astype(BF16)
        hook()
        for half in range(2):
            grad_half(4, 0, e.col_mixed_t, branch, half)
        done(5)
        need(AT.col_proj, AT.col_prob)
        proj = e.active

        def attend(at, carry):
            rows = pl.ds(pl.multiple_of((at // PAIRS) * 128, 128), 128)
            lane = lax.rem(at, PAIRS) * 128

            def lanes(part):
                return pl.ds(pl.multiple_of(part * D + lane, 128), 128)

            query = stacked(e.col_proj[rows, lanes(0)])
            key = e.col_proj[rows, lanes(1)]
            value = e.col_proj[rows, lanes(2)]
            above = stacked(mixed[rows, lanes(0)])
            prob = e.col_prob[at]
            grad = nt(above, value)
            grad = prob * (grad - jnp.sum(prob * grad, -1, keepdims=True))
            small = grad.astype(BF16)
            scale = HD ** (-0.5)
            proj[rows, lanes(0)] = (unstacked(nn(small, key), 128) * scale).astype(BF16)
            proj[rows, lanes(1)] = (tn(small, query) * scale).astype(BF16)
            proj[rows, lanes(2)] = tn(prob.astype(BF16), above).astype(BF16)
            return carry

        for part in range(6):
            lax.fori_loop(4 * part, 4 * part + 4, attend, 0, unroll=4)
            hook()
        need(weight(5))
        for half in range(2):
            back = nt(proj[:, half * 1152 : half * 1152 + 1152], view[5][half])
            upstream[...] = back if half == 0 else upstream[...] + back
            hook()
        need(AT.col_normed_t)
        for third in range(3):
            for half in range(2):
                grad_tile(5, 0, e.col_normed_t, proj, half, third * 384)
            done(6 + third)
        need(AT.unit_1, AT.rstd_1)
        scale_1, shift_1 = back_rows(e.unit_1, e.rstd_1, gain(1), upstream, stream, branch, False)
        hook()
        need(weight(6))
        mixed[...] = (nt(branch[:, :384], view[6][0]) + nt(branch[:, 384:], view[6][1])).astype(BF16)
        line = iota((8, D), 0)
        vectors = jnp.zeros((8, D), F32)
        moved = kept.moved[...]
        rows = (scale_1, scale_2, moved[0:1], shift_1, shift_2, moved[1:2])
        for number, row in enumerate(rows):
            vectors = jnp.where(line == number, row, vectors)
        extras = jnp.concatenate([kept.extras[0:1, :], jnp.zeros((1, D - 128), F32)], 1)
        kept.moved[...] = jnp.where(line == 6, extras, vectors)
        hook()

    pl.run_scoped(phase_one, *(pltpu.VMEM(*item) for item in pick_items(Early, SAVED)))

    def phase_two(*late_refs):
        e = Late(*late_refs[:-3])
        in_row, left_hi, left_lo = late_refs[-3:]
        for name in Late._fields:
            load(getattr(AT, name), getattr(saved, name), getattr(e, name))
        load(weight(count), in_row_far, in_row)
        view = grads[6].reshape(2, D, widths[6])
        late_parts.append(in_row)
        need(AT.row_mixed_t)
        for half in range(2):
            lanes = slice(half * 384, half * 384 + 384)
            view[half] = nn(e.row_mixed_t[...], branch[:, lanes]).astype(BF16)
        done(9)
        need(AT.hot_all, AT.weight_hi, AT.prob, AT.hot_ri, AT.hot_ir)
        shape = (HERE, HERE)
        back = (
            ((iota(shape, 1) >> 4) == (iota(shape, 0) & 31))
            & ((iota(shape, 1) & 15) == (iota(shape, 0) >> 5))
        )
        mixed[...] = nn(one_zero(back).astype(BF16), mixed[...]).astype(BF16)
        value_rows = []
        for hp in range(PAIRS):
            lanes = slice(hp * 128, hp * 128 + 128)
            part = mixed[:, lanes]
            upstream[:, lanes] = nt(part, kept.value_two[hp])
            value_rows.append(unstacked(tn(e.weight_hi[:, lanes], part), 64))
        hook()
        split_heads_to(upstream, left_hi, left_lo)
        hook()
        hot_all = e.hot_all[...]
        grad = nn(left_hi[...], hot_all) + nn(left_lo[...], hot_all)
        extra = jnp.concatenate(
            [kept.touch[...] * (contact_head[h] * COLS) for h in range(HEADS)], 0
        )
        grad = grad + extra
        prob = e.prob[...]
        grad = prob * (grad - jnp.sum(prob * grad, -1, keepdims=True))
        low_grad = grad.astype(BF16)
        hook()
        merge_heads(low_grad, e.hot_all, branch, None)
        hook()
        table_pair = nn(e.hot_ri[...], branch[...])
        stream_hi, stream_lo = split_two(stream[...])
        hot_ir = e.hot_ir[...]
        table_grad = kept.grad_head[...] + nn(hot_ir, stream_hi) + nn(hot_ir, stream_lo)
        value_grad = jnp.concatenate(value_rows, 1)
        blocks = ((0, table_pair), (5, value_grad), (10, table_grad), (15, kept.moved[...]))
        for start, block in blocks:
            for group in range(min(5, block.shape[0] // 8)):
                for half in range(2):
                    table[2 * (start + group) + half] = block[
                        group * 8 : group * 8 + 8, half * 384 : half * 384 + 384
                    ]
        each(lambda step: table_copy(step, False).start())
        hook()
        hook()

    pl.run_scoped(
        phase_two,
        *(pltpu.VMEM(*item) for item in pick_items(Late, SAVED)),
        pltpu.VMEM((2, NZ, NY, 2, 48, 1152), BF16),
        pltpu.VMEM((HEADS * WIDE, ROWS * VP), BF16),
        pltpu.VMEM((HEADS * WIDE, ROWS * VP), BF16),
    )
    assert not pending
    local_square = jnp.zeros((1, 1), F32)
    for m in range(count):
        for half in range(2):
            local_square = local_square + total_of(outs[m][half] * outs[m][half])

    def square_copy(step):
        other = lax.rem(me + step, 32)
        return remote(
            square, square_got.at[me], table_send.at[2, step], table_recv.at[2, step], (other // 2, lax.rem(other, 2))
        )

    square[...] = square[...] + local_square
    each(lambda step: square_copy(step).start())
    square_got[me] = square[...]
    each(lambda step: square_copy(step).wait())
    total_square = lax.fori_loop(1, 32, lambda at, held: held + square_got[at], square_got[0])[0:1]
    vector = table_out[30, 6:7, :128]
    counted = kept.extras[1:2, :]
    column = iota((1, 128), 1)
    contact = jnp.where(column <= HEADS, vector, 0.0)
    total_square = total_square + total_of(contact * contact)
    grad_norm = jnp.sqrt(total_square)
    factor = jnp.minimum(1.0, MAX_NORM / grad_norm)
    losses = (
        (0, vector[:, HEADS + 1 : HEADS + 2]),
        (1, counted[:, 0:1]),
        (2, vector[:, HEADS + 2 : HEADS + 3]),
        (3, counted[:, 1:2]),
    )
    loss_row = jnp.zeros((1, 128), F32)
    for at, value in losses:
        loss_row = jnp.where(column == at, value, loss_row)
    number = iota((8, 128), 0)
    result = jnp.zeros((8, 128), F32)
    for at, row in enumerate((contact, counted, factor, grad_norm, loss_row)):
        result = jnp.where(number == at, row, result)
    stats[...] = result
    each(lambda step: table_copy(step, True).wait_send())
    each(lambda step: table_copy(step, False).wait_send())
    for u in range(units):
        for item in [twin_copy(u)] + first(u) + second(u) + along(u) + pair(u):
            item.wait_send()


def backward_call(contact_head, weights, in_row, saved):
    widths = GRAD_WIDTHS
    count = len(widths)
    inside = pl.BlockSpec(memory_space=pltpu.VMEM)
    anywhere = pl.BlockSpec(memory_space=pl.ANY)

    units = len(GRAD_UNITS)

    def shapes(lead, dtype):
        return [pltpu.VMEM((*lead, n), dtype) for _, _, n, _ in GRAD_UNITS]

    outs = pl.pallas_call(
        backward_kernel,
        out_shape=[jax.ShapeDtypeStruct((2, 24, n), F32) for n in widths]
        + [
            jax.ShapeDtypeStruct((24, 3 * D), F32),
            jax.ShapeDtypeStruct((24, VP), F32),
            jax.ShapeDtypeStruct((8, 24), F32),
            jax.ShapeDtypeStruct((8, 128), F32),
        ],
        in_specs=[pl.BlockSpec(memory_space=pltpu.SMEM)] + [anywhere] * (1 + count + len(SAVED)),
        out_specs=[inside] * (4 + count),
        scratch_shapes=[pltpu.VMEM((2, NZ, NY, 2, 48, n), BF16) for n in widths]
        + [pltpu.VMEM(*item) for item in pick_items(Kept, SAVED)]
        + [
            pltpu.VMEM((HERE, D), F32),
            pltpu.VMEM((HERE, D), BF16),
            pltpu.VMEM((D, HERE), BF16),
            pltpu.VMEM((HERE, D), BF16),
        ]
        + [
            pltpu.VMEM((NZ, NY, 2, 48, n) if paired else (2, NZ, NY, 48, n), BF16)
            for _, _, n, paired in GRAD_UNITS
        ]
        + shapes((2, 2, 48), BF16)
        + shapes((2, 2, 48), BF16)
        + shapes((2, 48), BF16)
        + shapes((2, 48), BF16)
        + shapes((3, 48), BF16)
        + shapes((2, 24), F32)
        + shapes((24,), F32)
        + [
            pltpu.VMEM((32, 8, 384), F32),
            pltpu.VMEM((32, 8, 384), F32),
            pltpu.VMEM((32, 8, 384), F32),
            pltpu.VMEM((8, 128), F32),
            pltpu.VMEM((32, 8, 128), F32),
            pltpu.SemaphoreType.DMA((3, 32)),
            pltpu.SemaphoreType.DMA((3, 32)),
            pltpu.SemaphoreType.DMA((units, 9)),
            pltpu.SemaphoreType.DMA((units, 9)),
            pltpu.SemaphoreType.DMA((len(SAVED) + count + 1,)),
        ],
        compiler_params=pltpu.CompilerParams(
            collective_id=1, has_side_effects=True, vmem_limit_bytes=63 * 2**20
        ),
    )(contact_head, *weights, in_row, *saved)
    return outs[:count], outs[count:]


UPDATE_RATES = (LEARN_RATE,) * 4 + (VECTOR_RATE,) * 3


def update_kernel(*refs):
    given, far, held, results = refs[:32], refs[32:60], refs[60:92], refs[92:120]
    sems, out_sems = refs[120:122]
    outs, copies = results[:21], results[21:26]
    loss_ref, norm_ref = results[26:]

    def leave(*numbers):
        for n in numbers:
            pltpu.make_async_copy(results[n], far[n], out_sems.at[n]).start()

    moves = [pltpu.make_async_copy(a, b, sems.at[n]) for n, (a, b) in enumerate(zip(given, held))]
    for item in moves:
        item.start()
    reduced, g_in, g_emb, g_norm, stats = held[:7], held[7], held[8], held[9], held[10]
    states = [held[11 + 3 * n : 14 + 3 * n] for n in range(7)]
    outs = [outs[3 * n : 3 * n + 3] for n in range(7)]
    order = feature_order()
    for item in moves[4:11]:
        item.wait()
    factor = stats[2:3, 0:1]
    loss_ref[...] = stats[4:5, 0:4]
    norm_ref[...] = stats[3:4, 0:1]

    def natural(values):
        top, rest = split_two(values)
        last = (values - top.astype(F32) - rest.astype(F32)).astype(BF16)
        return nt(top, order) + nt(rest, order) + nt(last, order)

    def update(number, where, grad):
        master, first, second = (ref[where] for ref in states[number])
        new, first, second = adam_update(master, first, second, grad * factor, UPDATE_RATES[number])
        for ref, value in zip(outs[number], (new, first, second)):
            ref[where] = value
        if number < 5:
            copies[number][where] = new.astype(BF16)

    every = slice(None)
    g_out_col, g_in_col, g_out_row = reduced[4:]
    for item in moves[11:17]:
        item.wait()
    for half in range(2):
        lanes = slice(half * 1152, half * 1152 + 1152)
        update(0, (0, every, lanes), g_in[:, lanes])
        update(0, (1, every, lanes), g_in_col[half])
        lanes = slice(half * 384, half * 384 + 384)
        update(1, (0, every, lanes), natural(g_out_row[half]))
        update(1, (1, every, lanes), natural(g_out_col[half]))
    leave(0, 1, 2, 21, 3, 4, 5, 22, 26, 27)
    for item in moves[:4] + moves[17:]:
        item.wait()
    for half in range(2):
        for part in range(2):
            start = part * 1536 + half * 768
            lanes = slice(start, start + 768)
            update(2, (every, lanes), reduced[2 + part][half])
            update(3, (every, lanes), reduced[part][half])
    leave(6, 7, 8, 23, 9, 10, 11, 24)
    update(4, (every, every), g_emb[:, :VOCAB])
    update(5, (every, every), g_norm[...])
    update(6, (every, every), stats[0:1, : HEADS + 1])
    leave(12, 13, 14, 25, 15, 16, 17, 18, 19, 20)
    for n in range(28):
        pltpu.make_async_copy(results[n], far[n], out_sems.at[n]).wait()


def update_call(reduced, g_in, g_emb, g_norm, stats, states):
    anywhere = pl.BlockSpec(memory_space=pl.ANY)
    flat = [item for state in states for item in state]
    shapes = [jax.ShapeDtypeStruct(item.shape, F32) for item in flat]
    shapes += [jax.ShapeDtypeStruct(states[n][0].shape, BF16) for n in range(5)]
    shapes += [jax.ShapeDtypeStruct((1, 4), F32), jax.ShapeDtypeStruct((1, 1), F32)]
    given = (*reduced, g_in, g_emb, g_norm, stats, *flat)
    return pl.pallas_call(
        update_kernel,
        out_shape=shapes,
        in_specs=[anywhere] * len(given),
        out_specs=[anywhere] * len(shapes),
        scratch_shapes=[pltpu.VMEM(item.shape, F32) for item in given]
        + [pltpu.VMEM(item.shape, item.dtype) for item in shapes]
        + [
            pltpu.SemaphoreType.DMA((len(given),)),
            pltpu.SemaphoreType.DMA((len(shapes),)),
            pltpu.VMEM((44, 512, 512), F32),
        ],
        compiler_params=pltpu.CompilerParams(vmem_limit_bytes=62 * 2**20),
    )(*given)


def adam_update(master, first, second, grad_part, rate):
    first = BETA_ONE * first + (1.0 - BETA_ONE) * grad_part
    second = BETA_TWO * second + (1.0 - BETA_TWO) * grad_part * grad_part
    moved = first / (1.0 - BETA_ONE**STEP) / (jnp.sqrt(second / (1.0 - BETA_TWO**STEP)) + ADAM_EPS)
    return (master - rate * (moved + WEIGHT_DECAY * master), first, second)


def shards(
    tokens,
    targets,
    masked,
    contact_pairs,
    labels,
    attention_in_master,
    attention_in_first,
    attention_in_second,
    attention_out_master,
    attention_out_first,
    attention_out_second,
    feed_up_master,
    feed_up_first,
    feed_up_second,
    feed_down_master,
    feed_down_first,
    feed_down_second,
    embedding_master,
    embedding_first,
    embedding_second,
    norm_params_master,
    norm_params_first,
    norm_params_second,
    contact_head_master,
    contact_head_first,
    contact_head_second,
):
    both = ("seq", "col")
    micro, rows_here, cols_here = tokens.shape
    ncol = lax.axis_size("col")
    ndev = lax.axis_size("seq") * ncol
    cols = cols_here * ncol
    me = lax.axis_index("seq") * ncol + lax.axis_index("col")
    per = ndev // micro
    cw = cols // per
    mine = me // per
    base = (me % per) * cw
    shard = D // ndev

    tiled = lax.axis_size("seq") == 16 and ncol == 2
    if tiled:
        raw = (
            tokens,
            targets,
            masked,
            contact_pairs.transpose(0, 2, 1),
            labels,
            embedding_master.T,
            norm_params_master,
            attention_in_master,
            attention_out_master,
            feed_up_master,
            feed_down_master.T,
        )
        weights, saved = forward_call(raw, contact_head_master)
        reduced, (g_in, g_emb, g_norm, stats) = backward_call(
            contact_head_master, [weights[n] for n in (7, 8, 5, 6, 4, 3, 2)], weights[1], saved
        )
        states = (
            (attention_in_master, attention_in_first, attention_in_second),
            (attention_out_master, attention_out_first, attention_out_second),
            (feed_up_master, feed_up_first, feed_up_second),
            (feed_down_master.T, feed_down_first.T, feed_down_second.T),
            (embedding_master.T, embedding_first.T, embedding_second.T),
            (norm_params_master, norm_params_first, norm_params_second),
            (contact_head_master[None], contact_head_first[None], contact_head_second[None]),
        )
        outs = update_call(reduced, g_in, g_emb, g_norm, stats, states)
        return (
            *outs[:9],
            *(item.T for item in outs[9:15]),
            *outs[15:18],
            *(item[0] for item in outs[18:21]),
            *outs[21:24],
            *(item.T for item in outs[24:26]),
            outs[26][0],
            outs[27][0, 0],
        )
    inputs = jnp.where(masked > 0, MASK_ID, tokens)
    masters = [
        jnp.concatenate(
            [
                jnp.pad(embedding_master.T, ((0, 0), (0, 128 - VOCAB))),
                jnp.pad(norm_params_master.T, ((0, 0), (0, 120))),
            ],
            1,
        ),
        attention_in_master[0],
        attention_out_master[0],
        attention_in_master[1],
        attention_out_master[1],
        feed_up_master,
        feed_down_master.T,
    ]
    whole = jnp.stack([inputs, targets])
    whole = lax.all_gather(lax.all_gather(whole, "col", axis=3, tiled=True), "seq", axis=2, tiled=True)
    pairs_all = lax.all_gather(
        jnp.concatenate([contact_pairs, labels[:, :, None]], -1), both, axis=1, tiled=True
    )
    gathered = []
    for master in masters:
        full = lax.all_gather(master.astype(BF16), both, axis=0, tiled=True)
        gathered.append(full.reshape(D, 2, -1).transpose(1, 0, 2))
    counts = (
        jnp.sum(whole[0] == MASK_ID).astype(F32),
        jnp.sum(pairs_all[..., 2] >= 0).astype(F32),
    )
    ids_all = lax.dynamic_index_in_dim(whole[0], mine, 0, False)
    ids_local = lax.dynamic_slice_in_dim(ids_all, base, cw, 1)
    targets_local = lax.dynamic_slice_in_dim(
        lax.dynamic_index_in_dim(whole[1], mine, 0, False), base, cw, 1
    )
    pairs = lax.dynamic_index_in_dim(pairs_all, mine, 0, False)

    table = gathered[0][0][:, :VP].T
    norms = gathered[0][1][:, :8].T.astype(F32)
    in_row, out_row, in_col, out_col, up_w, down_t = (
        jnp.concatenate([g[0], g[1]], 1) for g in gathered[1:]
    )
    big = (in_row, in_col, out_row, out_col, up_w, down_t)

    grads, tables, contact_total, mlm_total, bce_total, kept = step(
        big,
        table,
        norms,
        contact_head_master,
        ids_all,
        ids_local.reshape(-1),
        ids_local.T.reshape(-1),
        targets_local.T.reshape(-1),
        pairs[:, 0] - base,
        pairs[:, 1],
        pairs[:, 2],
        counts,
        cw,
    )
    table_pair, value_grad, table_grad, vectors = tables
    extras = jnp.zeros((2, D), F32).at[0, : HEADS + 3].set(
        jnp.concatenate([contact_total, mlm_total[None], bce_total[None]])
    )
    sums = jnp.concatenate([table_pair[:40], value_grad[:40], table_grad[:40], vectors, extras])
    flat_grad = jnp.concatenate([g.astype(BF16) for g in grads], 1)
    reduced = lax.psum_scatter(flat_grad, both, scatter_dimension=0, tiled=True).astype(F32)
    g_in_col, g_out_row, g_out_col, g_up, g_down = jnp.split(
        reduced, [3 * D, 4 * D, 5 * D, 5 * D + FF], 1
    )
    sums = lax.psum(sums, both)
    unit_t, rstd_t, normed_t, query_t, key_t = kept
    rows_all = ids_all.shape[0]
    spare = ((0, VP - 40), (0, 0))
    table_pair, value_grad, table_grad = (
        jnp.pad(sums[a : a + 40], spare) for a in (0, 40, 80)
    )
    vectors = sums[120:126]
    contact_grad, mlm_total, bce_total = (
        sums[126, : HEADS + 1], sums[126, HEADS + 1], sums[126, HEADS + 2]
    )
    row_scale = (HD * rows_all) ** (-0.5)
    query_grad = []
    key_grad = []
    for h in range(HEADS):
        pair = heads_of(table_pair, h)
        query_grad.append(jnp.dot(pair, heads_of(key_t, h).astype(F32), precision=PRECISE))
        key_grad.append(jnp.dot(pair.T, heads_of(query_t, h).astype(F32), precision=PRECISE))
    proj_grad = jnp.concatenate(
        [
            jnp.concatenate(query_grad, 1) * row_scale,
            jnp.concatenate(key_grad, 1) * row_scale,
            value_grad,
        ],
        1,
    )
    proj_hi, proj_lo = split_two(proj_grad)
    normed_grad = nt(proj_hi, in_row) + nt(proj_lo, in_row)
    back_t, scale_0, shift_0 = norm_back(unit_t, rstd_t, norms[0], normed_grad)
    table_grad = table_grad + back_t
    low = me * shard
    normed_mine = lax.dynamic_slice_in_dim(normed_t, low, shard, 1)
    grad_in_row = tn(normed_mine, proj_hi) + tn(normed_mine, proj_lo)
    norm_grad = jnp.concatenate([scale_0[None], vectors[:3], shift_0[None], vectors[3:]])
    table_mine = lax.dynamic_slice_in_dim(table_grad[:VOCAB], low, shard, 1)
    norm_mine = lax.dynamic_slice_in_dim(norm_grad, low, shard, 1)
    reduced_all = (g_in_col, g_out_row, g_out_col, g_up, g_down)

    local_square = (
        sum(jnp.sum(g * g) for g in reduced_all)
        + jnp.sum(grad_in_row * grad_in_row)
        + jnp.sum(table_mine * table_mine)
        + jnp.sum(norm_mine * norm_mine)
    )
    square = lax.psum(local_square, both) + jnp.sum(contact_grad * contact_grad)
    grad_norm = jnp.sqrt(square)
    factor = jnp.minimum(1.0, MAX_NORM / grad_norm)
    in_new, in_moment, in_square = adam_update(
        attention_in_master, attention_in_first, attention_in_second, jnp.stack([grad_in_row, g_in_col]) * factor, LEARN_RATE
    )
    out_new, out_moment, out_square = adam_update(
        attention_out_master, attention_out_first, attention_out_second, jnp.stack([g_out_row, g_out_col]) * factor, LEARN_RATE
    )
    up_new, up_moment, up_square = adam_update(
        feed_up_master, feed_up_first, feed_up_second, g_up * factor, LEARN_RATE
    )
    down_new, down_moment, down_square = adam_update(
        feed_down_master, feed_down_first, feed_down_second, g_down.T * factor, LEARN_RATE
    )
    table_new, table_moment, table_square = adam_update(
        embedding_master, embedding_first, embedding_second, table_mine * factor, VECTOR_RATE
    )
    norm_new, norm_moment, norm_square = adam_update(
        norm_params_master, norm_params_first, norm_params_second, norm_mine * factor, VECTOR_RATE
    )
    head_new, head_moment, head_square = adam_update(
        contact_head_master, contact_head_first, contact_head_second, contact_grad * factor, VECTOR_RATE
    )
    loss_parts = jnp.stack([mlm_total, counts[0], bce_total, counts[1]])
    return (
        in_new, in_moment, in_square,
        out_new, out_moment, out_square,
        up_new, up_moment, up_square,
        down_new, down_moment, down_square,
        table_new, table_moment, table_square,
        norm_new, norm_moment, norm_square,
        head_new, head_moment, head_square,
        in_new.astype(BF16), out_new.astype(BF16), up_new.astype(BF16), down_new.astype(BF16), table_new.astype(BF16),
        loss_parts, grad_norm,
    )


def solution(mesh):
    both = ("seq", "col")
    cells = P(None, "seq", "col")
    stack = P(None, both, None)
    row_split = P(both, None)
    col_split = P(None, both)
    weights = [stack] * 6 + [row_split] * 3 + [col_split] * 9 + [P()] * 3
    return jax.shard_map(
        shards,
        mesh=mesh,
        in_specs=(cells, cells, cells, stack, col_split, *weights),
        out_specs=(*weights, stack, stack, row_split, col_split, col_split, P(), P()),
        check_vma=False,
    )
```

```python
import typing

import jax
import jax.numpy as jnp
from jax import lax
from jax.experimental import pallas as pl
from jax.experimental.pallas import tpu as pltpu
from jax.sharding import PartitionSpec as P

D = 768
HEADS = 12
HD = 64
FF = 3072
VOCAB = 33
VP = 64
STEP = 10

NORM_EPS = 1e-05
MASK_ID = 32
MAX_NORM = 0.001
LEARN_RATE = 0.05
VECTOR_RATE = 0.5
BETA_ONE = 0.9
BETA_TWO = 0.95
ADAM_EPS = 1e-08
WEIGHT_DECAY = 0.01
PRECISE = lax.Precision.HIGHEST
F32 = jnp.float32
BF16 = jnp.bfloat16


def nn(left, right):
    return lax.dot_general(left, right, (((1,), (0,)), ((), ())), preferred_element_type=F32)


def tn(left, right):
    return lax.dot_general(left, right, (((0,), (0,)), ((), ())), preferred_element_type=F32)


def nt(left, right):
    return lax.dot_general(left, right, (((1,), (1,)), ((), ())), preferred_element_type=F32)


def split_two(values):
    high = values.astype(BF16)
    return high, (values - high.astype(F32)).astype(BF16)


def norm_stats(values):
    centre = values - jnp.mean(values, -1, keepdims=True)
    rstd = lax.rsqrt(jnp.mean(centre * centre, -1, keepdims=True) + NORM_EPS)
    return centre * rstd, rstd


def norm_back(unit, rstd, scale_vec, upstream):
    inner = upstream * scale_vec
    grad = rstd * (
        inner - jnp.mean(inner, -1, keepdims=True) - unit * jnp.mean(inner * unit, -1, keepdims=True)
    )
    return grad, jnp.sum(upstream * unit, 0), jnp.sum(upstream, 0)


GELU_K = 0.7978845608028654
GELU_C = 0.044715


def gelu_parts(up):
    square = up * up
    bent = jnp.tanh(GELU_K * up * (1.0 + GELU_C * square))
    half = 0.5 * (1.0 + bent)
    slope = half + 0.5 * up * (1.0 - bent * bent) * GELU_K * (1.0 + 3.0 * GELU_C * square)
    return up * half, slope


def heads_of(block, head):
    return block[:, head * HD : (head + 1) * HD]


def step(big, table, norms, contact_head, ids_all, ids_ri, ids_ir, targets_ir, pair_first, pair_second, labels, counts, cw):
    in_row, in_col, out_row, out_col, up_w, down_t = big
    rows, cols = ids_all.shape
    here = rows * cw
    row_scale = (HD * rows) ** (-0.5)
    vocab = jnp.arange(VP)[:, None]
    hot_all = (ids_all[:, None, :] == vocab[None]).astype(BF16).reshape(rows * VP, cols)
    hot_ri = (ids_ri[None, :] == vocab).astype(BF16)
    hot_ir = (ids_ir[None, :] == vocab).astype(BF16)
    spot = jnp.arange(here)
    perm = (
        ((spot // rows)[:, None] == (spot % cw)[None, :])
        & ((spot % rows)[:, None] == (spot // cw)[None, :])
    ).astype(BF16)

    def to_heads(block):
        return block.reshape(rows, cw, HEADS, VP).transpose(2, 1, 0, 3).reshape(HEADS * cw, rows * VP)

    def to_tokens(block):
        return block.reshape(HEADS, cw, rows, VP).transpose(2, 1, 0, 3).reshape(here, HEADS * VP)

    def per_head(block, other, how):
        return jnp.concatenate(
            [how(heads_of(block, h), heads_of(other, h)) for h in range(HEADS)], -1
        )

    table_f = table.astype(F32)
    unit_t, rstd_t = norm_stats(table_f)
    normed_t = (unit_t * norms[0] + norms[4]).astype(BF16)
    proj_t = nn(normed_t, in_row).astype(BF16)
    query_t, key_t, value_t = proj_t[:, :D], proj_t[:, D : 2 * D], proj_t[:, 2 * D :]

    pair_t = per_head(query_t, key_t, nt)
    pair_hi, pair_lo = split_two(pair_t)
    left_hi = to_heads(tn(hot_ri, pair_hi).astype(BF16))
    left_lo = to_heads(tn(hot_ri, pair_lo).astype(BF16))
    score = (nn(left_hi, hot_all) + nn(left_lo, hot_all)) * row_scale
    prob = jax.nn.softmax(score, axis=-1)
    prob_low = prob.astype(BF16)
    weight_t = to_tokens(nt(prob_low, hot_all))
    weight_hi, weight_lo = split_two(weight_t)
    row_mixed_ri = (
        per_head(weight_hi, value_t, nn) + per_head(weight_lo, value_t, nn)
    ).astype(BF16)
    row_mixed = nn(perm, row_mixed_ri).astype(BF16)
    embedded = tn(hot_ir, table)
    after_row = embedded + nn(row_mixed, out_row)

    prob_cube = prob_low.astype(F32).reshape(HEADS, cw, cols)
    head_sum = jnp.sum(prob_cube * contact_head[:HEADS, None, None], 0)
    first_hot = (pair_first[None, :] == jnp.arange(cw)[:, None]).astype(F32)
    second_hot = (pair_second[None, :] == jnp.arange(cols)[:, None]).astype(BF16)
    sum_hi, sum_lo = split_two(head_sum)
    sum_last = (head_sum - sum_hi.astype(F32) - sum_lo.astype(F32)).astype(BF16)
    picked = nn(sum_hi, second_hot) + nn(sum_lo, second_hot) + nn(sum_last, second_hot)
    contact_logit = jnp.sum(picked * first_hot, 0) * cols + contact_head[HEADS]
    owned = jnp.sum(first_hot, 0) > 0
    valid = (labels >= 0) & owned
    positive = (labels == 1).astype(F32)
    bce_sum = jnp.sum(
        jnp.where(valid, jax.nn.softplus(contact_logit) - positive * contact_logit, 0.0)
    )
    coef = jnp.where(valid, jax.nn.sigmoid(contact_logit) - positive, 0.0) / counts[1]
    coef_hi, coef_lo = split_two(coef)
    first_low = first_hot.astype(BF16)
    touch = nt(first_low * coef_hi[None], second_hot) + nt(first_low * coef_lo[None], second_hot)
    grad_contact = jnp.concatenate(
        [jnp.sum(prob_cube * touch[None], (1, 2)) * cols, jnp.sum(coef)[None]]
    )

    unit_1, rstd_1 = norm_stats(after_row)
    col_normed = (unit_1 * norms[1] + norms[5]).astype(BF16)
    col_proj = nn(col_normed, in_col).astype(BF16)
    group = 128 if here % 128 == 0 and 128 % rows == 0 else here
    groups = here // group
    lane = jnp.arange(group)
    same = (lane[:, None] // rows) == (lane[None, :] // rows)

    def cut(block):
        return block.reshape(groups, group, HEADS, HD)

    col_query, col_key, col_value = (cut(col_proj[:, k * D : (k + 1) * D]) for k in range(3))
    col_score = jnp.einsum("gqhe,gkhe->ghqk", col_query, col_key, preferred_element_type=F32) * HD ** (-0.5)
    col_prob = jax.nn.softmax(jnp.where(same, col_score, -1e30), axis=-1)
    col_prob_low = col_prob.astype(BF16)
    col_mixed = (
        jnp.einsum("ghqk,gkhe->gqhe", col_prob_low, col_value, preferred_element_type=F32)
        .astype(BF16)
        .reshape(here, D)
    )
    after_col = after_row + nn(col_mixed, out_col)

    unit_2, rstd_2 = norm_stats(after_col)
    feed_normed = (unit_2 * norms[2] + norms[6]).astype(BF16)
    hidden_up = nn(feed_normed, up_w)
    active, slope = gelu_parts(hidden_up)
    active = active.astype(BF16)
    after_feed = after_col + nt(active, down_t)
    unit_3, rstd_3 = norm_stats(after_feed)
    head_normed = (unit_3 * norms[3] + norms[7]).astype(BF16)
    logits = nt(table, head_normed) * D ** (-0.5)
    logits = jnp.where(vocab < VOCAB, logits, -1e30)
    top = jnp.max(logits, 0, keepdims=True)
    shifted = logits - top
    log_probs = shifted - jnp.log(jnp.sum(jnp.exp(shifted), 0, keepdims=True))
    target_hot = (targets_ir[None, :] == vocab).astype(F32)
    keep = ids_ir[None, :] == MASK_ID
    mlm_sum = -jnp.sum(jnp.where(keep & (target_hot > 0), log_probs, 0.0))
    logit_grad = jnp.where(keep, jnp.exp(log_probs) - target_hot, 0.0) / counts[0]
    logit_low = (logit_grad * D ** (-0.5)).astype(BF16)

    grad_head = nn(logit_low, head_normed)
    stream, scale_3, shift_3 = norm_back(unit_3, rstd_3, norms[3], tn(logit_low, table))
    branch = stream.astype(BF16)
    grad_down = tn(branch, active)
    up_low = (nn(branch, down_t) * slope).astype(BF16)
    grad_up = tn(feed_normed, up_low)
    inner, scale_2, shift_2 = norm_back(unit_2, rstd_2, norms[2], nt(up_low, up_w))
    stream = stream + inner
    branch = stream.astype(BF16)
    grad_out_col = tn(col_mixed, branch)
    mixed_low = nt(branch, out_col).astype(BF16)
    mixed_cut = cut(mixed_low)
    prob_grad = jnp.einsum("gqhe,gkhe->ghqk", mixed_cut, col_value, preferred_element_type=F32)
    score_grad = col_prob * (prob_grad - jnp.sum(col_prob * prob_grad, -1, keepdims=True))
    score_low = score_grad.astype(BF16)
    grad_q = jnp.einsum("ghqk,gkhe->gqhe", score_low, col_key, preferred_element_type=F32)
    grad_k = jnp.einsum("ghqk,gqhe->gkhe", score_low, col_query, preferred_element_type=F32)
    grad_v = jnp.einsum("ghqk,gqhe->gkhe", col_prob_low, mixed_cut, preferred_element_type=F32)
    proj_low = jnp.concatenate(
        [
            (grad_q * HD ** (-0.5)).reshape(here, D),
            (grad_k * HD ** (-0.5)).reshape(here, D),
            grad_v.reshape(here, D),
        ],
        -1,
    ).astype(BF16)
    grad_in_col = tn(col_normed, proj_low)
    inner, scale_1, shift_1 = norm_back(unit_1, rstd_1, norms[1], nt(proj_low, in_col))
    stream = stream + inner
    branch = stream.astype(BF16)
    grad_out_row = tn(row_mixed, branch)
    mixed_low = nt(branch, out_row).astype(BF16)
    mixed_ri = tn(perm, mixed_low).astype(BF16)
    drive_hi, drive_lo = split_two(per_head(mixed_ri, value_t, nt))
    prob_grad = nn(to_heads(drive_hi), hot_all) + nn(to_heads(drive_lo), hot_all)
    prob_grad = prob_grad + (
        touch[None] * (contact_head[:HEADS, None, None] * cols)
    ).reshape(HEADS * cw, cols)
    score_grad = prob * (prob_grad - jnp.sum(prob * prob_grad, -1, keepdims=True))
    score_low = score_grad.astype(BF16)
    spread = to_tokens(nt(score_low, hot_all)).astype(BF16)
    table_pair = nn(hot_ri, spread)
    value_grad = per_head(weight_hi, mixed_ri, tn)
    stream_hi, stream_lo = split_two(stream)
    lookup_grad = nn(hot_ir, stream_hi) + nn(hot_ir, stream_lo)
    vectors = jnp.stack([scale_1, scale_2, scale_3, shift_1, shift_2, shift_3])
    return (
        (grad_in_col, grad_out_row, grad_out_col, grad_up, grad_down),
        (table_pair, value_grad, grad_head + lookup_grad, vectors),
        grad_contact,
        mlm_sum,
        bce_sum,
        (unit_t, rstd_t, normed_t, query_t, key_t),
    )


MESH = pl.DeviceIdType.MESH
NZ, NY = 4, 2


def place():
    s, c = lax.axis_index("seq"), lax.axis_index("col")
    z, y, k = s // 4, lax.rem(s // 2, 2), lax.rem(s, 2)
    return z, y, k, c


def device(z, y, k, c):
    return (z * 4 + y * 2 + k, c)


def greet_all():
    z, y, k, c = place()
    me = (z * 4 + y * 2 + k) * 2 + c
    barrier = pltpu.get_barrier_semaphore()

    def signal(step, carry):
        other = lax.rem(me + step, 32)
        pl.semaphore_signal(
            barrier, inc=1, device_id=(other // 2, lax.rem(other, 2)), device_id_type=MESH
        )
        return carry

    lax.fori_loop(1, 32, signal, 0)
    return barrier


def remote(src, dst, send, recv, target):
    return pltpu.make_async_remote_copy(
        src_ref=src, dst_ref=dst, send_sem=send, recv_sem=recv, device_id=target, device_id_type=MESH
    )


ROWS, COLS, WIDE, HERE = 16, 512, 32, 512
PAIRS = 6
SLOTS = 1024
UP_TILE = 384


def iota(shape, dim):
    return lax.broadcasted_iota(jnp.int32, shape, dim)


def one_zero(test):
    return jnp.where(test, 1.0, 0.0)


def total_of(values):
    return jnp.sum(jnp.sum(values, 0, keepdims=True), 1, keepdims=True)


def half_lanes(values, side):
    lane = iota(values.shape, len(values.shape) - 1)
    keep = (lane < 64) if side == 0 else (lane >= 64)
    return jnp.where(keep, values.astype(F32), 0.0).astype(BF16)


def stacked(values):
    return jnp.concatenate([half_lanes(values, 0), half_lanes(values, 1)], 0)


def unstacked(values, count):
    lane = iota((count, 128), 1)
    return jnp.where(lane < 64, values[:count], values[count:])


def swap_blocks(first, second):
    lane = iota(first.shape, 1)
    low = jnp.where(lane < 64, first, pltpu.roll(second, 64, 1))
    high = jnp.where(lane < 64, pltpu.roll(first, 64, 1), second)
    return low, high


def split_heads_to(source, high_ref, low_ref):
    for rp in range(ROWS // 2):
        for hp in range(PAIRS):
            lanes = slice(hp * 128, hp * 128 + 128)
            first = source[rp * 64 : rp * 64 + 32, lanes]
            second = source[rp * 64 + 32 : rp * 64 + 64, lanes]
            for side, block in enumerate(swap_blocks(first, second)):
                top, rest = split_two(block)
                rows = slice((2 * hp + side) * 32, (2 * hp + side) * 32 + 32)
                high_ref[rows, rp * 128 : rp * 128 + 128] = top
                low_ref[rows, rp * 128 : rp * 128 + 128] = rest


def merge_heads(probs, hot_all, high_ref, low_ref):
    for rp in range(ROWS // 2):
        block = nt(probs, hot_all[rp * 128 : rp * 128 + 128, :])
        for hp in range(PAIRS):
            first = block[hp * 64 : hp * 64 + 32]
            second = block[hp * 64 + 32 : hp * 64 + 64]
            for side, part in enumerate(swap_blocks(first, second)):
                top, rest = split_two(part)
                rows = slice(rp * 64 + side * 32, rp * 64 + side * 32 + 32)
                high_ref[rows, hp * 128 : hp * 128 + 128] = top
                if low_ref is not None:
                    low_ref[rows, hp * 128 : hp * 128 + 128] = rest


def norm_rows(source, gain, bias, unit_ref, rstd_ref, normed_ref):
    def body(at, carry):
        rows = pl.ds(pl.multiple_of(at * 64, 64), 64)
        values = source[rows, :]
        centre = values - jnp.sum(values, -1, keepdims=True) * (1.0 / D)
        rstd = lax.rsqrt(jnp.sum(centre * centre, -1, keepdims=True) * (1.0 / D) + NORM_EPS)
        unit = centre * rstd
        unit_ref[rows, :] = unit
        rstd_ref[rows, :] = jnp.broadcast_to(rstd, (64, 128))
        normed_ref[rows, :] = (unit * gain + bias).astype(BF16)
        return carry

    lax.fori_loop(0, HERE // 64, body, 0)


def transpose_into(source, target):
    def body(at, carry):
        rows = pl.ds(pl.multiple_of(at * 128, 128), 128)
        target[:, rows] = source[rows, :].astype(F32).T.astype(BF16)
        return carry

    lax.fori_loop(0, HERE // 128, body, 0)


def over_tiles(width, tile, body):
    for half in range(2):

        def step(at, carry, half=half):
            body(half, pl.multiple_of(at * tile, tile))
            return carry

        lax.fori_loop(0, width // tile, step, 0)


def column_mask():
    rows, lanes = iota((256, 128), 0), iota((256, 128), 1)
    return ((rows & 127) >> 4) == (lanes >> 4)


class Saved(typing.NamedTuple):
    stream: typing.Any
    branch: typing.Any
    unit_1: typing.Any
    unit_2: typing.Any
    rstd_1: typing.Any
    rstd_2: typing.Any
    row_mixed_t: typing.Any
    col_normed_t: typing.Any
    col_mixed_t: typing.Any
    feed_normed_t: typing.Any
    col_proj: typing.Any
    col_prob: typing.Any
    active: typing.Any
    slope: typing.Any
    grad_head: typing.Any
    hot_all: typing.Any
    hot_ri: typing.Any
    hot_ir: typing.Any
    prob: typing.Any
    weight_hi: typing.Any
    value_two: typing.Any
    touch: typing.Any
    table: typing.Any
    norms: typing.Any
    proj_t: typing.Any
    extras: typing.Any
    moved: typing.Any


AT = Saved(*range(len(Saved._fields)))
SAVED = Saved(
    stream=((HERE, D), F32),
    branch=((HERE, D), BF16),
    unit_1=((HERE, D), F32),
    unit_2=((HERE, D), F32),
    rstd_1=((HERE, 128), F32),
    rstd_2=((HERE, 128), F32),
    row_mixed_t=((D, HERE), BF16),
    col_normed_t=((D, HERE), BF16),
    col_mixed_t=((D, HERE), BF16),
    feed_normed_t=((D, HERE), BF16),
    col_proj=((HERE, 3 * D), BF16),
    col_prob=((4 * PAIRS, 256, 128), F32),
    active=((HERE, FF), BF16),
    slope=((HERE, FF), BF16),
    grad_head=((VP, D), F32),
    hot_all=((ROWS * VP, COLS), BF16),
    hot_ri=((VP, HERE), BF16),
    hot_ir=((VP, HERE), BF16),
    prob=((HEADS * WIDE, COLS), F32),
    weight_hi=((HERE, D), BF16),
    value_two=((PAIRS, 128, 128), BF16),
    touch=((WIDE, COLS), F32),
    table=((VP, D), F32),
    norms=((8, D), F32),
    proj_t=((VP, 3 * D), BF16),
    extras=((8, 128), F32),
    moved=((8, D), F32),
)


class Forward(typing.NamedTuple):
    ids: typing.Any
    targets: typing.Any
    slots: typing.Any
    normed: typing.Any
    mixed: typing.Any
    weight_lo: typing.Any
    left_hi: typing.Any
    left_lo: typing.Any
    lookup: typing.Any
    prob_low: typing.Any
    unit: typing.Any
    rstd: typing.Any


FORWARD = Forward(
    ids=((ROWS, COLS), jnp.int32),
    targets=((ROWS, 128), jnp.int32),
    slots=((8, SLOTS), jnp.int32),
    normed=((HERE, D), BF16),
    mixed=((HERE, D), BF16),
    weight_lo=((HERE, D), BF16),
    left_hi=((HEADS * WIDE, ROWS * VP), BF16),
    left_lo=((HEADS * WIDE, ROWS * VP), BF16),
    lookup=((HERE, D), F32),
    prob_low=((HEADS * WIDE, COLS), BF16),
    unit=((HERE, D), F32),
    rstd=((HERE, 128), F32),
)


def position():
    z, y, k, c = place()
    me = (z * 4 + y * 2 + k) * 2 + c
    return z // 2, lax.rem(me, 16)


def read_tokens(small, f):
    alignment, block = position()
    side, part = block // 8, lax.rem(block // 4, 2)
    for r in range(ROWS):
        for cc in range(2):
            for q in range(2):
                lanes = slice(cc * 256 + q * 128, cc * 256 + q * 128 + 128)
                f.ids[r : r + 1, lanes] = small[r * 2 + cc, pl.ds(2 * alignment + q, 1), :]
        f.targets[r : r + 1, :] = small[r * 2 + side, pl.ds(4 + 2 * alignment + part, 1), :]
    lane = iota((1, 128), 1)
    for number in range(SLOTS // 128):
        for which in range(3):
            row = pl.ds(8 + 3 * alignment + which, 1)
            first = small[number * 4 + side, row, :]
            second = pltpu.roll(small[number * 4 + 2 + side, row, :], 64, 1)
            f.slots[which : which + 1, number * 128 : number * 128 + 128] = jnp.where(
                lane < 64, first, second
            )


def local_hot(values, shift):
    values = pltpu.roll(values, shift, 1)
    turned = [values] + [pltpu.roll(values, 32 * n, 1) for n in (1, 2, 3)]
    lane = iota((1, 128), 1)
    tiles = []
    for tile in range(4):
        row = turned[3][4 * tile + 3 : 4 * tile + 4]
        for n in (2, 1, 0):
            row = jnp.where(lane < 32 * n + 32, turned[n][4 * tile + n : 4 * tile + n + 1], row)
        tiles.append(row)
    row = jnp.concatenate(tiles, 1)
    return one_zero(row == iota((VP, HERE), 0)).astype(BF16)


def contact_part(contact_head, f, s, pair_count):
    _, block = position()
    base = block * WIDE
    head_sum = jnp.zeros((WIDE, COLS), F32)
    for h in range(HEADS):
        head_sum = head_sum + contact_head[h] * f.prob_low[h * 32 : h * 32 + 32, :].astype(F32)
    top, rest = split_two(head_sum)
    last = (head_sum - top.astype(F32) - rest.astype(F32)).astype(BF16)
    parts = jnp.concatenate([top, rest, last], 0)
    touch = jnp.zeros((WIDE, COLS), F32)
    bce = jnp.zeros((1, 1), F32)
    coef_sum = jnp.zeros((1, 1), F32)
    for number in range(SLOTS // 512):
        lanes = slice(number * 512, number * 512 + 512)
        first, second, label = (f.slots[n : n + 1, lanes] for n in range(3))
        second_hot = one_zero(second == iota((COLS, 512), 0)).astype(BF16)
        picked = nn(parts, second_hot)
        picked = picked[:32] + picked[32:64] + picked[64:]
        first_hot = one_zero((first - base) == iota((WIDE, 512), 0))
        logit = jnp.sum(picked * first_hot, 0, keepdims=True) * COLS + contact_head[HEADS]
        owned = jnp.sum(first_hot, 0, keepdims=True) > 0.5
        valid = (label >= 0) & owned
        positive = one_zero(label == 1)
        small = jnp.exp(-jnp.abs(logit))
        soft = jnp.maximum(logit, 0.0) + jnp.log(1.0 + small)
        bce = bce + total_of(jnp.where(valid, soft - positive * logit, 0.0))
        sigmoid = jnp.where(logit >= 0.0, 1.0, small) / (1.0 + small)
        coef = jnp.where(valid, sigmoid - positive, 0.0) / pair_count
        coef_sum = coef_sum + total_of(coef)
        coef_top, coef_rest = split_two(first_hot * coef)
        touch = touch + nt(coef_top, second_hot) + nt(coef_rest, second_hot)
    s.touch[...] = touch
    column = iota((1, 128), 1)
    row = jnp.where(column == HEADS, coef_sum, 0.0)
    for h in range(HEADS):
        part = total_of(touch * f.prob_low[h * 32 : h * 32 + 32, :].astype(F32)) * COLS
        row = row + jnp.where(column == h, part, 0.0)
    return row, bce


def feature_order():
    shape = (384, 384)
    spot = iota(shape, 0)
    block = (spot * 2731) >> 16
    swapped = (block & 28) | ((block & 1) << 1) | ((block >> 1) & 1)
    return one_zero(spot + (swapped - block) * 24 == iota(shape, 1)).astype(BF16)


def forward_body(small, contact_head, weights, s, f, ready, hook, emit):
    emb, in_row, out_row, in_col, out_col = weights[:5]
    up_parts, down_parts = weights[5:7], weights[7:9]
    ready(-1)
    hook()
    read_tokens(small, f)
    _, block = position()
    shift = lax.rem(128 - lax.rem(block, 4) * 32, 128)
    window = pl.ds(pl.multiple_of((block // 4) * 128, 128), 128)
    hot_ri = local_hot(f.ids[:, window], shift)
    goal_ri = local_hot(f.targets[...], shift)
    s.hot_ri[...] = hot_ri
    for r in range(ROWS):
        row = f.ids[r : r + 1, :]
        s.hot_all[r * VP : r * VP + VP, :] = one_zero(row == iota((VP, COLS), 0)).astype(BF16)
    shape = (HERE, HERE)
    back = (
        ((iota(shape, 1) >> 4) == (iota(shape, 0) & 31))
        & ((iota(shape, 1) & 15) == (iota(shape, 0) >> 5))
    )
    back = one_zero(back).astype(BF16)
    hot_ir = nn(hot_ri, back).astype(BF16)
    s.hot_ir[...] = hot_ir
    goal = nn(goal_ri, back)
    entries = jnp.zeros((4, 128), F32)
    labelled = jnp.zeros((1, 128), F32)
    for d in range(32):
        entries = entries + one_zero(small[d, 0:4, :] == MASK_ID)
        labelled = labelled + one_zero(small[d, 10:11, :] >= 0) + one_zero(small[d, 13:14, :] >= 0)
    entries, labelled = total_of(entries), total_of(labelled)

    hook()
    table = emb[0].astype(F32).T[:VP]
    norms = emb[1].astype(F32).T[:8]
    s.table[...] = table
    s.norms[...] = norms
    table_low = table.astype(BF16)

    def vector(number):
        return norms[number : number + 1, :]

    unit_t, _ = norm_stats(table)
    normed_t = (unit_t * vector(0) + vector(4)).astype(BF16)
    hook()
    for half in range(2):
        s.proj_t[:, half * 1152 : half * 1152 + 1152] = nn(normed_t, in_row[half]).astype(BF16)
    pair_parts = []
    for hp in range(PAIRS):
        lanes = slice(hp * 128, hp * 128 + 128)
        key = s.proj_t[:, D + hp * 128 : D + hp * 128 + 128]
        value = s.proj_t[:, 2 * D + hp * 128 : 2 * D + hp * 128 + 128]
        s.value_two[hp] = stacked(value)
        pair_parts.append(nt(s.proj_t[:, lanes], stacked(key)))
    pair_hi, pair_lo = split_two(jnp.concatenate(pair_parts, 1))
    hook()
    f.lookup[...] = tn(hot_ri, pair_hi) + tn(hot_ri, pair_lo)
    split_heads_to(f.lookup, f.left_hi, f.left_lo)
    hook()
    hot_all = s.hot_all[...]
    score = (nn(f.left_hi[...], hot_all) + nn(f.left_lo[...], hot_all)) * (HD * ROWS) ** (-0.5)
    score = jnp.exp(score - jnp.max(score, -1, keepdims=True))
    prob = score / jnp.sum(score, -1, keepdims=True)
    s.prob[...] = prob
    f.prob_low[...] = prob.astype(BF16)
    hook()
    merge_heads(f.prob_low[...], s.hot_all, s.weight_hi, f.weight_lo)
    hook()
    for hp in range(PAIRS):
        lanes = slice(hp * 128, hp * 128 + 128)
        value = s.value_two[hp]
        f.mixed[:, lanes] = (nn(s.weight_hi[:, lanes], value) + nn(f.weight_lo[:, lanes], value)).astype(BF16)
    ahead = (
        ((iota(shape, 0) >> 4) == (iota(shape, 1) & 31))
        & ((iota(shape, 0) & 15) == (iota(shape, 1) >> 5))
    )
    f.mixed[...] = nn(one_zero(ahead).astype(BF16), f.mixed[...]).astype(BF16)
    transpose_into(f.mixed, s.row_mixed_t)
    s.stream[...] = tn(hot_ir, table_low)
    hook()
    contact_row, bce = contact_part(contact_head, f, s, labelled)
    emit(AT.hot_all, AT.hot_ri, AT.hot_ir, AT.table, AT.norms, AT.proj_t, AT.value_two, AT.prob, AT.weight_hi, AT.row_mixed_t, AT.touch)

    hook()
    for half in range(2):
        lanes = slice(half * 384, half * 384 + 384)
        s.stream[:, lanes] += nn(f.mixed[...], out_row[half])
    norm_rows(s.stream, vector(1), vector(5), s.unit_1, s.rstd_1, f.normed)
    transpose_into(f.normed, s.col_normed_t)
    emit(AT.unit_1, AT.rstd_1, AT.col_normed_t)
    def project(half, at):
        s.col_proj[:, half * 1152 + at : half * 1152 + at + 384] = nn(
            f.normed[...], in_col[half, :, at : at + 384]
        ).astype(BF16)

    for third in range(3):
        hook()
        for half in range(2):
            project(half, third * 384)
    emit(AT.col_proj)

    def attend(at, carry):
        rows = pl.ds(pl.multiple_of((at // PAIRS) * 128, 128), 128)
        lane = lax.rem(at, PAIRS) * 128

        def lanes(part):
            return pl.ds(pl.multiple_of(part * D + lane, 128), 128)

        query = stacked(s.col_proj[rows, lanes(0)])
        score = nt(query, s.col_proj[rows, lanes(1)]) * HD ** (-0.5)
        score = jnp.where(column_mask(), score, -1e30)
        score = jnp.exp(score - jnp.max(score, -1, keepdims=True))
        prob = score / jnp.sum(score, -1, keepdims=True)
        s.col_prob[at] = prob
        mixed = nn(prob.astype(BF16), s.col_proj[rows, lanes(2)])
        f.mixed[rows, lanes(0)] = unstacked(mixed, 128).astype(BF16)
        return carry

    for part in range(4):
        hook()
        lax.fori_loop(part * PAIRS, part * PAIRS + PAIRS, attend, 0, unroll=3)
    hook()
    transpose_into(f.mixed, s.col_mixed_t)
    emit(AT.col_prob, AT.col_mixed_t)
    for half in range(2):
        lanes = slice(half * 384, half * 384 + 384)
        s.stream[:, lanes] += nn(f.mixed[...], out_col[half])
    norm_rows(s.stream, vector(2), vector(6), s.unit_2, s.rstd_2, f.normed)
    transpose_into(f.normed, s.feed_normed_t)
    emit(AT.unit_2, AT.rstd_2, AT.feed_normed_t)
    for part in range(2):

        def widen(half, at, part=part):
            lanes = slice(part * 1536 + half * 768 + at, part * 1536 + half * 768 + at + UP_TILE)
            up = nn(f.normed[...], up_parts[part][half, :, at : at + UP_TILE])
            active, slope = gelu_parts(up)
            s.active[:, lanes] = active.astype(BF16)
            s.slope[:, lanes] = slope.astype(BF16)

        for half in range(2):
            hook()
            for at in range(0, 768, UP_TILE):
                widen(half, at)

    emit(AT.active, AT.slope)
    for part, at, size in ((0, 0, 768), (1, 0, 384), (1, 384, 384)):
        hook()
        for half in range(2):
            start = part * 1536 + half * 768 + at
            s.stream[...] += nt(
                s.active[:, start : start + size], down_parts[part][half, :, at : at + size]
            )
    hook()
    norm_rows(s.stream, vector(3), vector(7), f.unit, f.rstd, f.normed)
    logits = nt(table_low, f.normed[...]) * D ** (-0.5)
    vocab = iota((VP, HERE), 0)
    logits = jnp.where(vocab < VOCAB, logits, -1e30)
    shifted = logits - jnp.max(logits, 0, keepdims=True)
    log_probs = shifted - jnp.log(jnp.sum(jnp.exp(shifted), 0, keepdims=True))
    keep = hot_ir[MASK_ID : MASK_ID + 1].astype(F32) > 0.5
    mlm = -total_of(jnp.where(keep & (goal > 0.5), log_probs, 0.0))
    logit_grad = jnp.where(keep, jnp.exp(log_probs) - goal, 0.0) / entries
    logit_low = (logit_grad * D ** (-0.5)).astype(BF16)
    s.grad_head[...] = nn(logit_low, f.normed[...])
    hook()
    f.lookup[...] = tn(logit_low, table_low)
    scale_3, shift_3 = back_rows(f.unit, f.rstd, vector(3), f.lookup, s.stream, s.branch, True)
    emit(AT.stream, AT.branch)
    line = iota((8, D), 0)
    s.moved[...] = jnp.where(line == 0, scale_3, jnp.where(line == 1, shift_3, 0.0))
    column = iota((1, 128), 1)
    row = contact_row + jnp.where(column == HEADS + 1, mlm, 0.0) + jnp.where(column == HEADS + 2, bce, 0.0)
    counted = jnp.where(column == 0, entries, 0.0) + jnp.where(column == 1, labelled, 0.0)
    line = iota((8, 128), 0)
    s.extras[...] = jnp.where(line == 0, row, jnp.where(line == 1, counted, 0.0))
    emit(AT.grad_head, AT.extras, AT.moved)
    hook()


def back_rows(unit_ref, rstd_ref, gain, upstream_ref, stream_ref, low_ref, first):
    def body(at, carry):
        scale, move = carry
        rows = pl.ds(pl.multiple_of(at * 64, 64), 64)
        upstream = upstream_ref[rows, :]
        unit = unit_ref[rows, :]
        inner = upstream * gain
        mean = jnp.sum(inner, -1, keepdims=True) * (1.0 / D)
        along = jnp.sum(inner * unit, -1, keepdims=True) * (1.0 / D)
        grad = rstd_ref[rows, 0:1] * (inner - mean - unit * along)
        if not first:
            grad = grad + stream_ref[rows, :]
        stream_ref[rows, :] = grad
        low_ref[rows, :] = grad.astype(BF16)
        touched = upstream * unit
        for n in range(8):
            scale = scale + touched[n * 8 : n * 8 + 8]
            move = move + upstream[n * 8 : n * 8 + 8]
        return scale, move

    zero = jnp.zeros((8, D), F32)
    scale, move = lax.fori_loop(0, HERE // 64, body, (zero, zero))
    return jnp.sum(scale, 0, keepdims=True), jnp.sum(move, 0, keepdims=True)


MATRICES = (128, 1152, 384, 1152, 384, 768, 768, 768, 768)
UNITS = (
    (0, 0, 128, True),
    (1, 0, 384, True),
    (1, 384, 384, True),
    (1, 768, 384, True),
    (2, 0, 384, False),
    (3, 0, 384, True),
    (3, 384, 384, True),
    (3, 768, 384, True),
    (4, 0, 384, False),
    (5, 0, 768, True),
    (6, 0, 768, True),
    (7, 0, 768, True),
    (8, 0, 384, True),
    (8, 384, 384, True),
)
FORWARD_ORDER = (
    (),
    ((0, 0), (0, 1), (0, 2), (0, 3), (0, 4), (0, 5), (0, 6), (0, 7), (0, 8), (0, 9), (1, 0), (0, 10), (0, 11), (0, 12), (0, 13), (1, 1), (2, 0), (1, 2), (2, 1), (1, 3), (3, 0), (2, 2), (1, 4), (4, 0),),
    ((3, 1), (1, 5), (2, 3), (1, 6), (4, 1), (3, 2), (2, 4), (1, 7), (4, 2), (2, 5), (1, 8), (3, 3), (2, 6), (1, 9), (4, 3),),
    ((3, 4), (2, 7),),
    ((3, 5),),
    ((4, 4), (2, 8), (1, 10),),
    ((4, 5), (3, 6), (1, 11), (2, 9),),
    ((1, 12),),
    ((4, 6), (3, 7), (3, 8), (1, 13),),
    ((4, 7), (2, 10),),
    ((4, 8),),
    (),
    (),
    ((2, 11),),
    (),
    ((3, 9), (2, 12),),
    ((2, 13),),
    ((4, 9), (3, 10),),
    (),
    ((3, 11), (3, 12), (3, 13), (4, 10),),
    (),
    ((4, 11),),
    ((4, 12), (4, 13),),
    (),
    (),
    (),
    (),
)


def spot(paired, cc, zz, yy, k):
    return (k, zz, yy, cc) if paired else (cc, zz, yy, k)


def forward_kernel(*refs):
    count, parts = len(UNITS), len(MATRICES)
    raw = refs[:11]
    contact_head = refs[11]
    at = 12
    far = refs[at : at + parts]
    saved_far = refs[at + parts : at + parts + len(SAVED)]
    at += parts + len(SAVED)
    outs = refs[at : at + parts]
    at += parts
    outgoing = refs[at : at + count]
    incoming = refs[at + count : at + 2 * count]
    piece = refs[at + 2 * count : at + 3 * count]
    at += 3 * count
    saved = Saved(*refs[at : at + len(SAVED)])
    at += len(SAVED)
    scratch = Forward(*refs[at : at + len(FORWARD)])
    at += len(FORWARD)
    near = refs[at : at + 11]
    at += 11
    small, small_out, sides, corner = refs[at : at + 4]
    small_send, small_recv, send, recv, local, out_sem, raw_sem = refs[at + 4 :]
    tokens, targets, masked, pairs, labels, table, norms, in_w, out_w, up_w, down_w = near
    z, y, k, c = place()
    me = (z * 4 + y * 2 + k) * 2 + c
    barrier = greet_all()
    raw_copies = [pltpu.make_async_copy(a, b, raw_sem.at[n]) for n, (a, b) in enumerate(zip(raw, near))]
    for item in raw_copies:
        item.start()
    for item in raw_copies[:7]:
        item.wait()
    small[...] = jnp.full(small.shape, -1, jnp.int32)
    for micro in range(2):
        for half in range(2):
            lanes = slice(half * 128, half * 128 + 128)
            row = 2 * micro + half
            small[row : row + 1, :] = jnp.where(
                masked[micro, :, lanes] > 0, MASK_ID, tokens[micro, :, lanes]
            )
            small[4 + row : 5 + row, :] = targets[micro, :, lanes]
        row = 8 + 3 * micro
        for which in range(2):
            small[row + which : row + which + 1, 0:64] = pairs[micro, which : which + 1, :]
        small[row + 2 : row + 3, 0:64] = labels[micro : micro + 1, :]
    sides[...] = jnp.zeros(sides.shape, F32)
    sides[0, :, 0:VOCAB] = table[...]
    corner[...] = jnp.zeros(corner.shape, F32)
    corner[0:8, 0:24] = norms[...]
    sides[1] = corner[...].T[:24]
    def master(u, side):
        matrix, start, n, _ = UNITS[u]
        width = MATRICES[matrix]
        if matrix == 0:
            return sides[side]
        if matrix in (1, 3):
            return in_w[matrix // 2, :, side * 1152 + start : side * 1152 + start + n]
        if matrix in (2, 4):
            rows = out_w[matrix // 2 - 1, :, side * 384 : side * 384 + 384].astype(BF16)
            return nn(rows, order)
        begin = ((matrix - 5) % 2) * 1536 + side * width + start
        return (up_w if matrix < 7 else down_w)[:, begin : begin + n]

    def mine(u):
        return k if UNITS[u][3] else c

    def set_out(u):
        other = jnp.where(mine(u) == 0, master(u, 1), master(u, 0))
        other = jnp.concatenate([other, jnp.zeros((8, UNITS[u][2]), F32)], 0)
        outgoing[u][...] = other.astype(BF16)

    set_out(0)
    pl.semaphore_wait(barrier, 31)

    def small_copy(step):
        other = lax.rem(me + step, 32)
        return remote(
            small, small_out.at[me], small_send.at[step], small_recv.at[step], (other // 2, lax.rem(other, 2))
        )

    def spread(step, carry):
        small_copy(step).start()
        return carry

    across, beside, twin = device(z, y, k, 1 - c), device(z, 1 - y, k, c), device(z, y, 1 - k, c)

    def block(u, cc, zz, yy):
        matrix, start, n, paired = UNITS[u]
        where = spot(paired, cc, zz, yy, k)
        if n == MATRICES[matrix]:
            return outs[matrix].at[where]
        return outs[matrix].at[(*where, slice(None), pl.ds(start, n))]

    def copy(u, at, src, dst, target):
        return remote(src, dst, send.at[u, at], recv.at[u, at], target)

    def pair_copy(u):
        return copy(u, 0, outgoing[u], incoming[u], twin if UNITS[u][3] else across)

    def own_copy(u):
        return pltpu.make_async_copy(piece[u], block(u, c, z, y), local.at[u])

    def line_copy(u, step):
        return copy(u, step, piece[u], block(u, c, z, y), device(lax.rem(z + step, 4), y, k, c))

    def same(u, at, cc, zz, yy, target):
        view = block(u, cc, zz, yy)
        return copy(u, at, view, view, target)

    low, high, every = pl.ds(0, 2), pl.ds(2, 2), slice(None)

    def second(u):
        return [same(u, 4, c, low, y, across), same(u, 5, c, high, y, beside)]

    def third_own(u):
        return [same(u, 6, c, low, y, beside), same(u, 7, c, high, y, across)]

    def third_far(u):
        return [same(u, 8, 1 - c, low, y, beside), same(u, 9, c, high, 1 - y, across)]

    def twin_own(u):
        return [same(u, 10, c, every, y, twin)]

    def twin_second(u):
        return [same(u, 11, 1 - c, low, y, twin), same(u, 12, c, high, 1 - y, twin)]

    def twin_third(u):
        return [
            same(u, 13, c, low, 1 - y, twin),
            same(u, 14, 1 - c, high, y, twin),
            same(u, 15, 1 - c, low, 1 - y, twin),
            same(u, 16, 1 - c, high, 1 - y, twin),
        ]

    pair_copy(0).start()
    for item in raw_copies[7:]:
        item.wait()
    order = feature_order()
    for u in range(1, count):
        set_out(u)
        pair_copy(u).start()
        if u == 3:
            lax.fori_loop(1, 32, spread, 0)
    small_out[me] = small[...]

    def stage_line(u):
        pair_copy(u).wait_recv()
        side = mine(u)
        own = jnp.where(side == 0, master(u, 0), master(u, 1))
        theirs = incoming[u][...].astype(F32)[:24]
        top = jnp.where(side == 0, own, theirs)
        bottom = jnp.where(side == 0, theirs, own)
        piece[u][...] = jnp.concatenate([top, bottom], 0).astype(BF16)
        own_copy(u).start()
        for step in (1, 3, 2):
            line_copy(u, step).start()

    def stage_second(u):
        own_copy(u).wait()
        for step in (1, 3, 2):
            line_copy(u, step).wait_recv()
        for item in second(u) + third_own(u) + twin_own(u):
            item.start()

    def stage_third(u):
        for item in second(u):
            item.wait_recv()
        for item in third_far(u) + twin_second(u):
            item.start()

    def stage_twin(u):
        for item in third_own(u) + third_far(u):
            item.wait_recv()
        for item in twin_third(u):
            item.start()

    def far_copy(matrix):
        return pltpu.make_async_copy(outs[matrix], far[matrix], local.at[count + matrix])

    def stage_end(u):
        for item in twin_own(u) + twin_second(u) + twin_third(u):
            item.wait_recv()
        pair_copy(u).wait_send()
        for step in (1, 2, 3):
            line_copy(u, step).wait_send()
        for item in second(u) + third_own(u) + third_far(u) + twin_own(u) + twin_second(u):
            item.wait_send()
        if u + 1 == count or UNITS[u + 1][0] != UNITS[u][0]:
            far_copy(UNITS[u][0]).start()

    stages = (stage_line, stage_second, stage_third, stage_twin, stage_end)
    pending = list(FORWARD_ORDER)

    def hook():
        for stage, u in pending.pop(0):
            stages[stage](u)

    def ready(number):
        lax.fori_loop(1, 32, finish, 0)

    def out_copy(at):
        return pltpu.make_async_copy(saved[at], saved_far[at], out_sem.at[at])

    def emit(*numbers):
        for number in numbers:
            out_copy(number).start()

    def finish(step, carry):
        small_copy(step).wait()
        return carry

    views = [w.reshape(2, D, n) for w, n in zip(outs, MATRICES)]
    forward_body(small_out, contact_head, views, saved, scratch, ready, hook, emit)
    assert not pending
    for u in range(count):
        for item in twin_third(u):
            item.wait_send()
    for matrix in range(parts):
        far_copy(matrix).wait()
    for at in range(len(SAVED)):
        out_copy(at).wait()


def forward_call(raw, contact_head):
    count, parts = len(UNITS), len(MATRICES)
    anywhere = pl.BlockSpec(memory_space=pl.ANY)
    shapes = [(2, NZ, NY, 2, 48, n) for n in MATRICES]
    widths = [n for _, _, n, _ in UNITS]
    outs = pl.pallas_call(
        forward_kernel,
        out_shape=[jax.ShapeDtypeStruct(shape, BF16) for shape in shapes]
        + [jax.ShapeDtypeStruct(*item) for item in SAVED],
        in_specs=[anywhere] * 11 + [pl.BlockSpec(memory_space=pltpu.SMEM)],
        out_specs=[anywhere] * (parts + len(SAVED)),
        scratch_shapes=[pltpu.VMEM(shape, BF16) for shape in shapes]
        + [pltpu.VMEM((32, n), BF16) for n in widths] * 2
        + [pltpu.VMEM((48, n), BF16) for n in widths]
        + [pltpu.VMEM(*item) for item in SAVED]
        + [pltpu.VMEM(*item) for item in FORWARD]
        + [pltpu.VMEM(item.shape, item.dtype) for item in raw]
        + [
            pltpu.VMEM((16, 128), jnp.int32),
            pltpu.VMEM((32, 16, 128), jnp.int32),
            pltpu.VMEM((2, 24, 128), F32),
            pltpu.VMEM((128, 128), F32),
            pltpu.SemaphoreType.DMA((32,)),
            pltpu.SemaphoreType.DMA((32,)),
            pltpu.SemaphoreType.DMA((count, 17)),
            pltpu.SemaphoreType.DMA((count, 17)),
            pltpu.SemaphoreType.DMA((count + parts,)),
            pltpu.SemaphoreType.DMA((len(SAVED),)),
            pltpu.SemaphoreType.DMA((len(raw),)),
        ],
        compiler_params=pltpu.CompilerParams(
            collective_id=0, has_side_effects=True, vmem_limit_bytes=62 * 2**20
        ),
    )(*raw, contact_head)
    return outs[:parts], Saved(*outs[parts:])


def summed_rows(sums, group):
    return jnp.concatenate([sums[3 * group + third] for third in range(3)], 1).astype(F32)


def table_finish(sums, room, table_ref, norms_ref, proj_t, in_row, g_in, g_emb, g_norm):
    z, y, k, c = place()
    me = ((z * 2 + y) * 2 + c) * 2 + k
    room[0:128, :] = jnp.zeros((128, D), F32)
    for number in range(2):
        room[4 + 16 * number : 20 + 16 * number, :] = summed_rows(sums, number)
        room[68 + 16 * number : 84 + 16 * number, :] = summed_rows(sums, 2 + number)
    pair = room[0:64, :]
    value_grad = room[64:128, :]
    vectors = summed_rows(sums, 6)
    vectors = vectors[:8] + vectors[8:]
    line = iota((8, D), 0)
    table_grad = jnp.concatenate(
        [
            summed_rows(sums, 4),
            summed_rows(sums, 5),
            jnp.where(line == 0, vectors[7:8], 0.0),
            jnp.zeros((24, D), F32),
        ],
        0,
    )
    pair_hi, pair_lo = split_two(pair)
    scale = (HD * ROWS) ** (-0.5)
    query_grad, key_grad = [], []
    for hp in range(PAIRS):
        lanes = slice(hp * 128, hp * 128 + 128)
        query = proj_t[:, lanes]
        key = stacked(proj_t[:, D + hp * 128 : D + hp * 128 + 128])
        high, low = pair_hi[:, lanes], pair_lo[:, lanes]
        query_grad.append((nn(high, key) + nn(low, key)) * scale)
        key_grad.append(unstacked(tn(high, query) + tn(low, query), VP) * scale)
    proj_hi, proj_lo = split_two(jnp.concatenate(query_grad + key_grad + [value_grad], 1))
    normed_grad = jnp.zeros((VP, D), F32)
    for half in range(2):
        lanes = slice(half * 1152, half * 1152 + 1152)
        matrix = in_row[half]
        normed_grad = normed_grad + nt(proj_hi[:, lanes], matrix) + nt(proj_lo[:, lanes], matrix)
    unit, rstd = norm_stats(table_ref[...])
    gain = norms_ref[0:1, :]
    back, scale_0, shift_0 = norm_back(unit, rstd, gain, normed_grad)
    table_grad = table_grad + back
    line = iota((16, D), 0)
    norm_grad = jnp.zeros((16, D), F32)
    rows = [scale_0[None]] + [vectors[n : n + 1] for n in range(3)]
    rows += [shift_0[None]] + [vectors[n : n + 1] for n in range(3, 6)]
    for number, row in enumerate(rows):
        norm_grad = jnp.where(line == number, row, norm_grad)
    shard = D // 32
    pick = one_zero(iota((shard, D), 1) == iota((shard, D), 0) + me * shard).astype(BF16)
    normed = (unit * gain + norms_ref[4:5, :]).astype(BF16)
    mine = nt(pick, normed).astype(BF16)
    in_grad = nn(mine, proj_hi) + nn(mine, proj_lo)
    g_in[...] = in_grad

    def three(values):
        top, rest = split_two(values)
        return top, rest, (values - top.astype(F32) - rest.astype(F32)).astype(BF16)

    emb_grad = sum(nt(pick, part) for part in three(table_grad))
    g_emb[...] = emb_grad
    own_norm = sum(nt(part, pick) for part in three(norm_grad))[:8]
    g_norm[...] = own_norm
    return total_of(in_grad * in_grad) + total_of(emb_grad * emb_grad) + total_of(own_norm * own_norm)


PIECES = 21
GRAD_WIDTHS = (768, 768, 768, 768, 384, 1152, 384)
GRAD_UNITS = (
    (0, 0, 384, True),
    (0, 384, 384, True),
    (1, 0, 768, True),
    (2, 0, 768, True),
    (3, 0, 768, True),
    (4, 0, 384, False),
    (5, 0, 384, True),
    (5, 384, 384, True),
    (5, 768, 384, True),
    (6, 0, 384, False),
)
BACKWARD_ORDER = (
    (),
    (),
    (),
    (),
    (),
    (),
    (),
    ((0, 0),),
    ((0, 1),),
    (),
    (),
    (),
    ((1, 0),),
    (),
    ((0, 2), (1, 1),),
    (),
    ((2, 0),),
    ((0, 3),),
    (),
    (),
    ((3, 0), (1, 2), (0, 4), (2, 1),),
    ((4, 0), (0, 5),),
    (),
    ((3, 1), (1, 3),),
    ((2, 2),),
    ((4, 1),),
    (),
    (),
    ((1, 4),),
    (),
    ((1, 5), (3, 2),),
    ((0, 6), (2, 3),),
    ((0, 7),),
    ((4, 2), (2, 4), (0, 8),),
    ((2, 5),),
    ((1, 6), (0, 9),),
    ((3, 3), (1, 7),),
    ((1, 8), (4, 3),),
    ((3, 4), (2, 6), (1, 9),),
    ((3, 5), (2, 7), (4, 4), (2, 8), (5, 0), (2, 9), (4, 5), (3, 6), (3, 7), (4, 6), (3, 8), (4, 7), (4, 8), (6, 0), (3, 9), (4, 9),),
)


class Kept(typing.NamedTuple):
    stream: typing.Any
    norms: typing.Any
    table: typing.Any
    proj_t: typing.Any
    extras: typing.Any
    moved: typing.Any
    grad_head: typing.Any
    touch: typing.Any
    value_two: typing.Any


class Early(typing.NamedTuple):
    slope: typing.Any
    active: typing.Any
    feed_normed_t: typing.Any
    unit_2: typing.Any
    rstd_2: typing.Any
    col_mixed_t: typing.Any
    col_proj: typing.Any
    col_prob: typing.Any
    col_normed_t: typing.Any
    unit_1: typing.Any
    rstd_1: typing.Any


class Late(typing.NamedTuple):
    row_mixed_t: typing.Any
    hot_all: typing.Any
    weight_hi: typing.Any
    prob: typing.Any
    hot_ri: typing.Any
    hot_ir: typing.Any


def pick_items(group, source):
    return [getattr(source, name) for name in group._fields]


def backward_kernel(*refs):
    widths = GRAD_WIDTHS
    count = len(widths)
    contact_head = refs[0]
    far = refs[1 : 1 + count]
    in_row_far = refs[1 + count]
    saved = Saved(*refs[2 + count : 2 + count + len(SAVED)])
    at = 2 + count + len(SAVED)
    outs = refs[at : at + count]
    g_in, g_emb, g_norm, stats = refs[at + count : at + count + 4]
    at += count + 4
    grads = refs[at : at + count]
    kept = Kept(*refs[at + count : at + count + len(Kept._fields)])
    at += count + len(Kept._fields)
    upstream, branch, branch_t, mixed = refs[at : at + 4]
    scratch = refs[at + 4 :]
    units = len(GRAD_UNITS)
    got_0, got_1a, got_1b, got_2a, got_2b, got_3, total, got_4 = (
        scratch[i * units : (i + 1) * units] for i in range(8)
    )
    table, table_out, table_got, square, square_got = scratch[8 * units : 8 * units + 5]
    table_send, table_recv, send, recv, local = scratch[8 * units + 5 :]
    z, y, k, c = place()
    me = (z * 4 + y * 2 + k) * 2 + c
    across, beside, twin = device(z, y, k, 1 - c), device(z, 1 - y, k, c), device(z, y, 1 - k, c)
    barrier = greet_all()
    stream = kept.stream
    square[...] = jnp.zeros(square.shape, F32)

    copies = {}

    def load(number, source, target):
        copies[number] = pltpu.make_async_copy(source, target, local.at[number])
        copies[number].start()

    def need(*numbers):
        for number in numbers:
            copies[number].wait()

    def weight(m):
        return len(SAVED) + m

    def copy(m, at, src, dst, target):
        return remote(src, dst, send.at[m, at], recv.at[m, at], target)

    low, high = pl.ds(0, 2), pl.ds(2, 2)
    every = slice(None)

    def where(u, cc, zz, yy):
        matrix, start, n, paired = GRAD_UNITS[u]
        index = spot(paired, cc, zz, yy, k)
        return index if n == widths[matrix] else (*index, every, pl.ds(start, n))

    def block(u, cc, zz, yy):
        return grads[GRAD_UNITS[u][0]].at[where(u, cc, zz, yy)]

    def ordered(u, cc, rest):
        return (*rest, cc) if GRAD_UNITS[u][3] else (cc, *rest)

    def twin_copy(u):
        matrix, start, n, paired = GRAD_UNITS[u]
        index = (1 - k,) if paired else (every, every, every, 1 - k)
        if n != widths[matrix]:
            index = (*index, *(every,) * (5 - len(index)), pl.ds(start, n))
        return copy(u, 0, grads[matrix].at[index], got_0[u], twin)

    def first(u):
        return [
            copy(u, 1, block(u, every, low, 1 - y), got_1a[u], beside),
            copy(u, 2, block(u, 1 - c, high, every), got_1b[u], across),
        ]

    def second(u):
        return [
            copy(u, 3, block(u, 1 - c, low, y), got_2a[u], across),
            copy(u, 4, block(u, c, high, 1 - y), got_2b[u], beside),
        ]

    def along(u):
        return [
            copy(
                u,
                4 + step,
                block(u, c, lax.rem(z + step, 4), y),
                got_3[u].at[step - 1],
                device(lax.rem(z + step, 4), y, k, c),
            )
            for step in (1, 3, 2)
        ]

    def mine(u):
        return k if GRAD_UNITS[u][3] else c

    def pair(u):
        return [copy(u, 8, total[u].at[1 - mine(u)], got_4[u], twin if GRAD_UNITS[u][3] else across)]

    def peer(step):
        return lax.rem(me + step, 32)

    def source(step):
        return lax.rem(me + 32 - step, 32)

    def table_copy(step, back, index):
        target = (peer(step) // 2, lax.rem(peer(step), 2))
        if back:
            return remote(
                table_out.at[index], table_out.at[index], table_send.at[1, step], table_recv.at[1, step], target
            )
        return remote(
            table.at[index], table_got.at[me], table_send.at[0, step], table_recv.at[0, step], target
        )

    def table_start(step):
        @pl.when(peer(step) < PIECES)
        def _():
            table_copy(step, False, peer(step)).start()

    def table_wait_send(step):
        @pl.when(peer(step) < PIECES)
        def _():
            table_copy(step, False, 0).wait_send()

        @pl.when(me < PIECES)
        def _():
            table_copy(step, True, 0).wait_send()

    def table_wait_back(step):
        @pl.when(source(step) < PIECES)
        def _():
            table_copy(step, True, 0).wait_recv()

    def each(action):
        def body(step, carry):
            action(step)
            return carry

        lax.fori_loop(1, 32, body, 0)

    def gather_into(u, cc, zz, yy, *others):
        matrix = GRAD_UNITS[u][0]
        index = where(u, cc, zz, yy)
        value = grads[matrix][index].astype(F32) + got_0[u][ordered(u, cc, (zz, yy))].astype(F32)
        for other in others:
            value = value + other.astype(F32)
        grads[matrix][index] = value.astype(BF16)

    def stage_first(u):
        twin_copy(u).wait_recv()
        for a in range(2):
            for b in range(2):
                gather_into(u, a, b, 1 - y)
                gather_into(u, 1 - c, 2 + a, b)
        for item in first(u):
            item.start()

    def from_beside(u, cc, a):
        return got_1a[u][ordered(u, cc, (a,))]

    def stage_second(u):
        for item in first(u):
            item.wait_recv()
        for a in range(2):
            gather_into(u, 1 - c, a, y, from_beside(u, 1 - c, a))
            gather_into(u, c, 2 + a, 1 - y, got_1b[u][a, 1 - y])
        for item in second(u):
            item.start()

    def stage_along(u):
        for item in second(u):
            item.wait_recv()
        for a in range(2):
            gather_into(u, c, a, y, from_beside(u, c, a), got_2a[u][a])
            gather_into(u, c, 2 + a, y, got_1b[u][a, y], got_2b[u][a])
        for item in along(u):
            item.start()

    def stage_pair(u):
        for item in along(u):
            item.wait_recv()
        full = grads[GRAD_UNITS[u][0]][where(u, c, z, y)].astype(F32)
        for step in range(3):
            full = full + got_3[u][step].astype(F32)
        total[u][0] = full[:24]
        total[u][1] = full[24:]
        for item in pair(u):
            item.start()

    def stage_end(u):
        matrix, start, n, _ = GRAD_UNITS[u]
        lanes = slice(start, start + n)
        side = mine(u)
        outs[matrix][side, :, lanes] = total[u][side]
        for item in pair(u):
            item.wait_recv()
        outs[matrix][1 - side, :, lanes] = got_4[u][...]
        own, other = total[u][side], got_4[u][...]
        square[...] += jnp.broadcast_to(total_of(own * own) + total_of(other * other), (8, 128))
        for item in [twin_copy(u)] + first(u) + second(u) + along(u):
            item.wait_send()

    def table_sum(u):
        @pl.when(me < PIECES)
        def _():
            each(lambda step: table_copy(step, False, 0).wait_recv())
            table_got[me] = table[me]

            def add(at, held):
                return held + table_got[at].astype(F32)

            total_rows = lax.fori_loop(1, 32, add, table_got[0].astype(F32))
            top, rest = split_two(total_rows[:8] + total_rows[8:])
            exact = jnp.concatenate([top.astype(F32), rest.astype(F32)], 0)
            table_out[me] = jnp.where(me >= 18, exact, total_rows).astype(BF16)
            each(lambda step: table_copy(step, True, me).start())

    late_parts = []

    def table_end(u):
        each(table_wait_back)
        need(weight(count))
        found = table_finish(
            table_out, upstream, kept.table, kept.norms, kept.proj_t, late_parts[0].reshape(2, D, 1152), g_in, g_emb, g_norm
        )
        square[...] += jnp.broadcast_to(found, (8, 128))

    stages = (stage_first, stage_second, stage_along, stage_pair, stage_end, table_sum, table_end)
    pending = list(BACKWARD_ORDER)

    def hook():
        for stage, u in pending.pop(0):
            stages[stage](u)

    def done(u):
        if u == 0:
            pl.semaphore_wait(barrier, 31)
        twin_copy(u).start()
        hook()

    names = Kept._fields
    for name in names:
        load(getattr(AT, name), getattr(saved, name), getattr(kept, name))

    load(AT.branch, saved.branch, branch)

    def phase_one(*early_refs):
        e = Early(*early_refs)
        load(weight(0), far[0], grads[0])
        load(AT.slope, saved.slope, e.slope)
        load(AT.active, saved.active, e.active)
        for m in (1, 2, 3):
            load(weight(m), far[m], grads[m])
        for name in Early._fields[2:6]:
            load(getattr(AT, name), getattr(saved, name), getattr(e, name))
        load(weight(4), far[4], grads[4])
        for name in Early._fields[6:8]:
            load(getattr(AT, name), getattr(saved, name), getattr(e, name))
        load(weight(5), far[5], grads[5])
        for name in Early._fields[8:]:
            load(getattr(AT, name), getattr(saved, name), getattr(e, name))
        load(weight(6), far[6], grads[6])
        view = [g.reshape(2, D, n) for g, n in zip(grads, widths)]
        need(*(getattr(AT, name) for name in names))
        norms = kept.norms[...]

        def gain(number):
            return norms[number : number + 1, :]

        need(AT.branch)
        transpose_into(branch, branch_t)
        hook()

        def grad_tile(m, start, left_t, right, half, at):
            lanes = slice(start + half * widths[m] + at, start + half * widths[m] + at + 384)
            view[m][half, :, at : at + 384] = nn(left_t[...], right[:, lanes]).astype(BF16)

        def grad_half(m, start, left_t, right, half):
            for at in range(0, widths[m], 384):
                grad_tile(m, start, left_t, right, half, at)

        for part in range(2):
            need(weight(part))
            if part == 0:
                need(AT.slope)

            def down_back(half, at, part=part):
                lanes = slice(part * 1536 + half * 768 + at, part * 1536 + half * 768 + at + 384)
                back = nn(branch[...], view[part][half, :, at : at + 384])
                e.slope[:, lanes] = (back * e.slope[:, lanes].astype(F32)).astype(BF16)

            if part == 0:
                for at in (0, 384):
                    for half in range(2):
                        down_back(half, at)
                    hook()
                    if at == 0:
                        need(AT.active)
                    for half in range(2):
                        grad_tile(part, 0, branch_t, e.active, half, at)
                    done(at // 384)
            else:
                for half in range(2):
                    for at in (0, 384):
                        down_back(half, at)
                    hook()
                grad_half(part, part * 1536, branch_t, e.active, 0)
                hook()
                grad_half(part, part * 1536, branch_t, e.active, 1)
                done(2)
        for part in range(2):
            need(weight(2 + part))
            for half in range(2):
                start = part * 1536 + half * 768
                back = nt(e.slope[:, start : start + 768], view[2 + part][half])
                upstream[...] = back if start == 0 else upstream[...] + back
                hook()
            if part == 0:
                need(AT.feed_normed_t)
            grad_half(2 + part, part * 1536, e.feed_normed_t, e.slope, 0)
            hook()
            grad_half(2 + part, part * 1536, e.feed_normed_t, e.slope, 1)
            done(3 + part)
        need(AT.unit_2, AT.rstd_2)
        scale_2, shift_2 = back_rows(e.unit_2, e.rstd_2, gain(2), upstream, stream, branch, False)
        hook()
        need(weight(4), AT.col_mixed_t)
        mixed[...] = (nt(branch[:, :384], view[4][0]) + nt(branch[:, 384:], view[4][1])).astype(BF16)
        hook()
        for half in range(2):
            grad_half(4, 0, e.col_mixed_t, branch, half)
        done(5)
        need(AT.col_proj, AT.col_prob)
        proj = e.active

        def attend(at, carry):
            rows = pl.ds(pl.multiple_of((at // PAIRS) * 128, 128), 128)
            lane = lax.rem(at, PAIRS) * 128

            def lanes(part):
                return pl.ds(pl.multiple_of(part * D + lane, 128), 128)

            query = stacked(e.col_proj[rows, lanes(0)])
            key = e.col_proj[rows, lanes(1)]
            value = e.col_proj[rows, lanes(2)]
            above = stacked(mixed[rows, lanes(0)])
            prob = e.col_prob[at]
            grad = nt(above, value)
            grad = prob * (grad - jnp.sum(prob * grad, -1, keepdims=True))
            small = grad.astype(BF16)
            scale = HD ** (-0.5)
            proj[rows, lanes(0)] = (unstacked(nn(small, key), 128) * scale).astype(BF16)
            proj[rows, lanes(1)] = (tn(small, query) * scale).astype(BF16)
            proj[rows, lanes(2)] = tn(prob.astype(BF16), above).astype(BF16)
            return carry

        for part in range(6):
            lax.fori_loop(4 * part, 4 * part + 4, attend, 0, unroll=4)
            hook()
        need(weight(5))
        for half in range(2):
            back = nt(proj[:, half * 1152 : half * 1152 + 1152], view[5][half])
            upstream[...] = back if half == 0 else upstream[...] + back
            hook()
        need(AT.col_normed_t)
        for third in range(3):
            for half in range(2):
                grad_tile(5, 0, e.col_normed_t, proj, half, third * 384)
            done(6 + third)
        need(AT.unit_1, AT.rstd_1)
        scale_1, shift_1 = back_rows(e.unit_1, e.rstd_1, gain(1), upstream, stream, branch, False)
        hook()
        need(weight(6))
        mixed[...] = (nt(branch[:, :384], view[6][0]) + nt(branch[:, 384:], view[6][1])).astype(BF16)
        line = iota((8, D), 0)
        vectors = jnp.zeros((8, D), F32)
        moved = kept.moved[...]
        rows = (scale_1, scale_2, moved[0:1], shift_1, shift_2, moved[1:2])
        for number, row in enumerate(rows):
            vectors = jnp.where(line == number, row, vectors)
        extras = jnp.concatenate([kept.extras[0:1, :], jnp.zeros((1, D - 128), F32)], 1)
        kept.moved[...] = jnp.where(line == 6, extras, vectors)
        hook()

    pl.run_scoped(phase_one, *(pltpu.VMEM(*item) for item in pick_items(Early, SAVED)))

    def phase_two(*late_refs):
        e = Late(*late_refs[:-3])
        in_row, left_hi, left_lo = late_refs[-3:]
        for name in Late._fields:
            load(getattr(AT, name), getattr(saved, name), getattr(e, name))
        load(weight(count), in_row_far, in_row)
        view = grads[6].reshape(2, D, widths[6])
        late_parts.append(in_row)
        need(AT.row_mixed_t)
        for half in range(2):
            lanes = slice(half * 384, half * 384 + 384)
            view[half] = nn(e.row_mixed_t[...], branch[:, lanes]).astype(BF16)
        done(9)
        need(AT.hot_all, AT.weight_hi, AT.prob, AT.hot_ri, AT.hot_ir)
        shape = (HERE, HERE)
        back = (
            ((iota(shape, 1) >> 4) == (iota(shape, 0) & 31))
            & ((iota(shape, 1) & 15) == (iota(shape, 0) >> 5))
        )
        mixed[...] = nn(one_zero(back).astype(BF16), mixed[...]).astype(BF16)
        value_rows = []
        for hp in range(PAIRS):
            lanes = slice(hp * 128, hp * 128 + 128)
            part = mixed[:, lanes]
            upstream[:, lanes] = nt(part, kept.value_two[hp])
            value_rows.append(unstacked(tn(e.weight_hi[:, lanes], part), 64))
        hook()
        split_heads_to(upstream, left_hi, left_lo)
        hook()
        hot_all = e.hot_all[...]
        grad = nn(left_hi[...], hot_all) + nn(left_lo[...], hot_all)
        extra = jnp.concatenate(
            [kept.touch[...] * (contact_head[h] * COLS) for h in range(HEADS)], 0
        )
        grad = grad + extra
        prob = e.prob[...]
        grad = prob * (grad - jnp.sum(prob * grad, -1, keepdims=True))
        low_grad = grad.astype(BF16)
        hook()
        merge_heads(low_grad, e.hot_all, branch, None)
        hook()
        table_pair = nn(e.hot_ri[...], branch[...])
        stream_hi, stream_lo = split_two(stream[...])
        hot_ir = e.hot_ir[...]
        table_grad = kept.grad_head[...] + nn(hot_ir, stream_hi) + nn(hot_ir, stream_lo)
        value_grad = jnp.concatenate(value_rows, 1)
        last = jnp.where(iota((8, D), 0) == 7, table_grad[32:33], kept.moved[...])
        top, rest = split_two(last)
        groups = [table_pair[4:20], table_pair[20:36], value_grad[4:20], value_grad[20:36]]
        groups += [table_grad[0:16], table_grad[16:32]]
        groups += [jnp.concatenate([top.astype(F32), rest.astype(F32)], 0)]
        for number, group in enumerate(groups):
            for third in range(3):
                table[3 * number + third] = group[:, third * 256 : third * 256 + 256].astype(BF16)
        each(table_start)
        hook()
        hook()

    pl.run_scoped(
        phase_two,
        *(pltpu.VMEM(*item) for item in pick_items(Late, SAVED)),
        pltpu.VMEM((2, NZ, NY, 2, 48, 1152), BF16),
        pltpu.VMEM((HEADS * WIDE, ROWS * VP), BF16),
        pltpu.VMEM((HEADS * WIDE, ROWS * VP), BF16),
    )
    assert not pending

    def square_copy(step):
        other = lax.rem(me + step, 32)
        return remote(
            square, square_got.at[me], table_send.at[2, step], table_recv.at[2, step], (other // 2, lax.rem(other, 2))
        )

    each(lambda step: square_copy(step).start())
    square_got[me] = square[...]
    each(lambda step: table_wait_send(step))
    for u in range(units):
        for item in pair(u):
            item.wait_send()
    each(lambda step: square_copy(step).wait())
    total_square = lax.fori_loop(1, 32, lambda at, held: held + square_got[at], square_got[0])[0:1]
    vector = table_out[18].astype(F32)
    vector = vector[6:7, :128] + vector[14:15, :128]
    counted = kept.extras[1:2, :]
    column = iota((1, 128), 1)
    contact = jnp.where(column <= HEADS, vector, 0.0)
    total_square = total_square + total_of(contact * contact)
    grad_norm = jnp.sqrt(total_square)
    factor = jnp.minimum(1.0, MAX_NORM / grad_norm)
    losses = (
        (0, vector[:, HEADS + 1 : HEADS + 2]),
        (1, counted[:, 0:1]),
        (2, vector[:, HEADS + 2 : HEADS + 3]),
        (3, counted[:, 1:2]),
    )
    loss_row = jnp.zeros((1, 128), F32)
    for at, value in losses:
        loss_row = jnp.where(column == at, value, loss_row)
    number = iota((8, 128), 0)
    result = jnp.zeros((8, 128), F32)
    for at, row in enumerate((contact, counted, factor, grad_norm, loss_row)):
        result = jnp.where(number == at, row, result)
    stats[...] = result


def backward_call(contact_head, weights, in_row, saved):
    widths = GRAD_WIDTHS
    count = len(widths)
    inside = pl.BlockSpec(memory_space=pltpu.VMEM)
    anywhere = pl.BlockSpec(memory_space=pl.ANY)

    units = len(GRAD_UNITS)

    def shapes(lead, dtype):
        return [pltpu.VMEM((*lead, n), dtype) for _, _, n, _ in GRAD_UNITS]

    outs = pl.pallas_call(
        backward_kernel,
        out_shape=[jax.ShapeDtypeStruct((2, 24, n), F32) for n in widths]
        + [
            jax.ShapeDtypeStruct((24, 3 * D), F32),
            jax.ShapeDtypeStruct((24, VP), F32),
            jax.ShapeDtypeStruct((8, 24), F32),
            jax.ShapeDtypeStruct((8, 128), F32),
        ],
        in_specs=[pl.BlockSpec(memory_space=pltpu.SMEM)] + [anywhere] * (1 + count + len(SAVED)),
        out_specs=[inside] * (4 + count),
        scratch_shapes=[pltpu.VMEM((2, NZ, NY, 2, 48, n), BF16) for n in widths]
        + [pltpu.VMEM(*item) for item in pick_items(Kept, SAVED)]
        + [
            pltpu.VMEM((HERE, D), F32),
            pltpu.VMEM((HERE, D), BF16),
            pltpu.VMEM((D, HERE), BF16),
            pltpu.VMEM((HERE, D), BF16),
        ]
        + [
            pltpu.VMEM((NZ, NY, 2, 48, n) if paired else (2, NZ, NY, 48, n), BF16)
            for _, _, n, paired in GRAD_UNITS
        ]
        + shapes((2, 2, 48), BF16)
        + shapes((2, 2, 48), BF16)
        + shapes((2, 48), BF16)
        + shapes((2, 48), BF16)
        + shapes((3, 48), BF16)
        + shapes((2, 24), F32)
        + shapes((24,), F32)
        + [
            pltpu.VMEM((PIECES, 16, 256), BF16),
            pltpu.VMEM((PIECES, 16, 256), BF16),
            pltpu.VMEM((32, 16, 256), BF16),
            pltpu.VMEM((8, 128), F32),
            pltpu.VMEM((32, 8, 128), F32),
            pltpu.SemaphoreType.DMA((3, 32)),
            pltpu.SemaphoreType.DMA((3, 32)),
            pltpu.SemaphoreType.DMA((units, 9)),
            pltpu.SemaphoreType.DMA((units, 9)),
            pltpu.SemaphoreType.DMA((len(SAVED) + count + 1,)),
        ],
        compiler_params=pltpu.CompilerParams(
            collective_id=1, has_side_effects=True, vmem_limit_bytes=63 * 2**20
        ),
    )(contact_head, *weights, in_row, *saved)
    return outs[:count], outs[count:]


UPDATE_RATES = (LEARN_RATE,) * 4 + (VECTOR_RATE,) * 3


def update_kernel(*refs):
    given, far, held, results = refs[:32], refs[32:60], refs[60:92], refs[92:120]
    sems, out_sems = refs[120:122]
    outs, copies = results[:21], results[21:26]
    loss_ref, norm_ref = results[26:]

    def leave(*numbers):
        for n in numbers:
            pltpu.make_async_copy(results[n], far[n], out_sems.at[n]).start()

    moves = [pltpu.make_async_copy(a, b, sems.at[n]) for n, (a, b) in enumerate(zip(given, held))]
    for item in moves:
        item.start()
    reduced, g_in, g_emb, g_norm, stats = held[:7], held[7], held[8], held[9], held[10]
    states = [held[11 + 3 * n : 14 + 3 * n] for n in range(7)]
    outs = [outs[3 * n : 3 * n + 3] for n in range(7)]
    order = feature_order()
    for item in moves[4:11]:
        item.wait()
    factor = stats[2:3, 0:1]
    loss_ref[...] = stats[4:5, 0:4]
    norm_ref[...] = stats[3:4, 0:1]

    def natural(values):
        top, rest = split_two(values)
        last = (values - top.astype(F32) - rest.astype(F32)).astype(BF16)
        return nt(top, order) + nt(rest, order) + nt(last, order)

    def update(number, where, grad):
        master, first, second = (ref[where] for ref in states[number])
        new, first, second = adam_update(master, first, second, grad * factor, UPDATE_RATES[number])
        for ref, value in zip(outs[number], (new, first, second)):
            ref[where] = value
        if number < 5:
            copies[number][where] = new.astype(BF16)

    every = slice(None)
    g_out_col, g_in_col, g_out_row = reduced[4:]
    for item in moves[11:17]:
        item.wait()
    for half in range(2):
        lanes = slice(half * 1152, half * 1152 + 1152)
        update(0, (0, every, lanes), g_in[:, lanes])
        update(0, (1, every, lanes), g_in_col[half])
        lanes = slice(half * 384, half * 384 + 384)
        update(1, (0, every, lanes), natural(g_out_row[half]))
        update(1, (1, every, lanes), natural(g_out_col[half]))
    leave(0, 1, 2, 21, 3, 4, 5, 22, 26, 27)
    for item in moves[:4] + moves[17:]:
        item.wait()
    for half in range(2):
        for part in range(2):
            start = part * 1536 + half * 768
            lanes = slice(start, start + 768)
            update(2, (every, lanes), reduced[2 + part][half])
            update(3, (every, lanes), reduced[part][half])
    leave(6, 7, 8, 23, 9, 10, 11, 24)
    update(4, (every, every), g_emb[:, :VOCAB])
    update(5, (every, every), g_norm[...])
    update(6, (every, every), stats[0:1, : HEADS + 1])
    leave(12, 13, 14, 25, 15, 16, 17, 18, 19, 20)
    for n in range(28):
        pltpu.make_async_copy(results[n], far[n], out_sems.at[n]).wait()


def update_call(reduced, g_in, g_emb, g_norm, stats, states):
    anywhere = pl.BlockSpec(memory_space=pl.ANY)
    flat = [item for state in states for item in state]
    shapes = [jax.ShapeDtypeStruct(item.shape, F32) for item in flat]
    shapes += [jax.ShapeDtypeStruct(states[n][0].shape, BF16) for n in range(5)]
    shapes += [jax.ShapeDtypeStruct((1, 4), F32), jax.ShapeDtypeStruct((1, 1), F32)]
    given = (*reduced, g_in, g_emb, g_norm, stats, *flat)
    return pl.pallas_call(
        update_kernel,
        out_shape=shapes,
        in_specs=[anywhere] * len(given),
        out_specs=[anywhere] * len(shapes),
        scratch_shapes=[pltpu.VMEM(item.shape, F32) for item in given]
        + [pltpu.VMEM(item.shape, item.dtype) for item in shapes]
        + [
            pltpu.SemaphoreType.DMA((len(given),)),
            pltpu.SemaphoreType.DMA((len(shapes),)),
            pltpu.VMEM((44, 512, 512), F32),
        ],
        compiler_params=pltpu.CompilerParams(vmem_limit_bytes=62 * 2**20),
    )(*given)


def adam_update(master, first, second, grad_part, rate):
    first = BETA_ONE * first + (1.0 - BETA_ONE) * grad_part
    second = BETA_TWO * second + (1.0 - BETA_TWO) * grad_part * grad_part
    moved = first / (1.0 - BETA_ONE**STEP) / (jnp.sqrt(second / (1.0 - BETA_TWO**STEP)) + ADAM_EPS)
    return (master - rate * (moved + WEIGHT_DECAY * master), first, second)


def shards(
    tokens,
    targets,
    masked,
    contact_pairs,
    labels,
    attention_in_master,
    attention_in_first,
    attention_in_second,
    attention_out_master,
    attention_out_first,
    attention_out_second,
    feed_up_master,
    feed_up_first,
    feed_up_second,
    feed_down_master,
    feed_down_first,
    feed_down_second,
    embedding_master,
    embedding_first,
    embedding_second,
    norm_params_master,
    norm_params_first,
    norm_params_second,
    contact_head_master,
    contact_head_first,
    contact_head_second,
):
    both = ("seq", "col")
    micro, rows_here, cols_here = tokens.shape
    ncol = lax.axis_size("col")
    ndev = lax.axis_size("seq") * ncol
    cols = cols_here * ncol
    me = lax.axis_index("seq") * ncol + lax.axis_index("col")
    per = ndev // micro
    cw = cols // per
    mine = me // per
    base = (me % per) * cw
    shard = D // ndev

    tiled = lax.axis_size("seq") == 16 and ncol == 2
    if tiled:
        raw = (
            tokens,
            targets,
            masked,
            contact_pairs.transpose(0, 2, 1),
            labels,
            embedding_master.T,
            norm_params_master,
            attention_in_master,
            attention_out_master,
            feed_up_master,
            feed_down_master.T,
        )
        weights, saved = forward_call(raw, contact_head_master)
        reduced, (g_in, g_emb, g_norm, stats) = backward_call(
            contact_head_master, [weights[n] for n in (7, 8, 5, 6, 4, 3, 2)], weights[1], saved
        )
        states = (
            (attention_in_master, attention_in_first, attention_in_second),
            (attention_out_master, attention_out_first, attention_out_second),
            (feed_up_master, feed_up_first, feed_up_second),
            (feed_down_master.T, feed_down_first.T, feed_down_second.T),
            (embedding_master.T, embedding_first.T, embedding_second.T),
            (norm_params_master, norm_params_first, norm_params_second),
            (contact_head_master[None], contact_head_first[None], contact_head_second[None]),
        )
        outs = update_call(reduced, g_in, g_emb, g_norm, stats, states)
        return (
            *outs[:9],
            *(item.T for item in outs[9:15]),
            *outs[15:18],
            *(item[0] for item in outs[18:21]),
            *outs[21:24],
            *(item.T for item in outs[24:26]),
            outs[26][0],
            outs[27][0, 0],
        )
    inputs = jnp.where(masked > 0, MASK_ID, tokens)
    masters = [
        jnp.concatenate(
            [
                jnp.pad(embedding_master.T, ((0, 0), (0, 128 - VOCAB))),
                jnp.pad(norm_params_master.T, ((0, 0), (0, 120))),
            ],
            1,
        ),
        attention_in_master[0],
        attention_out_master[0],
        attention_in_master[1],
        attention_out_master[1],
        feed_up_master,
        feed_down_master.T,
    ]
    whole = jnp.stack([inputs, targets])
    whole = lax.all_gather(lax.all_gather(whole, "col", axis=3, tiled=True), "seq", axis=2, tiled=True)
    pairs_all = lax.all_gather(
        jnp.concatenate([contact_pairs, labels[:, :, None]], -1), both, axis=1, tiled=True
    )
    gathered = []
    for master in masters:
        full = lax.all_gather(master.astype(BF16), both, axis=0, tiled=True)
        gathered.append(full.reshape(D, 2, -1).transpose(1, 0, 2))
    counts = (
        jnp.sum(whole[0] == MASK_ID).astype(F32),
        jnp.sum(pairs_all[..., 2] >= 0).astype(F32),
    )
    ids_all = lax.dynamic_index_in_dim(whole[0], mine, 0, False)
    ids_local = lax.dynamic_slice_in_dim(ids_all, base, cw, 1)
    targets_local = lax.dynamic_slice_in_dim(
        lax.dynamic_index_in_dim(whole[1], mine, 0, False), base, cw, 1
    )
    pairs = lax.dynamic_index_in_dim(pairs_all, mine, 0, False)

    table = gathered[0][0][:, :VP].T
    norms = gathered[0][1][:, :8].T.astype(F32)
    in_row, out_row, in_col, out_col, up_w, down_t = (
        jnp.concatenate([g[0], g[1]], 1) for g in gathered[1:]
    )
    big = (in_row, in_col, out_row, out_col, up_w, down_t)

    grads, tables, contact_total, mlm_total, bce_total, kept = step(
        big,
        table,
        norms,
        contact_head_master,
        ids_all,
        ids_local.reshape(-1),
        ids_local.T.reshape(-1),
        targets_local.T.reshape(-1),
        pairs[:, 0] - base,
        pairs[:, 1],
        pairs[:, 2],
        counts,
        cw,
    )
    table_pair, value_grad, table_grad, vectors = tables
    extras = jnp.zeros((2, D), F32).at[0, : HEADS + 3].set(
        jnp.concatenate([contact_total, mlm_total[None], bce_total[None]])
    )
    sums = jnp.concatenate([table_pair[:40], value_grad[:40], table_grad[:40], vectors, extras])
    flat_grad = jnp.concatenate([g.astype(BF16) for g in grads], 1)
    reduced = lax.psum_scatter(flat_grad, both, scatter_dimension=0, tiled=True).astype(F32)
    g_in_col, g_out_row, g_out_col, g_up, g_down = jnp.split(
        reduced, [3 * D, 4 * D, 5 * D, 5 * D + FF], 1
    )
    sums = lax.psum(sums, both)
    unit_t, rstd_t, normed_t, query_t, key_t = kept
    rows_all = ids_all.shape[0]
    spare = ((0, VP - 40), (0, 0))
    table_pair, value_grad, table_grad = (
        jnp.pad(sums[a : a + 40], spare) for a in (0, 40, 80)
    )
    vectors = sums[120:126]
    contact_grad, mlm_total, bce_total = (
        sums[126, : HEADS + 1], sums[126, HEADS + 1], sums[126, HEADS + 2]
    )
    row_scale = (HD * rows_all) ** (-0.5)
    query_grad = []
    key_grad = []
    for h in range(HEADS):
        pair = heads_of(table_pair, h)
        query_grad.append(jnp.dot(pair, heads_of(key_t, h).astype(F32), precision=PRECISE))
        key_grad.append(jnp.dot(pair.T, heads_of(query_t, h).astype(F32), precision=PRECISE))
    proj_grad = jnp.concatenate(
        [
            jnp.concatenate(query_grad, 1) * row_scale,
            jnp.concatenate(key_grad, 1) * row_scale,
            value_grad,
        ],
        1,
    )
    proj_hi, proj_lo = split_two(proj_grad)
    normed_grad = nt(proj_hi, in_row) + nt(proj_lo, in_row)
    back_t, scale_0, shift_0 = norm_back(unit_t, rstd_t, norms[0], normed_grad)
    table_grad = table_grad + back_t
    low = me * shard
    normed_mine = lax.dynamic_slice_in_dim(normed_t, low, shard, 1)
    grad_in_row = tn(normed_mine, proj_hi) + tn(normed_mine, proj_lo)
    norm_grad = jnp.concatenate([scale_0[None], vectors[:3], shift_0[None], vectors[3:]])
    table_mine = lax.dynamic_slice_in_dim(table_grad[:VOCAB], low, shard, 1)
    norm_mine = lax.dynamic_slice_in_dim(norm_grad, low, shard, 1)
    reduced_all = (g_in_col, g_out_row, g_out_col, g_up, g_down)

    local_square = (
        sum(jnp.sum(g * g) for g in reduced_all)
        + jnp.sum(grad_in_row * grad_in_row)
        + jnp.sum(table_mine * table_mine)
        + jnp.sum(norm_mine * norm_mine)
    )
    square = lax.psum(local_square, both) + jnp.sum(contact_grad * contact_grad)
    grad_norm = jnp.sqrt(square)
    factor = jnp.minimum(1.0, MAX_NORM / grad_norm)
    in_new, in_moment, in_square = adam_update(
        attention_in_master, attention_in_first, attention_in_second, jnp.stack([grad_in_row, g_in_col]) * factor, LEARN_RATE
    )
    out_new, out_moment, out_square = adam_update(
        attention_out_master, attention_out_first, attention_out_second, jnp.stack([g_out_row, g_out_col]) * factor, LEARN_RATE
    )
    up_new, up_moment, up_square = adam_update(
        feed_up_master, feed_up_first, feed_up_second, g_up * factor, LEARN_RATE
    )
    down_new, down_moment, down_square = adam_update(
        feed_down_master, feed_down_first, feed_down_second, g_down.T * factor, LEARN_RATE
    )
    table_new, table_moment, table_square = adam_update(
        embedding_master, embedding_first, embedding_second, table_mine * factor, VECTOR_RATE
    )
    norm_new, norm_moment, norm_square = adam_update(
        norm_params_master, norm_params_first, norm_params_second, norm_mine * factor, VECTOR_RATE
    )
    head_new, head_moment, head_square = adam_update(
        contact_head_master, contact_head_first, contact_head_second, contact_grad * factor, VECTOR_RATE
    )
    loss_parts = jnp.stack([mlm_total, counts[0], bce_total, counts[1]])
    return (
        in_new, in_moment, in_square,
        out_new, out_moment, out_square,
        up_new, up_moment, up_square,
        down_new, down_moment, down_square,
        table_new, table_moment, table_square,
        norm_new, norm_moment, norm_square,
        head_new, head_moment, head_square,
        in_new.astype(BF16), out_new.astype(BF16), up_new.astype(BF16), down_new.astype(BF16), table_new.astype(BF16),
        loss_parts, grad_norm,
    )


def solution(mesh):
    both = ("seq", "col")
    cells = P(None, "seq", "col")
    stack = P(None, both, None)
    row_split = P(both, None)
    col_split = P(None, both)
    weights = [stack] * 6 + [row_split] * 3 + [col_split] * 9 + [P()] * 3
    return jax.shard_map(
        shards,
        mesh=mesh,
        in_specs=(cells, cells, cells, stack, col_split, *weights),
        out_specs=(*weights, stack, stack, row_split, col_split, col_split, P(), P()),
        check_vma=False,
    )
```

```python
import typing

import jax
import jax.numpy as jnp
from jax import lax
from jax.experimental import pallas as pl
from jax.experimental.pallas import tpu as pltpu
from jax.sharding import PartitionSpec as P

D = 768
HEADS = 12
HD = 64
FF = 3072
VOCAB = 33
VP = 64
STEP = 10

NORM_EPS = 1e-05
MASK_ID = 32
MAX_NORM = 0.001
LEARN_RATE = 0.05
VECTOR_RATE = 0.5
BETA_ONE = 0.9
BETA_TWO = 0.95
ADAM_EPS = 1e-08
WEIGHT_DECAY = 0.01
PRECISE = lax.Precision.HIGHEST
F32 = jnp.float32
BF16 = jnp.bfloat16


def nn(left, right):
    return lax.dot_general(left, right, (((1,), (0,)), ((), ())), preferred_element_type=F32)


def tn(left, right):
    return lax.dot_general(left, right, (((0,), (0,)), ((), ())), preferred_element_type=F32)


def nt(left, right):
    return lax.dot_general(left, right, (((1,), (1,)), ((), ())), preferred_element_type=F32)


def split_two(values):
    high = values.astype(BF16)
    return high, (values - high.astype(F32)).astype(BF16)


def norm_stats(values):
    centre = values - jnp.mean(values, -1, keepdims=True)
    rstd = lax.rsqrt(jnp.mean(centre * centre, -1, keepdims=True) + NORM_EPS)
    return centre * rstd, rstd


def norm_back(unit, rstd, scale_vec, upstream):
    inner = upstream * scale_vec
    grad = rstd * (
        inner - jnp.mean(inner, -1, keepdims=True) - unit * jnp.mean(inner * unit, -1, keepdims=True)
    )
    return grad, jnp.sum(upstream * unit, 0), jnp.sum(upstream, 0)


GELU_K = 0.7978845608028654
GELU_C = 0.044715


def gelu_parts(up):
    square = up * up
    bent = jnp.tanh(GELU_K * up * (1.0 + GELU_C * square))
    half = 0.5 * (1.0 + bent)
    slope = half + 0.5 * up * (1.0 - bent * bent) * GELU_K * (1.0 + 3.0 * GELU_C * square)
    return up * half, slope


def heads_of(block, head):
    return block[:, head * HD : (head + 1) * HD]


def step(big, table, norms, contact_head, ids_all, ids_ri, ids_ir, targets_ir, pair_first, pair_second, labels, counts, cw):
    in_row, in_col, out_row, out_col, up_w, down_t = big
    rows, cols = ids_all.shape
    here = rows * cw
    row_scale = (HD * rows) ** (-0.5)
    vocab = jnp.arange(VP)[:, None]
    hot_all = (ids_all[:, None, :] == vocab[None]).astype(BF16).reshape(rows * VP, cols)
    hot_ri = (ids_ri[None, :] == vocab).astype(BF16)
    hot_ir = (ids_ir[None, :] == vocab).astype(BF16)
    spot = jnp.arange(here)
    perm = (
        ((spot // rows)[:, None] == (spot % cw)[None, :])
        & ((spot % rows)[:, None] == (spot // cw)[None, :])
    ).astype(BF16)

    def to_heads(block):
        return block.reshape(rows, cw, HEADS, VP).transpose(2, 1, 0, 3).reshape(HEADS * cw, rows * VP)

    def to_tokens(block):
        return block.reshape(HEADS, cw, rows, VP).transpose(2, 1, 0, 3).reshape(here, HEADS * VP)

    def per_head(block, other, how):
        return jnp.concatenate(
            [how(heads_of(block, h), heads_of(other, h)) for h in range(HEADS)], -1
        )

    table_f = table.astype(F32)
    unit_t, rstd_t = norm_stats(table_f)
    normed_t = (unit_t * norms[0] + norms[4]).astype(BF16)
    proj_t = nn(normed_t, in_row).astype(BF16)
    query_t, key_t, value_t = proj_t[:, :D], proj_t[:, D : 2 * D], proj_t[:, 2 * D :]

    pair_t = per_head(query_t, key_t, nt)
    pair_hi, pair_lo = split_two(pair_t)
    left_hi = to_heads(tn(hot_ri, pair_hi).astype(BF16))
    left_lo = to_heads(tn(hot_ri, pair_lo).astype(BF16))
    score = (nn(left_hi, hot_all) + nn(left_lo, hot_all)) * row_scale
    prob = jax.nn.softmax(score, axis=-1)
    prob_low = prob.astype(BF16)
    weight_t = to_tokens(nt(prob_low, hot_all))
    weight_hi, weight_lo = split_two(weight_t)
    row_mixed_ri = (
        per_head(weight_hi, value_t, nn) + per_head(weight_lo, value_t, nn)
    ).astype(BF16)
    row_mixed = nn(perm, row_mixed_ri).astype(BF16)
    embedded = tn(hot_ir, table)
    after_row = embedded + nn(row_mixed, out_row)

    prob_cube = prob_low.astype(F32).reshape(HEADS, cw, cols)
    head_sum = jnp.sum(prob_cube * contact_head[:HEADS, None, None], 0)
    first_hot = (pair_first[None, :] == jnp.arange(cw)[:, None]).astype(F32)
    second_hot = (pair_second[None, :] == jnp.arange(cols)[:, None]).astype(BF16)
    sum_hi, sum_lo = split_two(head_sum)
    sum_last = (head_sum - sum_hi.astype(F32) - sum_lo.astype(F32)).astype(BF16)
    picked = nn(sum_hi, second_hot) + nn(sum_lo, second_hot) + nn(sum_last, second_hot)
    contact_logit = jnp.sum(picked * first_hot, 0) * cols + contact_head[HEADS]
    owned = jnp.sum(first_hot, 0) > 0
    valid = (labels >= 0) & owned
    positive = (labels == 1).astype(F32)
    bce_sum = jnp.sum(
        jnp.where(valid, jax.nn.softplus(contact_logit) - positive * contact_logit, 0.0)
    )
    coef = jnp.where(valid, jax.nn.sigmoid(contact_logit) - positive, 0.0) / counts[1]
    coef_hi, coef_lo = split_two(coef)
    first_low = first_hot.astype(BF16)
    touch = nt(first_low * coef_hi[None], second_hot) + nt(first_low * coef_lo[None], second_hot)
    grad_contact = jnp.concatenate(
        [jnp.sum(prob_cube * touch[None], (1, 2)) * cols, jnp.sum(coef)[None]]
    )

    unit_1, rstd_1 = norm_stats(after_row)
    col_normed = (unit_1 * norms[1] + norms[5]).astype(BF16)
    col_proj = nn(col_normed, in_col).astype(BF16)
    group = 128 if here % 128 == 0 and 128 % rows == 0 else here
    groups = here // group
    lane = jnp.arange(group)
    same = (lane[:, None] // rows) == (lane[None, :] // rows)

    def cut(block):
        return block.reshape(groups, group, HEADS, HD)

    col_query, col_key, col_value = (cut(col_proj[:, k * D : (k + 1) * D]) for k in range(3))
    col_score = jnp.einsum("gqhe,gkhe->ghqk", col_query, col_key, preferred_element_type=F32) * HD ** (-0.5)
    col_prob = jax.nn.softmax(jnp.where(same, col_score, -1e30), axis=-1)
    col_prob_low = col_prob.astype(BF16)
    col_mixed = (
        jnp.einsum("ghqk,gkhe->gqhe", col_prob_low, col_value, preferred_element_type=F32)
        .astype(BF16)
        .reshape(here, D)
    )
    after_col = after_row + nn(col_mixed, out_col)

    unit_2, rstd_2 = norm_stats(after_col)
    feed_normed = (unit_2 * norms[2] + norms[6]).astype(BF16)
    hidden_up = nn(feed_normed, up_w)
    active, slope = gelu_parts(hidden_up)
    active = active.astype(BF16)
    after_feed = after_col + nt(active, down_t)
    unit_3, rstd_3 = norm_stats(after_feed)
    head_normed = (unit_3 * norms[3] + norms[7]).astype(BF16)
    logits = nt(table, head_normed) * D ** (-0.5)
    logits = jnp.where(vocab < VOCAB, logits, -1e30)
    top = jnp.max(logits, 0, keepdims=True)
    shifted = logits - top
    log_probs = shifted - jnp.log(jnp.sum(jnp.exp(shifted), 0, keepdims=True))
    target_hot = (targets_ir[None, :] == vocab).astype(F32)
    keep = ids_ir[None, :] == MASK_ID
    mlm_sum = -jnp.sum(jnp.where(keep & (target_hot > 0), log_probs, 0.0))
    logit_grad = jnp.where(keep, jnp.exp(log_probs) - target_hot, 0.0) / counts[0]
    logit_low = (logit_grad * D ** (-0.5)).astype(BF16)

    grad_head = nn(logit_low, head_normed)
    stream, scale_3, shift_3 = norm_back(unit_3, rstd_3, norms[3], tn(logit_low, table))
    branch = stream.astype(BF16)
    grad_down = tn(branch, active)
    up_low = (nn(branch, down_t) * slope).astype(BF16)
    grad_up = tn(feed_normed, up_low)
    inner, scale_2, shift_2 = norm_back(unit_2, rstd_2, norms[2], nt(up_low, up_w))
    stream = stream + inner
    branch = stream.astype(BF16)
    grad_out_col = tn(col_mixed, branch)
    mixed_low = nt(branch, out_col).astype(BF16)
    mixed_cut = cut(mixed_low)
    prob_grad = jnp.einsum("gqhe,gkhe->ghqk", mixed_cut, col_value, preferred_element_type=F32)
    score_grad = col_prob * (prob_grad - jnp.sum(col_prob * prob_grad, -1, keepdims=True))
    score_low = score_grad.astype(BF16)
    grad_q = jnp.einsum("ghqk,gkhe->gqhe", score_low, col_key, preferred_element_type=F32)
    grad_k = jnp.einsum("ghqk,gqhe->gkhe", score_low, col_query, preferred_element_type=F32)
    grad_v = jnp.einsum("ghqk,gqhe->gkhe", col_prob_low, mixed_cut, preferred_element_type=F32)
    proj_low = jnp.concatenate(
        [
            (grad_q * HD ** (-0.5)).reshape(here, D),
            (grad_k * HD ** (-0.5)).reshape(here, D),
            grad_v.reshape(here, D),
        ],
        -1,
    ).astype(BF16)
    grad_in_col = tn(col_normed, proj_low)
    inner, scale_1, shift_1 = norm_back(unit_1, rstd_1, norms[1], nt(proj_low, in_col))
    stream = stream + inner
    branch = stream.astype(BF16)
    grad_out_row = tn(row_mixed, branch)
    mixed_low = nt(branch, out_row).astype(BF16)
    mixed_ri = tn(perm, mixed_low).astype(BF16)
    drive_hi, drive_lo = split_two(per_head(mixed_ri, value_t, nt))
    prob_grad = nn(to_heads(drive_hi), hot_all) + nn(to_heads(drive_lo), hot_all)
    prob_grad = prob_grad + (
        touch[None] * (contact_head[:HEADS, None, None] * cols)
    ).reshape(HEADS * cw, cols)
    score_grad = prob * (prob_grad - jnp.sum(prob * prob_grad, -1, keepdims=True))
    score_low = score_grad.astype(BF16)
    spread = to_tokens(nt(score_low, hot_all)).astype(BF16)
    table_pair = nn(hot_ri, spread)
    value_grad = per_head(weight_hi, mixed_ri, tn)
    stream_hi, stream_lo = split_two(stream)
    lookup_grad = nn(hot_ir, stream_hi) + nn(hot_ir, stream_lo)
    vectors = jnp.stack([scale_1, scale_2, scale_3, shift_1, shift_2, shift_3])
    return (
        (grad_in_col, grad_out_row, grad_out_col, grad_up, grad_down),
        (table_pair, value_grad, grad_head + lookup_grad, vectors),
        grad_contact,
        mlm_sum,
        bce_sum,
        (unit_t, rstd_t, normed_t, query_t, key_t),
    )


MESH = pl.DeviceIdType.MESH
NZ, NY = 4, 2


def place():
    s, c = lax.axis_index("seq"), lax.axis_index("col")
    z, y, k = s // 4, lax.rem(s // 2, 2), lax.rem(s, 2)
    return z, y, k, c


def device(z, y, k, c):
    return (z * 4 + y * 2 + k, c)


def greet_all():
    z, y, k, c = place()
    me = (z * 4 + y * 2 + k) * 2 + c
    barrier = pltpu.get_barrier_semaphore()

    def signal(step, carry):
        other = lax.rem(me + step, 32)
        pl.semaphore_signal(
            barrier, inc=1, device_id=(other // 2, lax.rem(other, 2)), device_id_type=MESH
        )
        return carry

    lax.fori_loop(1, 32, signal, 0)
    return barrier


def remote(src, dst, send, recv, target):
    return pltpu.make_async_remote_copy(
        src_ref=src, dst_ref=dst, send_sem=send, recv_sem=recv, device_id=target, device_id_type=MESH
    )


ROWS, COLS, WIDE, HERE = 16, 512, 32, 512
PAIRS = 6
SLOTS = 1024
UP_TILE = 384


def iota(shape, dim):
    return lax.broadcasted_iota(jnp.int32, shape, dim)


def one_zero(test):
    return jnp.where(test, 1.0, 0.0)


def total_of(values):
    return jnp.sum(jnp.sum(values, 0, keepdims=True), 1, keepdims=True)


def half_lanes(values, side):
    lane = iota(values.shape, len(values.shape) - 1)
    keep = (lane < 64) if side == 0 else (lane >= 64)
    return jnp.where(keep, values.astype(F32), 0.0).astype(BF16)


def stacked(values):
    return jnp.concatenate([half_lanes(values, 0), half_lanes(values, 1)], 0)


def unstacked(values, count):
    lane = iota((count, 128), 1)
    return jnp.where(lane < 64, values[:count], values[count:])


def swap_blocks(first, second):
    lane = iota(first.shape, 1)
    low = jnp.where(lane < 64, first, pltpu.roll(second, 64, 1))
    high = jnp.where(lane < 64, pltpu.roll(first, 64, 1), second)
    return low, high


def split_heads_to(source, high_ref, low_ref):
    for rp in range(ROWS // 2):
        for hp in range(PAIRS):
            lanes = slice(hp * 128, hp * 128 + 128)
            first = source[rp * 64 : rp * 64 + 32, lanes]
            second = source[rp * 64 + 32 : rp * 64 + 64, lanes]
            for side, block in enumerate(swap_blocks(first, second)):
                top, rest = split_two(block)
                rows = slice((2 * hp + side) * 32, (2 * hp + side) * 32 + 32)
                high_ref[rows, rp * 128 : rp * 128 + 128] = top
                low_ref[rows, rp * 128 : rp * 128 + 128] = rest


def merge_heads(probs, hot_all, high_ref, low_ref):
    for rp in range(ROWS // 2):
        block = nt(probs, hot_all[rp * 128 : rp * 128 + 128, :])
        for hp in range(PAIRS):
            first = block[hp * 64 : hp * 64 + 32]
            second = block[hp * 64 + 32 : hp * 64 + 64]
            for side, part in enumerate(swap_blocks(first, second)):
                top, rest = split_two(part)
                rows = slice(rp * 64 + side * 32, rp * 64 + side * 32 + 32)
                high_ref[rows, hp * 128 : hp * 128 + 128] = top
                if low_ref is not None:
                    low_ref[rows, hp * 128 : hp * 128 + 128] = rest


def norm_rows(source, gain, bias, unit_ref, rstd_ref, normed_ref):
    def body(at, carry):
        rows = pl.ds(pl.multiple_of(at * 64, 64), 64)
        values = source[rows, :]
        centre = values - jnp.sum(values, -1, keepdims=True) * (1.0 / D)
        rstd = lax.rsqrt(jnp.sum(centre * centre, -1, keepdims=True) * (1.0 / D) + NORM_EPS)
        unit = centre * rstd
        unit_ref[rows, :] = unit
        rstd_ref[rows, :] = jnp.broadcast_to(rstd, (64, 128))
        normed_ref[rows, :] = (unit * gain + bias).astype(BF16)
        return carry

    lax.fori_loop(0, HERE // 64, body, 0)


def transpose_into(source, target):
    def body(at, carry):
        rows = pl.ds(pl.multiple_of(at * 128, 128), 128)
        target[:, rows] = source[rows, :].astype(F32).T.astype(BF16)
        return carry

    lax.fori_loop(0, HERE // 128, body, 0)


def over_tiles(width, tile, body):
    for half in range(2):

        def step(at, carry, half=half):
            body(half, pl.multiple_of(at * tile, tile))
            return carry

        lax.fori_loop(0, width // tile, step, 0)


def column_mask():
    rows, lanes = iota((256, 128), 0), iota((256, 128), 1)
    return ((rows & 127) >> 4) == (lanes >> 4)


class Saved(typing.NamedTuple):
    stream: typing.Any
    branch: typing.Any
    unit_1: typing.Any
    unit_2: typing.Any
    rstd_1: typing.Any
    rstd_2: typing.Any
    row_mixed_t: typing.Any
    col_normed_t: typing.Any
    col_mixed_t: typing.Any
    feed_normed_t: typing.Any
    col_proj: typing.Any
    col_prob: typing.Any
    active: typing.Any
    slope: typing.Any
    grad_head: typing.Any
    hot_all: typing.Any
    hot_ri: typing.Any
    hot_ir: typing.Any
    prob: typing.Any
    weight_hi: typing.Any
    value_two: typing.Any
    touch: typing.Any
    table: typing.Any
    norms: typing.Any
    proj_t: typing.Any
    extras: typing.Any
    moved: typing.Any


AT = Saved(*range(len(Saved._fields)))
SAVED = Saved(
    stream=((HERE, D), F32),
    branch=((HERE, D), BF16),
    unit_1=((HERE, D), F32),
    unit_2=((HERE, D), F32),
    rstd_1=((HERE, 128), F32),
    rstd_2=((HERE, 128), F32),
    row_mixed_t=((D, HERE), BF16),
    col_normed_t=((D, HERE), BF16),
    col_mixed_t=((D, HERE), BF16),
    feed_normed_t=((D, HERE), BF16),
    col_proj=((HERE, 3 * D), BF16),
    col_prob=((4 * PAIRS, 256, 128), F32),
    active=((HERE, FF), BF16),
    slope=((HERE, FF), BF16),
    grad_head=((VP, D), F32),
    hot_all=((ROWS * VP, COLS), BF16),
    hot_ri=((VP, HERE), BF16),
    hot_ir=((VP, HERE), BF16),
    prob=((HEADS * WIDE, COLS), F32),
    weight_hi=((HERE, D), BF16),
    value_two=((PAIRS, 128, 128), BF16),
    touch=((WIDE, COLS), F32),
    table=((VP, D), F32),
    norms=((8, D), F32),
    proj_t=((VP, 3 * D), BF16),
    extras=((8, 128), F32),
    moved=((8, D), F32),
)


class Forward(typing.NamedTuple):
    ids: typing.Any
    targets: typing.Any
    slots: typing.Any
    normed: typing.Any
    mixed: typing.Any
    weight_lo: typing.Any
    left_hi: typing.Any
    left_lo: typing.Any
    lookup: typing.Any
    prob_low: typing.Any
    unit: typing.Any
    rstd: typing.Any


FORWARD = Forward(
    ids=((ROWS, COLS), jnp.int32),
    targets=((ROWS, 128), jnp.int32),
    slots=((8, SLOTS), jnp.int32),
    normed=((HERE, D), BF16),
    mixed=((HERE, D), BF16),
    weight_lo=((HERE, D), BF16),
    left_hi=((HEADS * WIDE, ROWS * VP), BF16),
    left_lo=((HEADS * WIDE, ROWS * VP), BF16),
    lookup=((HERE, D), F32),
    prob_low=((HEADS * WIDE, COLS), BF16),
    unit=((HERE, D), F32),
    rstd=((HERE, 128), F32),
)


def position():
    z, y, k, c = place()
    me = (z * 4 + y * 2 + k) * 2 + c
    return z // 2, lax.rem(me, 16)


def read_tokens(small, f):
    alignment, block = position()
    side, part = block // 8, lax.rem(block // 4, 2)
    for r in range(ROWS):
        for cc in range(2):
            for q in range(2):
                lanes = slice(cc * 256 + q * 128, cc * 256 + q * 128 + 128)
                f.ids[r : r + 1, lanes] = small[r * 2 + cc, pl.ds(2 * alignment + q, 1), :]
        f.targets[r : r + 1, :] = small[r * 2 + side, pl.ds(4 + 2 * alignment + part, 1), :]
    lane = iota((1, 128), 1)
    for number in range(SLOTS // 128):
        for which in range(3):
            row = pl.ds(8 + 3 * alignment + which, 1)
            first = small[number * 4 + side, row, :]
            second = pltpu.roll(small[number * 4 + 2 + side, row, :], 64, 1)
            f.slots[which : which + 1, number * 128 : number * 128 + 128] = jnp.where(
                lane < 64, first, second
            )


def local_hot(values, shift):
    values = pltpu.roll(values, shift, 1)
    turned = [values] + [pltpu.roll(values, 32 * n, 1) for n in (1, 2, 3)]
    lane = iota((1, 128), 1)
    tiles = []
    for tile in range(4):
        row = turned[3][4 * tile + 3 : 4 * tile + 4]
        for n in (2, 1, 0):
            row = jnp.where(lane < 32 * n + 32, turned[n][4 * tile + n : 4 * tile + n + 1], row)
        tiles.append(row)
    row = jnp.concatenate(tiles, 1)
    return one_zero(row == iota((VP, HERE), 0)).astype(BF16)


def contact_part(contact_head, f, s, pair_count):
    _, block = position()
    base = block * WIDE
    head_sum = jnp.zeros((WIDE, COLS), F32)
    for h in range(HEADS):
        head_sum = head_sum + contact_head[h] * f.prob_low[h * 32 : h * 32 + 32, :].astype(F32)
    top, rest = split_two(head_sum)
    last = (head_sum - top.astype(F32) - rest.astype(F32)).astype(BF16)
    parts = jnp.concatenate([top, rest, last], 0)
    touch = jnp.zeros((WIDE, COLS), F32)
    bce = jnp.zeros((1, 1), F32)
    coef_sum = jnp.zeros((1, 1), F32)
    for number in range(SLOTS // 512):
        lanes = slice(number * 512, number * 512 + 512)
        first, second, label = (f.slots[n : n + 1, lanes] for n in range(3))
        second_hot = one_zero(second == iota((COLS, 512), 0)).astype(BF16)
        picked = nn(parts, second_hot)
        picked = picked[:32] + picked[32:64] + picked[64:]
        first_hot = one_zero((first - base) == iota((WIDE, 512), 0))
        logit = jnp.sum(picked * first_hot, 0, keepdims=True) * COLS + contact_head[HEADS]
        owned = jnp.sum(first_hot, 0, keepdims=True) > 0.5
        valid = (label >= 0) & owned
        positive = one_zero(label == 1)
        small = jnp.exp(-jnp.abs(logit))
        soft = jnp.maximum(logit, 0.0) + jnp.log(1.0 + small)
        bce = bce + total_of(jnp.where(valid, soft - positive * logit, 0.0))
        sigmoid = jnp.where(logit >= 0.0, 1.0, small) / (1.0 + small)
        coef = jnp.where(valid, sigmoid - positive, 0.0) / pair_count
        coef_sum = coef_sum + total_of(coef)
        coef_top, coef_rest = split_two(first_hot * coef)
        touch = touch + nt(coef_top, second_hot) + nt(coef_rest, second_hot)
    s.touch[...] = touch
    column = iota((1, 128), 1)
    row = jnp.where(column == HEADS, coef_sum, 0.0)
    for h in range(HEADS):
        part = total_of(touch * f.prob_low[h * 32 : h * 32 + 32, :].astype(F32)) * COLS
        row = row + jnp.where(column == h, part, 0.0)
    return row, bce


def feature_order():
    shape = (384, 384)
    spot = iota(shape, 0)
    block = (spot * 2731) >> 16
    swapped = (block & 28) | ((block & 1) << 1) | ((block >> 1) & 1)
    return one_zero(spot + (swapped - block) * 24 == iota(shape, 1)).astype(BF16)


def forward_body(small, contact_head, weights, s, f, ready, hook, emit):
    emb, in_row, out_row, in_col, out_col = weights[:5]
    up_parts, down_parts = weights[5:7], weights[7:9]
    ready(-1)
    hook()
    read_tokens(small, f)
    _, block = position()
    shift = lax.rem(128 - lax.rem(block, 4) * 32, 128)
    window = pl.ds(pl.multiple_of((block // 4) * 128, 128), 128)
    hot_ri = local_hot(f.ids[:, window], shift)
    goal_ri = local_hot(f.targets[...], shift)
    s.hot_ri[...] = hot_ri
    for r in range(ROWS):
        row = f.ids[r : r + 1, :]
        s.hot_all[r * VP : r * VP + VP, :] = one_zero(row == iota((VP, COLS), 0)).astype(BF16)
    shape = (HERE, HERE)
    back = (
        ((iota(shape, 1) >> 4) == (iota(shape, 0) & 31))
        & ((iota(shape, 1) & 15) == (iota(shape, 0) >> 5))
    )
    back = one_zero(back).astype(BF16)
    hot_ir = nn(hot_ri, back).astype(BF16)
    s.hot_ir[...] = hot_ir
    goal = nn(goal_ri, back)
    entries = jnp.zeros((4, 128), F32)
    labelled = jnp.zeros((1, 128), F32)
    for d in range(32):
        entries = entries + one_zero(small[d, 0:4, :] == MASK_ID)
        labelled = labelled + one_zero(small[d, 10:11, :] >= 0) + one_zero(small[d, 13:14, :] >= 0)
    entries, labelled = total_of(entries), total_of(labelled)

    hook()
    table = emb[0].astype(F32).T[:VP]
    norms = emb[1].astype(F32).T[:8]
    s.table[...] = table
    s.norms[...] = norms
    table_low = table.astype(BF16)

    def vector(number):
        return norms[number : number + 1, :]

    unit_t, _ = norm_stats(table)
    normed_t = (unit_t * vector(0) + vector(4)).astype(BF16)
    hook()
    for half in range(2):
        s.proj_t[:, half * 1152 : half * 1152 + 1152] = nn(normed_t, in_row[half]).astype(BF16)
    pair_parts = []
    for hp in range(PAIRS):
        lanes = slice(hp * 128, hp * 128 + 128)
        key = s.proj_t[:, D + hp * 128 : D + hp * 128 + 128]
        value = s.proj_t[:, 2 * D + hp * 128 : 2 * D + hp * 128 + 128]
        s.value_two[hp] = stacked(value)
        pair_parts.append(nt(s.proj_t[:, lanes], stacked(key)))
    pair_hi, pair_lo = split_two(jnp.concatenate(pair_parts, 1))
    hook()
    f.lookup[...] = tn(hot_ri, pair_hi) + tn(hot_ri, pair_lo)
    split_heads_to(f.lookup, f.left_hi, f.left_lo)
    hook()
    hot_all = s.hot_all[...]
    score = (nn(f.left_hi[...], hot_all) + nn(f.left_lo[...], hot_all)) * (HD * ROWS) ** (-0.5)
    score = jnp.exp(score - jnp.max(score, -1, keepdims=True))
    prob = score / jnp.sum(score, -1, keepdims=True)
    s.prob[...] = prob
    f.prob_low[...] = prob.astype(BF16)
    hook()
    merge_heads(f.prob_low[...], s.hot_all, s.weight_hi, f.weight_lo)
    hook()
    for hp in range(PAIRS):
        lanes = slice(hp * 128, hp * 128 + 128)
        value = s.value_two[hp]
        f.mixed[:, lanes] = (nn(s.weight_hi[:, lanes], value) + nn(f.weight_lo[:, lanes], value)).astype(BF16)
    ahead = (
        ((iota(shape, 0) >> 4) == (iota(shape, 1) & 31))
        & ((iota(shape, 0) & 15) == (iota(shape, 1) >> 5))
    )
    f.mixed[...] = nn(one_zero(ahead).astype(BF16), f.mixed[...]).astype(BF16)
    transpose_into(f.mixed, s.row_mixed_t)
    s.stream[...] = tn(hot_ir, table_low)
    hook()
    contact_row, bce = contact_part(contact_head, f, s, labelled)
    emit(AT.hot_all, AT.hot_ri, AT.hot_ir, AT.table, AT.norms, AT.proj_t, AT.value_two, AT.prob, AT.weight_hi, AT.row_mixed_t, AT.touch)

    hook()
    for half in range(2):
        lanes = slice(half * 384, half * 384 + 384)
        s.stream[:, lanes] += nn(f.mixed[...], out_row[half])
    norm_rows(s.stream, vector(1), vector(5), s.unit_1, s.rstd_1, f.normed)
    transpose_into(f.normed, s.col_normed_t)
    emit(AT.unit_1, AT.rstd_1, AT.col_normed_t)
    def project(half, at):
        s.col_proj[:, half * 1152 + at : half * 1152 + at + 384] = nn(
            f.normed[...], in_col[half, :, at : at + 384]
        ).astype(BF16)

    for third in range(3):
        hook()
        for half in range(2):
            project(half, third * 384)
    emit(AT.col_proj)

    def attend(at, carry):
        rows = pl.ds(pl.multiple_of((at // PAIRS) * 128, 128), 128)
        lane = lax.rem(at, PAIRS) * 128

        def lanes(part):
            return pl.ds(pl.multiple_of(part * D + lane, 128), 128)

        query = stacked(s.col_proj[rows, lanes(0)])
        score = nt(query, s.col_proj[rows, lanes(1)]) * HD ** (-0.5)
        score = jnp.where(column_mask(), score, -1e30)
        score = jnp.exp(score - jnp.max(score, -1, keepdims=True))
        prob = score / jnp.sum(score, -1, keepdims=True)
        s.col_prob[at] = prob
        mixed = nn(prob.astype(BF16), s.col_proj[rows, lanes(2)])
        f.mixed[rows, lanes(0)] = unstacked(mixed, 128).astype(BF16)
        return carry

    for part in range(4):
        hook()
        lax.fori_loop(part * PAIRS, part * PAIRS + PAIRS, attend, 0, unroll=3)
    hook()
    transpose_into(f.mixed, s.col_mixed_t)
    emit(AT.col_prob, AT.col_mixed_t)
    for half in range(2):
        lanes = slice(half * 384, half * 384 + 384)
        s.stream[:, lanes] += nn(f.mixed[...], out_col[half])
    norm_rows(s.stream, vector(2), vector(6), s.unit_2, s.rstd_2, f.normed)
    transpose_into(f.normed, s.feed_normed_t)
    emit(AT.unit_2, AT.rstd_2, AT.feed_normed_t)
    for part in range(2):

        def widen(half, at, part=part):
            lanes = slice(part * 1536 + half * 768 + at, part * 1536 + half * 768 + at + UP_TILE)
            up = nn(f.normed[...], up_parts[part][half, :, at : at + UP_TILE])
            active, slope = gelu_parts(up)
            s.active[:, lanes] = active.astype(BF16)
            s.slope[:, lanes] = slope.astype(BF16)

        for half in range(2):
            hook()
            for at in range(0, 768, UP_TILE):
                widen(half, at)

    emit(AT.active, AT.slope)
    for part, at, size in ((0, 0, 768), (1, 0, 384), (1, 384, 384)):
        hook()
        for half in range(2):
            start = part * 1536 + half * 768 + at
            s.stream[...] += nt(
                s.active[:, start : start + size], down_parts[part][half, :, at : at + size]
            )
    hook()
    norm_rows(s.stream, vector(3), vector(7), f.unit, f.rstd, f.normed)
    logits = nt(table_low, f.normed[...]) * D ** (-0.5)
    vocab = iota((VP, HERE), 0)
    logits = jnp.where(vocab < VOCAB, logits, -1e30)
    shifted = logits - jnp.max(logits, 0, keepdims=True)
    log_probs = shifted - jnp.log(jnp.sum(jnp.exp(shifted), 0, keepdims=True))
    keep = hot_ir[MASK_ID : MASK_ID + 1].astype(F32) > 0.5
    mlm = -total_of(jnp.where(keep & (goal > 0.5), log_probs, 0.0))
    logit_grad = jnp.where(keep, jnp.exp(log_probs) - goal, 0.0) / entries
    logit_low = (logit_grad * D ** (-0.5)).astype(BF16)
    s.grad_head[...] = nn(logit_low, f.normed[...])
    hook()
    f.lookup[...] = tn(logit_low, table_low)
    scale_3, shift_3 = back_rows(f.unit, f.rstd, vector(3), f.lookup, s.stream, s.branch, True)
    emit(AT.stream, AT.branch)
    line = iota((8, D), 0)
    s.moved[...] = jnp.where(line == 0, scale_3, jnp.where(line == 1, shift_3, 0.0))
    column = iota((1, 128), 1)
    row = contact_row + jnp.where(column == HEADS + 1, mlm, 0.0) + jnp.where(column == HEADS + 2, bce, 0.0)
    counted = jnp.where(column == 0, entries, 0.0) + jnp.where(column == 1, labelled, 0.0)
    line = iota((8, 128), 0)
    s.extras[...] = jnp.where(line == 0, row, jnp.where(line == 1, counted, 0.0))
    emit(AT.grad_head, AT.extras, AT.moved)
    hook()


def back_rows(unit_ref, rstd_ref, gain, upstream_ref, stream_ref, low_ref, first):
    def body(at, carry):
        scale, move = carry
        rows = pl.ds(pl.multiple_of(at * 64, 64), 64)
        upstream = upstream_ref[rows, :]
        unit = unit_ref[rows, :]
        inner = upstream * gain
        mean = jnp.sum(inner, -1, keepdims=True) * (1.0 / D)
        along = jnp.sum(inner * unit, -1, keepdims=True) * (1.0 / D)
        grad = rstd_ref[rows, 0:1] * (inner - mean - unit * along)
        if not first:
            grad = grad + stream_ref[rows, :]
        stream_ref[rows, :] = grad
        low_ref[rows, :] = grad.astype(BF16)
        touched = upstream * unit
        for n in range(8):
            scale = scale + touched[n * 8 : n * 8 + 8]
            move = move + upstream[n * 8 : n * 8 + 8]
        return scale, move

    zero = jnp.zeros((8, D), F32)
    scale, move = lax.fori_loop(0, HERE // 64, body, (zero, zero))
    return jnp.sum(scale, 0, keepdims=True), jnp.sum(move, 0, keepdims=True)


MATRICES = (128, 1152, 384, 1152, 384, 768, 768, 768, 768)
UNITS = (
    (0, 0, 128, True),
    (1, 0, 384, True),
    (1, 384, 384, True),
    (1, 768, 384, True),
    (2, 0, 384, False),
    (3, 0, 384, True),
    (3, 384, 384, True),
    (3, 768, 384, True),
    (4, 0, 384, False),
    (5, 0, 768, True),
    (6, 0, 768, True),
    (7, 0, 768, True),
    (8, 0, 384, True),
    (8, 384, 384, True),
)
Z_LAST = {8: 1, 12: 2}
FORWARD_ORDER = (
    (),
    ((0, 0), (0, 1), (0, 2), (0, 3), (0, 4), (0, 5), (0, 6), (0, 7), (0, 8), (1, 0), (0, 9), (0, 10), (0, 11), (0, 12), (1, 8), (0, 13), (2, 0), (1, 1), (1, 12), (2, 8), (1, 2), (3, 0), (2, 1), (4, 0),),
    ((1, 3), (2, 12), (2, 2), (1, 4), (3, 1), (1, 5), (2, 3), (4, 1), (1, 6), (3, 2), (2, 4), (4, 2), (1, 7), (2, 5), (3, 3), (1, 9), (2, 6), (4, 3),),
    (),
    ((3, 4),),
    ((2, 7), (1, 10), (4, 4),),
    ((3, 5),),
    (),
    ((4, 5), (2, 9), (1, 11),),
    ((3, 6), (1, 13), (3, 7), (4, 6), (4, 7),),
    ((2, 10),),
    (),
    (),
    (),
    (),
    ((3, 8), (3, 9),),
    ((2, 11), (4, 8),),
    ((4, 9),),
    ((2, 13),),
    ((3, 10), (3, 12), (4, 10), (3, 11),),
    ((4, 12),),
    ((3, 13), (4, 11),),
    ((4, 13),),
    (),
    (),
    (),
    (),
)


def spot(paired, cc, zz, yy, k):
    return (k, zz, yy, cc) if paired else (cc, zz, yy, k)


def forward_kernel(*refs):
    count, parts = len(UNITS), len(MATRICES)
    raw = refs[:11]
    contact_head = refs[11]
    at = 12
    far = refs[at : at + parts]
    saved_far = refs[at + parts : at + parts + len(SAVED)]
    at += parts + len(SAVED)
    outs = refs[at : at + parts]
    at += parts
    outgoing = refs[at : at + count]
    incoming = refs[at + count : at + 2 * count]
    piece = refs[at + 2 * count : at + 3 * count]
    at += 3 * count
    saved = Saved(*refs[at : at + len(SAVED)])
    at += len(SAVED)
    scratch = Forward(*refs[at : at + len(FORWARD)])
    at += len(FORWARD)
    near = refs[at : at + 11]
    at += 11
    small, small_out, sides, corner = refs[at : at + 4]
    small_send, small_recv, send, recv, local, out_sem, raw_sem = refs[at + 4 :]
    tokens, targets, masked, pairs, labels, table, norms, in_w, out_w, up_w, down_w = near
    z, y, k, c = place()
    me = (z * 4 + y * 2 + k) * 2 + c
    barrier = greet_all()
    raw_copies = [pltpu.make_async_copy(a, b, raw_sem.at[n]) for n, (a, b) in enumerate(zip(raw, near))]
    for item in raw_copies:
        item.start()
    for item in raw_copies[:7]:
        item.wait()
    small[...] = jnp.full(small.shape, -1, jnp.int32)
    for micro in range(2):
        for half in range(2):
            lanes = slice(half * 128, half * 128 + 128)
            row = 2 * micro + half
            small[row : row + 1, :] = jnp.where(
                masked[micro, :, lanes] > 0, MASK_ID, tokens[micro, :, lanes]
            )
            small[4 + row : 5 + row, :] = targets[micro, :, lanes]
        row = 8 + 3 * micro
        for which in range(2):
            small[row + which : row + which + 1, 0:64] = pairs[micro, which : which + 1, :]
        small[row + 2 : row + 3, 0:64] = labels[micro : micro + 1, :]
    sides[...] = jnp.zeros(sides.shape, F32)
    sides[0, :, 0:VOCAB] = table[...]
    corner[...] = jnp.zeros(corner.shape, F32)
    corner[0:8, 0:24] = norms[...]
    sides[1] = corner[...].T[:24]
    def master(u, side):
        matrix, start, n, _ = UNITS[u]
        width = MATRICES[matrix]
        if matrix == 0:
            return sides[side]
        if matrix in (1, 3):
            return in_w[matrix // 2, :, side * 1152 + start : side * 1152 + start + n]
        if matrix in (2, 4):
            rows = out_w[matrix // 2 - 1, :, side * 384 : side * 384 + 384].astype(BF16)
            return nn(rows, order)
        begin = ((matrix - 5) % 2) * 1536 + side * width + start
        return (up_w if matrix < 7 else down_w)[:, begin : begin + n]

    def mine(u):
        return k if UNITS[u][3] else c

    def set_out(u):
        other = jnp.where(mine(u) == 0, master(u, 1), master(u, 0))
        other = jnp.concatenate([other, jnp.zeros((8, UNITS[u][2]), F32)], 0)
        outgoing[u][...] = other.astype(BF16)

    set_out(0)
    pl.semaphore_wait(barrier, 31)

    def small_copy(step):
        other = lax.rem(me + step, 32)
        return remote(
            small, small_out.at[me], small_send.at[step], small_recv.at[step], (other // 2, lax.rem(other, 2))
        )

    def spread(step, carry):
        small_copy(step).start()
        return carry

    across, beside, twin = device(z, y, k, 1 - c), device(z, 1 - y, k, c), device(z, y, 1 - k, c)

    def block(u, cc, zz, yy):
        matrix, start, n, paired = UNITS[u]
        where = spot(paired, cc, zz, yy, k)
        if n == MATRICES[matrix]:
            return outs[matrix].at[where]
        return outs[matrix].at[(*where, slice(None), pl.ds(start, n))]

    def copy(u, at, src, dst, target):
        return remote(src, dst, send.at[u, at], recv.at[u, at], target)

    def pair_copy(u):
        return copy(u, 0, outgoing[u], incoming[u], twin if UNITS[u][3] else across)

    def own_copy(u):
        return pltpu.make_async_copy(piece[u], block(u, c, z, y), local.at[u])

    def line_copy(u, step):
        return copy(u, step, piece[u], block(u, c, z, y), device(lax.rem(z + step, 4), y, k, c))

    def same(u, at, cc, zz, yy, target):
        view = block(u, cc, zz, yy)
        return copy(u, at, view, view, target)

    low, high, every = pl.ds(0, 2), pl.ds(2, 2), slice(None)

    def second(u):
        return [same(u, 4, c, low, y, across), same(u, 5, c, high, y, beside)]

    def third_own(u):
        return [same(u, 6, c, low, y, beside), same(u, 7, c, high, y, across)]

    def third_far(u):
        return [same(u, 8, 1 - c, low, y, beside), same(u, 9, c, high, 1 - y, across)]

    def twin_own(u):
        return [same(u, 10, c, every, y, twin)]

    def twin_second(u):
        return [same(u, 11, 1 - c, low, y, twin), same(u, 12, c, high, 1 - y, twin)]

    def twin_third(u):
        return [
            same(u, 13, c, low, 1 - y, twin),
            same(u, 14, 1 - c, high, y, twin),
            same(u, 15, 1 - c, low, 1 - y, twin),
            same(u, 16, 1 - c, high, 1 - y, twin),
        ]

    pair_copy(0).start()
    for item in raw_copies[7:]:
        item.wait()
    order = feature_order()
    for u in range(1, count):
        set_out(u)
        pair_copy(u).start()
        if u == 3:
            lax.fori_loop(1, 32, spread, 0)
    small_out[me] = small[...]

    def to_across(u):
        return copy(u, 4, piece[u], block(u, c, z, y), across)

    def to_beside(u):
        return copy(u, 5, piece[u], block(u, c, z, y), beside)

    def to_corner(u):
        if Z_LAST[u] == 1:
            return same(u, 6, 1 - c, z, y, beside)
        return same(u, 6, c, z, 1 - y, across)

    def to_line(u):
        return [
            same(u, step, every, z, every, device(lax.rem(z + step, 4), y, k, c)) for step in (1, 3, 2)
        ]

    def to_twin(u):
        return [same(u, 7, every, z, every, twin)]

    def rest_to_twin(u):
        return [same(u, 7 + step, every, lax.rem(z + 4 - step, 4), every, twin) for step in (1, 3, 2)]

    def stage_line(u):
        pair_copy(u).wait_recv()
        side = mine(u)
        own = jnp.where(side == 0, master(u, 0), master(u, 1))
        theirs = incoming[u][...].astype(F32)[:24]
        top = jnp.where(side == 0, own, theirs)
        bottom = jnp.where(side == 0, theirs, own)
        piece[u][...] = jnp.concatenate([top, bottom], 0).astype(BF16)
        own_copy(u).start()
        if u in Z_LAST:
            to_across(u).start()
            to_beside(u).start()
            return
        for step in (1, 3, 2):
            line_copy(u, step).start()

    def stage_second(u):
        own_copy(u).wait()
        if u in Z_LAST:
            to_across(u).wait_recv()
            to_beside(u).wait_recv()
            to_corner(u).start()
            return
        for step in (1, 3, 2):
            line_copy(u, step).wait_recv()
        for item in second(u) + third_own(u) + twin_own(u):
            item.start()

    def stage_third(u):
        if u in Z_LAST:
            to_corner(u).wait_recv()
            for item in to_line(u) + to_twin(u):
                item.start()
            return
        for item in second(u):
            item.wait_recv()
        for item in third_far(u) + twin_second(u):
            item.start()

    def stage_twin(u):
        if u in Z_LAST:
            for item in to_line(u):
                item.wait_recv()
            for item in rest_to_twin(u):
                item.start()
            return
        for item in third_own(u) + third_far(u):
            item.wait_recv()
        for item in twin_third(u):
            item.start()

    def far_copy(matrix):
        return pltpu.make_async_copy(outs[matrix], far[matrix], local.at[count + matrix])

    def stage_end(u):
        if u in Z_LAST:
            for item in to_twin(u) + rest_to_twin(u):
                item.wait_recv()
            sent = [to_across(u), to_beside(u), to_corner(u)] + to_line(u) + to_twin(u)
        else:
            for item in twin_own(u) + twin_second(u) + twin_third(u):
                item.wait_recv()
            sent = [line_copy(u, step) for step in (1, 2, 3)]
            sent += second(u) + third_own(u) + third_far(u) + twin_own(u) + twin_second(u)
        for item in [pair_copy(u)] + sent:
            item.wait_send()
        if u + 1 == count or UNITS[u + 1][0] != UNITS[u][0]:
            far_copy(UNITS[u][0]).start()

    stages = (stage_line, stage_second, stage_third, stage_twin, stage_end)
    pending = list(FORWARD_ORDER)

    def hook():
        for stage, u in pending.pop(0):
            stages[stage](u)

    def ready(number):
        lax.fori_loop(1, 32, finish, 0)

    def out_copy(at):
        return pltpu.make_async_copy(saved[at], saved_far[at], out_sem.at[at])

    def emit(*numbers):
        for number in numbers:
            out_copy(number).start()

    def finish(step, carry):
        small_copy(step).wait()
        return carry

    views = [w.reshape(2, D, n) for w, n in zip(outs, MATRICES)]
    forward_body(small_out, contact_head, views, saved, scratch, ready, hook, emit)
    assert not pending
    for u in range(count):
        for item in rest_to_twin(u) if u in Z_LAST else twin_third(u):
            item.wait_send()
    for matrix in range(parts):
        far_copy(matrix).wait()
    for at in range(len(SAVED)):
        out_copy(at).wait()


def forward_call(raw, contact_head):
    count, parts = len(UNITS), len(MATRICES)
    anywhere = pl.BlockSpec(memory_space=pl.ANY)
    shapes = [(2, NZ, NY, 2, 48, n) for n in MATRICES]
    widths = [n for _, _, n, _ in UNITS]
    outs = pl.pallas_call(
        forward_kernel,
        out_shape=[jax.ShapeDtypeStruct(shape, BF16) for shape in shapes]
        + [jax.ShapeDtypeStruct(*item) for item in SAVED],
        in_specs=[anywhere] * 11 + [pl.BlockSpec(memory_space=pltpu.SMEM)],
        out_specs=[anywhere] * (parts + len(SAVED)),
        scratch_shapes=[pltpu.VMEM(shape, BF16) for shape in shapes]
        + [pltpu.VMEM((32, n), BF16) for n in widths] * 2
        + [pltpu.VMEM((48, n), BF16) for n in widths]
        + [pltpu.VMEM(*item) for item in SAVED]
        + [pltpu.VMEM(*item) for item in FORWARD]
        + [pltpu.VMEM(item.shape, item.dtype) for item in raw]
        + [
            pltpu.VMEM((16, 128), jnp.int32),
            pltpu.VMEM((32, 16, 128), jnp.int32),
            pltpu.VMEM((2, 24, 128), F32),
            pltpu.VMEM((128, 128), F32),
            pltpu.SemaphoreType.DMA((32,)),
            pltpu.SemaphoreType.DMA((32,)),
            pltpu.SemaphoreType.DMA((count, 17)),
            pltpu.SemaphoreType.DMA((count, 17)),
            pltpu.SemaphoreType.DMA((count + parts,)),
            pltpu.SemaphoreType.DMA((len(SAVED),)),
            pltpu.SemaphoreType.DMA((len(raw),)),
        ],
        compiler_params=pltpu.CompilerParams(
            collective_id=0, has_side_effects=True, vmem_limit_bytes=62 * 2**20
        ),
    )(*raw, contact_head)
    return outs[:parts], Saved(*outs[parts:])


def summed_rows(sums, group):
    return jnp.concatenate([sums[3 * group + third] for third in range(3)], 1).astype(F32)


def table_finish(sums, room, table_ref, norms_ref, proj_t, in_row, g_in, g_emb, g_norm):
    z, y, k, c = place()
    me = ((z * 2 + y) * 2 + c) * 2 + k
    room[0:128, :] = jnp.zeros((128, D), F32)
    for number in range(2):
        room[4 + 16 * number : 20 + 16 * number, :] = summed_rows(sums, number)
        room[68 + 16 * number : 84 + 16 * number, :] = summed_rows(sums, 2 + number)
    pair = room[0:64, :]
    value_grad = room[64:128, :]
    vectors = summed_rows(sums, 6)
    vectors = vectors[:8] + vectors[8:]
    line = iota((8, D), 0)
    table_grad = jnp.concatenate(
        [
            summed_rows(sums, 4),
            summed_rows(sums, 5),
            jnp.where(line == 0, vectors[7:8], 0.0),
            jnp.zeros((24, D), F32),
        ],
        0,
    )
    pair_hi, pair_lo = split_two(pair)
    scale = (HD * ROWS) ** (-0.5)
    query_grad, key_grad = [], []
    for hp in range(PAIRS):
        lanes = slice(hp * 128, hp * 128 + 128)
        query = proj_t[:, lanes]
        key = stacked(proj_t[:, D + hp * 128 : D + hp * 128 + 128])
        high, low = pair_hi[:, lanes], pair_lo[:, lanes]
        query_grad.append((nn(high, key) + nn(low, key)) * scale)
        key_grad.append(unstacked(tn(high, query) + tn(low, query), VP) * scale)
    proj_hi, proj_lo = split_two(jnp.concatenate(query_grad + key_grad + [value_grad], 1))
    normed_grad = jnp.zeros((VP, D), F32)
    for half in range(2):
        lanes = slice(half * 1152, half * 1152 + 1152)
        matrix = in_row[half]
        normed_grad = normed_grad + nt(proj_hi[:, lanes], matrix) + nt(proj_lo[:, lanes], matrix)
    unit, rstd = norm_stats(table_ref[...])
    gain = norms_ref[0:1, :]
    back, scale_0, shift_0 = norm_back(unit, rstd, gain, normed_grad)
    table_grad = table_grad + back
    line = iota((16, D), 0)
    norm_grad = jnp.zeros((16, D), F32)
    rows = [scale_0[None]] + [vectors[n : n + 1] for n in range(3)]
    rows += [shift_0[None]] + [vectors[n : n + 1] for n in range(3, 6)]
    for number, row in enumerate(rows):
        norm_grad = jnp.where(line == number, row, norm_grad)
    shard = D // 32
    pick = one_zero(iota((shard, D), 1) == iota((shard, D), 0) + me * shard).astype(BF16)
    normed = (unit * gain + norms_ref[4:5, :]).astype(BF16)
    mine = nt(pick, normed).astype(BF16)
    in_grad = nn(mine, proj_hi) + nn(mine, proj_lo)
    g_in[...] = in_grad

    def three(values):
        top, rest = split_two(values)
        return top, rest, (values - top.astype(F32) - rest.astype(F32)).astype(BF16)

    emb_grad = sum(nt(pick, part) for part in three(table_grad))
    g_emb[...] = emb_grad
    own_norm = sum(nt(part, pick) for part in three(norm_grad))[:8]
    g_norm[...] = own_norm
    return total_of(in_grad * in_grad) + total_of(emb_grad * emb_grad) + total_of(own_norm * own_norm)


PIECES = 21
GRAD_WIDTHS = (768, 768, 768, 768, 384, 1152, 384)
GRAD_UNITS = (
    (0, 0, 384, True),
    (0, 384, 384, True),
    (1, 0, 768, True),
    (2, 0, 768, True),
    (3, 0, 768, True),
    (4, 0, 384, False),
    (5, 0, 384, True),
    (5, 384, 384, True),
    (5, 768, 384, True),
    (6, 0, 384, False),
)
Z_FIRST = {1: 1, 5: 2}
BACKWARD_ORDER = (
    (),
    (),
    (),
    (),
    (),
    (),
    ((0, 0),),
    ((0, 1),),
    (),
    (),
    (),
    ((1, 0),),
    (),
    ((0, 2),),
    ((2, 0),),
    (),
    ((0, 3),),
    (),
    (),
    (),
    ((1, 1), (1, 2), (0, 4),),
    ((3, 0), (0, 5),),
    ((4, 0),),
    ((1, 3),),
    ((2, 1),),
    (),
    ((2, 2),),
    (),
    (),
    (),
    (),
    ((1, 4), (1, 5), (0, 6), (0, 7),),
    ((3, 1), (2, 3), (0, 8),),
    ((4, 1),),
    ((2, 4),),
    ((3, 2), (2, 5), (0, 9),),
    ((4, 2), (1, 6),),
    ((3, 3), (1, 7),),
    ((4, 3), (3, 5), (1, 8),),
    ((3, 4), (1, 9), (2, 6), (4, 4), (2, 7), (5, 0), (4, 5), (3, 6), (2, 8), (2, 9), (4, 6), (3, 7), (4, 7), (6, 0), (3, 8), (4, 8), (3, 9), (4, 9),),
)


class Kept(typing.NamedTuple):
    stream: typing.Any
    norms: typing.Any
    table: typing.Any
    proj_t: typing.Any
    extras: typing.Any
    moved: typing.Any
    grad_head: typing.Any
    touch: typing.Any
    value_two: typing.Any


class Early(typing.NamedTuple):
    slope: typing.Any
    active: typing.Any
    feed_normed_t: typing.Any
    unit_2: typing.Any
    rstd_2: typing.Any
    col_mixed_t: typing.Any
    col_proj: typing.Any
    col_prob: typing.Any
    col_normed_t: typing.Any
    unit_1: typing.Any
    rstd_1: typing.Any


class Late(typing.NamedTuple):
    row_mixed_t: typing.Any
    hot_all: typing.Any
    weight_hi: typing.Any
    prob: typing.Any
    hot_ri: typing.Any
    hot_ir: typing.Any


def pick_items(group, source):
    return [getattr(source, name) for name in group._fields]


def backward_kernel(*refs):
    widths = GRAD_WIDTHS
    count = len(widths)
    contact_head = refs[0]
    far = refs[1 : 1 + count]
    in_row_far = refs[1 + count]
    saved = Saved(*refs[2 + count : 2 + count + len(SAVED)])
    at = 2 + count + len(SAVED)
    outs = refs[at : at + count]
    g_in, g_emb, g_norm, stats = refs[at + count : at + count + 4]
    at += count + 4
    grads = refs[at : at + count]
    kept = Kept(*refs[at + count : at + count + len(Kept._fields)])
    at += count + len(Kept._fields)
    upstream, branch, branch_t, mixed = refs[at : at + 4]
    scratch = refs[at + 4 :]
    units = len(GRAD_UNITS)
    got_0, got_1a, got_1b, got_2a, got_2b, got_3, total, got_4 = (
        scratch[i * units : (i + 1) * units] for i in range(8)
    )
    table, table_out, table_got, square, square_got = scratch[8 * units : 8 * units + 5]
    table_send, table_recv, send, recv, local = scratch[8 * units + 5 :]
    z, y, k, c = place()
    me = (z * 4 + y * 2 + k) * 2 + c
    across, beside, twin = device(z, y, k, 1 - c), device(z, 1 - y, k, c), device(z, y, 1 - k, c)
    barrier = greet_all()
    stream = kept.stream
    square[...] = jnp.zeros(square.shape, F32)

    copies = {}

    def load(number, source, target):
        copies[number] = pltpu.make_async_copy(source, target, local.at[number])
        copies[number].start()

    def need(*numbers):
        for number in numbers:
            copies[number].wait()

    def weight(m):
        return len(SAVED) + m

    def copy(m, at, src, dst, target):
        return remote(src, dst, send.at[m, at], recv.at[m, at], target)

    low, high = pl.ds(0, 2), pl.ds(2, 2)
    every = slice(None)

    def where(u, cc, zz, yy):
        matrix, start, n, paired = GRAD_UNITS[u]
        index = spot(paired, cc, zz, yy, k)
        return index if n == widths[matrix] else (*index, every, pl.ds(start, n))

    def block(u, cc, zz, yy):
        return grads[GRAD_UNITS[u][0]].at[where(u, cc, zz, yy)]

    def ordered(u, cc, rest):
        return (*rest, cc) if GRAD_UNITS[u][3] else (cc, *rest)

    def twin_copy(u):
        matrix, start, n, paired = GRAD_UNITS[u]
        index = (1 - k,) if paired else (every, every, every, 1 - k)
        if n != widths[matrix]:
            index = (*index, *(every,) * (5 - len(index)), pl.ds(start, n))
        return copy(u, 0, grads[matrix].at[index], got_0[u], twin)

    def first(u):
        return [
            copy(u, 1, block(u, every, low, 1 - y), got_1a[u], beside),
            copy(u, 2, block(u, 1 - c, high, every), got_1b[u], across),
        ]

    def second(u):
        return [
            copy(u, 3, block(u, 1 - c, low, y), got_2a[u], across),
            copy(u, 4, block(u, c, high, 1 - y), got_2b[u], beside),
        ]

    def along(u):
        return [
            copy(
                u,
                4 + step,
                block(u, c, lax.rem(z + step, 4), y),
                got_3[u].at[step - 1],
                device(lax.rem(z + step, 4), y, k, c),
            )
            for step in (1, 3, 2)
        ]

    def z_first(u):
        return [
            copy(
                u,
                step,
                block(u, every, lax.rem(z + step, 4), every),
                got_1a[u].at[step - 1],
                device(lax.rem(z + step, 4), y, k, c),
            )
            for step in (1, 3, 2)
        ]

    def plane_first(u):
        if Z_FIRST[u] == 1:
            return [copy(u, 4, block(u, every, z, 1 - y), got_2a[u], beside)]
        return [copy(u, 4, block(u, 1 - c, z, every), got_2a[u], across)]

    def plane_second(u):
        if Z_FIRST[u] == 1:
            return [copy(u, 5, block(u, 1 - c, z, y), got_2b[u], across)]
        return [copy(u, 5, block(u, c, z, 1 - y), got_2b[u], beside)]

    def mine(u):
        return k if GRAD_UNITS[u][3] else c

    def pair(u):
        return [copy(u, 8, total[u].at[1 - mine(u)], got_4[u], twin if GRAD_UNITS[u][3] else across)]

    def peer(step):
        return lax.rem(me + step, 32)

    def source(step):
        return lax.rem(me + 32 - step, 32)

    def table_copy(step, back, index):
        target = (peer(step) // 2, lax.rem(peer(step), 2))
        if back:
            return remote(
                table_out.at[index], table_out.at[index], table_send.at[1, step], table_recv.at[1, step], target
            )
        return remote(
            table.at[index], table_got.at[me], table_send.at[0, step], table_recv.at[0, step], target
        )

    def table_start(step):
        @pl.when(peer(step) < PIECES)
        def _():
            table_copy(step, False, peer(step)).start()

    def table_wait_send(step):
        @pl.when(peer(step) < PIECES)
        def _():
            table_copy(step, False, 0).wait_send()

        @pl.when(me < PIECES)
        def _():
            table_copy(step, True, 0).wait_send()

    def table_wait_back(step):
        @pl.when(source(step) < PIECES)
        def _():
            table_copy(step, True, 0).wait_recv()

    def each(action):
        def body(step, carry):
            action(step)
            return carry

        lax.fori_loop(1, 32, body, 0)

    def gather_into(u, cc, zz, yy, *others):
        matrix = GRAD_UNITS[u][0]
        index = where(u, cc, zz, yy)
        value = grads[matrix][index].astype(F32) + got_0[u][ordered(u, cc, (zz, yy))].astype(F32)
        for other in others:
            value = value + other.astype(F32)
        grads[matrix][index] = value.astype(BF16)

    def from_line(u, cc, yy):
        index = (yy, cc) if GRAD_UNITS[u][3] else (cc, yy)
        return [got_1a[u][(step, *index)] for step in range(3)]

    def stage_first(u):
        twin_copy(u).wait_recv()
        if u in Z_FIRST:
            for step in (1, 3, 2):
                for cc in range(2):
                    for yy in range(2):
                        gather_into(u, cc, lax.rem(z + step, 4), yy)
            for item in z_first(u):
                item.start()
            return
        for a in range(2):
            for b in range(2):
                gather_into(u, a, b, 1 - y)
                gather_into(u, 1 - c, 2 + a, b)
        for item in first(u):
            item.start()

    def from_beside(u, cc, a):
        return got_1a[u][ordered(u, cc, (a,))]

    def stage_second(u):
        if u in Z_FIRST:
            for item in z_first(u):
                item.wait_recv()
            for a in range(2):
                cc, yy = (a, 1 - y) if Z_FIRST[u] == 1 else (1 - c, a)
                gather_into(u, cc, z, yy, *from_line(u, cc, yy))
            for item in plane_first(u):
                item.start()
            return
        for item in first(u):
            item.wait_recv()
        for a in range(2):
            gather_into(u, 1 - c, a, y, from_beside(u, 1 - c, a))
            gather_into(u, c, 2 + a, 1 - y, got_1b[u][a, 1 - y])
        for item in second(u):
            item.start()

    def stage_along(u):
        if u in Z_FIRST:
            for item in plane_first(u):
                item.wait_recv()
            cc, yy = (1 - c, y) if Z_FIRST[u] == 1 else (c, 1 - y)
            gather_into(u, cc, z, yy, *from_line(u, cc, yy), got_2a[u][cc if Z_FIRST[u] == 1 else yy])
            for item in plane_second(u):
                item.start()
            return
        for item in second(u):
            item.wait_recv()
        for a in range(2):
            gather_into(u, c, a, y, from_beside(u, c, a), got_2a[u][a])
            gather_into(u, c, 2 + a, y, got_1b[u][a, y], got_2b[u][a])
        for item in along(u):
            item.start()

    def stage_pair(u):
        full = grads[GRAD_UNITS[u][0]][where(u, c, z, y)].astype(F32)
        if u in Z_FIRST:
            for item in plane_second(u):
                item.wait_recv()
            others = [got_0[u][ordered(u, c, (z, y))], *from_line(u, c, y)]
            others += [got_2a[u][c if Z_FIRST[u] == 1 else y], got_2b[u][...]]
        else:
            for item in along(u):
                item.wait_recv()
            others = [got_3[u][step] for step in range(3)]
        for other in others:
            full = full + other.astype(F32)
        total[u][0] = full[:24]
        total[u][1] = full[24:]
        for item in pair(u):
            item.start()

    def stage_end(u):
        matrix, start, n, _ = GRAD_UNITS[u]
        lanes = slice(start, start + n)
        side = mine(u)
        outs[matrix][side, :, lanes] = total[u][side]
        for item in pair(u):
            item.wait_recv()
        outs[matrix][1 - side, :, lanes] = got_4[u][...]
        own, other = total[u][side], got_4[u][...]
        square[...] += jnp.broadcast_to(total_of(own * own) + total_of(other * other), (8, 128))
        if u in Z_FIRST:
            sent = z_first(u) + plane_first(u) + plane_second(u)
        else:
            sent = first(u) + second(u) + along(u)
        for item in [twin_copy(u)] + sent:
            item.wait_send()

    def table_sum(u):
        @pl.when(me < PIECES)
        def _():
            each(lambda step: table_copy(step, False, 0).wait_recv())
            table_got[me] = table[me]

            def add(at, held):
                return held + table_got[at].astype(F32)

            total_rows = lax.fori_loop(1, 32, add, table_got[0].astype(F32))
            top, rest = split_two(total_rows[:8] + total_rows[8:])
            exact = jnp.concatenate([top.astype(F32), rest.astype(F32)], 0)
            table_out[me] = jnp.where(me >= 18, exact, total_rows).astype(BF16)
            each(lambda step: table_copy(step, True, me).start())

    late_parts = []

    def table_end(u):
        each(table_wait_back)
        need(weight(count))
        found = table_finish(
            table_out, upstream, kept.table, kept.norms, kept.proj_t, late_parts[0].reshape(2, D, 1152), g_in, g_emb, g_norm
        )
        square[...] += jnp.broadcast_to(found, (8, 128))

    stages = (stage_first, stage_second, stage_along, stage_pair, stage_end, table_sum, table_end)
    pending = list(BACKWARD_ORDER)

    def hook():
        for stage, u in pending.pop(0):
            stages[stage](u)

    def done(u):
        if u == 0:
            pl.semaphore_wait(barrier, 31)
        twin_copy(u).start()
        hook()

    names = Kept._fields
    for name in names:
        load(getattr(AT, name), getattr(saved, name), getattr(kept, name))

    load(AT.branch, saved.branch, branch)

    def phase_one(*early_refs):
        e = Early(*early_refs)
        load(weight(0), far[0], grads[0])
        load(AT.slope, saved.slope, e.slope)
        load(AT.active, saved.active, e.active)
        for m in (1, 2, 3):
            load(weight(m), far[m], grads[m])
        for name in Early._fields[2:6]:
            load(getattr(AT, name), getattr(saved, name), getattr(e, name))
        load(weight(4), far[4], grads[4])
        for name in Early._fields[6:8]:
            load(getattr(AT, name), getattr(saved, name), getattr(e, name))
        load(weight(5), far[5], grads[5])
        for name in Early._fields[8:]:
            load(getattr(AT, name), getattr(saved, name), getattr(e, name))
        load(weight(6), far[6], grads[6])
        view = [g.reshape(2, D, n) for g, n in zip(grads, widths)]
        need(*(getattr(AT, name) for name in names))
        norms = kept.norms[...]

        def gain(number):
            return norms[number : number + 1, :]

        need(AT.branch)
        transpose_into(branch, branch_t)
        hook()

        def grad_tile(m, start, left_t, right, half, at):
            lanes = slice(start + half * widths[m] + at, start + half * widths[m] + at + 384)
            view[m][half, :, at : at + 384] = nn(left_t[...], right[:, lanes]).astype(BF16)

        def grad_half(m, start, left_t, right, half):
            for at in range(0, widths[m], 384):
                grad_tile(m, start, left_t, right, half, at)

        for part in range(2):
            need(weight(part))
            if part == 0:
                need(AT.slope)

            def down_back(half, at, part=part):
                lanes = slice(part * 1536 + half * 768 + at, part * 1536 + half * 768 + at + 384)
                back = nn(branch[...], view[part][half, :, at : at + 384])
                e.slope[:, lanes] = (back * e.slope[:, lanes].astype(F32)).astype(BF16)

            if part == 0:
                for at in (0, 384):
                    for half in range(2):
                        down_back(half, at)
                    hook()
                    if at == 0:
                        need(AT.active)
                    for half in range(2):
                        grad_tile(part, 0, branch_t, e.active, half, at)
                    done(at // 384)
            else:
                for half in range(2):
                    for at in (0, 384):
                        down_back(half, at)
                    hook()
                grad_half(part, part * 1536, branch_t, e.active, 0)
                hook()
                grad_half(part, part * 1536, branch_t, e.active, 1)
                done(2)
        for part in range(2):
            need(weight(2 + part))
            for half in range(2):
                start = part * 1536 + half * 768
                back = nt(e.slope[:, start : start + 768], view[2 + part][half])
                upstream[...] = back if start == 0 else upstream[...] + back
                hook()
            if part == 0:
                need(AT.feed_normed_t)
            grad_half(2 + part, part * 1536, e.feed_normed_t, e.slope, 0)
            hook()
            grad_half(2 + part, part * 1536, e.feed_normed_t, e.slope, 1)
            done(3 + part)
        need(AT.unit_2, AT.rstd_2)
        scale_2, shift_2 = back_rows(e.unit_2, e.rstd_2, gain(2), upstream, stream, branch, False)
        hook()
        need(weight(4), AT.col_mixed_t)
        mixed[...] = (nt(branch[:, :384], view[4][0]) + nt(branch[:, 384:], view[4][1])).astype(BF16)
        hook()
        for half in range(2):
            grad_half(4, 0, e.col_mixed_t, branch, half)
        done(5)
        need(AT.col_proj, AT.col_prob)
        proj = e.active

        def attend(at, carry):
            rows = pl.ds(pl.multiple_of((at // PAIRS) * 128, 128), 128)
            lane = lax.rem(at, PAIRS) * 128

            def lanes(part):
                return pl.ds(pl.multiple_of(part * D + lane, 128), 128)

            query = stacked(e.col_proj[rows, lanes(0)])
            key = e.col_proj[rows, lanes(1)]
            value = e.col_proj[rows, lanes(2)]
            above = stacked(mixed[rows, lanes(0)])
            prob = e.col_prob[at]
            grad = nt(above, value)
            grad = prob * (grad - jnp.sum(prob * grad, -1, keepdims=True))
            small = grad.astype(BF16)
            scale = HD ** (-0.5)
            proj[rows, lanes(0)] = (unstacked(nn(small, key), 128) * scale).astype(BF16)
            proj[rows, lanes(1)] = (tn(small, query) * scale).astype(BF16)
            proj[rows, lanes(2)] = tn(prob.astype(BF16), above).astype(BF16)
            return carry

        for part in range(6):
            lax.fori_loop(4 * part, 4 * part + 4, attend, 0, unroll=4)
            hook()
        need(weight(5))
        for half in range(2):
            back = nt(proj[:, half * 1152 : half * 1152 + 1152], view[5][half])
            upstream[...] = back if half == 0 else upstream[...] + back
            hook()
        need(AT.col_normed_t)
        for third in range(3):
            for half in range(2):
                grad_tile(5, 0, e.col_normed_t, proj, half, third * 384)
            done(6 + third)
        need(AT.unit_1, AT.rstd_1)
        scale_1, shift_1 = back_rows(e.unit_1, e.rstd_1, gain(1), upstream, stream, branch, False)
        hook()
        need(weight(6))
        mixed[...] = (nt(branch[:, :384], view[6][0]) + nt(branch[:, 384:], view[6][1])).astype(BF16)
        line = iota((8, D), 0)
        vectors = jnp.zeros((8, D), F32)
        moved = kept.moved[...]
        rows = (scale_1, scale_2, moved[0:1], shift_1, shift_2, moved[1:2])
        for number, row in enumerate(rows):
            vectors = jnp.where(line == number, row, vectors)
        extras = jnp.concatenate([kept.extras[0:1, :], jnp.zeros((1, D - 128), F32)], 1)
        kept.moved[...] = jnp.where(line == 6, extras, vectors)
        hook()

    pl.run_scoped(phase_one, *(pltpu.VMEM(*item) for item in pick_items(Early, SAVED)))

    def phase_two(*late_refs):
        e = Late(*late_refs[:-3])
        in_row, left_hi, left_lo = late_refs[-3:]
        for name in Late._fields:
            load(getattr(AT, name), getattr(saved, name), getattr(e, name))
        load(weight(count), in_row_far, in_row)
        view = grads[6].reshape(2, D, widths[6])
        late_parts.append(in_row)
        need(AT.row_mixed_t)
        for half in range(2):
            lanes = slice(half * 384, half * 384 + 384)
            view[half] = nn(e.row_mixed_t[...], branch[:, lanes]).astype(BF16)
        done(9)
        need(AT.hot_all, AT.weight_hi, AT.prob, AT.hot_ri, AT.hot_ir)
        shape = (HERE, HERE)
        back = (
            ((iota(shape, 1) >> 4) == (iota(shape, 0) & 31))
            & ((iota(shape, 1) & 15) == (iota(shape, 0) >> 5))
        )
        mixed[...] = nn(one_zero(back).astype(BF16), mixed[...]).astype(BF16)
        value_rows = []
        for hp in range(PAIRS):
            lanes = slice(hp * 128, hp * 128 + 128)
            part = mixed[:, lanes]
            upstream[:, lanes] = nt(part, kept.value_two[hp])
            value_rows.append(unstacked(tn(e.weight_hi[:, lanes], part), 64))
        hook()
        split_heads_to(upstream, left_hi, left_lo)
        hook()
        hot_all = e.hot_all[...]
        grad = nn(left_hi[...], hot_all) + nn(left_lo[...], hot_all)
        extra = jnp.concatenate(
            [kept.touch[...] * (contact_head[h] * COLS) for h in range(HEADS)], 0
        )
        grad = grad + extra
        prob = e.prob[...]
        grad = prob * (grad - jnp.sum(prob * grad, -1, keepdims=True))
        low_grad = grad.astype(BF16)
        hook()
        merge_heads(low_grad, e.hot_all, branch, None)
        hook()
        table_pair = nn(e.hot_ri[...], branch[...])
        stream_hi, stream_lo = split_two(stream[...])
        hot_ir = e.hot_ir[...]
        table_grad = kept.grad_head[...] + nn(hot_ir, stream_hi) + nn(hot_ir, stream_lo)
        value_grad = jnp.concatenate(value_rows, 1)
        last = jnp.where(iota((8, D), 0) == 7, table_grad[32:33], kept.moved[...])
        top, rest = split_two(last)
        groups = [table_pair[4:20], table_pair[20:36], value_grad[4:20], value_grad[20:36]]
        groups += [table_grad[0:16], table_grad[16:32]]
        groups += [jnp.concatenate([top.astype(F32), rest.astype(F32)], 0)]
        for number, group in enumerate(groups):
            for third in range(3):
                table[3 * number + third] = group[:, third * 256 : third * 256 + 256].astype(BF16)
        each(table_start)
        hook()
        hook()

    pl.run_scoped(
        phase_two,
        *(pltpu.VMEM(*item) for item in pick_items(Late, SAVED)),
        pltpu.VMEM((2, NZ, NY, 2, 48, 1152), BF16),
        pltpu.VMEM((HEADS * WIDE, ROWS * VP), BF16),
        pltpu.VMEM((HEADS * WIDE, ROWS * VP), BF16),
    )
    assert not pending

    def square_copy(step):
        other = lax.rem(me + step, 32)
        return remote(
            square, square_got.at[me], table_send.at[2, step], table_recv.at[2, step], (other // 2, lax.rem(other, 2))
        )

    each(lambda step: square_copy(step).start())
    square_got[me] = square[...]
    each(lambda step: table_wait_send(step))
    for u in range(units):
        for item in pair(u):
            item.wait_send()
    each(lambda step: square_copy(step).wait())
    total_square = lax.fori_loop(1, 32, lambda at, held: held + square_got[at], square_got[0])[0:1]
    vector = table_out[18].astype(F32)
    vector = vector[6:7, :128] + vector[14:15, :128]
    counted = kept.extras[1:2, :]
    column = iota((1, 128), 1)
    contact = jnp.where(column <= HEADS, vector, 0.0)
    total_square = total_square + total_of(contact * contact)
    grad_norm = jnp.sqrt(total_square)
    factor = jnp.minimum(1.0, MAX_NORM / grad_norm)
    losses = (
        (0, vector[:, HEADS + 1 : HEADS + 2]),
        (1, counted[:, 0:1]),
        (2, vector[:, HEADS + 2 : HEADS + 3]),
        (3, counted[:, 1:2]),
    )
    loss_row = jnp.zeros((1, 128), F32)
    for at, value in losses:
        loss_row = jnp.where(column == at, value, loss_row)
    number = iota((8, 128), 0)
    result = jnp.zeros((8, 128), F32)
    for at, row in enumerate((contact, counted, factor, grad_norm, loss_row)):
        result = jnp.where(number == at, row, result)
    stats[...] = result


def backward_call(contact_head, weights, in_row, saved):
    widths = GRAD_WIDTHS
    count = len(widths)
    inside = pl.BlockSpec(memory_space=pltpu.VMEM)
    anywhere = pl.BlockSpec(memory_space=pl.ANY)

    units = len(GRAD_UNITS)

    def shapes(lead, dtype, other=None):
        leads = [other if other and u in Z_FIRST else lead for u in range(units)]
        return [pltpu.VMEM((*at, n), dtype) for at, (_, _, n, _) in zip(leads, GRAD_UNITS)]

    outs = pl.pallas_call(
        backward_kernel,
        out_shape=[jax.ShapeDtypeStruct((2, 24, n), F32) for n in widths]
        + [
            jax.ShapeDtypeStruct((24, 3 * D), F32),
            jax.ShapeDtypeStruct((24, VP), F32),
            jax.ShapeDtypeStruct((8, 24), F32),
            jax.ShapeDtypeStruct((8, 128), F32),
        ],
        in_specs=[pl.BlockSpec(memory_space=pltpu.SMEM)] + [anywhere] * (1 + count + len(SAVED)),
        out_specs=[inside] * (4 + count),
        scratch_shapes=[pltpu.VMEM((2, NZ, NY, 2, 48, n), BF16) for n in widths]
        + [pltpu.VMEM(*item) for item in pick_items(Kept, SAVED)]
        + [
            pltpu.VMEM((HERE, D), F32),
            pltpu.VMEM((HERE, D), BF16),
            pltpu.VMEM((D, HERE), BF16),
            pltpu.VMEM((HERE, D), BF16),
        ]
        + [
            pltpu.VMEM((NZ, NY, 2, 48, n) if paired else (2, NZ, NY, 48, n), BF16)
            for _, _, n, paired in GRAD_UNITS
        ]
        + shapes((2, 2, 48), BF16, (3, 2, 2, 48))
        + shapes((2, 2, 48), BF16, (16,))
        + shapes((2, 48), BF16, (2, 48))
        + shapes((2, 48), BF16, (48,))
        + shapes((3, 48), BF16, (16,))
        + shapes((2, 24), F32)
        + shapes((24,), F32)
        + [
            pltpu.VMEM((PIECES, 16, 256), BF16),
            pltpu.VMEM((PIECES, 16, 256), BF16),
            pltpu.VMEM((32, 16, 256), BF16),
            pltpu.VMEM((8, 128), F32),
            pltpu.VMEM((32, 8, 128), F32),
            pltpu.SemaphoreType.DMA((3, 32)),
            pltpu.SemaphoreType.DMA((3, 32)),
            pltpu.SemaphoreType.DMA((units, 9)),
            pltpu.SemaphoreType.DMA((units, 9)),
            pltpu.SemaphoreType.DMA((len(SAVED) + count + 1,)),
        ],
        compiler_params=pltpu.CompilerParams(
            collective_id=1, has_side_effects=True, vmem_limit_bytes=63 * 2**20
        ),
    )(contact_head, *weights, in_row, *saved)
    return outs[:count], outs[count:]


UPDATE_RATES = (LEARN_RATE,) * 4 + (VECTOR_RATE,) * 3


def update_kernel(*refs):
    given, far, held, results = refs[:32], refs[32:60], refs[60:92], refs[92:120]
    sems, out_sems = refs[120:122]
    outs, copies = results[:21], results[21:26]
    loss_ref, norm_ref = results[26:]

    def leave(*numbers):
        for n in numbers:
            pltpu.make_async_copy(results[n], far[n], out_sems.at[n]).start()

    moves = [pltpu.make_async_copy(a, b, sems.at[n]) for n, (a, b) in enumerate(zip(given, held))]
    for item in moves:
        item.start()
    reduced, g_in, g_emb, g_norm, stats = held[:7], held[7], held[8], held[9], held[10]
    states = [held[11 + 3 * n : 14 + 3 * n] for n in range(7)]
    outs = [outs[3 * n : 3 * n + 3] for n in range(7)]
    order = feature_order()
    for item in moves[4:11]:
        item.wait()
    factor = stats[2:3, 0:1]
    loss_ref[...] = stats[4:5, 0:4]
    norm_ref[...] = stats[3:4, 0:1]

    def natural(values):
        top, rest = split_two(values)
        last = (values - top.astype(F32) - rest.astype(F32)).astype(BF16)
        return nt(top, order) + nt(rest, order) + nt(last, order)

    def update(number, where, grad):
        master, first, second = (ref[where] for ref in states[number])
        new, first, second = adam_update(master, first, second, grad * factor, UPDATE_RATES[number])
        for ref, value in zip(outs[number], (new, first, second)):
            ref[where] = value
        if number < 5:
            copies[number][where] = new.astype(BF16)

    every = slice(None)
    g_out_col, g_in_col, g_out_row = reduced[4:]
    for item in moves[11:17]:
        item.wait()
    for half in range(2):
        lanes = slice(half * 1152, half * 1152 + 1152)
        update(0, (0, every, lanes), g_in[:, lanes])
        update(0, (1, every, lanes), g_in_col[half])
        lanes = slice(half * 384, half * 384 + 384)
        update(1, (0, every, lanes), natural(g_out_row[half]))
        update(1, (1, every, lanes), natural(g_out_col[half]))
    leave(0, 1, 2, 21, 3, 4, 5, 22, 26, 27)
    for item in moves[:4] + moves[17:]:
        item.wait()
    for half in range(2):
        for part in range(2):
            start = part * 1536 + half * 768
            lanes = slice(start, start + 768)
            update(2, (every, lanes), reduced[2 + part][half])
            update(3, (every, lanes), reduced[part][half])
    leave(6, 7, 8, 23, 9, 10, 11, 24)
    update(4, (every, every), g_emb[:, :VOCAB])
    update(5, (every, every), g_norm[...])
    update(6, (every, every), stats[0:1, : HEADS + 1])
    leave(12, 13, 14, 25, 15, 16, 17, 18, 19, 20)
    for n in range(28):
        pltpu.make_async_copy(results[n], far[n], out_sems.at[n]).wait()


def update_call(reduced, g_in, g_emb, g_norm, stats, states):
    anywhere = pl.BlockSpec(memory_space=pl.ANY)
    flat = [item for state in states for item in state]
    shapes = [jax.ShapeDtypeStruct(item.shape, F32) for item in flat]
    shapes += [jax.ShapeDtypeStruct(states[n][0].shape, BF16) for n in range(5)]
    shapes += [jax.ShapeDtypeStruct((1, 4), F32), jax.ShapeDtypeStruct((1, 1), F32)]
    given = (*reduced, g_in, g_emb, g_norm, stats, *flat)
    return pl.pallas_call(
        update_kernel,
        out_shape=shapes,
        in_specs=[anywhere] * len(given),
        out_specs=[anywhere] * len(shapes),
        scratch_shapes=[pltpu.VMEM(item.shape, F32) for item in given]
        + [pltpu.VMEM(item.shape, item.dtype) for item in shapes]
        + [
            pltpu.SemaphoreType.DMA((len(given),)),
            pltpu.SemaphoreType.DMA((len(shapes),)),
            pltpu.VMEM((44, 512, 512), F32),
        ],
        compiler_params=pltpu.CompilerParams(vmem_limit_bytes=62 * 2**20),
    )(*given)


def adam_update(master, first, second, grad_part, rate):
    first = BETA_ONE * first + (1.0 - BETA_ONE) * grad_part
    second = BETA_TWO * second + (1.0 - BETA_TWO) * grad_part * grad_part
    scaled = first * (1.0 / (1.0 - BETA_ONE**STEP))
    moved = scaled / (jnp.sqrt(second * (1.0 / (1.0 - BETA_TWO**STEP))) + ADAM_EPS)
    return (master - rate * (moved + WEIGHT_DECAY * master), first, second)


def shards(
    tokens,
    targets,
    masked,
    contact_pairs,
    labels,
    attention_in_master,
    attention_in_first,
    attention_in_second,
    attention_out_master,
    attention_out_first,
    attention_out_second,
    feed_up_master,
    feed_up_first,
    feed_up_second,
    feed_down_master,
    feed_down_first,
    feed_down_second,
    embedding_master,
    embedding_first,
    embedding_second,
    norm_params_master,
    norm_params_first,
    norm_params_second,
    contact_head_master,
    contact_head_first,
    contact_head_second,
):
    both = ("seq", "col")
    micro, rows_here, cols_here = tokens.shape
    ncol = lax.axis_size("col")
    ndev = lax.axis_size("seq") * ncol
    cols = cols_here * ncol
    me = lax.axis_index("seq") * ncol + lax.axis_index("col")
    per = ndev // micro
    cw = cols // per
    mine = me // per
    base = (me % per) * cw
    shard = D // ndev

    tiled = lax.axis_size("seq") == 16 and ncol == 2
    if tiled:
        raw = (
            tokens,
            targets,
            masked,
            contact_pairs.transpose(0, 2, 1),
            labels,
            embedding_master.T,
            norm_params_master,
            attention_in_master,
            attention_out_master,
            feed_up_master,
            feed_down_master.T,
        )
        weights, saved = forward_call(raw, contact_head_master)
        reduced, (g_in, g_emb, g_norm, stats) = backward_call(
            contact_head_master, [weights[n] for n in (7, 8, 5, 6, 4, 3, 2)], weights[1], saved
        )
        states = (
            (attention_in_master, attention_in_first, attention_in_second),
            (attention_out_master, attention_out_first, attention_out_second),
            (feed_up_master, feed_up_first, feed_up_second),
            (feed_down_master.T, feed_down_first.T, feed_down_second.T),
            (embedding_master.T, embedding_first.T, embedding_second.T),
            (norm_params_master, norm_params_first, norm_params_second),
            (contact_head_master[None], contact_head_first[None], contact_head_second[None]),
        )
        outs = update_call(reduced, g_in, g_emb, g_norm, stats, states)
        return (
            *outs[:9],
            *(item.T for item in outs[9:15]),
            *outs[15:18],
            *(item[0] for item in outs[18:21]),
            *outs[21:24],
            *(item.T for item in outs[24:26]),
            outs[26][0],
            outs[27][0, 0],
        )
    inputs = jnp.where(masked > 0, MASK_ID, tokens)
    masters = [
        jnp.concatenate(
            [
                jnp.pad(embedding_master.T, ((0, 0), (0, 128 - VOCAB))),
                jnp.pad(norm_params_master.T, ((0, 0), (0, 120))),
            ],
            1,
        ),
        attention_in_master[0],
        attention_out_master[0],
        attention_in_master[1],
        attention_out_master[1],
        feed_up_master,
        feed_down_master.T,
    ]
    whole = jnp.stack([inputs, targets])
    whole = lax.all_gather(lax.all_gather(whole, "col", axis=3, tiled=True), "seq", axis=2, tiled=True)
    pairs_all = lax.all_gather(
        jnp.concatenate([contact_pairs, labels[:, :, None]], -1), both, axis=1, tiled=True
    )
    gathered = []
    for master in masters:
        full = lax.all_gather(master.astype(BF16), both, axis=0, tiled=True)
        gathered.append(full.reshape(D, 2, -1).transpose(1, 0, 2))
    counts = (
        jnp.sum(whole[0] == MASK_ID).astype(F32),
        jnp.sum(pairs_all[..., 2] >= 0).astype(F32),
    )
    ids_all = lax.dynamic_index_in_dim(whole[0], mine, 0, False)
    ids_local = lax.dynamic_slice_in_dim(ids_all, base, cw, 1)
    targets_local = lax.dynamic_slice_in_dim(
        lax.dynamic_index_in_dim(whole[1], mine, 0, False), base, cw, 1
    )
    pairs = lax.dynamic_index_in_dim(pairs_all, mine, 0, False)

    table = gathered[0][0][:, :VP].T
    norms = gathered[0][1][:, :8].T.astype(F32)
    in_row, out_row, in_col, out_col, up_w, down_t = (
        jnp.concatenate([g[0], g[1]], 1) for g in gathered[1:]
    )
    big = (in_row, in_col, out_row, out_col, up_w, down_t)

    grads, tables, contact_total, mlm_total, bce_total, kept = step(
        big,
        table,
        norms,
        contact_head_master,
        ids_all,
        ids_local.reshape(-1),
        ids_local.T.reshape(-1),
        targets_local.T.reshape(-1),
        pairs[:, 0] - base,
        pairs[:, 1],
        pairs[:, 2],
        counts,
        cw,
    )
    table_pair, value_grad, table_grad, vectors = tables
    extras = jnp.zeros((2, D), F32).at[0, : HEADS + 3].set(
        jnp.concatenate([contact_total, mlm_total[None], bce_total[None]])
    )
    sums = jnp.concatenate([table_pair[:40], value_grad[:40], table_grad[:40], vectors, extras])
    flat_grad = jnp.concatenate([g.astype(BF16) for g in grads], 1)
    reduced = lax.psum_scatter(flat_grad, both, scatter_dimension=0, tiled=True).astype(F32)
    g_in_col, g_out_row, g_out_col, g_up, g_down = jnp.split(
        reduced, [3 * D, 4 * D, 5 * D, 5 * D + FF], 1
    )
    sums = lax.psum(sums, both)
    unit_t, rstd_t, normed_t, query_t, key_t = kept
    rows_all = ids_all.shape[0]
    spare = ((0, VP - 40), (0, 0))
    table_pair, value_grad, table_grad = (
        jnp.pad(sums[a : a + 40], spare) for a in (0, 40, 80)
    )
    vectors = sums[120:126]
    contact_grad, mlm_total, bce_total = (
        sums[126, : HEADS + 1], sums[126, HEADS + 1], sums[126, HEADS + 2]
    )
    row_scale = (HD * rows_all) ** (-0.5)
    query_grad = []
    key_grad = []
    for h in range(HEADS):
        pair = heads_of(table_pair, h)
        query_grad.append(jnp.dot(pair, heads_of(key_t, h).astype(F32), precision=PRECISE))
        key_grad.append(jnp.dot(pair.T, heads_of(query_t, h).astype(F32), precision=PRECISE))
    proj_grad = jnp.concatenate(
        [
            jnp.concatenate(query_grad, 1) * row_scale,
            jnp.concatenate(key_grad, 1) * row_scale,
            value_grad,
        ],
        1,
    )
    proj_hi, proj_lo = split_two(proj_grad)
    normed_grad = nt(proj_hi, in_row) + nt(proj_lo, in_row)
    back_t, scale_0, shift_0 = norm_back(unit_t, rstd_t, norms[0], normed_grad)
    table_grad = table_grad + back_t
    low = me * shard
    normed_mine = lax.dynamic_slice_in_dim(normed_t, low, shard, 1)
    grad_in_row = tn(normed_mine, proj_hi) + tn(normed_mine, proj_lo)
    norm_grad = jnp.concatenate([scale_0[None], vectors[:3], shift_0[None], vectors[3:]])
    table_mine = lax.dynamic_slice_in_dim(table_grad[:VOCAB], low, shard, 1)
    norm_mine = lax.dynamic_slice_in_dim(norm_grad, low, shard, 1)
    reduced_all = (g_in_col, g_out_row, g_out_col, g_up, g_down)

    local_square = (
        sum(jnp.sum(g * g) for g in reduced_all)
        + jnp.sum(grad_in_row * grad_in_row)
        + jnp.sum(table_mine * table_mine)
        + jnp.sum(norm_mine * norm_mine)
    )
    square = lax.psum(local_square, both) + jnp.sum(contact_grad * contact_grad)
    grad_norm = jnp.sqrt(square)
    factor = jnp.minimum(1.0, MAX_NORM / grad_norm)
    in_new, in_moment, in_square = adam_update(
        attention_in_master, attention_in_first, attention_in_second, jnp.stack([grad_in_row, g_in_col]) * factor, LEARN_RATE
    )
    out_new, out_moment, out_square = adam_update(
        attention_out_master, attention_out_first, attention_out_second, jnp.stack([g_out_row, g_out_col]) * factor, LEARN_RATE
    )
    up_new, up_moment, up_square = adam_update(
        feed_up_master, feed_up_first, feed_up_second, g_up * factor, LEARN_RATE
    )
    down_new, down_moment, down_square = adam_update(
        feed_down_master, feed_down_first, feed_down_second, g_down.T * factor, LEARN_RATE
    )
    table_new, table_moment, table_square = adam_update(
        embedding_master, embedding_first, embedding_second, table_mine * factor, VECTOR_RATE
    )
    norm_new, norm_moment, norm_square = adam_update(
        norm_params_master, norm_params_first, norm_params_second, norm_mine * factor, VECTOR_RATE
    )
    head_new, head_moment, head_square = adam_update(
        contact_head_master, contact_head_first, contact_head_second, contact_grad * factor, VECTOR_RATE
    )
    loss_parts = jnp.stack([mlm_total, counts[0], bce_total, counts[1]])
    return (
        in_new, in_moment, in_square,
        out_new, out_moment, out_square,
        up_new, up_moment, up_square,
        down_new, down_moment, down_square,
        table_new, table_moment, table_square,
        norm_new, norm_moment, norm_square,
        head_new, head_moment, head_square,
        in_new.astype(BF16), out_new.astype(BF16), up_new.astype(BF16), down_new.astype(BF16), table_new.astype(BF16),
        loss_parts, grad_norm,
    )


def solution(mesh):
    both = ("seq", "col")
    cells = P(None, "seq", "col")
    stack = P(None, both, None)
    row_split = P(both, None)
    col_split = P(None, both)
    weights = [stack] * 6 + [row_split] * 3 + [col_split] * 9 + [P()] * 3
    return jax.shard_map(
        shards,
        mesh=mesh,
        in_specs=(cells, cells, cells, stack, col_split, *weights),
        out_specs=(*weights, stack, stack, row_split, col_split, col_split, P(), P()),
        check_vma=False,
    )
```

```python
import typing

import jax
import jax.numpy as jnp
from jax import lax
from jax.experimental import pallas as pl
from jax.experimental.pallas import tpu as pltpu
from jax.sharding import PartitionSpec as P

D = 768
HEADS = 12
HD = 64
FF = 3072
VOCAB = 33
VP = 64
STEP = 10

NORM_EPS = 1e-05
MASK_ID = 32
MAX_NORM = 0.001
LEARN_RATE = 0.05
VECTOR_RATE = 0.5
BETA_ONE = 0.9
BETA_TWO = 0.95
ADAM_EPS = 1e-08
WEIGHT_DECAY = 0.01
PRECISE = lax.Precision.HIGHEST
F32 = jnp.float32
BF16 = jnp.bfloat16


def nn(left, right):
    return lax.dot_general(left, right, (((1,), (0,)), ((), ())), preferred_element_type=F32)


def tn(left, right):
    return lax.dot_general(left, right, (((0,), (0,)), ((), ())), preferred_element_type=F32)


def nt(left, right):
    return lax.dot_general(left, right, (((1,), (1,)), ((), ())), preferred_element_type=F32)


def split_two(values):
    high = values.astype(BF16)
    return high, (values - high.astype(F32)).astype(BF16)


def norm_stats(values):
    centre = values - jnp.mean(values, -1, keepdims=True)
    rstd = lax.rsqrt(jnp.mean(centre * centre, -1, keepdims=True) + NORM_EPS)
    return centre * rstd, rstd


def norm_back(unit, rstd, scale_vec, upstream):
    inner = upstream * scale_vec
    grad = rstd * (
        inner - jnp.mean(inner, -1, keepdims=True) - unit * jnp.mean(inner * unit, -1, keepdims=True)
    )
    return grad, jnp.sum(upstream * unit, 0), jnp.sum(upstream, 0)


GELU_K = 0.7978845608028654
GELU_C = 0.044715


def gelu_parts(up):
    square = up * up
    bent = jnp.tanh(GELU_K * up * (1.0 + GELU_C * square))
    half = 0.5 * (1.0 + bent)
    slope = half + 0.5 * up * (1.0 - bent * bent) * GELU_K * (1.0 + 3.0 * GELU_C * square)
    return up * half, slope


def heads_of(block, head):
    return block[:, head * HD : (head + 1) * HD]


def step(big, table, norms, contact_head, ids_all, ids_ri, ids_ir, targets_ir, pair_first, pair_second, labels, counts, cw):
    in_row, in_col, out_row, out_col, up_w, down_t = big
    rows, cols = ids_all.shape
    here = rows * cw
    row_scale = (HD * rows) ** (-0.5)
    vocab = jnp.arange(VP)[:, None]
    hot_all = (ids_all[:, None, :] == vocab[None]).astype(BF16).reshape(rows * VP, cols)
    hot_ri = (ids_ri[None, :] == vocab).astype(BF16)
    hot_ir = (ids_ir[None, :] == vocab).astype(BF16)
    spot = jnp.arange(here)
    perm = (
        ((spot // rows)[:, None] == (spot % cw)[None, :])
        & ((spot % rows)[:, None] == (spot // cw)[None, :])
    ).astype(BF16)

    def to_heads(block):
        return block.reshape(rows, cw, HEADS, VP).transpose(2, 1, 0, 3).reshape(HEADS * cw, rows * VP)

    def to_tokens(block):
        return block.reshape(HEADS, cw, rows, VP).transpose(2, 1, 0, 3).reshape(here, HEADS * VP)

    def per_head(block, other, how):
        return jnp.concatenate(
            [how(heads_of(block, h), heads_of(other, h)) for h in range(HEADS)], -1
        )

    table_f = table.astype(F32)
    unit_t, rstd_t = norm_stats(table_f)
    normed_t = (unit_t * norms[0] + norms[4]).astype(BF16)
    proj_t = nn(normed_t, in_row).astype(BF16)
    query_t, key_t, value_t = proj_t[:, :D], proj_t[:, D : 2 * D], proj_t[:, 2 * D :]

    pair_t = per_head(query_t, key_t, nt)
    pair_hi, pair_lo = split_two(pair_t)
    left_hi = to_heads(tn(hot_ri, pair_hi).astype(BF16))
    left_lo = to_heads(tn(hot_ri, pair_lo).astype(BF16))
    score = (nn(left_hi, hot_all) + nn(left_lo, hot_all)) * row_scale
    prob = jax.nn.softmax(score, axis=-1)
    prob_low = prob.astype(BF16)
    weight_t = to_tokens(nt(prob_low, hot_all))
    weight_hi, weight_lo = split_two(weight_t)
    row_mixed_ri = (
        per_head(weight_hi, value_t, nn) + per_head(weight_lo, value_t, nn)
    ).astype(BF16)
    row_mixed = nn(perm, row_mixed_ri).astype(BF16)
    embedded = tn(hot_ir, table)
    after_row = embedded + nn(row_mixed, out_row)

    prob_cube = prob_low.astype(F32).reshape(HEADS, cw, cols)
    head_sum = jnp.sum(prob_cube * contact_head[:HEADS, None, None], 0)
    first_hot = (pair_first[None, :] == jnp.arange(cw)[:, None]).astype(F32)
    second_hot = (pair_second[None, :] == jnp.arange(cols)[:, None]).astype(BF16)
    sum_hi, sum_lo = split_two(head_sum)
    sum_last = (head_sum - sum_hi.astype(F32) - sum_lo.astype(F32)).astype(BF16)
    picked = nn(sum_hi, second_hot) + nn(sum_lo, second_hot) + nn(sum_last, second_hot)
    contact_logit = jnp.sum(picked * first_hot, 0) * cols + contact_head[HEADS]
    owned = jnp.sum(first_hot, 0) > 0
    valid = (labels >= 0) & owned
    positive = (labels == 1).astype(F32)
    bce_sum = jnp.sum(
        jnp.where(valid, jax.nn.softplus(contact_logit) - positive * contact_logit, 0.0)
    )
    coef = jnp.where(valid, jax.nn.sigmoid(contact_logit) - positive, 0.0) / counts[1]
    coef_hi, coef_lo = split_two(coef)
    first_low = first_hot.astype(BF16)
    touch = nt(first_low * coef_hi[None], second_hot) + nt(first_low * coef_lo[None], second_hot)
    grad_contact = jnp.concatenate(
        [jnp.sum(prob_cube * touch[None], (1, 2)) * cols, jnp.sum(coef)[None]]
    )

    unit_1, rstd_1 = norm_stats(after_row)
    col_normed = (unit_1 * norms[1] + norms[5]).astype(BF16)
    col_proj = nn(col_normed, in_col).astype(BF16)
    group = 128 if here % 128 == 0 and 128 % rows == 0 else here
    groups = here // group
    lane = jnp.arange(group)
    same = (lane[:, None] // rows) == (lane[None, :] // rows)

    def cut(block):
        return block.reshape(groups, group, HEADS, HD)

    col_query, col_key, col_value = (cut(col_proj[:, k * D : (k + 1) * D]) for k in range(3))
    col_score = jnp.einsum("gqhe,gkhe->ghqk", col_query, col_key, preferred_element_type=F32) * HD ** (-0.5)
    col_prob = jax.nn.softmax(jnp.where(same, col_score, -1e30), axis=-1)
    col_prob_low = col_prob.astype(BF16)
    col_mixed = (
        jnp.einsum("ghqk,gkhe->gqhe", col_prob_low, col_value, preferred_element_type=F32)
        .astype(BF16)
        .reshape(here, D)
    )
    after_col = after_row + nn(col_mixed, out_col)

    unit_2, rstd_2 = norm_stats(after_col)
    feed_normed = (unit_2 * norms[2] + norms[6]).astype(BF16)
    hidden_up = nn(feed_normed, up_w)
    active, slope = gelu_parts(hidden_up)
    active = active.astype(BF16)
    after_feed = after_col + nt(active, down_t)
    unit_3, rstd_3 = norm_stats(after_feed)
    head_normed = (unit_3 * norms[3] + norms[7]).astype(BF16)
    logits = nt(table, head_normed) * D ** (-0.5)
    logits = jnp.where(vocab < VOCAB, logits, -1e30)
    top = jnp.max(logits, 0, keepdims=True)
    shifted = logits - top
    log_probs = shifted - jnp.log(jnp.sum(jnp.exp(shifted), 0, keepdims=True))
    target_hot = (targets_ir[None, :] == vocab).astype(F32)
    keep = ids_ir[None, :] == MASK_ID
    mlm_sum = -jnp.sum(jnp.where(keep & (target_hot > 0), log_probs, 0.0))
    logit_grad = jnp.where(keep, jnp.exp(log_probs) - target_hot, 0.0) / counts[0]
    logit_low = (logit_grad * D ** (-0.5)).astype(BF16)

    grad_head = nn(logit_low, head_normed)
    stream, scale_3, shift_3 = norm_back(unit_3, rstd_3, norms[3], tn(logit_low, table))
    branch = stream.astype(BF16)
    grad_down = tn(branch, active)
    up_low = (nn(branch, down_t) * slope).astype(BF16)
    grad_up = tn(feed_normed, up_low)
    inner, scale_2, shift_2 = norm_back(unit_2, rstd_2, norms[2], nt(up_low, up_w))
    stream = stream + inner
    branch = stream.astype(BF16)
    grad_out_col = tn(col_mixed, branch)
    mixed_low = nt(branch, out_col).astype(BF16)
    mixed_cut = cut(mixed_low)
    prob_grad = jnp.einsum("gqhe,gkhe->ghqk", mixed_cut, col_value, preferred_element_type=F32)
    score_grad = col_prob * (prob_grad - jnp.sum(col_prob * prob_grad, -1, keepdims=True))
    score_low = score_grad.astype(BF16)
    grad_q = jnp.einsum("ghqk,gkhe->gqhe", score_low, col_key, preferred_element_type=F32)
    grad_k = jnp.einsum("ghqk,gqhe->gkhe", score_low, col_query, preferred_element_type=F32)
    grad_v = jnp.einsum("ghqk,gqhe->gkhe", col_prob_low, mixed_cut, preferred_element_type=F32)
    proj_low = jnp.concatenate(
        [
            (grad_q * HD ** (-0.5)).reshape(here, D),
            (grad_k * HD ** (-0.5)).reshape(here, D),
            grad_v.reshape(here, D),
        ],
        -1,
    ).astype(BF16)
    grad_in_col = tn(col_normed, proj_low)
    inner, scale_1, shift_1 = norm_back(unit_1, rstd_1, norms[1], nt(proj_low, in_col))
    stream = stream + inner
    branch = stream.astype(BF16)
    grad_out_row = tn(row_mixed, branch)
    mixed_low = nt(branch, out_row).astype(BF16)
    mixed_ri = tn(perm, mixed_low).astype(BF16)
    drive_hi, drive_lo = split_two(per_head(mixed_ri, value_t, nt))
    prob_grad = nn(to_heads(drive_hi), hot_all) + nn(to_heads(drive_lo), hot_all)
    prob_grad = prob_grad + (
        touch[None] * (contact_head[:HEADS, None, None] * cols)
    ).reshape(HEADS * cw, cols)
    score_grad = prob * (prob_grad - jnp.sum(prob * prob_grad, -1, keepdims=True))
    score_low = score_grad.astype(BF16)
    spread = to_tokens(nt(score_low, hot_all)).astype(BF16)
    table_pair = nn(hot_ri, spread)
    value_grad = per_head(weight_hi, mixed_ri, tn)
    stream_hi, stream_lo = split_two(stream)
    lookup_grad = nn(hot_ir, stream_hi) + nn(hot_ir, stream_lo)
    vectors = jnp.stack([scale_1, scale_2, scale_3, shift_1, shift_2, shift_3])
    return (
        (grad_in_col, grad_out_row, grad_out_col, grad_up, grad_down),
        (table_pair, value_grad, grad_head + lookup_grad, vectors),
        grad_contact,
        mlm_sum,
        bce_sum,
        (unit_t, rstd_t, normed_t, query_t, key_t),
    )


MESH = pl.DeviceIdType.MESH
NZ, NY = 4, 2


def place():
    s, c = lax.axis_index("seq"), lax.axis_index("col")
    z, y, k = s // 4, lax.rem(s // 2, 2), lax.rem(s, 2)
    return z, y, k, c


def device(z, y, k, c):
    return (z * 4 + y * 2 + k, c)


def greet_all():
    z, y, k, c = place()
    me = (z * 4 + y * 2 + k) * 2 + c
    barrier = pltpu.get_barrier_semaphore()

    def signal(step, carry):
        other = lax.rem(me + step, 32)
        pl.semaphore_signal(
            barrier, inc=1, device_id=(other // 2, lax.rem(other, 2)), device_id_type=MESH
        )
        return carry

    lax.fori_loop(1, 32, signal, 0)
    return barrier


def remote(src, dst, send, recv, target):
    return pltpu.make_async_remote_copy(
        src_ref=src, dst_ref=dst, send_sem=send, recv_sem=recv, device_id=target, device_id_type=MESH
    )


ROWS, COLS, WIDE, HERE = 16, 512, 32, 512
PAIRS = 6
SLOTS = 1024
UP_TILE = 384


def iota(shape, dim):
    return lax.broadcasted_iota(jnp.int32, shape, dim)


def one_zero(test):
    return jnp.where(test, 1.0, 0.0)


def total_of(values):
    return jnp.sum(jnp.sum(values, 0, keepdims=True), 1, keepdims=True)


def half_lanes(values, side):
    lane = iota(values.shape, len(values.shape) - 1)
    keep = (lane < 64) if side == 0 else (lane >= 64)
    return jnp.where(keep, values.astype(F32), 0.0).astype(BF16)


def stacked(values):
    return jnp.concatenate([half_lanes(values, 0), half_lanes(values, 1)], 0)


def unstacked(values, count):
    lane = iota((count, 128), 1)
    return jnp.where(lane < 64, values[:count], values[count:])


def swap_blocks(first, second):
    lane = iota(first.shape, 1)
    low = jnp.where(lane < 64, first, pltpu.roll(second, 64, 1))
    high = jnp.where(lane < 64, pltpu.roll(first, 64, 1), second)
    return low, high


def split_heads_to(source, high_ref, low_ref):
    for rp in range(ROWS // 2):
        for hp in range(PAIRS):
            lanes = slice(hp * 128, hp * 128 + 128)
            first = source[rp * 64 : rp * 64 + 32, lanes]
            second = source[rp * 64 + 32 : rp * 64 + 64, lanes]
            for side, block in enumerate(swap_blocks(first, second)):
                top, rest = split_two(block)
                rows = slice((2 * hp + side) * 32, (2 * hp + side) * 32 + 32)
                high_ref[rows, rp * 128 : rp * 128 + 128] = top
                low_ref[rows, rp * 128 : rp * 128 + 128] = rest


def merge_heads(probs, hot_all, high_ref, low_ref):
    for rp in range(ROWS // 2):
        block = nt(probs, hot_all[rp * 128 : rp * 128 + 128, :])
        for hp in range(PAIRS):
            first = block[hp * 64 : hp * 64 + 32]
            second = block[hp * 64 + 32 : hp * 64 + 64]
            for side, part in enumerate(swap_blocks(first, second)):
                top, rest = split_two(part)
                rows = slice(rp * 64 + side * 32, rp * 64 + side * 32 + 32)
                high_ref[rows, hp * 128 : hp * 128 + 128] = top
                if low_ref is not None:
                    low_ref[rows, hp * 128 : hp * 128 + 128] = rest


def norm_rows(source, gain, bias, unit_ref, rstd_ref, normed_ref):
    def body(at, carry):
        rows = pl.ds(pl.multiple_of(at * 64, 64), 64)
        values = source[rows, :]
        centre = values - jnp.sum(values, -1, keepdims=True) * (1.0 / D)
        rstd = lax.rsqrt(jnp.sum(centre * centre, -1, keepdims=True) * (1.0 / D) + NORM_EPS)
        unit = centre * rstd
        unit_ref[rows, :] = unit
        rstd_ref[rows, :] = jnp.broadcast_to(rstd, (64, 128))
        normed_ref[rows, :] = (unit * gain + bias).astype(BF16)
        return carry

    lax.fori_loop(0, HERE // 64, body, 0)


def transpose_into(source, target):
    def body(at, carry):
        rows = pl.ds(pl.multiple_of(at * 128, 128), 128)
        target[:, rows] = source[rows, :].astype(F32).T.astype(BF16)
        return carry

    lax.fori_loop(0, HERE // 128, body, 0)


def over_tiles(width, tile, body):
    for half in range(2):

        def step(at, carry, half=half):
            body(half, pl.multiple_of(at * tile, tile))
            return carry

        lax.fori_loop(0, width // tile, step, 0)


def column_mask():
    rows, lanes = iota((256, 128), 0), iota((256, 128), 1)
    return ((rows & 127) >> 4) == (lanes >> 4)


class Saved(typing.NamedTuple):
    stream: typing.Any
    branch: typing.Any
    unit_1: typing.Any
    unit_2: typing.Any
    rstd_1: typing.Any
    rstd_2: typing.Any
    row_mixed_t: typing.Any
    col_normed_t: typing.Any
    col_mixed_t: typing.Any
    feed_normed_t: typing.Any
    col_proj: typing.Any
    col_prob: typing.Any
    active: typing.Any
    slope: typing.Any
    grad_head: typing.Any
    hot_all: typing.Any
    hot_ri: typing.Any
    hot_ir: typing.Any
    prob: typing.Any
    weight_hi: typing.Any
    value_two: typing.Any
    touch: typing.Any
    table: typing.Any
    norms: typing.Any
    proj_t: typing.Any
    extras: typing.Any
    moved: typing.Any


AT = Saved(*range(len(Saved._fields)))
SAVED = Saved(
    stream=((HERE, D), F32),
    branch=((HERE, D), BF16),
    unit_1=((HERE, D), F32),
    unit_2=((HERE, D), F32),
    rstd_1=((HERE, 128), F32),
    rstd_2=((HERE, 128), F32),
    row_mixed_t=((D, HERE), BF16),
    col_normed_t=((D, HERE), BF16),
    col_mixed_t=((D, HERE), BF16),
    feed_normed_t=((D, HERE), BF16),
    col_proj=((HERE, 3 * D), BF16),
    col_prob=((4 * PAIRS, 256, 128), F32),
    active=((HERE, FF), BF16),
    slope=((HERE, FF), BF16),
    grad_head=((VP, D), F32),
    hot_all=((ROWS * VP, COLS), BF16),
    hot_ri=((VP, HERE), BF16),
    hot_ir=((VP, HERE), BF16),
    prob=((HEADS * WIDE, COLS), F32),
    weight_hi=((HERE, D), BF16),
    value_two=((PAIRS, 128, 128), BF16),
    touch=((WIDE, COLS), F32),
    table=((VP, D), F32),
    norms=((8, D), F32),
    proj_t=((VP, 3 * D), BF16),
    extras=((8, 128), F32),
    moved=((8, D), F32),
)


class Forward(typing.NamedTuple):
    ids: typing.Any
    targets: typing.Any
    slots: typing.Any
    normed: typing.Any
    mixed: typing.Any
    weight_lo: typing.Any
    left_hi: typing.Any
    left_lo: typing.Any
    lookup: typing.Any
    prob_low: typing.Any
    unit: typing.Any
    rstd: typing.Any


FORWARD = Forward(
    ids=((ROWS, COLS), jnp.int32),
    targets=((ROWS, 128), jnp.int32),
    slots=((8, SLOTS), jnp.int32),
    normed=((HERE, D), BF16),
    mixed=((HERE, D), BF16),
    weight_lo=((HERE, D), BF16),
    left_hi=((HEADS * WIDE, ROWS * VP), BF16),
    left_lo=((HEADS * WIDE, ROWS * VP), BF16),
    lookup=((HERE, D), F32),
    prob_low=((HEADS * WIDE, COLS), BF16),
    unit=((HERE, D), F32),
    rstd=((HERE, 128), F32),
)


def position():
    z, y, k, c = place()
    me = (z * 4 + y * 2 + k) * 2 + c
    return z // 2, lax.rem(me, 16)


def read_tokens(small, f):
    alignment, block = position()
    side, part = block // 8, lax.rem(block // 4, 2)
    for r in range(ROWS):
        for cc in range(2):
            for q in range(2):
                lanes = slice(cc * 256 + q * 128, cc * 256 + q * 128 + 128)
                f.ids[r : r + 1, lanes] = small[r * 2 + cc, pl.ds(2 * alignment + q, 1), :]
        f.targets[r : r + 1, :] = small[r * 2 + side, pl.ds(4 + 2 * alignment + part, 1), :]
    lane = iota((1, 128), 1)
    for number in range(SLOTS // 128):
        for which in range(3):
            row = pl.ds(8 + 3 * alignment + which, 1)
            first = small[number * 4 + side, row, :]
            second = pltpu.roll(small[number * 4 + 2 + side, row, :], 64, 1)
            f.slots[which : which + 1, number * 128 : number * 128 + 128] = jnp.where(
                lane < 64, first, second
            )


def local_hot(values, shift):
    values = pltpu.roll(values, shift, 1)
    turned = [values] + [pltpu.roll(values, 32 * n, 1) for n in (1, 2, 3)]
    lane = iota((1, 128), 1)
    tiles = []
    for tile in range(4):
        row = turned[3][4 * tile + 3 : 4 * tile + 4]
        for n in (2, 1, 0):
            row = jnp.where(lane < 32 * n + 32, turned[n][4 * tile + n : 4 * tile + n + 1], row)
        tiles.append(row)
    row = jnp.concatenate(tiles, 1)
    return one_zero(row == iota((VP, HERE), 0)).astype(BF16)


def contact_part(contact_head, f, s, pair_count):
    _, block = position()
    base = block * WIDE
    head_sum = jnp.zeros((WIDE, COLS), F32)
    for h in range(HEADS):
        head_sum = head_sum + contact_head[h] * f.prob_low[h * 32 : h * 32 + 32, :].astype(F32)
    top, rest = split_two(head_sum)
    last = (head_sum - top.astype(F32) - rest.astype(F32)).astype(BF16)
    parts = jnp.concatenate([top, rest, last], 0)
    touch = jnp.zeros((WIDE, COLS), F32)
    bce = jnp.zeros((1, 1), F32)
    coef_sum = jnp.zeros((1, 1), F32)
    for number in range(SLOTS // 512):
        lanes = slice(number * 512, number * 512 + 512)
        first, second, label = (f.slots[n : n + 1, lanes] for n in range(3))
        second_hot = one_zero(second == iota((COLS, 512), 0)).astype(BF16)
        picked = nn(parts, second_hot)
        picked = picked[:32] + picked[32:64] + picked[64:]
        first_hot = one_zero((first - base) == iota((WIDE, 512), 0))
        logit = jnp.sum(picked * first_hot, 0, keepdims=True) * COLS + contact_head[HEADS]
        owned = jnp.sum(first_hot, 0, keepdims=True) > 0.5
        valid = (label >= 0) & owned
        positive = one_zero(label == 1)
        small = jnp.exp(-jnp.abs(logit))
        soft = jnp.maximum(logit, 0.0) + jnp.log(1.0 + small)
        bce = bce + total_of(jnp.where(valid, soft - positive * logit, 0.0))
        sigmoid = jnp.where(logit >= 0.0, 1.0, small) / (1.0 + small)
        coef = jnp.where(valid, sigmoid - positive, 0.0) / pair_count
        coef_sum = coef_sum + total_of(coef)
        coef_top, coef_rest = split_two(first_hot * coef)
        touch = touch + nt(coef_top, second_hot) + nt(coef_rest, second_hot)
    s.touch[...] = touch
    column = iota((1, 128), 1)
    row = jnp.where(column == HEADS, coef_sum, 0.0)
    for h in range(HEADS):
        part = total_of(touch * f.prob_low[h * 32 : h * 32 + 32, :].astype(F32)) * COLS
        row = row + jnp.where(column == h, part, 0.0)
    return row, bce


def feature_order():
    shape = (384, 384)
    spot = iota(shape, 0)
    block = (spot * 2731) >> 16
    swapped = (block & 28) | ((block & 1) << 1) | ((block >> 1) & 1)
    return one_zero(spot + (swapped - block) * 24 == iota(shape, 1)).astype(BF16)


def forward_body(small, contact_head, weights, s, f, cells, projected, hook, emit):
    out_row, in_col, out_col = weights[:3]
    up_parts, down_parts = weights[3:5], weights[5:7]
    hook()
    features = cells()
    read_tokens(small, f)
    _, block = position()
    shift = lax.rem(128 - lax.rem(block, 4) * 32, 128)
    window = pl.ds(pl.multiple_of((block // 4) * 128, 128), 128)
    hot_ri = local_hot(f.ids[:, window], shift)
    goal_ri = local_hot(f.targets[...], shift)
    s.hot_ri[...] = hot_ri
    for r in range(ROWS):
        row = f.ids[r : r + 1, :]
        s.hot_all[r * VP : r * VP + VP, :] = one_zero(row == iota((VP, COLS), 0)).astype(BF16)
    shape = (HERE, HERE)
    back = (
        ((iota(shape, 1) >> 4) == (iota(shape, 0) & 31))
        & ((iota(shape, 1) & 15) == (iota(shape, 0) >> 5))
    )
    back = one_zero(back).astype(BF16)
    hot_ir = nn(hot_ri, back).astype(BF16)
    s.hot_ir[...] = hot_ir
    goal = nn(goal_ri, back)
    entries = jnp.zeros((4, 128), F32)
    labelled = jnp.zeros((1, 128), F32)
    for d in range(32):
        entries = entries + one_zero(small[d, 0:4, :] == MASK_ID)
        labelled = labelled + one_zero(small[d, 10:11, :] >= 0) + one_zero(small[d, 13:14, :] >= 0)
    entries, labelled = total_of(entries), total_of(labelled)

    hook()
    features = features[...].T
    table = features[:VP]
    norms = features[VP : VP + 8]
    s.table[...] = table
    s.norms[...] = norms
    table_low = table.astype(BF16)

    def vector(number):
        return norms[number : number + 1, :]

    hook()
    projected(s.proj_t)
    pair_parts = []
    for hp in range(PAIRS):
        lanes = slice(hp * 128, hp * 128 + 128)
        key = s.proj_t[:, D + hp * 128 : D + hp * 128 + 128]
        value = s.proj_t[:, 2 * D + hp * 128 : 2 * D + hp * 128 + 128]
        s.value_two[hp] = stacked(value)
        pair_parts.append(nt(s.proj_t[:, lanes], stacked(key)))
    pair_hi, pair_lo = split_two(jnp.concatenate(pair_parts, 1))
    hook()
    f.lookup[...] = tn(hot_ri, pair_hi) + tn(hot_ri, pair_lo)
    split_heads_to(f.lookup, f.left_hi, f.left_lo)
    hook()
    hot_all = s.hot_all[...]
    score = (nn(f.left_hi[...], hot_all) + nn(f.left_lo[...], hot_all)) * (HD * ROWS) ** (-0.5)
    score = jnp.exp(score - jnp.max(score, -1, keepdims=True))
    prob = score / jnp.sum(score, -1, keepdims=True)
    s.prob[...] = prob
    f.prob_low[...] = prob.astype(BF16)
    hook()
    merge_heads(f.prob_low[...], s.hot_all, s.weight_hi, f.weight_lo)
    hook()
    for hp in range(PAIRS):
        lanes = slice(hp * 128, hp * 128 + 128)
        value = s.value_two[hp]
        f.mixed[:, lanes] = (nn(s.weight_hi[:, lanes], value) + nn(f.weight_lo[:, lanes], value)).astype(BF16)
    ahead = (
        ((iota(shape, 0) >> 4) == (iota(shape, 1) & 31))
        & ((iota(shape, 0) & 15) == (iota(shape, 1) >> 5))
    )
    f.mixed[...] = nn(one_zero(ahead).astype(BF16), f.mixed[...]).astype(BF16)
    transpose_into(f.mixed, s.row_mixed_t)
    s.stream[...] = tn(hot_ir, table_low)
    hook()
    contact_row, bce = contact_part(contact_head, f, s, labelled)
    emit(AT.hot_all, AT.hot_ri, AT.hot_ir, AT.table, AT.norms, AT.proj_t, AT.value_two, AT.prob, AT.weight_hi, AT.row_mixed_t, AT.touch)

    hook()
    for half in range(2):
        lanes = slice(half * 384, half * 384 + 384)
        s.stream[:, lanes] += nn(f.mixed[...], out_row[half])
    norm_rows(s.stream, vector(1), vector(5), s.unit_1, s.rstd_1, f.normed)
    transpose_into(f.normed, s.col_normed_t)
    emit(AT.unit_1, AT.rstd_1, AT.col_normed_t)
    def project(half, at):
        s.col_proj[:, half * 1152 + at : half * 1152 + at + 384] = nn(
            f.normed[...], in_col[half, :, at : at + 384]
        ).astype(BF16)

    for third in range(3):
        hook()
        for half in range(2):
            project(half, third * 384)
    emit(AT.col_proj)

    def attend(at, carry):
        rows = pl.ds(pl.multiple_of((at // PAIRS) * 128, 128), 128)
        lane = lax.rem(at, PAIRS) * 128

        def lanes(part):
            return pl.ds(pl.multiple_of(part * D + lane, 128), 128)

        query = stacked(s.col_proj[rows, lanes(0)])
        score = nt(query, s.col_proj[rows, lanes(1)]) * HD ** (-0.5)
        score = jnp.where(column_mask(), score, -1e30)
        score = jnp.exp(score - jnp.max(score, -1, keepdims=True))
        prob = score / jnp.sum(score, -1, keepdims=True)
        s.col_prob[at] = prob
        mixed = nn(prob.astype(BF16), s.col_proj[rows, lanes(2)])
        f.mixed[rows, lanes(0)] = unstacked(mixed, 128).astype(BF16)
        return carry

    for part in range(4):
        hook()
        lax.fori_loop(part * PAIRS, part * PAIRS + PAIRS, attend, 0, unroll=3)
    hook()
    transpose_into(f.mixed, s.col_mixed_t)
    emit(AT.col_prob, AT.col_mixed_t)
    for half in range(2):
        lanes = slice(half * 384, half * 384 + 384)
        s.stream[:, lanes] += nn(f.mixed[...], out_col[half])
    norm_rows(s.stream, vector(2), vector(6), s.unit_2, s.rstd_2, f.normed)
    transpose_into(f.normed, s.feed_normed_t)
    emit(AT.unit_2, AT.rstd_2, AT.feed_normed_t)
    for part in range(2):

        def widen(half, at, part=part):
            lanes = slice(part * 1536 + half * 768 + at, part * 1536 + half * 768 + at + UP_TILE)
            up = nn(f.normed[...], up_parts[part][half, :, at : at + UP_TILE])
            active, slope = gelu_parts(up)
            s.active[:, lanes] = active.astype(BF16)
            s.slope[:, lanes] = slope.astype(BF16)

        for half in range(2):
            hook()
            for at in range(0, 768, UP_TILE):
                widen(half, at)

    emit(AT.active, AT.slope)
    for part, at, size in ((0, 0, 768), (1, 0, 384), (1, 384, 384)):
        hook()
        for half in range(2):
            start = part * 1536 + half * 768 + at
            s.stream[...] += nt(
                s.active[:, start : start + size], down_parts[part][half, :, at : at + size]
            )
    hook()
    norm_rows(s.stream, vector(3), vector(7), f.unit, f.rstd, f.normed)
    logits = nt(table_low, f.normed[...]) * D ** (-0.5)
    vocab = iota((VP, HERE), 0)
    logits = jnp.where(vocab < VOCAB, logits, -1e30)
    shifted = logits - jnp.max(logits, 0, keepdims=True)
    log_probs = shifted - jnp.log(jnp.sum(jnp.exp(shifted), 0, keepdims=True))
    keep = hot_ir[MASK_ID : MASK_ID + 1].astype(F32) > 0.5
    mlm = -total_of(jnp.where(keep & (goal > 0.5), log_probs, 0.0))
    logit_grad = jnp.where(keep, jnp.exp(log_probs) - goal, 0.0) / entries
    logit_low = (logit_grad * D ** (-0.5)).astype(BF16)
    s.grad_head[...] = nn(logit_low, f.normed[...])
    hook()
    f.lookup[...] = tn(logit_low, table_low)
    scale_3, shift_3 = back_rows(f.unit, f.rstd, vector(3), f.lookup, s.stream, s.branch, True)
    emit(AT.stream, AT.branch)
    line = iota((8, D), 0)
    s.moved[...] = jnp.where(line == 0, scale_3, jnp.where(line == 1, shift_3, 0.0))
    column = iota((1, 128), 1)
    row = contact_row + jnp.where(column == HEADS + 1, mlm, 0.0) + jnp.where(column == HEADS + 2, bce, 0.0)
    counted = jnp.where(column == 0, entries, 0.0) + jnp.where(column == 1, labelled, 0.0)
    line = iota((8, 128), 0)
    s.extras[...] = jnp.where(line == 0, row, jnp.where(line == 1, counted, 0.0))
    emit(AT.grad_head, AT.extras, AT.moved)
    hook()


def back_rows(unit_ref, rstd_ref, gain, upstream_ref, stream_ref, low_ref, first):
    def body(at, carry):
        scale, move = carry
        rows = pl.ds(pl.multiple_of(at * 64, 64), 64)
        upstream = upstream_ref[rows, :]
        unit = unit_ref[rows, :]
        inner = upstream * gain
        mean = jnp.sum(inner, -1, keepdims=True) * (1.0 / D)
        along = jnp.sum(inner * unit, -1, keepdims=True) * (1.0 / D)
        grad = rstd_ref[rows, 0:1] * (inner - mean - unit * along)
        if not first:
            grad = grad + stream_ref[rows, :]
        stream_ref[rows, :] = grad
        low_ref[rows, :] = grad.astype(BF16)
        touched = upstream * unit
        for n in range(8):
            scale = scale + touched[n * 8 : n * 8 + 8]
            move = move + upstream[n * 8 : n * 8 + 8]
        return scale, move

    zero = jnp.zeros((8, D), F32)
    scale, move = lax.fori_loop(0, HERE // 64, body, (zero, zero))
    return jnp.sum(scale, 0, keepdims=True), jnp.sum(move, 0, keepdims=True)


MATRICES = (128, 384, 1152, 384, 768, 768, 768, 768)
UNITS = (
    (0, 0, 128, True),
    (1, 0, 384, False),
    (2, 0, 384, True),
    (2, 384, 384, True),
    (2, 768, 384, True),
    (3, 0, 384, False),
    (4, 0, 768, True),
    (5, 0, 768, True),
    (6, 0, 768, True),
    (7, 0, 384, True),
    (7, 384, 384, True),
)
Z_LAST = {9: 2}
FORWARD_ORDER = (
    ((0, 0), (0, 2), (0, 11), (1, 0), (0, 1), (0, 9), (1, 2), (1, 11), (2, 0), (0, 3), (1, 9), (0, 4), (1, 1), (2, 11), (3, 0), (0, 5), (2, 1), (4, 0),),
    ((3, 11), (2, 2), (0, 6), (3, 1), (1, 3),),
    ((4, 11), (1, 4),),
    ((4, 1), (3, 2), (2, 3), (0, 7), (1, 5),),
    ((4, 2), (2, 4),),
    ((1, 6), (3, 3), (0, 8),),
    (),
    ((4, 3), (3, 4), (2, 5), (2, 9),),
    ((2, 6),),
    ((4, 4), (1, 7),),
    ((3, 5),),
    (),
    (),
    ((4, 5), (3, 6), (1, 8), (0, 10),),
    (),
    ((4, 6),),
    ((2, 7), (3, 9),),
    ((2, 8),),
    ((1, 10),),
    ((4, 9), (3, 7), (3, 8), (2, 10), (4, 7),),
    (),
    ((4, 8),),
    ((3, 10),),
    ((4, 10),),
    (),
    (),
    (),
)


def spot(paired, cc, zz, yy, k):
    return (k, zz, yy, cc) if paired else (cc, zz, yy, k)


def forward_kernel(*refs):
    count, parts = len(UNITS), len(MATRICES)
    raw = refs[:11]
    contact_head = refs[11]
    at = 12
    far = (None, *refs[at : at + parts - 1])
    saved_far = refs[at + parts - 1 : at + parts - 1 + len(SAVED)]
    at += parts - 1 + len(SAVED)
    outs = refs[at : at + parts]
    at += parts
    outgoing = refs[at : at + count]
    incoming = refs[at + count : at + 2 * count]
    piece = refs[at + 2 * count : at + 3 * count]
    at += 3 * count
    saved = Saved(*refs[at : at + len(SAVED)])
    at += len(SAVED)
    scratch = Forward(*refs[at : at + len(FORWARD)])
    at += len(FORWARD)
    near = refs[at : at + 11]
    at += 11
    small, small_out, corner, features, stat, stat_got, part, part_got, part_line, proj, room = refs[at : at + 11]
    small_send, small_recv, send, recv, local, out_sem, raw_sem, twin_send, twin_recv = refs[at + 11 :]
    tokens, targets, masked, pairs, labels, table, norms, in_w, out_w, up_w, down_w = near
    z, y, k, c = place()
    me = (z * 4 + y * 2 + k) * 2 + c
    barrier = greet_all()
    raw_copies = [pltpu.make_async_copy(a, b, raw_sem.at[n]) for n, (a, b) in enumerate(zip(raw, near))]
    for item in raw_copies:
        item.start()
    for item in raw_copies[:7]:
        item.wait()
    small[...] = jnp.full(small.shape, -1, jnp.int32)
    for micro in range(2):
        for half in range(2):
            lanes = slice(half * 128, half * 128 + 128)
            row = 2 * micro + half
            small[row : row + 1, :] = jnp.where(
                masked[micro, :, lanes] > 0, MASK_ID, tokens[micro, :, lanes]
            )
            small[4 + row : 5 + row, :] = targets[micro, :, lanes]
        row = 8 + 3 * micro
        for which in range(2):
            small[row + which : row + which + 1, 0:64] = pairs[micro, which : which + 1, :]
        small[row + 2 : row + 3, 0:64] = labels[micro : micro + 1, :]
    corner[...] = jnp.zeros(corner.shape, F32)
    corner[0:8, 0:24] = norms[...]
    vectors = pltpu.roll(corner[...].T[:24], 64, 1)
    corner[0:8, 0:24] = jnp.zeros((8, 24), F32)
    corner[0:24, 0:VOCAB] = table[...]
    mine_rows = (corner[0:24, :] + vectors).astype(BF16).astype(F32)
    table_rows = jnp.where(iota((24, 128), 1) < VP, mine_rows, 0.0)
    gain, bias = mine_rows[:, 64:65], mine_rows[:, 68:69]
    piece[0][0:16, :] = small[...].astype(F32)
    piece[0][16:40, :] = mine_rows
    mean = jnp.sum(table_rows, 0, keepdims=True) * (1.0 / 24)
    centre = table_rows - mean
    spread = jnp.sum(centre * centre, 0, keepdims=True)
    line = iota((8, 128), 0)
    stat[...] = jnp.where(line == 0, mean, jnp.where(line == 1, spread, 0.0))
    def master(u, side):
        matrix, start, n, _ = UNITS[u]
        width = MATRICES[matrix]
        if matrix == 2:
            return in_w[1, :, side * 1152 + start : side * 1152 + start + n]
        if matrix in (1, 3):
            rows = out_w[matrix // 2, :, side * 384 : side * 384 + 384].astype(BF16)
            return nn(rows, order)
        begin = (matrix % 2) * 1536 + side * width + start
        return (up_w if matrix < 6 else down_w)[:, begin : begin + n]

    def mine(u):
        return k if UNITS[u][3] else c

    def set_out(u):
        other = jnp.where(mine(u) == 0, master(u, 1), master(u, 0))
        other = jnp.concatenate([other, jnp.zeros((8, UNITS[u][2]), F32)], 0)
        outgoing[u][...] = other.astype(BF16)

    pl.semaphore_wait(barrier, 31)

    def stat_copy(step):
        other = lax.rem(me + step, 32)
        return remote(
            stat, stat_got.at[me], small_send.at[0, step], small_recv.at[0, step], (other // 2, lax.rem(other, 2))
        )

    chip = (z * 2 + y) * 2 + c

    def chip_copy(phase, step):
        other = lax.rem(chip + step, 16)
        target = device(other // 4, lax.rem(other // 2, 2), k, lax.rem(other, 2))
        if phase == 1:
            src, dst = part.at[k, other], part_line.at[chip]
        else:
            src, dst = proj.at[k, chip], proj.at[k, chip]
        return remote(src, dst, small_send.at[phase, step], small_recv.at[phase, step], target)

    def each(last, action):
        def body(step, carry):
            action(step)
            return carry

        lax.fori_loop(1, last, body, 0)

    each(32, lambda step: stat_copy(step).start())

    across, beside, twin = device(z, y, k, 1 - c), device(z, 1 - y, k, c), device(z, y, 1 - k, c)

    def block(u, cc, zz, yy):
        matrix, start, n, paired = UNITS[u]
        where = spot(paired, cc, zz, yy, k)
        if n == MATRICES[matrix]:
            return outs[matrix].at[where]
        return outs[matrix].at[(*where, slice(None), pl.ds(start, n))]

    def copy(u, at, src, dst, target):
        return remote(src, dst, send.at[u, at], recv.at[u, at], target)

    def pair_copy(u):
        return copy(u, 0, outgoing[u], incoming[u], twin if UNITS[u][3] else across)

    def own_copy(u):
        return pltpu.make_async_copy(piece[u], block(u, c, z, y), local.at[u])

    def line_copy(u, step):
        return copy(u, step, piece[u], block(u, c, z, y), device(lax.rem(z + step, 4), y, k, c))

    def same(u, at, cc, zz, yy, target):
        view = block(u, cc, zz, yy)
        return copy(u, at, view, view, target)

    low, high, every = pl.ds(0, 2), pl.ds(2, 2), slice(None)

    def second(u):
        return [same(u, 4, c, low, y, across), same(u, 5, c, high, y, beside)]

    def third_own(u):
        return [same(u, 6, c, low, y, beside), same(u, 7, c, high, y, across)]

    def third_far(u):
        return [same(u, 8, 1 - c, low, y, beside), same(u, 9, c, high, 1 - y, across)]

    def twin_own(u):
        return [same(u, 10, c, every, y, twin)]

    def twin_second(u):
        return [same(u, 11, 1 - c, low, y, twin), same(u, 12, c, high, 1 - y, twin)]

    def twin_third(u):
        return [
            same(u, 13, c, low, 1 - y, twin),
            same(u, 14, 1 - c, high, y, twin),
            same(u, 15, 1 - c, low, 1 - y, twin),
            same(u, 16, 1 - c, high, 1 - y, twin),
        ]

    own_copy(0).start()
    for item in raw_copies[7:]:
        item.wait()
    order = feature_order()
    for u in range(1, count):
        set_out(u)
        pair_copy(u).start()

    def part_twin():
        return remote(part.at[1 - k], part_got, twin_send.at[0], twin_recv.at[0], twin)

    def proj_twin():
        return remote(proj.at[k], proj.at[k], twin_send.at[1], twin_recv.at[1], twin)

    def project_part():
        stat_got[me] = stat[...]
        each(32, lambda step: stat_copy(step).wait())
        means = jnp.zeros((1, 128), F32)
        spreads = jnp.zeros((1, 128), F32)
        for d in range(32):
            means = means + stat_got[d, 0:1, :]
            spreads = spreads + stat_got[d, 1:2, :]
        means = means * (1.0 / 32)
        for d in range(32):
            away = stat_got[d, 0:1, :] - means
            spreads = spreads + 24.0 * away * away
        rstd = lax.rsqrt(spreads * (1.0 / D) + NORM_EPS)
        normed = (table_rows - means) * rstd * gain + bias
        normed = jnp.concatenate([normed, jnp.zeros((8, 128), F32)], 0).astype(BF16)
        for block_at in range(6):
            lanes = slice(block_at * 384, block_at * 384 + 384)
            rows = jnp.concatenate([in_w[0, :, lanes], jnp.zeros((8, 384), F32)], 0).astype(BF16)
            product = tn(normed, rows)
            for group in range(5):
                number = group * 6 + block_at
                part[number // 16, number % 16] = product[group * 8 : group * 8 + 8]
        for number in (30, 31):
            part[number // 16, number % 16] = jnp.zeros((8, 384), F32)
        part_twin().start()

    def project_chip():
        part_twin().wait_recv()
        part[k] = part[k] + part_got[...]
        each(16, lambda step: chip_copy(1, step).start())

    def project_line():
        part_line[chip] = part[k, chip]
        each(16, lambda step: chip_copy(1, step).wait_recv())
        proj[k, chip] = lax.fori_loop(1, 16, lambda at, held: held + part_line[at], part_line[0])
        each(16, lambda step: chip_copy(2, step).start())

    def project_twin():
        each(16, lambda step: chip_copy(2, step).wait_recv())
        proj_twin().start()

    def project_end():
        proj_twin().wait_recv()

    projecting = (project_part, project_chip, project_line, project_twin, project_end)

    def cells():
        for d in range(32):
            at = ((d // 2) % 2, d // 8, (d // 4) % 2, d % 2)
            small_out[d] = outs[0][(*at, slice(0, 16))].astype(jnp.int32)
            start = (((at[1] * 2 + at[2]) * 2 + at[3]) * 2 + at[0]) * 24
            features[start : start + 24, :] = outs[0][(*at, slice(16, 40))]
        return features

    def projected(target):
        room[40:64, :] = jnp.zeros((24, 3 * D), F32)
        for number in range(30):
            rows, lanes = (number // 6) * 8, (number % 6) * 384
            room[rows : rows + 8, lanes : lanes + 384] = proj[number // 16, number % 16]
        target[...] = room[...].astype(BF16)

    def to_across(u):
        return copy(u, 4, piece[u], block(u, c, z, y), across)

    def to_beside(u):
        return copy(u, 5, piece[u], block(u, c, z, y), beside)

    def to_corner(u):
        if Z_LAST[u] == 1:
            return same(u, 6, 1 - c, z, y, beside)
        return same(u, 6, c, z, 1 - y, across)

    def to_line(u):
        return [
            same(u, step, every, z, every, device(lax.rem(z + step, 4), y, k, c)) for step in (1, 3, 2)
        ]

    def to_twin(u):
        return [same(u, 7, every, z, every, twin)]

    def rest_to_twin(u):
        return [same(u, 7 + step, every, lax.rem(z + 4 - step, 4), every, twin) for step in (1, 3, 2)]

    def stage_line(u):
        if u == 0:
            for step in (1, 3, 2):
                line_copy(u, step).start()
            return
        pair_copy(u).wait_recv()
        side = mine(u)
        own = jnp.where(side == 0, master(u, 0), master(u, 1))
        theirs = incoming[u][...].astype(F32)[:24]
        top = jnp.where(side == 0, own, theirs)
        bottom = jnp.where(side == 0, theirs, own)
        piece[u][...] = jnp.concatenate([top, bottom], 0).astype(BF16)
        own_copy(u).start()
        if u in Z_LAST:
            to_across(u).start()
            to_beside(u).start()
            return
        for step in (1, 3, 2):
            line_copy(u, step).start()

    def stage_second(u):
        own_copy(u).wait()
        if u in Z_LAST:
            to_across(u).wait_recv()
            to_beside(u).wait_recv()
            to_corner(u).start()
            return
        for step in (1, 3, 2):
            line_copy(u, step).wait_recv()
        for item in second(u) + third_own(u) + twin_own(u):
            item.start()

    def stage_third(u):
        if u in Z_LAST:
            to_corner(u).wait_recv()
            for item in to_line(u) + to_twin(u):
                item.start()
            return
        for item in second(u):
            item.wait_recv()
        for item in third_far(u) + twin_second(u):
            item.start()

    def stage_twin(u):
        if u in Z_LAST:
            for item in to_line(u):
                item.wait_recv()
            for item in rest_to_twin(u):
                item.start()
            return
        for item in third_own(u) + third_far(u):
            item.wait_recv()
        for item in twin_third(u):
            item.start()

    def far_copy(matrix):
        return pltpu.make_async_copy(outs[matrix], far[matrix], local.at[count + matrix])

    def stage_end(u):
        if u in Z_LAST:
            for item in to_twin(u) + rest_to_twin(u):
                item.wait_recv()
            sent = [to_across(u), to_beside(u), to_corner(u)] + to_line(u) + to_twin(u)
        else:
            for item in twin_own(u) + twin_second(u) + twin_third(u):
                item.wait_recv()
            sent = [line_copy(u, step) for step in (1, 2, 3)]
            sent += second(u) + third_own(u) + third_far(u) + twin_own(u) + twin_second(u)
        for item in sent if u == 0 else [pair_copy(u)] + sent:
            item.wait_send()
        if u == 0:
            return
        if u + 1 == count or UNITS[u + 1][0] != UNITS[u][0]:
            far_copy(UNITS[u][0]).start()

    stages = (stage_line, stage_second, stage_third, stage_twin, stage_end)
    pending = list(FORWARD_ORDER)

    def hook():
        for stage, u in pending.pop(0):
            if u == count:
                projecting[stage]()
            else:
                stages[stage](u)

    def out_copy(at):
        return pltpu.make_async_copy(saved[at], saved_far[at], out_sem.at[at])

    def emit(*numbers):
        for number in numbers:
            out_copy(number).start()

    views = [w.reshape(2, D, n) for w, n in zip(outs[1:], MATRICES[1:])]
    forward_body(small_out, contact_head, views, saved, scratch, cells, projected, hook, emit)
    part_twin().wait_send()
    proj_twin().wait_send()
    for phase in (1, 2):
        each(16, lambda step, phase=phase: chip_copy(phase, step).wait_send())
    assert not pending
    for u in range(count):
        for item in rest_to_twin(u) if u in Z_LAST else twin_third(u):
            item.wait_send()
    for matrix in range(1, parts):
        far_copy(matrix).wait()
    for at in range(len(SAVED)):
        out_copy(at).wait()


def forward_call(raw, contact_head):
    count, parts = len(UNITS), len(MATRICES)
    anywhere = pl.BlockSpec(memory_space=pl.ANY)
    shapes = [(2, NZ, NY, 2, 48, n) for n in MATRICES[1:]]
    widths = [n for _, _, n, _ in UNITS]
    outs = pl.pallas_call(
        forward_kernel,
        out_shape=[jax.ShapeDtypeStruct(shape, BF16) for shape in shapes]
        + [jax.ShapeDtypeStruct(*item) for item in SAVED],
        in_specs=[anywhere] * 11 + [pl.BlockSpec(memory_space=pltpu.SMEM)],
        out_specs=[anywhere] * (parts - 1 + len(SAVED)),
        scratch_shapes=[pltpu.VMEM((2, NZ, NY, 2, 40, 128), F32)]
        + [pltpu.VMEM(shape, BF16) for shape in shapes]
        + [pltpu.VMEM((32, n), BF16) for n in widths] * 2
        + [pltpu.VMEM((40, 128), F32)]
        + [pltpu.VMEM((48, n), BF16) for n in widths[1:]]
        + [pltpu.VMEM(*item) for item in SAVED]
        + [pltpu.VMEM(*item) for item in FORWARD]
        + [pltpu.VMEM(item.shape, item.dtype) for item in raw]
        + [
            pltpu.VMEM((16, 128), jnp.int32),
            pltpu.VMEM((32, 16, 128), jnp.int32),
            pltpu.VMEM((128, 128), F32),
            pltpu.VMEM((D, 128), F32),
            pltpu.VMEM((8, 128), F32),
            pltpu.VMEM((32, 8, 128), F32),
            pltpu.VMEM((2, 16, 8, 384), F32),
            pltpu.VMEM((16, 8, 384), F32),
            pltpu.VMEM((16, 8, 384), F32),
            pltpu.VMEM((2, 16, 8, 384), F32),
            pltpu.VMEM((VP, 3 * D), F32),
            pltpu.SemaphoreType.DMA((3, 32)),
            pltpu.SemaphoreType.DMA((3, 32)),
            pltpu.SemaphoreType.DMA((count, 17)),
            pltpu.SemaphoreType.DMA((count, 17)),
            pltpu.SemaphoreType.DMA((count + parts,)),
            pltpu.SemaphoreType.DMA((len(SAVED),)),
            pltpu.SemaphoreType.DMA((len(raw),)),
            pltpu.SemaphoreType.DMA((2,)),
            pltpu.SemaphoreType.DMA((2,)),
        ],
        compiler_params=pltpu.CompilerParams(
            collective_id=0, has_side_effects=True, vmem_limit_bytes=62 * 2**20
        ),
    )(*raw, contact_head)
    return outs[: parts - 1], Saved(*outs[parts - 1 :])


def summed_rows(sums, group):
    return jnp.concatenate([sums[3 * group + third] for third in range(3)], 1).astype(F32)


def table_finish(sums, room, table_ref, norms_ref, proj_t, in_row, g_in, g_norm):
    z, y, k, c = place()
    me = ((z * 2 + y) * 2 + c) * 2 + k
    room[0:128, :] = jnp.zeros((128, D), F32)
    for number in range(2):
        room[4 + 16 * number : 20 + 16 * number, :] = summed_rows(sums, number)
        room[68 + 16 * number : 84 + 16 * number, :] = summed_rows(sums, 2 + number)
    pair = room[0:64, :]
    value_grad = room[64:128, :]
    vectors = summed_rows(sums, 6)
    vectors = vectors[:8] + vectors[8:]
    line = iota((8, D), 0)
    table_grad = jnp.concatenate(
        [
            summed_rows(sums, 4),
            summed_rows(sums, 5),
            jnp.where(line == 0, vectors[7:8], 0.0),
            jnp.zeros((24, D), F32),
        ],
        0,
    )
    pair_hi, pair_lo = split_two(pair)
    scale = (HD * ROWS) ** (-0.5)
    query_grad, key_grad = [], []
    for hp in range(PAIRS):
        lanes = slice(hp * 128, hp * 128 + 128)
        query = proj_t[:, lanes]
        key = stacked(proj_t[:, D + hp * 128 : D + hp * 128 + 128])
        high, low = pair_hi[:, lanes], pair_lo[:, lanes]
        query_grad.append((nn(high, key) + nn(low, key)) * scale)
        key_grad.append(unstacked(tn(high, query) + tn(low, query), VP) * scale)
    proj_hi, proj_lo = split_two(jnp.concatenate(query_grad + key_grad + [value_grad], 1))
    shard = D // 32
    pick = one_zero(iota((shard, D), 1) == iota((shard, D), 0) + me * shard).astype(BF16)
    weight = in_row[...].astype(BF16)
    back_t = nt(weight, proj_hi) + nt(weight, proj_lo)
    back = nt(proj_hi, weight) + nt(proj_lo, weight)
    table = table_ref[...]
    table_low = table.astype(BF16)
    unit, rstd = norm_stats(table)
    mean = jnp.sum(table, -1, keepdims=True) * (1.0 / D)
    same = iota((VP, VP), 0) == iota((VP, VP), 1)

    def as_row(column):
        return jnp.sum(jnp.where(same, column, 0.0), 0, keepdims=True)

    rstd_row = as_row(rstd)
    unit_t = (nt(pick, table_low) - as_row(mean)) * rstd_row
    unit_mine = (nt(table_low, pick) - mean) * rstd
    norms = jnp.concatenate([norms_ref[...], jnp.zeros((8, D), F32)], 0).astype(BF16)
    inner = back_t * nt(pick, norms)[:, 0:1]
    sums_1 = jnp.sum(inner, 0, keepdims=True)
    sums_2 = jnp.sum(inner * unit_t, 0, keepdims=True)
    scale_0 = jnp.sum(back * unit_mine, 0, keepdims=True)
    shift_0 = jnp.sum(back, 0, keepdims=True)
    line = iota((16, D), 0)
    norm_grad = jnp.zeros((16, D), F32)
    for number, source in ((1, 0), (2, 1), (3, 2), (5, 3), (6, 4), (7, 5)):
        norm_grad = jnp.where(line == number, vectors[source : source + 1], norm_grad)
    normed = (unit * norms_ref[0:1, :] + norms_ref[4:5, :]).astype(BF16)
    mine = nt(pick, normed).astype(BF16)
    in_grad = nn(mine, proj_hi) + nn(mine, proj_lo)
    g_in[...] = in_grad

    def three(values):
        top, rest = split_two(values)
        return top, rest, (values - top.astype(F32) - rest.astype(F32)).astype(BF16)

    emb_grad = sum(nt(pick, part) for part in three(table_grad))
    own_norm = sum(nt(part, pick) for part in three(norm_grad))[:8]
    line = iota((8, shard), 0)
    own_norm = jnp.where(line == 0, scale_0, jnp.where(line == 4, shift_0, own_norm))
    g_norm[...] = own_norm
    found = total_of(in_grad * in_grad) + total_of(own_norm * own_norm)
    return sums_1, sums_2, inner, unit_t, rstd_row, emb_grad, found


PIECES = 21
GRAD_WIDTHS = (768, 768, 768, 768, 384, 1152, 384)
GRAD_UNITS = (
    (0, 0, 384, True),
    (0, 384, 384, True),
    (1, 0, 768, True),
    (2, 0, 768, True),
    (3, 0, 768, True),
    (4, 0, 384, False),
    (5, 0, 384, True),
    (5, 384, 384, True),
    (5, 768, 384, True),
    (6, 0, 384, False),
)
Z_FIRST = {1: 1, 5: 2}
BACKWARD_ORDER = (
    (),
    (),
    (),
    (),
    (),
    (),
    ((0, 0),),
    ((0, 1),),
    (),
    (),
    (),
    ((1, 0),),
    (),
    ((0, 2),),
    ((2, 0),),
    (),
    ((0, 3),),
    (),
    (),
    (),
    ((1, 1), (1, 2), (0, 4),),
    ((3, 0), (0, 5),),
    ((4, 0),),
    ((1, 3),),
    ((2, 1),),
    (),
    ((2, 2),),
    (),
    (),
    (),
    (),
    ((1, 4), (1, 5), (0, 6), (0, 7),),
    ((3, 1), (2, 3), (0, 8),),
    ((4, 1),),
    ((2, 4),),
    ((3, 2), (2, 5), (0, 9),),
    ((4, 2), (1, 6),),
    ((3, 3), (1, 7),),
    ((4, 3), (3, 5), (1, 8),),
    ((3, 4), (1, 9), (2, 6), (4, 4), (2, 7), (5, 0), (4, 5), (3, 6), (2, 8), (2, 9), (4, 6), (3, 7), (4, 7), (6, 0), (3, 8), (4, 8), (3, 9), (7, 0), (4, 9),),
)


class Kept(typing.NamedTuple):
    stream: typing.Any
    norms: typing.Any
    table: typing.Any
    proj_t: typing.Any
    extras: typing.Any
    moved: typing.Any
    grad_head: typing.Any
    touch: typing.Any
    value_two: typing.Any


class Early(typing.NamedTuple):
    slope: typing.Any
    active: typing.Any
    feed_normed_t: typing.Any
    unit_2: typing.Any
    rstd_2: typing.Any
    col_mixed_t: typing.Any
    col_proj: typing.Any
    col_prob: typing.Any
    col_normed_t: typing.Any
    unit_1: typing.Any
    rstd_1: typing.Any


class Late(typing.NamedTuple):
    row_mixed_t: typing.Any
    hot_all: typing.Any
    weight_hi: typing.Any
    prob: typing.Any
    hot_ri: typing.Any
    hot_ir: typing.Any


def pick_items(group, source):
    return [getattr(source, name) for name in group._fields]


def backward_kernel(*refs):
    widths = GRAD_WIDTHS
    count = len(widths)
    contact_head = refs[0]
    far = refs[1 : 1 + count]
    in_row_far = refs[1 + count]
    saved = Saved(*refs[2 + count : 2 + count + len(SAVED)])
    at = 2 + count + len(SAVED)
    outs = refs[at : at + count]
    g_in, g_emb, g_norm, stats = refs[at + count : at + count + 4]
    at += count + 4
    grads = refs[at : at + count]
    kept = Kept(*refs[at + count : at + count + len(Kept._fields)])
    at += count + len(Kept._fields)
    upstream, branch, branch_t, mixed = refs[at : at + 4]
    scratch = refs[at + 4 :]
    units = len(GRAD_UNITS)
    got_0, got_1a, got_1b, got_2a, got_2b, got_3, total, got_4 = (
        scratch[i * units : (i + 1) * units] for i in range(8)
    )
    table, table_out, table_got, square, square_got, stat, stat_got = scratch[8 * units : 8 * units + 7]
    table_send, table_recv, send, recv, local = scratch[8 * units + 7 :]
    z, y, k, c = place()
    me = (z * 4 + y * 2 + k) * 2 + c
    across, beside, twin = device(z, y, k, 1 - c), device(z, 1 - y, k, c), device(z, y, 1 - k, c)
    barrier = greet_all()
    stream = kept.stream
    square[...] = jnp.zeros(square.shape, F32)

    copies = {}

    def load(number, source, target):
        copies[number] = pltpu.make_async_copy(source, target, local.at[number])
        copies[number].start()

    def need(*numbers):
        for number in numbers:
            copies[number].wait()

    def weight(m):
        return len(SAVED) + m

    def copy(m, at, src, dst, target):
        return remote(src, dst, send.at[m, at], recv.at[m, at], target)

    low, high = pl.ds(0, 2), pl.ds(2, 2)
    every = slice(None)

    def where(u, cc, zz, yy):
        matrix, start, n, paired = GRAD_UNITS[u]
        index = spot(paired, cc, zz, yy, k)
        return index if n == widths[matrix] else (*index, every, pl.ds(start, n))

    def block(u, cc, zz, yy):
        return grads[GRAD_UNITS[u][0]].at[where(u, cc, zz, yy)]

    def ordered(u, cc, rest):
        return (*rest, cc) if GRAD_UNITS[u][3] else (cc, *rest)

    def twin_copy(u):
        matrix, start, n, paired = GRAD_UNITS[u]
        index = (1 - k,) if paired else (every, every, every, 1 - k)
        if n != widths[matrix]:
            index = (*index, *(every,) * (5 - len(index)), pl.ds(start, n))
        return copy(u, 0, grads[matrix].at[index], got_0[u], twin)

    def first(u):
        return [
            copy(u, 1, block(u, every, low, 1 - y), got_1a[u], beside),
            copy(u, 2, block(u, 1 - c, high, every), got_1b[u], across),
        ]

    def second(u):
        return [
            copy(u, 3, block(u, 1 - c, low, y), got_2a[u], across),
            copy(u, 4, block(u, c, high, 1 - y), got_2b[u], beside),
        ]

    def along(u):
        return [
            copy(
                u,
                4 + step,
                block(u, c, lax.rem(z + step, 4), y),
                got_3[u].at[step - 1],
                device(lax.rem(z + step, 4), y, k, c),
            )
            for step in (1, 3, 2)
        ]

    def z_first(u):
        return [
            copy(
                u,
                step,
                block(u, every, lax.rem(z + step, 4), every),
                got_1a[u].at[step - 1],
                device(lax.rem(z + step, 4), y, k, c),
            )
            for step in (1, 3, 2)
        ]

    def plane_first(u):
        if Z_FIRST[u] == 1:
            return [copy(u, 4, block(u, every, z, 1 - y), got_2a[u], beside)]
        return [copy(u, 4, block(u, 1 - c, z, every), got_2a[u], across)]

    def plane_second(u):
        if Z_FIRST[u] == 1:
            return [copy(u, 5, block(u, 1 - c, z, y), got_2b[u], across)]
        return [copy(u, 5, block(u, c, z, 1 - y), got_2b[u], beside)]

    def mine(u):
        return k if GRAD_UNITS[u][3] else c

    def pair(u):
        return [copy(u, 8, total[u].at[1 - mine(u)], got_4[u], twin if GRAD_UNITS[u][3] else across)]

    def peer(step):
        return lax.rem(me + step, 32)

    def source(step):
        return lax.rem(me + 32 - step, 32)

    def table_copy(step, back, index):
        target = (peer(step) // 2, lax.rem(peer(step), 2))
        if back:
            return remote(
                table_out.at[index], table_out.at[index], table_send.at[1, step], table_recv.at[1, step], target
            )
        return remote(
            table.at[index], table_got.at[me], table_send.at[0, step], table_recv.at[0, step], target
        )

    def table_start(step):
        @pl.when(peer(step) < PIECES)
        def _():
            table_copy(step, False, peer(step)).start()

    def table_wait_send(step):
        @pl.when(peer(step) < PIECES)
        def _():
            table_copy(step, False, 0).wait_send()

        @pl.when(me < PIECES)
        def _():
            table_copy(step, True, 0).wait_send()

    def table_wait_back(step):
        @pl.when(source(step) < PIECES)
        def _():
            table_copy(step, True, 0).wait_recv()

    def each(action):
        def body(step, carry):
            action(step)
            return carry

        lax.fori_loop(1, 32, body, 0)

    def gather_into(u, cc, zz, yy, *others):
        matrix = GRAD_UNITS[u][0]
        index = where(u, cc, zz, yy)
        value = grads[matrix][index].astype(F32) + got_0[u][ordered(u, cc, (zz, yy))].astype(F32)
        for other in others:
            value = value + other.astype(F32)
        grads[matrix][index] = value.astype(BF16)

    def from_line(u, cc, yy):
        index = (yy, cc) if GRAD_UNITS[u][3] else (cc, yy)
        return [got_1a[u][(step, *index)] for step in range(3)]

    def stage_first(u):
        twin_copy(u).wait_recv()
        if u in Z_FIRST:
            for step in (1, 3, 2):
                for cc in range(2):
                    for yy in range(2):
                        gather_into(u, cc, lax.rem(z + step, 4), yy)
            for item in z_first(u):
                item.start()
            return
        for a in range(2):
            for b in range(2):
                gather_into(u, a, b, 1 - y)
                gather_into(u, 1 - c, 2 + a, b)
        for item in first(u):
            item.start()

    def from_beside(u, cc, a):
        return got_1a[u][ordered(u, cc, (a,))]

    def stage_second(u):
        if u in Z_FIRST:
            for item in z_first(u):
                item.wait_recv()
            for a in range(2):
                cc, yy = (a, 1 - y) if Z_FIRST[u] == 1 else (1 - c, a)
                gather_into(u, cc, z, yy, *from_line(u, cc, yy))
            for item in plane_first(u):
                item.start()
            return
        for item in first(u):
            item.wait_recv()
        for a in range(2):
            gather_into(u, 1 - c, a, y, from_beside(u, 1 - c, a))
            gather_into(u, c, 2 + a, 1 - y, got_1b[u][a, 1 - y])
        for item in second(u):
            item.start()

    def stage_along(u):
        if u in Z_FIRST:
            for item in plane_first(u):
                item.wait_recv()
            cc, yy = (1 - c, y) if Z_FIRST[u] == 1 else (c, 1 - y)
            gather_into(u, cc, z, yy, *from_line(u, cc, yy), got_2a[u][cc if Z_FIRST[u] == 1 else yy])
            for item in plane_second(u):
                item.start()
            return
        for item in second(u):
            item.wait_recv()
        for a in range(2):
            gather_into(u, c, a, y, from_beside(u, c, a), got_2a[u][a])
            gather_into(u, c, 2 + a, y, got_1b[u][a, y], got_2b[u][a])
        for item in along(u):
            item.start()

    def stage_pair(u):
        full = grads[GRAD_UNITS[u][0]][where(u, c, z, y)].astype(F32)
        if u in Z_FIRST:
            for item in plane_second(u):
                item.wait_recv()
            others = [got_0[u][ordered(u, c, (z, y))], *from_line(u, c, y)]
            others += [got_2a[u][c if Z_FIRST[u] == 1 else y], got_2b[u][...]]
        else:
            for item in along(u):
                item.wait_recv()
            others = [got_3[u][step] for step in range(3)]
        for other in others:
            full = full + other.astype(F32)
        total[u][0] = full[:24]
        total[u][1] = full[24:]
        for item in pair(u):
            item.start()

    def stage_end(u):
        matrix, start, n, _ = GRAD_UNITS[u]
        lanes = slice(start, start + n)
        side = mine(u)
        outs[matrix][side, :, lanes] = total[u][side]
        for item in pair(u):
            item.wait_recv()
        outs[matrix][1 - side, :, lanes] = got_4[u][...]
        own, other = total[u][side], got_4[u][...]
        square[...] += jnp.broadcast_to(total_of(own * own) + total_of(other * other), (8, 128))
        if u in Z_FIRST:
            sent = z_first(u) + plane_first(u) + plane_second(u)
        else:
            sent = first(u) + second(u) + along(u)
        for item in [twin_copy(u)] + sent:
            item.wait_send()

    def table_sum(u):
        @pl.when(me < PIECES)
        def _():
            each(lambda step: table_copy(step, False, 0).wait_recv())
            table_got[me] = table[me]

            def add(at, held):
                return held + table_got[at].astype(F32)

            total_rows = lax.fori_loop(1, 32, add, table_got[0].astype(F32))
            top, rest = split_two(total_rows[:8] + total_rows[8:])
            exact = jnp.concatenate([top.astype(F32), rest.astype(F32)], 0)
            table_out[me] = jnp.where(me >= 18, exact, total_rows).astype(BF16)
            each(lambda step: table_copy(step, True, me).start())

    late_parts = []

    def table_end(u):
        each(table_wait_back)
        need(weight(count))
        late_parts.append(
            table_finish(table_out, upstream, kept.table, kept.norms, kept.proj_t, late_parts[0], g_in, g_norm)
        )
        state = late_parts[1]
        line = iota((8, VP), 0)
        stat[...] = jnp.where(line == 0, state[0], jnp.where(line == 1, state[1], 0.0))
        each(lambda step: stat_copy(step).start())
        stat_got[me] = stat[...]

    def stat_copy(step):
        target = (peer(step) // 2, lax.rem(peer(step), 2))
        return remote(stat, stat_got.at[me], table_send.at[3, step], table_recv.at[3, step], target)

    def table_last(u):
        each(lambda step: stat_copy(step).wait())
        totals = lax.fori_loop(1, 32, lambda at, held: held + stat_got[at], stat_got[0]) * (1.0 / D)
        _, _, inner, unit, rstd, emb_grad, found = late_parts[1]
        emb_grad = emb_grad + rstd * (inner - totals[0:1] - unit * totals[1:2])
        g_emb[...] = emb_grad
        square[...] += jnp.broadcast_to(found + total_of(emb_grad * emb_grad), (8, 128))

    stages = (stage_first, stage_second, stage_along, stage_pair, stage_end, table_sum, table_end, table_last)
    pending = list(BACKWARD_ORDER)

    def hook():
        for stage, u in pending.pop(0):
            stages[stage](u)

    def done(u):
        if u == 0:
            pl.semaphore_wait(barrier, 31)
        twin_copy(u).start()
        hook()

    names = Kept._fields
    for name in names:
        load(getattr(AT, name), getattr(saved, name), getattr(kept, name))

    load(AT.branch, saved.branch, branch)

    def phase_one(*early_refs):
        e = Early(*early_refs)
        load(weight(0), far[0], grads[0])
        load(AT.slope, saved.slope, e.slope)
        load(AT.active, saved.active, e.active)
        for m in (1, 2, 3):
            load(weight(m), far[m], grads[m])
        for name in Early._fields[2:6]:
            load(getattr(AT, name), getattr(saved, name), getattr(e, name))
        load(weight(4), far[4], grads[4])
        for name in Early._fields[6:8]:
            load(getattr(AT, name), getattr(saved, name), getattr(e, name))
        load(weight(5), far[5], grads[5])
        for name in Early._fields[8:]:
            load(getattr(AT, name), getattr(saved, name), getattr(e, name))
        load(weight(6), far[6], grads[6])
        view = [g.reshape(2, D, n) for g, n in zip(grads, widths)]
        need(*(getattr(AT, name) for name in names))
        norms = kept.norms[...]

        def gain(number):
            return norms[number : number + 1, :]

        need(AT.branch)
        transpose_into(branch, branch_t)
        hook()

        def grad_tile(m, start, left_t, right, half, at):
            lanes = slice(start + half * widths[m] + at, start + half * widths[m] + at + 384)
            view[m][half, :, at : at + 384] = nn(left_t[...], right[:, lanes]).astype(BF16)

        def grad_half(m, start, left_t, right, half):
            for at in range(0, widths[m], 384):
                grad_tile(m, start, left_t, right, half, at)

        for part in range(2):
            need(weight(part))
            if part == 0:
                need(AT.slope)

            def down_back(half, at, part=part):
                lanes = slice(part * 1536 + half * 768 + at, part * 1536 + half * 768 + at + 384)
                back = nn(branch[...], view[part][half, :, at : at + 384])
                e.slope[:, lanes] = (back * e.slope[:, lanes].astype(F32)).astype(BF16)

            if part == 0:
                for at in (0, 384):
                    for half in range(2):
                        down_back(half, at)
                    hook()
                    if at == 0:
                        need(AT.active)
                    for half in range(2):
                        grad_tile(part, 0, branch_t, e.active, half, at)
                    done(at // 384)
            else:
                for half in range(2):
                    for at in (0, 384):
                        down_back(half, at)
                    hook()
                grad_half(part, part * 1536, branch_t, e.active, 0)
                hook()
                grad_half(part, part * 1536, branch_t, e.active, 1)
                done(2)
        for part in range(2):
            need(weight(2 + part))
            for half in range(2):
                start = part * 1536 + half * 768
                back = nt(e.slope[:, start : start + 768], view[2 + part][half])
                upstream[...] = back if start == 0 else upstream[...] + back
                hook()
            if part == 0:
                need(AT.feed_normed_t)
            grad_half(2 + part, part * 1536, e.feed_normed_t, e.slope, 0)
            hook()
            grad_half(2 + part, part * 1536, e.feed_normed_t, e.slope, 1)
            done(3 + part)
        need(AT.unit_2, AT.rstd_2)
        scale_2, shift_2 = back_rows(e.unit_2, e.rstd_2, gain(2), upstream, stream, branch, False)
        hook()
        need(weight(4), AT.col_mixed_t)
        mixed[...] = (nt(branch[:, :384], view[4][0]) + nt(branch[:, 384:], view[4][1])).astype(BF16)
        hook()
        for half in range(2):
            grad_half(4, 0, e.col_mixed_t, branch, half)
        done(5)
        need(AT.col_proj, AT.col_prob)
        proj = e.active

        def attend(at, carry):
            rows = pl.ds(pl.multiple_of((at // PAIRS) * 128, 128), 128)
            lane = lax.rem(at, PAIRS) * 128

            def lanes(part):
                return pl.ds(pl.multiple_of(part * D + lane, 128), 128)

            query = stacked(e.col_proj[rows, lanes(0)])
            key = e.col_proj[rows, lanes(1)]
            value = e.col_proj[rows, lanes(2)]
            above = stacked(mixed[rows, lanes(0)])
            prob = e.col_prob[at]
            grad = nt(above, value)
            grad = prob * (grad - jnp.sum(prob * grad, -1, keepdims=True))
            small = grad.astype(BF16)
            scale = HD ** (-0.5)
            proj[rows, lanes(0)] = (unstacked(nn(small, key), 128) * scale).astype(BF16)
            proj[rows, lanes(1)] = (tn(small, query) * scale).astype(BF16)
            proj[rows, lanes(2)] = tn(prob.astype(BF16), above).astype(BF16)
            return carry

        for part in range(6):
            lax.fori_loop(4 * part, 4 * part + 4, attend, 0, unroll=4)
            hook()
        need(weight(5))
        for half in range(2):
            back = nt(proj[:, half * 1152 : half * 1152 + 1152], view[5][half])
            upstream[...] = back if half == 0 else upstream[...] + back
            hook()
        need(AT.col_normed_t)
        for third in range(3):
            for half in range(2):
                grad_tile(5, 0, e.col_normed_t, proj, half, third * 384)
            done(6 + third)
        need(AT.unit_1, AT.rstd_1)
        scale_1, shift_1 = back_rows(e.unit_1, e.rstd_1, gain(1), upstream, stream, branch, False)
        hook()
        need(weight(6))
        mixed[...] = (nt(branch[:, :384], view[6][0]) + nt(branch[:, 384:], view[6][1])).astype(BF16)
        line = iota((8, D), 0)
        vectors = jnp.zeros((8, D), F32)
        moved = kept.moved[...]
        rows = (scale_1, scale_2, moved[0:1], shift_1, shift_2, moved[1:2])
        for number, row in enumerate(rows):
            vectors = jnp.where(line == number, row, vectors)
        extras = jnp.concatenate([kept.extras[0:1, :], jnp.zeros((1, D - 128), F32)], 1)
        kept.moved[...] = jnp.where(line == 6, extras, vectors)
        hook()

    pl.run_scoped(phase_one, *(pltpu.VMEM(*item) for item in pick_items(Early, SAVED)))

    def phase_two(*late_refs):
        e = Late(*late_refs[:-3])
        in_row, left_hi, left_lo = late_refs[-3:]
        for name in Late._fields:
            load(getattr(AT, name), getattr(saved, name), getattr(e, name))
        load(weight(count), in_row_far.at[0], in_row)
        view = grads[6].reshape(2, D, widths[6])
        late_parts.append(in_row)
        need(AT.row_mixed_t)
        for half in range(2):
            lanes = slice(half * 384, half * 384 + 384)
            view[half] = nn(e.row_mixed_t[...], branch[:, lanes]).astype(BF16)
        done(9)
        need(AT.hot_all, AT.weight_hi, AT.prob, AT.hot_ri, AT.hot_ir)
        shape = (HERE, HERE)
        back = (
            ((iota(shape, 1) >> 4) == (iota(shape, 0) & 31))
            & ((iota(shape, 1) & 15) == (iota(shape, 0) >> 5))
        )
        mixed[...] = nn(one_zero(back).astype(BF16), mixed[...]).astype(BF16)
        value_rows = []
        for hp in range(PAIRS):
            lanes = slice(hp * 128, hp * 128 + 128)
            part = mixed[:, lanes]
            upstream[:, lanes] = nt(part, kept.value_two[hp])
            value_rows.append(unstacked(tn(e.weight_hi[:, lanes], part), 64))
        hook()
        split_heads_to(upstream, left_hi, left_lo)
        hook()
        hot_all = e.hot_all[...]
        grad = nn(left_hi[...], hot_all) + nn(left_lo[...], hot_all)
        extra = jnp.concatenate(
            [kept.touch[...] * (contact_head[h] * COLS) for h in range(HEADS)], 0
        )
        grad = grad + extra
        prob = e.prob[...]
        grad = prob * (grad - jnp.sum(prob * grad, -1, keepdims=True))
        low_grad = grad.astype(BF16)
        hook()
        merge_heads(low_grad, e.hot_all, branch, None)
        hook()
        table_pair = nn(e.hot_ri[...], branch[...])
        stream_hi, stream_lo = split_two(stream[...])
        hot_ir = e.hot_ir[...]
        table_grad = kept.grad_head[...] + nn(hot_ir, stream_hi) + nn(hot_ir, stream_lo)
        value_grad = jnp.concatenate(value_rows, 1)
        last = jnp.where(iota((8, D), 0) == 7, table_grad[32:33], kept.moved[...])
        top, rest = split_two(last)
        groups = [table_pair[4:20], table_pair[20:36], value_grad[4:20], value_grad[20:36]]
        groups += [table_grad[0:16], table_grad[16:32]]
        groups += [jnp.concatenate([top.astype(F32), rest.astype(F32)], 0)]
        for number, group in enumerate(groups):
            for third in range(3):
                table[3 * number + third] = group[:, third * 256 : third * 256 + 256].astype(BF16)
        each(table_start)
        hook()
        hook()

    pl.run_scoped(
        phase_two,
        *(pltpu.VMEM(*item) for item in pick_items(Late, SAVED)),
        pltpu.VMEM((24, 3 * D), F32),
        pltpu.VMEM((HEADS * WIDE, ROWS * VP), BF16),
        pltpu.VMEM((HEADS * WIDE, ROWS * VP), BF16),
    )
    assert not pending

    def square_copy(step):
        other = lax.rem(me + step, 32)
        return remote(
            square, square_got.at[me], table_send.at[2, step], table_recv.at[2, step], (other // 2, lax.rem(other, 2))
        )

    each(lambda step: square_copy(step).start())
    square_got[me] = square[...]
    each(lambda step: table_wait_send(step))
    for u in range(units):
        for item in pair(u):
            item.wait_send()
    each(lambda step: square_copy(step).wait())
    total_square = lax.fori_loop(1, 32, lambda at, held: held + square_got[at], square_got[0])[0:1]
    vector = table_out[18].astype(F32)
    vector = vector[6:7, :128] + vector[14:15, :128]
    counted = kept.extras[1:2, :]
    column = iota((1, 128), 1)
    contact = jnp.where(column <= HEADS, vector, 0.0)
    total_square = total_square + total_of(contact * contact)
    grad_norm = jnp.sqrt(total_square)
    factor = jnp.minimum(1.0, MAX_NORM / grad_norm)
    losses = (
        (0, vector[:, HEADS + 1 : HEADS + 2]),
        (1, counted[:, 0:1]),
        (2, vector[:, HEADS + 2 : HEADS + 3]),
        (3, counted[:, 1:2]),
    )
    loss_row = jnp.zeros((1, 128), F32)
    for at, value in losses:
        loss_row = jnp.where(column == at, value, loss_row)
    number = iota((8, 128), 0)
    result = jnp.zeros((8, 128), F32)
    for at, row in enumerate((contact, counted, factor, grad_norm, loss_row)):
        result = jnp.where(number == at, row, result)
    stats[...] = result


def backward_call(contact_head, weights, in_row, saved):
    widths = GRAD_WIDTHS
    count = len(widths)
    inside = pl.BlockSpec(memory_space=pltpu.VMEM)
    anywhere = pl.BlockSpec(memory_space=pl.ANY)

    units = len(GRAD_UNITS)

    def shapes(lead, dtype, other=None):
        leads = [other if other and u in Z_FIRST else lead for u in range(units)]
        return [pltpu.VMEM((*at, n), dtype) for at, (_, _, n, _) in zip(leads, GRAD_UNITS)]

    outs = pl.pallas_call(
        backward_kernel,
        out_shape=[jax.ShapeDtypeStruct((2, 24, n), F32) for n in widths]
        + [
            jax.ShapeDtypeStruct((24, 3 * D), F32),
            jax.ShapeDtypeStruct((24, VP), F32),
            jax.ShapeDtypeStruct((8, 24), F32),
            jax.ShapeDtypeStruct((8, 128), F32),
        ],
        in_specs=[pl.BlockSpec(memory_space=pltpu.SMEM)] + [anywhere] * (1 + count + len(SAVED)),
        out_specs=[inside] * (4 + count),
        scratch_shapes=[pltpu.VMEM((2, NZ, NY, 2, 48, n), BF16) for n in widths]
        + [pltpu.VMEM(*item) for item in pick_items(Kept, SAVED)]
        + [
            pltpu.VMEM((HERE, D), F32),
            pltpu.VMEM((HERE, D), BF16),
            pltpu.VMEM((D, HERE), BF16),
            pltpu.VMEM((HERE, D), BF16),
        ]
        + [
            pltpu.VMEM((NZ, NY, 2, 48, n) if paired else (2, NZ, NY, 48, n), BF16)
            for _, _, n, paired in GRAD_UNITS
        ]
        + shapes((2, 2, 48), BF16, (3, 2, 2, 48))
        + shapes((2, 2, 48), BF16, (16,))
        + shapes((2, 48), BF16, (2, 48))
        + shapes((2, 48), BF16, (48,))
        + shapes((3, 48), BF16, (16,))
        + shapes((2, 24), F32)
        + shapes((24,), F32)
        + [
            pltpu.VMEM((PIECES, 16, 256), BF16),
            pltpu.VMEM((PIECES, 16, 256), BF16),
            pltpu.VMEM((32, 16, 256), BF16),
            pltpu.VMEM((8, 128), F32),
            pltpu.VMEM((32, 8, 128), F32),
            pltpu.VMEM((8, VP), F32),
            pltpu.VMEM((32, 8, VP), F32),
            pltpu.SemaphoreType.DMA((4, 32)),
            pltpu.SemaphoreType.DMA((4, 32)),
            pltpu.SemaphoreType.DMA((units, 9)),
            pltpu.SemaphoreType.DMA((units, 9)),
            pltpu.SemaphoreType.DMA((len(SAVED) + count + 1,)),
        ],
        compiler_params=pltpu.CompilerParams(
            collective_id=1, has_side_effects=True, vmem_limit_bytes=63 * 2**20
        ),
    )(contact_head, *weights, in_row, *saved)
    return outs[:count], outs[count:]


UPDATE_RATES = (LEARN_RATE,) * 4 + (VECTOR_RATE,) * 3


def update_kernel(*refs):
    given, far, held, results = refs[:32], refs[32:60], refs[60:92], refs[92:120]
    sems, out_sems = refs[120:122]
    outs, copies = results[:21], results[21:26]
    loss_ref, norm_ref = results[26:]

    def leave(*numbers):
        for n in numbers:
            pltpu.make_async_copy(results[n], far[n], out_sems.at[n]).start()

    moves = [pltpu.make_async_copy(a, b, sems.at[n]) for n, (a, b) in enumerate(zip(given, held))]
    for item in moves:
        item.start()
    reduced, g_in, g_emb, g_norm, stats = held[:7], held[7], held[8], held[9], held[10]
    states = [held[11 + 3 * n : 14 + 3 * n] for n in range(7)]
    outs = [outs[3 * n : 3 * n + 3] for n in range(7)]
    order = feature_order()
    for item in moves[4:11]:
        item.wait()
    factor = stats[2:3, 0:1]
    loss_ref[...] = stats[4:5, 0:4]
    norm_ref[...] = stats[3:4, 0:1]

    def natural(values):
        top, rest = split_two(values)
        last = (values - top.astype(F32) - rest.astype(F32)).astype(BF16)
        return nt(top, order) + nt(rest, order) + nt(last, order)

    def update(number, where, grad):
        master, first, second = (ref[where] for ref in states[number])
        new, first, second = adam_update(master, first, second, grad * factor, UPDATE_RATES[number])
        for ref, value in zip(outs[number], (new, first, second)):
            ref[where] = value
        if number < 5:
            copies[number][where] = new.astype(BF16)

    every = slice(None)
    g_out_col, g_in_col, g_out_row = reduced[4:]
    for item in moves[11:17]:
        item.wait()
    for half in range(2):
        lanes = slice(half * 1152, half * 1152 + 1152)
        update(0, (0, every, lanes), g_in[:, lanes])
        update(0, (1, every, lanes), g_in_col[half])
        lanes = slice(half * 384, half * 384 + 384)
        update(1, (0, every, lanes), natural(g_out_row[half]))
        update(1, (1, every, lanes), natural(g_out_col[half]))
    leave(0, 1, 2, 21, 3, 4, 5, 22, 26, 27)
    for item in moves[:4] + moves[17:]:
        item.wait()
    for half in range(2):
        for part in range(2):
            start = part * 1536 + half * 768
            lanes = slice(start, start + 768)
            update(2, (every, lanes), reduced[2 + part][half])
            update(3, (every, lanes), reduced[part][half])
    leave(6, 7, 8, 23, 9, 10, 11, 24)
    update(4, (every, every), g_emb[:, :VOCAB])
    update(5, (every, every), g_norm[...])
    update(6, (every, every), stats[0:1, : HEADS + 1])
    leave(12, 13, 14, 25, 15, 16, 17, 18, 19, 20)
    for n in range(28):
        pltpu.make_async_copy(results[n], far[n], out_sems.at[n]).wait()


def update_call(reduced, g_in, g_emb, g_norm, stats, states):
    anywhere = pl.BlockSpec(memory_space=pl.ANY)
    flat = [item for state in states for item in state]
    shapes = [jax.ShapeDtypeStruct(item.shape, F32) for item in flat]
    shapes += [jax.ShapeDtypeStruct(states[n][0].shape, BF16) for n in range(5)]
    shapes += [jax.ShapeDtypeStruct((1, 4), F32), jax.ShapeDtypeStruct((1, 1), F32)]
    given = (*reduced, g_in, g_emb, g_norm, stats, *flat)
    return pl.pallas_call(
        update_kernel,
        out_shape=shapes,
        in_specs=[anywhere] * len(given),
        out_specs=[anywhere] * len(shapes),
        scratch_shapes=[pltpu.VMEM(item.shape, F32) for item in given]
        + [pltpu.VMEM(item.shape, item.dtype) for item in shapes]
        + [
            pltpu.SemaphoreType.DMA((len(given),)),
            pltpu.SemaphoreType.DMA((len(shapes),)),
            pltpu.VMEM((44, 512, 512), F32),
        ],
        compiler_params=pltpu.CompilerParams(vmem_limit_bytes=62 * 2**20),
    )(*given)


def adam_update(master, first, second, grad_part, rate):
    first = BETA_ONE * first + (1.0 - BETA_ONE) * grad_part
    second = BETA_TWO * second + (1.0 - BETA_TWO) * grad_part * grad_part
    scaled = first * (1.0 / (1.0 - BETA_ONE**STEP))
    moved = scaled / (jnp.sqrt(second * (1.0 / (1.0 - BETA_TWO**STEP))) + ADAM_EPS)
    return (master - rate * (moved + WEIGHT_DECAY * master), first, second)


def shards(
    tokens,
    targets,
    masked,
    contact_pairs,
    labels,
    attention_in_master,
    attention_in_first,
    attention_in_second,
    attention_out_master,
    attention_out_first,
    attention_out_second,
    feed_up_master,
    feed_up_first,
    feed_up_second,
    feed_down_master,
    feed_down_first,
    feed_down_second,
    embedding_master,
    embedding_first,
    embedding_second,
    norm_params_master,
    norm_params_first,
    norm_params_second,
    contact_head_master,
    contact_head_first,
    contact_head_second,
):
    both = ("seq", "col")
    micro, rows_here, cols_here = tokens.shape
    ncol = lax.axis_size("col")
    ndev = lax.axis_size("seq") * ncol
    cols = cols_here * ncol
    me = lax.axis_index("seq") * ncol + lax.axis_index("col")
    per = ndev // micro
    cw = cols // per
    mine = me // per
    base = (me % per) * cw
    shard = D // ndev

    tiled = lax.axis_size("seq") == 16 and ncol == 2
    if tiled:
        raw = (
            tokens,
            targets,
            masked,
            contact_pairs.transpose(0, 2, 1),
            labels,
            embedding_master.T,
            norm_params_master,
            attention_in_master,
            attention_out_master,
            feed_up_master,
            feed_down_master.T,
        )
        weights, saved = forward_call(raw, contact_head_master)
        reduced, (g_in, g_emb, g_norm, stats) = backward_call(
            contact_head_master, [weights[n] for n in (5, 6, 3, 4, 2, 1, 0)], attention_in_master, saved
        )
        states = (
            (attention_in_master, attention_in_first, attention_in_second),
            (attention_out_master, attention_out_first, attention_out_second),
            (feed_up_master, feed_up_first, feed_up_second),
            (feed_down_master.T, feed_down_first.T, feed_down_second.T),
            (embedding_master.T, embedding_first.T, embedding_second.T),
            (norm_params_master, norm_params_first, norm_params_second),
            (contact_head_master[None], contact_head_first[None], contact_head_second[None]),
        )
        outs = update_call(reduced, g_in, g_emb, g_norm, stats, states)
        return (
            *outs[:9],
            *(item.T for item in outs[9:15]),
            *outs[15:18],
            *(item[0] for item in outs[18:21]),
            *outs[21:24],
            *(item.T for item in outs[24:26]),
            outs[26][0],
            outs[27][0, 0],
        )
    inputs = jnp.where(masked > 0, MASK_ID, tokens)
    masters = [
        jnp.concatenate(
            [
                jnp.pad(embedding_master.T, ((0, 0), (0, 128 - VOCAB))),
                jnp.pad(norm_params_master.T, ((0, 0), (0, 120))),
            ],
            1,
        ),
        attention_in_master[0],
        attention_out_master[0],
        attention_in_master[1],
        attention_out_master[1],
        feed_up_master,
        feed_down_master.T,
    ]
    whole = jnp.stack([inputs, targets])
    whole = lax.all_gather(lax.all_gather(whole, "col", axis=3, tiled=True), "seq", axis=2, tiled=True)
    pairs_all = lax.all_gather(
        jnp.concatenate([contact_pairs, labels[:, :, None]], -1), both, axis=1, tiled=True
    )
    gathered = []
    for master in masters:
        full = lax.all_gather(master.astype(BF16), both, axis=0, tiled=True)
        gathered.append(full.reshape(D, 2, -1).transpose(1, 0, 2))
    counts = (
        jnp.sum(whole[0] == MASK_ID).astype(F32),
        jnp.sum(pairs_all[..., 2] >= 0).astype(F32),
    )
    ids_all = lax.dynamic_index_in_dim(whole[0], mine, 0, False)
    ids_local = lax.dynamic_slice_in_dim(ids_all, base, cw, 1)
    targets_local = lax.dynamic_slice_in_dim(
        lax.dynamic_index_in_dim(whole[1], mine, 0, False), base, cw, 1
    )
    pairs = lax.dynamic_index_in_dim(pairs_all, mine, 0, False)

    table = gathered[0][0][:, :VP].T
    norms = gathered[0][1][:, :8].T.astype(F32)
    in_row, out_row, in_col, out_col, up_w, down_t = (
        jnp.concatenate([g[0], g[1]], 1) for g in gathered[1:]
    )
    big = (in_row, in_col, out_row, out_col, up_w, down_t)

    grads, tables, contact_total, mlm_total, bce_total, kept = step(
        big,
        table,
        norms,
        contact_head_master,
        ids_all,
        ids_local.reshape(-1),
        ids_local.T.reshape(-1),
        targets_local.T.reshape(-1),
        pairs[:, 0] - base,
        pairs[:, 1],
        pairs[:, 2],
        counts,
        cw,
    )
    table_pair, value_grad, table_grad, vectors = tables
    extras = jnp.zeros((2, D), F32).at[0, : HEADS + 3].set(
        jnp.concatenate([contact_total, mlm_total[None], bce_total[None]])
    )
    sums = jnp.concatenate([table_pair[:40], value_grad[:40], table_grad[:40], vectors, extras])
    flat_grad = jnp.concatenate([g.astype(BF16) for g in grads], 1)
    reduced = lax.psum_scatter(flat_grad, both, scatter_dimension=0, tiled=True).astype(F32)
    g_in_col, g_out_row, g_out_col, g_up, g_down = jnp.split(
        reduced, [3 * D, 4 * D, 5 * D, 5 * D + FF], 1
    )
    sums = lax.psum(sums, both)
    unit_t, rstd_t, normed_t, query_t, key_t = kept
    rows_all = ids_all.shape[0]
    spare = ((0, VP - 40), (0, 0))
    table_pair, value_grad, table_grad = (
        jnp.pad(sums[a : a + 40], spare) for a in (0, 40, 80)
    )
    vectors = sums[120:126]
    contact_grad, mlm_total, bce_total = (
        sums[126, : HEADS + 1], sums[126, HEADS + 1], sums[126, HEADS + 2]
    )
    row_scale = (HD * rows_all) ** (-0.5)
    query_grad = []
    key_grad = []
    for h in range(HEADS):
        pair = heads_of(table_pair, h)
        query_grad.append(jnp.dot(pair, heads_of(key_t, h).astype(F32), precision=PRECISE))
        key_grad.append(jnp.dot(pair.T, heads_of(query_t, h).astype(F32), precision=PRECISE))
    proj_grad = jnp.concatenate(
        [
            jnp.concatenate(query_grad, 1) * row_scale,
            jnp.concatenate(key_grad, 1) * row_scale,
            value_grad,
        ],
        1,
    )
    proj_hi, proj_lo = split_two(proj_grad)
    normed_grad = nt(proj_hi, in_row) + nt(proj_lo, in_row)
    back_t, scale_0, shift_0 = norm_back(unit_t, rstd_t, norms[0], normed_grad)
    table_grad = table_grad + back_t
    low = me * shard
    normed_mine = lax.dynamic_slice_in_dim(normed_t, low, shard, 1)
    grad_in_row = tn(normed_mine, proj_hi) + tn(normed_mine, proj_lo)
    norm_grad = jnp.concatenate([scale_0[None], vectors[:3], shift_0[None], vectors[3:]])
    table_mine = lax.dynamic_slice_in_dim(table_grad[:VOCAB], low, shard, 1)
    norm_mine = lax.dynamic_slice_in_dim(norm_grad, low, shard, 1)
    reduced_all = (g_in_col, g_out_row, g_out_col, g_up, g_down)

    local_square = (
        sum(jnp.sum(g * g) for g in reduced_all)
        + jnp.sum(grad_in_row * grad_in_row)
        + jnp.sum(table_mine * table_mine)
        + jnp.sum(norm_mine * norm_mine)
    )
    square = lax.psum(local_square, both) + jnp.sum(contact_grad * contact_grad)
    grad_norm = jnp.sqrt(square)
    factor = jnp.minimum(1.0, MAX_NORM / grad_norm)
    in_new, in_moment, in_square = adam_update(
        attention_in_master, attention_in_first, attention_in_second, jnp.stack([grad_in_row, g_in_col]) * factor, LEARN_RATE
    )
    out_new, out_moment, out_square = adam_update(
        attention_out_master, attention_out_first, attention_out_second, jnp.stack([g_out_row, g_out_col]) * factor, LEARN_RATE
    )
    up_new, up_moment, up_square = adam_update(
        feed_up_master, feed_up_first, feed_up_second, g_up * factor, LEARN_RATE
    )
    down_new, down_moment, down_square = adam_update(
        feed_down_master, feed_down_first, feed_down_second, g_down.T * factor, LEARN_RATE
    )
    table_new, table_moment, table_square = adam_update(
        embedding_master, embedding_first, embedding_second, table_mine * factor, VECTOR_RATE
    )
    norm_new, norm_moment, norm_square = adam_update(
        norm_params_master, norm_params_first, norm_params_second, norm_mine * factor, VECTOR_RATE
    )
    head_new, head_moment, head_square = adam_update(
        contact_head_master, contact_head_first, contact_head_second, contact_grad * factor, VECTOR_RATE
    )
    loss_parts = jnp.stack([mlm_total, counts[0], bce_total, counts[1]])
    return (
        in_new, in_moment, in_square,
        out_new, out_moment, out_square,
        up_new, up_moment, up_square,
        down_new, down_moment, down_square,
        table_new, table_moment, table_square,
        norm_new, norm_moment, norm_square,
        head_new, head_moment, head_square,
        in_new.astype(BF16), out_new.astype(BF16), up_new.astype(BF16), down_new.astype(BF16), table_new.astype(BF16),
        loss_parts, grad_norm,
    )


def solution(mesh):
    both = ("seq", "col")
    cells = P(None, "seq", "col")
    stack = P(None, both, None)
    row_split = P(both, None)
    col_split = P(None, both)
    weights = [stack] * 6 + [row_split] * 3 + [col_split] * 9 + [P()] * 3
    return jax.shard_map(
        shards,
        mesh=mesh,
        in_specs=(cells, cells, cells, stack, col_split, *weights),
        out_specs=(*weights, stack, stack, row_split, col_split, col_split, P(), P()),
        check_vma=False,
    )
```

```python
import typing

import jax
import jax.numpy as jnp
from jax import lax
from jax.experimental import pallas as pl
from jax.experimental.pallas import tpu as pltpu
from jax.sharding import PartitionSpec as P

D = 768
HEADS = 12
HD = 64
FF = 3072
VOCAB = 33
VP = 64
STEP = 10

NORM_EPS = 1e-05
MASK_ID = 32
MAX_NORM = 0.001
LEARN_RATE = 0.05
VECTOR_RATE = 0.5
BETA_ONE = 0.9
BETA_TWO = 0.95
ADAM_EPS = 1e-08
WEIGHT_DECAY = 0.01
PRECISE = lax.Precision.HIGHEST
F32 = jnp.float32
BF16 = jnp.bfloat16


def nn(left, right):
    return lax.dot_general(left, right, (((1,), (0,)), ((), ())), preferred_element_type=F32)


def tn(left, right):
    return lax.dot_general(left, right, (((0,), (0,)), ((), ())), preferred_element_type=F32)


def nt(left, right):
    return lax.dot_general(left, right, (((1,), (1,)), ((), ())), preferred_element_type=F32)


def split_two(values):
    high = values.astype(BF16)
    return high, (values - high.astype(F32)).astype(BF16)


def norm_stats(values):
    centre = values - jnp.mean(values, -1, keepdims=True)
    rstd = lax.rsqrt(jnp.mean(centre * centre, -1, keepdims=True) + NORM_EPS)
    return centre * rstd, rstd


def norm_back(unit, rstd, scale_vec, upstream):
    inner = upstream * scale_vec
    grad = rstd * (
        inner - jnp.mean(inner, -1, keepdims=True) - unit * jnp.mean(inner * unit, -1, keepdims=True)
    )
    return grad, jnp.sum(upstream * unit, 0), jnp.sum(upstream, 0)


GELU_K = 0.7978845608028654
GELU_C = 0.044715


def gelu_parts(up):
    square = up * up
    bent = jnp.tanh(GELU_K * up * (1.0 + GELU_C * square))
    half = 0.5 * (1.0 + bent)
    slope = half + 0.5 * up * (1.0 - bent * bent) * GELU_K * (1.0 + 3.0 * GELU_C * square)
    return up * half, slope


def heads_of(block, head):
    return block[:, head * HD : (head + 1) * HD]


def step(big, table, norms, contact_head, ids_all, ids_ri, ids_ir, targets_ir, pair_first, pair_second, labels, counts, cw):
    in_row, in_col, out_row, out_col, up_w, down_t = big
    rows, cols = ids_all.shape
    here = rows * cw
    row_scale = (HD * rows) ** (-0.5)
    vocab = jnp.arange(VP)[:, None]
    hot_all = (ids_all[:, None, :] == vocab[None]).astype(BF16).reshape(rows * VP, cols)
    hot_ri = (ids_ri[None, :] == vocab).astype(BF16)
    hot_ir = (ids_ir[None, :] == vocab).astype(BF16)
    spot = jnp.arange(here)
    perm = (
        ((spot // rows)[:, None] == (spot % cw)[None, :])
        & ((spot % rows)[:, None] == (spot // cw)[None, :])
    ).astype(BF16)

    def to_heads(block):
        return block.reshape(rows, cw, HEADS, VP).transpose(2, 1, 0, 3).reshape(HEADS * cw, rows * VP)

    def to_tokens(block):
        return block.reshape(HEADS, cw, rows, VP).transpose(2, 1, 0, 3).reshape(here, HEADS * VP)

    def per_head(block, other, how):
        return jnp.concatenate(
            [how(heads_of(block, h), heads_of(other, h)) for h in range(HEADS)], -1
        )

    table_f = table.astype(F32)
    unit_t, rstd_t = norm_stats(table_f)
    normed_t = (unit_t * norms[0] + norms[4]).astype(BF16)
    proj_t = nn(normed_t, in_row).astype(BF16)
    query_t, key_t, value_t = proj_t[:, :D], proj_t[:, D : 2 * D], proj_t[:, 2 * D :]

    pair_t = per_head(query_t, key_t, nt)
    pair_hi, pair_lo = split_two(pair_t)
    left_hi = to_heads(tn(hot_ri, pair_hi).astype(BF16))
    left_lo = to_heads(tn(hot_ri, pair_lo).astype(BF16))
    score = (nn(left_hi, hot_all) + nn(left_lo, hot_all)) * row_scale
    prob = jax.nn.softmax(score, axis=-1)
    prob_low = prob.astype(BF16)
    weight_t = to_tokens(nt(prob_low, hot_all))
    weight_hi, weight_lo = split_two(weight_t)
    row_mixed_ri = (
        per_head(weight_hi, value_t, nn) + per_head(weight_lo, value_t, nn)
    ).astype(BF16)
    row_mixed = nn(perm, row_mixed_ri).astype(BF16)
    embedded = tn(hot_ir, table)
    after_row = embedded + nn(row_mixed, out_row)

    prob_cube = prob_low.astype(F32).reshape(HEADS, cw, cols)
    head_sum = jnp.sum(prob_cube * contact_head[:HEADS, None, None], 0)
    first_hot = (pair_first[None, :] == jnp.arange(cw)[:, None]).astype(F32)
    second_hot = (pair_second[None, :] == jnp.arange(cols)[:, None]).astype(BF16)
    sum_hi, sum_lo = split_two(head_sum)
    sum_last = (head_sum - sum_hi.astype(F32) - sum_lo.astype(F32)).astype(BF16)
    picked = nn(sum_hi, second_hot) + nn(sum_lo, second_hot) + nn(sum_last, second_hot)
    contact_logit = jnp.sum(picked * first_hot, 0) * cols + contact_head[HEADS]
    owned = jnp.sum(first_hot, 0) > 0
    valid = (labels >= 0) & owned
    positive = (labels == 1).astype(F32)
    bce_sum = jnp.sum(
        jnp.where(valid, jax.nn.softplus(contact_logit) - positive * contact_logit, 0.0)
    )
    coef = jnp.where(valid, jax.nn.sigmoid(contact_logit) - positive, 0.0) / counts[1]
    coef_hi, coef_lo = split_two(coef)
    first_low = first_hot.astype(BF16)
    touch = nt(first_low * coef_hi[None], second_hot) + nt(first_low * coef_lo[None], second_hot)
    grad_contact = jnp.concatenate(
        [jnp.sum(prob_cube * touch[None], (1, 2)) * cols, jnp.sum(coef)[None]]
    )

    unit_1, rstd_1 = norm_stats(after_row)
    col_normed = (unit_1 * norms[1] + norms[5]).astype(BF16)
    col_proj = nn(col_normed, in_col).astype(BF16)
    group = 128 if here % 128 == 0 and 128 % rows == 0 else here
    groups = here // group
    lane = jnp.arange(group)
    same = (lane[:, None] // rows) == (lane[None, :] // rows)

    def cut(block):
        return block.reshape(groups, group, HEADS, HD)

    col_query, col_key, col_value = (cut(col_proj[:, k * D : (k + 1) * D]) for k in range(3))
    col_score = jnp.einsum("gqhe,gkhe->ghqk", col_query, col_key, preferred_element_type=F32) * HD ** (-0.5)
    col_prob = jax.nn.softmax(jnp.where(same, col_score, -1e30), axis=-1)
    col_prob_low = col_prob.astype(BF16)
    col_mixed = (
        jnp.einsum("ghqk,gkhe->gqhe", col_prob_low, col_value, preferred_element_type=F32)
        .astype(BF16)
        .reshape(here, D)
    )
    after_col = after_row + nn(col_mixed, out_col)

    unit_2, rstd_2 = norm_stats(after_col)
    feed_normed = (unit_2 * norms[2] + norms[6]).astype(BF16)
    hidden_up = nn(feed_normed, up_w)
    active, slope = gelu_parts(hidden_up)
    active = active.astype(BF16)
    after_feed = after_col + nt(active, down_t)
    unit_3, rstd_3 = norm_stats(after_feed)
    head_normed = (unit_3 * norms[3] + norms[7]).astype(BF16)
    logits = nt(table, head_normed) * D ** (-0.5)
    logits = jnp.where(vocab < VOCAB, logits, -1e30)
    top = jnp.max(logits, 0, keepdims=True)
    shifted = logits - top
    log_probs = shifted - jnp.log(jnp.sum(jnp.exp(shifted), 0, keepdims=True))
    target_hot = (targets_ir[None, :] == vocab).astype(F32)
    keep = ids_ir[None, :] == MASK_ID
    mlm_sum = -jnp.sum(jnp.where(keep & (target_hot > 0), log_probs, 0.0))
    logit_grad = jnp.where(keep, jnp.exp(log_probs) - target_hot, 0.0) / counts[0]
    logit_low = (logit_grad * D ** (-0.5)).astype(BF16)

    grad_head = nn(logit_low, head_normed)
    stream, scale_3, shift_3 = norm_back(unit_3, rstd_3, norms[3], tn(logit_low, table))
    branch = stream.astype(BF16)
    grad_down = tn(branch, active)
    up_low = (nn(branch, down_t) * slope).astype(BF16)
    grad_up = tn(feed_normed, up_low)
    inner, scale_2, shift_2 = norm_back(unit_2, rstd_2, norms[2], nt(up_low, up_w))
    stream = stream + inner
    branch = stream.astype(BF16)
    grad_out_col = tn(col_mixed, branch)
    mixed_low = nt(branch, out_col).astype(BF16)
    mixed_cut = cut(mixed_low)
    prob_grad = jnp.einsum("gqhe,gkhe->ghqk", mixed_cut, col_value, preferred_element_type=F32)
    score_grad = col_prob * (prob_grad - jnp.sum(col_prob * prob_grad, -1, keepdims=True))
    score_low = score_grad.astype(BF16)
    grad_q = jnp.einsum("ghqk,gkhe->gqhe", score_low, col_key, preferred_element_type=F32)
    grad_k = jnp.einsum("ghqk,gqhe->gkhe", score_low, col_query, preferred_element_type=F32)
    grad_v = jnp.einsum("ghqk,gqhe->gkhe", col_prob_low, mixed_cut, preferred_element_type=F32)
    proj_low = jnp.concatenate(
        [
            (grad_q * HD ** (-0.5)).reshape(here, D),
            (grad_k * HD ** (-0.5)).reshape(here, D),
            grad_v.reshape(here, D),
        ],
        -1,
    ).astype(BF16)
    grad_in_col = tn(col_normed, proj_low)
    inner, scale_1, shift_1 = norm_back(unit_1, rstd_1, norms[1], nt(proj_low, in_col))
    stream = stream + inner
    branch = stream.astype(BF16)
    grad_out_row = tn(row_mixed, branch)
    mixed_low = nt(branch, out_row).astype(BF16)
    mixed_ri = tn(perm, mixed_low).astype(BF16)
    drive_hi, drive_lo = split_two(per_head(mixed_ri, value_t, nt))
    prob_grad = nn(to_heads(drive_hi), hot_all) + nn(to_heads(drive_lo), hot_all)
    prob_grad = prob_grad + (
        touch[None] * (contact_head[:HEADS, None, None] * cols)
    ).reshape(HEADS * cw, cols)
    score_grad = prob * (prob_grad - jnp.sum(prob * prob_grad, -1, keepdims=True))
    score_low = score_grad.astype(BF16)
    spread = to_tokens(nt(score_low, hot_all)).astype(BF16)
    table_pair = nn(hot_ri, spread)
    value_grad = per_head(weight_hi, mixed_ri, tn)
    stream_hi, stream_lo = split_two(stream)
    lookup_grad = nn(hot_ir, stream_hi) + nn(hot_ir, stream_lo)
    vectors = jnp.stack([scale_1, scale_2, scale_3, shift_1, shift_2, shift_3])
    return (
        (grad_in_col, grad_out_row, grad_out_col, grad_up, grad_down),
        (table_pair, value_grad, grad_head + lookup_grad, vectors),
        grad_contact,
        mlm_sum,
        bce_sum,
        (unit_t, rstd_t, normed_t, query_t, key_t),
    )


MESH = pl.DeviceIdType.MESH
NZ, NY = 4, 2


def place():
    s, c = lax.axis_index("seq"), lax.axis_index("col")
    z, y, k = s // 4, lax.rem(s // 2, 2), lax.rem(s, 2)
    return z, y, k, c


def device(z, y, k, c):
    return (z * 4 + y * 2 + k, c)


def greet_all():
    z, y, k, c = place()
    me = (z * 4 + y * 2 + k) * 2 + c
    barrier = pltpu.get_barrier_semaphore()

    def signal(step, carry):
        other = lax.rem(me + step, 32)
        pl.semaphore_signal(
            barrier, inc=1, device_id=(other // 2, lax.rem(other, 2)), device_id_type=MESH
        )
        return carry

    lax.fori_loop(1, 32, signal, 0)
    return barrier


def remote(src, dst, send, recv, target):
    return pltpu.make_async_remote_copy(
        src_ref=src, dst_ref=dst, send_sem=send, recv_sem=recv, device_id=target, device_id_type=MESH
    )


ROWS, COLS, WIDE, HERE = 16, 512, 32, 512
PAIRS = 6
SLOTS = 1024
UP_TILE = 384


def iota(shape, dim):
    return lax.broadcasted_iota(jnp.int32, shape, dim)


def one_zero(test):
    return jnp.where(test, 1.0, 0.0)


def total_of(values):
    return jnp.sum(jnp.sum(values, 0, keepdims=True), 1, keepdims=True)


def half_lanes(values, side):
    lane = iota(values.shape, len(values.shape) - 1)
    keep = (lane < 64) if side == 0 else (lane >= 64)
    return jnp.where(keep, values.astype(F32), 0.0).astype(BF16)


def stacked(values):
    return jnp.concatenate([half_lanes(values, 0), half_lanes(values, 1)], 0)


def unstacked(values, count):
    lane = iota((count, 128), 1)
    return jnp.where(lane < 64, values[:count], values[count:])


def swap_blocks(first, second):
    lane = iota(first.shape, 1)
    low = jnp.where(lane < 64, first, pltpu.roll(second, 64, 1))
    high = jnp.where(lane < 64, pltpu.roll(first, 64, 1), second)
    return low, high


def split_heads_to(source, high_ref, low_ref):
    for rp in range(ROWS // 2):
        for hp in range(PAIRS):
            lanes = slice(hp * 128, hp * 128 + 128)
            first = source[rp * 64 : rp * 64 + 32, lanes]
            second = source[rp * 64 + 32 : rp * 64 + 64, lanes]
            for side, block in enumerate(swap_blocks(first, second)):
                top, rest = split_two(block)
                rows = slice((2 * hp + side) * 32, (2 * hp + side) * 32 + 32)
                high_ref[rows, rp * 128 : rp * 128 + 128] = top
                low_ref[rows, rp * 128 : rp * 128 + 128] = rest


def merge_heads(probs, hot_all, high_ref, low_ref):
    for rp in range(ROWS // 2):
        if rp % 2 == 0:
            blocks = nt(probs, hot_all[rp * 128 : rp * 128 + 256, :])
        block = blocks[:, (rp % 2) * 128 : (rp % 2) * 128 + 128]
        for hp in range(PAIRS):
            first = block[hp * 64 : hp * 64 + 32]
            second = block[hp * 64 + 32 : hp * 64 + 64]
            for side, part in enumerate(swap_blocks(first, second)):
                top, rest = split_two(part)
                rows = slice(rp * 64 + side * 32, rp * 64 + side * 32 + 32)
                high_ref[rows, hp * 128 : hp * 128 + 128] = top
                if low_ref is not None:
                    low_ref[rows, hp * 128 : hp * 128 + 128] = rest


def norm_rows(source, gain, bias, unit_ref, rstd_ref, normed_ref):
    def body(at, carry):
        rows = pl.ds(pl.multiple_of(at * 64, 64), 64)
        values = source[rows, :]
        centre = values - jnp.sum(values, -1, keepdims=True) * (1.0 / D)
        rstd = lax.rsqrt(jnp.sum(centre * centre, -1, keepdims=True) * (1.0 / D) + NORM_EPS)
        unit = centre * rstd
        unit_ref[rows, :] = unit
        rstd_ref[rows, :] = jnp.broadcast_to(rstd, (64, 128))
        normed_ref[rows, :] = (unit * gain + bias).astype(BF16)
        return carry

    lax.fori_loop(0, HERE // 64, body, 0)


def transpose_into(source, target):
    def body(at, carry):
        rows = pl.ds(pl.multiple_of(at * 128, 128), 128)
        target[:, rows] = source[rows, :].astype(F32).T.astype(BF16)
        return carry

    lax.fori_loop(0, HERE // 128, body, 0)


def over_tiles(width, tile, body):
    for half in range(2):

        def step(at, carry, half=half):
            body(half, pl.multiple_of(at * tile, tile))
            return carry

        lax.fori_loop(0, width // tile, step, 0)


def column_mask():
    rows, lanes = iota((256, 128), 0), iota((256, 128), 1)
    return ((rows & 127) >> 4) == (lanes >> 4)


class Saved(typing.NamedTuple):
    stream: typing.Any
    branch: typing.Any
    unit_1: typing.Any
    unit_2: typing.Any
    rstd_1: typing.Any
    rstd_2: typing.Any
    row_mixed_t: typing.Any
    col_normed_t: typing.Any
    col_mixed_t: typing.Any
    feed_normed_t: typing.Any
    col_proj: typing.Any
    col_prob: typing.Any
    active: typing.Any
    slope: typing.Any
    grad_head: typing.Any
    hot_all: typing.Any
    hot_ri: typing.Any
    hot_ir: typing.Any
    prob: typing.Any
    weight_hi: typing.Any
    value_two: typing.Any
    touch: typing.Any
    table: typing.Any
    norms: typing.Any
    proj_t: typing.Any
    extras: typing.Any
    moved: typing.Any


AT = Saved(*range(len(Saved._fields)))
SAVED = Saved(
    stream=((HERE, D), F32),
    branch=((HERE, D), BF16),
    unit_1=((HERE, D), F32),
    unit_2=((HERE, D), F32),
    rstd_1=((HERE, 128), F32),
    rstd_2=((HERE, 128), F32),
    row_mixed_t=((D, HERE), BF16),
    col_normed_t=((D, HERE), BF16),
    col_mixed_t=((D, HERE), BF16),
    feed_normed_t=((D, HERE), BF16),
    col_proj=((HERE, 3 * D), BF16),
    col_prob=((4 * PAIRS, 256, 128), F32),
    active=((HERE, FF), BF16),
    slope=((HERE, FF), BF16),
    grad_head=((VP, D), F32),
    hot_all=((ROWS * VP, COLS), BF16),
    hot_ri=((VP, HERE), BF16),
    hot_ir=((VP, HERE), BF16),
    prob=((HEADS * WIDE, COLS), F32),
    weight_hi=((HERE, D), BF16),
    value_two=((PAIRS, 128, 128), BF16),
    touch=((WIDE, COLS), F32),
    table=((VP, D), F32),
    norms=((8, D), F32),
    proj_t=((VP, 3 * D), BF16),
    extras=((8, 128), F32),
    moved=((8, D), F32),
)


class Forward(typing.NamedTuple):
    ids: typing.Any
    targets: typing.Any
    slots: typing.Any
    normed: typing.Any
    mixed: typing.Any
    normed_2: typing.Any
    mixed_2: typing.Any
    second_hot: typing.Any
    weight_lo: typing.Any
    left_hi: typing.Any
    left_lo: typing.Any
    lookup: typing.Any
    prob_low: typing.Any
    unit: typing.Any
    rstd: typing.Any


FORWARD = Forward(
    ids=((ROWS, COLS), jnp.int32),
    targets=((ROWS, 128), jnp.int32),
    slots=((8, SLOTS), jnp.int32),
    normed=((HERE, D), BF16),
    mixed=((HERE, D), BF16),
    normed_2=((HERE, D), BF16),
    mixed_2=((HERE, D), BF16),
    second_hot=((COLS, SLOTS), BF16),
    weight_lo=((HERE, D), BF16),
    left_hi=((HEADS * WIDE, ROWS * VP), BF16),
    left_lo=((HEADS * WIDE, ROWS * VP), BF16),
    lookup=((HERE, D), F32),
    prob_low=((HEADS * WIDE, COLS), BF16),
    unit=((HERE, D), F32),
    rstd=((HERE, 128), F32),
)


def position():
    z, y, k, c = place()
    me = (z * 4 + y * 2 + k) * 2 + c
    return z // 2, lax.rem(me, 16)


def read_tokens(small, f):
    alignment, block = position()
    side, part = block // 8, lax.rem(block // 4, 2)
    for r in range(ROWS):
        for cc in range(2):
            for q in range(2):
                lanes = slice(cc * 256 + q * 128, cc * 256 + q * 128 + 128)
                f.ids[r : r + 1, lanes] = small[r * 2 + cc, pl.ds(2 * alignment + q, 1), :]
        f.targets[r : r + 1, :] = small[r * 2 + side, pl.ds(4 + 2 * alignment + part, 1), :]
    lane = iota((1, 128), 1)
    for number in range(SLOTS // 128):
        for which in range(3):
            row = pl.ds(8 + 3 * alignment + which, 1)
            first = small[number * 4 + side, row, :]
            second = pltpu.roll(small[number * 4 + 2 + side, row, :], 64, 1)
            f.slots[which : which + 1, number * 128 : number * 128 + 128] = jnp.where(
                lane < 64, first, second
            )


def local_hot(values, shift):
    values = pltpu.roll(values, shift, 1)
    turned = [values] + [pltpu.roll(values, 32 * n, 1) for n in (1, 2, 3)]
    lane = iota((1, 128), 1)
    tiles = []
    for tile in range(4):
        row = turned[3][4 * tile + 3 : 4 * tile + 4]
        for n in (2, 1, 0):
            row = jnp.where(lane < 32 * n + 32, turned[n][4 * tile + n : 4 * tile + n + 1], row)
        tiles.append(row)
    row = jnp.concatenate(tiles, 1)
    return one_zero(row == iota((VP, HERE), 0)).astype(BF16)


def contact_part(contact_head, f, s, pair_count):
    _, block = position()
    base = block * WIDE
    head_sum = jnp.zeros((WIDE, COLS), F32)
    for h in range(HEADS):
        head_sum = head_sum + contact_head[h] * f.prob_low[h * 32 : h * 32 + 32, :].astype(F32)
    top, rest = split_two(head_sum)
    last = (head_sum - top.astype(F32) - rest.astype(F32)).astype(BF16)
    parts = jnp.concatenate([top, rest, last], 0)
    touch = jnp.zeros((WIDE, COLS), F32)
    bce = jnp.zeros((1, 1), F32)
    coef_sum = jnp.zeros((1, 1), F32)
    for number in range(SLOTS // 512):
        lanes = slice(number * 512, number * 512 + 512)
        first, label = (f.slots[n : n + 1, lanes] for n in (0, 2))
        second_hot = f.second_hot[:, lanes]
        picked = nn(parts, second_hot)
        picked = picked[:32] + picked[32:64] + picked[64:]
        first_hot = one_zero((first - base) == iota((WIDE, 512), 0))
        logit = jnp.sum(picked * first_hot, 0, keepdims=True) * COLS + contact_head[HEADS]
        owned = jnp.sum(first_hot, 0, keepdims=True) > 0.5
        valid = (label >= 0) & owned
        positive = one_zero(label == 1)
        small = jnp.exp(-jnp.abs(logit))
        soft = jnp.maximum(logit, 0.0) + jnp.log(1.0 + small)
        bce = bce + total_of(jnp.where(valid, soft - positive * logit, 0.0))
        sigmoid = jnp.where(logit >= 0.0, 1.0, small) / (1.0 + small)
        coef = jnp.where(valid, sigmoid - positive, 0.0) / pair_count
        coef_sum = coef_sum + total_of(coef)
        coef_top, coef_rest = split_two(first_hot * coef)
        touch = touch + nt(coef_top, second_hot) + nt(coef_rest, second_hot)
    s.touch[...] = touch
    column = iota((1, 128), 1)
    row = jnp.where(column == HEADS, coef_sum, 0.0)
    for h in range(HEADS):
        part = total_of(touch * f.prob_low[h * 32 : h * 32 + 32, :].astype(F32)) * COLS
        row = row + jnp.where(column == h, part, 0.0)
    return row, bce


def feature_order():
    shape = (384, 384)
    spot = iota(shape, 0)
    block = (spot * 2731) >> 16
    swapped = (block & 28) | ((block & 1) << 1) | ((block >> 1) & 1)
    return one_zero(spot + (swapped - block) * 24 == iota(shape, 1)).astype(BF16)


def forward_body(small, contact_head, weights, s, f, cells, projected, hook, emit):
    out_row, in_col, out_col = weights[:3]
    up_parts, down_parts = weights[3:5], weights[5:7]
    hook()
    features = cells()
    ahead = (
        ((iota((HERE, HERE), 0) >> 4) == (iota((HERE, HERE), 1) & 31))
        & ((iota((HERE, HERE), 0) & 15) == (iota((HERE, HERE), 1) >> 5))
    )
    ahead = one_zero(ahead).astype(BF16)
    read_tokens(small, f)
    _, block = position()
    shift = lax.rem(128 - lax.rem(block, 4) * 32, 128)
    window = pl.ds(pl.multiple_of((block // 4) * 128, 128), 128)
    hot_ri = local_hot(f.ids[:, window], shift)
    goal_ri = local_hot(f.targets[...], shift)
    s.hot_ri[...] = hot_ri
    for number in range(SLOTS // 512):
        lanes = slice(number * 512, number * 512 + 512)
        f.second_hot[:, lanes] = one_zero(f.slots[1:2, lanes] == iota((COLS, 512), 0)).astype(BF16)
    for r in range(ROWS):
        row = f.ids[r : r + 1, :]
        s.hot_all[r * VP : r * VP + VP, :] = one_zero(row == iota((VP, COLS), 0)).astype(BF16)
    shape = (HERE, HERE)
    back = (
        ((iota(shape, 1) >> 4) == (iota(shape, 0) & 31))
        & ((iota(shape, 1) & 15) == (iota(shape, 0) >> 5))
    )
    back = one_zero(back).astype(BF16)
    hot_ir = nn(hot_ri, back).astype(BF16)
    s.hot_ir[...] = hot_ir
    goal = nn(goal_ri, back)
    entries = jnp.zeros((4, 128), F32)
    labelled = jnp.zeros((1, 128), F32)
    for d in range(32):
        entries = entries + one_zero(small[d, 0:4, :] == MASK_ID)
        labelled = labelled + one_zero(small[d, 10:11, :] >= 0) + one_zero(small[d, 13:14, :] >= 0)
    entries, labelled = total_of(entries), total_of(labelled)

    hook()
    features = features[...].T
    table = features[:VP]
    norms = features[VP : VP + 8]
    s.table[...] = table
    s.norms[...] = norms
    table_low = table.astype(BF16)

    def vector(number):
        return norms[number : number + 1, :]

    hook()
    projected(s.proj_t)
    pair_parts = []
    for hp in range(PAIRS):
        lanes = slice(hp * 128, hp * 128 + 128)
        key = s.proj_t[:, D + hp * 128 : D + hp * 128 + 128]
        value = s.proj_t[:, 2 * D + hp * 128 : 2 * D + hp * 128 + 128]
        s.value_two[hp] = stacked(value)
        pair_parts.append(nt(s.proj_t[:, lanes], stacked(key)))
    pair_hi, pair_lo = split_two(jnp.concatenate(pair_parts, 1))
    hook()
    f.lookup[...] = tn(hot_ri, pair_hi) + tn(hot_ri, pair_lo)
    split_heads_to(f.lookup, f.left_hi, f.left_lo)
    hook()
    hot_all = s.hot_all[...]
    score = (nn(f.left_hi[...], hot_all) + nn(f.left_lo[...], hot_all)) * (HD * ROWS) ** (-0.5)
    score = jnp.exp(score - jnp.max(score, -1, keepdims=True))
    prob = score / jnp.sum(score, -1, keepdims=True)
    s.prob[...] = prob
    f.prob_low[...] = prob.astype(BF16)
    hook()
    merge_heads(f.prob_low[...], s.hot_all, s.weight_hi, f.weight_lo)
    hook()
    for hp in range(PAIRS):
        lanes = slice(hp * 128, hp * 128 + 128)
        value = s.value_two[hp]
        both = jnp.concatenate([s.weight_hi[:, lanes], f.weight_lo[:, lanes]], 1)
        f.mixed[:, lanes] = nn(both, jnp.concatenate([value, value], 0)).astype(BF16)
    f.mixed[...] = nn(ahead, f.mixed[...]).astype(BF16)
    s.stream[...] = tn(hot_ir, table_low)
    emit(AT.hot_all, AT.hot_ri, AT.hot_ir, AT.table, AT.norms, AT.proj_t, AT.value_two, AT.prob, AT.weight_hi)
    hook()
    for half in range(2):
        lanes = slice(half * 384, half * 384 + 384)
        s.stream[:, lanes] += nn(f.mixed[...], out_row[half])
    norm_rows(s.stream, vector(1), vector(5), s.unit_1, s.rstd_1, f.normed)
    emit(AT.unit_1, AT.rstd_1)

    def project(half, at):
        s.col_proj[:, half * 1152 + at : half * 1152 + at + 384] = nn(
            f.normed[...], in_col[half, :, at : at + 384]
        ).astype(BF16)

    for third in range(3):
        hook()
        for half in range(2):
            project(half, third * 384)
    emit(AT.col_proj)

    def attend(at, carry):
        rows = pl.ds(pl.multiple_of((at // PAIRS) * 128, 128), 128)
        lane = lax.rem(at, PAIRS) * 128

        def lanes(part):
            return pl.ds(pl.multiple_of(part * D + lane, 128), 128)

        query = stacked(s.col_proj[rows, lanes(0)])
        score = nt(query, s.col_proj[rows, lanes(1)]) * HD ** (-0.5)
        score = jnp.where(column_mask(), score, -1e30)
        score = jnp.exp(score - jnp.max(score, -1, keepdims=True))
        prob = score / jnp.sum(score, -1, keepdims=True)
        s.col_prob[at] = prob
        mixed = nn(prob.astype(BF16), s.col_proj[rows, lanes(2)])
        f.mixed_2[rows, lanes(0)] = unstacked(mixed, 128).astype(BF16)
        return carry

    for part in range(4):
        hook()
        lax.fori_loop(part * PAIRS, part * PAIRS + PAIRS, attend, 0, unroll=3)
    hook()
    emit(AT.col_prob)
    for half in range(2):
        lanes = slice(half * 384, half * 384 + 384)
        s.stream[:, lanes] += nn(f.mixed_2[...], out_col[half])
    norm_rows(s.stream, vector(2), vector(6), s.unit_2, s.rstd_2, f.normed_2)
    emit(AT.unit_2, AT.rstd_2)
    hook()
    contact_row, bce = contact_part(contact_head, f, s, labelled)
    emit(AT.touch)
    for part in range(2):

        def widen(half, at, part=part):
            lanes = slice(part * 1536 + half * 768 + at, part * 1536 + half * 768 + at + UP_TILE)
            up = nn(f.normed_2[...], up_parts[part][half, :, at : at + UP_TILE])
            active, slope = gelu_parts(up)
            s.active[:, lanes] = active.astype(BF16)
            s.slope[:, lanes] = slope.astype(BF16)

        for half in range(2):
            hook()
            for at in range(0, 768, UP_TILE):
                widen(half, at)
        hook()
        if part == 0:
            transpose_into(f.mixed, s.row_mixed_t)
            transpose_into(f.normed, s.col_normed_t)
            emit(AT.row_mixed_t, AT.col_normed_t)
        else:
            transpose_into(f.mixed_2, s.col_mixed_t)
            emit(AT.col_mixed_t)

    emit(AT.active, AT.slope)
    for part, at, size in ((0, 0, 768), (1, 0, 384), (1, 384, 384)):
        hook()
        added = []
        for half in range(2):
            start = part * 1536 + half * 768 + at
            matrix = down_parts[part][half, :, at : at + size]
            added.append(nt(s.active[:, start : start + size], matrix))
        s.stream[...] += added[0] + added[1]
        if part == 0:
            hook()
            transpose_into(f.normed_2, s.feed_normed_t)
            emit(AT.feed_normed_t)
    hook()
    norm_rows(s.stream, vector(3), vector(7), f.unit, f.rstd, f.normed)
    logits = nt(table_low, f.normed[...]) * D ** (-0.5)
    vocab = iota((VP, HERE), 0)
    logits = jnp.where(vocab < VOCAB, logits, -1e30)
    shifted = logits - jnp.max(logits, 0, keepdims=True)
    log_probs = shifted - jnp.log(jnp.sum(jnp.exp(shifted), 0, keepdims=True))
    keep = hot_ir[MASK_ID : MASK_ID + 1].astype(F32) > 0.5
    mlm = -total_of(jnp.where(keep & (goal > 0.5), log_probs, 0.0))
    logit_grad = jnp.where(keep, jnp.exp(log_probs) - goal, 0.0) / entries
    logit_low = (logit_grad * D ** (-0.5)).astype(BF16)
    s.grad_head[...] = nn(logit_low, f.normed[...])
    hook()
    f.lookup[...] = tn(logit_low, table_low)
    scale_3, shift_3 = back_rows(f.unit, f.rstd, vector(3), f.lookup, s.stream, s.branch, True)
    emit(AT.stream, AT.branch)
    line = iota((8, D), 0)
    s.moved[...] = jnp.where(line == 0, scale_3, jnp.where(line == 1, shift_3, 0.0))
    column = iota((1, 128), 1)
    row = contact_row + jnp.where(column == HEADS + 1, mlm, 0.0) + jnp.where(column == HEADS + 2, bce, 0.0)
    counted = jnp.where(column == 0, entries, 0.0) + jnp.where(column == 1, labelled, 0.0)
    line = iota((8, 128), 0)
    s.extras[...] = jnp.where(line == 0, row, jnp.where(line == 1, counted, 0.0))
    emit(AT.grad_head, AT.extras, AT.moved)
    hook()


def back_rows(unit_ref, rstd_ref, gain, upstream_ref, stream_ref, low_ref, first):
    def body(at, carry):
        scale, move = carry
        rows = pl.ds(pl.multiple_of(at * 64, 64), 64)
        upstream = upstream_ref[rows, :]
        unit = unit_ref[rows, :]
        inner = upstream * gain
        mean = jnp.sum(inner, -1, keepdims=True) * (1.0 / D)
        along = jnp.sum(inner * unit, -1, keepdims=True) * (1.0 / D)
        grad = rstd_ref[rows, 0:1] * (inner - mean - unit * along)
        if not first:
            grad = grad + stream_ref[rows, :]
        stream_ref[rows, :] = grad
        low_ref[rows, :] = grad.astype(BF16)
        touched = upstream * unit
        for n in range(8):
            scale = scale + touched[n * 8 : n * 8 + 8]
            move = move + upstream[n * 8 : n * 8 + 8]
        return scale, move

    zero = jnp.zeros((8, D), F32)
    scale, move = lax.fori_loop(0, HERE // 64, body, (zero, zero))
    return jnp.sum(scale, 0, keepdims=True), jnp.sum(move, 0, keepdims=True)


MATRICES = (128, 384, 1152, 384, 768, 768, 768, 768)
UNITS = (
    (0, 0, 128, True),
    (1, 0, 384, False),
    (2, 0, 384, True),
    (2, 384, 384, True),
    (2, 768, 384, True),
    (3, 0, 384, False),
    (4, 0, 768, True),
    (5, 0, 768, True),
    (6, 0, 768, True),
    (7, 0, 384, True),
    (7, 384, 384, True),
)
Z_LAST = {9: 2}
FORWARD_ORDER = (
    ((0, 0), (0, 2), (0, 11), (1, 0), (0, 1), (0, 9), (1, 2), (1, 11), (2, 0), (0, 3), (1, 9), (0, 4), (1, 1), (2, 11), (3, 0), (0, 5), (2, 1), (4, 0),),
    ((3, 11), (2, 2), (3, 1), (0, 6), (1, 3),),
    ((4, 11), (1, 4), (1, 5), (3, 2), (0, 7),),
    ((4, 1), (2, 3), (0, 8),),
    ((4, 2), (2, 4), (1, 6),),
    (),
    ((2, 5), (2, 9), (3, 3),),
    ((1, 7),),
    ((3, 4), (4, 3), (2, 6), (4, 4),),
    (),
    ((3, 5), (1, 8),),
    ((0, 10),),
    ((4, 5),),
    ((2, 7),),
    (),
    ((3, 6), (3, 9),),
    ((2, 8), (1, 10),),
    ((4, 6),),
    (),
    ((4, 9),),
    ((3, 7), (3, 8), (2, 10), (4, 7),),
    (),
    (),
    ((4, 8), (3, 10),),
    (),
    (),
    ((4, 10),),
    (),
    (),
    (),
)


def spot(paired, cc, zz, yy, k):
    return (k, zz, yy, cc) if paired else (cc, zz, yy, k)


def forward_kernel(*refs):
    count, parts = len(UNITS), len(MATRICES)
    raw = refs[:11]
    contact_head = refs[11]
    at = 12
    far = (None, *refs[at : at + parts - 1])
    saved_far = refs[at + parts - 1 : at + parts - 1 + len(SAVED)]
    at += parts - 1 + len(SAVED)
    outs = refs[at : at + parts]
    at += parts
    outgoing = refs[at : at + count]
    incoming = refs[at + count : at + 2 * count]
    piece = refs[at + 2 * count : at + 3 * count]
    at += 3 * count
    saved = Saved(*refs[at : at + len(SAVED)])
    at += len(SAVED)
    scratch = Forward(*refs[at : at + len(FORWARD)])
    at += len(FORWARD)
    near = refs[at : at + 11]
    at += 11
    small, small_out, corner, features, stat, stat_got, part, part_got, part_line, proj, room = refs[at : at + 11]
    small_send, small_recv, send, recv, local, out_sem, raw_sem, twin_send, twin_recv = refs[at + 11 :]
    tokens, targets, masked, pairs, labels, table, norms, in_w, out_w, up_w, down_w = near
    z, y, k, c = place()
    me = (z * 4 + y * 2 + k) * 2 + c
    barrier = greet_all()
    raw_copies = [pltpu.make_async_copy(a, b, raw_sem.at[n]) for n, (a, b) in enumerate(zip(raw, near))]
    for item in raw_copies:
        item.start()
    for item in raw_copies[:7]:
        item.wait()
    small[...] = jnp.full(small.shape, -1, jnp.int32)
    for micro in range(2):
        for half in range(2):
            lanes = slice(half * 128, half * 128 + 128)
            row = 2 * micro + half
            small[row : row + 1, :] = jnp.where(
                masked[micro, :, lanes] > 0, MASK_ID, tokens[micro, :, lanes]
            )
            small[4 + row : 5 + row, :] = targets[micro, :, lanes]
        row = 8 + 3 * micro
        for which in range(2):
            small[row + which : row + which + 1, 0:64] = pairs[micro, which : which + 1, :]
        small[row + 2 : row + 3, 0:64] = labels[micro : micro + 1, :]
    corner[...] = jnp.zeros(corner.shape, F32)
    corner[0:8, 0:24] = norms[...]
    vectors = pltpu.roll(corner[...].T[:24], 64, 1)
    corner[0:8, 0:24] = jnp.zeros((8, 24), F32)
    corner[0:24, 0:VOCAB] = table[...]
    mine_rows = (corner[0:24, :] + vectors).astype(BF16).astype(F32)
    table_rows = jnp.where(iota((24, 128), 1) < VP, mine_rows, 0.0)
    gain, bias = mine_rows[:, 64:65], mine_rows[:, 68:69]
    piece[0][0:16, :] = small[...].astype(F32)
    piece[0][16:40, :] = mine_rows
    mean = jnp.sum(table_rows, 0, keepdims=True) * (1.0 / 24)
    centre = table_rows - mean
    spread = jnp.sum(centre * centre, 0, keepdims=True)
    line = iota((8, 128), 0)
    stat[...] = jnp.where(line == 0, mean, jnp.where(line == 1, spread, 0.0))
    def master(u, side):
        matrix, start, n, _ = UNITS[u]
        width = MATRICES[matrix]
        if matrix == 2:
            return in_w[1, :, side * 1152 + start : side * 1152 + start + n]
        if matrix in (1, 3):
            rows = out_w[matrix // 2, :, side * 384 : side * 384 + 384].astype(BF16)
            return nn(rows, order)
        begin = (matrix % 2) * 1536 + side * width + start
        return (up_w if matrix < 6 else down_w)[:, begin : begin + n]

    def mine(u):
        return k if UNITS[u][3] else c

    def set_out(u):
        other = jnp.where(mine(u) == 0, master(u, 1), master(u, 0))
        other = jnp.concatenate([other, jnp.zeros((8, UNITS[u][2]), F32)], 0)
        outgoing[u][...] = other.astype(BF16)

    pl.semaphore_wait(barrier, 31)

    def stat_copy(step):
        other = lax.rem(me + step, 32)
        return remote(
            stat, stat_got.at[me], small_send.at[0, step], small_recv.at[0, step], (other // 2, lax.rem(other, 2))
        )

    chip = (z * 2 + y) * 2 + c

    def chip_copy(phase, step):
        other = lax.rem(chip + step, 16)
        target = device(other // 4, lax.rem(other // 2, 2), k, lax.rem(other, 2))
        if phase == 1:
            src, dst = part.at[k, other], part_line.at[chip]
        else:
            src, dst = proj.at[k, chip], proj.at[k, chip]
        return remote(src, dst, small_send.at[phase, step], small_recv.at[phase, step], target)

    def each(last, action):
        def body(step, carry):
            action(step)
            return carry

        lax.fori_loop(1, last, body, 0)

    each(32, lambda step: stat_copy(step).start())

    across, beside, twin = device(z, y, k, 1 - c), device(z, 1 - y, k, c), device(z, y, 1 - k, c)

    def block(u, cc, zz, yy):
        matrix, start, n, paired = UNITS[u]
        where = spot(paired, cc, zz, yy, k)
        if n == MATRICES[matrix]:
            return outs[matrix].at[where]
        return outs[matrix].at[(*where, slice(None), pl.ds(start, n))]

    def copy(u, at, src, dst, target):
        return remote(src, dst, send.at[u, at], recv.at[u, at], target)

    def pair_copy(u):
        return copy(u, 0, outgoing[u], incoming[u], twin if UNITS[u][3] else across)

    def own_copy(u):
        return pltpu.make_async_copy(piece[u], block(u, c, z, y), local.at[u])

    def line_copy(u, step):
        return copy(u, step, piece[u], block(u, c, z, y), device(lax.rem(z + step, 4), y, k, c))

    def same(u, at, cc, zz, yy, target):
        view = block(u, cc, zz, yy)
        return copy(u, at, view, view, target)

    low, high, every = pl.ds(0, 2), pl.ds(2, 2), slice(None)

    def second(u):
        return [same(u, 4, c, low, y, across), same(u, 5, c, high, y, beside)]

    def third_own(u):
        return [same(u, 6, c, low, y, beside), same(u, 7, c, high, y, across)]

    def third_far(u):
        return [same(u, 8, 1 - c, low, y, beside), same(u, 9, c, high, 1 - y, across)]

    def twin_own(u):
        return [same(u, 10, c, every, y, twin)]

    def twin_second(u):
        return [same(u, 11, 1 - c, low, y, twin), same(u, 12, c, high, 1 - y, twin)]

    def twin_third(u):
        return [
            same(u, 13, c, low, 1 - y, twin),
            same(u, 14, 1 - c, high, y, twin),
            same(u, 15, 1 - c, low, 1 - y, twin),
            same(u, 16, 1 - c, high, 1 - y, twin),
        ]

    own_copy(0).start()
    for item in raw_copies[7:]:
        item.wait()
    order = feature_order()
    for u in range(1, count):
        set_out(u)
        pair_copy(u).start()

    def part_twin():
        return remote(part.at[1 - k], part_got, twin_send.at[0], twin_recv.at[0], twin)

    def proj_twin():
        return remote(proj.at[k], proj.at[k], twin_send.at[1], twin_recv.at[1], twin)

    def project_part():
        stat_got[me] = stat[...]
        each(32, lambda step: stat_copy(step).wait())
        means = jnp.zeros((1, 128), F32)
        spreads = jnp.zeros((1, 128), F32)
        for d in range(32):
            means = means + stat_got[d, 0:1, :]
            spreads = spreads + stat_got[d, 1:2, :]
        means = means * (1.0 / 32)
        for d in range(32):
            away = stat_got[d, 0:1, :] - means
            spreads = spreads + 24.0 * away * away
        rstd = lax.rsqrt(spreads * (1.0 / D) + NORM_EPS)
        normed = (table_rows - means) * rstd * gain + bias
        normed = jnp.concatenate([normed, jnp.zeros((8, 128), F32)], 0).astype(BF16)
        for block_at in range(6):
            lanes = slice(block_at * 384, block_at * 384 + 384)
            rows = jnp.concatenate([in_w[0, :, lanes], jnp.zeros((8, 384), F32)], 0).astype(BF16)
            product = tn(normed, rows)
            for group in range(5):
                number = group * 6 + block_at
                part[number // 16, number % 16] = product[group * 8 : group * 8 + 8]
        for number in (30, 31):
            part[number // 16, number % 16] = jnp.zeros((8, 384), F32)
        part_twin().start()

    def project_chip():
        part_twin().wait_recv()
        part[k] = part[k] + part_got[...]
        each(16, lambda step: chip_copy(1, step).start())

    def project_line():
        part_line[chip] = part[k, chip]
        each(16, lambda step: chip_copy(1, step).wait_recv())
        proj[k, chip] = lax.fori_loop(1, 16, lambda at, held: held + part_line[at], part_line[0])
        each(16, lambda step: chip_copy(2, step).start())

    def project_twin():
        each(16, lambda step: chip_copy(2, step).wait_recv())
        proj_twin().start()

    def project_end():
        proj_twin().wait_recv()

    projecting = (project_part, project_chip, project_line, project_twin, project_end)

    def cells():
        for d in range(32):
            at = ((d // 2) % 2, d // 8, (d // 4) % 2, d % 2)
            small_out[d] = outs[0][(*at, slice(0, 16))].astype(jnp.int32)
            start = (((at[1] * 2 + at[2]) * 2 + at[3]) * 2 + at[0]) * 24
            features[start : start + 24, :] = outs[0][(*at, slice(16, 40))]
        return features

    def projected(target):
        room[40:64, :] = jnp.zeros((24, 3 * D), F32)
        for number in range(30):
            rows, lanes = (number // 6) * 8, (number % 6) * 384
            room[rows : rows + 8, lanes : lanes + 384] = proj[number // 16, number % 16]
        target[...] = room[...].astype(BF16)

    def to_across(u):
        return copy(u, 4, piece[u], block(u, c, z, y), across)

    def to_beside(u):
        return copy(u, 5, piece[u], block(u, c, z, y), beside)

    def to_corner(u):
        if Z_LAST[u] == 1:
            return same(u, 6, 1 - c, z, y, beside)
        return same(u, 6, c, z, 1 - y, across)

    def to_line(u):
        return [
            same(u, step, every, z, every, device(lax.rem(z + step, 4), y, k, c)) for step in (1, 3, 2)
        ]

    def to_twin(u):
        return [same(u, 7, every, z, every, twin)]

    def rest_to_twin(u):
        return [same(u, 7 + step, every, lax.rem(z + 4 - step, 4), every, twin) for step in (1, 3, 2)]

    def stage_line(u):
        if u == 0:
            for step in (1, 3, 2):
                line_copy(u, step).start()
            return
        pair_copy(u).wait_recv()
        side = mine(u)
        own = jnp.where(side == 0, master(u, 0), master(u, 1))
        theirs = incoming[u][...].astype(F32)[:24]
        top = jnp.where(side == 0, own, theirs)
        bottom = jnp.where(side == 0, theirs, own)
        piece[u][...] = jnp.concatenate([top, bottom], 0).astype(BF16)
        own_copy(u).start()
        if u in Z_LAST:
            to_across(u).start()
            to_beside(u).start()
            return
        for step in (1, 3, 2):
            line_copy(u, step).start()

    def stage_second(u):
        own_copy(u).wait()
        if u in Z_LAST:
            to_across(u).wait_recv()
            to_beside(u).wait_recv()
            to_corner(u).start()
            return
        for step in (1, 3, 2):
            line_copy(u, step).wait_recv()
        for item in second(u) + third_own(u) + twin_own(u):
            item.start()

    def stage_third(u):
        if u in Z_LAST:
            to_corner(u).wait_recv()
            for item in to_line(u) + to_twin(u):
                item.start()
            return
        for item in second(u):
            item.wait_recv()
        for item in third_far(u) + twin_second(u):
            item.start()

    def stage_twin(u):
        if u in Z_LAST:
            for item in to_line(u):
                item.wait_recv()
            for item in rest_to_twin(u):
                item.start()
            return
        for item in third_own(u) + third_far(u):
            item.wait_recv()
        for item in twin_third(u):
            item.start()

    def far_copy(matrix):
        return pltpu.make_async_copy(outs[matrix], far[matrix], local.at[count + matrix])

    def stage_end(u):
        if u in Z_LAST:
            for item in to_twin(u) + rest_to_twin(u):
                item.wait_recv()
            sent = [to_across(u), to_beside(u), to_corner(u)] + to_line(u) + to_twin(u)
        else:
            for item in twin_own(u) + twin_second(u) + twin_third(u):
                item.wait_recv()
            sent = [line_copy(u, step) for step in (1, 2, 3)]
            sent += second(u) + third_own(u) + third_far(u) + twin_own(u) + twin_second(u)
        for item in sent if u == 0 else [pair_copy(u)] + sent:
            item.wait_send()
        if u == 0:
            return
        if u + 1 == count or UNITS[u + 1][0] != UNITS[u][0]:
            far_copy(UNITS[u][0]).start()

    stages = (stage_line, stage_second, stage_third, stage_twin, stage_end)
    pending = list(FORWARD_ORDER)

    def hook():
        for stage, u in pending.pop(0):
            if u == count:
                projecting[stage]()
            else:
                stages[stage](u)

    def out_copy(at):
        return pltpu.make_async_copy(saved[at], saved_far[at], out_sem.at[at])

    def emit(*numbers):
        for number in numbers:
            out_copy(number).start()

    views = [w.reshape(2, D, n) for w, n in zip(outs[1:], MATRICES[1:])]
    forward_body(small_out, contact_head, views, saved, scratch, cells, projected, hook, emit)
    part_twin().wait_send()
    proj_twin().wait_send()
    for phase in (1, 2):
        each(16, lambda step, phase=phase: chip_copy(phase, step).wait_send())
    assert not pending
    for u in range(count):
        for item in rest_to_twin(u) if u in Z_LAST else twin_third(u):
            item.wait_send()
    for matrix in range(1, parts):
        far_copy(matrix).wait()
    for at in range(len(SAVED)):
        out_copy(at).wait()


def forward_call(raw, contact_head):
    count, parts = len(UNITS), len(MATRICES)
    anywhere = pl.BlockSpec(memory_space=pl.ANY)
    shapes = [(2, NZ, NY, 2, 48, n) for n in MATRICES[1:]]
    widths = [n for _, _, n, _ in UNITS]
    outs = pl.pallas_call(
        forward_kernel,
        out_shape=[jax.ShapeDtypeStruct(shape, BF16) for shape in shapes]
        + [jax.ShapeDtypeStruct(*item) for item in SAVED],
        in_specs=[anywhere] * 11 + [pl.BlockSpec(memory_space=pltpu.SMEM)],
        out_specs=[anywhere] * (parts - 1 + len(SAVED)),
        scratch_shapes=[pltpu.VMEM((2, NZ, NY, 2, 40, 128), F32)]
        + [pltpu.VMEM(shape, BF16) for shape in shapes]
        + [pltpu.VMEM((32, n), BF16) for n in widths] * 2
        + [pltpu.VMEM((40, 128), F32)]
        + [pltpu.VMEM((48, n), BF16) for n in widths[1:]]
        + [pltpu.VMEM(*item) for item in SAVED]
        + [pltpu.VMEM(*item) for item in FORWARD]
        + [pltpu.VMEM(item.shape, item.dtype) for item in raw]
        + [
            pltpu.VMEM((16, 128), jnp.int32),
            pltpu.VMEM((32, 16, 128), jnp.int32),
            pltpu.VMEM((128, 128), F32),
            pltpu.VMEM((D, 128), F32),
            pltpu.VMEM((8, 128), F32),
            pltpu.VMEM((32, 8, 128), F32),
            pltpu.VMEM((2, 16, 8, 384), F32),
            pltpu.VMEM((16, 8, 384), F32),
            pltpu.VMEM((16, 8, 384), F32),
            pltpu.VMEM((2, 16, 8, 384), F32),
            pltpu.VMEM((VP, 3 * D), F32),
            pltpu.SemaphoreType.DMA((3, 32)),
            pltpu.SemaphoreType.DMA((3, 32)),
            pltpu.SemaphoreType.DMA((count, 17)),
            pltpu.SemaphoreType.DMA((count, 17)),
            pltpu.SemaphoreType.DMA((count + parts,)),
            pltpu.SemaphoreType.DMA((len(SAVED),)),
            pltpu.SemaphoreType.DMA((len(raw),)),
            pltpu.SemaphoreType.DMA((2,)),
            pltpu.SemaphoreType.DMA((2,)),
        ],
        compiler_params=pltpu.CompilerParams(
            collective_id=0, has_side_effects=True, vmem_limit_bytes=62 * 2**20
        ),
    )(*raw, contact_head)
    return outs[: parts - 1], Saved(*outs[parts - 1 :])


def summed_rows(sums, group):
    return jnp.concatenate([sums[3 * group + third] for third in range(3)], 1).astype(F32)


def table_finish(sums, room, table_ref, norms_ref, proj_t, in_row, g_in, g_norm, send_stat):
    z, y, k, c = place()
    me = ((z * 2 + y) * 2 + c) * 2 + k
    room[0:128, :] = jnp.zeros((128, D), F32)
    for number in range(2):
        room[4 + 16 * number : 20 + 16 * number, :] = summed_rows(sums, number)
        room[68 + 16 * number : 84 + 16 * number, :] = summed_rows(sums, 2 + number)
    pair = room[0:64, :]
    value_grad = room[64:128, :]
    vectors = summed_rows(sums, 6)
    vectors = vectors[:8] + vectors[8:]
    line = iota((8, D), 0)
    table_grad = jnp.concatenate(
        [
            summed_rows(sums, 4),
            summed_rows(sums, 5),
            jnp.where(line == 0, vectors[7:8], 0.0),
            jnp.zeros((24, D), F32),
        ],
        0,
    )
    pair_hi, pair_lo = split_two(pair)
    scale = (HD * ROWS) ** (-0.5)
    query_grad, key_grad = [], []
    for hp in range(PAIRS):
        lanes = slice(hp * 128, hp * 128 + 128)
        query = proj_t[:, lanes]
        key = stacked(proj_t[:, D + hp * 128 : D + hp * 128 + 128])
        high, low = pair_hi[:, lanes], pair_lo[:, lanes]
        query_grad.append((nn(high, key) + nn(low, key)) * scale)
        key_grad.append(unstacked(tn(high, query) + tn(low, query), VP) * scale)
    proj_hi, proj_lo = split_two(jnp.concatenate(query_grad + key_grad + [value_grad], 1))
    shard = D // 32
    pick = one_zero(iota((shard, D), 1) == iota((shard, D), 0) + me * shard).astype(BF16)
    weight = in_row[...].astype(BF16)
    back_t = nt(weight, proj_hi) + nt(weight, proj_lo)
    back = nt(proj_hi, weight) + nt(proj_lo, weight)
    table = table_ref[...]
    table_low = table.astype(BF16)
    unit, rstd = norm_stats(table)
    mean = jnp.sum(table, -1, keepdims=True) * (1.0 / D)
    same = iota((VP, VP), 0) == iota((VP, VP), 1)

    def as_row(column):
        return jnp.sum(jnp.where(same, column, 0.0), 0, keepdims=True)

    rstd_row = as_row(rstd)
    unit_t = (nt(pick, table_low) - as_row(mean)) * rstd_row
    unit_mine = (nt(table_low, pick) - mean) * rstd
    norms = jnp.concatenate([norms_ref[...], jnp.zeros((8, D), F32)], 0).astype(BF16)
    inner = back_t * nt(pick, norms)[:, 0:1]

    def three(values):
        top, rest = split_two(values)
        return top, rest, (values - top.astype(F32) - rest.astype(F32)).astype(BF16)

    emb_grad = sum(nt(pick, part) for part in three(table_grad))
    before = emb_grad + rstd_row * inner
    parts = (inner, inner * unit_t, before, before * unit_t, unit_t, unit_t * unit_t, before * before)
    send_stat([jnp.sum(part, 0, keepdims=True) for part in parts])
    scale_0 = jnp.sum(back * unit_mine, 0, keepdims=True)
    shift_0 = jnp.sum(back, 0, keepdims=True)
    line = iota((16, D), 0)
    norm_grad = jnp.zeros((16, D), F32)
    for number, source in ((1, 0), (2, 1), (3, 2), (5, 3), (6, 4), (7, 5)):
        norm_grad = jnp.where(line == number, vectors[source : source + 1], norm_grad)
    normed = (unit * norms_ref[0:1, :] + norms_ref[4:5, :]).astype(BF16)
    mine = nt(pick, normed).astype(BF16)
    in_grad = nn(mine, proj_hi) + nn(mine, proj_lo)
    g_in[...] = in_grad
    own_norm = sum(nt(part, pick) for part in three(norm_grad))[:8]
    line = iota((8, shard), 0)
    own_norm = jnp.where(line == 0, scale_0, jnp.where(line == 4, shift_0, own_norm))
    g_norm[...] = own_norm
    found = total_of(in_grad * in_grad) + total_of(own_norm * own_norm)
    return inner, unit_t, rstd_row, emb_grad, found


PIECES = 21
GRAD_WIDTHS = (768, 768, 768, 768, 384, 1152, 384)
GRAD_UNITS = (
    (0, 0, 384, True),
    (0, 384, 384, True),
    (1, 0, 768, True),
    (2, 0, 768, True),
    (3, 0, 768, True),
    (4, 0, 384, False),
    (5, 0, 384, True),
    (5, 384, 384, True),
    (5, 768, 384, True),
    (6, 0, 384, False),
)
Z_FIRST = {1: 1, 5: 2}
BACKWARD_ORDER = (
    (),
    (),
    (),
    (),
    (),
    (),
    ((0, 0),),
    (),
    ((0, 1),),
    (),
    (),
    ((1, 0),),
    (),
    ((0, 2),),
    ((2, 0),),
    (),
    (),
    ((0, 3),),
    (),
    (),
    ((1, 1), (1, 2), (0, 4),),
    ((3, 0), (0, 5),),
    ((4, 0), (1, 3),),
    ((2, 1),),
    (),
    ((2, 2),),
    (),
    (),
    (),
    (),
    ((1, 4),),
    ((3, 1), (1, 5), (2, 3), (0, 6), (0, 7),),
    (),
    ((4, 1), (2, 4), (2, 5), (0, 8),),
    ((3, 2),),
    ((1, 6), (4, 2), (0, 9),),
    ((3, 5), (3, 3), (1, 7),),
    ((4, 3), (1, 8),),
    ((2, 6),),
    ((3, 4), (1, 9), (4, 5), (4, 4), (2, 7), (2, 8), (5, 0), (3, 6), (2, 9), (3, 7), (4, 6), (4, 7), (3, 8), (4, 8), (6, 0), (3, 9), (4, 9),),
)


class Kept(typing.NamedTuple):
    stream: typing.Any
    norms: typing.Any
    table: typing.Any
    proj_t: typing.Any
    extras: typing.Any
    moved: typing.Any
    grad_head: typing.Any
    touch: typing.Any
    value_two: typing.Any


class Early(typing.NamedTuple):
    slope: typing.Any
    active: typing.Any
    feed_normed_t: typing.Any
    unit_2: typing.Any
    rstd_2: typing.Any
    col_mixed_t: typing.Any
    col_proj: typing.Any
    col_prob: typing.Any
    col_normed_t: typing.Any
    unit_1: typing.Any
    rstd_1: typing.Any


class Late(typing.NamedTuple):
    row_mixed_t: typing.Any
    hot_all: typing.Any
    weight_hi: typing.Any
    prob: typing.Any
    hot_ri: typing.Any
    hot_ir: typing.Any


def pick_items(group, source):
    return [getattr(source, name) for name in group._fields]


def backward_kernel(*refs):
    widths = GRAD_WIDTHS
    count = len(widths)
    contact_head = refs[0]
    far = refs[1 : 1 + count]
    in_row_far = refs[1 + count]
    saved = Saved(*refs[2 + count : 2 + count + len(SAVED)])
    at = 2 + count + len(SAVED)
    outs = refs[at : at + count]
    g_in, g_emb, g_norm, stats = refs[at + count : at + count + 4]
    at += count + 4
    grads = refs[at : at + count]
    kept = Kept(*refs[at + count : at + count + len(Kept._fields)])
    at += count + len(Kept._fields)
    upstream, branch, branch_t, mixed = refs[at : at + 4]
    scratch = refs[at + 4 :]
    units = len(GRAD_UNITS)
    got_0, got_1a, got_1b, got_2a, got_2b, got_3, total, got_4 = (
        scratch[i * units : (i + 1) * units] for i in range(8)
    )
    table, table_out, table_got, square, square_got, stat, stat_got, late_rows = scratch[8 * units : 8 * units + 8]
    table_send, table_recv, send, recv, local = scratch[8 * units + 8 :]
    z, y, k, c = place()
    me = (z * 4 + y * 2 + k) * 2 + c
    across, beside, twin = device(z, y, k, 1 - c), device(z, 1 - y, k, c), device(z, y, 1 - k, c)
    barrier = greet_all()
    stream = kept.stream
    square[...] = jnp.zeros(square.shape, F32)

    copies = {}

    def load(number, source, target):
        copies[number] = pltpu.make_async_copy(source, target, local.at[number])
        copies[number].start()

    def need(*numbers):
        for number in numbers:
            copies[number].wait()

    def weight(m):
        return len(SAVED) + m

    def copy(m, at, src, dst, target):
        return remote(src, dst, send.at[m, at], recv.at[m, at], target)

    low, high = pl.ds(0, 2), pl.ds(2, 2)
    every = slice(None)

    def where(u, cc, zz, yy):
        matrix, start, n, paired = GRAD_UNITS[u]
        index = spot(paired, cc, zz, yy, k)
        return index if n == widths[matrix] else (*index, every, pl.ds(start, n))

    def block(u, cc, zz, yy):
        return grads[GRAD_UNITS[u][0]].at[where(u, cc, zz, yy)]

    def ordered(u, cc, rest):
        return (*rest, cc) if GRAD_UNITS[u][3] else (cc, *rest)

    def twin_copy(u):
        matrix, start, n, paired = GRAD_UNITS[u]
        index = (1 - k,) if paired else (every, every, every, 1 - k)
        if n != widths[matrix]:
            index = (*index, *(every,) * (5 - len(index)), pl.ds(start, n))
        return copy(u, 0, grads[matrix].at[index], got_0[u], twin)

    def first(u):
        return [
            copy(u, 1, block(u, every, low, 1 - y), got_1a[u], beside),
            copy(u, 2, block(u, 1 - c, high, every), got_1b[u], across),
        ]

    def second(u):
        return [
            copy(u, 3, block(u, 1 - c, low, y), got_2a[u], across),
            copy(u, 4, block(u, c, high, 1 - y), got_2b[u], beside),
        ]

    def along(u):
        return [
            copy(
                u,
                4 + step,
                block(u, c, lax.rem(z + step, 4), y),
                got_3[u].at[step - 1],
                device(lax.rem(z + step, 4), y, k, c),
            )
            for step in (1, 3, 2)
        ]

    def z_first(u):
        return [
            copy(
                u,
                step,
                block(u, every, lax.rem(z + step, 4), every),
                got_1a[u].at[step - 1],
                device(lax.rem(z + step, 4), y, k, c),
            )
            for step in (1, 3, 2)
        ]

    def plane_first(u):
        if Z_FIRST[u] == 1:
            return [copy(u, 4, block(u, every, z, 1 - y), got_2a[u], beside)]
        return [copy(u, 4, block(u, 1 - c, z, every), got_2a[u], across)]

    def plane_second(u):
        if Z_FIRST[u] == 1:
            return [copy(u, 5, block(u, 1 - c, z, y), got_2b[u], across)]
        return [copy(u, 5, block(u, c, z, 1 - y), got_2b[u], beside)]

    def mine(u):
        return k if GRAD_UNITS[u][3] else c

    def pair(u):
        return [copy(u, 8, total[u].at[1 - mine(u)], got_4[u], twin if GRAD_UNITS[u][3] else across)]

    def peer(step):
        return lax.rem(me + step, 32)

    def source(step):
        return lax.rem(me + 32 - step, 32)

    def table_copy(step, back, index):
        target = (peer(step) // 2, lax.rem(peer(step), 2))
        if back:
            return remote(
                table_out.at[index], table_out.at[index], table_send.at[1, step], table_recv.at[1, step], target
            )
        return remote(
            table.at[index], table_got.at[me], table_send.at[0, step], table_recv.at[0, step], target
        )

    def table_start(step):
        @pl.when(peer(step) < PIECES)
        def _():
            table_copy(step, False, peer(step)).start()

    def table_wait_send(step):
        @pl.when(peer(step) < PIECES)
        def _():
            table_copy(step, False, 0).wait_send()

        @pl.when(me < PIECES)
        def _():
            table_copy(step, True, 0).wait_send()

    def table_wait_back(step):
        @pl.when(source(step) < PIECES)
        def _():
            table_copy(step, True, 0).wait_recv()

    def each(action):
        def body(step, carry):
            action(step)
            return carry

        lax.fori_loop(1, 32, body, 0)

    def gather_into(u, cc, zz, yy, *others):
        matrix = GRAD_UNITS[u][0]
        index = where(u, cc, zz, yy)
        if not others:
            grads[matrix][index] = grads[matrix][index] + got_0[u][ordered(u, cc, (zz, yy))]
            return
        value = grads[matrix][index].astype(F32) + got_0[u][ordered(u, cc, (zz, yy))].astype(F32)
        for other in others:
            value = value + other.astype(F32)
        grads[matrix][index] = value.astype(BF16)

    def from_line(u, cc, yy):
        index = (yy, cc) if GRAD_UNITS[u][3] else (cc, yy)
        return [got_1a[u][(step, *index)] for step in range(3)]

    def stage_first(u):
        twin_copy(u).wait_recv()
        if u in Z_FIRST:
            for step in (1, 3, 2):
                for cc in range(2):
                    for yy in range(2):
                        gather_into(u, cc, lax.rem(z + step, 4), yy)
            for item in z_first(u):
                item.start()
            return
        for a in range(2):
            for b in range(2):
                gather_into(u, a, b, 1 - y)
                gather_into(u, 1 - c, 2 + a, b)
        for item in first(u):
            item.start()

    def from_beside(u, cc, a):
        return got_1a[u][ordered(u, cc, (a,))]

    def stage_second(u):
        if u in Z_FIRST:
            for item in z_first(u):
                item.wait_recv()
            for a in range(2):
                cc, yy = (a, 1 - y) if Z_FIRST[u] == 1 else (1 - c, a)
                gather_into(u, cc, z, yy, *from_line(u, cc, yy))
            for item in plane_first(u):
                item.start()
            return
        for item in first(u):
            item.wait_recv()
        for a in range(2):
            gather_into(u, 1 - c, a, y, from_beside(u, 1 - c, a))
            gather_into(u, c, 2 + a, 1 - y, got_1b[u][a, 1 - y])
        for item in second(u):
            item.start()

    def stage_along(u):
        if u in Z_FIRST:
            for item in plane_first(u):
                item.wait_recv()
            cc, yy = (1 - c, y) if Z_FIRST[u] == 1 else (c, 1 - y)
            gather_into(u, cc, z, yy, *from_line(u, cc, yy), got_2a[u][cc if Z_FIRST[u] == 1 else yy])
            for item in plane_second(u):
                item.start()
            return
        for item in second(u):
            item.wait_recv()
        for a in range(2):
            gather_into(u, c, a, y, from_beside(u, c, a), got_2a[u][a])
            gather_into(u, c, 2 + a, y, got_1b[u][a, y], got_2b[u][a])
        for item in along(u):
            item.start()

    def stage_pair(u):
        full = grads[GRAD_UNITS[u][0]][where(u, c, z, y)].astype(F32)
        if u in Z_FIRST:
            for item in plane_second(u):
                item.wait_recv()
            others = [got_0[u][ordered(u, c, (z, y))], *from_line(u, c, y)]
            others += [got_2a[u][c if Z_FIRST[u] == 1 else y], got_2b[u][...]]
        else:
            for item in along(u):
                item.wait_recv()
            others = [got_3[u][step] for step in range(3)]
        for other in others:
            full = full + other.astype(F32)
        total[u][0] = full[:24]
        total[u][1] = full[24:]
        for item in pair(u):
            item.start()

    def stage_end(u):
        matrix, start, n, _ = GRAD_UNITS[u]
        lanes = slice(start, start + n)
        side = mine(u)
        outs[matrix][side, :, lanes] = total[u][side]
        for item in pair(u):
            item.wait_recv()
        outs[matrix][1 - side, :, lanes] = got_4[u][...]
        own, other = total[u][side], got_4[u][...]
        square[...] += jnp.broadcast_to(total_of(own * own) + total_of(other * other), (8, 128))
        if u in Z_FIRST:
            sent = z_first(u) + plane_first(u) + plane_second(u)
        else:
            sent = first(u) + second(u) + along(u)
        for item in [twin_copy(u)] + sent:
            item.wait_send()

    def table_sum(u):
        @pl.when(me < PIECES)
        def _():
            each(lambda step: table_copy(step, False, 0).wait_recv())
            table_got[me] = table[me]

            def add(at, held):
                return held + table_got[at].astype(F32)

            total_rows = lax.fori_loop(1, 32, add, table_got[0].astype(F32))
            top, rest = split_two(total_rows[:8] + total_rows[8:])
            exact = jnp.concatenate([top.astype(F32), rest.astype(F32)], 0)
            table_out[me] = jnp.where(me >= 18, exact, total_rows).astype(BF16)
            each(lambda step: table_copy(step, True, me).start())

    late_parts = []

    def table_end(u):
        each(table_wait_back)
        need(weight(count))
        late_parts.append(
            table_finish(
                table_out, upstream, kept.table, kept.norms, kept.proj_t, late_parts[0], g_in, g_norm, send_stat
            )
        )
        for at, value in enumerate(late_parts[1][:4]):
            late_rows[at] = jnp.broadcast_to(value, (24, VP))
        square[...] += jnp.broadcast_to(late_parts[1][-1], (8, 128))

    def stat_copy(step):
        target = (peer(step) // 2, lax.rem(peer(step), 2))
        return remote(stat, stat_got.at[me], table_send.at[3, step], table_recv.at[3, step], target)

    def send_stat(rows):
        line = iota((8, VP), 0)
        result = jnp.zeros((8, VP), F32)
        for at, row in enumerate(rows):
            result = jnp.where(line == at, row, result)
        stat[...] = result
        each(lambda step: stat_copy(step).start())
        stat_got[me] = stat[...]

    def table_last():
        each(lambda step: stat_copy(step).wait())
        totals = lax.fori_loop(1, 32, lambda at, held: held + stat_got[at], stat_got[0])
        mean_1, mean_2 = totals[0:1] * (1.0 / D), totals[1:2] * (1.0 / D)
        inner, unit, rstd, emb_grad = (late_rows[at] for at in range(4))
        g_emb[...] = emb_grad + rstd * (inner - mean_1 - unit * mean_2)
        first, second = rstd[0:1] * mean_1, rstd[0:1] * mean_2
        whole = totals[6:7] - 2.0 * (first * totals[2:3] + second * totals[3:4])
        whole = whole + first * first * D + 2.0 * first * second * totals[4:5] + second * second * totals[5:6]
        return total_of(whole)

    stages = (stage_first, stage_second, stage_along, stage_pair, stage_end, table_sum, table_end)
    pending = list(BACKWARD_ORDER)

    def hook():
        for stage, u in pending.pop(0):
            stages[stage](u)

    def done(u):
        if u == 0:
            pl.semaphore_wait(barrier, 31)
        twin_copy(u).start()
        hook()

    names = Kept._fields

    load(AT.branch, saved.branch, branch)

    def phase_one(*early_refs):
        e = Early(*early_refs)
        load(weight(0), far[0], grads[0])
        load(AT.slope, saved.slope, e.slope)
        load(AT.active, saved.active, e.active)
        load(weight(1), far[1], grads[1])
        for name in names:
            load(getattr(AT, name), getattr(saved, name), getattr(kept, name))
        for m in (2, 3):
            load(weight(m), far[m], grads[m])
        for name in Early._fields[2:6]:
            load(getattr(AT, name), getattr(saved, name), getattr(e, name))
        load(weight(4), far[4], grads[4])
        for name in Early._fields[6:8]:
            load(getattr(AT, name), getattr(saved, name), getattr(e, name))
        load(weight(5), far[5], grads[5])
        for name in Early._fields[8:]:
            load(getattr(AT, name), getattr(saved, name), getattr(e, name))
        load(weight(6), far[6], grads[6])
        view = [g.reshape(2, D, n) for g, n in zip(grads, widths)]
        need(AT.branch)
        transpose_into(branch, branch_t)
        hook()

        def grad_tile(m, start, left_t, right, half, at):
            lanes = slice(start + half * widths[m] + at, start + half * widths[m] + at + 384)
            view[m][half, :, at : at + 384] = nn(left_t[...], right[:, lanes]).astype(BF16)

        def grad_half(m, start, left_t, right, half):
            for at in range(0, widths[m], 384):
                grad_tile(m, start, left_t, right, half, at)

        for part in range(2):
            need(weight(part))
            if part == 0:
                need(AT.slope)

            def down_back(half, at, part=part):
                lanes = slice(part * 1536 + half * 768 + at, part * 1536 + half * 768 + at + 384)
                back = nn(branch[...], view[part][half, :, at : at + 384])
                e.slope[:, lanes] = (back * e.slope[:, lanes].astype(F32)).astype(BF16)

            if part == 0:
                for at in (0, 384):
                    for half in range(2):
                        down_back(half, at)
                    hook()
                    if at == 0:
                        need(AT.active)
                    for half in range(2):
                        grad_tile(part, 0, branch_t, e.active, half, at)
                    done(at // 384)
            else:
                for half in range(2):
                    for at in (0, 384):
                        down_back(half, at)
                    hook()
                grad_half(part, part * 1536, branch_t, e.active, 0)
                hook()
                grad_half(part, part * 1536, branch_t, e.active, 1)
                done(2)
        for part in range(2):
            need(weight(2 + part))
            for half in range(2):
                start = part * 1536 + half * 768
                back = nt(e.slope[:, start : start + 768], view[2 + part][half])
                upstream[...] = back if start == 0 else upstream[...] + back
                hook()
            if part == 0:
                need(AT.feed_normed_t)
            grad_half(2 + part, part * 1536, e.feed_normed_t, e.slope, 0)
            hook()
            grad_half(2 + part, part * 1536, e.feed_normed_t, e.slope, 1)
            done(3 + part)
        need(*(getattr(AT, name) for name in names))
        norms = kept.norms[...]

        def gain(number):
            return norms[number : number + 1, :]

        need(AT.unit_2, AT.rstd_2)
        scale_2, shift_2 = back_rows(e.unit_2, e.rstd_2, gain(2), upstream, stream, branch, False)
        hook()
        need(weight(4), AT.col_mixed_t)
        mixed[...] = (nt(branch[:, :384], view[4][0]) + nt(branch[:, 384:], view[4][1])).astype(BF16)
        hook()
        for half in range(2):
            grad_half(4, 0, e.col_mixed_t, branch, half)
        done(5)
        need(AT.col_proj, AT.col_prob)
        proj = e.active

        def attend(at, carry):
            rows = pl.ds(pl.multiple_of((at // PAIRS) * 128, 128), 128)
            lane = lax.rem(at, PAIRS) * 128

            def lanes(part):
                return pl.ds(pl.multiple_of(part * D + lane, 128), 128)

            query = stacked(e.col_proj[rows, lanes(0)])
            key = e.col_proj[rows, lanes(1)]
            value = e.col_proj[rows, lanes(2)]
            above = stacked(mixed[rows, lanes(0)])
            prob = e.col_prob[at]
            grad = nt(above, value)
            grad = prob * (grad - jnp.sum(prob * grad, -1, keepdims=True))
            small = grad.astype(BF16)
            scale = HD ** (-0.5)
            proj[rows, lanes(0)] = (unstacked(nn(small, key), 128) * scale).astype(BF16)
            proj[rows, lanes(1)] = (tn(small, query) * scale).astype(BF16)
            proj[rows, lanes(2)] = tn(prob.astype(BF16), above).astype(BF16)
            return carry

        for part in range(6):
            lax.fori_loop(4 * part, 4 * part + 4, attend, 0, unroll=4)
            hook()
        need(weight(5))
        for half in range(2):
            back = nt(proj[:, half * 1152 : half * 1152 + 1152], view[5][half])
            upstream[...] = back if half == 0 else upstream[...] + back
            hook()
        need(AT.col_normed_t)
        for third in range(3):
            for half in range(2):
                grad_tile(5, 0, e.col_normed_t, proj, half, third * 384)
            done(6 + third)
        need(AT.unit_1, AT.rstd_1)
        scale_1, shift_1 = back_rows(e.unit_1, e.rstd_1, gain(1), upstream, stream, branch, False)
        hook()
        need(weight(6))
        mixed[...] = (nt(branch[:, :384], view[6][0]) + nt(branch[:, 384:], view[6][1])).astype(BF16)
        line = iota((8, D), 0)
        vectors = jnp.zeros((8, D), F32)
        moved = kept.moved[...]
        rows = (scale_1, scale_2, moved[0:1], shift_1, shift_2, moved[1:2])
        for number, row in enumerate(rows):
            vectors = jnp.where(line == number, row, vectors)
        extras = jnp.concatenate([kept.extras[0:1, :], jnp.zeros((1, D - 128), F32)], 1)
        kept.moved[...] = jnp.where(line == 6, extras, vectors)
        hook()

    pl.run_scoped(phase_one, *(pltpu.VMEM(*item) for item in pick_items(Early, SAVED)))

    def phase_two(*late_refs):
        e = Late(*late_refs[:-3])
        in_row, left_hi, left_lo = late_refs[-3:]
        for name in Late._fields:
            load(getattr(AT, name), getattr(saved, name), getattr(e, name))
        load(weight(count), in_row_far.at[0], in_row)
        view = grads[6].reshape(2, D, widths[6])
        late_parts.append(in_row)
        need(AT.row_mixed_t)
        for half in range(2):
            lanes = slice(half * 384, half * 384 + 384)
            view[half] = nn(e.row_mixed_t[...], branch[:, lanes]).astype(BF16)
        done(9)
        need(AT.hot_all, AT.weight_hi, AT.prob, AT.hot_ri, AT.hot_ir)
        shape = (HERE, HERE)
        back = (
            ((iota(shape, 1) >> 4) == (iota(shape, 0) & 31))
            & ((iota(shape, 1) & 15) == (iota(shape, 0) >> 5))
        )
        mixed[...] = nn(one_zero(back).astype(BF16), mixed[...]).astype(BF16)
        value_rows = []
        for hp in range(PAIRS):
            lanes = slice(hp * 128, hp * 128 + 128)
            part = mixed[:, lanes]
            upstream[:, lanes] = nt(part, kept.value_two[hp])
            value_rows.append(unstacked(tn(e.weight_hi[:, lanes], part), 64))
        hook()
        split_heads_to(upstream, left_hi, left_lo)
        hook()
        hot_all = e.hot_all[...]
        grad = nn(left_hi[...], hot_all) + nn(left_lo[...], hot_all)
        extra = jnp.concatenate(
            [kept.touch[...] * (contact_head[h] * COLS) for h in range(HEADS)], 0
        )
        grad = grad + extra
        prob = e.prob[...]
        grad = prob * (grad - jnp.sum(prob * grad, -1, keepdims=True))
        low_grad = grad.astype(BF16)
        hook()
        merge_heads(low_grad, e.hot_all, branch, None)
        hook()
        table_pair = nn(e.hot_ri[...], branch[...])
        stream_hi, stream_lo = split_two(stream[...])
        hot_ir = e.hot_ir[...]
        table_grad = kept.grad_head[...] + nn(hot_ir, stream_hi) + nn(hot_ir, stream_lo)
        value_grad = jnp.concatenate(value_rows, 1)
        last = jnp.where(iota((8, D), 0) == 7, table_grad[32:33], kept.moved[...])
        top, rest = split_two(last)
        groups = [table_pair[4:20], table_pair[20:36], value_grad[4:20], value_grad[20:36]]
        groups += [table_grad[0:16], table_grad[16:32]]
        groups += [jnp.concatenate([top.astype(F32), rest.astype(F32)], 0)]
        for number, group in enumerate(groups):
            for third in range(3):
                table[3 * number + third] = group[:, third * 256 : third * 256 + 256].astype(BF16)
        each(table_start)
        hook()
        hook()

    pl.run_scoped(
        phase_two,
        *(pltpu.VMEM(*item) for item in pick_items(Late, SAVED)),
        pltpu.VMEM((24, 3 * D), F32),
        pltpu.VMEM((HEADS * WIDE, ROWS * VP), BF16),
        pltpu.VMEM((HEADS * WIDE, ROWS * VP), BF16),
    )
    assert not pending

    def square_copy(step):
        other = lax.rem(me + step, 32)
        return remote(
            square, square_got.at[me], table_send.at[2, step], table_recv.at[2, step], (other // 2, lax.rem(other, 2))
        )

    each(lambda step: square_copy(step).start())
    square_got[me] = square[...]
    each(lambda step: table_wait_send(step))
    for u in range(units):
        for item in pair(u):
            item.wait_send()
    emb_square = table_last()
    each(lambda step: square_copy(step).wait())
    total_square = lax.fori_loop(1, 32, lambda at, held: held + square_got[at], square_got[0])[0:1]
    vector = table_out[18].astype(F32)
    vector = vector[6:7, :128] + vector[14:15, :128]
    counted = kept.extras[1:2, :]
    column = iota((1, 128), 1)
    contact = jnp.where(column <= HEADS, vector, 0.0)
    total_square = total_square + total_of(contact * contact) + emb_square
    grad_norm = jnp.sqrt(total_square)
    factor = jnp.minimum(1.0, MAX_NORM / grad_norm)
    losses = (
        (0, vector[:, HEADS + 1 : HEADS + 2]),
        (1, counted[:, 0:1]),
        (2, vector[:, HEADS + 2 : HEADS + 3]),
        (3, counted[:, 1:2]),
    )
    loss_row = jnp.zeros((1, 128), F32)
    for at, value in losses:
        loss_row = jnp.where(column == at, value, loss_row)
    number = iota((8, 128), 0)
    result = jnp.zeros((8, 128), F32)
    for at, row in enumerate((contact, counted, factor, grad_norm, loss_row)):
        result = jnp.where(number == at, row, result)
    stats[...] = result


def backward_call(contact_head, weights, in_row, saved):
    widths = GRAD_WIDTHS
    count = len(widths)
    inside = pl.BlockSpec(memory_space=pltpu.VMEM)
    anywhere = pl.BlockSpec(memory_space=pl.ANY)

    units = len(GRAD_UNITS)

    def shapes(lead, dtype, other=None):
        leads = [other if other and u in Z_FIRST else lead for u in range(units)]
        return [pltpu.VMEM((*at, n), dtype) for at, (_, _, n, _) in zip(leads, GRAD_UNITS)]

    outs = pl.pallas_call(
        backward_kernel,
        out_shape=[jax.ShapeDtypeStruct((2, 24, n), F32) for n in widths]
        + [
            jax.ShapeDtypeStruct((24, 3 * D), F32),
            jax.ShapeDtypeStruct((24, VP), F32),
            jax.ShapeDtypeStruct((8, 24), F32),
            jax.ShapeDtypeStruct((8, 128), F32),
        ],
        in_specs=[pl.BlockSpec(memory_space=pltpu.SMEM)] + [anywhere] * (1 + count + len(SAVED)),
        out_specs=[inside] * (4 + count),
        scratch_shapes=[pltpu.VMEM((2, NZ, NY, 2, 48, n), BF16) for n in widths]
        + [pltpu.VMEM(*item) for item in pick_items(Kept, SAVED)]
        + [
            pltpu.VMEM((HERE, D), F32),
            pltpu.VMEM((HERE, D), BF16),
            pltpu.VMEM((D, HERE), BF16),
            pltpu.VMEM((HERE, D), BF16),
        ]
        + [
            pltpu.VMEM((NZ, NY, 2, 48, n) if paired else (2, NZ, NY, 48, n), BF16)
            for _, _, n, paired in GRAD_UNITS
        ]
        + shapes((2, 2, 48), BF16, (3, 2, 2, 48))
        + shapes((2, 2, 48), BF16, (16,))
        + shapes((2, 48), BF16, (2, 48))
        + shapes((2, 48), BF16, (48,))
        + shapes((3, 48), BF16, (16,))
        + shapes((2, 24), F32)
        + shapes((24,), F32)
        + [
            pltpu.VMEM((PIECES, 16, 256), BF16),
            pltpu.VMEM((PIECES, 16, 256), BF16),
            pltpu.VMEM((32, 16, 256), BF16),
            pltpu.VMEM((8, 128), F32),
            pltpu.VMEM((32, 8, 128), F32),
            pltpu.VMEM((8, VP), F32),
            pltpu.VMEM((32, 8, VP), F32),
            pltpu.VMEM((4, 24, VP), F32),
            pltpu.SemaphoreType.DMA((4, 32)),
            pltpu.SemaphoreType.DMA((4, 32)),
            pltpu.SemaphoreType.DMA((units, 9)),
            pltpu.SemaphoreType.DMA((units, 9)),
            pltpu.SemaphoreType.DMA((len(SAVED) + count + 1,)),
        ],
        compiler_params=pltpu.CompilerParams(
            collective_id=1, has_side_effects=True, vmem_limit_bytes=63 * 2**20
        ),
    )(contact_head, *weights, in_row, *saved)
    return outs[:count], outs[count:]


UPDATE_RATES = (LEARN_RATE,) * 4 + (VECTOR_RATE,) * 3


def update_kernel(*refs):
    given, far, held, results = refs[:32], refs[32:60], refs[60:92], refs[92:120]
    sems, out_sems = refs[120:122]
    outs, copies = results[:21], results[21:26]
    loss_ref, norm_ref = results[26:]

    def leave(*numbers):
        for n in numbers:
            pltpu.make_async_copy(results[n], far[n], out_sems.at[n]).start()

    moves = [pltpu.make_async_copy(a, b, sems.at[n]) for n, (a, b) in enumerate(zip(given, held))]
    groups = (
        (10, 7, 5, 11, 12, 13),
        (4, 6, 14, 15, 16),
        (2, 3, 17, 18, 19),
        (0, 1, 20, 21, 22),
        (8, 9, *range(23, 32)),
    )
    for group in groups:
        for n in group:
            moves[n].start()

    def arrive(number):
        for n in groups[number]:
            moves[n].wait()

    reduced, g_in, g_emb, g_norm, stats = held[:7], held[7], held[8], held[9], held[10]
    states = [held[11 + 3 * n : 14 + 3 * n] for n in range(7)]
    outs = [outs[3 * n : 3 * n + 3] for n in range(7)]
    order = feature_order()
    arrive(0)
    factor = stats[2:3, 0:1]
    loss_ref[...] = stats[4:5, 0:4]
    norm_ref[...] = stats[3:4, 0:1]

    def natural(values):
        top, rest = split_two(values)
        last = (values - top.astype(F32) - rest.astype(F32)).astype(BF16)
        return nt(top, order) + nt(rest, order) + nt(last, order)

    def update(number, where, grad):
        master, first, second = (ref[where] for ref in states[number])
        new, first, second = adam_update(master, first, second, grad * factor, UPDATE_RATES[number])
        for ref, value in zip(outs[number], (new, first, second)):
            ref[where] = value
        if number < 5:
            copies[number][where] = new.astype(BF16)

    every = slice(None)
    g_out_col, g_in_col, g_out_row = reduced[4:]
    for half in range(2):
        lanes = slice(half * 1152, half * 1152 + 1152)
        update(0, (0, every, lanes), g_in[:, lanes])
        update(0, (1, every, lanes), g_in_col[half])
    leave(0, 1, 2, 21, 26, 27)
    arrive(1)
    for half in range(2):
        lanes = slice(half * 384, half * 384 + 384)
        update(1, (0, every, lanes), natural(g_out_row[half]))
        update(1, (1, every, lanes), natural(g_out_col[half]))
    leave(3, 4, 5, 22)
    for number, first in ((2, 2), (3, 0)):
        arrive(number)
        for half in range(2):
            for part in range(2):
                start = part * 1536 + half * 768
                lanes = slice(start, start + 768)
                update(number, (every, lanes), reduced[first + part][half])
        leave(*((6, 7, 8, 23) if number == 2 else (9, 10, 11, 24)))
    arrive(4)
    update(4, (every, every), g_emb[:, :VOCAB])
    update(5, (every, every), g_norm[...])
    update(6, (every, every), stats[0:1, : HEADS + 1])
    leave(12, 13, 14, 25, 15, 16, 17, 18, 19, 20)
    for n in range(28):
        pltpu.make_async_copy(results[n], far[n], out_sems.at[n]).wait()


def update_call(reduced, g_in, g_emb, g_norm, stats, states):
    anywhere = pl.BlockSpec(memory_space=pl.ANY)
    flat = [item for state in states for item in state]
    shapes = [jax.ShapeDtypeStruct(item.shape, F32) for item in flat]
    shapes += [jax.ShapeDtypeStruct(states[n][0].shape, BF16) for n in range(5)]
    shapes += [jax.ShapeDtypeStruct((1, 4), F32), jax.ShapeDtypeStruct((1, 1), F32)]
    given = (*reduced, g_in, g_emb, g_norm, stats, *flat)
    return pl.pallas_call(
        update_kernel,
        out_shape=shapes,
        in_specs=[anywhere] * len(given),
        out_specs=[anywhere] * len(shapes),
        scratch_shapes=[pltpu.VMEM(item.shape, F32) for item in given]
        + [pltpu.VMEM(item.shape, item.dtype) for item in shapes]
        + [
            pltpu.SemaphoreType.DMA((len(given),)),
            pltpu.SemaphoreType.DMA((len(shapes),)),
            pltpu.VMEM((44, 512, 512), F32),
        ],
        compiler_params=pltpu.CompilerParams(vmem_limit_bytes=62 * 2**20),
    )(*given)


def adam_update(master, first, second, grad_part, rate):
    first = BETA_ONE * first + (1.0 - BETA_ONE) * grad_part
    second = BETA_TWO * second + (1.0 - BETA_TWO) * grad_part * grad_part
    scaled = first * (1.0 / (1.0 - BETA_ONE**STEP))
    moved = scaled / (jnp.sqrt(second * (1.0 / (1.0 - BETA_TWO**STEP))) + ADAM_EPS)
    return (master - rate * (moved + WEIGHT_DECAY * master), first, second)


def shards(
    tokens,
    targets,
    masked,
    contact_pairs,
    labels,
    attention_in_master,
    attention_in_first,
    attention_in_second,
    attention_out_master,
    attention_out_first,
    attention_out_second,
    feed_up_master,
    feed_up_first,
    feed_up_second,
    feed_down_master,
    feed_down_first,
    feed_down_second,
    embedding_master,
    embedding_first,
    embedding_second,
    norm_params_master,
    norm_params_first,
    norm_params_second,
    contact_head_master,
    contact_head_first,
    contact_head_second,
):
    both = ("seq", "col")
    micro, rows_here, cols_here = tokens.shape
    ncol = lax.axis_size("col")
    ndev = lax.axis_size("seq") * ncol
    cols = cols_here * ncol
    me = lax.axis_index("seq") * ncol + lax.axis_index("col")
    per = ndev // micro
    cw = cols // per
    mine = me // per
    base = (me % per) * cw
    shard = D // ndev

    tiled = lax.axis_size("seq") == 16 and ncol == 2
    if tiled:
        raw = (
            tokens,
            targets,
            masked,
            contact_pairs.transpose(0, 2, 1),
            labels,
            embedding_master.T,
            norm_params_master,
            attention_in_master,
            attention_out_master,
            feed_up_master,
            feed_down_master.T,
        )
        weights, saved = forward_call(raw, contact_head_master)
        reduced, (g_in, g_emb, g_norm, stats) = backward_call(
            contact_head_master, [weights[n] for n in (5, 6, 3, 4, 2, 1, 0)], attention_in_master, saved
        )
        states = (
            (attention_in_master, attention_in_first, attention_in_second),
            (attention_out_master, attention_out_first, attention_out_second),
            (feed_up_master, feed_up_first, feed_up_second),
            (feed_down_master.T, feed_down_first.T, feed_down_second.T),
            (embedding_master.T, embedding_first.T, embedding_second.T),
            (norm_params_master, norm_params_first, norm_params_second),
            (contact_head_master[None], contact_head_first[None], contact_head_second[None]),
        )
        outs = update_call(reduced, g_in, g_emb, g_norm, stats, states)
        return (
            *outs[:9],
            *(item.T for item in outs[9:15]),
            *outs[15:18],
            *(item[0] for item in outs[18:21]),
            *outs[21:24],
            *(item.T for item in outs[24:26]),
            outs[26][0],
            outs[27][0, 0],
        )
    inputs = jnp.where(masked > 0, MASK_ID, tokens)
    masters = [
        jnp.concatenate(
            [
                jnp.pad(embedding_master.T, ((0, 0), (0, 128 - VOCAB))),
                jnp.pad(norm_params_master.T, ((0, 0), (0, 120))),
            ],
            1,
        ),
        attention_in_master[0],
        attention_out_master[0],
        attention_in_master[1],
        attention_out_master[1],
        feed_up_master,
        feed_down_master.T,
    ]
    whole = jnp.stack([inputs, targets])
    whole = lax.all_gather(lax.all_gather(whole, "col", axis=3, tiled=True), "seq", axis=2, tiled=True)
    pairs_all = lax.all_gather(
        jnp.concatenate([contact_pairs, labels[:, :, None]], -1), both, axis=1, tiled=True
    )
    gathered = []
    for master in masters:
        full = lax.all_gather(master.astype(BF16), both, axis=0, tiled=True)
        gathered.append(full.reshape(D, 2, -1).transpose(1, 0, 2))
    counts = (
        jnp.sum(whole[0] == MASK_ID).astype(F32),
        jnp.sum(pairs_all[..., 2] >= 0).astype(F32),
    )
    ids_all = lax.dynamic_index_in_dim(whole[0], mine, 0, False)
    ids_local = lax.dynamic_slice_in_dim(ids_all, base, cw, 1)
    targets_local = lax.dynamic_slice_in_dim(
        lax.dynamic_index_in_dim(whole[1], mine, 0, False), base, cw, 1
    )
    pairs = lax.dynamic_index_in_dim(pairs_all, mine, 0, False)

    table = gathered[0][0][:, :VP].T
    norms = gathered[0][1][:, :8].T.astype(F32)
    in_row, out_row, in_col, out_col, up_w, down_t = (
        jnp.concatenate([g[0], g[1]], 1) for g in gathered[1:]
    )
    big = (in_row, in_col, out_row, out_col, up_w, down_t)

    grads, tables, contact_total, mlm_total, bce_total, kept = step(
        big,
        table,
        norms,
        contact_head_master,
        ids_all,
        ids_local.reshape(-1),
        ids_local.T.reshape(-1),
        targets_local.T.reshape(-1),
        pairs[:, 0] - base,
        pairs[:, 1],
        pairs[:, 2],
        counts,
        cw,
    )
    table_pair, value_grad, table_grad, vectors = tables
    extras = jnp.zeros((2, D), F32).at[0, : HEADS + 3].set(
        jnp.concatenate([contact_total, mlm_total[None], bce_total[None]])
    )
    sums = jnp.concatenate([table_pair[:40], value_grad[:40], table_grad[:40], vectors, extras])
    flat_grad = jnp.concatenate([g.astype(BF16) for g in grads], 1)
    reduced = lax.psum_scatter(flat_grad, both, scatter_dimension=0, tiled=True).astype(F32)
    g_in_col, g_out_row, g_out_col, g_up, g_down = jnp.split(
        reduced, [3 * D, 4 * D, 5 * D, 5 * D + FF], 1
    )
    sums = lax.psum(sums, both)
    unit_t, rstd_t, normed_t, query_t, key_t = kept
    rows_all = ids_all.shape[0]
    spare = ((0, VP - 40), (0, 0))
    table_pair, value_grad, table_grad = (
        jnp.pad(sums[a : a + 40], spare) for a in (0, 40, 80)
    )
    vectors = sums[120:126]
    contact_grad, mlm_total, bce_total = (
        sums[126, : HEADS + 1], sums[126, HEADS + 1], sums[126, HEADS + 2]
    )
    row_scale = (HD * rows_all) ** (-0.5)
    query_grad = []
    key_grad = []
    for h in range(HEADS):
        pair = heads_of(table_pair, h)
        query_grad.append(jnp.dot(pair, heads_of(key_t, h).astype(F32), precision=PRECISE))
        key_grad.append(jnp.dot(pair.T, heads_of(query_t, h).astype(F32), precision=PRECISE))
    proj_grad = jnp.concatenate(
        [
            jnp.concatenate(query_grad, 1) * row_scale,
            jnp.concatenate(key_grad, 1) * row_scale,
            value_grad,
        ],
        1,
    )
    proj_hi, proj_lo = split_two(proj_grad)
    normed_grad = nt(proj_hi, in_row) + nt(proj_lo, in_row)
    back_t, scale_0, shift_0 = norm_back(unit_t, rstd_t, norms[0], normed_grad)
    table_grad = table_grad + back_t
    low = me * shard
    normed_mine = lax.dynamic_slice_in_dim(normed_t, low, shard, 1)
    grad_in_row = tn(normed_mine, proj_hi) + tn(normed_mine, proj_lo)
    norm_grad = jnp.concatenate([scale_0[None], vectors[:3], shift_0[None], vectors[3:]])
    table_mine = lax.dynamic_slice_in_dim(table_grad[:VOCAB], low, shard, 1)
    norm_mine = lax.dynamic_slice_in_dim(norm_grad, low, shard, 1)
    reduced_all = (g_in_col, g_out_row, g_out_col, g_up, g_down)

    local_square = (
        sum(jnp.sum(g * g) for g in reduced_all)
        + jnp.sum(grad_in_row * grad_in_row)
        + jnp.sum(table_mine * table_mine)
        + jnp.sum(norm_mine * norm_mine)
    )
    square = lax.psum(local_square, both) + jnp.sum(contact_grad * contact_grad)
    grad_norm = jnp.sqrt(square)
    factor = jnp.minimum(1.0, MAX_NORM / grad_norm)
    in_new, in_moment, in_square = adam_update(
        attention_in_master, attention_in_first, attention_in_second, jnp.stack([grad_in_row, g_in_col]) * factor, LEARN_RATE
    )
    out_new, out_moment, out_square = adam_update(
        attention_out_master, attention_out_first, attention_out_second, jnp.stack([g_out_row, g_out_col]) * factor, LEARN_RATE
    )
    up_new, up_moment, up_square = adam_update(
        feed_up_master, feed_up_first, feed_up_second, g_up * factor, LEARN_RATE
    )
    down_new, down_moment, down_square = adam_update(
        feed_down_master, feed_down_first, feed_down_second, g_down.T * factor, LEARN_RATE
    )
    table_new, table_moment, table_square = adam_update(
        embedding_master, embedding_first, embedding_second, table_mine * factor, VECTOR_RATE
    )
    norm_new, norm_moment, norm_square = adam_update(
        norm_params_master, norm_params_first, norm_params_second, norm_mine * factor, VECTOR_RATE
    )
    head_new, head_moment, head_square = adam_update(
        contact_head_master, contact_head_first, contact_head_second, contact_grad * factor, VECTOR_RATE
    )
    loss_parts = jnp.stack([mlm_total, counts[0], bce_total, counts[1]])
    return (
        in_new, in_moment, in_square,
        out_new, out_moment, out_square,
        up_new, up_moment, up_square,
        down_new, down_moment, down_square,
        table_new, table_moment, table_square,
        norm_new, norm_moment, norm_square,
        head_new, head_moment, head_square,
        in_new.astype(BF16), out_new.astype(BF16), up_new.astype(BF16), down_new.astype(BF16), table_new.astype(BF16),
        loss_parts, grad_norm,
    )


def solution(mesh):
    both = ("seq", "col")
    cells = P(None, "seq", "col")
    stack = P(None, both, None)
    row_split = P(both, None)
    col_split = P(None, both)
    weights = [stack] * 6 + [row_split] * 3 + [col_split] * 9 + [P()] * 3
    return jax.shard_map(
        shards,
        mesh=mesh,
        in_specs=(cells, cells, cells, stack, col_split, *weights),
        out_specs=(*weights, stack, stack, row_split, col_split, col_split, P(), P()),
        check_vma=False,
    )
```

```python
import typing

import jax
import jax.numpy as jnp
from jax import lax
from jax.experimental import pallas as pl
from jax.experimental.pallas import tpu as pltpu
from jax.sharding import PartitionSpec as P

D = 768
HEADS = 12
HD = 64
FF = 3072
VOCAB = 33
VP = 64
STEP = 10

NORM_EPS = 1e-05
MASK_ID = 32
MAX_NORM = 0.001
LEARN_RATE = 0.05
VECTOR_RATE = 0.5
BETA_ONE = 0.9
BETA_TWO = 0.95
ADAM_EPS = 1e-08
WEIGHT_DECAY = 0.01
PRECISE = lax.Precision.HIGHEST
F32 = jnp.float32
BF16 = jnp.bfloat16


def nn(left, right):
    return lax.dot_general(left, right, (((1,), (0,)), ((), ())), preferred_element_type=F32)


def tn(left, right):
    return lax.dot_general(left, right, (((0,), (0,)), ((), ())), preferred_element_type=F32)


def nt(left, right):
    return lax.dot_general(left, right, (((1,), (1,)), ((), ())), preferred_element_type=F32)


def split_two(values):
    high = values.astype(BF16)
    return high, (values - high.astype(F32)).astype(BF16)


def norm_stats(values):
    centre = values - jnp.mean(values, -1, keepdims=True)
    rstd = lax.rsqrt(jnp.mean(centre * centre, -1, keepdims=True) + NORM_EPS)
    return centre * rstd, rstd


def norm_back(unit, rstd, scale_vec, upstream):
    inner = upstream * scale_vec
    grad = rstd * (
        inner - jnp.mean(inner, -1, keepdims=True) - unit * jnp.mean(inner * unit, -1, keepdims=True)
    )
    return grad, jnp.sum(upstream * unit, 0), jnp.sum(upstream, 0)


GELU_K = 0.7978845608028654
GELU_C = 0.044715


def gelu_parts(up):
    square = up * up
    bent = jnp.tanh(GELU_K * up * (1.0 + GELU_C * square))
    half = 0.5 * (1.0 + bent)
    slope = half + 0.5 * up * (1.0 - bent * bent) * GELU_K * (1.0 + 3.0 * GELU_C * square)
    return up * half, slope


def heads_of(block, head):
    return block[:, head * HD : (head + 1) * HD]


def step(big, table, norms, contact_head, ids_all, ids_ri, ids_ir, targets_ir, pair_first, pair_second, labels, counts, cw):
    in_row, in_col, out_row, out_col, up_w, down_t = big
    rows, cols = ids_all.shape
    here = rows * cw
    row_scale = (HD * rows) ** (-0.5)
    vocab = jnp.arange(VP)[:, None]
    hot_all = (ids_all[:, None, :] == vocab[None]).astype(BF16).reshape(rows * VP, cols)
    hot_ri = (ids_ri[None, :] == vocab).astype(BF16)
    hot_ir = (ids_ir[None, :] == vocab).astype(BF16)
    spot = jnp.arange(here)
    perm = (
        ((spot // rows)[:, None] == (spot % cw)[None, :])
        & ((spot % rows)[:, None] == (spot // cw)[None, :])
    ).astype(BF16)

    def to_heads(block):
        return block.reshape(rows, cw, HEADS, VP).transpose(2, 1, 0, 3).reshape(HEADS * cw, rows * VP)

    def to_tokens(block):
        return block.reshape(HEADS, cw, rows, VP).transpose(2, 1, 0, 3).reshape(here, HEADS * VP)

    def per_head(block, other, how):
        return jnp.concatenate(
            [how(heads_of(block, h), heads_of(other, h)) for h in range(HEADS)], -1
        )

    table_f = table.astype(F32)
    unit_t, rstd_t = norm_stats(table_f)
    normed_t = (unit_t * norms[0] + norms[4]).astype(BF16)
    proj_t = nn(normed_t, in_row).astype(BF16)
    query_t, key_t, value_t = proj_t[:, :D], proj_t[:, D : 2 * D], proj_t[:, 2 * D :]

    pair_t = per_head(query_t, key_t, nt)
    pair_hi, pair_lo = split_two(pair_t)
    left_hi = to_heads(tn(hot_ri, pair_hi).astype(BF16))
    left_lo = to_heads(tn(hot_ri, pair_lo).astype(BF16))
    score = (nn(left_hi, hot_all) + nn(left_lo, hot_all)) * row_scale
    prob = jax.nn.softmax(score, axis=-1)
    prob_low = prob.astype(BF16)
    weight_t = to_tokens(nt(prob_low, hot_all))
    weight_hi, weight_lo = split_two(weight_t)
    row_mixed_ri = (
        per_head(weight_hi, value_t, nn) + per_head(weight_lo, value_t, nn)
    ).astype(BF16)
    row_mixed = nn(perm, row_mixed_ri).astype(BF16)
    embedded = tn(hot_ir, table)
    after_row = embedded + nn(row_mixed, out_row)

    prob_cube = prob_low.astype(F32).reshape(HEADS, cw, cols)
    head_sum = jnp.sum(prob_cube * contact_head[:HEADS, None, None], 0)
    first_hot = (pair_first[None, :] == jnp.arange(cw)[:, None]).astype(F32)
    second_hot = (pair_second[None, :] == jnp.arange(cols)[:, None]).astype(BF16)
    sum_hi, sum_lo = split_two(head_sum)
    sum_last = (head_sum - sum_hi.astype(F32) - sum_lo.astype(F32)).astype(BF16)
    picked = nn(sum_hi, second_hot) + nn(sum_lo, second_hot) + nn(sum_last, second_hot)
    contact_logit = jnp.sum(picked * first_hot, 0) * cols + contact_head[HEADS]
    owned = jnp.sum(first_hot, 0) > 0
    valid = (labels >= 0) & owned
    positive = (labels == 1).astype(F32)
    bce_sum = jnp.sum(
        jnp.where(valid, jax.nn.softplus(contact_logit) - positive * contact_logit, 0.0)
    )
    coef = jnp.where(valid, jax.nn.sigmoid(contact_logit) - positive, 0.0) / counts[1]
    coef_hi, coef_lo = split_two(coef)
    first_low = first_hot.astype(BF16)
    touch = nt(first_low * coef_hi[None], second_hot) + nt(first_low * coef_lo[None], second_hot)
    grad_contact = jnp.concatenate(
        [jnp.sum(prob_cube * touch[None], (1, 2)) * cols, jnp.sum(coef)[None]]
    )

    unit_1, rstd_1 = norm_stats(after_row)
    col_normed = (unit_1 * norms[1] + norms[5]).astype(BF16)
    col_proj = nn(col_normed, in_col).astype(BF16)
    group = 128 if here % 128 == 0 and 128 % rows == 0 else here
    groups = here // group
    lane = jnp.arange(group)
    same = (lane[:, None] // rows) == (lane[None, :] // rows)

    def cut(block):
        return block.reshape(groups, group, HEADS, HD)

    col_query, col_key, col_value = (cut(col_proj[:, k * D : (k + 1) * D]) for k in range(3))
    col_score = jnp.einsum("gqhe,gkhe->ghqk", col_query, col_key, preferred_element_type=F32) * HD ** (-0.5)
    col_prob = jax.nn.softmax(jnp.where(same, col_score, -1e30), axis=-1)
    col_prob_low = col_prob.astype(BF16)
    col_mixed = (
        jnp.einsum("ghqk,gkhe->gqhe", col_prob_low, col_value, preferred_element_type=F32)
        .astype(BF16)
        .reshape(here, D)
    )
    after_col = after_row + nn(col_mixed, out_col)

    unit_2, rstd_2 = norm_stats(after_col)
    feed_normed = (unit_2 * norms[2] + norms[6]).astype(BF16)
    hidden_up = nn(feed_normed, up_w)
    active, slope = gelu_parts(hidden_up)
    active = active.astype(BF16)
    after_feed = after_col + nt(active, down_t)
    unit_3, rstd_3 = norm_stats(after_feed)
    head_normed = (unit_3 * norms[3] + norms[7]).astype(BF16)
    logits = nt(table, head_normed) * D ** (-0.5)
    logits = jnp.where(vocab < VOCAB, logits, -1e30)
    top = jnp.max(logits, 0, keepdims=True)
    shifted = logits - top
    log_probs = shifted - jnp.log(jnp.sum(jnp.exp(shifted), 0, keepdims=True))
    target_hot = (targets_ir[None, :] == vocab).astype(F32)
    keep = ids_ir[None, :] == MASK_ID
    mlm_sum = -jnp.sum(jnp.where(keep & (target_hot > 0), log_probs, 0.0))
    logit_grad = jnp.where(keep, jnp.exp(log_probs) - target_hot, 0.0) / counts[0]
    logit_low = (logit_grad * D ** (-0.5)).astype(BF16)

    grad_head = nn(logit_low, head_normed)
    stream, scale_3, shift_3 = norm_back(unit_3, rstd_3, norms[3], tn(logit_low, table))
    branch = stream.astype(BF16)
    grad_down = tn(branch, active)
    up_low = (nn(branch, down_t) * slope).astype(BF16)
    grad_up = tn(feed_normed, up_low)
    inner, scale_2, shift_2 = norm_back(unit_2, rstd_2, norms[2], nt(up_low, up_w))
    stream = stream + inner
    branch = stream.astype(BF16)
    grad_out_col = tn(col_mixed, branch)
    mixed_low = nt(branch, out_col).astype(BF16)
    mixed_cut = cut(mixed_low)
    prob_grad = jnp.einsum("gqhe,gkhe->ghqk", mixed_cut, col_value, preferred_element_type=F32)
    score_grad = col_prob * (prob_grad - jnp.sum(col_prob * prob_grad, -1, keepdims=True))
    score_low = score_grad.astype(BF16)
    grad_q = jnp.einsum("ghqk,gkhe->gqhe", score_low, col_key, preferred_element_type=F32)
    grad_k = jnp.einsum("ghqk,gqhe->gkhe", score_low, col_query, preferred_element_type=F32)
    grad_v = jnp.einsum("ghqk,gqhe->gkhe", col_prob_low, mixed_cut, preferred_element_type=F32)
    proj_low = jnp.concatenate(
        [
            (grad_q * HD ** (-0.5)).reshape(here, D),
            (grad_k * HD ** (-0.5)).reshape(here, D),
            grad_v.reshape(here, D),
        ],
        -1,
    ).astype(BF16)
    grad_in_col = tn(col_normed, proj_low)
    inner, scale_1, shift_1 = norm_back(unit_1, rstd_1, norms[1], nt(proj_low, in_col))
    stream = stream + inner
    branch = stream.astype(BF16)
    grad_out_row = tn(row_mixed, branch)
    mixed_low = nt(branch, out_row).astype(BF16)
    mixed_ri = tn(perm, mixed_low).astype(BF16)
    drive_hi, drive_lo = split_two(per_head(mixed_ri, value_t, nt))
    prob_grad = nn(to_heads(drive_hi), hot_all) + nn(to_heads(drive_lo), hot_all)
    prob_grad = prob_grad + (
        touch[None] * (contact_head[:HEADS, None, None] * cols)
    ).reshape(HEADS * cw, cols)
    score_grad = prob * (prob_grad - jnp.sum(prob * prob_grad, -1, keepdims=True))
    score_low = score_grad.astype(BF16)
    spread = to_tokens(nt(score_low, hot_all)).astype(BF16)
    table_pair = nn(hot_ri, spread)
    value_grad = per_head(weight_hi, mixed_ri, tn)
    stream_hi, stream_lo = split_two(stream)
    lookup_grad = nn(hot_ir, stream_hi) + nn(hot_ir, stream_lo)
    vectors = jnp.stack([scale_1, scale_2, scale_3, shift_1, shift_2, shift_3])
    return (
        (grad_in_col, grad_out_row, grad_out_col, grad_up, grad_down),
        (table_pair, value_grad, grad_head + lookup_grad, vectors),
        grad_contact,
        mlm_sum,
        bce_sum,
        (unit_t, rstd_t, normed_t, query_t, key_t),
    )


MESH = pl.DeviceIdType.MESH
NZ, NY = 4, 2


def place():
    s, c = lax.axis_index("seq"), lax.axis_index("col")
    z, y, k = s // 4, lax.rem(s // 2, 2), lax.rem(s, 2)
    return z, y, k, c


def device(z, y, k, c):
    return (z * 4 + y * 2 + k, c)


def greet_all():
    z, y, k, c = place()
    me = (z * 4 + y * 2 + k) * 2 + c
    barrier = pltpu.get_barrier_semaphore()

    def signal(step, carry):
        other = lax.rem(me + step, 32)
        pl.semaphore_signal(
            barrier, inc=1, device_id=(other // 2, lax.rem(other, 2)), device_id_type=MESH
        )
        return carry

    lax.fori_loop(1, 32, signal, 0)
    return barrier


def remote(src, dst, send, recv, target):
    return pltpu.make_async_remote_copy(
        src_ref=src, dst_ref=dst, send_sem=send, recv_sem=recv, device_id=target, device_id_type=MESH
    )


ROWS, COLS, WIDE, HERE = 16, 512, 32, 512
PAIRS = 6
SLOTS = 1024
UP_TILE = 384


def iota(shape, dim):
    return lax.broadcasted_iota(jnp.int32, shape, dim)


def one_zero(test):
    return jnp.where(test, 1.0, 0.0)


def total_of(values):
    return jnp.sum(jnp.sum(values, 0, keepdims=True), 1, keepdims=True)


def half_lanes(values, side):
    lane = iota(values.shape, len(values.shape) - 1)
    keep = (lane < 64) if side == 0 else (lane >= 64)
    return jnp.where(keep, values.astype(F32), 0.0).astype(BF16)


def stacked(values):
    return jnp.concatenate([half_lanes(values, 0), half_lanes(values, 1)], 0)


def unstacked(values, count):
    lane = iota((count, 128), 1)
    return jnp.where(lane < 64, values[:count], values[count:])


def swap_blocks(first, second):
    lane = iota(first.shape, 1)
    low = jnp.where(lane < 64, first, pltpu.roll(second, 64, 1))
    high = jnp.where(lane < 64, pltpu.roll(first, 64, 1), second)
    return low, high


def split_heads_to(source, high_ref, low_ref):
    for rp in range(ROWS // 2):
        for hp in range(PAIRS):
            lanes = slice(hp * 128, hp * 128 + 128)
            first = source[rp * 64 : rp * 64 + 32, lanes]
            second = source[rp * 64 + 32 : rp * 64 + 64, lanes]
            for side, block in enumerate(swap_blocks(first, second)):
                top, rest = split_two(block)
                rows = slice((2 * hp + side) * 32, (2 * hp + side) * 32 + 32)
                high_ref[rows, rp * 128 : rp * 128 + 128] = top
                low_ref[rows, rp * 128 : rp * 128 + 128] = rest


def merge_heads(probs, hot_all, high_ref, low_ref):
    for rp in range(ROWS // 2):
        if rp % 2 == 0:
            blocks = nt(probs, hot_all[rp * 128 : rp * 128 + 256, :])
        block = blocks[:, (rp % 2) * 128 : (rp % 2) * 128 + 128]
        for hp in range(PAIRS):
            first = block[hp * 64 : hp * 64 + 32]
            second = block[hp * 64 + 32 : hp * 64 + 64]
            for side, part in enumerate(swap_blocks(first, second)):
                top, rest = split_two(part)
                rows = slice(rp * 64 + side * 32, rp * 64 + side * 32 + 32)
                high_ref[rows, hp * 128 : hp * 128 + 128] = top
                if low_ref is not None:
                    low_ref[rows, hp * 128 : hp * 128 + 128] = rest


def norm_rows(source, gain, bias, unit_ref, rstd_ref, normed_ref):
    def body(at, carry):
        rows = pl.ds(pl.multiple_of(at * 64, 64), 64)
        values = source[rows, :]
        centre = values - jnp.sum(values, -1, keepdims=True) * (1.0 / D)
        rstd = lax.rsqrt(jnp.sum(centre * centre, -1, keepdims=True) * (1.0 / D) + NORM_EPS)
        unit = centre * rstd
        unit_ref[rows, :] = unit
        rstd_ref[rows, :] = jnp.broadcast_to(rstd, (64, 128))
        normed_ref[rows, :] = (unit * gain + bias).astype(BF16)
        return carry

    lax.fori_loop(0, HERE // 64, body, 0)


def transpose_into(source, target):
    def body(at, carry):
        rows = pl.ds(pl.multiple_of(at * 128, 128), 128)
        target[:, rows] = source[rows, :].astype(F32).T.astype(BF16)
        return carry

    lax.fori_loop(0, HERE // 128, body, 0)


def over_tiles(width, tile, body):
    for half in range(2):

        def step(at, carry, half=half):
            body(half, pl.multiple_of(at * tile, tile))
            return carry

        lax.fori_loop(0, width // tile, step, 0)


def column_mask():
    rows, lanes = iota((256, 128), 0), iota((256, 128), 1)
    return ((rows & 127) >> 4) == (lanes >> 4)


class Saved(typing.NamedTuple):
    stream: typing.Any
    branch: typing.Any
    unit_1: typing.Any
    unit_2: typing.Any
    rstd_1: typing.Any
    rstd_2: typing.Any
    row_mixed_t: typing.Any
    col_normed_t: typing.Any
    col_mixed_t: typing.Any
    feed_normed_t: typing.Any
    col_proj: typing.Any
    col_prob: typing.Any
    active: typing.Any
    slope: typing.Any
    grad_head: typing.Any
    hot_all: typing.Any
    hot_ri: typing.Any
    hot_ir: typing.Any
    prob: typing.Any
    weight_hi: typing.Any
    value_two: typing.Any
    touch: typing.Any
    table: typing.Any
    norms: typing.Any
    proj_t: typing.Any
    extras: typing.Any
    moved: typing.Any


AT = Saved(*range(len(Saved._fields)))
SAVED = Saved(
    stream=((HERE, D), F32),
    branch=((HERE, D), BF16),
    unit_1=((HERE, D), F32),
    unit_2=((HERE, D), F32),
    rstd_1=((HERE, 128), F32),
    rstd_2=((HERE, 128), F32),
    row_mixed_t=((D, HERE), BF16),
    col_normed_t=((D, HERE), BF16),
    col_mixed_t=((D, HERE), BF16),
    feed_normed_t=((D, HERE), BF16),
    col_proj=((HERE, 3 * D), BF16),
    col_prob=((4 * PAIRS, 256, 128), F32),
    active=((HERE, FF), BF16),
    slope=((HERE, FF), BF16),
    grad_head=((VP, D), F32),
    hot_all=((ROWS * VP, COLS), BF16),
    hot_ri=((VP, HERE), BF16),
    hot_ir=((VP, HERE), BF16),
    prob=((HEADS * WIDE, COLS), F32),
    weight_hi=((HERE, D), BF16),
    value_two=((PAIRS, 128, 128), BF16),
    touch=((WIDE, COLS), F32),
    table=((VP, D), F32),
    norms=((8, D), F32),
    proj_t=((VP, 3 * D), BF16),
    extras=((8, 128), F32),
    moved=((8, D), F32),
)


class Forward(typing.NamedTuple):
    ids: typing.Any
    targets: typing.Any
    slots: typing.Any
    normed: typing.Any
    mixed: typing.Any
    normed_2: typing.Any
    mixed_2: typing.Any
    second_hot: typing.Any
    weight_lo: typing.Any
    left_hi: typing.Any
    left_lo: typing.Any
    lookup: typing.Any
    prob_low: typing.Any
    unit: typing.Any
    rstd: typing.Any


FORWARD = Forward(
    ids=((ROWS, COLS), jnp.int32),
    targets=((ROWS, 128), jnp.int32),
    slots=((8, SLOTS), jnp.int32),
    normed=((HERE, D), BF16),
    mixed=((HERE, D), BF16),
    normed_2=((HERE, D), BF16),
    mixed_2=((HERE, D), BF16),
    second_hot=((COLS, SLOTS), BF16),
    weight_lo=((HERE, D), BF16),
    left_hi=((HEADS * WIDE, ROWS * VP), BF16),
    left_lo=((HEADS * WIDE, ROWS * VP), BF16),
    lookup=((HERE, D), F32),
    prob_low=((HEADS * WIDE, COLS), BF16),
    unit=((HERE, D), F32),
    rstd=((HERE, 128), F32),
)


def position():
    z, y, k, c = place()
    me = (z * 4 + y * 2 + k) * 2 + c
    return z // 2, lax.rem(me, 16)


def read_tokens(small, f):
    alignment, block = position()
    side, part = block // 8, lax.rem(block // 4, 2)
    for r in range(ROWS):
        for cc in range(2):
            for q in range(2):
                lanes = slice(cc * 256 + q * 128, cc * 256 + q * 128 + 128)
                f.ids[r : r + 1, lanes] = small[r * 2 + cc, pl.ds(2 * alignment + q, 1), :]
        f.targets[r : r + 1, :] = small[r * 2 + side, pl.ds(4 + 2 * alignment + part, 1), :]
    lane = iota((1, 128), 1)
    for number in range(SLOTS // 128):
        for which in range(3):
            row = pl.ds(8 + 3 * alignment + which, 1)
            first = small[number * 4 + side, row, :]
            second = pltpu.roll(small[number * 4 + 2 + side, row, :], 64, 1)
            f.slots[which : which + 1, number * 128 : number * 128 + 128] = jnp.where(
                lane < 64, first, second
            )


def local_hot(values, shift):
    values = pltpu.roll(values, shift, 1)
    turned = [values] + [pltpu.roll(values, 32 * n, 1) for n in (1, 2, 3)]
    lane = iota((1, 128), 1)
    tiles = []
    for tile in range(4):
        row = turned[3][4 * tile + 3 : 4 * tile + 4]
        for n in (2, 1, 0):
            row = jnp.where(lane < 32 * n + 32, turned[n][4 * tile + n : 4 * tile + n + 1], row)
        tiles.append(row)
    row = jnp.concatenate(tiles, 1)
    return one_zero(row == iota((VP, HERE), 0)).astype(BF16)


def contact_part(contact_head, f, s, pair_count):
    _, block = position()
    base = block * WIDE
    head_sum = jnp.zeros((WIDE, COLS), F32)
    for h in range(HEADS):
        head_sum = head_sum + contact_head[h] * f.prob_low[h * 32 : h * 32 + 32, :].astype(F32)
    top, rest = split_two(head_sum)
    last = (head_sum - top.astype(F32) - rest.astype(F32)).astype(BF16)
    parts = jnp.concatenate([top, rest, last], 0)
    touch = jnp.zeros((WIDE, COLS), F32)
    bce = jnp.zeros((1, 1), F32)
    coef_sum = jnp.zeros((1, 1), F32)
    for number in range(SLOTS // 512):
        lanes = slice(number * 512, number * 512 + 512)
        first, label = (f.slots[n : n + 1, lanes] for n in (0, 2))
        second_hot = f.second_hot[:, lanes]
        picked = nn(parts, second_hot)
        picked = picked[:32] + picked[32:64] + picked[64:]
        first_hot = one_zero((first - base) == iota((WIDE, 512), 0))
        logit = jnp.sum(picked * first_hot, 0, keepdims=True) * COLS + contact_head[HEADS]
        owned = jnp.sum(first_hot, 0, keepdims=True) > 0.5
        valid = (label >= 0) & owned
        positive = one_zero(label == 1)
        small = jnp.exp(-jnp.abs(logit))
        soft = jnp.maximum(logit, 0.0) + jnp.log(1.0 + small)
        bce = bce + total_of(jnp.where(valid, soft - positive * logit, 0.0))
        sigmoid = jnp.where(logit >= 0.0, 1.0, small) / (1.0 + small)
        coef = jnp.where(valid, sigmoid - positive, 0.0) / pair_count
        coef_sum = coef_sum + total_of(coef)
        coef_top, coef_rest = split_two(first_hot * coef)
        touch = touch + nt(coef_top, second_hot) + nt(coef_rest, second_hot)
    s.touch[...] = touch
    column = iota((1, 128), 1)
    row = jnp.where(column == HEADS, coef_sum, 0.0)
    for h in range(HEADS):
        part = total_of(touch * f.prob_low[h * 32 : h * 32 + 32, :].astype(F32)) * COLS
        row = row + jnp.where(column == h, part, 0.0)
    return row, bce


def feature_order():
    shape = (384, 384)
    spot = iota(shape, 0)
    block = (spot * 2731) >> 16
    swapped = (block & 28) | ((block & 1) << 1) | ((block >> 1) & 1)
    return one_zero(spot + (swapped - block) * 24 == iota(shape, 1)).astype(BF16)


def forward_body(small, contact_head, weights, s, f, cells, projected, hook, emit):
    out_row, in_col, out_col = weights[:3]
    up_parts, down_parts = weights[3:5], weights[5:7]
    hook()
    features = cells()
    ahead = (
        ((iota((HERE, HERE), 0) >> 4) == (iota((HERE, HERE), 1) & 31))
        & ((iota((HERE, HERE), 0) & 15) == (iota((HERE, HERE), 1) >> 5))
    )
    ahead = one_zero(ahead).astype(BF16)
    read_tokens(small, f)
    _, block = position()
    shift = lax.rem(128 - lax.rem(block, 4) * 32, 128)
    window = pl.ds(pl.multiple_of((block // 4) * 128, 128), 128)
    hot_ri = local_hot(f.ids[:, window], shift)
    goal_ri = local_hot(f.targets[...], shift)
    s.hot_ri[...] = hot_ri
    for number in range(SLOTS // 512):
        lanes = slice(number * 512, number * 512 + 512)
        f.second_hot[:, lanes] = one_zero(f.slots[1:2, lanes] == iota((COLS, 512), 0)).astype(BF16)
    for r in range(ROWS):
        row = f.ids[r : r + 1, :]
        s.hot_all[r * VP : r * VP + VP, :] = one_zero(row == iota((VP, COLS), 0)).astype(BF16)
    shape = (HERE, HERE)
    back = (
        ((iota(shape, 1) >> 4) == (iota(shape, 0) & 31))
        & ((iota(shape, 1) & 15) == (iota(shape, 0) >> 5))
    )
    back = one_zero(back).astype(BF16)
    hot_ir = nn(hot_ri, back).astype(BF16)
    s.hot_ir[...] = hot_ir
    goal = nn(goal_ri, back)
    entries = jnp.zeros((4, 128), F32)
    labelled = jnp.zeros((1, 128), F32)
    for d in range(32):
        entries = entries + one_zero(small[d, 0:4, :] == MASK_ID)
        labelled = labelled + one_zero(small[d, 10:11, :] >= 0) + one_zero(small[d, 13:14, :] >= 0)
    entries, labelled = total_of(entries), total_of(labelled)

    hook()
    features = features[...].T
    table = features[:VP]
    norms = features[VP : VP + 8]
    s.table[...] = table
    s.norms[...] = norms
    table_low = table.astype(BF16)

    def vector(number):
        return norms[number : number + 1, :]

    hook()
    projected(s.proj_t)
    pair_parts = []
    for hp in range(PAIRS):
        lanes = slice(hp * 128, hp * 128 + 128)
        key = s.proj_t[:, D + hp * 128 : D + hp * 128 + 128]
        value = s.proj_t[:, 2 * D + hp * 128 : 2 * D + hp * 128 + 128]
        s.value_two[hp] = stacked(value)
        pair_parts.append(nt(s.proj_t[:, lanes], stacked(key)))
    pair_hi, pair_lo = split_two(jnp.concatenate(pair_parts, 1))
    hook()
    f.lookup[...] = tn(hot_ri, pair_hi) + tn(hot_ri, pair_lo)
    split_heads_to(f.lookup, f.left_hi, f.left_lo)
    hook()
    hot_all = s.hot_all[...]
    score = (nn(f.left_hi[...], hot_all) + nn(f.left_lo[...], hot_all)) * (HD * ROWS) ** (-0.5)
    score = jnp.exp(score - jnp.max(score, -1, keepdims=True))
    prob = score / jnp.sum(score, -1, keepdims=True)
    s.prob[...] = prob
    f.prob_low[...] = prob.astype(BF16)
    hook()
    merge_heads(f.prob_low[...], s.hot_all, s.weight_hi, f.weight_lo)
    hook()
    for hp in range(PAIRS):
        lanes = slice(hp * 128, hp * 128 + 128)
        value = s.value_two[hp]
        both = jnp.concatenate([s.weight_hi[:, lanes], f.weight_lo[:, lanes]], 1)
        f.mixed[:, lanes] = nn(both, jnp.concatenate([value, value], 0)).astype(BF16)
    f.mixed[...] = nn(ahead, f.mixed[...]).astype(BF16)
    s.stream[...] = tn(hot_ir, table_low)
    emit(AT.hot_all, AT.hot_ri, AT.hot_ir, AT.table, AT.norms, AT.proj_t, AT.value_two, AT.prob, AT.weight_hi)
    hook()
    for half in range(2):
        lanes = slice(half * 384, half * 384 + 384)
        s.stream[:, lanes] += nn(f.mixed[...], out_row[half])
    norm_rows(s.stream, vector(1), vector(5), s.unit_1, s.rstd_1, f.normed)
    emit(AT.unit_1, AT.rstd_1)

    def project(half, at):
        s.col_proj[:, half * 1152 + at : half * 1152 + at + 384] = nn(
            f.normed[...], in_col[half, :, at : at + 384]
        ).astype(BF16)

    for third in range(3):
        hook()
        for half in range(2):
            project(half, third * 384)
    emit(AT.col_proj)

    def attend(at, carry):
        rows = pl.ds(pl.multiple_of((at // PAIRS) * 128, 128), 128)
        lane = lax.rem(at, PAIRS) * 128

        def lanes(part):
            return pl.ds(pl.multiple_of(part * D + lane, 128), 128)

        query = stacked(s.col_proj[rows, lanes(0)])
        score = nt(query, s.col_proj[rows, lanes(1)]) * HD ** (-0.5)
        score = jnp.where(column_mask(), score, -1e30)
        score = jnp.exp(score - jnp.max(score, -1, keepdims=True))
        prob = score / jnp.sum(score, -1, keepdims=True)
        s.col_prob[at] = prob
        mixed = nn(prob.astype(BF16), s.col_proj[rows, lanes(2)])
        f.mixed_2[rows, lanes(0)] = unstacked(mixed, 128).astype(BF16)
        return carry

    for part in range(4):
        hook()
        lax.fori_loop(part * PAIRS, part * PAIRS + PAIRS, attend, 0, unroll=3)
    hook()
    emit(AT.col_prob)
    for half in range(2):
        lanes = slice(half * 384, half * 384 + 384)
        s.stream[:, lanes] += nn(f.mixed_2[...], out_col[half])
    norm_rows(s.stream, vector(2), vector(6), s.unit_2, s.rstd_2, f.normed_2)
    emit(AT.unit_2, AT.rstd_2)
    hook()
    contact_row, bce = contact_part(contact_head, f, s, labelled)
    emit(AT.touch)
    for part in range(2):

        def widen(half, at, part=part):
            lanes = slice(part * 1536 + half * 768 + at, part * 1536 + half * 768 + at + UP_TILE)
            up = nn(f.normed_2[...], up_parts[part][half, :, at : at + UP_TILE])
            active, slope = gelu_parts(up)
            s.active[:, lanes] = active.astype(BF16)
            s.slope[:, lanes] = slope.astype(BF16)

        for half in range(2):
            hook()
            for at in range(0, 768, UP_TILE):
                widen(half, at)
        hook()
        if part == 0:
            transpose_into(f.mixed, s.row_mixed_t)
            transpose_into(f.normed, s.col_normed_t)
            emit(AT.row_mixed_t, AT.col_normed_t)
        else:
            transpose_into(f.mixed_2, s.col_mixed_t)
            emit(AT.col_mixed_t)

    emit(AT.active, AT.slope)
    for part, at, size in ((0, 0, 768), (1, 0, 384), (1, 384, 384)):
        hook()
        added = []
        for half in range(2):
            start = part * 1536 + half * 768 + at
            matrix = down_parts[part][half, :, at : at + size]
            added.append(nt(s.active[:, start : start + size], matrix))
        s.stream[...] += added[0] + added[1]
        if part == 0:
            hook()
            transpose_into(f.normed_2, s.feed_normed_t)
            emit(AT.feed_normed_t)
    hook()
    norm_rows(s.stream, vector(3), vector(7), f.unit, f.rstd, f.normed)
    logits = nt(table_low, f.normed[...]) * D ** (-0.5)
    vocab = iota((VP, HERE), 0)
    logits = jnp.where(vocab < VOCAB, logits, -1e30)
    shifted = logits - jnp.max(logits, 0, keepdims=True)
    log_probs = shifted - jnp.log(jnp.sum(jnp.exp(shifted), 0, keepdims=True))
    keep = hot_ir[MASK_ID : MASK_ID + 1].astype(F32) > 0.5
    mlm = -total_of(jnp.where(keep & (goal > 0.5), log_probs, 0.0))
    logit_grad = jnp.where(keep, jnp.exp(log_probs) - goal, 0.0) / entries
    logit_low = (logit_grad * D ** (-0.5)).astype(BF16)
    s.grad_head[...] = nn(logit_low, f.normed[...])
    hook()
    f.lookup[...] = tn(logit_low, table_low)
    scale_3, shift_3 = back_rows(f.unit, f.rstd, vector(3), f.lookup, s.stream, s.branch, True)
    emit(AT.stream, AT.branch)
    line = iota((8, D), 0)
    s.moved[...] = jnp.where(line == 0, scale_3, jnp.where(line == 1, shift_3, 0.0))
    column = iota((1, 128), 1)
    row = contact_row + jnp.where(column == HEADS + 1, mlm, 0.0) + jnp.where(column == HEADS + 2, bce, 0.0)
    counted = jnp.where(column == 0, entries, 0.0) + jnp.where(column == 1, labelled, 0.0)
    line = iota((8, 128), 0)
    s.extras[...] = jnp.where(line == 0, row, jnp.where(line == 1, counted, 0.0))
    emit(AT.grad_head, AT.extras, AT.moved)
    hook()


def back_rows(unit_ref, rstd_ref, gain, upstream_ref, stream_ref, low_ref, first):
    def body(at, carry):
        scale, move = carry
        rows = pl.ds(pl.multiple_of(at * 64, 64), 64)
        upstream = upstream_ref[rows, :]
        unit = unit_ref[rows, :]
        inner = upstream * gain
        mean = jnp.sum(inner, -1, keepdims=True) * (1.0 / D)
        along = jnp.sum(inner * unit, -1, keepdims=True) * (1.0 / D)
        grad = rstd_ref[rows, 0:1] * (inner - mean - unit * along)
        if not first:
            grad = grad + stream_ref[rows, :]
        stream_ref[rows, :] = grad
        low_ref[rows, :] = grad.astype(BF16)
        touched = upstream * unit
        for n in range(8):
            scale = scale + touched[n * 8 : n * 8 + 8]
            move = move + upstream[n * 8 : n * 8 + 8]
        return scale, move

    zero = jnp.zeros((8, D), F32)
    scale, move = lax.fori_loop(0, HERE // 64, body, (zero, zero))
    return jnp.sum(scale, 0, keepdims=True), jnp.sum(move, 0, keepdims=True)


MATRICES = (128, 384, 1152, 384, 768, 768, 768, 768)
UNITS = (
    (0, 0, 128, True),
    (1, 0, 384, False),
    (2, 0, 384, True),
    (2, 384, 384, True),
    (2, 768, 384, True),
    (3, 0, 384, False),
    (4, 0, 768, True),
    (5, 0, 768, True),
    (6, 0, 768, True),
    (7, 0, 384, True),
    (7, 384, 384, True),
)
Z_LAST = {9: 1, 10: 2}
FORWARD_ORDER = (
    ((0, 0), (0, 2), (0, 11), (1, 0), (0, 1), (0, 9), (0, 10), (1, 11), (2, 0), (0, 3), (1, 2), (0, 4), (2, 11), (3, 0), (1, 10), (1, 9), (1, 1), (4, 0),),
    ((2, 2), (0, 5), (2, 1),),
    ((3, 11), (1, 3), (0, 6), (3, 2), (4, 11), (1, 4),),
    ((3, 1), (4, 2), (1, 5), (0, 7),),
    ((4, 1), (2, 3), (2, 4),),
    ((1, 6), (0, 8),),
    (),
    ((3, 3),),
    ((3, 4), (2, 5), (4, 3), (2, 9), (1, 7), (4, 4),),
    (),
    (),
    (),
    ((3, 5), (2, 6),),
    (),
    ((4, 5), (2, 7), (2, 10),),
    ((1, 8),),
    ((3, 6),),
    ((3, 9), (3, 7), (4, 6),),
    (),
    ((2, 8), (4, 9),),
    ((4, 7),),
    (),
    (),
    ((3, 8), (3, 10), (4, 8),),
    ((4, 10),),
    (),
    (),
    (),
    (),
    (),
)


def spot(paired, cc, zz, yy, k):
    return (k, zz, yy, cc) if paired else (cc, zz, yy, k)


def forward_kernel(*refs):
    count, parts = len(UNITS), len(MATRICES)
    raw = refs[:11]
    contact_head = refs[11]
    at = 12
    far = (None, *refs[at : at + parts - 1])
    saved_far = refs[at + parts - 1 : at + parts - 1 + len(SAVED)]
    at += parts - 1 + len(SAVED)
    outs = refs[at : at + parts]
    at += parts
    outgoing = refs[at : at + count]
    incoming = refs[at + count : at + 2 * count]
    piece = refs[at + 2 * count : at + 3 * count]
    at += 3 * count
    saved = Saved(*refs[at : at + len(SAVED)])
    at += len(SAVED)
    scratch = Forward(*refs[at : at + len(FORWARD)])
    at += len(FORWARD)
    near = refs[at : at + 11]
    at += 11
    small, small_out, corner, features, stat, stat_got, part, part_got, part_line, proj, room = refs[at : at + 11]
    small_send, small_recv, send, recv, local, out_sem, raw_sem, twin_send, twin_recv = refs[at + 11 :]
    tokens, targets, masked, pairs, labels, table, norms, in_w, out_w, up_w, down_w = near
    z, y, k, c = place()
    me = (z * 4 + y * 2 + k) * 2 + c
    barrier = greet_all()
    raw_copies = [pltpu.make_async_copy(a, b, raw_sem.at[n]) for n, (a, b) in enumerate(zip(raw, near))]
    for item in raw_copies:
        item.start()
    for item in raw_copies[:7]:
        item.wait()
    small[...] = jnp.full(small.shape, -1, jnp.int32)
    for micro in range(2):
        for half in range(2):
            lanes = slice(half * 128, half * 128 + 128)
            row = 2 * micro + half
            small[row : row + 1, :] = jnp.where(
                masked[micro, :, lanes] > 0, MASK_ID, tokens[micro, :, lanes]
            )
            small[4 + row : 5 + row, :] = targets[micro, :, lanes]
        row = 8 + 3 * micro
        for which in range(2):
            small[row + which : row + which + 1, 0:64] = pairs[micro, which : which + 1, :]
        small[row + 2 : row + 3, 0:64] = labels[micro : micro + 1, :]
    corner[...] = jnp.zeros(corner.shape, F32)
    corner[0:8, 0:24] = norms[...]
    vectors = pltpu.roll(corner[...].T[:24], 64, 1)
    corner[0:8, 0:24] = jnp.zeros((8, 24), F32)
    corner[0:24, 0:VOCAB] = table[...]
    mine_rows = (corner[0:24, :] + vectors).astype(BF16).astype(F32)
    table_rows = jnp.where(iota((24, 128), 1) < VP, mine_rows, 0.0)
    gain, bias = mine_rows[:, 64:65], mine_rows[:, 68:69]
    piece[0][0:16, :] = small[...].astype(F32)
    piece[0][16:40, :] = mine_rows
    mean = jnp.sum(table_rows, 0, keepdims=True) * (1.0 / 24)
    centre = table_rows - mean
    spread = jnp.sum(centre * centre, 0, keepdims=True)
    line = iota((8, 128), 0)
    stat[...] = jnp.where(line == 0, mean, jnp.where(line == 1, spread, 0.0))
    def master(u, side):
        matrix, start, n, _ = UNITS[u]
        width = MATRICES[matrix]
        if matrix == 2:
            return in_w[1, :, side * 1152 + start : side * 1152 + start + n]
        if matrix in (1, 3):
            rows = out_w[matrix // 2, :, side * 384 : side * 384 + 384].astype(BF16)
            return nn(rows, order)
        begin = (matrix % 2) * 1536 + side * width + start
        return (up_w if matrix < 6 else down_w)[:, begin : begin + n]

    def mine(u):
        return k if UNITS[u][3] else c

    def set_out(u):
        other = jnp.where(mine(u) == 0, master(u, 1), master(u, 0))
        other = jnp.concatenate([other, jnp.zeros((8, UNITS[u][2]), F32)], 0)
        outgoing[u][...] = other.astype(BF16)

    pl.semaphore_wait(barrier, 31)

    def stat_copy(step):
        other = lax.rem(me + step, 32)
        return remote(
            stat, stat_got.at[me], small_send.at[0, step], small_recv.at[0, step], (other // 2, lax.rem(other, 2))
        )

    chip = (z * 2 + y) * 2 + c

    def chip_copy(phase, step):
        other = lax.rem(chip + step, 16)
        target = device(other // 4, lax.rem(other // 2, 2), k, lax.rem(other, 2))
        if phase == 1:
            src, dst = part.at[k, other], part_line.at[chip]
        else:
            src, dst = proj.at[k, chip], proj.at[k, chip]
        return remote(src, dst, small_send.at[phase, step], small_recv.at[phase, step], target)

    def each(last, action):
        def body(step, carry):
            action(step)
            return carry

        lax.fori_loop(1, last, body, 0)

    each(32, lambda step: stat_copy(step).start())

    across, beside, twin = device(z, y, k, 1 - c), device(z, 1 - y, k, c), device(z, y, 1 - k, c)

    def block(u, cc, zz, yy):
        matrix, start, n, paired = UNITS[u]
        where = spot(paired, cc, zz, yy, k)
        if n == MATRICES[matrix]:
            return outs[matrix].at[where]
        return outs[matrix].at[(*where, slice(None), pl.ds(start, n))]

    def copy(u, at, src, dst, target):
        return remote(src, dst, send.at[u, at], recv.at[u, at], target)

    def pair_copy(u):
        return copy(u, 0, outgoing[u], incoming[u], twin if UNITS[u][3] else across)

    def own_copy(u):
        return pltpu.make_async_copy(piece[u], block(u, c, z, y), local.at[u])

    def line_copy(u, step):
        return copy(u, step, piece[u], block(u, c, z, y), device(lax.rem(z + step, 4), y, k, c))

    def same(u, at, cc, zz, yy, target):
        view = block(u, cc, zz, yy)
        return copy(u, at, view, view, target)

    low, high, every = pl.ds(0, 2), pl.ds(2, 2), slice(None)

    def second(u):
        return [same(u, 4, c, low, y, across), same(u, 5, c, high, y, beside)]

    def third_own(u):
        return [same(u, 6, c, low, y, beside), same(u, 7, c, high, y, across)]

    def third_far(u):
        return [same(u, 8, 1 - c, low, y, beside), same(u, 9, c, high, 1 - y, across)]

    def twin_own(u):
        return [same(u, 10, c, every, y, twin)]

    def twin_second(u):
        return [same(u, 11, 1 - c, low, y, twin), same(u, 12, c, high, 1 - y, twin)]

    def twin_third(u):
        return [
            same(u, 13, c, low, 1 - y, twin),
            same(u, 14, 1 - c, high, y, twin),
            same(u, 15, 1 - c, low, 1 - y, twin),
            same(u, 16, 1 - c, high, 1 - y, twin),
        ]

    own_copy(0).start()
    for item in raw_copies[7:]:
        item.wait()
    order = feature_order()
    for u in range(1, count):
        set_out(u)
        pair_copy(u).start()

    def part_twin():
        return remote(part.at[1 - k], part_got, twin_send.at[0], twin_recv.at[0], twin)

    def proj_twin():
        return remote(proj.at[k], proj.at[k], twin_send.at[1], twin_recv.at[1], twin)

    def project_part():
        stat_got[me] = stat[...]
        each(32, lambda step: stat_copy(step).wait())
        means = jnp.zeros((1, 128), F32)
        spreads = jnp.zeros((1, 128), F32)
        for d in range(32):
            means = means + stat_got[d, 0:1, :]
            spreads = spreads + stat_got[d, 1:2, :]
        means = means * (1.0 / 32)
        for d in range(32):
            away = stat_got[d, 0:1, :] - means
            spreads = spreads + 24.0 * away * away
        rstd = lax.rsqrt(spreads * (1.0 / D) + NORM_EPS)
        normed = (table_rows - means) * rstd * gain + bias
        normed = jnp.concatenate([normed, jnp.zeros((8, 128), F32)], 0).astype(BF16)
        for block_at in range(6):
            lanes = slice(block_at * 384, block_at * 384 + 384)
            rows = jnp.concatenate([in_w[0, :, lanes], jnp.zeros((8, 384), F32)], 0).astype(BF16)
            product = tn(normed, rows)
            for group in range(5):
                number = group * 6 + block_at
                part[number // 16, number % 16] = product[group * 8 : group * 8 + 8]
        for number in (30, 31):
            part[number // 16, number % 16] = jnp.zeros((8, 384), F32)
        part_twin().start()

    def project_chip():
        part_twin().wait_recv()
        part[k] = part[k] + part_got[...]
        each(16, lambda step: chip_copy(1, step).start())

    def project_line():
        part_line[chip] = part[k, chip]
        each(16, lambda step: chip_copy(1, step).wait_recv())
        proj[k, chip] = lax.fori_loop(1, 16, lambda at, held: held + part_line[at], part_line[0])
        each(16, lambda step: chip_copy(2, step).start())

    def project_twin():
        each(16, lambda step: chip_copy(2, step).wait_recv())
        proj_twin().start()

    def project_end():
        proj_twin().wait_recv()

    projecting = (project_part, project_chip, project_line, project_twin, project_end)

    def cells():
        for d in range(32):
            at = ((d // 2) % 2, d // 8, (d // 4) % 2, d % 2)
            small_out[d] = outs[0][(*at, slice(0, 16))].astype(jnp.int32)
            start = (((at[1] * 2 + at[2]) * 2 + at[3]) * 2 + at[0]) * 24
            features[start : start + 24, :] = outs[0][(*at, slice(16, 40))]
        return features

    def projected(target):
        room[40:64, :] = jnp.zeros((24, 3 * D), F32)
        for number in range(30):
            rows, lanes = (number // 6) * 8, (number % 6) * 384
            room[rows : rows + 8, lanes : lanes + 384] = proj[number // 16, number % 16]
        target[...] = room[...].astype(BF16)

    def to_across(u):
        return copy(u, 4, piece[u], block(u, c, z, y), across)

    def to_beside(u):
        return copy(u, 5, piece[u], block(u, c, z, y), beside)

    def to_corner(u):
        if Z_LAST[u] == 1:
            return same(u, 6, 1 - c, z, y, beside)
        return same(u, 6, c, z, 1 - y, across)

    def to_line(u):
        return [
            same(u, step, every, z, every, device(lax.rem(z + step, 4), y, k, c)) for step in (1, 3, 2)
        ]

    def to_twin(u):
        return [same(u, 7, every, z, every, twin)]

    def rest_to_twin(u):
        return [same(u, 7 + step, every, lax.rem(z + 4 - step, 4), every, twin) for step in (1, 3, 2)]

    def stage_line(u):
        if u == 0:
            for step in (1, 3, 2):
                line_copy(u, step).start()
            return
        pair_copy(u).wait_recv()
        side = mine(u)
        own = jnp.where(side == 0, master(u, 0), master(u, 1))
        theirs = incoming[u][...].astype(F32)[:24]
        top = jnp.where(side == 0, own, theirs)
        bottom = jnp.where(side == 0, theirs, own)
        piece[u][...] = jnp.concatenate([top, bottom], 0).astype(BF16)
        own_copy(u).start()
        if u in Z_LAST:
            to_across(u).start()
            to_beside(u).start()
            return
        for step in (1, 3, 2):
            line_copy(u, step).start()

    def stage_second(u):
        own_copy(u).wait()
        if u in Z_LAST:
            to_across(u).wait_recv()
            to_beside(u).wait_recv()
            to_corner(u).start()
            return
        for step in (1, 3, 2):
            line_copy(u, step).wait_recv()
        for item in second(u) + third_own(u) + twin_own(u):
            item.start()

    def stage_third(u):
        if u in Z_LAST:
            to_corner(u).wait_recv()
            for item in to_line(u) + to_twin(u):
                item.start()
            return
        for item in second(u):
            item.wait_recv()
        for item in third_far(u) + twin_second(u):
            item.start()

    def stage_twin(u):
        if u in Z_LAST:
            for item in to_line(u):
                item.wait_recv()
            for item in rest_to_twin(u):
                item.start()
            return
        for item in third_own(u) + third_far(u):
            item.wait_recv()
        for item in twin_third(u):
            item.start()

    def far_copy(matrix):
        return pltpu.make_async_copy(outs[matrix], far[matrix], local.at[count + matrix])

    def stage_end(u):
        if u in Z_LAST:
            for item in to_twin(u) + rest_to_twin(u):
                item.wait_recv()
            sent = [to_across(u), to_beside(u), to_corner(u)] + to_line(u) + to_twin(u)
        else:
            for item in twin_own(u) + twin_second(u) + twin_third(u):
                item.wait_recv()
            sent = [line_copy(u, step) for step in (1, 2, 3)]
            sent += second(u) + third_own(u) + third_far(u) + twin_own(u) + twin_second(u)
        for item in sent if u == 0 else [pair_copy(u)] + sent:
            item.wait_send()
        if u == 0:
            return
        if u + 1 == count or UNITS[u + 1][0] != UNITS[u][0]:
            far_copy(UNITS[u][0]).start()

    stages = (stage_line, stage_second, stage_third, stage_twin, stage_end)
    pending = list(FORWARD_ORDER)

    def hook():
        for stage, u in pending.pop(0):
            if u == count:
                projecting[stage]()
            else:
                stages[stage](u)

    def out_copy(at):
        return pltpu.make_async_copy(saved[at], saved_far[at], out_sem.at[at])

    def emit(*numbers):
        for number in numbers:
            out_copy(number).start()

    views = [w.reshape(2, D, n) for w, n in zip(outs[1:], MATRICES[1:])]
    forward_body(small_out, contact_head, views, saved, scratch, cells, projected, hook, emit)
    part_twin().wait_send()
    proj_twin().wait_send()
    for phase in (1, 2):
        each(16, lambda step, phase=phase: chip_copy(phase, step).wait_send())
    assert not pending
    for u in range(count):
        for item in rest_to_twin(u) if u in Z_LAST else twin_third(u):
            item.wait_send()
    for matrix in range(1, parts):
        far_copy(matrix).wait()
    for at in range(len(SAVED)):
        out_copy(at).wait()


def forward_call(raw, contact_head):
    count, parts = len(UNITS), len(MATRICES)
    anywhere = pl.BlockSpec(memory_space=pl.ANY)
    shapes = [(2, NZ, NY, 2, 48, n) for n in MATRICES[1:]]
    widths = [n for _, _, n, _ in UNITS]
    outs = pl.pallas_call(
        forward_kernel,
        out_shape=[jax.ShapeDtypeStruct(shape, BF16) for shape in shapes]
        + [jax.ShapeDtypeStruct(*item) for item in SAVED],
        in_specs=[anywhere] * 11 + [pl.BlockSpec(memory_space=pltpu.SMEM)],
        out_specs=[anywhere] * (parts - 1 + len(SAVED)),
        scratch_shapes=[pltpu.VMEM((2, NZ, NY, 2, 40, 128), F32)]
        + [pltpu.VMEM(shape, BF16) for shape in shapes]
        + [pltpu.VMEM((32, n), BF16) for n in widths] * 2
        + [pltpu.VMEM((40, 128), F32)]
        + [pltpu.VMEM((48, n), BF16) for n in widths[1:]]
        + [pltpu.VMEM(*item) for item in SAVED]
        + [pltpu.VMEM(*item) for item in FORWARD]
        + [pltpu.VMEM(item.shape, item.dtype) for item in raw]
        + [
            pltpu.VMEM((16, 128), jnp.int32),
            pltpu.VMEM((32, 16, 128), jnp.int32),
            pltpu.VMEM((128, 128), F32),
            pltpu.VMEM((D, 128), F32),
            pltpu.VMEM((8, 128), F32),
            pltpu.VMEM((32, 8, 128), F32),
            pltpu.VMEM((2, 16, 8, 384), F32),
            pltpu.VMEM((16, 8, 384), F32),
            pltpu.VMEM((16, 8, 384), F32),
            pltpu.VMEM((2, 16, 8, 384), F32),
            pltpu.VMEM((VP, 3 * D), F32),
            pltpu.SemaphoreType.DMA((3, 32)),
            pltpu.SemaphoreType.DMA((3, 32)),
            pltpu.SemaphoreType.DMA((count, 17)),
            pltpu.SemaphoreType.DMA((count, 17)),
            pltpu.SemaphoreType.DMA((count + parts,)),
            pltpu.SemaphoreType.DMA((len(SAVED),)),
            pltpu.SemaphoreType.DMA((len(raw),)),
            pltpu.SemaphoreType.DMA((2,)),
            pltpu.SemaphoreType.DMA((2,)),
        ],
        compiler_params=pltpu.CompilerParams(
            collective_id=0, has_side_effects=True, vmem_limit_bytes=62 * 2**20
        ),
    )(*raw, contact_head)
    return outs[: parts - 1], Saved(*outs[parts - 1 :])


def summed_rows(sums, group):
    return jnp.concatenate([sums[3 * group + third] for third in range(3)], 1).astype(F32)


def table_finish(sums, room, table_ref, norms_ref, proj_t, in_row, g_in, g_norm, send_stat):
    z, y, k, c = place()
    me = ((z * 2 + y) * 2 + c) * 2 + k
    room[0:128, :] = jnp.zeros((128, D), F32)
    for number in range(2):
        room[4 + 16 * number : 20 + 16 * number, :] = summed_rows(sums, number)
        room[68 + 16 * number : 84 + 16 * number, :] = summed_rows(sums, 2 + number)
    pair = room[0:64, :]
    value_grad = room[64:128, :]
    vectors = summed_rows(sums, 6)
    vectors = vectors[:8] + vectors[8:]
    line = iota((8, D), 0)
    table_grad = jnp.concatenate(
        [
            summed_rows(sums, 4),
            summed_rows(sums, 5),
            jnp.where(line == 0, vectors[7:8], 0.0),
            jnp.zeros((24, D), F32),
        ],
        0,
    )
    pair_hi, pair_lo = split_two(pair)
    scale = (HD * ROWS) ** (-0.5)
    query_grad, key_grad = [], []
    for hp in range(PAIRS):
        lanes = slice(hp * 128, hp * 128 + 128)
        query = proj_t[:, lanes]
        key = stacked(proj_t[:, D + hp * 128 : D + hp * 128 + 128])
        high, low = pair_hi[:, lanes], pair_lo[:, lanes]
        query_grad.append((nn(high, key) + nn(low, key)) * scale)
        key_grad.append(unstacked(tn(high, query) + tn(low, query), VP) * scale)
    proj_hi, proj_lo = split_two(jnp.concatenate(query_grad + key_grad + [value_grad], 1))
    shard = D // 32
    pick = one_zero(iota((shard, D), 1) == iota((shard, D), 0) + me * shard).astype(BF16)
    weight = in_row[...].astype(BF16)
    back_t = nt(weight, proj_hi) + nt(weight, proj_lo)
    back = nt(proj_hi, weight) + nt(proj_lo, weight)
    table = table_ref[...]
    table_low = table.astype(BF16)
    unit, rstd = norm_stats(table)
    mean = jnp.sum(table, -1, keepdims=True) * (1.0 / D)
    same = iota((VP, VP), 0) == iota((VP, VP), 1)

    def as_row(column):
        return jnp.sum(jnp.where(same, column, 0.0), 0, keepdims=True)

    rstd_row = as_row(rstd)
    unit_t = (nt(pick, table_low) - as_row(mean)) * rstd_row
    unit_mine = (nt(table_low, pick) - mean) * rstd
    norms = jnp.concatenate([norms_ref[...], jnp.zeros((8, D), F32)], 0).astype(BF16)
    inner = back_t * nt(pick, norms)[:, 0:1]

    def three(values):
        top, rest = split_two(values)
        return top, rest, (values - top.astype(F32) - rest.astype(F32)).astype(BF16)

    emb_grad = sum(nt(pick, part) for part in three(table_grad))
    before = emb_grad + rstd_row * inner
    parts = (inner, inner * unit_t, before, before * unit_t, unit_t, unit_t * unit_t, before * before)
    send_stat([jnp.sum(part, 0, keepdims=True) for part in parts])
    scale_0 = jnp.sum(back * unit_mine, 0, keepdims=True)
    shift_0 = jnp.sum(back, 0, keepdims=True)
    line = iota((16, D), 0)
    norm_grad = jnp.zeros((16, D), F32)
    for number, source in ((1, 0), (2, 1), (3, 2), (5, 3), (6, 4), (7, 5)):
        norm_grad = jnp.where(line == number, vectors[source : source + 1], norm_grad)
    normed = (unit * norms_ref[0:1, :] + norms_ref[4:5, :]).astype(BF16)
    mine = nt(pick, normed).astype(BF16)
    in_grad = nn(mine, proj_hi) + nn(mine, proj_lo)
    g_in[...] = in_grad
    own_norm = sum(nt(part, pick) for part in three(norm_grad))[:8]
    line = iota((8, shard), 0)
    own_norm = jnp.where(line == 0, scale_0, jnp.where(line == 4, shift_0, own_norm))
    g_norm[...] = own_norm
    found = total_of(in_grad * in_grad) + total_of(own_norm * own_norm)
    return inner, unit_t, rstd_row, emb_grad, found


PIECES = 21
GRAD_WIDTHS = (768, 768, 768, 768, 384, 1152, 384)
GRAD_UNITS = (
    (0, 0, 384, True),
    (0, 384, 384, True),
    (1, 0, 768, True),
    (2, 0, 768, True),
    (3, 0, 768, True),
    (4, 0, 384, False),
    (5, 0, 384, True),
    (5, 384, 384, True),
    (5, 768, 384, True),
    (6, 0, 384, False),
)
Z_FIRST = {1: 1, 5: 2}
BACKWARD_ORDER = (
    (),
    (),
    (),
    (),
    (),
    (),
    ((0, 0),),
    (),
    ((0, 1),),
    (),
    (),
    ((1, 0),),
    (),
    ((0, 2),),
    ((2, 0),),
    (),
    (),
    ((0, 3),),
    (),
    (),
    ((1, 2), (0, 4), (1, 1),),
    ((0, 5),),
    ((3, 0),),
    ((1, 3), (4, 0),),
    (),
    ((2, 2),),
    (),
    (),
    (),
    (),
    (),
    ((2, 1), (1, 4), (1, 5), (0, 6),),
    ((0, 7), (3, 1),),
    ((2, 3), (0, 8), (4, 1),),
    (),
    ((3, 2), (2, 4), (2, 5), (0, 9),),
    ((4, 2), (1, 6),),
    ((3, 3), (1, 7),),
    ((4, 3),),
    ((3, 5), (1, 8), (3, 4), (1, 9), (4, 4), (2, 6), (2, 7), (5, 0), (4, 5), (3, 6), (2, 8), (4, 6), (2, 9), (3, 7), (4, 7), (6, 0), (3, 8), (3, 9), (4, 8), (4, 9),),
)


class Kept(typing.NamedTuple):
    stream: typing.Any
    norms: typing.Any
    table: typing.Any
    proj_t: typing.Any
    extras: typing.Any
    moved: typing.Any
    grad_head: typing.Any
    touch: typing.Any
    value_two: typing.Any


class Early(typing.NamedTuple):
    slope: typing.Any
    active: typing.Any
    feed_normed_t: typing.Any
    unit_2: typing.Any
    rstd_2: typing.Any
    col_mixed_t: typing.Any
    col_proj: typing.Any
    col_prob: typing.Any
    col_normed_t: typing.Any
    unit_1: typing.Any
    rstd_1: typing.Any


class Late(typing.NamedTuple):
    row_mixed_t: typing.Any
    hot_all: typing.Any
    weight_hi: typing.Any
    prob: typing.Any
    hot_ri: typing.Any
    hot_ir: typing.Any


def pick_items(group, source):
    return [getattr(source, name) for name in group._fields]


def backward_kernel(*refs):
    widths = GRAD_WIDTHS
    count = len(widths)
    contact_head = refs[0]
    far = refs[1 : 1 + count]
    in_row_far = refs[1 + count]
    saved = Saved(*refs[2 + count : 2 + count + len(SAVED)])
    at = 2 + count + len(SAVED)
    outs = refs[at : at + count]
    g_in, g_emb, g_norm, stats = refs[at + count : at + count + 4]
    at += count + 4
    grads = refs[at : at + count]
    kept = Kept(*refs[at + count : at + count + len(Kept._fields)])
    at += count + len(Kept._fields)
    upstream, branch, branch_t, mixed = refs[at : at + 4]
    scratch = refs[at + 4 :]
    units = len(GRAD_UNITS)
    got_0, got_1a, got_1b, got_2a, got_2b, got_3, total, got_4 = (
        scratch[i * units : (i + 1) * units] for i in range(8)
    )
    table, table_out, table_got, square, square_got, stat, stat_got, late_rows = scratch[8 * units : 8 * units + 8]
    table_send, table_recv, send, recv, local = scratch[8 * units + 8 :]
    z, y, k, c = place()
    me = (z * 4 + y * 2 + k) * 2 + c
    across, beside, twin = device(z, y, k, 1 - c), device(z, 1 - y, k, c), device(z, y, 1 - k, c)
    barrier = greet_all()
    stream = kept.stream
    square[...] = jnp.zeros(square.shape, F32)

    copies = {}

    def load(number, source, target):
        copies[number] = pltpu.make_async_copy(source, target, local.at[number])
        copies[number].start()

    def need(*numbers):
        for number in numbers:
            copies[number].wait()

    def weight(m):
        return len(SAVED) + m

    def copy(m, at, src, dst, target):
        return remote(src, dst, send.at[m, at], recv.at[m, at], target)

    low, high = pl.ds(0, 2), pl.ds(2, 2)
    every = slice(None)

    def where(u, cc, zz, yy):
        matrix, start, n, paired = GRAD_UNITS[u]
        index = spot(paired, cc, zz, yy, k)
        return index if n == widths[matrix] else (*index, every, pl.ds(start, n))

    def block(u, cc, zz, yy):
        return grads[GRAD_UNITS[u][0]].at[where(u, cc, zz, yy)]

    def ordered(u, cc, rest):
        return (*rest, cc) if GRAD_UNITS[u][3] else (cc, *rest)

    def twin_copy(u):
        matrix, start, n, paired = GRAD_UNITS[u]
        index = (1 - k,) if paired else (every, every, every, 1 - k)
        if n != widths[matrix]:
            index = (*index, *(every,) * (5 - len(index)), pl.ds(start, n))
        return copy(u, 0, grads[matrix].at[index], got_0[u], twin)

    def first(u):
        return [
            copy(u, 1, block(u, every, low, 1 - y), got_1a[u], beside),
            copy(u, 2, block(u, 1 - c, high, every), got_1b[u], across),
        ]

    def second(u):
        return [
            copy(u, 3, block(u, 1 - c, low, y), got_2a[u], across),
            copy(u, 4, block(u, c, high, 1 - y), got_2b[u], beside),
        ]

    def along(u):
        return [
            copy(
                u,
                4 + step,
                block(u, c, lax.rem(z + step, 4), y),
                got_3[u].at[step - 1],
                device(lax.rem(z + step, 4), y, k, c),
            )
            for step in (1, 3, 2)
        ]

    def z_first(u):
        return [
            copy(
                u,
                step,
                block(u, every, lax.rem(z + step, 4), every),
                got_1a[u].at[step - 1],
                device(lax.rem(z + step, 4), y, k, c),
            )
            for step in (1, 3, 2)
        ]

    def plane_first(u):
        if Z_FIRST[u] == 1:
            return [copy(u, 4, block(u, every, z, 1 - y), got_2a[u], beside)]
        return [copy(u, 4, block(u, 1 - c, z, every), got_2a[u], across)]

    def plane_second(u):
        if Z_FIRST[u] == 1:
            return [copy(u, 5, block(u, 1 - c, z, y), got_2b[u], across)]
        return [copy(u, 5, block(u, c, z, 1 - y), got_2b[u], beside)]

    def mine(u):
        return k if GRAD_UNITS[u][3] else c

    def pair(u):
        return [copy(u, 8, total[u].at[1 - mine(u)], got_4[u], twin if GRAD_UNITS[u][3] else across)]

    def peer(step):
        return lax.rem(me + step, 32)

    def source(step):
        return lax.rem(me + 32 - step, 32)

    def table_copy(step, back, index):
        target = (peer(step) // 2, lax.rem(peer(step), 2))
        if back:
            return remote(
                table_out.at[index], table_out.at[index], table_send.at[1, step], table_recv.at[1, step], target
            )
        return remote(
            table.at[index], table_got.at[me], table_send.at[0, step], table_recv.at[0, step], target
        )

    def table_start(step):
        @pl.when(peer(step) < PIECES)
        def _():
            table_copy(step, False, peer(step)).start()

    def table_wait_send(step):
        @pl.when(peer(step) < PIECES)
        def _():
            table_copy(step, False, 0).wait_send()

        @pl.when(me < PIECES)
        def _():
            table_copy(step, True, 0).wait_send()

    def table_wait_back(step):
        @pl.when(source(step) < PIECES)
        def _():
            table_copy(step, True, 0).wait_recv()

    def each(action):
        def body(step, carry):
            action(step)
            return carry

        lax.fori_loop(1, 32, body, 0)

    def gather_into(u, cc, zz, yy, *others):
        matrix = GRAD_UNITS[u][0]
        index = where(u, cc, zz, yy)
        if not others:
            grads[matrix][index] = grads[matrix][index] + got_0[u][ordered(u, cc, (zz, yy))]
            return
        value = grads[matrix][index].astype(F32) + got_0[u][ordered(u, cc, (zz, yy))].astype(F32)
        for other in others:
            value = value + other.astype(F32)
        grads[matrix][index] = value.astype(BF16)

    def from_line(u, cc, yy):
        index = (yy, cc) if GRAD_UNITS[u][3] else (cc, yy)
        return [got_1a[u][(step, *index)] for step in range(3)]

    def stage_first(u):
        twin_copy(u).wait_recv()
        if u in Z_FIRST:
            for step in (1, 3, 2):
                for cc in range(2):
                    for yy in range(2):
                        gather_into(u, cc, lax.rem(z + step, 4), yy)
            for item in z_first(u):
                item.start()
            return
        for a in range(2):
            for b in range(2):
                gather_into(u, a, b, 1 - y)
                gather_into(u, 1 - c, 2 + a, b)
        for item in first(u):
            item.start()

    def from_beside(u, cc, a):
        return got_1a[u][ordered(u, cc, (a,))]

    def stage_second(u):
        if u in Z_FIRST:
            for item in z_first(u):
                item.wait_recv()
            for a in range(2):
                cc, yy = (a, 1 - y) if Z_FIRST[u] == 1 else (1 - c, a)
                gather_into(u, cc, z, yy, *from_line(u, cc, yy))
            for item in plane_first(u):
                item.start()
            return
        for item in first(u):
            item.wait_recv()
        for a in range(2):
            gather_into(u, 1 - c, a, y, from_beside(u, 1 - c, a))
            gather_into(u, c, 2 + a, 1 - y, got_1b[u][a, 1 - y])
        for item in second(u):
            item.start()

    def stage_along(u):
        if u in Z_FIRST:
            for item in plane_first(u):
                item.wait_recv()
            cc, yy = (1 - c, y) if Z_FIRST[u] == 1 else (c, 1 - y)
            gather_into(u, cc, z, yy, *from_line(u, cc, yy), got_2a[u][cc if Z_FIRST[u] == 1 else yy])
            for item in plane_second(u):
                item.start()
            return
        for item in second(u):
            item.wait_recv()
        for a in range(2):
            gather_into(u, c, a, y, from_beside(u, c, a), got_2a[u][a])
            gather_into(u, c, 2 + a, y, got_1b[u][a, y], got_2b[u][a])
        for item in along(u):
            item.start()

    def stage_pair(u):
        full = grads[GRAD_UNITS[u][0]][where(u, c, z, y)].astype(F32)
        if u in Z_FIRST:
            for item in plane_second(u):
                item.wait_recv()
            others = [got_0[u][ordered(u, c, (z, y))], *from_line(u, c, y)]
            others += [got_2a[u][c if Z_FIRST[u] == 1 else y], got_2b[u][...]]
        else:
            for item in along(u):
                item.wait_recv()
            others = [got_3[u][step] for step in range(3)]
        for other in others:
            full = full + other.astype(F32)
        total[u][0] = full[:24]
        total[u][1] = full[24:]
        for item in pair(u):
            item.start()

    def stage_end(u):
        matrix, start, n, _ = GRAD_UNITS[u]
        lanes = slice(start, start + n)
        side = mine(u)
        outs[matrix][side, :, lanes] = total[u][side]
        for item in pair(u):
            item.wait_recv()
        outs[matrix][1 - side, :, lanes] = got_4[u][...]
        own, other = total[u][side], got_4[u][...]
        square[...] += jnp.broadcast_to(total_of(own * own) + total_of(other * other), (8, 128))
        if u in Z_FIRST:
            sent = z_first(u) + plane_first(u) + plane_second(u)
        else:
            sent = first(u) + second(u) + along(u)
        for item in [twin_copy(u)] + sent:
            item.wait_send()

    def table_sum(u):
        @pl.when(me < PIECES)
        def _():
            each(lambda step: table_copy(step, False, 0).wait_recv())
            table_got[me] = table[me]

            def add(at, held):
                return held + table_got[at].astype(F32)

            total_rows = lax.fori_loop(1, 32, add, table_got[0].astype(F32))
            top, rest = split_two(total_rows[:8] + total_rows[8:])
            exact = jnp.concatenate([top.astype(F32), rest.astype(F32)], 0)
            table_out[me] = jnp.where(me >= 18, exact, total_rows).astype(BF16)
            each(lambda step: table_copy(step, True, me).start())

    late_parts = []

    def table_end(u):
        each(table_wait_back)
        need(weight(count))
        late_parts.append(
            table_finish(
                table_out, upstream, kept.table, kept.norms, kept.proj_t, late_parts[0], g_in, g_norm, send_stat
            )
        )
        for at, value in enumerate(late_parts[1][:4]):
            late_rows[at] = jnp.broadcast_to(value, (24, VP))
        square[...] += jnp.broadcast_to(late_parts[1][-1], (8, 128))

    def stat_copy(step):
        target = (peer(step) // 2, lax.rem(peer(step), 2))
        return remote(stat, stat_got.at[me], table_send.at[3, step], table_recv.at[3, step], target)

    def send_stat(rows):
        line = iota((8, VP), 0)
        result = jnp.zeros((8, VP), F32)
        for at, row in enumerate(rows):
            result = jnp.where(line == at, row, result)
        stat[...] = result
        each(lambda step: stat_copy(step).start())
        stat_got[me] = stat[...]

    def table_last():
        each(lambda step: stat_copy(step).wait())
        totals = lax.fori_loop(1, 32, lambda at, held: held + stat_got[at], stat_got[0])
        mean_1, mean_2 = totals[0:1] * (1.0 / D), totals[1:2] * (1.0 / D)
        inner, unit, rstd, emb_grad = (late_rows[at] for at in range(4))
        g_emb[...] = emb_grad + rstd * (inner - mean_1 - unit * mean_2)
        first, second = rstd[0:1] * mean_1, rstd[0:1] * mean_2
        whole = totals[6:7] - 2.0 * (first * totals[2:3] + second * totals[3:4])
        whole = whole + first * first * D + 2.0 * first * second * totals[4:5] + second * second * totals[5:6]
        return total_of(whole)

    stages = (stage_first, stage_second, stage_along, stage_pair, stage_end, table_sum, table_end)
    pending = list(BACKWARD_ORDER)

    def hook():
        for stage, u in pending.pop(0):
            stages[stage](u)

    def done(u):
        if u == 0:
            pl.semaphore_wait(barrier, 31)
        twin_copy(u).start()
        hook()

    names = Kept._fields

    load(AT.branch, saved.branch, branch)

    def phase_one(*early_refs):
        e = Early(*early_refs)
        load(weight(0), far[0], grads[0])
        load(AT.slope, saved.slope, e.slope)
        load(AT.active, saved.active, e.active)
        load(weight(1), far[1], grads[1])
        for name in names:
            load(getattr(AT, name), getattr(saved, name), getattr(kept, name))
        for m in (2, 3):
            load(weight(m), far[m], grads[m])
        for name in Early._fields[2:6]:
            load(getattr(AT, name), getattr(saved, name), getattr(e, name))
        load(weight(4), far[4], grads[4])
        for name in Early._fields[6:8]:
            load(getattr(AT, name), getattr(saved, name), getattr(e, name))
        load(weight(5), far[5], grads[5])
        for name in Early._fields[8:]:
            load(getattr(AT, name), getattr(saved, name), getattr(e, name))
        load(weight(6), far[6], grads[6])
        view = [g.reshape(2, D, n) for g, n in zip(grads, widths)]
        need(AT.branch)
        transpose_into(branch, branch_t)
        hook()

        def grad_tile(m, start, left_t, right, half, at):
            lanes = slice(start + half * widths[m] + at, start + half * widths[m] + at + 384)
            view[m][half, :, at : at + 384] = nn(left_t[...], right[:, lanes]).astype(BF16)

        def grad_half(m, start, left_t, right, half):
            for at in range(0, widths[m], 384):
                grad_tile(m, start, left_t, right, half, at)

        for part in range(2):
            need(weight(part))
            if part == 0:
                need(AT.slope)

            def down_back(half, at, part=part):
                lanes = slice(part * 1536 + half * 768 + at, part * 1536 + half * 768 + at + 384)
                back = nn(branch[...], view[part][half, :, at : at + 384])
                e.slope[:, lanes] = (back * e.slope[:, lanes].astype(F32)).astype(BF16)

            if part == 0:
                for at in (0, 384):
                    for half in range(2):
                        down_back(half, at)
                    hook()
                    if at == 0:
                        need(AT.active)
                    for half in range(2):
                        grad_tile(part, 0, branch_t, e.active, half, at)
                    done(at // 384)
            else:
                for half in range(2):
                    for at in (0, 384):
                        down_back(half, at)
                    hook()
                grad_half(part, part * 1536, branch_t, e.active, 0)
                hook()
                grad_half(part, part * 1536, branch_t, e.active, 1)
                done(2)
        for part in range(2):
            need(weight(2 + part))
            for half in range(2):
                start = part * 1536 + half * 768
                back = nt(e.slope[:, start : start + 768], view[2 + part][half])
                upstream[...] = back if start == 0 else upstream[...] + back
                hook()
            if part == 0:
                need(AT.feed_normed_t)
            grad_half(2 + part, part * 1536, e.feed_normed_t, e.slope, 0)
            hook()
            grad_half(2 + part, part * 1536, e.feed_normed_t, e.slope, 1)
            done(3 + part)
        need(*(getattr(AT, name) for name in names))
        norms = kept.norms[...]

        def gain(number):
            return norms[number : number + 1, :]

        need(AT.unit_2, AT.rstd_2)
        scale_2, shift_2 = back_rows(e.unit_2, e.rstd_2, gain(2), upstream, stream, branch, False)
        hook()
        need(weight(4), AT.col_mixed_t)
        mixed[...] = (nt(branch[:, :384], view[4][0]) + nt(branch[:, 384:], view[4][1])).astype(BF16)
        hook()
        for half in range(2):
            grad_half(4, 0, e.col_mixed_t, branch, half)
        done(5)
        need(AT.col_proj, AT.col_prob)
        proj = e.active

        def attend(at, carry):
            rows = pl.ds(pl.multiple_of((at // PAIRS) * 128, 128), 128)
            lane = lax.rem(at, PAIRS) * 128

            def lanes(part):
                return pl.ds(pl.multiple_of(part * D + lane, 128), 128)

            query = stacked(e.col_proj[rows, lanes(0)])
            key = e.col_proj[rows, lanes(1)]
            value = e.col_proj[rows, lanes(2)]
            above = stacked(mixed[rows, lanes(0)])
            prob = e.col_prob[at]
            grad = nt(above, value)
            grad = prob * (grad - jnp.sum(prob * grad, -1, keepdims=True))
            small = grad.astype(BF16)
            scale = HD ** (-0.5)
            proj[rows, lanes(0)] = (unstacked(nn(small, key), 128) * scale).astype(BF16)
            proj[rows, lanes(1)] = (tn(small, query) * scale).astype(BF16)
            proj[rows, lanes(2)] = tn(prob.astype(BF16), above).astype(BF16)
            return carry

        for part in range(6):
            lax.fori_loop(4 * part, 4 * part + 4, attend, 0, unroll=4)
            hook()
        need(weight(5))
        for half in range(2):
            back = nt(proj[:, half * 1152 : half * 1152 + 1152], view[5][half])
            upstream[...] = back if half == 0 else upstream[...] + back
            hook()
        need(AT.col_normed_t)
        for third in range(3):
            for half in range(2):
                grad_tile(5, 0, e.col_normed_t, proj, half, third * 384)
            done(6 + third)
        need(AT.unit_1, AT.rstd_1)
        scale_1, shift_1 = back_rows(e.unit_1, e.rstd_1, gain(1), upstream, stream, branch, False)
        hook()
        need(weight(6))
        mixed[...] = (nt(branch[:, :384], view[6][0]) + nt(branch[:, 384:], view[6][1])).astype(BF16)
        line = iota((8, D), 0)
        vectors = jnp.zeros((8, D), F32)
        moved = kept.moved[...]
        rows = (scale_1, scale_2, moved[0:1], shift_1, shift_2, moved[1:2])
        for number, row in enumerate(rows):
            vectors = jnp.where(line == number, row, vectors)
        extras = jnp.concatenate([kept.extras[0:1, :], jnp.zeros((1, D - 128), F32)], 1)
        kept.moved[...] = jnp.where(line == 6, extras, vectors)
        hook()

    pl.run_scoped(phase_one, *(pltpu.VMEM(*item) for item in pick_items(Early, SAVED)))

    def phase_two(*late_refs):
        e = Late(*late_refs[:-3])
        in_row, left_hi, left_lo = late_refs[-3:]
        for name in Late._fields:
            load(getattr(AT, name), getattr(saved, name), getattr(e, name))
        load(weight(count), in_row_far.at[0], in_row)
        view = grads[6].reshape(2, D, widths[6])
        late_parts.append(in_row)
        need(AT.row_mixed_t)
        for half in range(2):
            lanes = slice(half * 384, half * 384 + 384)
            view[half] = nn(e.row_mixed_t[...], branch[:, lanes]).astype(BF16)
        done(9)
        need(AT.hot_all, AT.weight_hi, AT.prob, AT.hot_ri, AT.hot_ir)
        shape = (HERE, HERE)
        back = (
            ((iota(shape, 1) >> 4) == (iota(shape, 0) & 31))
            & ((iota(shape, 1) & 15) == (iota(shape, 0) >> 5))
        )
        mixed[...] = nn(one_zero(back).astype(BF16), mixed[...]).astype(BF16)
        value_rows = []
        for hp in range(PAIRS):
            lanes = slice(hp * 128, hp * 128 + 128)
            part = mixed[:, lanes]
            upstream[:, lanes] = nt(part, kept.value_two[hp])
            value_rows.append(unstacked(tn(e.weight_hi[:, lanes], part), 64))
        hook()
        split_heads_to(upstream, left_hi, left_lo)
        hook()
        hot_all = e.hot_all[...]
        grad = nn(left_hi[...], hot_all) + nn(left_lo[...], hot_all)
        extra = jnp.concatenate(
            [kept.touch[...] * (contact_head[h] * COLS) for h in range(HEADS)], 0
        )
        grad = grad + extra
        prob = e.prob[...]
        grad = prob * (grad - jnp.sum(prob * grad, -1, keepdims=True))
        low_grad = grad.astype(BF16)
        hook()
        merge_heads(low_grad, e.hot_all, branch, None)
        hook()
        table_pair = nn(e.hot_ri[...], branch[...])
        stream_hi, stream_lo = split_two(stream[...])
        hot_ir = e.hot_ir[...]
        table_grad = kept.grad_head[...] + nn(hot_ir, stream_hi) + nn(hot_ir, stream_lo)
        value_grad = jnp.concatenate(value_rows, 1)
        last = jnp.where(iota((8, D), 0) == 7, table_grad[32:33], kept.moved[...])
        top, rest = split_two(last)
        groups = [table_pair[4:20], table_pair[20:36], value_grad[4:20], value_grad[20:36]]
        groups += [table_grad[0:16], table_grad[16:32]]
        groups += [jnp.concatenate([top.astype(F32), rest.astype(F32)], 0)]
        for number, group in enumerate(groups):
            for third in range(3):
                table[3 * number + third] = group[:, third * 256 : third * 256 + 256].astype(BF16)
        each(table_start)
        hook()
        hook()

    pl.run_scoped(
        phase_two,
        *(pltpu.VMEM(*item) for item in pick_items(Late, SAVED)),
        pltpu.VMEM((24, 3 * D), F32),
        pltpu.VMEM((HEADS * WIDE, ROWS * VP), BF16),
        pltpu.VMEM((HEADS * WIDE, ROWS * VP), BF16),
    )
    assert not pending

    def square_copy(step):
        other = lax.rem(me + step, 32)
        return remote(
            square, square_got.at[me], table_send.at[2, step], table_recv.at[2, step], (other // 2, lax.rem(other, 2))
        )

    each(lambda step: square_copy(step).start())
    square_got[me] = square[...]
    each(lambda step: table_wait_send(step))
    for u in range(units):
        for item in pair(u):
            item.wait_send()
    emb_square = table_last()
    each(lambda step: square_copy(step).wait())
    total_square = lax.fori_loop(1, 32, lambda at, held: held + square_got[at], square_got[0])[0:1]
    vector = table_out[18].astype(F32)
    vector = vector[6:7, :128] + vector[14:15, :128]
    counted = kept.extras[1:2, :]
    column = iota((1, 128), 1)
    contact = jnp.where(column <= HEADS, vector, 0.0)
    total_square = total_square + total_of(contact * contact) + emb_square
    grad_norm = jnp.sqrt(total_square)
    factor = jnp.minimum(1.0, MAX_NORM / grad_norm)
    losses = (
        (0, vector[:, HEADS + 1 : HEADS + 2]),
        (1, counted[:, 0:1]),
        (2, vector[:, HEADS + 2 : HEADS + 3]),
        (3, counted[:, 1:2]),
    )
    loss_row = jnp.zeros((1, 128), F32)
    for at, value in losses:
        loss_row = jnp.where(column == at, value, loss_row)
    number = iota((8, 128), 0)
    result = jnp.zeros((8, 128), F32)
    for at, row in enumerate((contact, counted, factor, grad_norm, loss_row)):
        result = jnp.where(number == at, row, result)
    stats[...] = result


def backward_call(contact_head, weights, in_row, saved):
    widths = GRAD_WIDTHS
    count = len(widths)
    inside = pl.BlockSpec(memory_space=pltpu.VMEM)
    anywhere = pl.BlockSpec(memory_space=pl.ANY)

    units = len(GRAD_UNITS)

    def shapes(lead, dtype, other=None):
        leads = [other if other and u in Z_FIRST else lead for u in range(units)]
        return [pltpu.VMEM((*at, n), dtype) for at, (_, _, n, _) in zip(leads, GRAD_UNITS)]

    outs = pl.pallas_call(
        backward_kernel,
        out_shape=[jax.ShapeDtypeStruct((2, 24, n), F32) for n in widths]
        + [
            jax.ShapeDtypeStruct((24, 3 * D), F32),
            jax.ShapeDtypeStruct((24, VP), F32),
            jax.ShapeDtypeStruct((8, 24), F32),
            jax.ShapeDtypeStruct((8, 128), F32),
        ],
        in_specs=[pl.BlockSpec(memory_space=pltpu.SMEM)] + [anywhere] * (1 + count + len(SAVED)),
        out_specs=[inside] * (4 + count),
        scratch_shapes=[pltpu.VMEM((2, NZ, NY, 2, 48, n), BF16) for n in widths]
        + [pltpu.VMEM(*item) for item in pick_items(Kept, SAVED)]
        + [
            pltpu.VMEM((HERE, D), F32),
            pltpu.VMEM((HERE, D), BF16),
            pltpu.VMEM((D, HERE), BF16),
            pltpu.VMEM((HERE, D), BF16),
        ]
        + [
            pltpu.VMEM((NZ, NY, 2, 48, n) if paired else (2, NZ, NY, 48, n), BF16)
            for _, _, n, paired in GRAD_UNITS
        ]
        + shapes((2, 2, 48), BF16, (3, 2, 2, 48))
        + shapes((2, 2, 48), BF16, (16,))
        + shapes((2, 48), BF16, (2, 48))
        + shapes((2, 48), BF16, (48,))
        + shapes((3, 48), BF16, (16,))
        + shapes((2, 24), F32)
        + shapes((24,), F32)
        + [
            pltpu.VMEM((PIECES, 16, 256), BF16),
            pltpu.VMEM((PIECES, 16, 256), BF16),
            pltpu.VMEM((32, 16, 256), BF16),
            pltpu.VMEM((8, 128), F32),
            pltpu.VMEM((32, 8, 128), F32),
            pltpu.VMEM((8, VP), F32),
            pltpu.VMEM((32, 8, VP), F32),
            pltpu.VMEM((4, 24, VP), F32),
            pltpu.SemaphoreType.DMA((4, 32)),
            pltpu.SemaphoreType.DMA((4, 32)),
            pltpu.SemaphoreType.DMA((units, 9)),
            pltpu.SemaphoreType.DMA((units, 9)),
            pltpu.SemaphoreType.DMA((len(SAVED) + count + 1,)),
        ],
        compiler_params=pltpu.CompilerParams(
            collective_id=1, has_side_effects=True, vmem_limit_bytes=63 * 2**20
        ),
    )(contact_head, *weights, in_row, *saved)
    return outs[:count], outs[count:]


UPDATE_RATES = (LEARN_RATE,) * 4 + (VECTOR_RATE,) * 3


def update_kernel(*refs):
    given, far, held, results = refs[:32], refs[32:60], refs[60:92], refs[92:120]
    sems, out_sems = refs[120:122]
    outs, copies = results[:21], results[21:26]
    loss_ref, norm_ref = results[26:]

    def leave(*numbers):
        for n in numbers:
            pltpu.make_async_copy(results[n], far[n], out_sems.at[n]).start()

    moves = [pltpu.make_async_copy(a, b, sems.at[n]) for n, (a, b) in enumerate(zip(given, held))]
    groups = (
        (10, 7, 5, 11, 12, 13),
        (4, 6, 14, 15, 16),
        (2, 3, 17, 18, 19),
        (0, 1, 20, 21, 22),
        (8, 9, *range(23, 32)),
    )
    for group in groups:
        for n in group:
            moves[n].start()

    def arrive(number):
        for n in groups[number]:
            moves[n].wait()

    reduced, g_in, g_emb, g_norm, stats = held[:7], held[7], held[8], held[9], held[10]
    states = [held[11 + 3 * n : 14 + 3 * n] for n in range(7)]
    outs = [outs[3 * n : 3 * n + 3] for n in range(7)]
    order = feature_order()
    arrive(0)
    factor = stats[2:3, 0:1]
    loss_ref[...] = stats[4:5, 0:4]
    norm_ref[...] = stats[3:4, 0:1]

    def natural(values):
        top, rest = split_two(values)
        last = (values - top.astype(F32) - rest.astype(F32)).astype(BF16)
        return nt(top, order) + nt(rest, order) + nt(last, order)

    def update(number, where, grad):
        master, first, second = (ref[where] for ref in states[number])
        new, first, second = adam_update(master, first, second, grad * factor, UPDATE_RATES[number])
        for ref, value in zip(outs[number], (new, first, second)):
            ref[where] = value
        if number < 5:
            copies[number][where] = new.astype(BF16)

    every = slice(None)
    g_out_col, g_in_col, g_out_row = reduced[4:]
    for half in range(2):
        lanes = slice(half * 1152, half * 1152 + 1152)
        update(0, (0, every, lanes), g_in[:, lanes])
        update(0, (1, every, lanes), g_in_col[half])
    leave(0, 1, 2, 21, 26, 27)
    arrive(1)
    for half in range(2):
        lanes = slice(half * 384, half * 384 + 384)
        update(1, (0, every, lanes), natural(g_out_row[half]))
        update(1, (1, every, lanes), natural(g_out_col[half]))
    leave(3, 4, 5, 22)
    for number, first in ((2, 2), (3, 0)):
        arrive(number)
        for half in range(2):
            for part in range(2):
                start = part * 1536 + half * 768
                lanes = slice(start, start + 768)
                update(number, (every, lanes), reduced[first + part][half])
        leave(*((6, 7, 8, 23) if number == 2 else (9, 10, 11, 24)))
    arrive(4)
    update(4, (every, every), g_emb[:, :VOCAB])
    update(5, (every, every), g_norm[...])
    update(6, (every, every), stats[0:1, : HEADS + 1])
    leave(12, 13, 14, 25, 15, 16, 17, 18, 19, 20)
    for n in range(28):
        pltpu.make_async_copy(results[n], far[n], out_sems.at[n]).wait()


def update_call(reduced, g_in, g_emb, g_norm, stats, states):
    anywhere = pl.BlockSpec(memory_space=pl.ANY)
    flat = [item for state in states for item in state]
    shapes = [jax.ShapeDtypeStruct(item.shape, F32) for item in flat]
    shapes += [jax.ShapeDtypeStruct(states[n][0].shape, BF16) for n in range(5)]
    shapes += [jax.ShapeDtypeStruct((1, 4), F32), jax.ShapeDtypeStruct((1, 1), F32)]
    given = (*reduced, g_in, g_emb, g_norm, stats, *flat)
    return pl.pallas_call(
        update_kernel,
        out_shape=shapes,
        in_specs=[anywhere] * len(given),
        out_specs=[anywhere] * len(shapes),
        scratch_shapes=[pltpu.VMEM(item.shape, F32) for item in given]
        + [pltpu.VMEM(item.shape, item.dtype) for item in shapes]
        + [
            pltpu.SemaphoreType.DMA((len(given),)),
            pltpu.SemaphoreType.DMA((len(shapes),)),
            pltpu.VMEM((44, 512, 512), F32),
        ],
        compiler_params=pltpu.CompilerParams(vmem_limit_bytes=62 * 2**20),
    )(*given)


def adam_update(master, first, second, grad_part, rate):
    first = BETA_ONE * first + (1.0 - BETA_ONE) * grad_part
    second = BETA_TWO * second + (1.0 - BETA_TWO) * grad_part * grad_part
    scaled = first * (1.0 / (1.0 - BETA_ONE**STEP))
    moved = scaled / (jnp.sqrt(second * (1.0 / (1.0 - BETA_TWO**STEP))) + ADAM_EPS)
    return (master - rate * (moved + WEIGHT_DECAY * master), first, second)


def shards(
    tokens,
    targets,
    masked,
    contact_pairs,
    labels,
    attention_in_master,
    attention_in_first,
    attention_in_second,
    attention_out_master,
    attention_out_first,
    attention_out_second,
    feed_up_master,
    feed_up_first,
    feed_up_second,
    feed_down_master,
    feed_down_first,
    feed_down_second,
    embedding_master,
    embedding_first,
    embedding_second,
    norm_params_master,
    norm_params_first,
    norm_params_second,
    contact_head_master,
    contact_head_first,
    contact_head_second,
):
    both = ("seq", "col")
    micro, rows_here, cols_here = tokens.shape
    ncol = lax.axis_size("col")
    ndev = lax.axis_size("seq") * ncol
    cols = cols_here * ncol
    me = lax.axis_index("seq") * ncol + lax.axis_index("col")
    per = ndev // micro
    cw = cols // per
    mine = me // per
    base = (me % per) * cw
    shard = D // ndev

    tiled = lax.axis_size("seq") == 16 and ncol == 2
    if tiled:
        raw = (
            tokens,
            targets,
            masked,
            contact_pairs.transpose(0, 2, 1),
            labels,
            embedding_master.T,
            norm_params_master,
            attention_in_master,
            attention_out_master,
            feed_up_master,
            feed_down_master.T,
        )
        weights, saved = forward_call(raw, contact_head_master)
        reduced, (g_in, g_emb, g_norm, stats) = backward_call(
            contact_head_master, [weights[n] for n in (5, 6, 3, 4, 2, 1, 0)], attention_in_master, saved
        )
        states = (
            (attention_in_master, attention_in_first, attention_in_second),
            (attention_out_master, attention_out_first, attention_out_second),
            (feed_up_master, feed_up_first, feed_up_second),
            (feed_down_master.T, feed_down_first.T, feed_down_second.T),
            (embedding_master.T, embedding_first.T, embedding_second.T),
            (norm_params_master, norm_params_first, norm_params_second),
            (contact_head_master[None], contact_head_first[None], contact_head_second[None]),
        )
        outs = update_call(reduced, g_in, g_emb, g_norm, stats, states)
        return (
            *outs[:9],
            *(item.T for item in outs[9:15]),
            *outs[15:18],
            *(item[0] for item in outs[18:21]),
            *outs[21:24],
            *(item.T for item in outs[24:26]),
            outs[26][0],
            outs[27][0, 0],
        )
    inputs = jnp.where(masked > 0, MASK_ID, tokens)
    masters = [
        jnp.concatenate(
            [
                jnp.pad(embedding_master.T, ((0, 0), (0, 128 - VOCAB))),
                jnp.pad(norm_params_master.T, ((0, 0), (0, 120))),
            ],
            1,
        ),
        attention_in_master[0],
        attention_out_master[0],
        attention_in_master[1],
        attention_out_master[1],
        feed_up_master,
        feed_down_master.T,
    ]
    whole = jnp.stack([inputs, targets])
    whole = lax.all_gather(lax.all_gather(whole, "col", axis=3, tiled=True), "seq", axis=2, tiled=True)
    pairs_all = lax.all_gather(
        jnp.concatenate([contact_pairs, labels[:, :, None]], -1), both, axis=1, tiled=True
    )
    gathered = []
    for master in masters:
        full = lax.all_gather(master.astype(BF16), both, axis=0, tiled=True)
        gathered.append(full.reshape(D, 2, -1).transpose(1, 0, 2))
    counts = (
        jnp.sum(whole[0] == MASK_ID).astype(F32),
        jnp.sum(pairs_all[..., 2] >= 0).astype(F32),
    )
    ids_all = lax.dynamic_index_in_dim(whole[0], mine, 0, False)
    ids_local = lax.dynamic_slice_in_dim(ids_all, base, cw, 1)
    targets_local = lax.dynamic_slice_in_dim(
        lax.dynamic_index_in_dim(whole[1], mine, 0, False), base, cw, 1
    )
    pairs = lax.dynamic_index_in_dim(pairs_all, mine, 0, False)

    table = gathered[0][0][:, :VP].T
    norms = gathered[0][1][:, :8].T.astype(F32)
    in_row, out_row, in_col, out_col, up_w, down_t = (
        jnp.concatenate([g[0], g[1]], 1) for g in gathered[1:]
    )
    big = (in_row, in_col, out_row, out_col, up_w, down_t)

    grads, tables, contact_total, mlm_total, bce_total, kept = step(
        big,
        table,
        norms,
        contact_head_master,
        ids_all,
        ids_local.reshape(-1),
        ids_local.T.reshape(-1),
        targets_local.T.reshape(-1),
        pairs[:, 0] - base,
        pairs[:, 1],
        pairs[:, 2],
        counts,
        cw,
    )
    table_pair, value_grad, table_grad, vectors = tables
    extras = jnp.zeros((2, D), F32).at[0, : HEADS + 3].set(
        jnp.concatenate([contact_total, mlm_total[None], bce_total[None]])
    )
    sums = jnp.concatenate([table_pair[:40], value_grad[:40], table_grad[:40], vectors, extras])
    flat_grad = jnp.concatenate([g.astype(BF16) for g in grads], 1)
    reduced = lax.psum_scatter(flat_grad, both, scatter_dimension=0, tiled=True).astype(F32)
    g_in_col, g_out_row, g_out_col, g_up, g_down = jnp.split(
        reduced, [3 * D, 4 * D, 5 * D, 5 * D + FF], 1
    )
    sums = lax.psum(sums, both)
    unit_t, rstd_t, normed_t, query_t, key_t = kept
    rows_all = ids_all.shape[0]
    spare = ((0, VP - 40), (0, 0))
    table_pair, value_grad, table_grad = (
        jnp.pad(sums[a : a + 40], spare) for a in (0, 40, 80)
    )
    vectors = sums[120:126]
    contact_grad, mlm_total, bce_total = (
        sums[126, : HEADS + 1], sums[126, HEADS + 1], sums[126, HEADS + 2]
    )
    row_scale = (HD * rows_all) ** (-0.5)
    query_grad = []
    key_grad = []
    for h in range(HEADS):
        pair = heads_of(table_pair, h)
        query_grad.append(jnp.dot(pair, heads_of(key_t, h).astype(F32), precision=PRECISE))
        key_grad.append(jnp.dot(pair.T, heads_of(query_t, h).astype(F32), precision=PRECISE))
    proj_grad = jnp.concatenate(
        [
            jnp.concatenate(query_grad, 1) * row_scale,
            jnp.concatenate(key_grad, 1) * row_scale,
            value_grad,
        ],
        1,
    )
    proj_hi, proj_lo = split_two(proj_grad)
    normed_grad = nt(proj_hi, in_row) + nt(proj_lo, in_row)
    back_t, scale_0, shift_0 = norm_back(unit_t, rstd_t, norms[0], normed_grad)
    table_grad = table_grad + back_t
    low = me * shard
    normed_mine = lax.dynamic_slice_in_dim(normed_t, low, shard, 1)
    grad_in_row = tn(normed_mine, proj_hi) + tn(normed_mine, proj_lo)
    norm_grad = jnp.concatenate([scale_0[None], vectors[:3], shift_0[None], vectors[3:]])
    table_mine = lax.dynamic_slice_in_dim(table_grad[:VOCAB], low, shard, 1)
    norm_mine = lax.dynamic_slice_in_dim(norm_grad, low, shard, 1)
    reduced_all = (g_in_col, g_out_row, g_out_col, g_up, g_down)

    local_square = (
        sum(jnp.sum(g * g) for g in reduced_all)
        + jnp.sum(grad_in_row * grad_in_row)
        + jnp.sum(table_mine * table_mine)
        + jnp.sum(norm_mine * norm_mine)
    )
    square = lax.psum(local_square, both) + jnp.sum(contact_grad * contact_grad)
    grad_norm = jnp.sqrt(square)
    factor = jnp.minimum(1.0, MAX_NORM / grad_norm)
    in_new, in_moment, in_square = adam_update(
        attention_in_master, attention_in_first, attention_in_second, jnp.stack([grad_in_row, g_in_col]) * factor, LEARN_RATE
    )
    out_new, out_moment, out_square = adam_update(
        attention_out_master, attention_out_first, attention_out_second, jnp.stack([g_out_row, g_out_col]) * factor, LEARN_RATE
    )
    up_new, up_moment, up_square = adam_update(
        feed_up_master, feed_up_first, feed_up_second, g_up * factor, LEARN_RATE
    )
    down_new, down_moment, down_square = adam_update(
        feed_down_master, feed_down_first, feed_down_second, g_down.T * factor, LEARN_RATE
    )
    table_new, table_moment, table_square = adam_update(
        embedding_master, embedding_first, embedding_second, table_mine * factor, VECTOR_RATE
    )
    norm_new, norm_moment, norm_square = adam_update(
        norm_params_master, norm_params_first, norm_params_second, norm_mine * factor, VECTOR_RATE
    )
    head_new, head_moment, head_square = adam_update(
        contact_head_master, contact_head_first, contact_head_second, contact_grad * factor, VECTOR_RATE
    )
    loss_parts = jnp.stack([mlm_total, counts[0], bce_total, counts[1]])
    return (
        in_new, in_moment, in_square,
        out_new, out_moment, out_square,
        up_new, up_moment, up_square,
        down_new, down_moment, down_square,
        table_new, table_moment, table_square,
        norm_new, norm_moment, norm_square,
        head_new, head_moment, head_square,
        in_new.astype(BF16), out_new.astype(BF16), up_new.astype(BF16), down_new.astype(BF16), table_new.astype(BF16),
        loss_parts, grad_norm,
    )


def solution(mesh):
    both = ("seq", "col")
    cells = P(None, "seq", "col")
    stack = P(None, both, None)
    row_split = P(both, None)
    col_split = P(None, both)
    weights = [stack] * 6 + [row_split] * 3 + [col_split] * 9 + [P()] * 3
    return jax.shard_map(
        shards,
        mesh=mesh,
        in_specs=(cells, cells, cells, stack, col_split, *weights),
        out_specs=(*weights, stack, stack, row_split, col_split, col_split, P(), P()),
        check_vma=False,
    )
```

```python
import typing

import jax
import jax.numpy as jnp
from jax import lax
from jax.experimental import pallas as pl
from jax.experimental.pallas import tpu as pltpu
from jax.sharding import PartitionSpec as P

D = 768
HEADS = 12
HD = 64
FF = 3072
VOCAB = 33
VP = 64
STEP = 10

NORM_EPS = 1e-05
MASK_ID = 32
MAX_NORM = 0.001
LEARN_RATE = 0.05
VECTOR_RATE = 0.5
BETA_ONE = 0.9
BETA_TWO = 0.95
ADAM_EPS = 1e-08
WEIGHT_DECAY = 0.01
PRECISE = lax.Precision.HIGHEST
F32 = jnp.float32
BF16 = jnp.bfloat16


def nn(left, right):
    return lax.dot_general(left, right, (((1,), (0,)), ((), ())), preferred_element_type=F32)


def tn(left, right):
    return lax.dot_general(left, right, (((0,), (0,)), ((), ())), preferred_element_type=F32)


def nt(left, right):
    return lax.dot_general(left, right, (((1,), (1,)), ((), ())), preferred_element_type=F32)


def split_two(values):
    high = values.astype(BF16)
    return high, (values - high.astype(F32)).astype(BF16)


def norm_stats(values):
    centre = values - jnp.mean(values, -1, keepdims=True)
    rstd = lax.rsqrt(jnp.mean(centre * centre, -1, keepdims=True) + NORM_EPS)
    return centre * rstd, rstd


def norm_back(unit, rstd, scale_vec, upstream):
    inner = upstream * scale_vec
    grad = rstd * (
        inner - jnp.mean(inner, -1, keepdims=True) - unit * jnp.mean(inner * unit, -1, keepdims=True)
    )
    return grad, jnp.sum(upstream * unit, 0), jnp.sum(upstream, 0)


GELU_K = 0.7978845608028654
GELU_C = 0.044715


def gelu_parts(up):
    square = up * up
    bent = jnp.tanh(GELU_K * up * (1.0 + GELU_C * square))
    half = 0.5 * (1.0 + bent)
    slope = half + 0.5 * up * (1.0 - bent * bent) * GELU_K * (1.0 + 3.0 * GELU_C * square)
    return up * half, slope


def heads_of(block, head):
    return block[:, head * HD : (head + 1) * HD]


def step(big, table, norms, contact_head, ids_all, ids_ri, ids_ir, targets_ir, pair_first, pair_second, labels, counts, cw):
    in_row, in_col, out_row, out_col, up_w, down_t = big
    rows, cols = ids_all.shape
    here = rows * cw
    row_scale = (HD * rows) ** (-0.5)
    vocab = jnp.arange(VP)[:, None]
    hot_all = (ids_all[:, None, :] == vocab[None]).astype(BF16).reshape(rows * VP, cols)
    hot_ri = (ids_ri[None, :] == vocab).astype(BF16)
    hot_ir = (ids_ir[None, :] == vocab).astype(BF16)
    spot = jnp.arange(here)
    perm = (
        ((spot // rows)[:, None] == (spot % cw)[None, :])
        & ((spot % rows)[:, None] == (spot // cw)[None, :])
    ).astype(BF16)

    def to_heads(block):
        return block.reshape(rows, cw, HEADS, VP).transpose(2, 1, 0, 3).reshape(HEADS * cw, rows * VP)

    def to_tokens(block):
        return block.reshape(HEADS, cw, rows, VP).transpose(2, 1, 0, 3).reshape(here, HEADS * VP)

    def per_head(block, other, how):
        return jnp.concatenate(
            [how(heads_of(block, h), heads_of(other, h)) for h in range(HEADS)], -1
        )

    table_f = table.astype(F32)
    unit_t, rstd_t = norm_stats(table_f)
    normed_t = (unit_t * norms[0] + norms[4]).astype(BF16)
    proj_t = nn(normed_t, in_row).astype(BF16)
    query_t, key_t, value_t = proj_t[:, :D], proj_t[:, D : 2 * D], proj_t[:, 2 * D :]

    pair_t = per_head(query_t, key_t, nt)
    pair_hi, pair_lo = split_two(pair_t)
    left_hi = to_heads(tn(hot_ri, pair_hi).astype(BF16))
    left_lo = to_heads(tn(hot_ri, pair_lo).astype(BF16))
    score = (nn(left_hi, hot_all) + nn(left_lo, hot_all)) * row_scale
    prob = jax.nn.softmax(score, axis=-1)
    prob_low = prob.astype(BF16)
    weight_t = to_tokens(nt(prob_low, hot_all))
    weight_hi, weight_lo = split_two(weight_t)
    row_mixed_ri = (
        per_head(weight_hi, value_t, nn) + per_head(weight_lo, value_t, nn)
    ).astype(BF16)
    row_mixed = nn(perm, row_mixed_ri).astype(BF16)
    embedded = tn(hot_ir, table)
    after_row = embedded + nn(row_mixed, out_row)

    prob_cube = prob_low.astype(F32).reshape(HEADS, cw, cols)
    head_sum = jnp.sum(prob_cube * contact_head[:HEADS, None, None], 0)
    first_hot = (pair_first[None, :] == jnp.arange(cw)[:, None]).astype(F32)
    second_hot = (pair_second[None, :] == jnp.arange(cols)[:, None]).astype(BF16)
    sum_hi, sum_lo = split_two(head_sum)
    sum_last = (head_sum - sum_hi.astype(F32) - sum_lo.astype(F32)).astype(BF16)
    picked = nn(sum_hi, second_hot) + nn(sum_lo, second_hot) + nn(sum_last, second_hot)
    contact_logit = jnp.sum(picked * first_hot, 0) * cols + contact_head[HEADS]
    owned = jnp.sum(first_hot, 0) > 0
    valid = (labels >= 0) & owned
    positive = (labels == 1).astype(F32)
    bce_sum = jnp.sum(
        jnp.where(valid, jax.nn.softplus(contact_logit) - positive * contact_logit, 0.0)
    )
    coef = jnp.where(valid, jax.nn.sigmoid(contact_logit) - positive, 0.0) / counts[1]
    coef_hi, coef_lo = split_two(coef)
    first_low = first_hot.astype(BF16)
    touch = nt(first_low * coef_hi[None], second_hot) + nt(first_low * coef_lo[None], second_hot)
    grad_contact = jnp.concatenate(
        [jnp.sum(prob_cube * touch[None], (1, 2)) * cols, jnp.sum(coef)[None]]
    )

    unit_1, rstd_1 = norm_stats(after_row)
    col_normed = (unit_1 * norms[1] + norms[5]).astype(BF16)
    col_proj = nn(col_normed, in_col).astype(BF16)
    group = 128 if here % 128 == 0 and 128 % rows == 0 else here
    groups = here // group
    lane = jnp.arange(group)
    same = (lane[:, None] // rows) == (lane[None, :] // rows)

    def cut(block):
        return block.reshape(groups, group, HEADS, HD)

    col_query, col_key, col_value = (cut(col_proj[:, k * D : (k + 1) * D]) for k in range(3))
    col_score = jnp.einsum("gqhe,gkhe->ghqk", col_query, col_key, preferred_element_type=F32) * HD ** (-0.5)
    col_prob = jax.nn.softmax(jnp.where(same, col_score, -1e30), axis=-1)
    col_prob_low = col_prob.astype(BF16)
    col_mixed = (
        jnp.einsum("ghqk,gkhe->gqhe", col_prob_low, col_value, preferred_element_type=F32)
        .astype(BF16)
        .reshape(here, D)
    )
    after_col = after_row + nn(col_mixed, out_col)

    unit_2, rstd_2 = norm_stats(after_col)
    feed_normed = (unit_2 * norms[2] + norms[6]).astype(BF16)
    hidden_up = nn(feed_normed, up_w)
    active, slope = gelu_parts(hidden_up)
    active = active.astype(BF16)
    after_feed = after_col + nt(active, down_t)
    unit_3, rstd_3 = norm_stats(after_feed)
    head_normed = (unit_3 * norms[3] + norms[7]).astype(BF16)
    logits = nt(table, head_normed) * D ** (-0.5)
    logits = jnp.where(vocab < VOCAB, logits, -1e30)
    top = jnp.max(logits, 0, keepdims=True)
    shifted = logits - top
    log_probs = shifted - jnp.log(jnp.sum(jnp.exp(shifted), 0, keepdims=True))
    target_hot = (targets_ir[None, :] == vocab).astype(F32)
    keep = ids_ir[None, :] == MASK_ID
    mlm_sum = -jnp.sum(jnp.where(keep & (target_hot > 0), log_probs, 0.0))
    logit_grad = jnp.where(keep, jnp.exp(log_probs) - target_hot, 0.0) / counts[0]
    logit_low = (logit_grad * D ** (-0.5)).astype(BF16)

    grad_head = nn(logit_low, head_normed)
    stream, scale_3, shift_3 = norm_back(unit_3, rstd_3, norms[3], tn(logit_low, table))
    branch = stream.astype(BF16)
    grad_down = tn(branch, active)
    up_low = (nn(branch, down_t) * slope).astype(BF16)
    grad_up = tn(feed_normed, up_low)
    inner, scale_2, shift_2 = norm_back(unit_2, rstd_2, norms[2], nt(up_low, up_w))
    stream = stream + inner
    branch = stream.astype(BF16)
    grad_out_col = tn(col_mixed, branch)
    mixed_low = nt(branch, out_col).astype(BF16)
    mixed_cut = cut(mixed_low)
    prob_grad = jnp.einsum("gqhe,gkhe->ghqk", mixed_cut, col_value, preferred_element_type=F32)
    score_grad = col_prob * (prob_grad - jnp.sum(col_prob * prob_grad, -1, keepdims=True))
    score_low = score_grad.astype(BF16)
    grad_q = jnp.einsum("ghqk,gkhe->gqhe", score_low, col_key, preferred_element_type=F32)
    grad_k = jnp.einsum("ghqk,gqhe->gkhe", score_low, col_query, preferred_element_type=F32)
    grad_v = jnp.einsum("ghqk,gqhe->gkhe", col_prob_low, mixed_cut, preferred_element_type=F32)
    proj_low = jnp.concatenate(
        [
            (grad_q * HD ** (-0.5)).reshape(here, D),
            (grad_k * HD ** (-0.5)).reshape(here, D),
            grad_v.reshape(here, D),
        ],
        -1,
    ).astype(BF16)
    grad_in_col = tn(col_normed, proj_low)
    inner, scale_1, shift_1 = norm_back(unit_1, rstd_1, norms[1], nt(proj_low, in_col))
    stream = stream + inner
    branch = stream.astype(BF16)
    grad_out_row = tn(row_mixed, branch)
    mixed_low = nt(branch, out_row).astype(BF16)
    mixed_ri = tn(perm, mixed_low).astype(BF16)
    drive_hi, drive_lo = split_two(per_head(mixed_ri, value_t, nt))
    prob_grad = nn(to_heads(drive_hi), hot_all) + nn(to_heads(drive_lo), hot_all)
    prob_grad = prob_grad + (
        touch[None] * (contact_head[:HEADS, None, None] * cols)
    ).reshape(HEADS * cw, cols)
    score_grad = prob * (prob_grad - jnp.sum(prob * prob_grad, -1, keepdims=True))
    score_low = score_grad.astype(BF16)
    spread = to_tokens(nt(score_low, hot_all)).astype(BF16)
    table_pair = nn(hot_ri, spread)
    value_grad = per_head(weight_hi, mixed_ri, tn)
    stream_hi, stream_lo = split_two(stream)
    lookup_grad = nn(hot_ir, stream_hi) + nn(hot_ir, stream_lo)
    vectors = jnp.stack([scale_1, scale_2, scale_3, shift_1, shift_2, shift_3])
    return (
        (grad_in_col, grad_out_row, grad_out_col, grad_up, grad_down),
        (table_pair, value_grad, grad_head + lookup_grad, vectors),
        grad_contact,
        mlm_sum,
        bce_sum,
        (unit_t, rstd_t, normed_t, query_t, key_t),
    )


MESH = pl.DeviceIdType.MESH
NZ, NY = 4, 2


def place():
    s, c = lax.axis_index("seq"), lax.axis_index("col")
    z, y, k = s // 4, lax.rem(s // 2, 2), lax.rem(s, 2)
    return z, y, k, c


def device(z, y, k, c):
    return (z * 4 + y * 2 + k, c)


def greet_all():
    z, y, k, c = place()
    me = (z * 4 + y * 2 + k) * 2 + c
    barrier = pltpu.get_barrier_semaphore()

    def signal(step, carry):
        other = lax.rem(me + step, 32)
        pl.semaphore_signal(
            barrier, inc=1, device_id=(other // 2, lax.rem(other, 2)), device_id_type=MESH
        )
        return carry

    lax.fori_loop(1, 32, signal, 0)
    return barrier


def remote(src, dst, send, recv, target):
    return pltpu.make_async_remote_copy(
        src_ref=src, dst_ref=dst, send_sem=send, recv_sem=recv, device_id=target, device_id_type=MESH
    )


ROWS, COLS, WIDE, HERE = 16, 512, 32, 512
PAIRS = 6
SLOTS = 1024
UP_TILE = 384


def iota(shape, dim):
    return lax.broadcasted_iota(jnp.int32, shape, dim)


def one_zero(test):
    return jnp.where(test, 1.0, 0.0)


def total_of(values):
    return jnp.sum(jnp.sum(values, 0, keepdims=True), 1, keepdims=True)


def half_lanes(values, side):
    lane = iota(values.shape, len(values.shape) - 1)
    keep = (lane < 64) if side == 0 else (lane >= 64)
    return jnp.where(keep, values.astype(F32), 0.0).astype(BF16)


def stacked(values):
    return jnp.concatenate([half_lanes(values, 0), half_lanes(values, 1)], 0)


def unstacked(values, count):
    lane = iota((count, 128), 1)
    return jnp.where(lane < 64, values[:count], values[count:])


def swap_blocks(first, second):
    lane = iota(first.shape, 1)
    low = jnp.where(lane < 64, first, pltpu.roll(second, 64, 1))
    high = jnp.where(lane < 64, pltpu.roll(first, 64, 1), second)
    return low, high


def split_heads_to(source, high_ref, low_ref):
    for rp in range(ROWS // 2):
        for hp in range(PAIRS):
            lanes = slice(hp * 128, hp * 128 + 128)
            first = source[rp * 64 : rp * 64 + 32, lanes]
            second = source[rp * 64 + 32 : rp * 64 + 64, lanes]
            for side, block in enumerate(swap_blocks(first, second)):
                top, rest = split_two(block)
                rows = slice((2 * hp + side) * 32, (2 * hp + side) * 32 + 32)
                high_ref[rows, rp * 128 : rp * 128 + 128] = top
                low_ref[rows, rp * 128 : rp * 128 + 128] = rest


def merge_heads(probs, hot_all, high_ref, low_ref):
    for rp in range(ROWS // 2):
        if rp % 2 == 0:
            blocks = nt(probs, hot_all[rp * 128 : rp * 128 + 256, :])
        block = blocks[:, (rp % 2) * 128 : (rp % 2) * 128 + 128]
        for hp in range(PAIRS):
            first = block[hp * 64 : hp * 64 + 32]
            second = block[hp * 64 + 32 : hp * 64 + 64]
            for side, part in enumerate(swap_blocks(first, second)):
                top, rest = split_two(part)
                rows = slice(rp * 64 + side * 32, rp * 64 + side * 32 + 32)
                high_ref[rows, hp * 128 : hp * 128 + 128] = top
                if low_ref is not None:
                    low_ref[rows, hp * 128 : hp * 128 + 128] = rest


def norm_rows(source, gain, bias, unit_ref, rstd_ref, normed_ref):
    def body(at, carry):
        rows = pl.ds(pl.multiple_of(at * 64, 64), 64)
        values = source[rows, :]
        centre = values - jnp.sum(values, -1, keepdims=True) * (1.0 / D)
        rstd = lax.rsqrt(jnp.sum(centre * centre, -1, keepdims=True) * (1.0 / D) + NORM_EPS)
        unit = centre * rstd
        unit_ref[rows, :] = unit
        rstd_ref[rows, :] = jnp.broadcast_to(rstd, (64, 128))
        normed_ref[rows, :] = (unit * gain + bias).astype(BF16)
        return carry

    lax.fori_loop(0, HERE // 64, body, 0, unroll=2)


def transpose_into(source, target):
    def body(at, carry):
        rows = pl.ds(pl.multiple_of(at * 128, 128), 128)
        target[:, rows] = source[rows, :].astype(F32).T.astype(BF16)
        return carry

    lax.fori_loop(0, HERE // 128, body, 0)


def over_tiles(width, tile, body):
    for half in range(2):

        def step(at, carry, half=half):
            body(half, pl.multiple_of(at * tile, tile))
            return carry

        lax.fori_loop(0, width // tile, step, 0)


def column_mask():
    rows, lanes = iota((256, 128), 0), iota((256, 128), 1)
    return ((rows & 127) >> 4) == (lanes >> 4)


class Saved(typing.NamedTuple):
    stream: typing.Any
    branch: typing.Any
    unit_1: typing.Any
    unit_2: typing.Any
    rstd_1: typing.Any
    rstd_2: typing.Any
    row_mixed_t: typing.Any
    col_normed_t: typing.Any
    col_mixed_t: typing.Any
    feed_normed_t: typing.Any
    col_proj: typing.Any
    col_prob: typing.Any
    active: typing.Any
    slope: typing.Any
    grad_head: typing.Any
    hot_all: typing.Any
    hot_ri: typing.Any
    hot_ir: typing.Any
    prob: typing.Any
    weight_hi: typing.Any
    value_two: typing.Any
    touch: typing.Any
    table: typing.Any
    norms: typing.Any
    proj_t: typing.Any
    extras: typing.Any
    moved: typing.Any


AT = Saved(*range(len(Saved._fields)))
SAVED = Saved(
    stream=((HERE, D), F32),
    branch=((HERE, D), BF16),
    unit_1=((HERE, D), F32),
    unit_2=((HERE, D), F32),
    rstd_1=((HERE, 128), F32),
    rstd_2=((HERE, 128), F32),
    row_mixed_t=((D, HERE), BF16),
    col_normed_t=((D, HERE), BF16),
    col_mixed_t=((D, HERE), BF16),
    feed_normed_t=((D, HERE), BF16),
    col_proj=((HERE, 3 * D), BF16),
    col_prob=((4 * PAIRS, 256, 128), F32),
    active=((HERE, FF), BF16),
    slope=((HERE, FF), BF16),
    grad_head=((VP, D), F32),
    hot_all=((ROWS * VP, COLS), BF16),
    hot_ri=((VP, HERE), BF16),
    hot_ir=((VP, HERE), BF16),
    prob=((HEADS * WIDE, COLS), F32),
    weight_hi=((HERE, D), BF16),
    value_two=((PAIRS, 128, 128), BF16),
    touch=((WIDE, COLS), F32),
    table=((VP, D), F32),
    norms=((8, D), F32),
    proj_t=((VP, 3 * D), BF16),
    extras=((8, 128), F32),
    moved=((8, D), F32),
)


class Forward(typing.NamedTuple):
    ids: typing.Any
    targets: typing.Any
    slots: typing.Any
    normed: typing.Any
    mixed: typing.Any
    normed_2: typing.Any
    mixed_2: typing.Any
    second_hot: typing.Any
    weight_lo: typing.Any
    left_hi: typing.Any
    left_lo: typing.Any
    lookup: typing.Any
    prob_low: typing.Any
    unit: typing.Any
    rstd: typing.Any


FORWARD = Forward(
    ids=((ROWS, COLS), jnp.int32),
    targets=((ROWS, 128), jnp.int32),
    slots=((8, SLOTS), jnp.int32),
    normed=((HERE, D), BF16),
    mixed=((HERE, D), BF16),
    normed_2=((HERE, D), BF16),
    mixed_2=((HERE, D), BF16),
    second_hot=((COLS, SLOTS), BF16),
    weight_lo=((HERE, D), BF16),
    left_hi=((HEADS * WIDE, ROWS * VP), BF16),
    left_lo=((HEADS * WIDE, ROWS * VP), BF16),
    lookup=((HERE, D), F32),
    prob_low=((HEADS * WIDE, COLS), BF16),
    unit=((HERE, D), F32),
    rstd=((HERE, 128), F32),
)


def position():
    z, y, k, c = place()
    me = (z * 4 + y * 2 + k) * 2 + c
    return z // 2, lax.rem(me, 16)


def read_tokens(small, f):
    alignment, block = position()
    side, part = block // 8, lax.rem(block // 4, 2)
    for r in range(ROWS):
        for cc in range(2):
            for q in range(2):
                lanes = slice(cc * 256 + q * 128, cc * 256 + q * 128 + 128)
                f.ids[r : r + 1, lanes] = small[r * 2 + cc, pl.ds(2 * alignment + q, 1), :]
        f.targets[r : r + 1, :] = small[r * 2 + side, pl.ds(4 + 2 * alignment + part, 1), :]
    lane = iota((1, 128), 1)
    for number in range(SLOTS // 128):
        for which in range(3):
            row = pl.ds(8 + 3 * alignment + which, 1)
            first = small[number * 4 + side, row, :]
            second = pltpu.roll(small[number * 4 + 2 + side, row, :], 64, 1)
            f.slots[which : which + 1, number * 128 : number * 128 + 128] = jnp.where(
                lane < 64, first, second
            )


def local_hot(values, shift):
    values = pltpu.roll(values, shift, 1)
    turned = [values] + [pltpu.roll(values, 32 * n, 1) for n in (1, 2, 3)]
    lane = iota((1, 128), 1)
    tiles = []
    for tile in range(4):
        row = turned[3][4 * tile + 3 : 4 * tile + 4]
        for n in (2, 1, 0):
            row = jnp.where(lane < 32 * n + 32, turned[n][4 * tile + n : 4 * tile + n + 1], row)
        tiles.append(row)
    row = jnp.concatenate(tiles, 1)
    return one_zero(row == iota((VP, HERE), 0)).astype(BF16)


def contact_part(contact_head, f, s, pair_count):
    _, block = position()
    base = block * WIDE
    head_sum = jnp.zeros((WIDE, COLS), F32)
    for h in range(HEADS):
        head_sum = head_sum + contact_head[h] * f.prob_low[h * 32 : h * 32 + 32, :].astype(F32)
    top, rest = split_two(head_sum)
    last = (head_sum - top.astype(F32) - rest.astype(F32)).astype(BF16)
    parts = jnp.concatenate([top, rest, last], 0)
    touch = jnp.zeros((WIDE, COLS), F32)
    bce = jnp.zeros((1, 1), F32)
    coef_sum = jnp.zeros((1, 1), F32)
    for number in range(SLOTS // 512):
        lanes = slice(number * 512, number * 512 + 512)
        first, label = (f.slots[n : n + 1, lanes] for n in (0, 2))
        second_hot = f.second_hot[:, lanes]
        picked = nn(parts, second_hot)
        picked = picked[:32] + picked[32:64] + picked[64:]
        first_hot = one_zero((first - base) == iota((WIDE, 512), 0))
        logit = jnp.sum(picked * first_hot, 0, keepdims=True) * COLS + contact_head[HEADS]
        owned = jnp.sum(first_hot, 0, keepdims=True) > 0.5
        valid = (label >= 0) & owned
        positive = one_zero(label == 1)
        small = jnp.exp(-jnp.abs(logit))
        soft = jnp.maximum(logit, 0.0) + jnp.log(1.0 + small)
        bce = bce + total_of(jnp.where(valid, soft - positive * logit, 0.0))
        sigmoid = jnp.where(logit >= 0.0, 1.0, small) / (1.0 + small)
        coef = jnp.where(valid, sigmoid - positive, 0.0) / pair_count
        coef_sum = coef_sum + total_of(coef)
        coef_top, coef_rest = split_two(first_hot * coef)
        touch = touch + nt(coef_top, second_hot) + nt(coef_rest, second_hot)
    s.touch[...] = touch
    column = iota((1, 128), 1)
    row = jnp.where(column == HEADS, coef_sum, 0.0)
    for h in range(HEADS):
        part = total_of(touch * f.prob_low[h * 32 : h * 32 + 32, :].astype(F32)) * COLS
        row = row + jnp.where(column == h, part, 0.0)
    return row, bce


def feature_order():
    shape = (384, 384)
    spot = iota(shape, 0)
    block = (spot * 2731) >> 16
    swapped = (block & 28) | ((block & 1) << 1) | ((block >> 1) & 1)
    return one_zero(spot + (swapped - block) * 24 == iota(shape, 1)).astype(BF16)


def forward_body(small, contact_head, weights, s, f, cells, projected, hook, emit):
    out_row, in_col, out_col = weights[:3]
    up_parts, down_parts = weights[3:5], weights[5:7]
    hook()
    features = cells()
    ahead = (
        ((iota((HERE, HERE), 0) >> 4) == (iota((HERE, HERE), 1) & 31))
        & ((iota((HERE, HERE), 0) & 15) == (iota((HERE, HERE), 1) >> 5))
    )
    ahead = one_zero(ahead).astype(BF16)
    read_tokens(small, f)
    _, block = position()
    shift = lax.rem(128 - lax.rem(block, 4) * 32, 128)
    window = pl.ds(pl.multiple_of((block // 4) * 128, 128), 128)
    hot_ri = local_hot(f.ids[:, window], shift)
    goal_ri = local_hot(f.targets[...], shift)
    s.hot_ri[...] = hot_ri
    for number in range(SLOTS // 512):
        lanes = slice(number * 512, number * 512 + 512)
        f.second_hot[:, lanes] = one_zero(f.slots[1:2, lanes] == iota((COLS, 512), 0)).astype(BF16)
    for r in range(ROWS):
        row = f.ids[r : r + 1, :]
        s.hot_all[r * VP : r * VP + VP, :] = one_zero(row == iota((VP, COLS), 0)).astype(BF16)
    shape = (HERE, HERE)
    back = (
        ((iota(shape, 1) >> 4) == (iota(shape, 0) & 31))
        & ((iota(shape, 1) & 15) == (iota(shape, 0) >> 5))
    )
    back = one_zero(back).astype(BF16)
    hot_ir = nn(hot_ri, back).astype(BF16)
    s.hot_ir[...] = hot_ir
    goal = nn(goal_ri, back)
    entries = jnp.zeros((4, 128), F32)
    labelled = jnp.zeros((1, 128), F32)
    for d in range(32):
        entries = entries + one_zero(small[d, 0:4, :] == MASK_ID)
        labelled = labelled + one_zero(small[d, 10:11, :] >= 0) + one_zero(small[d, 13:14, :] >= 0)
    entries, labelled = total_of(entries), total_of(labelled)

    hook()
    features = features[...].T
    table = features[:VP]
    norms = features[VP : VP + 8]
    s.table[...] = table
    s.norms[...] = norms
    table_low = table.astype(BF16)

    def vector(number):
        return norms[number : number + 1, :]

    hook()
    projected(s.proj_t)
    pair_parts = []
    for hp in range(PAIRS):
        lanes = slice(hp * 128, hp * 128 + 128)
        key = s.proj_t[:, D + hp * 128 : D + hp * 128 + 128]
        value = s.proj_t[:, 2 * D + hp * 128 : 2 * D + hp * 128 + 128]
        s.value_two[hp] = stacked(value)
        pair_parts.append(nt(s.proj_t[:, lanes], stacked(key)))
    pair_hi, pair_lo = split_two(jnp.concatenate(pair_parts, 1))
    hook()
    f.lookup[...] = tn(hot_ri, pair_hi) + tn(hot_ri, pair_lo)
    split_heads_to(f.lookup, f.left_hi, f.left_lo)
    hook()
    hot_all = s.hot_all[...]
    score = (nn(f.left_hi[...], hot_all) + nn(f.left_lo[...], hot_all)) * (HD * ROWS) ** (-0.5)
    score = jnp.exp(score - jnp.max(score, -1, keepdims=True))
    prob = score / jnp.sum(score, -1, keepdims=True)
    s.prob[...] = prob
    f.prob_low[...] = prob.astype(BF16)
    hook()
    merge_heads(f.prob_low[...], s.hot_all, s.weight_hi, f.weight_lo)
    hook()
    for hp in range(PAIRS):
        lanes = slice(hp * 128, hp * 128 + 128)
        value = s.value_two[hp]
        both = jnp.concatenate([s.weight_hi[:, lanes], f.weight_lo[:, lanes]], 1)
        f.mixed[:, lanes] = nn(both, jnp.concatenate([value, value], 0)).astype(BF16)
    f.mixed[...] = nn(ahead, f.mixed[...]).astype(BF16)
    s.stream[...] = tn(hot_ir, table_low)
    emit(AT.hot_all, AT.hot_ri, AT.hot_ir, AT.table, AT.norms, AT.proj_t, AT.value_two, AT.prob, AT.weight_hi)
    hook()
    for half in range(2):
        lanes = slice(half * 384, half * 384 + 384)
        s.stream[:, lanes] += nn(f.mixed[...], out_row[half])
    norm_rows(s.stream, vector(1), vector(5), s.unit_1, s.rstd_1, f.normed)
    emit(AT.unit_1, AT.rstd_1)

    def project(half, at):
        s.col_proj[:, half * 1152 + at : half * 1152 + at + 384] = nn(
            f.normed[...], in_col[half, :, at : at + 384]
        ).astype(BF16)

    for third in range(3):
        hook()
        for half in range(2):
            project(half, third * 384)
    emit(AT.col_proj)

    def attend(at, carry):
        rows = pl.ds(pl.multiple_of((at // PAIRS) * 128, 128), 128)
        lane = lax.rem(at, PAIRS) * 128

        def lanes(part):
            return pl.ds(pl.multiple_of(part * D + lane, 128), 128)

        query = stacked(s.col_proj[rows, lanes(0)])
        score = nt(query, s.col_proj[rows, lanes(1)]) * HD ** (-0.5)
        score = jnp.where(column_mask(), score, -1e30)
        score = jnp.exp(score - jnp.max(score, -1, keepdims=True))
        prob = score / jnp.sum(score, -1, keepdims=True)
        s.col_prob[at] = prob
        mixed = nn(prob.astype(BF16), s.col_proj[rows, lanes(2)])
        f.mixed_2[rows, lanes(0)] = unstacked(mixed, 128).astype(BF16)
        return carry

    for part in range(4):
        hook()
        lax.fori_loop(part * PAIRS, part * PAIRS + PAIRS, attend, 0, unroll=3)
    hook()
    emit(AT.col_prob)
    for half in range(2):
        lanes = slice(half * 384, half * 384 + 384)
        s.stream[:, lanes] += nn(f.mixed_2[...], out_col[half])
    norm_rows(s.stream, vector(2), vector(6), s.unit_2, s.rstd_2, f.normed_2)
    emit(AT.unit_2, AT.rstd_2)
    hook()
    contact_row, bce = contact_part(contact_head, f, s, labelled)
    emit(AT.touch)
    for part in range(2):

        def widen(half, at, part=part):
            lanes = slice(part * 1536 + half * 768 + at, part * 1536 + half * 768 + at + UP_TILE)
            up = nn(f.normed_2[...], up_parts[part][half, :, at : at + UP_TILE])
            active, slope = gelu_parts(up)
            s.active[:, lanes] = active.astype(BF16)
            s.slope[:, lanes] = slope.astype(BF16)

        for half in range(2):
            hook()
            for at in range(0, 768, UP_TILE):
                widen(half, at)
        hook()
        if part == 0:
            transpose_into(f.mixed, s.row_mixed_t)
            transpose_into(f.normed, s.col_normed_t)
            emit(AT.row_mixed_t, AT.col_normed_t)
        else:
            transpose_into(f.mixed_2, s.col_mixed_t)
            emit(AT.col_mixed_t)

    emit(AT.active, AT.slope)
    for part, at, size in ((0, 0, 768), (1, 0, 384), (1, 384, 384)):
        hook()
        added = []
        for half in range(2):
            start = part * 1536 + half * 768 + at
            matrix = down_parts[part][half, :, at : at + size]
            added.append(nt(s.active[:, start : start + size], matrix))
        s.stream[...] += added[0] + added[1]
        if part == 0:
            hook()
            transpose_into(f.normed_2, s.feed_normed_t)
            emit(AT.feed_normed_t)
    hook()
    norm_rows(s.stream, vector(3), vector(7), f.unit, f.rstd, f.normed)
    logits = nt(table_low, f.normed[...]) * D ** (-0.5)
    vocab = iota((VP, HERE), 0)
    logits = jnp.where(vocab < VOCAB, logits, -1e30)
    shifted = logits - jnp.max(logits, 0, keepdims=True)
    log_probs = shifted - jnp.log(jnp.sum(jnp.exp(shifted), 0, keepdims=True))
    keep = hot_ir[MASK_ID : MASK_ID + 1].astype(F32) > 0.5
    mlm = -total_of(jnp.where(keep & (goal > 0.5), log_probs, 0.0))
    logit_grad = jnp.where(keep, jnp.exp(log_probs) - goal, 0.0) / entries
    logit_low = (logit_grad * D ** (-0.5)).astype(BF16)
    s.grad_head[...] = nn(logit_low, f.normed[...])
    hook()
    f.lookup[...] = tn(logit_low, table_low)
    scale_3, shift_3 = back_rows(f.unit, f.rstd, vector(3), f.lookup, s.stream, s.branch, True)
    emit(AT.stream, AT.branch)
    line = iota((8, D), 0)
    s.moved[...] = jnp.where(line == 0, scale_3, jnp.where(line == 1, shift_3, 0.0))
    column = iota((1, 128), 1)
    row = contact_row + jnp.where(column == HEADS + 1, mlm, 0.0) + jnp.where(column == HEADS + 2, bce, 0.0)
    counted = jnp.where(column == 0, entries, 0.0) + jnp.where(column == 1, labelled, 0.0)
    line = iota((8, 128), 0)
    s.extras[...] = jnp.where(line == 0, row, jnp.where(line == 1, counted, 0.0))
    emit(AT.grad_head, AT.extras, AT.moved)
    hook()


def back_rows(unit_ref, rstd_ref, gain, upstream_ref, stream_ref, low_ref, first):
    def body(at, carry):
        scale, move = carry
        rows = pl.ds(pl.multiple_of(at * 64, 64), 64)
        upstream = upstream_ref[rows, :]
        unit = unit_ref[rows, :]
        inner = upstream * gain
        mean = jnp.sum(inner, -1, keepdims=True) * (1.0 / D)
        along = jnp.sum(inner * unit, -1, keepdims=True) * (1.0 / D)
        grad = rstd_ref[rows, 0:1] * (inner - mean - unit * along)
        if not first:
            grad = grad + stream_ref[rows, :]
        stream_ref[rows, :] = grad
        low_ref[rows, :] = grad.astype(BF16)
        touched = upstream * unit
        for n in range(8):
            scale = scale + touched[n * 8 : n * 8 + 8]
            move = move + upstream[n * 8 : n * 8 + 8]
        return scale, move

    zero = jnp.zeros((8, D), F32)
    scale, move = lax.fori_loop(0, HERE // 64, body, (zero, zero), unroll=2)
    return jnp.sum(scale, 0, keepdims=True), jnp.sum(move, 0, keepdims=True)


MATRICES = (128, 384, 1152, 384, 768, 768, 768, 768)
UNITS = (
    (0, 0, 128, True),
    (1, 0, 384, False),
    (2, 0, 384, True),
    (2, 384, 384, True),
    (2, 768, 384, True),
    (3, 0, 384, False),
    (4, 0, 768, True),
    (5, 0, 768, True),
    (6, 0, 768, True),
    (7, 0, 384, True),
    (7, 384, 384, True),
)
Z_LAST = {9: 1, 10: 2}
FORWARD_ORDER = (
    ((0, 0), (0, 2), (0, 11), (1, 0), (0, 1), (0, 9), (0, 10), (1, 11), (2, 0), (0, 3), (1, 2), (0, 4), (2, 11), (3, 0), (1, 10), (1, 9), (1, 1), (4, 0),),
    ((2, 2), (0, 5), (2, 1),),
    ((3, 11), (1, 3), (0, 6), (3, 2), (4, 11), (1, 4),),
    ((3, 1), (4, 2), (1, 5), (0, 7),),
    ((4, 1), (2, 3), (2, 4),),
    ((1, 6), (0, 8),),
    (),
    ((3, 3),),
    ((3, 4), (2, 5), (4, 3), (2, 9), (1, 7), (4, 4),),
    (),
    (),
    (),
    ((3, 5), (2, 6),),
    (),
    ((4, 5), (2, 7), (2, 10),),
    ((1, 8),),
    ((3, 6),),
    ((3, 9), (3, 7), (4, 6),),
    (),
    ((2, 8), (4, 9),),
    ((4, 7),),
    (),
    (),
    ((3, 8), (3, 10), (4, 8),),
    ((4, 10),),
    (),
    (),
    (),
    (),
    (),
)


def spot(paired, cc, zz, yy, k):
    return (k, zz, yy, cc) if paired else (cc, zz, yy, k)


def forward_kernel(*refs):
    count, parts = len(UNITS), len(MATRICES)
    raw = refs[:11]
    contact_head = refs[11]
    at = 12
    far = (None, *refs[at : at + parts - 1])
    saved_far = refs[at + parts - 1 : at + parts - 1 + len(SAVED)]
    at += parts - 1 + len(SAVED)
    outs = refs[at : at + parts]
    at += parts
    outgoing = refs[at : at + count]
    incoming = refs[at + count : at + 2 * count]
    piece = refs[at + 2 * count : at + 3 * count]
    at += 3 * count
    saved = Saved(*refs[at : at + len(SAVED)])
    at += len(SAVED)
    scratch = Forward(*refs[at : at + len(FORWARD)])
    at += len(FORWARD)
    near = refs[at : at + 11]
    at += 11
    small, small_out, corner, features, stat, stat_got, part, part_got, part_line, proj, room = refs[at : at + 11]
    small_send, small_recv, send, recv, local, out_sem, raw_sem, twin_send, twin_recv = refs[at + 11 :]
    tokens, targets, masked, pairs, labels, table, norms, in_w, out_w, up_w, down_w = near
    z, y, k, c = place()
    me = (z * 4 + y * 2 + k) * 2 + c
    barrier = greet_all()
    raw_copies = [pltpu.make_async_copy(a, b, raw_sem.at[n]) for n, (a, b) in enumerate(zip(raw, near))]
    for item in raw_copies:
        item.start()
    for item in raw_copies[:7]:
        item.wait()
    small[...] = jnp.full(small.shape, -1, jnp.int32)
    for micro in range(2):
        for half in range(2):
            lanes = slice(half * 128, half * 128 + 128)
            row = 2 * micro + half
            small[row : row + 1, :] = jnp.where(
                masked[micro, :, lanes] > 0, MASK_ID, tokens[micro, :, lanes]
            )
            small[4 + row : 5 + row, :] = targets[micro, :, lanes]
        row = 8 + 3 * micro
        for which in range(2):
            small[row + which : row + which + 1, 0:64] = pairs[micro, which : which + 1, :]
        small[row + 2 : row + 3, 0:64] = labels[micro : micro + 1, :]
    corner[...] = jnp.zeros(corner.shape, F32)
    corner[0:8, 0:24] = norms[...]
    vectors = pltpu.roll(corner[...].T[:24], 64, 1)
    corner[0:8, 0:24] = jnp.zeros((8, 24), F32)
    corner[0:24, 0:VOCAB] = table[...]
    mine_rows = (corner[0:24, :] + vectors).astype(BF16).astype(F32)
    table_rows = jnp.where(iota((24, 128), 1) < VP, mine_rows, 0.0)
    gain, bias = mine_rows[:, 64:65], mine_rows[:, 68:69]
    piece[0][0:16, :] = small[...].astype(F32)
    piece[0][16:40, :] = mine_rows
    mean = jnp.sum(table_rows, 0, keepdims=True) * (1.0 / 24)
    centre = table_rows - mean
    spread = jnp.sum(centre * centre, 0, keepdims=True)
    line = iota((8, 128), 0)
    stat[...] = jnp.where(line == 0, mean, jnp.where(line == 1, spread, 0.0))
    def master(u, side):
        matrix, start, n, _ = UNITS[u]
        width = MATRICES[matrix]
        if matrix == 2:
            return in_w[1, :, side * 1152 + start : side * 1152 + start + n]
        if matrix in (1, 3):
            rows = out_w[matrix // 2, :, side * 384 : side * 384 + 384].astype(BF16)
            return nn(rows, order)
        begin = (matrix % 2) * 1536 + side * width + start
        return (up_w if matrix < 6 else down_w)[:, begin : begin + n]

    def mine(u):
        return k if UNITS[u][3] else c

    def set_out(u):
        other = jnp.where(mine(u) == 0, master(u, 1), master(u, 0))
        other = jnp.concatenate([other, jnp.zeros((8, UNITS[u][2]), F32)], 0)
        outgoing[u][...] = other.astype(BF16)

    pl.semaphore_wait(barrier, 31)

    def stat_copy(step):
        other = lax.rem(me + step, 32)
        return remote(
            stat, stat_got.at[me], small_send.at[0, step], small_recv.at[0, step], (other // 2, lax.rem(other, 2))
        )

    chip = (z * 2 + y) * 2 + c

    def chip_copy(phase, step):
        other = lax.rem(chip + step, 16)
        target = device(other // 4, lax.rem(other // 2, 2), k, lax.rem(other, 2))
        if phase == 1:
            src, dst = part.at[k, other], part_line.at[chip]
        else:
            src, dst = proj.at[k, chip], proj.at[k, chip]
        return remote(src, dst, small_send.at[phase, step], small_recv.at[phase, step], target)

    def each(last, action):
        def body(step, carry):
            action(step)
            return carry

        lax.fori_loop(1, last, body, 0)

    each(32, lambda step: stat_copy(step).start())

    across, beside, twin = device(z, y, k, 1 - c), device(z, 1 - y, k, c), device(z, y, 1 - k, c)

    def block(u, cc, zz, yy):
        matrix, start, n, paired = UNITS[u]
        where = spot(paired, cc, zz, yy, k)
        if n == MATRICES[matrix]:
            return outs[matrix].at[where]
        return outs[matrix].at[(*where, slice(None), pl.ds(start, n))]

    def copy(u, at, src, dst, target):
        return remote(src, dst, send.at[u, at], recv.at[u, at], target)

    def pair_copy(u):
        return copy(u, 0, outgoing[u], incoming[u], twin if UNITS[u][3] else across)

    def own_copy(u):
        return pltpu.make_async_copy(piece[u], block(u, c, z, y), local.at[u])

    def line_copy(u, step):
        return copy(u, step, piece[u], block(u, c, z, y), device(lax.rem(z + step, 4), y, k, c))

    def same(u, at, cc, zz, yy, target):
        view = block(u, cc, zz, yy)
        return copy(u, at, view, view, target)

    low, high, every = pl.ds(0, 2), pl.ds(2, 2), slice(None)

    def second(u):
        return [same(u, 4, c, low, y, across), same(u, 5, c, high, y, beside)]

    def third_own(u):
        return [same(u, 6, c, low, y, beside), same(u, 7, c, high, y, across)]

    def third_far(u):
        return [same(u, 8, 1 - c, low, y, beside), same(u, 9, c, high, 1 - y, across)]

    def twin_own(u):
        return [same(u, 10, c, every, y, twin)]

    def twin_second(u):
        return [same(u, 11, 1 - c, low, y, twin), same(u, 12, c, high, 1 - y, twin)]

    def twin_third(u):
        return [
            same(u, 13, c, low, 1 - y, twin),
            same(u, 14, 1 - c, high, y, twin),
            same(u, 15, 1 - c, low, 1 - y, twin),
            same(u, 16, 1 - c, high, 1 - y, twin),
        ]

    own_copy(0).start()
    for item in raw_copies[7:]:
        item.wait()
    order = feature_order()
    for u in range(1, count):
        set_out(u)
        pair_copy(u).start()

    def part_twin():
        return remote(part.at[1 - k], part_got, twin_send.at[0], twin_recv.at[0], twin)

    def proj_twin():
        return remote(proj.at[k], proj.at[k], twin_send.at[1], twin_recv.at[1], twin)

    def project_part():
        stat_got[me] = stat[...]
        each(32, lambda step: stat_copy(step).wait())
        means = jnp.zeros((1, 128), F32)
        spreads = jnp.zeros((1, 128), F32)
        for d in range(32):
            means = means + stat_got[d, 0:1, :]
            spreads = spreads + stat_got[d, 1:2, :]
        means = means * (1.0 / 32)
        for d in range(32):
            away = stat_got[d, 0:1, :] - means
            spreads = spreads + 24.0 * away * away
        rstd = lax.rsqrt(spreads * (1.0 / D) + NORM_EPS)
        normed = (table_rows - means) * rstd * gain + bias
        normed = jnp.concatenate([normed, jnp.zeros((8, 128), F32)], 0).astype(BF16)
        for block_at in range(6):
            lanes = slice(block_at * 384, block_at * 384 + 384)
            rows = jnp.concatenate([in_w[0, :, lanes], jnp.zeros((8, 384), F32)], 0).astype(BF16)
            product = tn(normed, rows)
            for group in range(5):
                number = group * 6 + block_at
                part[number // 16, number % 16] = product[group * 8 : group * 8 + 8]
        for number in (30, 31):
            part[number // 16, number % 16] = jnp.zeros((8, 384), F32)
        part_twin().start()

    def project_chip():
        part_twin().wait_recv()
        part[k] = part[k] + part_got[...]
        each(16, lambda step: chip_copy(1, step).start())

    def project_line():
        part_line[chip] = part[k, chip]
        each(16, lambda step: chip_copy(1, step).wait_recv())
        proj[k, chip] = lax.fori_loop(1, 16, lambda at, held: held + part_line[at], part_line[0])
        each(16, lambda step: chip_copy(2, step).start())

    def project_twin():
        each(16, lambda step: chip_copy(2, step).wait_recv())
        proj_twin().start()

    def project_end():
        proj_twin().wait_recv()

    projecting = (project_part, project_chip, project_line, project_twin, project_end)

    def cells():
        for d in range(32):
            at = ((d // 2) % 2, d // 8, (d // 4) % 2, d % 2)
            small_out[d] = outs[0][(*at, slice(0, 16))].astype(jnp.int32)
            start = (((at[1] * 2 + at[2]) * 2 + at[3]) * 2 + at[0]) * 24
            features[start : start + 24, :] = outs[0][(*at, slice(16, 40))]
        return features

    def projected(target):
        room[40:64, :] = jnp.zeros((24, 3 * D), F32)
        for number in range(30):
            rows, lanes = (number // 6) * 8, (number % 6) * 384
            room[rows : rows + 8, lanes : lanes + 384] = proj[number // 16, number % 16]
        target[...] = room[...].astype(BF16)

    def to_across(u):
        return copy(u, 4, piece[u], block(u, c, z, y), across)

    def to_beside(u):
        return copy(u, 5, piece[u], block(u, c, z, y), beside)

    def to_corner(u):
        if Z_LAST[u] == 1:
            return same(u, 6, 1 - c, z, y, beside)
        return same(u, 6, c, z, 1 - y, across)

    def to_line(u):
        return [
            same(u, step, every, z, every, device(lax.rem(z + step, 4), y, k, c)) for step in (1, 3, 2)
        ]

    def to_twin(u):
        return [same(u, 7, every, z, every, twin)]

    def rest_to_twin(u):
        return [same(u, 7 + step, every, lax.rem(z + 4 - step, 4), every, twin) for step in (1, 3, 2)]

    def stage_line(u):
        if u == 0:
            for step in (1, 3, 2):
                line_copy(u, step).start()
            return
        pair_copy(u).wait_recv()
        side = mine(u)
        own = jnp.where(side == 0, master(u, 0), master(u, 1))
        theirs = incoming[u][...].astype(F32)[:24]
        top = jnp.where(side == 0, own, theirs)
        bottom = jnp.where(side == 0, theirs, own)
        piece[u][...] = jnp.concatenate([top, bottom], 0).astype(BF16)
        own_copy(u).start()
        if u in Z_LAST:
            to_across(u).start()
            to_beside(u).start()
            return
        for step in (1, 3, 2):
            line_copy(u, step).start()

    def stage_second(u):
        own_copy(u).wait()
        if u in Z_LAST:
            to_across(u).wait_recv()
            to_beside(u).wait_recv()
            to_corner(u).start()
            return
        for step in (1, 3, 2):
            line_copy(u, step).wait_recv()
        for item in second(u) + third_own(u) + twin_own(u):
            item.start()

    def stage_third(u):
        if u in Z_LAST:
            to_corner(u).wait_recv()
            for item in to_line(u) + to_twin(u):
                item.start()
            return
        for item in second(u):
            item.wait_recv()
        for item in third_far(u) + twin_second(u):
            item.start()

    def stage_twin(u):
        if u in Z_LAST:
            for item in to_line(u):
                item.wait_recv()
            for item in rest_to_twin(u):
                item.start()
            return
        for item in third_own(u) + third_far(u):
            item.wait_recv()
        for item in twin_third(u):
            item.start()

    def far_copy(matrix):
        return pltpu.make_async_copy(outs[matrix], far[matrix], local.at[count + matrix])

    def stage_end(u):
        if u in Z_LAST:
            for item in to_twin(u) + rest_to_twin(u):
                item.wait_recv()
            sent = [to_across(u), to_beside(u), to_corner(u)] + to_line(u) + to_twin(u)
        else:
            for item in twin_own(u) + twin_second(u) + twin_third(u):
                item.wait_recv()
            sent = [line_copy(u, step) for step in (1, 2, 3)]
            sent += second(u) + third_own(u) + third_far(u) + twin_own(u) + twin_second(u)
        for item in sent if u == 0 else [pair_copy(u)] + sent:
            item.wait_send()
        if u == 0:
            return
        if u + 1 == count or UNITS[u + 1][0] != UNITS[u][0]:
            far_copy(UNITS[u][0]).start()

    stages = (stage_line, stage_second, stage_third, stage_twin, stage_end)
    pending = list(FORWARD_ORDER)

    def hook():
        for stage, u in pending.pop(0):
            if u == count:
                projecting[stage]()
            else:
                stages[stage](u)

    def out_copy(at):
        return pltpu.make_async_copy(saved[at], saved_far[at], out_sem.at[at])

    def emit(*numbers):
        for number in numbers:
            out_copy(number).start()

    views = [w.reshape(2, D, n) for w, n in zip(outs[1:], MATRICES[1:])]
    forward_body(small_out, contact_head, views, saved, scratch, cells, projected, hook, emit)
    part_twin().wait_send()
    proj_twin().wait_send()
    for phase in (1, 2):
        each(16, lambda step, phase=phase: chip_copy(phase, step).wait_send())
    assert not pending
    for u in range(count):
        for item in rest_to_twin(u) if u in Z_LAST else twin_third(u):
            item.wait_send()
    for matrix in range(1, parts):
        far_copy(matrix).wait()
    for at in range(len(SAVED)):
        out_copy(at).wait()


def forward_call(raw, contact_head):
    count, parts = len(UNITS), len(MATRICES)
    anywhere = pl.BlockSpec(memory_space=pl.ANY)
    shapes = [(2, NZ, NY, 2, 48, n) for n in MATRICES[1:]]
    widths = [n for _, _, n, _ in UNITS]
    outs = pl.pallas_call(
        forward_kernel,
        out_shape=[jax.ShapeDtypeStruct(shape, BF16) for shape in shapes]
        + [jax.ShapeDtypeStruct(*item) for item in SAVED],
        in_specs=[anywhere] * 11 + [pl.BlockSpec(memory_space=pltpu.SMEM)],
        out_specs=[anywhere] * (parts - 1 + len(SAVED)),
        scratch_shapes=[pltpu.VMEM((2, NZ, NY, 2, 40, 128), F32)]
        + [pltpu.VMEM(shape, BF16) for shape in shapes]
        + [pltpu.VMEM((32, n), BF16) for n in widths] * 2
        + [pltpu.VMEM((40, 128), F32)]
        + [pltpu.VMEM((48, n), BF16) for n in widths[1:]]
        + [pltpu.VMEM(*item) for item in SAVED]
        + [pltpu.VMEM(*item) for item in FORWARD]
        + [pltpu.VMEM(item.shape, item.dtype) for item in raw]
        + [
            pltpu.VMEM((16, 128), jnp.int32),
            pltpu.VMEM((32, 16, 128), jnp.int32),
            pltpu.VMEM((128, 128), F32),
            pltpu.VMEM((D, 128), F32),
            pltpu.VMEM((8, 128), F32),
            pltpu.VMEM((32, 8, 128), F32),
            pltpu.VMEM((2, 16, 8, 384), F32),
            pltpu.VMEM((16, 8, 384), F32),
            pltpu.VMEM((16, 8, 384), F32),
            pltpu.VMEM((2, 16, 8, 384), F32),
            pltpu.VMEM((VP, 3 * D), F32),
            pltpu.SemaphoreType.DMA((3, 32)),
            pltpu.SemaphoreType.DMA((3, 32)),
            pltpu.SemaphoreType.DMA((count, 17)),
            pltpu.SemaphoreType.DMA((count, 17)),
            pltpu.SemaphoreType.DMA((count + parts,)),
            pltpu.SemaphoreType.DMA((len(SAVED),)),
            pltpu.SemaphoreType.DMA((len(raw),)),
            pltpu.SemaphoreType.DMA((2,)),
            pltpu.SemaphoreType.DMA((2,)),
        ],
        compiler_params=pltpu.CompilerParams(
            collective_id=0, has_side_effects=True, vmem_limit_bytes=62 * 2**20
        ),
    )(*raw, contact_head)
    return outs[: parts - 1], Saved(*outs[parts - 1 :])


def summed_rows(sums, group):
    return jnp.concatenate([sums[3 * group + third] for third in range(3)], 1).astype(F32)


def table_finish(sums, room, table_ref, norms_ref, proj_t, in_row, g_in, g_norm, send_stat):
    z, y, k, c = place()
    me = ((z * 2 + y) * 2 + c) * 2 + k
    room[0:128, :] = jnp.zeros((128, D), F32)
    for number in range(2):
        room[4 + 16 * number : 20 + 16 * number, :] = summed_rows(sums, number)
        room[68 + 16 * number : 84 + 16 * number, :] = summed_rows(sums, 2 + number)
    pair = room[0:64, :]
    value_grad = room[64:128, :]
    vectors = summed_rows(sums, 6)
    vectors = vectors[:8] + vectors[8:]
    line = iota((8, D), 0)
    table_grad = jnp.concatenate(
        [
            summed_rows(sums, 4),
            summed_rows(sums, 5),
            jnp.where(line == 0, vectors[7:8], 0.0),
            jnp.zeros((24, D), F32),
        ],
        0,
    )
    pair_hi, pair_lo = split_two(pair)
    scale = (HD * ROWS) ** (-0.5)
    query_grad, key_grad = [], []
    for hp in range(PAIRS):
        lanes = slice(hp * 128, hp * 128 + 128)
        query = proj_t[:, lanes]
        key = stacked(proj_t[:, D + hp * 128 : D + hp * 128 + 128])
        high, low = pair_hi[:, lanes], pair_lo[:, lanes]
        query_grad.append((nn(high, key) + nn(low, key)) * scale)
        key_grad.append(unstacked(tn(high, query) + tn(low, query), VP) * scale)
    proj_hi, proj_lo = split_two(jnp.concatenate(query_grad + key_grad + [value_grad], 1))
    shard = D // 32
    pick = one_zero(iota((shard, D), 1) == iota((shard, D), 0) + me * shard).astype(BF16)
    weight = in_row[...].astype(BF16)
    back_t = nt(weight, proj_hi) + nt(weight, proj_lo)
    back = nt(proj_hi, weight) + nt(proj_lo, weight)
    table = table_ref[...]
    table_low = table.astype(BF16)
    unit, rstd = norm_stats(table)
    mean = jnp.sum(table, -1, keepdims=True) * (1.0 / D)
    same = iota((VP, VP), 0) == iota((VP, VP), 1)

    def as_row(column):
        return jnp.sum(jnp.where(same, column, 0.0), 0, keepdims=True)

    rstd_row = as_row(rstd)
    unit_t = (nt(pick, table_low) - as_row(mean)) * rstd_row
    unit_mine = (nt(table_low, pick) - mean) * rstd
    norms = jnp.concatenate([norms_ref[...], jnp.zeros((8, D), F32)], 0).astype(BF16)
    inner = back_t * nt(pick, norms)[:, 0:1]

    def three(values):
        top, rest = split_two(values)
        return top, rest, (values - top.astype(F32) - rest.astype(F32)).astype(BF16)

    emb_grad = sum(nt(pick, part) for part in three(table_grad))
    before = emb_grad + rstd_row * inner
    parts = (inner, inner * unit_t, before, before * unit_t, unit_t, unit_t * unit_t, before * before)
    send_stat([jnp.sum(part, 0, keepdims=True) for part in parts])
    scale_0 = jnp.sum(back * unit_mine, 0, keepdims=True)
    shift_0 = jnp.sum(back, 0, keepdims=True)
    line = iota((16, D), 0)
    norm_grad = jnp.zeros((16, D), F32)
    for number, source in ((1, 0), (2, 1), (3, 2), (5, 3), (6, 4), (7, 5)):
        norm_grad = jnp.where(line == number, vectors[source : source + 1], norm_grad)
    normed = (unit * norms_ref[0:1, :] + norms_ref[4:5, :]).astype(BF16)
    mine = nt(pick, normed).astype(BF16)
    in_grad = nn(mine, proj_hi) + nn(mine, proj_lo)
    g_in[...] = in_grad
    own_norm = sum(nt(part, pick) for part in three(norm_grad))[:8]
    line = iota((8, shard), 0)
    own_norm = jnp.where(line == 0, scale_0, jnp.where(line == 4, shift_0, own_norm))
    g_norm[...] = own_norm
    found = total_of(in_grad * in_grad) + total_of(own_norm * own_norm)
    return inner, unit_t, rstd_row, emb_grad, found


PIECES = 21
GRAD_WIDTHS = (768, 768, 768, 768, 384, 1152, 384)
GRAD_UNITS = (
    (0, 0, 384, True),
    (0, 384, 384, True),
    (1, 0, 768, True),
    (2, 0, 768, True),
    (3, 0, 768, True),
    (4, 0, 384, False),
    (5, 0, 384, True),
    (5, 384, 384, True),
    (5, 768, 384, True),
    (6, 0, 384, False),
)
Z_FIRST = {1: 1, 5: 2}
BACKWARD_ORDER = (
    (),
    (),
    (),
    (),
    (),
    (),
    ((0, 0),),
    (),
    ((0, 1),),
    (),
    (),
    ((1, 0),),
    (),
    (),
    ((0, 2), (2, 0),),
    (),
    (),
    ((0, 3),),
    (),
    (),
    ((0, 4), (1, 1), (1, 2),),
    ((0, 5),),
    (),
    (),
    ((1, 3),),
    (),
    (),
    (),
    (),
    ((1, 4),),
    ((2, 1),),
    ((0, 6),),
    ((2, 2), (1, 5), (0, 7),),
    ((0, 8),),
    ((2, 3),),
    ((2, 4), (0, 9),),
    (),
    ((2, 5), (1, 6),),
    ((1, 7),),
    ((3, 0), (3, 1), (3, 2), (3, 3), (1, 8), (4, 0), (4, 1), (4, 2), (4, 3), (1, 9), (3, 5), (2, 6), (3, 4), (4, 4), (2, 7), (5, 0), (2, 8), (2, 9), (3, 6), (4, 5), (4, 6), (3, 7), (4, 7), (6, 0), (3, 8), (3, 9), (4, 8), (4, 9),),
)


class Kept(typing.NamedTuple):
    stream: typing.Any
    norms: typing.Any
    table: typing.Any
    proj_t: typing.Any
    extras: typing.Any
    moved: typing.Any
    grad_head: typing.Any
    touch: typing.Any
    value_two: typing.Any


class Early(typing.NamedTuple):
    slope: typing.Any
    active: typing.Any
    feed_normed_t: typing.Any
    unit_2: typing.Any
    rstd_2: typing.Any
    col_mixed_t: typing.Any
    col_proj: typing.Any
    col_prob: typing.Any
    col_normed_t: typing.Any
    unit_1: typing.Any
    rstd_1: typing.Any


class Late(typing.NamedTuple):
    row_mixed_t: typing.Any
    hot_all: typing.Any
    weight_hi: typing.Any
    prob: typing.Any
    hot_ri: typing.Any
    hot_ir: typing.Any


def pick_items(group, source):
    return [getattr(source, name) for name in group._fields]


def backward_kernel(*refs):
    widths = GRAD_WIDTHS
    count = len(widths)
    contact_head = refs[0]
    far = refs[1 : 1 + count]
    in_row_far = refs[1 + count]
    saved = Saved(*refs[2 + count : 2 + count + len(SAVED)])
    at = 2 + count + len(SAVED)
    outs = refs[at : at + count]
    g_in, g_emb, g_norm, stats = refs[at + count : at + count + 4]
    at += count + 4
    grads = refs[at : at + count]
    kept = Kept(*refs[at + count : at + count + len(Kept._fields)])
    at += count + len(Kept._fields)
    upstream, branch, branch_t, mixed = refs[at : at + 4]
    scratch = refs[at + 4 :]
    units = len(GRAD_UNITS)
    got_0, got_1a, got_1b, got_2a, got_2b, got_3, total, got_4 = (
        scratch[i * units : (i + 1) * units] for i in range(8)
    )
    table, table_out, table_got, square, square_got, stat, stat_got, late_rows = scratch[8 * units : 8 * units + 8]
    table_send, table_recv, send, recv, local = scratch[8 * units + 8 :]
    z, y, k, c = place()
    me = (z * 4 + y * 2 + k) * 2 + c
    across, beside, twin = device(z, y, k, 1 - c), device(z, 1 - y, k, c), device(z, y, 1 - k, c)
    barrier = greet_all()
    stream = kept.stream
    square[...] = jnp.zeros(square.shape, F32)

    copies = {}

    def load(number, source, target):
        copies[number] = pltpu.make_async_copy(source, target, local.at[number])
        copies[number].start()

    def need(*numbers):
        for number in numbers:
            copies[number].wait()

    def weight(m):
        return len(SAVED) + m

    def copy(m, at, src, dst, target):
        return remote(src, dst, send.at[m, at], recv.at[m, at], target)

    low, high = pl.ds(0, 2), pl.ds(2, 2)
    every = slice(None)

    def where(u, cc, zz, yy):
        matrix, start, n, paired = GRAD_UNITS[u]
        index = spot(paired, cc, zz, yy, k)
        return index if n == widths[matrix] else (*index, every, pl.ds(start, n))

    def block(u, cc, zz, yy):
        return grads[GRAD_UNITS[u][0]].at[where(u, cc, zz, yy)]

    def ordered(u, cc, rest):
        return (*rest, cc) if GRAD_UNITS[u][3] else (cc, *rest)

    def twin_copy(u):
        matrix, start, n, paired = GRAD_UNITS[u]
        index = (1 - k,) if paired else (every, every, every, 1 - k)
        if n != widths[matrix]:
            index = (*index, *(every,) * (5 - len(index)), pl.ds(start, n))
        return copy(u, 0, grads[matrix].at[index], got_0[u], twin)

    def first(u):
        return [
            copy(u, 1, block(u, every, low, 1 - y), got_1a[u], beside),
            copy(u, 2, block(u, 1 - c, high, every), got_1b[u], across),
        ]

    def second(u):
        return [
            copy(u, 3, block(u, 1 - c, low, y), got_2a[u], across),
            copy(u, 4, block(u, c, high, 1 - y), got_2b[u], beside),
        ]

    def along(u):
        return [
            copy(
                u,
                4 + step,
                block(u, c, lax.rem(z + step, 4), y),
                got_3[u].at[step - 1],
                device(lax.rem(z + step, 4), y, k, c),
            )
            for step in (1, 3, 2)
        ]

    def z_first(u):
        return [
            copy(
                u,
                step,
                block(u, every, lax.rem(z + step, 4), every),
                got_1a[u].at[step - 1],
                device(lax.rem(z + step, 4), y, k, c),
            )
            for step in (1, 3, 2)
        ]

    def plane_first(u):
        if Z_FIRST[u] == 1:
            return [copy(u, 4, block(u, every, z, 1 - y), got_2a[u], beside)]
        return [copy(u, 4, block(u, 1 - c, z, every), got_2a[u], across)]

    def plane_second(u):
        if Z_FIRST[u] == 1:
            return [copy(u, 5, block(u, 1 - c, z, y), got_2b[u], across)]
        return [copy(u, 5, block(u, c, z, 1 - y), got_2b[u], beside)]

    def mine(u):
        return k if GRAD_UNITS[u][3] else c

    def pair(u):
        return [copy(u, 8, total[u].at[1 - mine(u)], got_4[u], twin if GRAD_UNITS[u][3] else across)]

    def peer(step):
        return lax.rem(me + step, 32)

    def source(step):
        return lax.rem(me + 32 - step, 32)

    def table_copy(step, back, index):
        target = (peer(step) // 2, lax.rem(peer(step), 2))
        if back:
            return remote(
                table_out.at[index], table_out.at[index], table_send.at[1, step], table_recv.at[1, step], target
            )
        return remote(
            table.at[index], table_got.at[me], table_send.at[0, step], table_recv.at[0, step], target
        )

    def table_start(step):
        @pl.when(peer(step) < PIECES)
        def _():
            table_copy(step, False, peer(step)).start()

    def table_wait_send(step):
        @pl.when(peer(step) < PIECES)
        def _():
            table_copy(step, False, 0).wait_send()

        @pl.when(me < PIECES)
        def _():
            table_copy(step, True, 0).wait_send()

    def table_wait_back(step):
        @pl.when(source(step) < PIECES)
        def _():
            table_copy(step, True, 0).wait_recv()

    def each(action):
        def body(step, carry):
            action(step)
            return carry

        lax.fori_loop(1, 32, body, 0)

    def gather_into(u, cc, zz, yy, *others):
        matrix = GRAD_UNITS[u][0]
        index = where(u, cc, zz, yy)
        if not others:
            grads[matrix][index] = grads[matrix][index] + got_0[u][ordered(u, cc, (zz, yy))]
            return
        value = grads[matrix][index].astype(F32) + got_0[u][ordered(u, cc, (zz, yy))].astype(F32)
        for other in others:
            value = value + other.astype(F32)
        grads[matrix][index] = value.astype(BF16)

    def from_line(u, cc, yy):
        index = (yy, cc) if GRAD_UNITS[u][3] else (cc, yy)
        return [got_1a[u][(step, *index)] for step in range(3)]

    def stage_first(u):
        twin_copy(u).wait_recv()
        if u in Z_FIRST:
            for step in (1, 3, 2):
                for cc in range(2):
                    for yy in range(2):
                        gather_into(u, cc, lax.rem(z + step, 4), yy)
            for item in z_first(u):
                item.start()
            return
        for a in range(2):
            for b in range(2):
                gather_into(u, a, b, 1 - y)
                gather_into(u, 1 - c, 2 + a, b)
        for item in first(u):
            item.start()

    def from_beside(u, cc, a):
        return got_1a[u][ordered(u, cc, (a,))]

    def stage_second(u):
        if u in Z_FIRST:
            for item in z_first(u):
                item.wait_recv()
            for a in range(2):
                cc, yy = (a, 1 - y) if Z_FIRST[u] == 1 else (1 - c, a)
                gather_into(u, cc, z, yy, *from_line(u, cc, yy))
            for item in plane_first(u):
                item.start()
            return
        for item in first(u):
            item.wait_recv()
        for a in range(2):
            gather_into(u, 1 - c, a, y, from_beside(u, 1 - c, a))
            gather_into(u, c, 2 + a, 1 - y, got_1b[u][a, 1 - y])
        for item in second(u):
            item.start()

    def stage_along(u):
        if u in Z_FIRST:
            for item in plane_first(u):
                item.wait_recv()
            cc, yy = (1 - c, y) if Z_FIRST[u] == 1 else (c, 1 - y)
            gather_into(u, cc, z, yy, *from_line(u, cc, yy), got_2a[u][cc if Z_FIRST[u] == 1 else yy])
            for item in plane_second(u):
                item.start()
            return
        for item in second(u):
            item.wait_recv()
        for a in range(2):
            gather_into(u, c, a, y, from_beside(u, c, a), got_2a[u][a])
            gather_into(u, c, 2 + a, y, got_1b[u][a, y], got_2b[u][a])
        for item in along(u):
            item.start()

    def stage_pair(u):
        full = grads[GRAD_UNITS[u][0]][where(u, c, z, y)].astype(F32)
        if u in Z_FIRST:
            for item in plane_second(u):
                item.wait_recv()
            others = [got_0[u][ordered(u, c, (z, y))], *from_line(u, c, y)]
            others += [got_2a[u][c if Z_FIRST[u] == 1 else y], got_2b[u][...]]
        else:
            for item in along(u):
                item.wait_recv()
            others = [got_3[u][step] for step in range(3)]
        for other in others:
            full = full + other.astype(F32)
        total[u][0] = full[:24]
        total[u][1] = full[24:]
        for item in pair(u):
            item.start()

    def stage_end(u):
        matrix, start, n, _ = GRAD_UNITS[u]
        lanes = slice(start, start + n)
        side = mine(u)
        outs[matrix][side, :, lanes] = total[u][side]
        for item in pair(u):
            item.wait_recv()
        outs[matrix][1 - side, :, lanes] = got_4[u][...]
        own, other = total[u][side], got_4[u][...]
        square[...] += jnp.broadcast_to(total_of(own * own + other * other), (8, 128))
        if u in Z_FIRST:
            sent = z_first(u) + plane_first(u) + plane_second(u)
        else:
            sent = first(u) + second(u) + along(u)
        for item in [twin_copy(u)] + sent:
            item.wait_send()

    def table_sum(u):
        @pl.when(me < PIECES)
        def _():
            each(lambda step: table_copy(step, False, 0).wait_recv())
            table_got[me] = table[me]

            def add(at, held):
                return held + table_got[at].astype(F32)

            total_rows = lax.fori_loop(1, 32, add, table_got[0].astype(F32))
            top, rest = split_two(total_rows[:8] + total_rows[8:])
            exact = jnp.concatenate([top.astype(F32), rest.astype(F32)], 0)
            table_out[me] = jnp.where(me >= 18, exact, total_rows).astype(BF16)
            each(lambda step: table_copy(step, True, me).start())

    late_parts = []

    def table_end(u):
        each(table_wait_back)
        need(weight(count))
        late_parts.append(
            table_finish(
                table_out, upstream, kept.table, kept.norms, kept.proj_t, late_parts[0], g_in, g_norm, send_stat
            )
        )
        for at, value in enumerate(late_parts[1][:4]):
            late_rows[at] = jnp.broadcast_to(value, (24, VP))
        square[...] += jnp.broadcast_to(late_parts[1][-1], (8, 128))

    def stat_copy(step):
        target = (peer(step) // 2, lax.rem(peer(step), 2))
        return remote(stat, stat_got.at[me], table_send.at[3, step], table_recv.at[3, step], target)

    def send_stat(rows):
        line = iota((8, VP), 0)
        result = jnp.zeros((8, VP), F32)
        for at, row in enumerate(rows):
            result = jnp.where(line == at, row, result)
        stat[...] = result
        each(lambda step: stat_copy(step).start())
        stat_got[me] = stat[...]

    def table_last():
        each(lambda step: stat_copy(step).wait())
        totals = lax.fori_loop(1, 32, lambda at, held: held + stat_got[at], stat_got[0])
        mean_1, mean_2 = totals[0:1] * (1.0 / D), totals[1:2] * (1.0 / D)
        inner, unit, rstd, emb_grad = (late_rows[at] for at in range(4))
        g_emb[...] = emb_grad + rstd * (inner - mean_1 - unit * mean_2)
        first, second = rstd[0:1] * mean_1, rstd[0:1] * mean_2
        whole = totals[6:7] - 2.0 * (first * totals[2:3] + second * totals[3:4])
        whole = whole + first * first * D + 2.0 * first * second * totals[4:5] + second * second * totals[5:6]
        return total_of(whole)

    stages = (stage_first, stage_second, stage_along, stage_pair, stage_end, table_sum, table_end)
    pending = list(BACKWARD_ORDER)

    def hook():
        for stage, u in pending.pop(0):
            stages[stage](u)

    def done(u):
        if u == 0:
            pl.semaphore_wait(barrier, 31)
        twin_copy(u).start()
        hook()

    names = Kept._fields

    load(AT.branch, saved.branch, branch)

    def phase_one(*early_refs):
        e = Early(*early_refs)
        load(weight(0), far[0], grads[0])
        load(AT.slope, saved.slope, e.slope)
        load(AT.active, saved.active, e.active)
        load(weight(1), far[1], grads[1])
        for name in names:
            load(getattr(AT, name), getattr(saved, name), getattr(kept, name))
        for m in (2, 3):
            load(weight(m), far[m], grads[m])
        for name in Early._fields[2:6]:
            load(getattr(AT, name), getattr(saved, name), getattr(e, name))
        load(weight(4), far[4], grads[4])
        for name in Early._fields[6:8]:
            load(getattr(AT, name), getattr(saved, name), getattr(e, name))
        load(weight(5), far[5], grads[5])
        for name in Early._fields[8:]:
            load(getattr(AT, name), getattr(saved, name), getattr(e, name))
        load(weight(6), far[6], grads[6])
        view = [g.reshape(2, D, n) for g, n in zip(grads, widths)]
        need(AT.branch)
        transpose_into(branch, branch_t)
        hook()

        def grad_tile(m, start, left_t, right, half, at):
            lanes = slice(start + half * widths[m] + at, start + half * widths[m] + at + 384)
            view[m][half, :, at : at + 384] = nn(left_t[...], right[:, lanes]).astype(BF16)

        def grad_half(m, start, left_t, right, half):
            for at in range(0, widths[m], 384):
                grad_tile(m, start, left_t, right, half, at)

        for part in range(2):
            need(weight(part))
            if part == 0:
                need(AT.slope)

            def down_back(half, at, part=part):
                lanes = slice(part * 1536 + half * 768 + at, part * 1536 + half * 768 + at + 384)
                back = nn(branch[...], view[part][half, :, at : at + 384])
                e.slope[:, lanes] = (back * e.slope[:, lanes].astype(F32)).astype(BF16)

            if part == 0:
                for at in (0, 384):
                    for half in range(2):
                        down_back(half, at)
                    hook()
                    if at == 0:
                        need(AT.active)
                    for half in range(2):
                        grad_tile(part, 0, branch_t, e.active, half, at)
                    done(at // 384)
            else:
                for half in range(2):
                    for at in (0, 384):
                        down_back(half, at)
                    hook()
                grad_half(part, part * 1536, branch_t, e.active, 0)
                hook()
                grad_half(part, part * 1536, branch_t, e.active, 1)
                done(2)
        for part in range(2):
            need(weight(2 + part))
            for half in range(2):
                start = part * 1536 + half * 768
                back = nt(e.slope[:, start : start + 768], view[2 + part][half])
                upstream[...] = back if start == 0 else upstream[...] + back
                hook()
            if part == 0:
                need(AT.feed_normed_t)
            grad_half(2 + part, part * 1536, e.feed_normed_t, e.slope, 0)
            hook()
            grad_half(2 + part, part * 1536, e.feed_normed_t, e.slope, 1)
            done(3 + part)
        need(*(getattr(AT, name) for name in names))
        norms = kept.norms[...]

        def gain(number):
            return norms[number : number + 1, :]

        need(AT.unit_2, AT.rstd_2)
        scale_2, shift_2 = back_rows(e.unit_2, e.rstd_2, gain(2), upstream, stream, branch, False)
        hook()
        need(weight(4), AT.col_mixed_t)
        mixed[...] = (nt(branch[:, :384], view[4][0]) + nt(branch[:, 384:], view[4][1])).astype(BF16)
        hook()
        for half in range(2):
            grad_half(4, 0, e.col_mixed_t, branch, half)
        done(5)
        need(AT.col_proj, AT.col_prob)
        proj = e.active

        def attend(at, carry):
            rows = pl.ds(pl.multiple_of((at // PAIRS) * 128, 128), 128)
            lane = lax.rem(at, PAIRS) * 128

            def lanes(part):
                return pl.ds(pl.multiple_of(part * D + lane, 128), 128)

            query = stacked(e.col_proj[rows, lanes(0)])
            key = e.col_proj[rows, lanes(1)]
            value = e.col_proj[rows, lanes(2)]
            above = stacked(mixed[rows, lanes(0)])
            prob = e.col_prob[at]
            grad = nt(above, value)
            grad = prob * (grad - jnp.sum(prob * grad, -1, keepdims=True))
            small = grad.astype(BF16)
            scale = HD ** (-0.5)
            proj[rows, lanes(0)] = (unstacked(nn(small, key), 128) * scale).astype(BF16)
            proj[rows, lanes(1)] = (tn(small, query) * scale).astype(BF16)
            proj[rows, lanes(2)] = tn(prob.astype(BF16), above).astype(BF16)
            return carry

        for part in range(6):
            lax.fori_loop(4 * part, 4 * part + 4, attend, 0, unroll=4)
            hook()
        need(weight(5))
        for half in range(2):
            back = nt(proj[:, half * 1152 : half * 1152 + 1152], view[5][half])
            upstream[...] = back if half == 0 else upstream[...] + back
            hook()
        need(AT.col_normed_t)
        for third in range(3):
            for half in range(2):
                grad_tile(5, 0, e.col_normed_t, proj, half, third * 384)
            done(6 + third)
        need(AT.unit_1, AT.rstd_1)
        scale_1, shift_1 = back_rows(e.unit_1, e.rstd_1, gain(1), upstream, stream, branch, False)
        hook()
        need(weight(6))
        mixed[...] = (nt(branch[:, :384], view[6][0]) + nt(branch[:, 384:], view[6][1])).astype(BF16)
        line = iota((8, D), 0)
        vectors = jnp.zeros((8, D), F32)
        moved = kept.moved[...]
        rows = (scale_1, scale_2, moved[0:1], shift_1, shift_2, moved[1:2])
        for number, row in enumerate(rows):
            vectors = jnp.where(line == number, row, vectors)
        extras = jnp.concatenate([kept.extras[0:1, :], jnp.zeros((1, D - 128), F32)], 1)
        kept.moved[...] = jnp.where(line == 6, extras, vectors)
        hook()

    pl.run_scoped(phase_one, *(pltpu.VMEM(*item) for item in pick_items(Early, SAVED)))

    def phase_two(*late_refs):
        e = Late(*late_refs[:-3])
        in_row, left_hi, left_lo = late_refs[-3:]
        for name in Late._fields:
            load(getattr(AT, name), getattr(saved, name), getattr(e, name))
        load(weight(count), in_row_far.at[0], in_row)
        view = grads[6].reshape(2, D, widths[6])
        late_parts.append(in_row)
        need(AT.row_mixed_t)
        for half in range(2):
            lanes = slice(half * 384, half * 384 + 384)
            view[half] = nn(e.row_mixed_t[...], branch[:, lanes]).astype(BF16)
        done(9)
        need(AT.hot_all, AT.weight_hi, AT.prob, AT.hot_ri, AT.hot_ir)
        shape = (HERE, HERE)
        back = (
            ((iota(shape, 1) >> 4) == (iota(shape, 0) & 31))
            & ((iota(shape, 1) & 15) == (iota(shape, 0) >> 5))
        )
        mixed[...] = nn(one_zero(back).astype(BF16), mixed[...]).astype(BF16)
        value_rows = []
        for hp in range(PAIRS):
            lanes = slice(hp * 128, hp * 128 + 128)
            part = mixed[:, lanes]
            upstream[:, lanes] = nt(part, kept.value_two[hp])
            value_rows.append(unstacked(tn(e.weight_hi[:, lanes], part), 64))
        hook()
        split_heads_to(upstream, left_hi, left_lo)
        hook()
        hot_all = e.hot_all[...]
        grad = nn(left_hi[...], hot_all) + nn(left_lo[...], hot_all)
        extra = jnp.concatenate(
            [kept.touch[...] * (contact_head[h] * COLS) for h in range(HEADS)], 0
        )
        grad = grad + extra
        prob = e.prob[...]
        grad = prob * (grad - jnp.sum(prob * grad, -1, keepdims=True))
        low_grad = grad.astype(BF16)
        hook()
        merge_heads(low_grad, e.hot_all, branch, None)
        hook()
        table_pair = nn(e.hot_ri[...], branch[...])
        stream_hi, stream_lo = split_two(stream[...])
        hot_ir = e.hot_ir[...]
        table_grad = kept.grad_head[...] + nn(hot_ir, stream_hi) + nn(hot_ir, stream_lo)
        value_grad = jnp.concatenate(value_rows, 1)
        last = jnp.where(iota((8, D), 0) == 7, table_grad[32:33], kept.moved[...])
        top, rest = split_two(last)
        groups = [table_pair[4:20], table_pair[20:36], value_grad[4:20], value_grad[20:36]]
        groups += [table_grad[0:16], table_grad[16:32]]
        groups += [jnp.concatenate([top.astype(F32), rest.astype(F32)], 0)]
        for number, group in enumerate(groups):
            for third in range(3):
                table[3 * number + third] = group[:, third * 256 : third * 256 + 256].astype(BF16)
        each(table_start)
        hook()
        hook()

    pl.run_scoped(
        phase_two,
        *(pltpu.VMEM(*item) for item in pick_items(Late, SAVED)),
        pltpu.VMEM((24, 3 * D), F32),
        pltpu.VMEM((HEADS * WIDE, ROWS * VP), BF16),
        pltpu.VMEM((HEADS * WIDE, ROWS * VP), BF16),
    )
    assert not pending

    def square_copy(step):
        other = lax.rem(me + step, 32)
        return remote(
            square, square_got.at[me], table_send.at[2, step], table_recv.at[2, step], (other // 2, lax.rem(other, 2))
        )

    each(lambda step: square_copy(step).start())
    square_got[me] = square[...]
    each(lambda step: table_wait_send(step))
    for u in range(units):
        for item in pair(u):
            item.wait_send()
    emb_square = table_last()
    each(lambda step: square_copy(step).wait())
    total_square = lax.fori_loop(1, 32, lambda at, held: held + square_got[at], square_got[0])[0:1]
    vector = table_out[18].astype(F32)
    vector = vector[6:7, :128] + vector[14:15, :128]
    counted = kept.extras[1:2, :]
    column = iota((1, 128), 1)
    contact = jnp.where(column <= HEADS, vector, 0.0)
    total_square = total_square + total_of(contact * contact) + emb_square
    grad_norm = jnp.sqrt(total_square)
    factor = jnp.minimum(1.0, MAX_NORM / grad_norm)
    losses = (
        (0, vector[:, HEADS + 1 : HEADS + 2]),
        (1, counted[:, 0:1]),
        (2, vector[:, HEADS + 2 : HEADS + 3]),
        (3, counted[:, 1:2]),
    )
    loss_row = jnp.zeros((1, 128), F32)
    for at, value in losses:
        loss_row = jnp.where(column == at, value, loss_row)
    number = iota((8, 128), 0)
    result = jnp.zeros((8, 128), F32)
    for at, row in enumerate((contact, counted, factor, grad_norm, loss_row)):
        result = jnp.where(number == at, row, result)
    stats[...] = result


def backward_call(contact_head, weights, in_row, saved):
    widths = GRAD_WIDTHS
    count = len(widths)
    inside = pl.BlockSpec(memory_space=pltpu.VMEM)
    anywhere = pl.BlockSpec(memory_space=pl.ANY)

    units = len(GRAD_UNITS)

    def shapes(lead, dtype, other=None):
        leads = [other if other and u in Z_FIRST else lead for u in range(units)]
        return [pltpu.VMEM((*at, n), dtype) for at, (_, _, n, _) in zip(leads, GRAD_UNITS)]

    outs = pl.pallas_call(
        backward_kernel,
        out_shape=[jax.ShapeDtypeStruct((2, 24, n), F32) for n in widths]
        + [
            jax.ShapeDtypeStruct((24, 3 * D), F32),
            jax.ShapeDtypeStruct((24, VP), F32),
            jax.ShapeDtypeStruct((8, 24), F32),
            jax.ShapeDtypeStruct((8, 128), F32),
        ],
        in_specs=[pl.BlockSpec(memory_space=pltpu.SMEM)] + [anywhere] * (1 + count + len(SAVED)),
        out_specs=[inside] * (4 + count),
        scratch_shapes=[pltpu.VMEM((2, NZ, NY, 2, 48, n), BF16) for n in widths]
        + [pltpu.VMEM(*item) for item in pick_items(Kept, SAVED)]
        + [
            pltpu.VMEM((HERE, D), F32),
            pltpu.VMEM((HERE, D), BF16),
            pltpu.VMEM((D, HERE), BF16),
            pltpu.VMEM((HERE, D), BF16),
        ]
        + [
            pltpu.VMEM((NZ, NY, 2, 48, n) if paired else (2, NZ, NY, 48, n), BF16)
            for _, _, n, paired in GRAD_UNITS
        ]
        + shapes((2, 2, 48), BF16, (3, 2, 2, 48))
        + shapes((2, 2, 48), BF16, (16,))
        + shapes((2, 48), BF16, (2, 48))
        + shapes((2, 48), BF16, (48,))
        + shapes((3, 48), BF16, (16,))
        + shapes((2, 24), F32)
        + shapes((24,), F32)
        + [
            pltpu.VMEM((PIECES, 16, 256), BF16),
            pltpu.VMEM((PIECES, 16, 256), BF16),
            pltpu.VMEM((32, 16, 256), BF16),
            pltpu.VMEM((8, 128), F32),
            pltpu.VMEM((32, 8, 128), F32),
            pltpu.VMEM((8, VP), F32),
            pltpu.VMEM((32, 8, VP), F32),
            pltpu.VMEM((4, 24, VP), F32),
            pltpu.SemaphoreType.DMA((4, 32)),
            pltpu.SemaphoreType.DMA((4, 32)),
            pltpu.SemaphoreType.DMA((units, 9)),
            pltpu.SemaphoreType.DMA((units, 9)),
            pltpu.SemaphoreType.DMA((len(SAVED) + count + 1,)),
        ],
        compiler_params=pltpu.CompilerParams(
            collective_id=1, has_side_effects=True, vmem_limit_bytes=63 * 2**20
        ),
    )(contact_head, *weights, in_row, *saved)
    return outs[:count], outs[count:]


UPDATE_RATES = (LEARN_RATE,) * 4 + (VECTOR_RATE,) * 3


def update_kernel(*refs):
    given, far, held, results = refs[:32], refs[32:60], refs[60:92], refs[92:120]
    sems, out_sems = refs[120:122]
    outs, copies = results[:21], results[21:26]
    loss_ref, norm_ref = results[26:]

    def leave(*numbers):
        for n in numbers:
            pltpu.make_async_copy(results[n], far[n], out_sems.at[n]).start()

    moves = [pltpu.make_async_copy(a, b, sems.at[n]) for n, (a, b) in enumerate(zip(given, held))]
    groups = (
        (10, 7, 5, 11, 12, 13),
        (4, 6, 14, 15, 16),
        (2, 3, 17, 18, 19),
        (0, 1, 20, 21, 22),
        (8, 9, *range(23, 32)),
    )
    for group in groups:
        for n in group:
            moves[n].start()

    def arrive(number):
        for n in groups[number]:
            moves[n].wait()

    reduced, g_in, g_emb, g_norm, stats = held[:7], held[7], held[8], held[9], held[10]
    states = [held[11 + 3 * n : 14 + 3 * n] for n in range(7)]
    outs = [outs[3 * n : 3 * n + 3] for n in range(7)]
    order = feature_order()
    arrive(0)
    factor = stats[2:3, 0:1]
    loss_ref[...] = stats[4:5, 0:4]
    norm_ref[...] = stats[3:4, 0:1]

    def natural(values):
        top, rest = split_two(values)
        last = (values - top.astype(F32) - rest.astype(F32)).astype(BF16)
        return nt(top, order) + nt(rest, order) + nt(last, order)

    def update(number, where, grad):
        master, first, second = (ref[where] for ref in states[number])
        new, first, second = adam_update(master, first, second, grad * factor, UPDATE_RATES[number])
        for ref, value in zip(outs[number], (new, first, second)):
            ref[where] = value
        if number < 5:
            copies[number][where] = new.astype(BF16)

    every = slice(None)
    g_out_col, g_in_col, g_out_row = reduced[4:]
    for half in range(2):
        lanes = slice(half * 1152, half * 1152 + 1152)
        update(0, (0, every, lanes), g_in[:, lanes])
        update(0, (1, every, lanes), g_in_col[half])
    leave(0, 1, 2, 21, 26, 27)
    arrive(1)
    for half in range(2):
        lanes = slice(half * 384, half * 384 + 384)
        update(1, (0, every, lanes), natural(g_out_row[half]))
        update(1, (1, every, lanes), natural(g_out_col[half]))
    leave(3, 4, 5, 22)
    for number, first in ((2, 2), (3, 0)):
        arrive(number)
        for half in range(2):
            for part in range(2):
                start = part * 1536 + half * 768
                lanes = slice(start, start + 768)
                update(number, (every, lanes), reduced[first + part][half])
        leave(*((6, 7, 8, 23) if number == 2 else (9, 10, 11, 24)))
    arrive(4)
    update(4, (every, every), g_emb[:, :VOCAB])
    update(5, (every, every), g_norm[...])
    update(6, (every, every), stats[0:1, : HEADS + 1])
    leave(12, 13, 14, 25, 15, 16, 17, 18, 19, 20)
    for n in range(28):
        pltpu.make_async_copy(results[n], far[n], out_sems.at[n]).wait()


def update_call(reduced, g_in, g_emb, g_norm, stats, states):
    anywhere = pl.BlockSpec(memory_space=pl.ANY)
    flat = [item for state in states for item in state]
    shapes = [jax.ShapeDtypeStruct(item.shape, F32) for item in flat]
    shapes += [jax.ShapeDtypeStruct(states[n][0].shape, BF16) for n in range(5)]
    shapes += [jax.ShapeDtypeStruct((1, 4), F32), jax.ShapeDtypeStruct((1, 1), F32)]
    given = (*reduced, g_in, g_emb, g_norm, stats, *flat)
    return pl.pallas_call(
        update_kernel,
        out_shape=shapes,
        in_specs=[anywhere] * len(given),
        out_specs=[anywhere] * len(shapes),
        scratch_shapes=[pltpu.VMEM(item.shape, F32) for item in given]
        + [pltpu.VMEM(item.shape, item.dtype) for item in shapes]
        + [
            pltpu.SemaphoreType.DMA((len(given),)),
            pltpu.SemaphoreType.DMA((len(shapes),)),
            pltpu.VMEM((44, 512, 512), F32),
        ],
        compiler_params=pltpu.CompilerParams(vmem_limit_bytes=62 * 2**20),
    )(*given)


def adam_update(master, first, second, grad_part, rate):
    first = BETA_ONE * first + (1.0 - BETA_ONE) * grad_part
    second = BETA_TWO * second + (1.0 - BETA_TWO) * grad_part * grad_part
    scaled = first * (1.0 / (1.0 - BETA_ONE**STEP))
    moved = scaled / (jnp.sqrt(second * (1.0 / (1.0 - BETA_TWO**STEP))) + ADAM_EPS)
    return (master - rate * (moved + WEIGHT_DECAY * master), first, second)


def shards(
    tokens,
    targets,
    masked,
    contact_pairs,
    labels,
    attention_in_master,
    attention_in_first,
    attention_in_second,
    attention_out_master,
    attention_out_first,
    attention_out_second,
    feed_up_master,
    feed_up_first,
    feed_up_second,
    feed_down_master,
    feed_down_first,
    feed_down_second,
    embedding_master,
    embedding_first,
    embedding_second,
    norm_params_master,
    norm_params_first,
    norm_params_second,
    contact_head_master,
    contact_head_first,
    contact_head_second,
):
    both = ("seq", "col")
    micro, rows_here, cols_here = tokens.shape
    ncol = lax.axis_size("col")
    ndev = lax.axis_size("seq") * ncol
    cols = cols_here * ncol
    me = lax.axis_index("seq") * ncol + lax.axis_index("col")
    per = ndev // micro
    cw = cols // per
    mine = me // per
    base = (me % per) * cw
    shard = D // ndev

    tiled = lax.axis_size("seq") == 16 and ncol == 2
    if tiled:
        raw = (
            tokens,
            targets,
            masked,
            contact_pairs.transpose(0, 2, 1),
            labels,
            embedding_master.T,
            norm_params_master,
            attention_in_master,
            attention_out_master,
            feed_up_master,
            feed_down_master.T,
        )
        weights, saved = forward_call(raw, contact_head_master)
        reduced, (g_in, g_emb, g_norm, stats) = backward_call(
            contact_head_master, [weights[n] for n in (5, 6, 3, 4, 2, 1, 0)], attention_in_master, saved
        )
        states = (
            (attention_in_master, attention_in_first, attention_in_second),
            (attention_out_master, attention_out_first, attention_out_second),
            (feed_up_master, feed_up_first, feed_up_second),
            (feed_down_master.T, feed_down_first.T, feed_down_second.T),
            (embedding_master.T, embedding_first.T, embedding_second.T),
            (norm_params_master, norm_params_first, norm_params_second),
            (contact_head_master[None], contact_head_first[None], contact_head_second[None]),
        )
        outs = update_call(reduced, g_in, g_emb, g_norm, stats, states)
        return (
            *outs[:9],
            *(item.T for item in outs[9:15]),
            *outs[15:18],
            *(item[0] for item in outs[18:21]),
            *outs[21:24],
            *(item.T for item in outs[24:26]),
            outs[26][0],
            outs[27][0, 0],
        )
    inputs = jnp.where(masked > 0, MASK_ID, tokens)
    masters = [
        jnp.concatenate(
            [
                jnp.pad(embedding_master.T, ((0, 0), (0, 128 - VOCAB))),
                jnp.pad(norm_params_master.T, ((0, 0), (0, 120))),
            ],
            1,
        ),
        attention_in_master[0],
        attention_out_master[0],
        attention_in_master[1],
        attention_out_master[1],
        feed_up_master,
        feed_down_master.T,
    ]
    whole = jnp.stack([inputs, targets])
    whole = lax.all_gather(lax.all_gather(whole, "col", axis=3, tiled=True), "seq", axis=2, tiled=True)
    pairs_all = lax.all_gather(
        jnp.concatenate([contact_pairs, labels[:, :, None]], -1), both, axis=1, tiled=True
    )
    gathered = []
    for master in masters:
        full = lax.all_gather(master.astype(BF16), both, axis=0, tiled=True)
        gathered.append(full.reshape(D, 2, -1).transpose(1, 0, 2))
    counts = (
        jnp.sum(whole[0] == MASK_ID).astype(F32),
        jnp.sum(pairs_all[..., 2] >= 0).astype(F32),
    )
    ids_all = lax.dynamic_index_in_dim(whole[0], mine, 0, False)
    ids_local = lax.dynamic_slice_in_dim(ids_all, base, cw, 1)
    targets_local = lax.dynamic_slice_in_dim(
        lax.dynamic_index_in_dim(whole[1], mine, 0, False), base, cw, 1
    )
    pairs = lax.dynamic_index_in_dim(pairs_all, mine, 0, False)

    table = gathered[0][0][:, :VP].T
    norms = gathered[0][1][:, :8].T.astype(F32)
    in_row, out_row, in_col, out_col, up_w, down_t = (
        jnp.concatenate([g[0], g[1]], 1) for g in gathered[1:]
    )
    big = (in_row, in_col, out_row, out_col, up_w, down_t)

    grads, tables, contact_total, mlm_total, bce_total, kept = step(
        big,
        table,
        norms,
        contact_head_master,
        ids_all,
        ids_local.reshape(-1),
        ids_local.T.reshape(-1),
        targets_local.T.reshape(-1),
        pairs[:, 0] - base,
        pairs[:, 1],
        pairs[:, 2],
        counts,
        cw,
    )
    table_pair, value_grad, table_grad, vectors = tables
    extras = jnp.zeros((2, D), F32).at[0, : HEADS + 3].set(
        jnp.concatenate([contact_total, mlm_total[None], bce_total[None]])
    )
    sums = jnp.concatenate([table_pair[:40], value_grad[:40], table_grad[:40], vectors, extras])
    flat_grad = jnp.concatenate([g.astype(BF16) for g in grads], 1)
    reduced = lax.psum_scatter(flat_grad, both, scatter_dimension=0, tiled=True).astype(F32)
    g_in_col, g_out_row, g_out_col, g_up, g_down = jnp.split(
        reduced, [3 * D, 4 * D, 5 * D, 5 * D + FF], 1
    )
    sums = lax.psum(sums, both)
    unit_t, rstd_t, normed_t, query_t, key_t = kept
    rows_all = ids_all.shape[0]
    spare = ((0, VP - 40), (0, 0))
    table_pair, value_grad, table_grad = (
        jnp.pad(sums[a : a + 40], spare) for a in (0, 40, 80)
    )
    vectors = sums[120:126]
    contact_grad, mlm_total, bce_total = (
        sums[126, : HEADS + 1], sums[126, HEADS + 1], sums[126, HEADS + 2]
    )
    row_scale = (HD * rows_all) ** (-0.5)
    query_grad = []
    key_grad = []
    for h in range(HEADS):
        pair = heads_of(table_pair, h)
        query_grad.append(jnp.dot(pair, heads_of(key_t, h).astype(F32), precision=PRECISE))
        key_grad.append(jnp.dot(pair.T, heads_of(query_t, h).astype(F32), precision=PRECISE))
    proj_grad = jnp.concatenate(
        [
            jnp.concatenate(query_grad, 1) * row_scale,
            jnp.concatenate(key_grad, 1) * row_scale,
            value_grad,
        ],
        1,
    )
    proj_hi, proj_lo = split_two(proj_grad)
    normed_grad = nt(proj_hi, in_row) + nt(proj_lo, in_row)
    back_t, scale_0, shift_0 = norm_back(unit_t, rstd_t, norms[0], normed_grad)
    table_grad = table_grad + back_t
    low = me * shard
    normed_mine = lax.dynamic_slice_in_dim(normed_t, low, shard, 1)
    grad_in_row = tn(normed_mine, proj_hi) + tn(normed_mine, proj_lo)
    norm_grad = jnp.concatenate([scale_0[None], vectors[:3], shift_0[None], vectors[3:]])
    table_mine = lax.dynamic_slice_in_dim(table_grad[:VOCAB], low, shard, 1)
    norm_mine = lax.dynamic_slice_in_dim(norm_grad, low, shard, 1)
    reduced_all = (g_in_col, g_out_row, g_out_col, g_up, g_down)

    local_square = (
        sum(jnp.sum(g * g) for g in reduced_all)
        + jnp.sum(grad_in_row * grad_in_row)
        + jnp.sum(table_mine * table_mine)
        + jnp.sum(norm_mine * norm_mine)
    )
    square = lax.psum(local_square, both) + jnp.sum(contact_grad * contact_grad)
    grad_norm = jnp.sqrt(square)
    factor = jnp.minimum(1.0, MAX_NORM / grad_norm)
    in_new, in_moment, in_square = adam_update(
        attention_in_master, attention_in_first, attention_in_second, jnp.stack([grad_in_row, g_in_col]) * factor, LEARN_RATE
    )
    out_new, out_moment, out_square = adam_update(
        attention_out_master, attention_out_first, attention_out_second, jnp.stack([g_out_row, g_out_col]) * factor, LEARN_RATE
    )
    up_new, up_moment, up_square = adam_update(
        feed_up_master, feed_up_first, feed_up_second, g_up * factor, LEARN_RATE
    )
    down_new, down_moment, down_square = adam_update(
        feed_down_master, feed_down_first, feed_down_second, g_down.T * factor, LEARN_RATE
    )
    table_new, table_moment, table_square = adam_update(
        embedding_master, embedding_first, embedding_second, table_mine * factor, VECTOR_RATE
    )
    norm_new, norm_moment, norm_square = adam_update(
        norm_params_master, norm_params_first, norm_params_second, norm_mine * factor, VECTOR_RATE
    )
    head_new, head_moment, head_square = adam_update(
        contact_head_master, contact_head_first, contact_head_second, contact_grad * factor, VECTOR_RATE
    )
    loss_parts = jnp.stack([mlm_total, counts[0], bce_total, counts[1]])
    return (
        in_new, in_moment, in_square,
        out_new, out_moment, out_square,
        up_new, up_moment, up_square,
        down_new, down_moment, down_square,
        table_new, table_moment, table_square,
        norm_new, norm_moment, norm_square,
        head_new, head_moment, head_square,
        in_new.astype(BF16), out_new.astype(BF16), up_new.astype(BF16), down_new.astype(BF16), table_new.astype(BF16),
        loss_parts, grad_norm,
    )


def solution(mesh):
    both = ("seq", "col")
    cells = P(None, "seq", "col")
    stack = P(None, both, None)
    row_split = P(both, None)
    col_split = P(None, both)
    weights = [stack] * 6 + [row_split] * 3 + [col_split] * 9 + [P()] * 3
    return jax.shard_map(
        shards,
        mesh=mesh,
        in_specs=(cells, cells, cells, stack, col_split, *weights),
        out_specs=(*weights, stack, stack, row_split, col_split, col_split, P(), P()),
        check_vma=False,
    )
```

```python
import typing

import jax
import jax.numpy as jnp
from jax import lax
from jax.experimental import pallas as pl
from jax.experimental.pallas import tpu as pltpu
from jax.sharding import PartitionSpec as P

D = 768
HEADS = 12
HD = 64
FF = 3072
VOCAB = 33
VP = 64
STEP = 10

NORM_EPS = 1e-05
MASK_ID = 32
MAX_NORM = 0.001
LEARN_RATE = 0.05
VECTOR_RATE = 0.5
BETA_ONE = 0.9
BETA_TWO = 0.95
ADAM_EPS = 1e-08
WEIGHT_DECAY = 0.01
PRECISE = lax.Precision.HIGHEST
F32 = jnp.float32
BF16 = jnp.bfloat16


def nn(left, right):
    return lax.dot_general(left, right, (((1,), (0,)), ((), ())), preferred_element_type=F32)


def tn(left, right):
    return lax.dot_general(left, right, (((0,), (0,)), ((), ())), preferred_element_type=F32)


def nt(left, right):
    return lax.dot_general(left, right, (((1,), (1,)), ((), ())), preferred_element_type=F32)


def split_two(values):
    high = values.astype(BF16)
    return high, (values - high.astype(F32)).astype(BF16)


def norm_stats(values):
    centre = values - jnp.mean(values, -1, keepdims=True)
    rstd = lax.rsqrt(jnp.mean(centre * centre, -1, keepdims=True) + NORM_EPS)
    return centre * rstd, rstd


def norm_back(unit, rstd, scale_vec, upstream):
    inner = upstream * scale_vec
    grad = rstd * (
        inner - jnp.mean(inner, -1, keepdims=True) - unit * jnp.mean(inner * unit, -1, keepdims=True)
    )
    return grad, jnp.sum(upstream * unit, 0), jnp.sum(upstream, 0)


GELU_K = 0.7978845608028654
GELU_C = 0.044715


def gelu_parts(up):
    square = up * up
    bent = jnp.tanh(GELU_K * up * (1.0 + GELU_C * square))
    half = 0.5 * (1.0 + bent)
    slope = half + 0.5 * up * (1.0 - bent * bent) * GELU_K * (1.0 + 3.0 * GELU_C * square)
    return up * half, slope


def heads_of(block, head):
    return block[:, head * HD : (head + 1) * HD]


def step(big, table, norms, contact_head, ids_all, ids_ri, ids_ir, targets_ir, pair_first, pair_second, labels, counts, cw):
    in_row, in_col, out_row, out_col, up_w, down_t = big
    rows, cols = ids_all.shape
    here = rows * cw
    row_scale = (HD * rows) ** (-0.5)
    vocab = jnp.arange(VP)[:, None]
    hot_all = (ids_all[:, None, :] == vocab[None]).astype(BF16).reshape(rows * VP, cols)
    hot_ri = (ids_ri[None, :] == vocab).astype(BF16)
    hot_ir = (ids_ir[None, :] == vocab).astype(BF16)
    spot = jnp.arange(here)
    perm = (
        ((spot // rows)[:, None] == (spot % cw)[None, :])
        & ((spot % rows)[:, None] == (spot // cw)[None, :])
    ).astype(BF16)

    def to_heads(block):
        return block.reshape(rows, cw, HEADS, VP).transpose(2, 1, 0, 3).reshape(HEADS * cw, rows * VP)

    def to_tokens(block):
        return block.reshape(HEADS, cw, rows, VP).transpose(2, 1, 0, 3).reshape(here, HEADS * VP)

    def per_head(block, other, how):
        return jnp.concatenate(
            [how(heads_of(block, h), heads_of(other, h)) for h in range(HEADS)], -1
        )

    table_f = table.astype(F32)
    unit_t, rstd_t = norm_stats(table_f)
    normed_t = (unit_t * norms[0] + norms[4]).astype(BF16)
    proj_t = nn(normed_t, in_row).astype(BF16)
    query_t, key_t, value_t = proj_t[:, :D], proj_t[:, D : 2 * D], proj_t[:, 2 * D :]

    pair_t = per_head(query_t, key_t, nt)
    pair_hi, pair_lo = split_two(pair_t)
    left_hi = to_heads(tn(hot_ri, pair_hi).astype(BF16))
    left_lo = to_heads(tn(hot_ri, pair_lo).astype(BF16))
    score = (nn(left_hi, hot_all) + nn(left_lo, hot_all)) * row_scale
    prob = jax.nn.softmax(score, axis=-1)
    prob_low = prob.astype(BF16)
    weight_t = to_tokens(nt(prob_low, hot_all))
    weight_hi, weight_lo = split_two(weight_t)
    row_mixed_ri = (
        per_head(weight_hi, value_t, nn) + per_head(weight_lo, value_t, nn)
    ).astype(BF16)
    row_mixed = nn(perm, row_mixed_ri).astype(BF16)
    embedded = tn(hot_ir, table)
    after_row = embedded + nn(row_mixed, out_row)

    prob_cube = prob_low.astype(F32).reshape(HEADS, cw, cols)
    head_sum = jnp.sum(prob_cube * contact_head[:HEADS, None, None], 0)
    first_hot = (pair_first[None, :] == jnp.arange(cw)[:, None]).astype(F32)
    second_hot = (pair_second[None, :] == jnp.arange(cols)[:, None]).astype(BF16)
    sum_hi, sum_lo = split_two(head_sum)
    sum_last = (head_sum - sum_hi.astype(F32) - sum_lo.astype(F32)).astype(BF16)
    picked = nn(sum_hi, second_hot) + nn(sum_lo, second_hot) + nn(sum_last, second_hot)
    contact_logit = jnp.sum(picked * first_hot, 0) * cols + contact_head[HEADS]
    owned = jnp.sum(first_hot, 0) > 0
    valid = (labels >= 0) & owned
    positive = (labels == 1).astype(F32)
    bce_sum = jnp.sum(
        jnp.where(valid, jax.nn.softplus(contact_logit) - positive * contact_logit, 0.0)
    )
    coef = jnp.where(valid, jax.nn.sigmoid(contact_logit) - positive, 0.0) / counts[1]
    coef_hi, coef_lo = split_two(coef)
    first_low = first_hot.astype(BF16)
    touch = nt(first_low * coef_hi[None], second_hot) + nt(first_low * coef_lo[None], second_hot)
    grad_contact = jnp.concatenate(
        [jnp.sum(prob_cube * touch[None], (1, 2)) * cols, jnp.sum(coef)[None]]
    )

    unit_1, rstd_1 = norm_stats(after_row)
    col_normed = (unit_1 * norms[1] + norms[5]).astype(BF16)
    col_proj = nn(col_normed, in_col).astype(BF16)
    group = 128 if here % 128 == 0 and 128 % rows == 0 else here
    groups = here // group
    lane = jnp.arange(group)
    same = (lane[:, None] // rows) == (lane[None, :] // rows)

    def cut(block):
        return block.reshape(groups, group, HEADS, HD)

    col_query, col_key, col_value = (cut(col_proj[:, k * D : (k + 1) * D]) for k in range(3))
    col_score = jnp.einsum("gqhe,gkhe->ghqk", col_query, col_key, preferred_element_type=F32) * HD ** (-0.5)
    col_prob = jax.nn.softmax(jnp.where(same, col_score, -1e30), axis=-1)
    col_prob_low = col_prob.astype(BF16)
    col_mixed = (
        jnp.einsum("ghqk,gkhe->gqhe", col_prob_low, col_value, preferred_element_type=F32)
        .astype(BF16)
        .reshape(here, D)
    )
    after_col = after_row + nn(col_mixed, out_col)

    unit_2, rstd_2 = norm_stats(after_col)
    feed_normed = (unit_2 * norms[2] + norms[6]).astype(BF16)
    hidden_up = nn(feed_normed, up_w)
    active, slope = gelu_parts(hidden_up)
    active = active.astype(BF16)
    after_feed = after_col + nt(active, down_t)
    unit_3, rstd_3 = norm_stats(after_feed)
    head_normed = (unit_3 * norms[3] + norms[7]).astype(BF16)
    logits = nt(table, head_normed) * D ** (-0.5)
    logits = jnp.where(vocab < VOCAB, logits, -1e30)
    top = jnp.max(logits, 0, keepdims=True)
    shifted = logits - top
    log_probs = shifted - jnp.log(jnp.sum(jnp.exp(shifted), 0, keepdims=True))
    target_hot = (targets_ir[None, :] == vocab).astype(F32)
    keep = ids_ir[None, :] == MASK_ID
    mlm_sum = -jnp.sum(jnp.where(keep & (target_hot > 0), log_probs, 0.0))
    logit_grad = jnp.where(keep, jnp.exp(log_probs) - target_hot, 0.0) / counts[0]
    logit_low = (logit_grad * D ** (-0.5)).astype(BF16)

    grad_head = nn(logit_low, head_normed)
    stream, scale_3, shift_3 = norm_back(unit_3, rstd_3, norms[3], tn(logit_low, table))
    branch = stream.astype(BF16)
    grad_down = tn(branch, active)
    up_low = (nn(branch, down_t) * slope).astype(BF16)
    grad_up = tn(feed_normed, up_low)
    inner, scale_2, shift_2 = norm_back(unit_2, rstd_2, norms[2], nt(up_low, up_w))
    stream = stream + inner
    branch = stream.astype(BF16)
    grad_out_col = tn(col_mixed, branch)
    mixed_low = nt(branch, out_col).astype(BF16)
    mixed_cut = cut(mixed_low)
    prob_grad = jnp.einsum("gqhe,gkhe->ghqk", mixed_cut, col_value, preferred_element_type=F32)
    score_grad = col_prob * (prob_grad - jnp.sum(col_prob * prob_grad, -1, keepdims=True))
    score_low = score_grad.astype(BF16)
    grad_q = jnp.einsum("ghqk,gkhe->gqhe", score_low, col_key, preferred_element_type=F32)
    grad_k = jnp.einsum("ghqk,gqhe->gkhe", score_low, col_query, preferred_element_type=F32)
    grad_v = jnp.einsum("ghqk,gqhe->gkhe", col_prob_low, mixed_cut, preferred_element_type=F32)
    proj_low = jnp.concatenate(
        [
            (grad_q * HD ** (-0.5)).reshape(here, D),
            (grad_k * HD ** (-0.5)).reshape(here, D),
            grad_v.reshape(here, D),
        ],
        -1,
    ).astype(BF16)
    grad_in_col = tn(col_normed, proj_low)
    inner, scale_1, shift_1 = norm_back(unit_1, rstd_1, norms[1], nt(proj_low, in_col))
    stream = stream + inner
    branch = stream.astype(BF16)
    grad_out_row = tn(row_mixed, branch)
    mixed_low = nt(branch, out_row).astype(BF16)
    mixed_ri = tn(perm, mixed_low).astype(BF16)
    drive_hi, drive_lo = split_two(per_head(mixed_ri, value_t, nt))
    prob_grad = nn(to_heads(drive_hi), hot_all) + nn(to_heads(drive_lo), hot_all)
    prob_grad = prob_grad + (
        touch[None] * (contact_head[:HEADS, None, None] * cols)
    ).reshape(HEADS * cw, cols)
    score_grad = prob * (prob_grad - jnp.sum(prob * prob_grad, -1, keepdims=True))
    score_low = score_grad.astype(BF16)
    spread = to_tokens(nt(score_low, hot_all)).astype(BF16)
    table_pair = nn(hot_ri, spread)
    value_grad = per_head(weight_hi, mixed_ri, tn)
    stream_hi, stream_lo = split_two(stream)
    lookup_grad = nn(hot_ir, stream_hi) + nn(hot_ir, stream_lo)
    vectors = jnp.stack([scale_1, scale_2, scale_3, shift_1, shift_2, shift_3])
    return (
        (grad_in_col, grad_out_row, grad_out_col, grad_up, grad_down),
        (table_pair, value_grad, grad_head + lookup_grad, vectors),
        grad_contact,
        mlm_sum,
        bce_sum,
        (unit_t, rstd_t, normed_t, query_t, key_t),
    )


MESH = pl.DeviceIdType.MESH
NZ, NY = 4, 2


def place():
    s, c = lax.axis_index("seq"), lax.axis_index("col")
    z, y, k = s // 4, lax.rem(s // 2, 2), lax.rem(s, 2)
    return z, y, k, c


def device(z, y, k, c):
    return (z * 4 + y * 2 + k, c)


def greet_all():
    z, y, k, c = place()
    me = (z * 4 + y * 2 + k) * 2 + c
    barrier = pltpu.get_barrier_semaphore()

    def signal(step, carry):
        other = lax.rem(me + step, 32)
        pl.semaphore_signal(
            barrier, inc=1, device_id=(other // 2, lax.rem(other, 2)), device_id_type=MESH
        )
        return carry

    lax.fori_loop(1, 32, signal, 0)
    return barrier


def remote(src, dst, send, recv, target):
    return pltpu.make_async_remote_copy(
        src_ref=src, dst_ref=dst, send_sem=send, recv_sem=recv, device_id=target, device_id_type=MESH
    )


ROWS, COLS, WIDE, HERE = 16, 512, 32, 512
PAIRS = 6
SLOTS = 1024
UP_TILE = 384


def iota(shape, dim):
    return lax.broadcasted_iota(jnp.int32, shape, dim)


def one_zero(test):
    return jnp.where(test, 1.0, 0.0)


def total_of(values):
    return jnp.sum(jnp.sum(values, 0, keepdims=True), 1, keepdims=True)


def half_lanes(values, side):
    lane = iota(values.shape, len(values.shape) - 1)
    keep = (lane < 64) if side == 0 else (lane >= 64)
    return jnp.where(keep, values.astype(F32), 0.0).astype(BF16)


def stacked(values):
    return jnp.concatenate([half_lanes(values, 0), half_lanes(values, 1)], 0)


def unstacked(values, count):
    lane = iota((count, 128), 1)
    return jnp.where(lane < 64, values[:count], values[count:])


def swap_blocks(first, second):
    lane = iota(first.shape, 1)
    low = jnp.where(lane < 64, first, pltpu.roll(second, 64, 1))
    high = jnp.where(lane < 64, pltpu.roll(first, 64, 1), second)
    return low, high


def split_heads_to(source, high_ref, low_ref):
    for rp in range(ROWS // 2):
        for hp in range(PAIRS):
            lanes = slice(hp * 128, hp * 128 + 128)
            first = source[rp * 64 : rp * 64 + 32, lanes]
            second = source[rp * 64 + 32 : rp * 64 + 64, lanes]
            for side, block in enumerate(swap_blocks(first, second)):
                top, rest = split_two(block)
                rows = slice((2 * hp + side) * 32, (2 * hp + side) * 32 + 32)
                high_ref[rows, rp * 128 : rp * 128 + 128] = top
                low_ref[rows, rp * 128 : rp * 128 + 128] = rest


def merge_heads(probs, hot_all, high_ref, low_ref):
    for rp in range(ROWS // 2):
        if rp % 2 == 0:
            blocks = nt(probs, hot_all[rp * 128 : rp * 128 + 256, :])
        block = blocks[:, (rp % 2) * 128 : (rp % 2) * 128 + 128]
        for hp in range(PAIRS):
            first = block[hp * 64 : hp * 64 + 32]
            second = block[hp * 64 + 32 : hp * 64 + 64]
            for side, part in enumerate(swap_blocks(first, second)):
                top, rest = split_two(part)
                rows = slice(rp * 64 + side * 32, rp * 64 + side * 32 + 32)
                high_ref[rows, hp * 128 : hp * 128 + 128] = top
                if low_ref is not None:
                    low_ref[rows, hp * 128 : hp * 128 + 128] = rest


def norm_rows(source, gain, bias, unit_ref, rstd_ref, normed_ref):
    def body(at, carry):
        rows = pl.ds(pl.multiple_of(at * 64, 64), 64)
        values = source[rows, :]
        centre = values - jnp.sum(values, -1, keepdims=True) * (1.0 / D)
        rstd = lax.rsqrt(jnp.sum(centre * centre, -1, keepdims=True) * (1.0 / D) + NORM_EPS)
        unit = centre * rstd
        unit_ref[rows, :] = unit
        rstd_ref[rows, :] = jnp.broadcast_to(rstd, (64, 128))
        normed_ref[rows, :] = (unit * gain + bias).astype(BF16)
        return carry

    lax.fori_loop(0, HERE // 64, body, 0, unroll=2)


def transpose_into(source, target):
    def body(at, carry):
        rows = pl.ds(pl.multiple_of(at * 128, 128), 128)
        target[:, rows] = source[rows, :].astype(F32).T.astype(BF16)
        return carry

    lax.fori_loop(0, HERE // 128, body, 0)


def over_tiles(width, tile, body):
    for half in range(2):

        def step(at, carry, half=half):
            body(half, pl.multiple_of(at * tile, tile))
            return carry

        lax.fori_loop(0, width // tile, step, 0)


def column_mask():
    rows, lanes = iota((256, 128), 0), iota((256, 128), 1)
    return ((rows & 127) >> 4) == (lanes >> 4)


class Saved(typing.NamedTuple):
    stream: typing.Any
    branch: typing.Any
    unit_1: typing.Any
    unit_2: typing.Any
    rstd_1: typing.Any
    rstd_2: typing.Any
    row_mixed_t: typing.Any
    col_normed_t: typing.Any
    col_mixed_t: typing.Any
    feed_normed_t: typing.Any
    col_proj: typing.Any
    col_prob: typing.Any
    active: typing.Any
    slope: typing.Any
    grad_head: typing.Any
    hot_all: typing.Any
    hot_ri: typing.Any
    hot_ir: typing.Any
    prob: typing.Any
    weight_hi: typing.Any
    value_two: typing.Any
    touch: typing.Any
    table: typing.Any
    norms: typing.Any
    proj_t: typing.Any
    extras: typing.Any
    moved: typing.Any


AT = Saved(*range(len(Saved._fields)))
SAVED = Saved(
    stream=((HERE, D), F32),
    branch=((HERE, D), BF16),
    unit_1=((HERE, D), F32),
    unit_2=((HERE, D), F32),
    rstd_1=((HERE, 128), F32),
    rstd_2=((HERE, 128), F32),
    row_mixed_t=((D, HERE), BF16),
    col_normed_t=((D, HERE), BF16),
    col_mixed_t=((D, HERE), BF16),
    feed_normed_t=((D, HERE), BF16),
    col_proj=((HERE, 3 * D), BF16),
    col_prob=((4 * PAIRS, 256, 128), F32),
    active=((HERE, FF), BF16),
    slope=((HERE, FF), BF16),
    grad_head=((VP, D), F32),
    hot_all=((ROWS * VP, COLS), BF16),
    hot_ri=((VP, HERE), BF16),
    hot_ir=((VP, HERE), BF16),
    prob=((HEADS * WIDE, COLS), F32),
    weight_hi=((HERE, D), BF16),
    value_two=((PAIRS, 128, 128), BF16),
    touch=((WIDE, COLS), F32),
    table=((VP, D), F32),
    norms=((8, D), F32),
    proj_t=((VP, 3 * D), BF16),
    extras=((8, 128), F32),
    moved=((8, D), F32),
)


class Forward(typing.NamedTuple):
    ids: typing.Any
    targets: typing.Any
    slots: typing.Any
    normed: typing.Any
    mixed: typing.Any
    normed_2: typing.Any
    mixed_2: typing.Any
    second_hot: typing.Any
    weight_lo: typing.Any
    left_hi: typing.Any
    left_lo: typing.Any
    lookup: typing.Any
    prob_low: typing.Any
    unit: typing.Any
    rstd: typing.Any


FORWARD = Forward(
    ids=((ROWS, COLS), jnp.int32),
    targets=((ROWS, 128), jnp.int32),
    slots=((8, SLOTS), jnp.int32),
    normed=((HERE, D), BF16),
    mixed=((HERE, D), BF16),
    normed_2=((HERE, D), BF16),
    mixed_2=((HERE, D), BF16),
    second_hot=((COLS, SLOTS), BF16),
    weight_lo=((HERE, D), BF16),
    left_hi=((HEADS * WIDE, ROWS * VP), BF16),
    left_lo=((HEADS * WIDE, ROWS * VP), BF16),
    lookup=((HERE, D), F32),
    prob_low=((HEADS * WIDE, COLS), BF16),
    unit=((HERE, D), F32),
    rstd=((HERE, 128), F32),
)


def position():
    z, y, k, c = place()
    me = (z * 4 + y * 2 + k) * 2 + c
    return z // 2, lax.rem(me, 16)


def read_tokens(small, f):
    alignment, block = position()
    side, part = block // 8, lax.rem(block // 4, 2)
    for r in range(ROWS):
        for cc in range(2):
            for q in range(2):
                lanes = slice(cc * 256 + q * 128, cc * 256 + q * 128 + 128)
                f.ids[r : r + 1, lanes] = small[r * 2 + cc, pl.ds(2 * alignment + q, 1), :]
        f.targets[r : r + 1, :] = small[r * 2 + side, pl.ds(4 + 2 * alignment + part, 1), :]
    lane = iota((1, 128), 1)
    for number in range(SLOTS // 128):
        for which in range(3):
            row = pl.ds(8 + 3 * alignment + which, 1)
            first = small[number * 4 + side, row, :]
            second = pltpu.roll(small[number * 4 + 2 + side, row, :], 64, 1)
            f.slots[which : which + 1, number * 128 : number * 128 + 128] = jnp.where(
                lane < 64, first, second
            )


def local_hot(values, shift):
    values = pltpu.roll(values, shift, 1)
    turned = [values] + [pltpu.roll(values, 32 * n, 1) for n in (1, 2, 3)]
    lane = iota((1, 128), 1)
    tiles = []
    for tile in range(4):
        row = turned[3][4 * tile + 3 : 4 * tile + 4]
        for n in (2, 1, 0):
            row = jnp.where(lane < 32 * n + 32, turned[n][4 * tile + n : 4 * tile + n + 1], row)
        tiles.append(row)
    row = jnp.concatenate(tiles, 1)
    return one_zero(row == iota((VP, HERE), 0)).astype(BF16)


def contact_part(contact_head, f, s, pair_count):
    _, block = position()
    base = block * WIDE
    head_sum = jnp.zeros((WIDE, COLS), F32)
    for h in range(HEADS):
        head_sum = head_sum + contact_head[h] * f.prob_low[h * 32 : h * 32 + 32, :].astype(F32)
    top, rest = split_two(head_sum)
    last = (head_sum - top.astype(F32) - rest.astype(F32)).astype(BF16)
    parts = jnp.concatenate([top, rest, last], 0)
    touch = jnp.zeros((WIDE, COLS), F32)
    bce = jnp.zeros((1, 1), F32)
    coef_sum = jnp.zeros((1, 1), F32)
    for number in range(SLOTS // 512):
        lanes = slice(number * 512, number * 512 + 512)
        first, label = (f.slots[n : n + 1, lanes] for n in (0, 2))
        second_hot = f.second_hot[:, lanes]
        picked = nn(parts, second_hot)
        picked = picked[:32] + picked[32:64] + picked[64:]
        first_hot = one_zero((first - base) == iota((WIDE, 512), 0))
        logit = jnp.sum(picked * first_hot, 0, keepdims=True) * COLS + contact_head[HEADS]
        owned = jnp.sum(first_hot, 0, keepdims=True) > 0.5
        valid = (label >= 0) & owned
        positive = one_zero(label == 1)
        small = jnp.exp(-jnp.abs(logit))
        soft = jnp.maximum(logit, 0.0) + jnp.log(1.0 + small)
        bce = bce + total_of(jnp.where(valid, soft - positive * logit, 0.0))
        sigmoid = jnp.where(logit >= 0.0, 1.0, small) / (1.0 + small)
        coef = jnp.where(valid, sigmoid - positive, 0.0) / pair_count
        coef_sum = coef_sum + total_of(coef)
        coef_top, coef_rest = split_two(first_hot * coef)
        touch = touch + nt(coef_top, second_hot) + nt(coef_rest, second_hot)
    s.touch[...] = touch
    column = iota((1, 128), 1)
    row = jnp.where(column == HEADS, coef_sum, 0.0)
    for h in range(HEADS):
        part = total_of(touch * f.prob_low[h * 32 : h * 32 + 32, :].astype(F32)) * COLS
        row = row + jnp.where(column == h, part, 0.0)
    return row, bce


def feature_order():
    shape = (384, 384)
    spot = iota(shape, 0)
    block = (spot * 2731) >> 16
    swapped = (block & 28) | ((block & 1) << 1) | ((block >> 1) & 1)
    return one_zero(spot + (swapped - block) * 24 == iota(shape, 1)).astype(BF16)


def forward_body(small, contact_head, weights, s, f, cells, projected, hook, emit):
    out_row, in_col, out_col = weights[:3]
    up_parts, down_parts = weights[3:5], weights[5:7]
    hook()
    features = cells()
    ahead = (
        ((iota((HERE, HERE), 0) >> 4) == (iota((HERE, HERE), 1) & 31))
        & ((iota((HERE, HERE), 0) & 15) == (iota((HERE, HERE), 1) >> 5))
    )
    ahead = one_zero(ahead).astype(BF16)
    read_tokens(small, f)
    _, block = position()
    shift = lax.rem(128 - lax.rem(block, 4) * 32, 128)
    window = pl.ds(pl.multiple_of((block // 4) * 128, 128), 128)
    hot_ri = local_hot(f.ids[:, window], shift)
    goal_ri = local_hot(f.targets[...], shift)
    s.hot_ri[...] = hot_ri
    for number in range(SLOTS // 512):
        lanes = slice(number * 512, number * 512 + 512)
        f.second_hot[:, lanes] = one_zero(f.slots[1:2, lanes] == iota((COLS, 512), 0)).astype(BF16)
    for r in range(ROWS):
        row = f.ids[r : r + 1, :]
        s.hot_all[r * VP : r * VP + VP, :] = one_zero(row == iota((VP, COLS), 0)).astype(BF16)
    shape = (HERE, HERE)
    back = (
        ((iota(shape, 1) >> 4) == (iota(shape, 0) & 31))
        & ((iota(shape, 1) & 15) == (iota(shape, 0) >> 5))
    )
    back = one_zero(back).astype(BF16)
    hot_ir = nn(hot_ri, back).astype(BF16)
    s.hot_ir[...] = hot_ir
    goal = nn(goal_ri, back)
    entries = jnp.zeros((4, 128), F32)
    labelled = jnp.zeros((1, 128), F32)
    for d in range(32):
        entries = entries + one_zero(small[d, 0:4, :] == MASK_ID)
        labelled = labelled + one_zero(small[d, 10:11, :] >= 0) + one_zero(small[d, 13:14, :] >= 0)
    entries, labelled = total_of(entries), total_of(labelled)

    hook()
    features = features[...].T
    table = features[:VP]
    norms = features[VP : VP + 8]
    s.table[...] = table
    s.norms[...] = norms
    table_low = table.astype(BF16)

    def vector(number):
        return norms[number : number + 1, :]

    hook()
    projected(s.proj_t)
    pair_parts = []
    for hp in range(PAIRS):
        lanes = slice(hp * 128, hp * 128 + 128)
        key = s.proj_t[:, D + hp * 128 : D + hp * 128 + 128]
        value = s.proj_t[:, 2 * D + hp * 128 : 2 * D + hp * 128 + 128]
        s.value_two[hp] = stacked(value)
        pair_parts.append(nt(s.proj_t[:, lanes], stacked(key)))
    pair_hi, pair_lo = split_two(jnp.concatenate(pair_parts, 1))
    hook()
    f.lookup[...] = tn(hot_ri, pair_hi) + tn(hot_ri, pair_lo)
    split_heads_to(f.lookup, f.left_hi, f.left_lo)
    hook()
    hot_all = s.hot_all[...]
    score = (nn(f.left_hi[...], hot_all) + nn(f.left_lo[...], hot_all)) * (HD * ROWS) ** (-0.5)
    score = jnp.exp(score - jnp.max(score, -1, keepdims=True))
    prob = score / jnp.sum(score, -1, keepdims=True)
    s.prob[...] = prob
    f.prob_low[...] = prob.astype(BF16)
    hook()
    merge_heads(f.prob_low[...], s.hot_all, s.weight_hi, f.weight_lo)
    hook()
    for hp in range(PAIRS):
        lanes = slice(hp * 128, hp * 128 + 128)
        value = s.value_two[hp]
        both = jnp.concatenate([s.weight_hi[:, lanes], f.weight_lo[:, lanes]], 1)
        f.mixed[:, lanes] = nn(both, jnp.concatenate([value, value], 0)).astype(BF16)
    f.mixed[...] = nn(ahead, f.mixed[...]).astype(BF16)
    s.stream[...] = tn(hot_ir, table_low)
    emit(AT.hot_all, AT.hot_ri, AT.hot_ir, AT.table, AT.norms, AT.proj_t, AT.value_two, AT.prob, AT.weight_hi)
    hook()
    for half in range(2):
        lanes = slice(half * 384, half * 384 + 384)
        s.stream[:, lanes] += nn(f.mixed[...], out_row[half])
    norm_rows(s.stream, vector(1), vector(5), s.unit_1, s.rstd_1, f.normed)
    emit(AT.unit_1, AT.rstd_1)

    def project(half, at):
        s.col_proj[:, half * 1152 + at : half * 1152 + at + 384] = nn(
            f.normed[...], in_col[half, :, at : at + 384]
        ).astype(BF16)

    for third in range(3):
        hook()
        for half in range(2):
            project(half, third * 384)
    emit(AT.col_proj)

    def attend(at, carry):
        rows = pl.ds(pl.multiple_of((at // PAIRS) * 128, 128), 128)
        lane = lax.rem(at, PAIRS) * 128

        def lanes(part):
            return pl.ds(pl.multiple_of(part * D + lane, 128), 128)

        query = stacked(s.col_proj[rows, lanes(0)])
        score = nt(query, s.col_proj[rows, lanes(1)]) * HD ** (-0.5)
        score = jnp.where(column_mask(), score, -1e30)
        score = jnp.exp(score - jnp.max(score, -1, keepdims=True))
        prob = score / jnp.sum(score, -1, keepdims=True)
        s.col_prob[at] = prob
        mixed = nn(prob.astype(BF16), s.col_proj[rows, lanes(2)])
        f.mixed_2[rows, lanes(0)] = unstacked(mixed, 128).astype(BF16)
        return carry

    for part in range(4):
        hook()
        lax.fori_loop(part * PAIRS, part * PAIRS + PAIRS, attend, 0, unroll=3)
    hook()
    emit(AT.col_prob)
    for half in range(2):
        lanes = slice(half * 384, half * 384 + 384)
        s.stream[:, lanes] += nn(f.mixed_2[...], out_col[half])
    norm_rows(s.stream, vector(2), vector(6), s.unit_2, s.rstd_2, f.normed_2)
    emit(AT.unit_2, AT.rstd_2)
    hook()
    contact_row, bce = contact_part(contact_head, f, s, labelled)
    emit(AT.touch)
    for part in range(2):

        def widen(half, at, part=part):
            lanes = slice(part * 1536 + half * 768 + at, part * 1536 + half * 768 + at + UP_TILE)
            up = nn(f.normed_2[...], up_parts[part][half, :, at : at + UP_TILE])
            active, slope = gelu_parts(up)
            s.active[:, lanes] = active.astype(BF16)
            s.slope[:, lanes] = slope.astype(BF16)

        for half in range(2):
            hook()
            for at in range(0, 768, UP_TILE):
                widen(half, at)
        hook()
        if part == 0:
            transpose_into(f.mixed, s.row_mixed_t)
            transpose_into(f.normed, s.col_normed_t)
            emit(AT.row_mixed_t, AT.col_normed_t)
        else:
            transpose_into(f.mixed_2, s.col_mixed_t)
            emit(AT.col_mixed_t)

    emit(AT.active, AT.slope)
    for part, at, size in ((0, 0, 768), (1, 0, 384), (1, 384, 384)):
        hook()
        added = []
        for half in range(2):
            start = part * 1536 + half * 768 + at
            matrix = down_parts[part][half, :, at : at + size]
            added.append(nt(s.active[:, start : start + size], matrix))
        s.stream[...] += added[0] + added[1]
        if part == 0:
            hook()
            transpose_into(f.normed_2, s.feed_normed_t)
            emit(AT.feed_normed_t)
    hook()
    norm_rows(s.stream, vector(3), vector(7), f.unit, f.rstd, f.normed)
    logits = nt(table_low, f.normed[...]) * D ** (-0.5)
    vocab = iota((VP, HERE), 0)
    logits = jnp.where(vocab < VOCAB, logits, -1e30)
    shifted = logits - jnp.max(logits, 0, keepdims=True)
    log_probs = shifted - jnp.log(jnp.sum(jnp.exp(shifted), 0, keepdims=True))
    keep = hot_ir[MASK_ID : MASK_ID + 1].astype(F32) > 0.5
    mlm = -total_of(jnp.where(keep & (goal > 0.5), log_probs, 0.0))
    logit_grad = jnp.where(keep, jnp.exp(log_probs) - goal, 0.0) / entries
    logit_low = (logit_grad * D ** (-0.5)).astype(BF16)
    s.grad_head[...] = nn(logit_low, f.normed[...])
    hook()
    f.lookup[...] = tn(logit_low, table_low)
    scale_3, shift_3 = back_rows(f.unit, f.rstd, vector(3), f.lookup, s.stream, s.branch, True)
    emit(AT.stream, AT.branch)
    line = iota((8, D), 0)
    s.moved[...] = jnp.where(line == 0, scale_3, jnp.where(line == 1, shift_3, 0.0))
    column = iota((1, 128), 1)
    row = contact_row + jnp.where(column == HEADS + 1, mlm, 0.0) + jnp.where(column == HEADS + 2, bce, 0.0)
    counted = jnp.where(column == 0, entries, 0.0) + jnp.where(column == 1, labelled, 0.0)
    line = iota((8, 128), 0)
    s.extras[...] = jnp.where(line == 0, row, jnp.where(line == 1, counted, 0.0))
    emit(AT.grad_head, AT.extras, AT.moved)
    hook()


def back_rows(unit_ref, rstd_ref, gain, upstream_ref, stream_ref, low_ref, first):
    def body(at, carry):
        scale, move = carry
        rows = pl.ds(pl.multiple_of(at * 64, 64), 64)
        upstream = upstream_ref[rows, :]
        unit = unit_ref[rows, :]
        inner = upstream * gain
        mean = jnp.sum(inner, -1, keepdims=True) * (1.0 / D)
        along = jnp.sum(inner * unit, -1, keepdims=True) * (1.0 / D)
        grad = rstd_ref[rows, 0:1] * (inner - mean - unit * along)
        if not first:
            grad = grad + stream_ref[rows, :]
        stream_ref[rows, :] = grad
        low_ref[rows, :] = grad.astype(BF16)
        touched = upstream * unit
        for n in range(8):
            scale = scale + touched[n * 8 : n * 8 + 8]
            move = move + upstream[n * 8 : n * 8 + 8]
        return scale, move

    zero = jnp.zeros((8, D), F32)
    scale, move = lax.fori_loop(0, HERE // 64, body, (zero, zero), unroll=2)
    return jnp.sum(scale, 0, keepdims=True), jnp.sum(move, 0, keepdims=True)


MATRICES = (128, 384, 1152, 384, 768, 768, 768, 768)
UNITS = (
    (0, 0, 128, True),
    (1, 0, 384, False),
    (2, 0, 384, True),
    (2, 384, 384, True),
    (2, 768, 384, True),
    (3, 0, 384, False),
    (4, 0, 768, True),
    (5, 0, 768, True),
    (6, 0, 768, True),
    (7, 0, 384, True),
    (7, 384, 384, True),
)
Z_LAST = {9: 1, 10: 2}
FORWARD_ORDER = (
    ((0, 0), (0, 2), (0, 11), (1, 0), (0, 1), (0, 9), (0, 10), (1, 11), (2, 0), (0, 3), (1, 2), (0, 4), (2, 11), (3, 0), (1, 10), (1, 9), (1, 1), (4, 0),),
    ((2, 2), (0, 5), (2, 1),),
    ((3, 11), (1, 3), (0, 6), (3, 2), (4, 11), (1, 4),),
    ((3, 1), (4, 2), (1, 5), (0, 7),),
    ((4, 1), (2, 3), (2, 4),),
    ((1, 6), (0, 8),),
    (),
    ((3, 3),),
    ((3, 4), (2, 5), (4, 3), (2, 9), (1, 7), (4, 4),),
    (),
    (),
    (),
    ((3, 5), (2, 6),),
    (),
    ((4, 5), (2, 7), (2, 10),),
    ((1, 8),),
    ((3, 6),),
    ((3, 9), (3, 7), (4, 6),),
    (),
    ((2, 8), (4, 9),),
    ((4, 7),),
    (),
    (),
    ((3, 8), (3, 10), (4, 8),),
    ((4, 10),),
    (),
    (),
    (),
    (),
    (),
)


def spot(paired, cc, zz, yy, k):
    return (k, zz, yy, cc) if paired else (cc, zz, yy, k)


def forward_kernel(*refs):
    count, parts = len(UNITS), len(MATRICES)
    raw = refs[:11]
    contact_head = refs[11]
    at = 12
    far = (None, *refs[at : at + parts - 1])
    saved_far = refs[at + parts - 1 : at + parts - 1 + len(SAVED)]
    at += parts - 1 + len(SAVED)
    outs = refs[at : at + parts]
    at += parts
    outgoing = refs[at : at + count]
    incoming = refs[at + count : at + 2 * count]
    piece = refs[at + 2 * count : at + 3 * count]
    at += 3 * count
    saved = Saved(*refs[at : at + len(SAVED)])
    at += len(SAVED)
    scratch = Forward(*refs[at : at + len(FORWARD)])
    at += len(FORWARD)
    near = refs[at : at + 11]
    at += 11
    small, small_out, corner, features, stat, stat_got, part, part_got, part_line, proj, room = refs[at : at + 11]
    small_send, small_recv, send, recv, local, out_sem, raw_sem, twin_send, twin_recv = refs[at + 11 :]
    tokens, targets, masked, pairs, labels, table, norms, in_w, out_w, up_w, down_w = near
    z, y, k, c = place()
    me = (z * 4 + y * 2 + k) * 2 + c
    raw_copies = [pltpu.make_async_copy(a, b, raw_sem.at[n]) for n, (a, b) in enumerate(zip(raw, near))]
    for item in raw_copies:
        item.start()
    barrier = greet_all()
    for item in raw_copies[:7]:
        item.wait()
    small[...] = jnp.full(small.shape, -1, jnp.int32)
    for micro in range(2):
        for half in range(2):
            lanes = slice(half * 128, half * 128 + 128)
            row = 2 * micro + half
            small[row : row + 1, :] = jnp.where(
                masked[micro, :, lanes] > 0, MASK_ID, tokens[micro, :, lanes]
            )
            small[4 + row : 5 + row, :] = targets[micro, :, lanes]
        row = 8 + 3 * micro
        for which in range(2):
            small[row + which : row + which + 1, 0:64] = pairs[micro, which : which + 1, :]
        small[row + 2 : row + 3, 0:64] = labels[micro : micro + 1, :]
    corner[...] = jnp.zeros(corner.shape, F32)
    corner[0:8, 0:24] = norms[...]
    vectors = pltpu.roll(corner[...].T[:24], 64, 1)
    corner[0:8, 0:24] = jnp.zeros((8, 24), F32)
    corner[0:24, 0:VOCAB] = table[...]
    mine_rows = (corner[0:24, :] + vectors).astype(BF16).astype(F32)
    table_rows = jnp.where(iota((24, 128), 1) < VP, mine_rows, 0.0)
    gain, bias = mine_rows[:, 64:65], mine_rows[:, 68:69]
    piece[0][0:16, :] = small[...].astype(F32)
    piece[0][16:40, :] = mine_rows
    mean = jnp.sum(table_rows, 0, keepdims=True) * (1.0 / 24)
    centre = table_rows - mean
    spread = jnp.sum(centre * centre, 0, keepdims=True)
    line = iota((8, 128), 0)
    stat[...] = jnp.where(line == 0, mean, jnp.where(line == 1, spread, 0.0))
    def master(u, side):
        matrix, start, n, _ = UNITS[u]
        width = MATRICES[matrix]
        if matrix == 2:
            return in_w[1, :, side * 1152 + start : side * 1152 + start + n]
        if matrix in (1, 3):
            rows = out_w[matrix // 2, :, side * 384 : side * 384 + 384].astype(BF16)
            return nn(rows, order)
        begin = (matrix % 2) * 1536 + side * width + start
        return (up_w if matrix < 6 else down_w)[:, begin : begin + n]

    def mine(u):
        return k if UNITS[u][3] else c

    def set_out(u):
        other = jnp.where(mine(u) == 0, master(u, 1), master(u, 0))
        other = jnp.concatenate([other, jnp.zeros((8, UNITS[u][2]), F32)], 0)
        outgoing[u][...] = other.astype(BF16)

    pl.semaphore_wait(barrier, 31)

    def stat_copy(step):
        other = lax.rem(me + step, 32)
        return remote(
            stat, stat_got.at[me], small_send.at[0, step], small_recv.at[0, step], (other // 2, lax.rem(other, 2))
        )

    chip = (z * 2 + y) * 2 + c

    def chip_copy(phase, step):
        other = lax.rem(chip + step, 16)
        target = device(other // 4, lax.rem(other // 2, 2), k, lax.rem(other, 2))
        if phase == 1:
            src, dst = part.at[k, other], part_line.at[chip]
        else:
            src, dst = proj.at[k, chip], proj.at[k, chip]
        return remote(src, dst, small_send.at[phase, step], small_recv.at[phase, step], target)

    def each(last, action):
        def body(step, carry):
            action(step)
            return carry

        lax.fori_loop(1, last, body, 0)

    each(32, lambda step: stat_copy(step).start())

    across, beside, twin = device(z, y, k, 1 - c), device(z, 1 - y, k, c), device(z, y, 1 - k, c)

    def block(u, cc, zz, yy):
        matrix, start, n, paired = UNITS[u]
        where = spot(paired, cc, zz, yy, k)
        if n == MATRICES[matrix]:
            return outs[matrix].at[where]
        return outs[matrix].at[(*where, slice(None), pl.ds(start, n))]

    def copy(u, at, src, dst, target):
        return remote(src, dst, send.at[u, at], recv.at[u, at], target)

    def pair_copy(u):
        return copy(u, 0, outgoing[u], incoming[u], twin if UNITS[u][3] else across)

    def own_copy(u):
        return pltpu.make_async_copy(piece[u], block(u, c, z, y), local.at[u])

    def line_copy(u, step):
        return copy(u, step, piece[u], block(u, c, z, y), device(lax.rem(z + step, 4), y, k, c))

    def same(u, at, cc, zz, yy, target):
        view = block(u, cc, zz, yy)
        return copy(u, at, view, view, target)

    low, high, every = pl.ds(0, 2), pl.ds(2, 2), slice(None)

    def second(u):
        return [same(u, 4, c, low, y, across), same(u, 5, c, high, y, beside)]

    def third_own(u):
        return [same(u, 6, c, low, y, beside), same(u, 7, c, high, y, across)]

    def third_far(u):
        return [same(u, 8, 1 - c, low, y, beside), same(u, 9, c, high, 1 - y, across)]

    def twin_own(u):
        return [same(u, 10, c, every, y, twin)]

    def twin_second(u):
        return [same(u, 11, 1 - c, low, y, twin), same(u, 12, c, high, 1 - y, twin)]

    def twin_third(u):
        return [
            same(u, 13, c, low, 1 - y, twin),
            same(u, 14, 1 - c, high, y, twin),
            same(u, 15, 1 - c, low, 1 - y, twin),
            same(u, 16, 1 - c, high, 1 - y, twin),
        ]

    own_copy(0).start()
    for item in raw_copies[7:]:
        item.wait()
    order = feature_order()
    for u in range(1, count):
        set_out(u)
        pair_copy(u).start()

    def part_twin():
        return remote(part.at[1 - k], part_got, twin_send.at[0], twin_recv.at[0], twin)

    def proj_twin():
        return remote(proj.at[k], proj.at[k], twin_send.at[1], twin_recv.at[1], twin)

    def project_part():
        stat_got[me] = stat[...]
        each(32, lambda step: stat_copy(step).wait())
        means = jnp.zeros((1, 128), F32)
        spreads = jnp.zeros((1, 128), F32)
        for d in range(32):
            means = means + stat_got[d, 0:1, :]
            spreads = spreads + stat_got[d, 1:2, :]
        means = means * (1.0 / 32)
        for d in range(32):
            away = stat_got[d, 0:1, :] - means
            spreads = spreads + 24.0 * away * away
        rstd = lax.rsqrt(spreads * (1.0 / D) + NORM_EPS)
        normed = (table_rows - means) * rstd * gain + bias
        normed = jnp.concatenate([normed, jnp.zeros((8, 128), F32)], 0).astype(BF16)
        for block_at in range(6):
            lanes = slice(block_at * 384, block_at * 384 + 384)
            rows = jnp.concatenate([in_w[0, :, lanes], jnp.zeros((8, 384), F32)], 0).astype(BF16)
            product = tn(normed, rows)
            for group in range(5):
                number = group * 6 + block_at
                part[number // 16, number % 16] = product[group * 8 : group * 8 + 8]
        for number in (30, 31):
            part[number // 16, number % 16] = jnp.zeros((8, 384), F32)
        part_twin().start()

    def project_chip():
        part_twin().wait_recv()
        part[k] = part[k] + part_got[...]
        each(16, lambda step: chip_copy(1, step).start())

    def project_line():
        part_line[chip] = part[k, chip]
        each(16, lambda step: chip_copy(1, step).wait_recv())
        proj[k, chip] = lax.fori_loop(1, 16, lambda at, held: held + part_line[at], part_line[0])
        each(16, lambda step: chip_copy(2, step).start())

    def project_twin():
        each(16, lambda step: chip_copy(2, step).wait_recv())
        proj_twin().start()

    def project_end():
        proj_twin().wait_recv()

    projecting = (project_part, project_chip, project_line, project_twin, project_end)

    def cells():
        for d in range(32):
            at = ((d // 2) % 2, d // 8, (d // 4) % 2, d % 2)
            small_out[d] = outs[0][(*at, slice(0, 16))].astype(jnp.int32)
            start = (((at[1] * 2 + at[2]) * 2 + at[3]) * 2 + at[0]) * 24
            features[start : start + 24, :] = outs[0][(*at, slice(16, 40))]
        return features

    def projected(target):
        room[40:64, :] = jnp.zeros((24, 3 * D), F32)
        for number in range(30):
            rows, lanes = (number // 6) * 8, (number % 6) * 384
            room[rows : rows + 8, lanes : lanes + 384] = proj[number // 16, number % 16]
        target[...] = room[...].astype(BF16)

    def to_across(u):
        return copy(u, 4, piece[u], block(u, c, z, y), across)

    def to_beside(u):
        return copy(u, 5, piece[u], block(u, c, z, y), beside)

    def to_corner(u):
        if Z_LAST[u] == 1:
            return same(u, 6, 1 - c, z, y, beside)
        return same(u, 6, c, z, 1 - y, across)

    def to_line(u):
        return [
            same(u, step, every, z, every, device(lax.rem(z + step, 4), y, k, c)) for step in (1, 3, 2)
        ]

    def to_twin(u):
        return [same(u, 7, every, z, every, twin)]

    def rest_to_twin(u):
        return [same(u, 7 + step, every, lax.rem(z + 4 - step, 4), every, twin) for step in (1, 3, 2)]

    def stage_line(u):
        if u == 0:
            for step in (1, 3, 2):
                line_copy(u, step).start()
            return
        pair_copy(u).wait_recv()
        side = mine(u)
        own = jnp.where(side == 0, master(u, 0), master(u, 1))
        theirs = incoming[u][...].astype(F32)[:24]
        top = jnp.where(side == 0, own, theirs)
        bottom = jnp.where(side == 0, theirs, own)
        piece[u][...] = jnp.concatenate([top, bottom], 0).astype(BF16)
        own_copy(u).start()
        if u in Z_LAST:
            to_across(u).start()
            to_beside(u).start()
            return
        for step in (1, 3, 2):
            line_copy(u, step).start()

    def stage_second(u):
        own_copy(u).wait()
        if u in Z_LAST:
            to_across(u).wait_recv()
            to_beside(u).wait_recv()
            to_corner(u).start()
            return
        for step in (1, 3, 2):
            line_copy(u, step).wait_recv()
        for item in second(u) + third_own(u) + twin_own(u):
            item.start()

    def stage_third(u):
        if u in Z_LAST:
            to_corner(u).wait_recv()
            for item in to_line(u) + to_twin(u):
                item.start()
            return
        for item in second(u):
            item.wait_recv()
        for item in third_far(u) + twin_second(u):
            item.start()

    def stage_twin(u):
        if u in Z_LAST:
            for item in to_line(u):
                item.wait_recv()
            for item in rest_to_twin(u):
                item.start()
            return
        for item in third_own(u) + third_far(u):
            item.wait_recv()
        for item in twin_third(u):
            item.start()

    def far_copy(matrix):
        return pltpu.make_async_copy(outs[matrix], far[matrix], local.at[count + matrix])

    def stage_end(u):
        if u in Z_LAST:
            for item in to_twin(u) + rest_to_twin(u):
                item.wait_recv()
            sent = [to_across(u), to_beside(u), to_corner(u)] + to_line(u) + to_twin(u)
        else:
            for item in twin_own(u) + twin_second(u) + twin_third(u):
                item.wait_recv()
            sent = [line_copy(u, step) for step in (1, 2, 3)]
            sent += second(u) + third_own(u) + third_far(u) + twin_own(u) + twin_second(u)
        for item in sent if u == 0 else [pair_copy(u)] + sent:
            item.wait_send()
        if u == 0:
            return
        if u + 1 == count or UNITS[u + 1][0] != UNITS[u][0]:
            far_copy(UNITS[u][0]).start()

    stages = (stage_line, stage_second, stage_third, stage_twin, stage_end)
    pending = list(FORWARD_ORDER)

    def hook():
        for stage, u in pending.pop(0):
            if u == count:
                projecting[stage]()
            else:
                stages[stage](u)

    def out_copy(at):
        return pltpu.make_async_copy(saved[at], saved_far[at], out_sem.at[at])

    def emit(*numbers):
        for number in numbers:
            out_copy(number).start()

    views = [w.reshape(2, D, n) for w, n in zip(outs[1:], MATRICES[1:])]
    forward_body(small_out, contact_head, views, saved, scratch, cells, projected, hook, emit)
    part_twin().wait_send()
    proj_twin().wait_send()
    for phase in (1, 2):
        each(16, lambda step, phase=phase: chip_copy(phase, step).wait_send())
    assert not pending
    for u in range(count):
        for item in rest_to_twin(u) if u in Z_LAST else twin_third(u):
            item.wait_send()
    for matrix in range(1, parts):
        far_copy(matrix).wait()
    for at in range(len(SAVED)):
        out_copy(at).wait()


def forward_call(raw, contact_head):
    count, parts = len(UNITS), len(MATRICES)
    anywhere = pl.BlockSpec(memory_space=pl.ANY)
    shapes = [(2, NZ, NY, 2, 48, n) for n in MATRICES[1:]]
    widths = [n for _, _, n, _ in UNITS]
    outs = pl.pallas_call(
        forward_kernel,
        out_shape=[jax.ShapeDtypeStruct(shape, BF16) for shape in shapes]
        + [jax.ShapeDtypeStruct(*item) for item in SAVED],
        in_specs=[anywhere] * 11 + [pl.BlockSpec(memory_space=pltpu.SMEM)],
        out_specs=[anywhere] * (parts - 1 + len(SAVED)),
        scratch_shapes=[pltpu.VMEM((2, NZ, NY, 2, 40, 128), F32)]
        + [pltpu.VMEM(shape, BF16) for shape in shapes]
        + [pltpu.VMEM((32, n), BF16) for n in widths] * 2
        + [pltpu.VMEM((40, 128), F32)]
        + [pltpu.VMEM((48, n), BF16) for n in widths[1:]]
        + [pltpu.VMEM(*item) for item in SAVED]
        + [pltpu.VMEM(*item) for item in FORWARD]
        + [pltpu.VMEM(item.shape, item.dtype) for item in raw]
        + [
            pltpu.VMEM((16, 128), jnp.int32),
            pltpu.VMEM((32, 16, 128), jnp.int32),
            pltpu.VMEM((128, 128), F32),
            pltpu.VMEM((D, 128), F32),
            pltpu.VMEM((8, 128), F32),
            pltpu.VMEM((32, 8, 128), F32),
            pltpu.VMEM((2, 16, 8, 384), F32),
            pltpu.VMEM((16, 8, 384), F32),
            pltpu.VMEM((16, 8, 384), F32),
            pltpu.VMEM((2, 16, 8, 384), F32),
            pltpu.VMEM((VP, 3 * D), F32),
            pltpu.SemaphoreType.DMA((3, 32)),
            pltpu.SemaphoreType.DMA((3, 32)),
            pltpu.SemaphoreType.DMA((count, 17)),
            pltpu.SemaphoreType.DMA((count, 17)),
            pltpu.SemaphoreType.DMA((count + parts,)),
            pltpu.SemaphoreType.DMA((len(SAVED),)),
            pltpu.SemaphoreType.DMA((len(raw),)),
            pltpu.SemaphoreType.DMA((2,)),
            pltpu.SemaphoreType.DMA((2,)),
        ],
        compiler_params=pltpu.CompilerParams(
            collective_id=0, has_side_effects=True, vmem_limit_bytes=62 * 2**20
        ),
    )(*raw, contact_head)
    return outs[: parts - 1], Saved(*outs[parts - 1 :])


def summed_rows(sums, group):
    return jnp.concatenate([sums[3 * group + third] for third in range(3)], 1).astype(F32)


def table_finish(sums, room, table_ref, norms_ref, proj_t, in_row, g_in, g_norm, send_stat):
    z, y, k, c = place()
    me = ((z * 2 + y) * 2 + c) * 2 + k
    room[0:128, :] = jnp.zeros((128, D), F32)
    for number in range(2):
        room[4 + 16 * number : 20 + 16 * number, :] = summed_rows(sums, number)
        room[68 + 16 * number : 84 + 16 * number, :] = summed_rows(sums, 2 + number)
    pair = room[0:64, :]
    value_grad = room[64:128, :]
    vectors = summed_rows(sums, 6)
    vectors = vectors[:8] + vectors[8:]
    line = iota((8, D), 0)
    table_grad = jnp.concatenate(
        [
            summed_rows(sums, 4),
            summed_rows(sums, 5),
            jnp.where(line == 0, vectors[7:8], 0.0),
            jnp.zeros((24, D), F32),
        ],
        0,
    )
    pair_hi, pair_lo = split_two(pair)
    scale = (HD * ROWS) ** (-0.5)
    query_grad, key_grad = [], []
    for hp in range(PAIRS):
        lanes = slice(hp * 128, hp * 128 + 128)
        query = proj_t[:, lanes]
        key = stacked(proj_t[:, D + hp * 128 : D + hp * 128 + 128])
        high, low = pair_hi[:, lanes], pair_lo[:, lanes]
        query_grad.append((nn(high, key) + nn(low, key)) * scale)
        key_grad.append(unstacked(tn(high, query) + tn(low, query), VP) * scale)
    proj_hi, proj_lo = split_two(jnp.concatenate(query_grad + key_grad + [value_grad], 1))
    shard = D // 32
    pick = one_zero(iota((shard, D), 1) == iota((shard, D), 0) + me * shard).astype(BF16)
    weight = in_row[...].astype(BF16)
    back_t = nt(weight, proj_hi) + nt(weight, proj_lo)
    back = nt(proj_hi, weight) + nt(proj_lo, weight)
    table = table_ref[...]
    table_low = table.astype(BF16)
    unit, rstd = norm_stats(table)
    mean = jnp.sum(table, -1, keepdims=True) * (1.0 / D)
    same = iota((VP, VP), 0) == iota((VP, VP), 1)

    def as_row(column):
        return jnp.sum(jnp.where(same, column, 0.0), 0, keepdims=True)

    rstd_row = as_row(rstd)
    unit_t = (nt(pick, table_low) - as_row(mean)) * rstd_row
    unit_mine = (nt(table_low, pick) - mean) * rstd
    norms = jnp.concatenate([norms_ref[...], jnp.zeros((8, D), F32)], 0).astype(BF16)
    inner = back_t * nt(pick, norms)[:, 0:1]

    def three(values):
        top, rest = split_two(values)
        return top, rest, (values - top.astype(F32) - rest.astype(F32)).astype(BF16)

    emb_grad = sum(nt(pick, part) for part in three(table_grad))
    before = emb_grad + rstd_row * inner
    parts = (inner, inner * unit_t, before, before * unit_t, unit_t, unit_t * unit_t, before * before)
    send_stat([jnp.sum(part, 0, keepdims=True) for part in parts])
    scale_0 = jnp.sum(back * unit_mine, 0, keepdims=True)
    shift_0 = jnp.sum(back, 0, keepdims=True)
    line = iota((16, D), 0)
    norm_grad = jnp.zeros((16, D), F32)
    for number, source in ((1, 0), (2, 1), (3, 2), (5, 3), (6, 4), (7, 5)):
        norm_grad = jnp.where(line == number, vectors[source : source + 1], norm_grad)
    normed = (unit * norms_ref[0:1, :] + norms_ref[4:5, :]).astype(BF16)
    mine = nt(pick, normed).astype(BF16)
    in_grad = nn(mine, proj_hi) + nn(mine, proj_lo)
    g_in[...] = in_grad
    own_norm = sum(nt(part, pick) for part in three(norm_grad))[:8]
    line = iota((8, shard), 0)
    own_norm = jnp.where(line == 0, scale_0, jnp.where(line == 4, shift_0, own_norm))
    g_norm[...] = own_norm
    found = total_of(in_grad * in_grad) + total_of(own_norm * own_norm)
    return inner, unit_t, rstd_row, emb_grad, found


PIECES = 21
GRAD_WIDTHS = (768, 768, 768, 768, 384, 1152, 384)
GRAD_UNITS = (
    (0, 0, 384, True),
    (0, 384, 384, True),
    (1, 0, 768, True),
    (2, 0, 768, True),
    (3, 0, 768, True),
    (4, 0, 384, False),
    (5, 0, 384, True),
    (5, 384, 384, True),
    (5, 768, 384, True),
    (6, 0, 384, False),
)
Z_FIRST = {1: 1, 5: 2}
BACKWARD_ORDER = (
    (),
    (),
    (),
    (),
    (),
    (),
    ((0, 0),),
    (),
    ((0, 1),),
    (),
    (),
    ((1, 0),),
    (),
    (),
    ((0, 2), (2, 0),),
    (),
    (),
    ((0, 3),),
    (),
    (),
    ((0, 4), (1, 1), (1, 2),),
    ((0, 5),),
    (),
    (),
    ((1, 3),),
    (),
    (),
    (),
    (),
    ((1, 4),),
    ((2, 1),),
    ((0, 6),),
    ((2, 2), (1, 5), (0, 7),),
    ((0, 8),),
    ((2, 3),),
    ((2, 4), (0, 9),),
    (),
    ((2, 5), (1, 6),),
    ((1, 7),),
    ((3, 0), (3, 1), (3, 2), (3, 3), (1, 8), (4, 0), (4, 1), (4, 2), (4, 3), (1, 9), (3, 5), (2, 6), (3, 4), (4, 4), (2, 7), (5, 0), (2, 8), (2, 9), (3, 6), (4, 5), (4, 6), (3, 7), (4, 7), (6, 0), (3, 8), (3, 9), (4, 8), (4, 9),),
)


class Kept(typing.NamedTuple):
    stream: typing.Any
    norms: typing.Any
    table: typing.Any
    proj_t: typing.Any
    extras: typing.Any
    moved: typing.Any
    grad_head: typing.Any
    touch: typing.Any
    value_two: typing.Any


class Early(typing.NamedTuple):
    slope: typing.Any
    active: typing.Any
    feed_normed_t: typing.Any
    unit_2: typing.Any
    rstd_2: typing.Any
    col_mixed_t: typing.Any
    col_proj: typing.Any
    col_prob: typing.Any
    col_normed_t: typing.Any
    unit_1: typing.Any
    rstd_1: typing.Any


class Late(typing.NamedTuple):
    row_mixed_t: typing.Any
    hot_all: typing.Any
    weight_hi: typing.Any
    prob: typing.Any
    hot_ri: typing.Any
    hot_ir: typing.Any


def pick_items(group, source):
    return [getattr(source, name) for name in group._fields]


def backward_kernel(*refs):
    widths = GRAD_WIDTHS
    count = len(widths)
    contact_head = refs[0]
    far = refs[1 : 1 + count]
    in_row_far = refs[1 + count]
    saved = Saved(*refs[2 + count : 2 + count + len(SAVED)])
    at = 2 + count + len(SAVED)
    outs = refs[at : at + count]
    g_in, g_emb, g_norm, stats = refs[at + count : at + count + 4]
    at += count + 4
    grads = refs[at : at + count]
    kept = Kept(*refs[at + count : at + count + len(Kept._fields)])
    at += count + len(Kept._fields)
    upstream, branch, branch_t, mixed = refs[at : at + 4]
    scratch = refs[at + 4 :]
    units = len(GRAD_UNITS)
    got_0, got_1a, got_1b, got_2a, got_2b, got_3, total, got_4 = (
        scratch[i * units : (i + 1) * units] for i in range(8)
    )
    table, table_out, table_got, square, square_got, stat, stat_got, late_rows = scratch[8 * units : 8 * units + 8]
    table_send, table_recv, send, recv, local = scratch[8 * units + 8 :]
    z, y, k, c = place()
    me = (z * 4 + y * 2 + k) * 2 + c
    across, beside, twin = device(z, y, k, 1 - c), device(z, 1 - y, k, c), device(z, y, 1 - k, c)
    stream = kept.stream
    square[...] = jnp.zeros(square.shape, F32)

    copies = {}

    def load(number, source, target):
        copies[number] = pltpu.make_async_copy(source, target, local.at[number])
        copies[number].start()

    def need(*numbers):
        for number in numbers:
            copies[number].wait()

    def weight(m):
        return len(SAVED) + m

    load(AT.branch, saved.branch, branch)
    load(weight(0), far[0], grads[0])
    barrier = greet_all()

    def copy(m, at, src, dst, target):
        return remote(src, dst, send.at[m, at], recv.at[m, at], target)

    low, high = pl.ds(0, 2), pl.ds(2, 2)
    every = slice(None)

    def where(u, cc, zz, yy):
        matrix, start, n, paired = GRAD_UNITS[u]
        index = spot(paired, cc, zz, yy, k)
        return index if n == widths[matrix] else (*index, every, pl.ds(start, n))

    def block(u, cc, zz, yy):
        return grads[GRAD_UNITS[u][0]].at[where(u, cc, zz, yy)]

    def ordered(u, cc, rest):
        return (*rest, cc) if GRAD_UNITS[u][3] else (cc, *rest)

    def twin_copy(u):
        matrix, start, n, paired = GRAD_UNITS[u]
        index = (1 - k,) if paired else (every, every, every, 1 - k)
        if n != widths[matrix]:
            index = (*index, *(every,) * (5 - len(index)), pl.ds(start, n))
        return copy(u, 0, grads[matrix].at[index], got_0[u], twin)

    def first(u):
        return [
            copy(u, 1, block(u, every, low, 1 - y), got_1a[u], beside),
            copy(u, 2, block(u, 1 - c, high, every), got_1b[u], across),
        ]

    def second(u):
        return [
            copy(u, 3, block(u, 1 - c, low, y), got_2a[u], across),
            copy(u, 4, block(u, c, high, 1 - y), got_2b[u], beside),
        ]

    def along(u):
        return [
            copy(
                u,
                4 + step,
                block(u, c, lax.rem(z + step, 4), y),
                got_3[u].at[step - 1],
                device(lax.rem(z + step, 4), y, k, c),
            )
            for step in (1, 3, 2)
        ]

    def z_first(u):
        return [
            copy(
                u,
                step,
                block(u, every, lax.rem(z + step, 4), every),
                got_1a[u].at[step - 1],
                device(lax.rem(z + step, 4), y, k, c),
            )
            for step in (1, 3, 2)
        ]

    def plane_first(u):
        if Z_FIRST[u] == 1:
            return [copy(u, 4, block(u, every, z, 1 - y), got_2a[u], beside)]
        return [copy(u, 4, block(u, 1 - c, z, every), got_2a[u], across)]

    def plane_second(u):
        if Z_FIRST[u] == 1:
            return [copy(u, 5, block(u, 1 - c, z, y), got_2b[u], across)]
        return [copy(u, 5, block(u, c, z, 1 - y), got_2b[u], beside)]

    def mine(u):
        return k if GRAD_UNITS[u][3] else c

    def pair(u):
        return [copy(u, 8, total[u].at[1 - mine(u)], got_4[u], twin if GRAD_UNITS[u][3] else across)]

    def peer(step):
        return lax.rem(me + step, 32)

    def source(step):
        return lax.rem(me + 32 - step, 32)

    def table_copy(step, back, index):
        target = (peer(step) // 2, lax.rem(peer(step), 2))
        if back:
            return remote(
                table_out.at[index], table_out.at[index], table_send.at[1, step], table_recv.at[1, step], target
            )
        return remote(
            table.at[index], table_got.at[me], table_send.at[0, step], table_recv.at[0, step], target
        )

    def table_start(step):
        @pl.when(peer(step) < PIECES)
        def _():
            table_copy(step, False, peer(step)).start()

    def table_wait_send(step):
        @pl.when(peer(step) < PIECES)
        def _():
            table_copy(step, False, 0).wait_send()

        @pl.when(me < PIECES)
        def _():
            table_copy(step, True, 0).wait_send()

    def table_wait_back(step):
        @pl.when(source(step) < PIECES)
        def _():
            table_copy(step, True, 0).wait_recv()

    def each(action):
        def body(step, carry):
            action(step)
            return carry

        lax.fori_loop(1, 32, body, 0)

    def gather_into(u, cc, zz, yy, *others):
        matrix = GRAD_UNITS[u][0]
        index = where(u, cc, zz, yy)
        if not others:
            grads[matrix][index] = grads[matrix][index] + got_0[u][ordered(u, cc, (zz, yy))]
            return
        value = grads[matrix][index].astype(F32) + got_0[u][ordered(u, cc, (zz, yy))].astype(F32)
        for other in others:
            value = value + other.astype(F32)
        grads[matrix][index] = value.astype(BF16)

    def from_line(u, cc, yy):
        index = (yy, cc) if GRAD_UNITS[u][3] else (cc, yy)
        return [got_1a[u][(step, *index)] for step in range(3)]

    def stage_first(u):
        twin_copy(u).wait_recv()
        if u in Z_FIRST:
            for step in (1, 3, 2):
                for cc in range(2):
                    for yy in range(2):
                        gather_into(u, cc, lax.rem(z + step, 4), yy)
            for item in z_first(u):
                item.start()
            return
        for a in range(2):
            for b in range(2):
                gather_into(u, a, b, 1 - y)
                gather_into(u, 1 - c, 2 + a, b)
        for item in first(u):
            item.start()

    def from_beside(u, cc, a):
        return got_1a[u][ordered(u, cc, (a,))]

    def stage_second(u):
        if u in Z_FIRST:
            for item in z_first(u):
                item.wait_recv()
            for a in range(2):
                cc, yy = (a, 1 - y) if Z_FIRST[u] == 1 else (1 - c, a)
                gather_into(u, cc, z, yy, *from_line(u, cc, yy))
            for item in plane_first(u):
                item.start()
            return
        for item in first(u):
            item.wait_recv()
        for a in range(2):
            gather_into(u, 1 - c, a, y, from_beside(u, 1 - c, a))
            gather_into(u, c, 2 + a, 1 - y, got_1b[u][a, 1 - y])
        for item in second(u):
            item.start()

    def stage_along(u):
        if u in Z_FIRST:
            for item in plane_first(u):
                item.wait_recv()
            cc, yy = (1 - c, y) if Z_FIRST[u] == 1 else (c, 1 - y)
            gather_into(u, cc, z, yy, *from_line(u, cc, yy), got_2a[u][cc if Z_FIRST[u] == 1 else yy])
            for item in plane_second(u):
                item.start()
            return
        for item in second(u):
            item.wait_recv()
        for a in range(2):
            gather_into(u, c, a, y, from_beside(u, c, a), got_2a[u][a])
            gather_into(u, c, 2 + a, y, got_1b[u][a, y], got_2b[u][a])
        for item in along(u):
            item.start()

    def stage_pair(u):
        full = grads[GRAD_UNITS[u][0]][where(u, c, z, y)].astype(F32)
        if u in Z_FIRST:
            for item in plane_second(u):
                item.wait_recv()
            others = [got_0[u][ordered(u, c, (z, y))], *from_line(u, c, y)]
            others += [got_2a[u][c if Z_FIRST[u] == 1 else y], got_2b[u][...]]
        else:
            for item in along(u):
                item.wait_recv()
            others = [got_3[u][step] for step in range(3)]
        for other in others:
            full = full + other.astype(F32)
        total[u][0] = full[:24]
        total[u][1] = full[24:]
        for item in pair(u):
            item.start()

    def stage_end(u):
        matrix, start, n, _ = GRAD_UNITS[u]
        lanes = slice(start, start + n)
        side = mine(u)
        outs[matrix][side, :, lanes] = total[u][side]
        for item in pair(u):
            item.wait_recv()
        outs[matrix][1 - side, :, lanes] = got_4[u][...]
        own, other = total[u][side], got_4[u][...]
        square[...] += jnp.broadcast_to(total_of(own * own + other * other), (8, 128))
        if u in Z_FIRST:
            sent = z_first(u) + plane_first(u) + plane_second(u)
        else:
            sent = first(u) + second(u) + along(u)
        for item in [twin_copy(u)] + sent:
            item.wait_send()

    def table_sum(u):
        @pl.when(me < PIECES)
        def _():
            each(lambda step: table_copy(step, False, 0).wait_recv())
            table_got[me] = table[me]

            def add(at, held):
                return held + table_got[at].astype(F32)

            total_rows = lax.fori_loop(1, 32, add, table_got[0].astype(F32))
            top, rest = split_two(total_rows[:8] + total_rows[8:])
            exact = jnp.concatenate([top.astype(F32), rest.astype(F32)], 0)
            table_out[me] = jnp.where(me >= 18, exact, total_rows).astype(BF16)
            each(lambda step: table_copy(step, True, me).start())

    late_parts = []

    def table_end(u):
        each(table_wait_back)
        need(weight(count))
        late_parts.append(
            table_finish(
                table_out, upstream, kept.table, kept.norms, kept.proj_t, late_parts[0], g_in, g_norm, send_stat
            )
        )
        for at, value in enumerate(late_parts[1][:4]):
            late_rows[at] = jnp.broadcast_to(value, (24, VP))
        square[...] += jnp.broadcast_to(late_parts[1][-1], (8, 128))

    def stat_copy(step):
        target = (peer(step) // 2, lax.rem(peer(step), 2))
        return remote(stat, stat_got.at[me], table_send.at[3, step], table_recv.at[3, step], target)

    def send_stat(rows):
        line = iota((8, VP), 0)
        result = jnp.zeros((8, VP), F32)
        for at, row in enumerate(rows):
            result = jnp.where(line == at, row, result)
        stat[...] = result
        each(lambda step: stat_copy(step).start())
        stat_got[me] = stat[...]

    def table_last():
        each(lambda step: stat_copy(step).wait())
        totals = lax.fori_loop(1, 32, lambda at, held: held + stat_got[at], stat_got[0])
        mean_1, mean_2 = totals[0:1] * (1.0 / D), totals[1:2] * (1.0 / D)
        inner, unit, rstd, emb_grad = (late_rows[at] for at in range(4))
        g_emb[...] = emb_grad + rstd * (inner - mean_1 - unit * mean_2)
        first, second = rstd[0:1] * mean_1, rstd[0:1] * mean_2
        whole = totals[6:7] - 2.0 * (first * totals[2:3] + second * totals[3:4])
        whole = whole + first * first * D + 2.0 * first * second * totals[4:5] + second * second * totals[5:6]
        return total_of(whole)

    stages = (stage_first, stage_second, stage_along, stage_pair, stage_end, table_sum, table_end)
    pending = list(BACKWARD_ORDER)

    def hook():
        for stage, u in pending.pop(0):
            stages[stage](u)

    def done(u):
        if u == 0:
            pl.semaphore_wait(barrier, 31)
        twin_copy(u).start()
        hook()

    names = Kept._fields

    def phase_one(*early_refs):
        e = Early(*early_refs)
        left, right = slice(0, 1536), slice(1536, 3072)
        spare = len(SAVED) + count + 1
        load(AT.slope, saved.slope.at[:, left], e.slope.at[:, left])
        load(AT.active, saved.active.at[:, left], e.active.at[:, left])
        load(spare, saved.slope.at[:, right], e.slope.at[:, right])
        load(spare + 1, saved.active.at[:, right], e.active.at[:, right])
        load(weight(1), far[1], grads[1])
        for name in names:
            load(getattr(AT, name), getattr(saved, name), getattr(kept, name))
        for m in (2, 3):
            load(weight(m), far[m], grads[m])
        for name in Early._fields[2:6]:
            load(getattr(AT, name), getattr(saved, name), getattr(e, name))
        load(weight(4), far[4], grads[4])
        for name in Early._fields[6:8]:
            load(getattr(AT, name), getattr(saved, name), getattr(e, name))
        load(weight(5), far[5], grads[5])
        for name in Early._fields[8:]:
            load(getattr(AT, name), getattr(saved, name), getattr(e, name))
        load(weight(6), far[6], grads[6])
        view = [g.reshape(2, D, n) for g, n in zip(grads, widths)]
        need(AT.branch)
        transpose_into(branch, branch_t)
        hook()

        def grad_tile(m, start, left_t, right, half, at):
            lanes = slice(start + half * widths[m] + at, start + half * widths[m] + at + 384)
            view[m][half, :, at : at + 384] = nn(left_t[...], right[:, lanes]).astype(BF16)

        def grad_half(m, start, left_t, right, half):
            for at in range(0, widths[m], 384):
                grad_tile(m, start, left_t, right, half, at)

        for part in range(2):
            need(weight(part))
            need(*((AT.slope,) if part == 0 else (spare, spare + 1)))

            def down_back(half, at, part=part):
                lanes = slice(part * 1536 + half * 768 + at, part * 1536 + half * 768 + at + 384)
                back = nn(branch[...], view[part][half, :, at : at + 384])
                e.slope[:, lanes] = (back * e.slope[:, lanes].astype(F32)).astype(BF16)

            if part == 0:
                for at in (0, 384):
                    for half in range(2):
                        down_back(half, at)
                    hook()
                    if at == 0:
                        need(AT.active)
                    for half in range(2):
                        grad_tile(part, 0, branch_t, e.active, half, at)
                    done(at // 384)
            else:
                for half in range(2):
                    for at in (0, 384):
                        down_back(half, at)
                    hook()
                grad_half(part, part * 1536, branch_t, e.active, 0)
                hook()
                grad_half(part, part * 1536, branch_t, e.active, 1)
                done(2)
        for part in range(2):
            need(weight(2 + part))
            for half in range(2):
                start = part * 1536 + half * 768
                back = nt(e.slope[:, start : start + 768], view[2 + part][half])
                upstream[...] = back if start == 0 else upstream[...] + back
                hook()
            if part == 0:
                need(AT.feed_normed_t)
            grad_half(2 + part, part * 1536, e.feed_normed_t, e.slope, 0)
            hook()
            grad_half(2 + part, part * 1536, e.feed_normed_t, e.slope, 1)
            done(3 + part)
        need(*(getattr(AT, name) for name in names))
        norms = kept.norms[...]

        def gain(number):
            return norms[number : number + 1, :]

        need(AT.unit_2, AT.rstd_2)
        scale_2, shift_2 = back_rows(e.unit_2, e.rstd_2, gain(2), upstream, stream, branch, False)
        hook()
        need(weight(4), AT.col_mixed_t)
        mixed[...] = (nt(branch[:, :384], view[4][0]) + nt(branch[:, 384:], view[4][1])).astype(BF16)
        hook()
        for half in range(2):
            grad_half(4, 0, e.col_mixed_t, branch, half)
        done(5)
        need(AT.col_proj, AT.col_prob)
        proj = e.active

        def attend(at, carry):
            rows = pl.ds(pl.multiple_of((at // PAIRS) * 128, 128), 128)
            lane = lax.rem(at, PAIRS) * 128

            def lanes(part):
                return pl.ds(pl.multiple_of(part * D + lane, 128), 128)

            query = stacked(e.col_proj[rows, lanes(0)])
            key = e.col_proj[rows, lanes(1)]
            value = e.col_proj[rows, lanes(2)]
            above = stacked(mixed[rows, lanes(0)])
            prob = e.col_prob[at]
            grad = nt(above, value)
            grad = prob * (grad - jnp.sum(prob * grad, -1, keepdims=True))
            small = grad.astype(BF16)
            scale = HD ** (-0.5)
            proj[rows, lanes(0)] = (unstacked(nn(small, key), 128) * scale).astype(BF16)
            proj[rows, lanes(1)] = (tn(small, query) * scale).astype(BF16)
            proj[rows, lanes(2)] = tn(prob.astype(BF16), above).astype(BF16)
            return carry

        for part in range(6):
            lax.fori_loop(4 * part, 4 * part + 4, attend, 0, unroll=4)
            hook()
        need(weight(5))
        for half in range(2):
            back = nt(proj[:, half * 1152 : half * 1152 + 1152], view[5][half])
            upstream[...] = back if half == 0 else upstream[...] + back
            hook()
        need(AT.col_normed_t)
        for third in range(3):
            for half in range(2):
                grad_tile(5, 0, e.col_normed_t, proj, half, third * 384)
            done(6 + third)
        need(AT.unit_1, AT.rstd_1)
        scale_1, shift_1 = back_rows(e.unit_1, e.rstd_1, gain(1), upstream, stream, branch, False)
        hook()
        need(weight(6))
        mixed[...] = (nt(branch[:, :384], view[6][0]) + nt(branch[:, 384:], view[6][1])).astype(BF16)
        line = iota((8, D), 0)
        vectors = jnp.zeros((8, D), F32)
        moved = kept.moved[...]
        rows = (scale_1, scale_2, moved[0:1], shift_1, shift_2, moved[1:2])
        for number, row in enumerate(rows):
            vectors = jnp.where(line == number, row, vectors)
        extras = jnp.concatenate([kept.extras[0:1, :], jnp.zeros((1, D - 128), F32)], 1)
        kept.moved[...] = jnp.where(line == 6, extras, vectors)
        hook()

    pl.run_scoped(phase_one, *(pltpu.VMEM(*item) for item in pick_items(Early, SAVED)))

    def phase_two(*late_refs):
        e = Late(*late_refs[:-3])
        in_row, left_hi, left_lo = late_refs[-3:]
        for name in Late._fields:
            load(getattr(AT, name), getattr(saved, name), getattr(e, name))
        load(weight(count), in_row_far.at[0], in_row)
        view = grads[6].reshape(2, D, widths[6])
        late_parts.append(in_row)
        need(AT.row_mixed_t)
        for half in range(2):
            lanes = slice(half * 384, half * 384 + 384)
            view[half] = nn(e.row_mixed_t[...], branch[:, lanes]).astype(BF16)
        done(9)
        need(AT.hot_all, AT.weight_hi, AT.prob, AT.hot_ri, AT.hot_ir)
        shape = (HERE, HERE)
        back = (
            ((iota(shape, 1) >> 4) == (iota(shape, 0) & 31))
            & ((iota(shape, 1) & 15) == (iota(shape, 0) >> 5))
        )
        mixed[...] = nn(one_zero(back).astype(BF16), mixed[...]).astype(BF16)
        value_rows = []
        for hp in range(PAIRS):
            lanes = slice(hp * 128, hp * 128 + 128)
            part = mixed[:, lanes]
            upstream[:, lanes] = nt(part, kept.value_two[hp])
            value_rows.append(unstacked(tn(e.weight_hi[:, lanes], part), 64))
        hook()
        split_heads_to(upstream, left_hi, left_lo)
        hook()
        hot_all = e.hot_all[...]
        grad = nn(left_hi[...], hot_all) + nn(left_lo[...], hot_all)
        extra = jnp.concatenate(
            [kept.touch[...] * (contact_head[h] * COLS) for h in range(HEADS)], 0
        )
        grad = grad + extra
        prob = e.prob[...]
        grad = prob * (grad - jnp.sum(prob * grad, -1, keepdims=True))
        low_grad = grad.astype(BF16)
        hook()
        merge_heads(low_grad, e.hot_all, branch, None)
        hook()
        table_pair = nn(e.hot_ri[...], branch[...])
        stream_hi, stream_lo = split_two(stream[...])
        hot_ir = e.hot_ir[...]
        table_grad = kept.grad_head[...] + nn(hot_ir, stream_hi) + nn(hot_ir, stream_lo)
        value_grad = jnp.concatenate(value_rows, 1)
        last = jnp.where(iota((8, D), 0) == 7, table_grad[32:33], kept.moved[...])
        top, rest = split_two(last)
        groups = [table_pair[4:20], table_pair[20:36], value_grad[4:20], value_grad[20:36]]
        groups += [table_grad[0:16], table_grad[16:32]]
        groups += [jnp.concatenate([top.astype(F32), rest.astype(F32)], 0)]
        for number, group in enumerate(groups):
            for third in range(3):
                table[3 * number + third] = group[:, third * 256 : third * 256 + 256].astype(BF16)
        each(table_start)
        hook()
        hook()

    pl.run_scoped(
        phase_two,
        *(pltpu.VMEM(*item) for item in pick_items(Late, SAVED)),
        pltpu.VMEM((24, 3 * D), F32),
        pltpu.VMEM((HEADS * WIDE, ROWS * VP), BF16),
        pltpu.VMEM((HEADS * WIDE, ROWS * VP), BF16),
    )
    assert not pending

    def square_copy(step):
        other = lax.rem(me + step, 32)
        return remote(
            square, square_got.at[me], table_send.at[2, step], table_recv.at[2, step], (other // 2, lax.rem(other, 2))
        )

    each(lambda step: square_copy(step).start())
    square_got[me] = square[...]
    each(lambda step: table_wait_send(step))
    for u in range(units):
        for item in pair(u):
            item.wait_send()
    emb_square = table_last()
    each(lambda step: square_copy(step).wait())
    total_square = lax.fori_loop(1, 32, lambda at, held: held + square_got[at], square_got[0])[0:1]
    vector = table_out[18].astype(F32)
    vector = vector[6:7, :128] + vector[14:15, :128]
    counted = kept.extras[1:2, :]
    column = iota((1, 128), 1)
    contact = jnp.where(column <= HEADS, vector, 0.0)
    total_square = total_square + total_of(contact * contact) + emb_square
    grad_norm = jnp.sqrt(total_square)
    factor = jnp.minimum(1.0, MAX_NORM / grad_norm)
    losses = (
        (0, vector[:, HEADS + 1 : HEADS + 2]),
        (1, counted[:, 0:1]),
        (2, vector[:, HEADS + 2 : HEADS + 3]),
        (3, counted[:, 1:2]),
    )
    loss_row = jnp.zeros((1, 128), F32)
    for at, value in losses:
        loss_row = jnp.where(column == at, value, loss_row)
    number = iota((8, 128), 0)
    result = jnp.zeros((8, 128), F32)
    for at, row in enumerate((contact, counted, factor, grad_norm, loss_row)):
        result = jnp.where(number == at, row, result)
    stats[...] = result


def backward_call(contact_head, weights, in_row, saved):
    widths = GRAD_WIDTHS
    count = len(widths)
    inside = pl.BlockSpec(memory_space=pltpu.VMEM)
    anywhere = pl.BlockSpec(memory_space=pl.ANY)

    units = len(GRAD_UNITS)

    def shapes(lead, dtype, other=None):
        leads = [other if other and u in Z_FIRST else lead for u in range(units)]
        return [pltpu.VMEM((*at, n), dtype) for at, (_, _, n, _) in zip(leads, GRAD_UNITS)]

    outs = pl.pallas_call(
        backward_kernel,
        out_shape=[jax.ShapeDtypeStruct((2, 24, n), F32) for n in widths]
        + [
            jax.ShapeDtypeStruct((24, 3 * D), F32),
            jax.ShapeDtypeStruct((24, VP), F32),
            jax.ShapeDtypeStruct((8, 24), F32),
            jax.ShapeDtypeStruct((8, 128), F32),
        ],
        in_specs=[pl.BlockSpec(memory_space=pltpu.SMEM)] + [anywhere] * (1 + count + len(SAVED)),
        out_specs=[inside] * (4 + count),
        scratch_shapes=[pltpu.VMEM((2, NZ, NY, 2, 48, n), BF16) for n in widths]
        + [pltpu.VMEM(*item) for item in pick_items(Kept, SAVED)]
        + [
            pltpu.VMEM((HERE, D), F32),
            pltpu.VMEM((HERE, D), BF16),
            pltpu.VMEM((D, HERE), BF16),
            pltpu.VMEM((HERE, D), BF16),
        ]
        + [
            pltpu.VMEM((NZ, NY, 2, 48, n) if paired else (2, NZ, NY, 48, n), BF16)
            for _, _, n, paired in GRAD_UNITS
        ]
        + shapes((2, 2, 48), BF16, (3, 2, 2, 48))
        + shapes((2, 2, 48), BF16, (16,))
        + shapes((2, 48), BF16, (2, 48))
        + shapes((2, 48), BF16, (48,))
        + shapes((3, 48), BF16, (16,))
        + shapes((2, 24), F32)
        + shapes((24,), F32)
        + [
            pltpu.VMEM((PIECES, 16, 256), BF16),
            pltpu.VMEM((PIECES, 16, 256), BF16),
            pltpu.VMEM((32, 16, 256), BF16),
            pltpu.VMEM((8, 128), F32),
            pltpu.VMEM((32, 8, 128), F32),
            pltpu.VMEM((8, VP), F32),
            pltpu.VMEM((32, 8, VP), F32),
            pltpu.VMEM((4, 24, VP), F32),
            pltpu.SemaphoreType.DMA((4, 32)),
            pltpu.SemaphoreType.DMA((4, 32)),
            pltpu.SemaphoreType.DMA((units, 9)),
            pltpu.SemaphoreType.DMA((units, 9)),
            pltpu.SemaphoreType.DMA((len(SAVED) + count + 3,)),
        ],
        compiler_params=pltpu.CompilerParams(
            collective_id=1, has_side_effects=True, vmem_limit_bytes=63 * 2**20
        ),
    )(contact_head, *weights, in_row, *saved)
    return outs[:count], outs[count:]


UPDATE_RATES = (LEARN_RATE,) * 4 + (VECTOR_RATE,) * 3


def update_kernel(*refs):
    given, far, held, results = refs[:32], refs[32:60], refs[60:92], refs[92:120]
    sems, out_sems = refs[120:122]
    outs, copies = results[:21], results[21:26]
    loss_ref, norm_ref = results[26:]

    def leave(*numbers):
        for n in numbers:
            pltpu.make_async_copy(results[n], far[n], out_sems.at[n]).start()

    moves = [pltpu.make_async_copy(a, b, sems.at[n]) for n, (a, b) in enumerate(zip(given, held))]
    groups = (
        (10, 7, 5, 11, 12, 13),
        (4, 6, 14, 15, 16),
        (2, 3, 17, 18, 19),
        (0, 1, 20, 21, 22),
        (8, 9, *range(23, 32)),
    )
    for group in groups:
        for n in group:
            moves[n].start()

    def arrive(number):
        for n in groups[number]:
            moves[n].wait()

    reduced, g_in, g_emb, g_norm, stats = held[:7], held[7], held[8], held[9], held[10]
    states = [held[11 + 3 * n : 14 + 3 * n] for n in range(7)]
    outs = [outs[3 * n : 3 * n + 3] for n in range(7)]
    order = feature_order()
    arrive(0)
    factor = stats[2:3, 0:1]
    loss_ref[...] = stats[4:5, 0:4]
    norm_ref[...] = stats[3:4, 0:1]

    def natural(values):
        top, rest = split_two(values)
        last = (values - top.astype(F32) - rest.astype(F32)).astype(BF16)
        return nt(top, order) + nt(rest, order) + nt(last, order)

    def update(number, where, grad):
        master, first, second = (ref[where] for ref in states[number])
        new, first, second = adam_update(master, first, second, grad * factor, UPDATE_RATES[number])
        for ref, value in zip(outs[number], (new, first, second)):
            ref[where] = value
        if number < 5:
            copies[number][where] = new.astype(BF16)

    every = slice(None)
    g_out_col, g_in_col, g_out_row = reduced[4:]
    for half in range(2):
        lanes = slice(half * 1152, half * 1152 + 1152)
        update(0, (0, every, lanes), g_in[:, lanes])
        update(0, (1, every, lanes), g_in_col[half])
    leave(0, 1, 2, 21, 26, 27)
    arrive(1)
    for half in range(2):
        lanes = slice(half * 384, half * 384 + 384)
        update(1, (0, every, lanes), natural(g_out_row[half]))
        update(1, (1, every, lanes), natural(g_out_col[half]))
    leave(3, 4, 5, 22)
    for number, first in ((2, 2), (3, 0)):
        arrive(number)
        for half in range(2):
            for part in range(2):
                start = part * 1536 + half * 768
                lanes = slice(start, start + 768)
                update(number, (every, lanes), reduced[first + part][half])
        leave(*((6, 7, 8, 23) if number == 2 else (9, 10, 11, 24)))
    arrive(4)
    update(4, (every, every), g_emb[:, :VOCAB])
    update(5, (every, every), g_norm[...])
    update(6, (every, every), stats[0:1, : HEADS + 1])
    leave(12, 13, 14, 25, 15, 16, 17, 18, 19, 20)
    for n in range(28):
        pltpu.make_async_copy(results[n], far[n], out_sems.at[n]).wait()


def update_call(reduced, g_in, g_emb, g_norm, stats, states):
    anywhere = pl.BlockSpec(memory_space=pl.ANY)
    flat = [item for state in states for item in state]
    shapes = [jax.ShapeDtypeStruct(item.shape, F32) for item in flat]
    shapes += [jax.ShapeDtypeStruct(states[n][0].shape, BF16) for n in range(5)]
    shapes += [jax.ShapeDtypeStruct((1, 4), F32), jax.ShapeDtypeStruct((1, 1), F32)]
    given = (*reduced, g_in, g_emb, g_norm, stats, *flat)
    return pl.pallas_call(
        update_kernel,
        out_shape=shapes,
        in_specs=[anywhere] * len(given),
        out_specs=[anywhere] * len(shapes),
        scratch_shapes=[pltpu.VMEM(item.shape, F32) for item in given]
        + [pltpu.VMEM(item.shape, item.dtype) for item in shapes]
        + [
            pltpu.SemaphoreType.DMA((len(given),)),
            pltpu.SemaphoreType.DMA((len(shapes),)),
            pltpu.VMEM((44, 512, 512), F32),
        ],
        compiler_params=pltpu.CompilerParams(vmem_limit_bytes=62 * 2**20),
    )(*given)


def adam_update(master, first, second, grad_part, rate):
    first = BETA_ONE * first + (1.0 - BETA_ONE) * grad_part
    second = BETA_TWO * second + (1.0 - BETA_TWO) * grad_part * grad_part
    scaled = first * (1.0 / (1.0 - BETA_ONE**STEP))
    moved = scaled / (jnp.sqrt(second * (1.0 / (1.0 - BETA_TWO**STEP))) + ADAM_EPS)
    return (master - rate * (moved + WEIGHT_DECAY * master), first, second)


def shards(
    tokens,
    targets,
    masked,
    contact_pairs,
    labels,
    attention_in_master,
    attention_in_first,
    attention_in_second,
    attention_out_master,
    attention_out_first,
    attention_out_second,
    feed_up_master,
    feed_up_first,
    feed_up_second,
    feed_down_master,
    feed_down_first,
    feed_down_second,
    embedding_master,
    embedding_first,
    embedding_second,
    norm_params_master,
    norm_params_first,
    norm_params_second,
    contact_head_master,
    contact_head_first,
    contact_head_second,
):
    both = ("seq", "col")
    micro, rows_here, cols_here = tokens.shape
    ncol = lax.axis_size("col")
    ndev = lax.axis_size("seq") * ncol
    cols = cols_here * ncol
    me = lax.axis_index("seq") * ncol + lax.axis_index("col")
    per = ndev // micro
    cw = cols // per
    mine = me // per
    base = (me % per) * cw
    shard = D // ndev

    tiled = lax.axis_size("seq") == 16 and ncol == 2
    if tiled:
        raw = (
            tokens,
            targets,
            masked,
            contact_pairs.transpose(0, 2, 1),
            labels,
            embedding_master.T,
            norm_params_master,
            attention_in_master,
            attention_out_master,
            feed_up_master,
            feed_down_master.T,
        )
        weights, saved = forward_call(raw, contact_head_master)
        reduced, (g_in, g_emb, g_norm, stats) = backward_call(
            contact_head_master, [weights[n] for n in (5, 6, 3, 4, 2, 1, 0)], attention_in_master, saved
        )
        states = (
            (attention_in_master, attention_in_first, attention_in_second),
            (attention_out_master, attention_out_first, attention_out_second),
            (feed_up_master, feed_up_first, feed_up_second),
            (feed_down_master.T, feed_down_first.T, feed_down_second.T),
            (embedding_master.T, embedding_first.T, embedding_second.T),
            (norm_params_master, norm_params_first, norm_params_second),
            (contact_head_master[None], contact_head_first[None], contact_head_second[None]),
        )
        outs = update_call(reduced, g_in, g_emb, g_norm, stats, states)
        return (
            *outs[:9],
            *(item.T for item in outs[9:15]),
            *outs[15:18],
            *(item[0] for item in outs[18:21]),
            *outs[21:24],
            *(item.T for item in outs[24:26]),
            outs[26][0],
            outs[27][0, 0],
        )
    inputs = jnp.where(masked > 0, MASK_ID, tokens)
    masters = [
        jnp.concatenate(
            [
                jnp.pad(embedding_master.T, ((0, 0), (0, 128 - VOCAB))),
                jnp.pad(norm_params_master.T, ((0, 0), (0, 120))),
            ],
            1,
        ),
        attention_in_master[0],
        attention_out_master[0],
        attention_in_master[1],
        attention_out_master[1],
        feed_up_master,
        feed_down_master.T,
    ]
    whole = jnp.stack([inputs, targets])
    whole = lax.all_gather(lax.all_gather(whole, "col", axis=3, tiled=True), "seq", axis=2, tiled=True)
    pairs_all = lax.all_gather(
        jnp.concatenate([contact_pairs, labels[:, :, None]], -1), both, axis=1, tiled=True
    )
    gathered = []
    for master in masters:
        full = lax.all_gather(master.astype(BF16), both, axis=0, tiled=True)
        gathered.append(full.reshape(D, 2, -1).transpose(1, 0, 2))
    counts = (
        jnp.sum(whole[0] == MASK_ID).astype(F32),
        jnp.sum(pairs_all[..., 2] >= 0).astype(F32),
    )
    ids_all = lax.dynamic_index_in_dim(whole[0], mine, 0, False)
    ids_local = lax.dynamic_slice_in_dim(ids_all, base, cw, 1)
    targets_local = lax.dynamic_slice_in_dim(
        lax.dynamic_index_in_dim(whole[1], mine, 0, False), base, cw, 1
    )
    pairs = lax.dynamic_index_in_dim(pairs_all, mine, 0, False)

    table = gathered[0][0][:, :VP].T
    norms = gathered[0][1][:, :8].T.astype(F32)
    in_row, out_row, in_col, out_col, up_w, down_t = (
        jnp.concatenate([g[0], g[1]], 1) for g in gathered[1:]
    )
    big = (in_row, in_col, out_row, out_col, up_w, down_t)

    grads, tables, contact_total, mlm_total, bce_total, kept = step(
        big,
        table,
        norms,
        contact_head_master,
        ids_all,
        ids_local.reshape(-1),
        ids_local.T.reshape(-1),
        targets_local.T.reshape(-1),
        pairs[:, 0] - base,
        pairs[:, 1],
        pairs[:, 2],
        counts,
        cw,
    )
    table_pair, value_grad, table_grad, vectors = tables
    extras = jnp.zeros((2, D), F32).at[0, : HEADS + 3].set(
        jnp.concatenate([contact_total, mlm_total[None], bce_total[None]])
    )
    sums = jnp.concatenate([table_pair[:40], value_grad[:40], table_grad[:40], vectors, extras])
    flat_grad = jnp.concatenate([g.astype(BF16) for g in grads], 1)
    reduced = lax.psum_scatter(flat_grad, both, scatter_dimension=0, tiled=True).astype(F32)
    g_in_col, g_out_row, g_out_col, g_up, g_down = jnp.split(
        reduced, [3 * D, 4 * D, 5 * D, 5 * D + FF], 1
    )
    sums = lax.psum(sums, both)
    unit_t, rstd_t, normed_t, query_t, key_t = kept
    rows_all = ids_all.shape[0]
    spare = ((0, VP - 40), (0, 0))
    table_pair, value_grad, table_grad = (
        jnp.pad(sums[a : a + 40], spare) for a in (0, 40, 80)
    )
    vectors = sums[120:126]
    contact_grad, mlm_total, bce_total = (
        sums[126, : HEADS + 1], sums[126, HEADS + 1], sums[126, HEADS + 2]
    )
    row_scale = (HD * rows_all) ** (-0.5)
    query_grad = []
    key_grad = []
    for h in range(HEADS):
        pair = heads_of(table_pair, h)
        query_grad.append(jnp.dot(pair, heads_of(key_t, h).astype(F32), precision=PRECISE))
        key_grad.append(jnp.dot(pair.T, heads_of(query_t, h).astype(F32), precision=PRECISE))
    proj_grad = jnp.concatenate(
        [
            jnp.concatenate(query_grad, 1) * row_scale,
            jnp.concatenate(key_grad, 1) * row_scale,
            value_grad,
        ],
        1,
    )
    proj_hi, proj_lo = split_two(proj_grad)
    normed_grad = nt(proj_hi, in_row) + nt(proj_lo, in_row)
    back_t, scale_0, shift_0 = norm_back(unit_t, rstd_t, norms[0], normed_grad)
    table_grad = table_grad + back_t
    low = me * shard
    normed_mine = lax.dynamic_slice_in_dim(normed_t, low, shard, 1)
    grad_in_row = tn(normed_mine, proj_hi) + tn(normed_mine, proj_lo)
    norm_grad = jnp.concatenate([scale_0[None], vectors[:3], shift_0[None], vectors[3:]])
    table_mine = lax.dynamic_slice_in_dim(table_grad[:VOCAB], low, shard, 1)
    norm_mine = lax.dynamic_slice_in_dim(norm_grad, low, shard, 1)
    reduced_all = (g_in_col, g_out_row, g_out_col, g_up, g_down)

    local_square = (
        sum(jnp.sum(g * g) for g in reduced_all)
        + jnp.sum(grad_in_row * grad_in_row)
        + jnp.sum(table_mine * table_mine)
        + jnp.sum(norm_mine * norm_mine)
    )
    square = lax.psum(local_square, both) + jnp.sum(contact_grad * contact_grad)
    grad_norm = jnp.sqrt(square)
    factor = jnp.minimum(1.0, MAX_NORM / grad_norm)
    in_new, in_moment, in_square = adam_update(
        attention_in_master, attention_in_first, attention_in_second, jnp.stack([grad_in_row, g_in_col]) * factor, LEARN_RATE
    )
    out_new, out_moment, out_square = adam_update(
        attention_out_master, attention_out_first, attention_out_second, jnp.stack([g_out_row, g_out_col]) * factor, LEARN_RATE
    )
    up_new, up_moment, up_square = adam_update(
        feed_up_master, feed_up_first, feed_up_second, g_up * factor, LEARN_RATE
    )
    down_new, down_moment, down_square = adam_update(
        feed_down_master, feed_down_first, feed_down_second, g_down.T * factor, LEARN_RATE
    )
    table_new, table_moment, table_square = adam_update(
        embedding_master, embedding_first, embedding_second, table_mine * factor, VECTOR_RATE
    )
    norm_new, norm_moment, norm_square = adam_update(
        norm_params_master, norm_params_first, norm_params_second, norm_mine * factor, VECTOR_RATE
    )
    head_new, head_moment, head_square = adam_update(
        contact_head_master, contact_head_first, contact_head_second, contact_grad * factor, VECTOR_RATE
    )
    loss_parts = jnp.stack([mlm_total, counts[0], bce_total, counts[1]])
    return (
        in_new, in_moment, in_square,
        out_new, out_moment, out_square,
        up_new, up_moment, up_square,
        down_new, down_moment, down_square,
        table_new, table_moment, table_square,
        norm_new, norm_moment, norm_square,
        head_new, head_moment, head_square,
        in_new.astype(BF16), out_new.astype(BF16), up_new.astype(BF16), down_new.astype(BF16), table_new.astype(BF16),
        loss_parts, grad_norm,
    )


def solution(mesh):
    both = ("seq", "col")
    cells = P(None, "seq", "col")
    stack = P(None, both, None)
    row_split = P(both, None)
    col_split = P(None, both)
    weights = [stack] * 6 + [row_split] * 3 + [col_split] * 9 + [P()] * 3
    return jax.shard_map(
        shards,
        mesh=mesh,
        in_specs=(cells, cells, cells, stack, col_split, *weights),
        out_specs=(*weights, stack, stack, row_split, col_split, col_split, P(), P()),
        check_vma=False,
    )
```

```python
import typing

import jax
import jax.numpy as jnp
from jax import lax
from jax.experimental import pallas as pl
from jax.experimental.pallas import tpu as pltpu
from jax.sharding import PartitionSpec as P

D = 768
HEADS = 12
HD = 64
FF = 3072
VOCAB = 33
VP = 64
STEP = 10

NORM_EPS = 1e-05
MASK_ID = 32
MAX_NORM = 0.001
LEARN_RATE = 0.05
VECTOR_RATE = 0.5
BETA_ONE = 0.9
BETA_TWO = 0.95
ADAM_EPS = 1e-08
WEIGHT_DECAY = 0.01
PRECISE = lax.Precision.HIGHEST
F32 = jnp.float32
BF16 = jnp.bfloat16


def nn(left, right):
    return lax.dot_general(left, right, (((1,), (0,)), ((), ())), preferred_element_type=F32)


def tn(left, right):
    return lax.dot_general(left, right, (((0,), (0,)), ((), ())), preferred_element_type=F32)


def nt(left, right):
    return lax.dot_general(left, right, (((1,), (1,)), ((), ())), preferred_element_type=F32)


def split_two(values):
    high = values.astype(BF16)
    return high, (values - high.astype(F32)).astype(BF16)


def norm_stats(values):
    centre = values - jnp.mean(values, -1, keepdims=True)
    rstd = lax.rsqrt(jnp.mean(centre * centre, -1, keepdims=True) + NORM_EPS)
    return centre * rstd, rstd


def norm_back(unit, rstd, scale_vec, upstream):
    inner = upstream * scale_vec
    grad = rstd * (
        inner - jnp.mean(inner, -1, keepdims=True) - unit * jnp.mean(inner * unit, -1, keepdims=True)
    )
    return grad, jnp.sum(upstream * unit, 0), jnp.sum(upstream, 0)


GELU_K = 0.7978845608028654
GELU_C = 0.044715


def gelu_parts(up):
    square = up * up
    bent = jnp.tanh(GELU_K * up * (1.0 + GELU_C * square))
    half = 0.5 * (1.0 + bent)
    slope = half + 0.5 * up * (1.0 - bent * bent) * GELU_K * (1.0 + 3.0 * GELU_C * square)
    return up * half, slope


def heads_of(block, head):
    return block[:, head * HD : (head + 1) * HD]


def step(big, table, norms, contact_head, ids_all, ids_ri, ids_ir, targets_ir, pair_first, pair_second, labels, counts, cw):
    in_row, in_col, out_row, out_col, up_w, down_t = big
    rows, cols = ids_all.shape
    here = rows * cw
    row_scale = (HD * rows) ** (-0.5)
    vocab = jnp.arange(VP)[:, None]
    hot_all = (ids_all[:, None, :] == vocab[None]).astype(BF16).reshape(rows * VP, cols)
    hot_ri = (ids_ri[None, :] == vocab).astype(BF16)
    hot_ir = (ids_ir[None, :] == vocab).astype(BF16)
    spot = jnp.arange(here)
    perm = (
        ((spot // rows)[:, None] == (spot % cw)[None, :])
        & ((spot % rows)[:, None] == (spot // cw)[None, :])
    ).astype(BF16)

    def to_heads(block):
        return block.reshape(rows, cw, HEADS, VP).transpose(2, 1, 0, 3).reshape(HEADS * cw, rows * VP)

    def to_tokens(block):
        return block.reshape(HEADS, cw, rows, VP).transpose(2, 1, 0, 3).reshape(here, HEADS * VP)

    def per_head(block, other, how):
        return jnp.concatenate(
            [how(heads_of(block, h), heads_of(other, h)) for h in range(HEADS)], -1
        )

    table_f = table.astype(F32)
    unit_t, rstd_t = norm_stats(table_f)
    normed_t = (unit_t * norms[0] + norms[4]).astype(BF16)
    proj_t = nn(normed_t, in_row).astype(BF16)
    query_t, key_t, value_t = proj_t[:, :D], proj_t[:, D : 2 * D], proj_t[:, 2 * D :]

    pair_t = per_head(query_t, key_t, nt)
    pair_hi, pair_lo = split_two(pair_t)
    left_hi = to_heads(tn(hot_ri, pair_hi).astype(BF16))
    left_lo = to_heads(tn(hot_ri, pair_lo).astype(BF16))
    score = (nn(left_hi, hot_all) + nn(left_lo, hot_all)) * row_scale
    prob = jax.nn.softmax(score, axis=-1)
    prob_low = prob.astype(BF16)
    weight_t = to_tokens(nt(prob_low, hot_all))
    weight_hi, weight_lo = split_two(weight_t)
    row_mixed_ri = (
        per_head(weight_hi, value_t, nn) + per_head(weight_lo, value_t, nn)
    ).astype(BF16)
    row_mixed = nn(perm, row_mixed_ri).astype(BF16)
    embedded = tn(hot_ir, table)
    after_row = embedded + nn(row_mixed, out_row)

    prob_cube = prob_low.astype(F32).reshape(HEADS, cw, cols)
    head_sum = jnp.sum(prob_cube * contact_head[:HEADS, None, None], 0)
    first_hot = (pair_first[None, :] == jnp.arange(cw)[:, None]).astype(F32)
    second_hot = (pair_second[None, :] == jnp.arange(cols)[:, None]).astype(BF16)
    sum_hi, sum_lo = split_two(head_sum)
    sum_last = (head_sum - sum_hi.astype(F32) - sum_lo.astype(F32)).astype(BF16)
    picked = nn(sum_hi, second_hot) + nn(sum_lo, second_hot) + nn(sum_last, second_hot)
    contact_logit = jnp.sum(picked * first_hot, 0) * cols + contact_head[HEADS]
    owned = jnp.sum(first_hot, 0) > 0
    valid = (labels >= 0) & owned
    positive = (labels == 1).astype(F32)
    bce_sum = jnp.sum(
        jnp.where(valid, jax.nn.softplus(contact_logit) - positive * contact_logit, 0.0)
    )
    coef = jnp.where(valid, jax.nn.sigmoid(contact_logit) - positive, 0.0) / counts[1]
    coef_hi, coef_lo = split_two(coef)
    first_low = first_hot.astype(BF16)
    touch = nt(first_low * coef_hi[None], second_hot) + nt(first_low * coef_lo[None], second_hot)
    grad_contact = jnp.concatenate(
        [jnp.sum(prob_cube * touch[None], (1, 2)) * cols, jnp.sum(coef)[None]]
    )

    unit_1, rstd_1 = norm_stats(after_row)
    col_normed = (unit_1 * norms[1] + norms[5]).astype(BF16)
    col_proj = nn(col_normed, in_col).astype(BF16)
    group = 128 if here % 128 == 0 and 128 % rows == 0 else here
    groups = here // group
    lane = jnp.arange(group)
    same = (lane[:, None] // rows) == (lane[None, :] // rows)

    def cut(block):
        return block.reshape(groups, group, HEADS, HD)

    col_query, col_key, col_value = (cut(col_proj[:, k * D : (k + 1) * D]) for k in range(3))
    col_score = jnp.einsum("gqhe,gkhe->ghqk", col_query, col_key, preferred_element_type=F32) * HD ** (-0.5)
    col_prob = jax.nn.softmax(jnp.where(same, col_score, -1e30), axis=-1)
    col_prob_low = col_prob.astype(BF16)
    col_mixed = (
        jnp.einsum("ghqk,gkhe->gqhe", col_prob_low, col_value, preferred_element_type=F32)
        .astype(BF16)
        .reshape(here, D)
    )
    after_col = after_row + nn(col_mixed, out_col)

    unit_2, rstd_2 = norm_stats(after_col)
    feed_normed = (unit_2 * norms[2] + norms[6]).astype(BF16)
    hidden_up = nn(feed_normed, up_w)
    active, slope = gelu_parts(hidden_up)
    active = active.astype(BF16)
    after_feed = after_col + nt(active, down_t)
    unit_3, rstd_3 = norm_stats(after_feed)
    head_normed = (unit_3 * norms[3] + norms[7]).astype(BF16)
    logits = nt(table, head_normed) * D ** (-0.5)
    logits = jnp.where(vocab < VOCAB, logits, -1e30)
    top = jnp.max(logits, 0, keepdims=True)
    shifted = logits - top
    log_probs = shifted - jnp.log(jnp.sum(jnp.exp(shifted), 0, keepdims=True))
    target_hot = (targets_ir[None, :] == vocab).astype(F32)
    keep = ids_ir[None, :] == MASK_ID
    mlm_sum = -jnp.sum(jnp.where(keep & (target_hot > 0), log_probs, 0.0))
    logit_grad = jnp.where(keep, jnp.exp(log_probs) - target_hot, 0.0) / counts[0]
    logit_low = (logit_grad * D ** (-0.5)).astype(BF16)

    grad_head = nn(logit_low, head_normed)
    stream, scale_3, shift_3 = norm_back(unit_3, rstd_3, norms[3], tn(logit_low, table))
    branch = stream.astype(BF16)
    grad_down = tn(branch, active)
    up_low = (nn(branch, down_t) * slope).astype(BF16)
    grad_up = tn(feed_normed, up_low)
    inner, scale_2, shift_2 = norm_back(unit_2, rstd_2, norms[2], nt(up_low, up_w))
    stream = stream + inner
    branch = stream.astype(BF16)
    grad_out_col = tn(col_mixed, branch)
    mixed_low = nt(branch, out_col).astype(BF16)
    mixed_cut = cut(mixed_low)
    prob_grad = jnp.einsum("gqhe,gkhe->ghqk", mixed_cut, col_value, preferred_element_type=F32)
    score_grad = col_prob * (prob_grad - jnp.sum(col_prob * prob_grad, -1, keepdims=True))
    score_low = score_grad.astype(BF16)
    grad_q = jnp.einsum("ghqk,gkhe->gqhe", score_low, col_key, preferred_element_type=F32)
    grad_k = jnp.einsum("ghqk,gqhe->gkhe", score_low, col_query, preferred_element_type=F32)
    grad_v = jnp.einsum("ghqk,gqhe->gkhe", col_prob_low, mixed_cut, preferred_element_type=F32)
    proj_low = jnp.concatenate(
        [
            (grad_q * HD ** (-0.5)).reshape(here, D),
            (grad_k * HD ** (-0.5)).reshape(here, D),
            grad_v.reshape(here, D),
        ],
        -1,
    ).astype(BF16)
    grad_in_col = tn(col_normed, proj_low)
    inner, scale_1, shift_1 = norm_back(unit_1, rstd_1, norms[1], nt(proj_low, in_col))
    stream = stream + inner
    branch = stream.astype(BF16)
    grad_out_row = tn(row_mixed, branch)
    mixed_low = nt(branch, out_row).astype(BF16)
    mixed_ri = tn(perm, mixed_low).astype(BF16)
    drive_hi, drive_lo = split_two(per_head(mixed_ri, value_t, nt))
    prob_grad = nn(to_heads(drive_hi), hot_all) + nn(to_heads(drive_lo), hot_all)
    prob_grad = prob_grad + (
        touch[None] * (contact_head[:HEADS, None, None] * cols)
    ).reshape(HEADS * cw, cols)
    score_grad = prob * (prob_grad - jnp.sum(prob * prob_grad, -1, keepdims=True))
    score_low = score_grad.astype(BF16)
    spread = to_tokens(nt(score_low, hot_all)).astype(BF16)
    table_pair = nn(hot_ri, spread)
    value_grad = per_head(weight_hi, mixed_ri, tn)
    stream_hi, stream_lo = split_two(stream)
    lookup_grad = nn(hot_ir, stream_hi) + nn(hot_ir, stream_lo)
    vectors = jnp.stack([scale_1, scale_2, scale_3, shift_1, shift_2, shift_3])
    return (
        (grad_in_col, grad_out_row, grad_out_col, grad_up, grad_down),
        (table_pair, value_grad, grad_head + lookup_grad, vectors),
        grad_contact,
        mlm_sum,
        bce_sum,
        (unit_t, rstd_t, normed_t, query_t, key_t),
    )


MESH = pl.DeviceIdType.MESH
NZ, NY = 4, 2


def place():
    s, c = lax.axis_index("seq"), lax.axis_index("col")
    z, y, k = s // 4, lax.rem(s // 2, 2), lax.rem(s, 2)
    return z, y, k, c


def device(z, y, k, c):
    return (z * 4 + y * 2 + k, c)


def greet_all():
    z, y, k, c = place()
    me = (z * 4 + y * 2 + k) * 2 + c
    barrier = pltpu.get_barrier_semaphore()

    def signal(step, carry):
        other = lax.rem(me + step, 32)
        pl.semaphore_signal(
            barrier, inc=1, device_id=(other // 2, lax.rem(other, 2)), device_id_type=MESH
        )
        return carry

    lax.fori_loop(1, 32, signal, 0)
    return barrier


def remote(src, dst, send, recv, target):
    return pltpu.make_async_remote_copy(
        src_ref=src, dst_ref=dst, send_sem=send, recv_sem=recv, device_id=target, device_id_type=MESH
    )


ROWS, COLS, WIDE, HERE = 16, 512, 32, 512
PAIRS = 6
SLOTS = 1024
UP_TILE = 384


def iota(shape, dim):
    return lax.broadcasted_iota(jnp.int32, shape, dim)


def one_zero(test):
    return jnp.where(test, 1.0, 0.0)


def total_of(values):
    return jnp.sum(jnp.sum(values, 0, keepdims=True), 1, keepdims=True)


def half_lanes(values, side):
    lane = iota(values.shape, len(values.shape) - 1)
    keep = (lane < 64) if side == 0 else (lane >= 64)
    return jnp.where(keep, values.astype(F32), 0.0).astype(BF16)


def stacked(values):
    return jnp.concatenate([half_lanes(values, 0), half_lanes(values, 1)], 0)


def unstacked(values, count):
    lane = iota((count, 128), 1)
    return jnp.where(lane < 64, values[:count], values[count:])


def swap_blocks(first, second):
    lane = iota(first.shape, 1)
    low = jnp.where(lane < 64, first, pltpu.roll(second, 64, 1))
    high = jnp.where(lane < 64, pltpu.roll(first, 64, 1), second)
    return low, high


def split_heads_to(source, high_ref, low_ref):
    for rp in range(ROWS // 2):
        for hp in range(PAIRS):
            lanes = slice(hp * 128, hp * 128 + 128)
            first = source[rp * 64 : rp * 64 + 32, lanes]
            second = source[rp * 64 + 32 : rp * 64 + 64, lanes]
            for side, block in enumerate(swap_blocks(first, second)):
                top, rest = split_two(block)
                rows = slice((2 * hp + side) * 32, (2 * hp + side) * 32 + 32)
                high_ref[rows, rp * 128 : rp * 128 + 128] = top
                low_ref[rows, rp * 128 : rp * 128 + 128] = rest


def merge_heads(probs, hot_all, high_ref, low_ref):
    for rp in range(ROWS // 2):
        if rp % 2 == 0:
            blocks = nt(probs, hot_all[rp * 128 : rp * 128 + 256, :])
        block = blocks[:, (rp % 2) * 128 : (rp % 2) * 128 + 128]
        for hp in range(PAIRS):
            first = block[hp * 64 : hp * 64 + 32]
            second = block[hp * 64 + 32 : hp * 64 + 64]
            for side, part in enumerate(swap_blocks(first, second)):
                top, rest = split_two(part)
                rows = slice(rp * 64 + side * 32, rp * 64 + side * 32 + 32)
                high_ref[rows, hp * 128 : hp * 128 + 128] = top
                if low_ref is not None:
                    low_ref[rows, hp * 128 : hp * 128 + 128] = rest


def norm_rows(source, gain, bias, unit_ref, rstd_ref, normed_ref):
    def body(at, carry):
        rows = pl.ds(pl.multiple_of(at * 64, 64), 64)
        values = source[rows, :]
        centre = values - jnp.sum(values, -1, keepdims=True) * (1.0 / D)
        rstd = lax.rsqrt(jnp.sum(centre * centre, -1, keepdims=True) * (1.0 / D) + NORM_EPS)
        unit = centre * rstd
        unit_ref[rows, :] = unit
        rstd_ref[rows, :] = jnp.broadcast_to(rstd, (64, 128))
        normed_ref[rows, :] = (unit * gain + bias).astype(BF16)
        return carry

    lax.fori_loop(0, HERE // 64, body, 0, unroll=2)


def transpose_into(source, target):
    def body(at, carry):
        rows = pl.ds(pl.multiple_of(at * 128, 128), 128)
        target[:, rows] = source[rows, :].astype(F32).T.astype(BF16)
        return carry

    lax.fori_loop(0, HERE // 128, body, 0)


def over_tiles(width, tile, body):
    for half in range(2):

        def step(at, carry, half=half):
            body(half, pl.multiple_of(at * tile, tile))
            return carry

        lax.fori_loop(0, width // tile, step, 0)


def column_mask():
    rows, lanes = iota((256, 128), 0), iota((256, 128), 1)
    return ((rows & 127) >> 4) == (lanes >> 4)


class Saved(typing.NamedTuple):
    stream: typing.Any
    branch: typing.Any
    unit_1: typing.Any
    unit_2: typing.Any
    rstd_1: typing.Any
    rstd_2: typing.Any
    row_mixed_t: typing.Any
    col_normed_t: typing.Any
    col_mixed_t: typing.Any
    feed_normed_t: typing.Any
    col_proj: typing.Any
    col_prob: typing.Any
    active: typing.Any
    slope: typing.Any
    grad_head: typing.Any
    hot_all: typing.Any
    hot_ri: typing.Any
    hot_ir: typing.Any
    prob: typing.Any
    weight_hi: typing.Any
    value_two: typing.Any
    touch: typing.Any
    table: typing.Any
    norms: typing.Any
    proj_t: typing.Any
    extras: typing.Any
    moved: typing.Any


AT = Saved(*range(len(Saved._fields)))
SAVED = Saved(
    stream=((HERE, D), F32),
    branch=((HERE, D), BF16),
    unit_1=((HERE, D), F32),
    unit_2=((HERE, D), F32),
    rstd_1=((HERE, 128), F32),
    rstd_2=((HERE, 128), F32),
    row_mixed_t=((D, HERE), BF16),
    col_normed_t=((D, HERE), BF16),
    col_mixed_t=((D, HERE), BF16),
    feed_normed_t=((D, HERE), BF16),
    col_proj=((HERE, 3 * D), BF16),
    col_prob=((4 * PAIRS, 256, 128), F32),
    active=((HERE, FF), BF16),
    slope=((HERE, FF), BF16),
    grad_head=((VP, D), F32),
    hot_all=((ROWS * VP, COLS), BF16),
    hot_ri=((VP, HERE), BF16),
    hot_ir=((VP, HERE), BF16),
    prob=((HEADS * WIDE, COLS), F32),
    weight_hi=((HERE, D), BF16),
    value_two=((PAIRS, 128, 128), BF16),
    touch=((WIDE, COLS), F32),
    table=((VP, D), F32),
    norms=((8, D), F32),
    proj_t=((VP, 3 * D), BF16),
    extras=((8, 128), F32),
    moved=((8, D), F32),
)


class Forward(typing.NamedTuple):
    ids: typing.Any
    targets: typing.Any
    slots: typing.Any
    normed: typing.Any
    mixed: typing.Any
    normed_2: typing.Any
    mixed_2: typing.Any
    second_hot: typing.Any
    weight_lo: typing.Any
    left_hi: typing.Any
    left_lo: typing.Any
    lookup: typing.Any
    prob_low: typing.Any
    unit: typing.Any
    rstd: typing.Any


FORWARD = Forward(
    ids=((ROWS, COLS), jnp.int32),
    targets=((ROWS, 128), jnp.int32),
    slots=((8, SLOTS), jnp.int32),
    normed=((HERE, D), BF16),
    mixed=((HERE, D), BF16),
    normed_2=((HERE, D), BF16),
    mixed_2=((HERE, D), BF16),
    second_hot=((COLS, SLOTS), BF16),
    weight_lo=((HERE, D), BF16),
    left_hi=((HEADS * WIDE, ROWS * VP), BF16),
    left_lo=((HEADS * WIDE, ROWS * VP), BF16),
    lookup=((HERE, D), F32),
    prob_low=((HEADS * WIDE, COLS), BF16),
    unit=((HERE, D), F32),
    rstd=((HERE, 128), F32),
)


def position():
    z, y, k, c = place()
    me = (z * 4 + y * 2 + k) * 2 + c
    return z // 2, lax.rem(me, 16)


def read_tokens(small, f):
    alignment, block = position()
    side, part = block // 8, lax.rem(block // 4, 2)
    for r in range(ROWS):
        for cc in range(2):
            for q in range(2):
                lanes = slice(cc * 256 + q * 128, cc * 256 + q * 128 + 128)
                f.ids[r : r + 1, lanes] = small[r * 2 + cc, pl.ds(2 * alignment + q, 1), :]
        f.targets[r : r + 1, :] = small[r * 2 + side, pl.ds(4 + 2 * alignment + part, 1), :]
    lane = iota((1, 128), 1)
    for number in range(SLOTS // 128):
        for which in range(3):
            row = pl.ds(8 + 3 * alignment + which, 1)
            first = small[number * 4 + side, row, :]
            second = pltpu.roll(small[number * 4 + 2 + side, row, :], 64, 1)
            f.slots[which : which + 1, number * 128 : number * 128 + 128] = jnp.where(
                lane < 64, first, second
            )


def local_hot(values, shift):
    values = pltpu.roll(values, shift, 1)
    turned = [values] + [pltpu.roll(values, 32 * n, 1) for n in (1, 2, 3)]
    lane = iota((1, 128), 1)
    tiles = []
    for tile in range(4):
        row = turned[3][4 * tile + 3 : 4 * tile + 4]
        for n in (2, 1, 0):
            row = jnp.where(lane < 32 * n + 32, turned[n][4 * tile + n : 4 * tile + n + 1], row)
        tiles.append(row)
    row = jnp.concatenate(tiles, 1)
    return one_zero(row == iota((VP, HERE), 0)).astype(BF16)


def contact_part(contact_head, f, s, pair_count):
    _, block = position()
    base = block * WIDE
    head_sum = jnp.zeros((WIDE, COLS), F32)
    for h in range(HEADS):
        head_sum = head_sum + contact_head[h] * f.prob_low[h * 32 : h * 32 + 32, :].astype(F32)
    top, rest = split_two(head_sum)
    last = (head_sum - top.astype(F32) - rest.astype(F32)).astype(BF16)
    parts = jnp.concatenate([top, rest, last], 0)
    touch = jnp.zeros((WIDE, COLS), F32)
    bce = jnp.zeros((1, 1), F32)
    coef_sum = jnp.zeros((1, 1), F32)
    for number in range(SLOTS // 512):
        lanes = slice(number * 512, number * 512 + 512)
        first, label = (f.slots[n : n + 1, lanes] for n in (0, 2))
        second_hot = f.second_hot[:, lanes]
        picked = nn(parts, second_hot)
        picked = picked[:32] + picked[32:64] + picked[64:]
        first_hot = one_zero((first - base) == iota((WIDE, 512), 0))
        logit = jnp.sum(picked * first_hot, 0, keepdims=True) * COLS + contact_head[HEADS]
        owned = jnp.sum(first_hot, 0, keepdims=True) > 0.5
        valid = (label >= 0) & owned
        positive = one_zero(label == 1)
        small = jnp.exp(-jnp.abs(logit))
        soft = jnp.maximum(logit, 0.0) + jnp.log(1.0 + small)
        bce = bce + total_of(jnp.where(valid, soft - positive * logit, 0.0))
        sigmoid = jnp.where(logit >= 0.0, 1.0, small) / (1.0 + small)
        coef = jnp.where(valid, sigmoid - positive, 0.0) / pair_count
        coef_sum = coef_sum + total_of(coef)
        coef_top, coef_rest = split_two(first_hot * coef)
        touch = touch + nt(coef_top, second_hot) + nt(coef_rest, second_hot)
    s.touch[...] = touch
    column = iota((1, 128), 1)
    row = jnp.where(column == HEADS, coef_sum, 0.0)
    for h in range(HEADS):
        part = total_of(touch * f.prob_low[h * 32 : h * 32 + 32, :].astype(F32)) * COLS
        row = row + jnp.where(column == h, part, 0.0)
    return row, bce


def feature_order():
    shape = (384, 384)
    spot = iota(shape, 0)
    block = (spot * 2731) >> 16
    swapped = (block & 28) | ((block & 1) << 1) | ((block >> 1) & 1)
    return one_zero(spot + (swapped - block) * 24 == iota(shape, 1)).astype(BF16)


def forward_body(small, contact_head, weights, s, f, cells, projected, hook, emit):
    out_row, in_col, out_col = weights[:3]
    up_parts, down_parts = weights[3:5], weights[5:7]
    hook()
    features = cells()
    ahead = (
        ((iota((HERE, HERE), 0) >> 4) == (iota((HERE, HERE), 1) & 31))
        & ((iota((HERE, HERE), 0) & 15) == (iota((HERE, HERE), 1) >> 5))
    )
    ahead = one_zero(ahead).astype(BF16)
    read_tokens(small, f)
    _, block = position()
    shift = lax.rem(128 - lax.rem(block, 4) * 32, 128)
    window = pl.ds(pl.multiple_of((block // 4) * 128, 128), 128)
    hot_ri = local_hot(f.ids[:, window], shift)
    goal_ri = local_hot(f.targets[...], shift)
    s.hot_ri[...] = hot_ri
    for number in range(SLOTS // 512):
        lanes = slice(number * 512, number * 512 + 512)
        f.second_hot[:, lanes] = one_zero(f.slots[1:2, lanes] == iota((COLS, 512), 0)).astype(BF16)
    for r in range(ROWS):
        row = f.ids[r : r + 1, :]
        s.hot_all[r * VP : r * VP + VP, :] = one_zero(row == iota((VP, COLS), 0)).astype(BF16)
    shape = (HERE, HERE)
    back = (
        ((iota(shape, 1) >> 4) == (iota(shape, 0) & 31))
        & ((iota(shape, 1) & 15) == (iota(shape, 0) >> 5))
    )
    back = one_zero(back).astype(BF16)
    hot_ir = nn(hot_ri, back).astype(BF16)
    s.hot_ir[...] = hot_ir
    goal = nn(goal_ri, back)
    entries = jnp.zeros((4, 128), F32)
    labelled = jnp.zeros((1, 128), F32)
    for d in range(32):
        entries = entries + one_zero(small[d, 0:4, :] == MASK_ID)
        labelled = labelled + one_zero(small[d, 10:11, :] >= 0) + one_zero(small[d, 13:14, :] >= 0)
    entries, labelled = total_of(entries), total_of(labelled)

    hook()
    features = features[...].T
    table = features[:VP]
    norms = features[VP : VP + 8]
    s.table[...] = table
    s.norms[...] = norms
    table_low = table.astype(BF16)

    def vector(number):
        return norms[number : number + 1, :]

    hook()
    projected(s.proj_t)
    pair_parts = []
    for hp in range(PAIRS):
        lanes = slice(hp * 128, hp * 128 + 128)
        key = s.proj_t[:, D + hp * 128 : D + hp * 128 + 128]
        value = s.proj_t[:, 2 * D + hp * 128 : 2 * D + hp * 128 + 128]
        s.value_two[hp] = stacked(value)
        pair_parts.append(nt(s.proj_t[:, lanes], stacked(key)))
    pair_hi, pair_lo = split_two(jnp.concatenate(pair_parts, 1))
    hook()
    f.lookup[...] = tn(hot_ri, pair_hi) + tn(hot_ri, pair_lo)
    split_heads_to(f.lookup, f.left_hi, f.left_lo)
    hook()
    hot_all = s.hot_all[...]
    score = (nn(f.left_hi[...], hot_all) + nn(f.left_lo[...], hot_all)) * (HD * ROWS) ** (-0.5)
    score = jnp.exp(score - jnp.max(score, -1, keepdims=True))
    prob = score / jnp.sum(score, -1, keepdims=True)
    s.prob[...] = prob
    f.prob_low[...] = prob.astype(BF16)
    hook()
    merge_heads(f.prob_low[...], s.hot_all, s.weight_hi, f.weight_lo)
    hook()
    for hp in range(PAIRS):
        lanes = slice(hp * 128, hp * 128 + 128)
        value = s.value_two[hp]
        both = jnp.concatenate([s.weight_hi[:, lanes], f.weight_lo[:, lanes]], 1)
        f.mixed[:, lanes] = nn(both, jnp.concatenate([value, value], 0)).astype(BF16)
    f.mixed[...] = nn(ahead, f.mixed[...]).astype(BF16)
    s.stream[...] = tn(hot_ir, table_low)
    emit(AT.hot_all, AT.hot_ri, AT.hot_ir, AT.table, AT.norms, AT.proj_t, AT.value_two, AT.prob, AT.weight_hi)
    hook()
    for half in range(2):
        lanes = slice(half * 384, half * 384 + 384)
        s.stream[:, lanes] += nn(f.mixed[...], out_row[half])
    norm_rows(s.stream, vector(1), vector(5), s.unit_1, s.rstd_1, f.normed)
    emit(AT.unit_1, AT.rstd_1)

    def project(half, at):
        s.col_proj[:, half * 1152 + at : half * 1152 + at + 384] = nn(
            f.normed[...], in_col[half, :, at : at + 384]
        ).astype(BF16)

    for third in range(3):
        hook()
        for half in range(2):
            project(half, third * 384)
    emit(AT.col_proj)

    def attend(at, carry):
        rows = pl.ds(pl.multiple_of((at // PAIRS) * 128, 128), 128)
        lane = lax.rem(at, PAIRS) * 128

        def lanes(part):
            return pl.ds(pl.multiple_of(part * D + lane, 128), 128)

        query = stacked(s.col_proj[rows, lanes(0)])
        score = nt(query, s.col_proj[rows, lanes(1)]) * HD ** (-0.5)
        score = jnp.where(column_mask(), score, -1e30)
        score = jnp.exp(score - jnp.max(score, -1, keepdims=True))
        prob = score / jnp.sum(score, -1, keepdims=True)
        s.col_prob[at] = prob
        mixed = nn(prob.astype(BF16), s.col_proj[rows, lanes(2)])
        f.mixed_2[rows, lanes(0)] = unstacked(mixed, 128).astype(BF16)
        return carry

    for part in range(4):
        hook()
        lax.fori_loop(part * PAIRS, part * PAIRS + PAIRS, attend, 0, unroll=3)
    hook()
    emit(AT.col_prob)
    for half in range(2):
        lanes = slice(half * 384, half * 384 + 384)
        s.stream[:, lanes] += nn(f.mixed_2[...], out_col[half])
    norm_rows(s.stream, vector(2), vector(6), s.unit_2, s.rstd_2, f.normed_2)
    emit(AT.unit_2, AT.rstd_2)
    hook()
    contact_row, bce = contact_part(contact_head, f, s, labelled)
    emit(AT.touch)
    for part in range(2):

        def widen(half, at, part=part):
            lanes = slice(part * 1536 + half * 768 + at, part * 1536 + half * 768 + at + UP_TILE)
            up = nn(f.normed_2[...], up_parts[part][half, :, at : at + UP_TILE])
            active, slope = gelu_parts(up)
            s.active[:, lanes] = active.astype(BF16)
            s.slope[:, lanes] = slope.astype(BF16)

        for half in range(2):
            hook()
            for at in range(0, 768, UP_TILE):
                widen(half, at)
        hook()
        if part == 0:
            transpose_into(f.mixed, s.row_mixed_t)
            transpose_into(f.normed, s.col_normed_t)
            emit(AT.row_mixed_t, AT.col_normed_t)
        else:
            transpose_into(f.mixed_2, s.col_mixed_t)
            emit(AT.col_mixed_t)

    emit(AT.active, AT.slope)
    for part, at, size in ((0, 0, 768), (1, 0, 384), (1, 384, 384)):
        hook()
        added = []
        for half in range(2):
            start = part * 1536 + half * 768 + at
            matrix = down_parts[part][half, :, at : at + size]
            added.append(nt(s.active[:, start : start + size], matrix))
        s.stream[...] += added[0] + added[1]
        if part == 0:
            hook()
            transpose_into(f.normed_2, s.feed_normed_t)
            emit(AT.feed_normed_t)
    hook()
    norm_rows(s.stream, vector(3), vector(7), f.unit, f.rstd, f.normed)
    logits = nt(table_low, f.normed[...]) * D ** (-0.5)
    vocab = iota((VP, HERE), 0)
    logits = jnp.where(vocab < VOCAB, logits, -1e30)
    shifted = logits - jnp.max(logits, 0, keepdims=True)
    log_probs = shifted - jnp.log(jnp.sum(jnp.exp(shifted), 0, keepdims=True))
    keep = hot_ir[MASK_ID : MASK_ID + 1].astype(F32) > 0.5
    mlm = -total_of(jnp.where(keep & (goal > 0.5), log_probs, 0.0))
    logit_grad = jnp.where(keep, jnp.exp(log_probs) - goal, 0.0) / entries
    logit_low = (logit_grad * D ** (-0.5)).astype(BF16)
    s.grad_head[...] = nn(logit_low, f.normed[...])
    hook()
    f.lookup[...] = tn(logit_low, table_low)
    scale_3, shift_3 = back_rows(f.unit, f.rstd, vector(3), f.lookup, s.stream, s.branch, True)
    emit(AT.stream, AT.branch)
    line = iota((8, D), 0)
    s.moved[...] = jnp.where(line == 0, scale_3, jnp.where(line == 1, shift_3, 0.0))
    column = iota((1, 128), 1)
    row = contact_row + jnp.where(column == HEADS + 1, mlm, 0.0) + jnp.where(column == HEADS + 2, bce, 0.0)
    counted = jnp.where(column == 0, entries, 0.0) + jnp.where(column == 1, labelled, 0.0)
    line = iota((8, 128), 0)
    s.extras[...] = jnp.where(line == 0, row, jnp.where(line == 1, counted, 0.0))
    emit(AT.grad_head, AT.extras, AT.moved)
    hook()


def back_rows(unit_ref, rstd_ref, gain, upstream_ref, stream_ref, low_ref, first):
    def body(at, carry):
        scale, move = carry
        rows = pl.ds(pl.multiple_of(at * 64, 64), 64)
        upstream = upstream_ref[rows, :]
        unit = unit_ref[rows, :]
        inner = upstream * gain
        mean = jnp.sum(inner, -1, keepdims=True) * (1.0 / D)
        along = jnp.sum(inner * unit, -1, keepdims=True) * (1.0 / D)
        grad = rstd_ref[rows, 0:1] * (inner - mean - unit * along)
        if not first:
            grad = grad + stream_ref[rows, :]
        stream_ref[rows, :] = grad
        low_ref[rows, :] = grad.astype(BF16)
        touched = upstream * unit
        for n in range(8):
            scale = scale + touched[n * 8 : n * 8 + 8]
            move = move + upstream[n * 8 : n * 8 + 8]
        return scale, move

    zero = jnp.zeros((8, D), F32)
    scale, move = lax.fori_loop(0, HERE // 64, body, (zero, zero), unroll=2)
    return jnp.sum(scale, 0, keepdims=True), jnp.sum(move, 0, keepdims=True)


MATRICES = (128, 384, 1152, 384, 768, 768, 768, 768)
UNITS = (
    (0, 0, 128, True),
    (1, 0, 384, False),
    (2, 0, 384, True),
    (2, 384, 384, True),
    (2, 768, 384, True),
    (3, 0, 384, False),
    (4, 0, 768, True),
    (5, 0, 768, True),
    (6, 0, 768, True),
    (7, 0, 384, True),
    (7, 384, 384, True),
)
Z_LAST = {9: 1, 10: 2}
FORWARD_ORDER = (
    ((0, 0), (0, 2), (0, 11), (1, 0), (0, 1), (0, 9), (0, 10), (1, 11), (2, 0), (0, 3), (1, 2), (0, 4), (2, 11), (3, 0), (1, 10), (1, 9), (1, 1), (4, 0),),
    ((2, 2), (0, 5), (2, 1),),
    ((3, 11), (1, 3), (0, 6), (3, 2), (4, 11), (1, 4),),
    ((3, 1), (4, 2), (1, 5), (0, 7),),
    ((4, 1), (2, 3), (2, 4),),
    ((1, 6), (0, 8),),
    (),
    ((3, 3),),
    ((3, 4), (2, 5), (4, 3), (2, 9), (1, 7), (4, 4),),
    (),
    (),
    (),
    ((3, 5), (2, 6),),
    (),
    ((4, 5), (2, 7), (2, 10),),
    ((1, 8),),
    ((3, 6),),
    ((3, 9), (3, 7), (4, 6),),
    (),
    ((2, 8), (4, 9),),
    ((4, 7),),
    (),
    (),
    ((3, 8), (3, 10), (4, 8),),
    ((4, 10),),
    (),
    (),
    (),
    (),
    (),
)


def spot(paired, cc, zz, yy, k):
    return (k, zz, yy, cc) if paired else (cc, zz, yy, k)


def forward_kernel(*refs):
    count, parts = len(UNITS), len(MATRICES)
    raw = refs[:11]
    contact_head = refs[11]
    at = 12
    far = (None, *refs[at : at + parts - 1])
    saved_far = refs[at + parts - 1 : at + parts - 1 + len(SAVED)]
    at += parts - 1 + len(SAVED)
    outs = refs[at : at + parts]
    at += parts
    outgoing = refs[at : at + count]
    incoming = refs[at + count : at + 2 * count]
    piece = refs[at + 2 * count : at + 3 * count]
    at += 3 * count
    saved = Saved(*refs[at : at + len(SAVED)])
    at += len(SAVED)
    scratch = Forward(*refs[at : at + len(FORWARD)])
    at += len(FORWARD)
    near = refs[at : at + 11]
    at += 11
    small, small_out, corner, features, stat, stat_got, part, part_got, part_line, proj, room = refs[at : at + 11]
    small_send, small_recv, send, recv, local, out_sem, raw_sem, twin_send, twin_recv = refs[at + 11 :]
    tokens, targets, masked, pairs, labels, table, norms, in_w, out_w, up_w, down_w = near
    z, y, k, c = place()
    me = (z * 4 + y * 2 + k) * 2 + c
    raw_copies = [pltpu.make_async_copy(a, b, raw_sem.at[n]) for n, (a, b) in enumerate(zip(raw, near))]
    for item in raw_copies:
        item.start()
    barrier = greet_all()
    for item in raw_copies[:7]:
        item.wait()
    small[...] = jnp.full(small.shape, -1, jnp.int32)
    for micro in range(2):
        for half in range(2):
            lanes = slice(half * 128, half * 128 + 128)
            row = 2 * micro + half
            small[row : row + 1, :] = jnp.where(
                masked[micro, :, lanes] > 0, MASK_ID, tokens[micro, :, lanes]
            )
            small[4 + row : 5 + row, :] = targets[micro, :, lanes]
        row = 8 + 3 * micro
        for which in range(2):
            small[row + which : row + which + 1, 0:64] = pairs[micro, which : which + 1, :]
        small[row + 2 : row + 3, 0:64] = labels[micro : micro + 1, :]
    corner[...] = jnp.zeros(corner.shape, F32)
    corner[0:8, 0:24] = norms[...]
    vectors = pltpu.roll(corner[...].T[:24], 64, 1)
    corner[0:8, 0:24] = jnp.zeros((8, 24), F32)
    corner[0:24, 0:VOCAB] = table[...]
    mine_rows = (corner[0:24, :] + vectors).astype(BF16).astype(F32)
    table_rows = jnp.where(iota((24, 128), 1) < VP, mine_rows, 0.0)
    gain, bias = mine_rows[:, 64:65], mine_rows[:, 68:69]
    piece[0][0:16, :] = small[...].astype(F32)
    piece[0][16:40, :] = mine_rows
    mean = jnp.sum(table_rows, 0, keepdims=True) * (1.0 / 24)
    centre = table_rows - mean
    spread = jnp.sum(centre * centre, 0, keepdims=True)
    line = iota((8, 128), 0)
    stat[...] = jnp.where(line == 0, mean, jnp.where(line == 1, spread, 0.0))
    def master(u, side):
        matrix, start, n, _ = UNITS[u]
        width = MATRICES[matrix]
        if matrix == 2:
            return in_w[1, :, side * 1152 + start : side * 1152 + start + n]
        if matrix in (1, 3):
            rows = out_w[matrix // 2, :, side * 384 : side * 384 + 384].astype(BF16)
            return nn(rows, order)
        begin = (matrix % 2) * 1536 + side * width + start
        return (up_w if matrix < 6 else down_w)[:, begin : begin + n]

    def mine(u):
        return k if UNITS[u][3] else c

    def set_out(u):
        other = jnp.where(mine(u) == 0, master(u, 1), master(u, 0))
        other = jnp.concatenate([other, jnp.zeros((8, UNITS[u][2]), F32)], 0)
        outgoing[u][...] = other.astype(BF16)

    pl.semaphore_wait(barrier, 31)

    def stat_copy(step):
        other = lax.rem(me + step, 32)
        return remote(
            stat, stat_got.at[me], small_send.at[0, step], small_recv.at[0, step], (other // 2, lax.rem(other, 2))
        )

    chip = (z * 2 + y) * 2 + c

    def chip_copy(phase, step):
        other = lax.rem(chip + step, 16)
        target = device(other // 4, lax.rem(other // 2, 2), k, lax.rem(other, 2))
        if phase == 1:
            src, dst = part.at[k, other], part_line.at[chip]
        else:
            src, dst = proj.at[k, chip], proj.at[k, chip]
        return remote(src, dst, small_send.at[phase, step], small_recv.at[phase, step], target)

    def each(last, action):
        def body(step, carry):
            action(step)
            return carry

        lax.fori_loop(1, last, body, 0)

    each(32, lambda step: stat_copy(step).start())

    across, beside, twin = device(z, y, k, 1 - c), device(z, 1 - y, k, c), device(z, y, 1 - k, c)

    def block(u, cc, zz, yy):
        matrix, start, n, paired = UNITS[u]
        where = spot(paired, cc, zz, yy, k)
        if n == MATRICES[matrix]:
            return outs[matrix].at[where]
        return outs[matrix].at[(*where, slice(None), pl.ds(start, n))]

    def copy(u, at, src, dst, target):
        return remote(src, dst, send.at[u, at], recv.at[u, at], target)

    def pair_copy(u):
        return copy(u, 0, outgoing[u], incoming[u], twin if UNITS[u][3] else across)

    def own_copy(u):
        return pltpu.make_async_copy(piece[u], block(u, c, z, y), local.at[u])

    def line_copy(u, step):
        return copy(u, step, piece[u], block(u, c, z, y), device(lax.rem(z + step, 4), y, k, c))

    def same(u, at, cc, zz, yy, target):
        view = block(u, cc, zz, yy)
        return copy(u, at, view, view, target)

    low, high, every = pl.ds(0, 2), pl.ds(2, 2), slice(None)

    def second(u):
        return [same(u, 4, c, low, y, across), same(u, 5, c, high, y, beside)]

    def third_own(u):
        return [same(u, 6, c, low, y, beside), same(u, 7, c, high, y, across)]

    def third_far(u):
        return [same(u, 8, 1 - c, low, y, beside), same(u, 9, c, high, 1 - y, across)]

    def twin_own(u):
        return [same(u, 10, c, every, y, twin)]

    def twin_second(u):
        return [same(u, 11, 1 - c, low, y, twin), same(u, 12, c, high, 1 - y, twin)]

    def twin_third(u):
        return [
            same(u, 13, c, low, 1 - y, twin),
            same(u, 14, 1 - c, high, y, twin),
            same(u, 15, 1 - c, low, 1 - y, twin),
            same(u, 16, 1 - c, high, 1 - y, twin),
        ]

    own_copy(0).start()
    for item in raw_copies[7:]:
        item.wait()
    order = feature_order()
    for u in range(1, count):
        set_out(u)
        pair_copy(u).start()

    def part_twin():
        return remote(part.at[1 - k], part_got, twin_send.at[0], twin_recv.at[0], twin)

    def proj_twin():
        return remote(proj.at[k], proj.at[k], twin_send.at[1], twin_recv.at[1], twin)

    def project_part():
        stat_got[me] = stat[...]
        each(32, lambda step: stat_copy(step).wait())
        means = jnp.zeros((1, 128), F32)
        spreads = jnp.zeros((1, 128), F32)
        for d in range(32):
            means = means + stat_got[d, 0:1, :]
            spreads = spreads + stat_got[d, 1:2, :]
        means = means * (1.0 / 32)
        for d in range(32):
            away = stat_got[d, 0:1, :] - means
            spreads = spreads + 24.0 * away * away
        rstd = lax.rsqrt(spreads * (1.0 / D) + NORM_EPS)
        normed = (table_rows - means) * rstd * gain + bias
        normed = jnp.concatenate([normed, jnp.zeros((8, 128), F32)], 0).astype(BF16)
        for block_at in range(6):
            lanes = slice(block_at * 384, block_at * 384 + 384)
            rows = jnp.concatenate([in_w[0, :, lanes], jnp.zeros((8, 384), F32)], 0).astype(BF16)
            product = tn(normed, rows)
            for group in range(5):
                number = group * 6 + block_at
                part[number // 16, number % 16] = product[group * 8 : group * 8 + 8]
        for number in (30, 31):
            part[number // 16, number % 16] = jnp.zeros((8, 384), F32)
        part_twin().start()

    def project_chip():
        part_twin().wait_recv()
        part[k] = part[k] + part_got[...]
        each(16, lambda step: chip_copy(1, step).start())

    def project_line():
        part_line[chip] = part[k, chip]
        each(16, lambda step: chip_copy(1, step).wait_recv())
        proj[k, chip] = lax.fori_loop(1, 16, lambda at, held: held + part_line[at], part_line[0])
        each(16, lambda step: chip_copy(2, step).start())

    def project_twin():
        each(16, lambda step: chip_copy(2, step).wait_recv())
        proj_twin().start()

    def project_end():
        proj_twin().wait_recv()

    projecting = (project_part, project_chip, project_line, project_twin, project_end)

    def cells():
        for d in range(32):
            at = ((d // 2) % 2, d // 8, (d // 4) % 2, d % 2)
            small_out[d] = outs[0][(*at, slice(0, 16))].astype(jnp.int32)
            start = (((at[1] * 2 + at[2]) * 2 + at[3]) * 2 + at[0]) * 24
            features[start : start + 24, :] = outs[0][(*at, slice(16, 40))]
        return features

    def projected(target):
        room[40:64, :] = jnp.zeros((24, 3 * D), F32)
        for number in range(30):
            rows, lanes = (number // 6) * 8, (number % 6) * 384
            room[rows : rows + 8, lanes : lanes + 384] = proj[number // 16, number % 16]
        target[...] = room[...].astype(BF16)

    def to_across(u):
        return copy(u, 4, piece[u], block(u, c, z, y), across)

    def to_beside(u):
        return copy(u, 5, piece[u], block(u, c, z, y), beside)

    def to_corner(u):
        if Z_LAST[u] == 1:
            return same(u, 6, 1 - c, z, y, beside)
        return same(u, 6, c, z, 1 - y, across)

    def to_line(u):
        return [
            same(u, step, every, z, every, device(lax.rem(z + step, 4), y, k, c)) for step in (1, 3, 2)
        ]

    def to_twin(u):
        return [same(u, 7, every, z, every, twin)]

    def rest_to_twin(u):
        return [same(u, 7 + step, every, lax.rem(z + 4 - step, 4), every, twin) for step in (1, 3, 2)]

    def stage_line(u):
        if u == 0:
            for step in (1, 3, 2):
                line_copy(u, step).start()
            return
        pair_copy(u).wait_recv()
        side = mine(u)
        own = jnp.where(side == 0, master(u, 0), master(u, 1))
        theirs = incoming[u][...].astype(F32)[:24]
        top = jnp.where(side == 0, own, theirs)
        bottom = jnp.where(side == 0, theirs, own)
        piece[u][...] = jnp.concatenate([top, bottom], 0).astype(BF16)
        own_copy(u).start()
        if u in Z_LAST:
            to_across(u).start()
            to_beside(u).start()
            return
        for step in (1, 3, 2):
            line_copy(u, step).start()

    def stage_second(u):
        own_copy(u).wait()
        if u in Z_LAST:
            to_across(u).wait_recv()
            to_beside(u).wait_recv()
            to_corner(u).start()
            return
        for step in (1, 3, 2):
            line_copy(u, step).wait_recv()
        for item in second(u) + third_own(u) + twin_own(u):
            item.start()

    def stage_third(u):
        if u in Z_LAST:
            to_corner(u).wait_recv()
            for item in to_line(u) + to_twin(u):
                item.start()
            return
        for item in second(u):
            item.wait_recv()
        for item in third_far(u) + twin_second(u):
            item.start()

    def stage_twin(u):
        if u in Z_LAST:
            for item in to_line(u):
                item.wait_recv()
            for item in rest_to_twin(u):
                item.start()
            return
        for item in third_own(u) + third_far(u):
            item.wait_recv()
        for item in twin_third(u):
            item.start()

    def far_copy(matrix):
        return pltpu.make_async_copy(outs[matrix], far[matrix], local.at[count + matrix])

    def stage_end(u):
        if u in Z_LAST:
            for item in to_twin(u) + rest_to_twin(u):
                item.wait_recv()
            sent = [to_across(u), to_beside(u), to_corner(u)] + to_line(u) + to_twin(u)
        else:
            for item in twin_own(u) + twin_second(u) + twin_third(u):
                item.wait_recv()
            sent = [line_copy(u, step) for step in (1, 2, 3)]
            sent += second(u) + third_own(u) + third_far(u) + twin_own(u) + twin_second(u)
        for item in sent if u == 0 else [pair_copy(u)] + sent:
            item.wait_send()
        if u == 0:
            return
        if u + 1 == count or UNITS[u + 1][0] != UNITS[u][0]:
            far_copy(UNITS[u][0]).start()

    stages = (stage_line, stage_second, stage_third, stage_twin, stage_end)
    pending = list(FORWARD_ORDER)

    def hook():
        for stage, u in pending.pop(0):
            if u == count:
                projecting[stage]()
            else:
                stages[stage](u)

    def out_copy(at):
        return pltpu.make_async_copy(saved[at], saved_far[at], out_sem.at[at])

    def emit(*numbers):
        for number in numbers:
            out_copy(number).start()

    views = [w.reshape(2, D, n) for w, n in zip(outs[1:], MATRICES[1:])]
    forward_body(small_out, contact_head, views, saved, scratch, cells, projected, hook, emit)
    part_twin().wait_send()
    proj_twin().wait_send()
    for phase in (1, 2):
        each(16, lambda step, phase=phase: chip_copy(phase, step).wait_send())
    assert not pending
    for u in range(count):
        for item in rest_to_twin(u) if u in Z_LAST else twin_third(u):
            item.wait_send()
    for matrix in range(1, parts):
        far_copy(matrix).wait()
    for at in range(len(SAVED)):
        out_copy(at).wait()


def forward_call(raw, contact_head):
    count, parts = len(UNITS), len(MATRICES)
    anywhere = pl.BlockSpec(memory_space=pl.ANY)
    shapes = [(2, NZ, NY, 2, 48, n) for n in MATRICES[1:]]
    widths = [n for _, _, n, _ in UNITS]
    outs = pl.pallas_call(
        forward_kernel,
        out_shape=[jax.ShapeDtypeStruct(shape, BF16) for shape in shapes]
        + [jax.ShapeDtypeStruct(*item) for item in SAVED],
        in_specs=[anywhere] * 11 + [pl.BlockSpec(memory_space=pltpu.SMEM)],
        out_specs=[anywhere] * (parts - 1 + len(SAVED)),
        scratch_shapes=[pltpu.VMEM((2, NZ, NY, 2, 40, 128), F32)]
        + [pltpu.VMEM(shape, BF16) for shape in shapes]
        + [pltpu.VMEM((32, n), BF16) for n in widths] * 2
        + [pltpu.VMEM((40, 128), F32)]
        + [pltpu.VMEM((48, n), BF16) for n in widths[1:]]
        + [pltpu.VMEM(*item) for item in SAVED]
        + [pltpu.VMEM(*item) for item in FORWARD]
        + [pltpu.VMEM(item.shape, item.dtype) for item in raw]
        + [
            pltpu.VMEM((16, 128), jnp.int32),
            pltpu.VMEM((32, 16, 128), jnp.int32),
            pltpu.VMEM((128, 128), F32),
            pltpu.VMEM((D, 128), F32),
            pltpu.VMEM((8, 128), F32),
            pltpu.VMEM((32, 8, 128), F32),
            pltpu.VMEM((2, 16, 8, 384), F32),
            pltpu.VMEM((16, 8, 384), F32),
            pltpu.VMEM((16, 8, 384), F32),
            pltpu.VMEM((2, 16, 8, 384), F32),
            pltpu.VMEM((VP, 3 * D), F32),
            pltpu.SemaphoreType.DMA((3, 32)),
            pltpu.SemaphoreType.DMA((3, 32)),
            pltpu.SemaphoreType.DMA((count, 17)),
            pltpu.SemaphoreType.DMA((count, 17)),
            pltpu.SemaphoreType.DMA((count + parts,)),
            pltpu.SemaphoreType.DMA((len(SAVED),)),
            pltpu.SemaphoreType.DMA((len(raw),)),
            pltpu.SemaphoreType.DMA((2,)),
            pltpu.SemaphoreType.DMA((2,)),
        ],
        compiler_params=pltpu.CompilerParams(
            collective_id=0, has_side_effects=True, vmem_limit_bytes=62 * 2**20
        ),
    )(*raw, contact_head)
    return outs[: parts - 1], Saved(*outs[parts - 1 :])


def summed_rows(sums, group):
    return jnp.concatenate([sums[3 * group + third] for third in range(3)], 1).astype(F32)


def table_finish(sums, room, table_ref, norms_ref, proj_t, in_row, g_in, g_norm, send_stat):
    z, y, k, c = place()
    me = ((z * 2 + y) * 2 + c) * 2 + k
    room[0:128, :] = jnp.zeros((128, D), F32)
    for number in range(2):
        room[4 + 16 * number : 20 + 16 * number, :] = summed_rows(sums, number)
        room[68 + 16 * number : 84 + 16 * number, :] = summed_rows(sums, 2 + number)
    pair = room[0:64, :]
    value_grad = room[64:128, :]
    vectors = summed_rows(sums, 6)
    vectors = vectors[:8] + vectors[8:]
    line = iota((8, D), 0)
    table_grad = jnp.concatenate(
        [
            summed_rows(sums, 4),
            summed_rows(sums, 5),
            jnp.where(line == 0, vectors[7:8], 0.0),
            jnp.zeros((24, D), F32),
        ],
        0,
    )
    pair_hi, pair_lo = split_two(pair)
    scale = (HD * ROWS) ** (-0.5)
    query_grad, key_grad = [], []
    for hp in range(PAIRS):
        lanes = slice(hp * 128, hp * 128 + 128)
        query = proj_t[:, lanes]
        key = stacked(proj_t[:, D + hp * 128 : D + hp * 128 + 128])
        high, low = pair_hi[:, lanes], pair_lo[:, lanes]
        query_grad.append((nn(high, key) + nn(low, key)) * scale)
        key_grad.append(unstacked(tn(high, query) + tn(low, query), VP) * scale)
    proj_hi, proj_lo = split_two(jnp.concatenate(query_grad + key_grad + [value_grad], 1))
    shard = D // 32
    pick = one_zero(iota((shard, D), 1) == iota((shard, D), 0) + me * shard).astype(BF16)
    weight = in_row[...].astype(BF16)
    back_t = nt(weight, proj_hi) + nt(weight, proj_lo)
    back = nt(proj_hi, weight) + nt(proj_lo, weight)
    table = table_ref[...]
    table_low = table.astype(BF16)
    unit, rstd = norm_stats(table)
    mean = jnp.sum(table, -1, keepdims=True) * (1.0 / D)
    same = iota((VP, VP), 0) == iota((VP, VP), 1)

    def as_row(column):
        return jnp.sum(jnp.where(same, column, 0.0), 0, keepdims=True)

    rstd_row = as_row(rstd)
    unit_t = (nt(pick, table_low) - as_row(mean)) * rstd_row
    unit_mine = (nt(table_low, pick) - mean) * rstd
    norms = jnp.concatenate([norms_ref[...], jnp.zeros((8, D), F32)], 0).astype(BF16)
    inner = back_t * nt(pick, norms)[:, 0:1]

    def three(values):
        top, rest = split_two(values)
        return top, rest, (values - top.astype(F32) - rest.astype(F32)).astype(BF16)

    emb_grad = sum(nt(pick, part) for part in three(table_grad))
    before = emb_grad + rstd_row * inner
    parts = (inner, inner * unit_t, before, before * unit_t, unit_t, unit_t * unit_t, before * before)
    send_stat([jnp.sum(part, 0, keepdims=True) for part in parts])
    scale_0 = jnp.sum(back * unit_mine, 0, keepdims=True)
    shift_0 = jnp.sum(back, 0, keepdims=True)
    line = iota((16, D), 0)
    norm_grad = jnp.zeros((16, D), F32)
    for number, source in ((1, 0), (2, 1), (3, 2), (5, 3), (6, 4), (7, 5)):
        norm_grad = jnp.where(line == number, vectors[source : source + 1], norm_grad)
    normed = (unit * norms_ref[0:1, :] + norms_ref[4:5, :]).astype(BF16)
    mine = nt(pick, normed).astype(BF16)
    in_grad = nn(mine, proj_hi) + nn(mine, proj_lo)
    g_in[...] = in_grad
    own_norm = sum(nt(part, pick) for part in three(norm_grad))[:8]
    line = iota((8, shard), 0)
    own_norm = jnp.where(line == 0, scale_0, jnp.where(line == 4, shift_0, own_norm))
    g_norm[...] = own_norm
    found = total_of(in_grad * in_grad) + total_of(own_norm * own_norm)
    return inner, unit_t, rstd_row, emb_grad, found


PIECES = 21
GRAD_WIDTHS = (768, 768, 768, 768, 384, 1152, 384)
GRAD_UNITS = (
    (0, 0, 384, True),
    (0, 384, 384, True),
    (1, 0, 384, True),
    (1, 384, 384, True),
    (2, 0, 384, True),
    (2, 384, 384, True),
    (3, 0, 384, True),
    (3, 384, 384, True),
    (4, 0, 384, False),
    (5, 0, 384, True),
    (5, 384, 384, True),
    (5, 768, 384, True),
    (6, 0, 384, False),
)
Z_FIRST = {1: 1, 5: 2}
BACKWARD_ORDER = (
    (),
    (),
    (),
    (),
    (),
    (),
    ((0, 0),),
    (),
    ((0, 1),),
    (),
    (),
    ((1, 0), (0, 2),),
    ((0, 3),),
    (),
    ((2, 0), (0, 4),),
    ((0, 5),),
    (),
    ((1, 2),),
    ((0, 6),),
    ((1, 3), (0, 7),),
    ((1, 1), (1, 4),),
    ((2, 2), (0, 8),),
    (),
    ((1, 6),),
    ((2, 3),),
    (),
    ((1, 7),),
    ((2, 1),),
    ((2, 4),),
    (),
    ((1, 5),),
    ((1, 8), (0, 9), (2, 6),),
    ((0, 10), (2, 7),),
    ((2, 5), (0, 11),),
    ((2, 8),),
    ((0, 12),),
    ((1, 9),),
    ((1, 10),),
    ((1, 11),),
    ((3, 0), (3, 1), (3, 2), (3, 3), (3, 4), (3, 5), (3, 6), (1, 12), (3, 7), (3, 8), (4, 0), (2, 9), (4, 1), (2, 10), (4, 2), (4, 3), (4, 4), (5, 0), (2, 11), (3, 9), (2, 12), (4, 5), (4, 6), (4, 7), (3, 10), (4, 8), (4, 9), (4, 10), (6, 0), (3, 11), (3, 12), (4, 11), (4, 12),),
)


class Kept(typing.NamedTuple):
    stream: typing.Any
    norms: typing.Any
    table: typing.Any
    proj_t: typing.Any
    extras: typing.Any
    moved: typing.Any
    grad_head: typing.Any
    touch: typing.Any
    value_two: typing.Any


class Early(typing.NamedTuple):
    slope: typing.Any
    active: typing.Any
    feed_normed_t: typing.Any
    unit_2: typing.Any
    rstd_2: typing.Any
    col_mixed_t: typing.Any
    col_proj: typing.Any
    col_prob: typing.Any
    col_normed_t: typing.Any
    unit_1: typing.Any
    rstd_1: typing.Any


class Late(typing.NamedTuple):
    row_mixed_t: typing.Any
    hot_all: typing.Any
    weight_hi: typing.Any
    prob: typing.Any
    hot_ri: typing.Any
    hot_ir: typing.Any


def pick_items(group, source):
    return [getattr(source, name) for name in group._fields]


def backward_kernel(*refs):
    widths = GRAD_WIDTHS
    count = len(widths)
    contact_head = refs[0]
    far = refs[1 : 1 + count]
    in_row_far = refs[1 + count]
    saved = Saved(*refs[2 + count : 2 + count + len(SAVED)])
    at = 2 + count + len(SAVED)
    outs = refs[at : at + count]
    g_in, g_emb, g_norm, stats = refs[at + count : at + count + 4]
    at += count + 4
    grads = refs[at : at + count]
    kept = Kept(*refs[at + count : at + count + len(Kept._fields)])
    at += count + len(Kept._fields)
    upstream, branch, branch_t, mixed = refs[at : at + 4]
    scratch = refs[at + 4 :]
    units = len(GRAD_UNITS)
    got_0, got_1a, got_1b, got_2a, got_2b, got_3, total, got_4 = (
        scratch[i * units : (i + 1) * units] for i in range(8)
    )
    table, table_out, table_got, square, square_got, stat, stat_got, late_rows = scratch[8 * units : 8 * units + 8]
    table_send, table_recv, send, recv, local = scratch[8 * units + 8 :]
    z, y, k, c = place()
    me = (z * 4 + y * 2 + k) * 2 + c
    across, beside, twin = device(z, y, k, 1 - c), device(z, 1 - y, k, c), device(z, y, 1 - k, c)
    stream = kept.stream
    square[...] = jnp.zeros(square.shape, F32)

    copies = {}

    def load(number, source, target):
        copies[number] = pltpu.make_async_copy(source, target, local.at[number])
        copies[number].start()

    def need(*numbers):
        for number in numbers:
            copies[number].wait()

    def weight(m):
        return len(SAVED) + m

    load(AT.branch, saved.branch, branch)
    load(weight(0), far[0], grads[0])
    barrier = greet_all()

    def copy(m, at, src, dst, target):
        return remote(src, dst, send.at[m, at], recv.at[m, at], target)

    low, high = pl.ds(0, 2), pl.ds(2, 2)
    every = slice(None)

    def where(u, cc, zz, yy):
        matrix, start, n, paired = GRAD_UNITS[u]
        index = spot(paired, cc, zz, yy, k)
        return index if n == widths[matrix] else (*index, every, pl.ds(start, n))

    def block(u, cc, zz, yy):
        return grads[GRAD_UNITS[u][0]].at[where(u, cc, zz, yy)]

    def ordered(u, cc, rest):
        return (*rest, cc) if GRAD_UNITS[u][3] else (cc, *rest)

    def twin_copy(u):
        matrix, start, n, paired = GRAD_UNITS[u]
        index = (1 - k,) if paired else (every, every, every, 1 - k)
        if n != widths[matrix]:
            index = (*index, *(every,) * (5 - len(index)), pl.ds(start, n))
        return copy(u, 0, grads[matrix].at[index], got_0[u], twin)

    def first(u):
        return [
            copy(u, 1, block(u, every, low, 1 - y), got_1a[u], beside),
            copy(u, 2, block(u, 1 - c, high, every), got_1b[u], across),
        ]

    def second(u):
        return [
            copy(u, 3, block(u, 1 - c, low, y), got_2a[u], across),
            copy(u, 4, block(u, c, high, 1 - y), got_2b[u], beside),
        ]

    def along(u):
        return [
            copy(
                u,
                4 + step,
                block(u, c, lax.rem(z + step, 4), y),
                got_3[u].at[step - 1],
                device(lax.rem(z + step, 4), y, k, c),
            )
            for step in (1, 3, 2)
        ]

    def z_first(u):
        return [
            copy(
                u,
                step,
                block(u, every, lax.rem(z + step, 4), every),
                got_1a[u].at[step - 1],
                device(lax.rem(z + step, 4), y, k, c),
            )
            for step in (1, 3, 2)
        ]

    def plane_first(u):
        if Z_FIRST[u] == 1:
            return [copy(u, 4, block(u, every, z, 1 - y), got_2a[u], beside)]
        return [copy(u, 4, block(u, 1 - c, z, every), got_2a[u], across)]

    def plane_second(u):
        if Z_FIRST[u] == 1:
            return [copy(u, 5, block(u, 1 - c, z, y), got_2b[u], across)]
        return [copy(u, 5, block(u, c, z, 1 - y), got_2b[u], beside)]

    def mine(u):
        return k if GRAD_UNITS[u][3] else c

    def pair(u):
        return [copy(u, 8, total[u].at[1 - mine(u)], got_4[u], twin if GRAD_UNITS[u][3] else across)]

    def peer(step):
        return lax.rem(me + step, 32)

    def source(step):
        return lax.rem(me + 32 - step, 32)

    def table_copy(step, back, index):
        target = (peer(step) // 2, lax.rem(peer(step), 2))
        if back:
            return remote(
                table_out.at[index], table_out.at[index], table_send.at[1, step], table_recv.at[1, step], target
            )
        return remote(
            table.at[index], table_got.at[me], table_send.at[0, step], table_recv.at[0, step], target
        )

    def table_start(step):
        @pl.when(peer(step) < PIECES)
        def _():
            table_copy(step, False, peer(step)).start()

    def table_wait_send(step):
        @pl.when(peer(step) < PIECES)
        def _():
            table_copy(step, False, 0).wait_send()

        @pl.when(me < PIECES)
        def _():
            table_copy(step, True, 0).wait_send()

    def table_wait_back(step):
        @pl.when(source(step) < PIECES)
        def _():
            table_copy(step, True, 0).wait_recv()

    def each(action):
        def body(step, carry):
            action(step)
            return carry

        lax.fori_loop(1, 32, body, 0)

    def gather_into(u, cc, zz, yy, *others):
        matrix = GRAD_UNITS[u][0]
        index = where(u, cc, zz, yy)
        if not others:
            grads[matrix][index] = grads[matrix][index] + got_0[u][ordered(u, cc, (zz, yy))]
            return
        value = grads[matrix][index].astype(F32) + got_0[u][ordered(u, cc, (zz, yy))].astype(F32)
        for other in others:
            value = value + other.astype(F32)
        grads[matrix][index] = value.astype(BF16)

    def from_line(u, cc, yy):
        index = (yy, cc) if GRAD_UNITS[u][3] else (cc, yy)
        return [got_1a[u][(step, *index)] for step in range(3)]

    def stage_first(u):
        twin_copy(u).wait_recv()
        if u in Z_FIRST:
            for step in (1, 3, 2):
                for cc in range(2):
                    for yy in range(2):
                        gather_into(u, cc, lax.rem(z + step, 4), yy)
            for item in z_first(u):
                item.start()
            return
        for a in range(2):
            for b in range(2):
                gather_into(u, a, b, 1 - y)
                gather_into(u, 1 - c, 2 + a, b)
        for item in first(u):
            item.start()

    def from_beside(u, cc, a):
        return got_1a[u][ordered(u, cc, (a,))]

    def stage_second(u):
        if u in Z_FIRST:
            for item in z_first(u):
                item.wait_recv()
            for a in range(2):
                cc, yy = (a, 1 - y) if Z_FIRST[u] == 1 else (1 - c, a)
                gather_into(u, cc, z, yy, *from_line(u, cc, yy))
            for item in plane_first(u):
                item.start()
            return
        for item in first(u):
            item.wait_recv()
        for a in range(2):
            gather_into(u, 1 - c, a, y, from_beside(u, 1 - c, a))
            gather_into(u, c, 2 + a, 1 - y, got_1b[u][a, 1 - y])
        for item in second(u):
            item.start()

    def stage_along(u):
        if u in Z_FIRST:
            for item in plane_first(u):
                item.wait_recv()
            cc, yy = (1 - c, y) if Z_FIRST[u] == 1 else (c, 1 - y)
            gather_into(u, cc, z, yy, *from_line(u, cc, yy), got_2a[u][cc if Z_FIRST[u] == 1 else yy])
            for item in plane_second(u):
                item.start()
            return
        for item in second(u):
            item.wait_recv()
        for a in range(2):
            gather_into(u, c, a, y, from_beside(u, c, a), got_2a[u][a])
            gather_into(u, c, 2 + a, y, got_1b[u][a, y], got_2b[u][a])
        for item in along(u):
            item.start()

    def stage_pair(u):
        full = grads[GRAD_UNITS[u][0]][where(u, c, z, y)].astype(F32)
        if u in Z_FIRST:
            for item in plane_second(u):
                item.wait_recv()
            others = [got_0[u][ordered(u, c, (z, y))], *from_line(u, c, y)]
            others += [got_2a[u][c if Z_FIRST[u] == 1 else y], got_2b[u][...]]
        else:
            for item in along(u):
                item.wait_recv()
            others = [got_3[u][step] for step in range(3)]
        for other in others:
            full = full + other.astype(F32)
        total[u][0] = full[:24]
        total[u][1] = full[24:]
        for item in pair(u):
            item.start()

    def stage_end(u):
        matrix, start, n, _ = GRAD_UNITS[u]
        lanes = slice(start, start + n)
        side = mine(u)
        outs[matrix][side, :, lanes] = total[u][side]
        for item in pair(u):
            item.wait_recv()
        outs[matrix][1 - side, :, lanes] = got_4[u][...]
        own, other = total[u][side], got_4[u][...]
        square[...] += jnp.broadcast_to(total_of(own * own + other * other), (8, 128))
        if u in Z_FIRST:
            sent = z_first(u) + plane_first(u) + plane_second(u)
        else:
            sent = first(u) + second(u) + along(u)
        for item in [twin_copy(u)] + sent:
            item.wait_send()

    def table_sum(u):
        @pl.when(me < PIECES)
        def _():
            each(lambda step: table_copy(step, False, 0).wait_recv())
            table_got[me] = table[me]

            def add(at, held):
                return held + table_got[at].astype(F32)

            total_rows = lax.fori_loop(1, 32, add, table_got[0].astype(F32))
            top, rest = split_two(total_rows[:8] + total_rows[8:])
            exact = jnp.concatenate([top.astype(F32), rest.astype(F32)], 0)
            table_out[me] = jnp.where(me >= 18, exact, total_rows).astype(BF16)
            each(lambda step: table_copy(step, True, me).start())

    late_parts = []

    def table_end(u):
        each(table_wait_back)
        need(weight(count))
        late_parts.append(
            table_finish(
                table_out, upstream, kept.table, kept.norms, kept.proj_t, late_parts[0], g_in, g_norm, send_stat
            )
        )
        for at, value in enumerate(late_parts[1][:4]):
            late_rows[at] = jnp.broadcast_to(value, (24, VP))
        square[...] += jnp.broadcast_to(late_parts[1][-1], (8, 128))

    def stat_copy(step):
        target = (peer(step) // 2, lax.rem(peer(step), 2))
        return remote(stat, stat_got.at[me], table_send.at[3, step], table_recv.at[3, step], target)

    def send_stat(rows):
        line = iota((8, VP), 0)
        result = jnp.zeros((8, VP), F32)
        for at, row in enumerate(rows):
            result = jnp.where(line == at, row, result)
        stat[...] = result
        each(lambda step: stat_copy(step).start())
        stat_got[me] = stat[...]

    def table_last():
        each(lambda step: stat_copy(step).wait())
        totals = lax.fori_loop(1, 32, lambda at, held: held + stat_got[at], stat_got[0])
        mean_1, mean_2 = totals[0:1] * (1.0 / D), totals[1:2] * (1.0 / D)
        inner, unit, rstd, emb_grad = (late_rows[at] for at in range(4))
        g_emb[...] = emb_grad + rstd * (inner - mean_1 - unit * mean_2)
        first, second = rstd[0:1] * mean_1, rstd[0:1] * mean_2
        whole = totals[6:7] - 2.0 * (first * totals[2:3] + second * totals[3:4])
        whole = whole + first * first * D + 2.0 * first * second * totals[4:5] + second * second * totals[5:6]
        return total_of(whole)

    stages = (stage_first, stage_second, stage_along, stage_pair, stage_end, table_sum, table_end)
    pending = list(BACKWARD_ORDER)

    def hook():
        for stage, u in pending.pop(0):
            stages[stage](u)

    def done(u):
        if u == 0:
            pl.semaphore_wait(barrier, 31)
        twin_copy(u).start()
        hook()

    names = Kept._fields

    def phase_one(*early_refs):
        e = Early(*early_refs)
        left, right = slice(0, 1536), slice(1536, 3072)
        spare = len(SAVED) + count + 1
        load(AT.slope, saved.slope.at[:, left], e.slope.at[:, left])
        load(AT.active, saved.active.at[:, left], e.active.at[:, left])
        load(spare, saved.slope.at[:, right], e.slope.at[:, right])
        load(spare + 1, saved.active.at[:, right], e.active.at[:, right])
        load(weight(1), far[1], grads[1])
        for name in names:
            load(getattr(AT, name), getattr(saved, name), getattr(kept, name))
        for m in (2, 3):
            load(weight(m), far[m], grads[m])
        for name in Early._fields[2:6]:
            load(getattr(AT, name), getattr(saved, name), getattr(e, name))
        load(weight(4), far[4], grads[4])
        for name in Early._fields[6:8]:
            load(getattr(AT, name), getattr(saved, name), getattr(e, name))
        load(weight(5), far[5], grads[5])
        for name in Early._fields[8:]:
            load(getattr(AT, name), getattr(saved, name), getattr(e, name))
        load(weight(6), far[6], grads[6])
        view = [g.reshape(2, D, n) for g, n in zip(grads, widths)]
        need(AT.branch)
        transpose_into(branch, branch_t)
        hook()

        def grad_tile(m, start, left_t, right, half, at):
            lanes = slice(start + half * widths[m] + at, start + half * widths[m] + at + 384)
            view[m][half, :, at : at + 384] = nn(left_t[...], right[:, lanes]).astype(BF16)

        def grad_half(m, start, left_t, right, half):
            for at in range(0, widths[m], 384):
                grad_tile(m, start, left_t, right, half, at)

        for part in range(2):
            need(weight(part))
            need(*((AT.slope,) if part == 0 else (spare, spare + 1)))

            def down_back(half, at, part=part):
                lanes = slice(part * 1536 + half * 768 + at, part * 1536 + half * 768 + at + 384)
                back = nn(branch[...], view[part][half, :, at : at + 384])
                e.slope[:, lanes] = (back * e.slope[:, lanes].astype(F32)).astype(BF16)

            if part == 0:
                for at in (0, 384):
                    for half in range(2):
                        down_back(half, at)
                    hook()
                    if at == 0:
                        need(AT.active)
                    for half in range(2):
                        grad_tile(part, 0, branch_t, e.active, half, at)
                    done(at // 384)
            else:
                for half in range(2):
                    for at in (0, 384):
                        down_back(half, at)
                    hook()
                for at in (0, 384):
                    for half in range(2):
                        grad_tile(part, part * 1536, branch_t, e.active, half, at)
                    done(2 + at // 384)
        for part in range(2):
            need(weight(2 + part))
            for half in range(2):
                start = part * 1536 + half * 768
                back = nt(e.slope[:, start : start + 768], view[2 + part][half])
                upstream[...] = back if start == 0 else upstream[...] + back
                hook()
            if part == 0:
                need(AT.feed_normed_t)
            for at in (0, 384):
                for half in range(2):
                    grad_tile(2 + part, part * 1536, e.feed_normed_t, e.slope, half, at)
                done(4 + 2 * part + at // 384)
        need(*(getattr(AT, name) for name in names))
        norms = kept.norms[...]

        def gain(number):
            return norms[number : number + 1, :]

        need(AT.unit_2, AT.rstd_2)
        scale_2, shift_2 = back_rows(e.unit_2, e.rstd_2, gain(2), upstream, stream, branch, False)
        hook()
        need(weight(4), AT.col_mixed_t)
        mixed[...] = (nt(branch[:, :384], view[4][0]) + nt(branch[:, 384:], view[4][1])).astype(BF16)
        hook()
        for half in range(2):
            grad_half(4, 0, e.col_mixed_t, branch, half)
        done(8)
        need(AT.col_proj, AT.col_prob)
        proj = e.active

        def attend(at, carry):
            rows = pl.ds(pl.multiple_of((at // PAIRS) * 128, 128), 128)
            lane = lax.rem(at, PAIRS) * 128

            def lanes(part):
                return pl.ds(pl.multiple_of(part * D + lane, 128), 128)

            query = stacked(e.col_proj[rows, lanes(0)])
            key = e.col_proj[rows, lanes(1)]
            value = e.col_proj[rows, lanes(2)]
            above = stacked(mixed[rows, lanes(0)])
            prob = e.col_prob[at]
            grad = nt(above, value)
            grad = prob * (grad - jnp.sum(prob * grad, -1, keepdims=True))
            small = grad.astype(BF16)
            scale = HD ** (-0.5)
            proj[rows, lanes(0)] = (unstacked(nn(small, key), 128) * scale).astype(BF16)
            proj[rows, lanes(1)] = (tn(small, query) * scale).astype(BF16)
            proj[rows, lanes(2)] = tn(prob.astype(BF16), above).astype(BF16)
            return carry

        for part in range(6):
            lax.fori_loop(4 * part, 4 * part + 4, attend, 0, unroll=4)
            hook()
        need(weight(5))
        for half in range(2):
            back = nt(proj[:, half * 1152 : half * 1152 + 1152], view[5][half])
            upstream[...] = back if half == 0 else upstream[...] + back
            hook()
        need(AT.col_normed_t)
        for third in range(3):
            for half in range(2):
                grad_tile(5, 0, e.col_normed_t, proj, half, third * 384)
            done(9 + third)
        need(AT.unit_1, AT.rstd_1)
        scale_1, shift_1 = back_rows(e.unit_1, e.rstd_1, gain(1), upstream, stream, branch, False)
        hook()
        need(weight(6))
        mixed[...] = (nt(branch[:, :384], view[6][0]) + nt(branch[:, 384:], view[6][1])).astype(BF16)
        line = iota((8, D), 0)
        vectors = jnp.zeros((8, D), F32)
        moved = kept.moved[...]
        rows = (scale_1, scale_2, moved[0:1], shift_1, shift_2, moved[1:2])
        for number, row in enumerate(rows):
            vectors = jnp.where(line == number, row, vectors)
        extras = jnp.concatenate([kept.extras[0:1, :], jnp.zeros((1, D - 128), F32)], 1)
        kept.moved[...] = jnp.where(line == 6, extras, vectors)
        hook()

    pl.run_scoped(phase_one, *(pltpu.VMEM(*item) for item in pick_items(Early, SAVED)))

    def phase_two(*late_refs):
        e = Late(*late_refs[:-3])
        in_row, left_hi, left_lo = late_refs[-3:]
        for name in Late._fields:
            load(getattr(AT, name), getattr(saved, name), getattr(e, name))
        load(weight(count), in_row_far.at[0], in_row)
        view = grads[6].reshape(2, D, widths[6])
        late_parts.append(in_row)
        need(AT.row_mixed_t)
        for half in range(2):
            lanes = slice(half * 384, half * 384 + 384)
            view[half] = nn(e.row_mixed_t[...], branch[:, lanes]).astype(BF16)
        done(12)
        need(AT.hot_all, AT.weight_hi, AT.prob, AT.hot_ri, AT.hot_ir)
        shape = (HERE, HERE)
        back = (
            ((iota(shape, 1) >> 4) == (iota(shape, 0) & 31))
            & ((iota(shape, 1) & 15) == (iota(shape, 0) >> 5))
        )
        mixed[...] = nn(one_zero(back).astype(BF16), mixed[...]).astype(BF16)
        value_rows = []
        for hp in range(PAIRS):
            lanes = slice(hp * 128, hp * 128 + 128)
            part = mixed[:, lanes]
            upstream[:, lanes] = nt(part, kept.value_two[hp])
            value_rows.append(unstacked(tn(e.weight_hi[:, lanes], part), 64))
        hook()
        split_heads_to(upstream, left_hi, left_lo)
        hook()
        hot_all = e.hot_all[...]
        grad = nn(left_hi[...], hot_all) + nn(left_lo[...], hot_all)
        extra = jnp.concatenate(
            [kept.touch[...] * (contact_head[h] * COLS) for h in range(HEADS)], 0
        )
        grad = grad + extra
        prob = e.prob[...]
        grad = prob * (grad - jnp.sum(prob * grad, -1, keepdims=True))
        low_grad = grad.astype(BF16)
        hook()
        merge_heads(low_grad, e.hot_all, branch, None)
        hook()
        table_pair = nn(e.hot_ri[...], branch[...])
        stream_hi, stream_lo = split_two(stream[...])
        hot_ir = e.hot_ir[...]
        table_grad = kept.grad_head[...] + nn(hot_ir, stream_hi) + nn(hot_ir, stream_lo)
        value_grad = jnp.concatenate(value_rows, 1)
        last = jnp.where(iota((8, D), 0) == 7, table_grad[32:33], kept.moved[...])
        top, rest = split_two(last)
        groups = [table_pair[4:20], table_pair[20:36], value_grad[4:20], value_grad[20:36]]
        groups += [table_grad[0:16], table_grad[16:32]]
        groups += [jnp.concatenate([top.astype(F32), rest.astype(F32)], 0)]
        for number, group in enumerate(groups):
            for third in range(3):
                table[3 * number + third] = group[:, third * 256 : third * 256 + 256].astype(BF16)
        each(table_start)
        hook()
        hook()

    pl.run_scoped(
        phase_two,
        *(pltpu.VMEM(*item) for item in pick_items(Late, SAVED)),
        pltpu.VMEM((24, 3 * D), F32),
        pltpu.VMEM((HEADS * WIDE, ROWS * VP), BF16),
        pltpu.VMEM((HEADS * WIDE, ROWS * VP), BF16),
    )
    assert not pending

    def square_copy(step):
        other = lax.rem(me + step, 32)
        return remote(
            square, square_got.at[me], table_send.at[2, step], table_recv.at[2, step], (other // 2, lax.rem(other, 2))
        )

    each(lambda step: square_copy(step).start())
    square_got[me] = square[...]
    each(lambda step: table_wait_send(step))
    for u in range(units):
        for item in pair(u):
            item.wait_send()
    emb_square = table_last()
    each(lambda step: square_copy(step).wait())
    total_square = lax.fori_loop(1, 32, lambda at, held: held + square_got[at], square_got[0])[0:1]
    vector = table_out[18].astype(F32)
    vector = vector[6:7, :128] + vector[14:15, :128]
    counted = kept.extras[1:2, :]
    column = iota((1, 128), 1)
    contact = jnp.where(column <= HEADS, vector, 0.0)
    total_square = total_square + total_of(contact * contact) + emb_square
    grad_norm = jnp.sqrt(total_square)
    factor = jnp.minimum(1.0, MAX_NORM / grad_norm)
    losses = (
        (0, vector[:, HEADS + 1 : HEADS + 2]),
        (1, counted[:, 0:1]),
        (2, vector[:, HEADS + 2 : HEADS + 3]),
        (3, counted[:, 1:2]),
    )
    loss_row = jnp.zeros((1, 128), F32)
    for at, value in losses:
        loss_row = jnp.where(column == at, value, loss_row)
    number = iota((8, 128), 0)
    result = jnp.zeros((8, 128), F32)
    for at, row in enumerate((contact, counted, factor, grad_norm, loss_row)):
        result = jnp.where(number == at, row, result)
    stats[...] = result


def backward_call(contact_head, weights, in_row, saved):
    widths = GRAD_WIDTHS
    count = len(widths)
    inside = pl.BlockSpec(memory_space=pltpu.VMEM)
    anywhere = pl.BlockSpec(memory_space=pl.ANY)

    units = len(GRAD_UNITS)

    def shapes(lead, dtype, other=None):
        leads = [other if other and u in Z_FIRST else lead for u in range(units)]
        return [pltpu.VMEM((*at, n), dtype) for at, (_, _, n, _) in zip(leads, GRAD_UNITS)]

    outs = pl.pallas_call(
        backward_kernel,
        out_shape=[jax.ShapeDtypeStruct((2, 24, n), F32) for n in widths]
        + [
            jax.ShapeDtypeStruct((24, 3 * D), F32),
            jax.ShapeDtypeStruct((24, VP), F32),
            jax.ShapeDtypeStruct((8, 24), F32),
            jax.ShapeDtypeStruct((8, 128), F32),
        ],
        in_specs=[pl.BlockSpec(memory_space=pltpu.SMEM)] + [anywhere] * (1 + count + len(SAVED)),
        out_specs=[inside] * (4 + count),
        scratch_shapes=[pltpu.VMEM((2, NZ, NY, 2, 48, n), BF16) for n in widths]
        + [pltpu.VMEM(*item) for item in pick_items(Kept, SAVED)]
        + [
            pltpu.VMEM((HERE, D), F32),
            pltpu.VMEM((HERE, D), BF16),
            pltpu.VMEM((D, HERE), BF16),
            pltpu.VMEM((HERE, D), BF16),
        ]
        + [
            pltpu.VMEM((NZ, NY, 2, 48, n) if paired else (2, NZ, NY, 48, n), BF16)
            for _, _, n, paired in GRAD_UNITS
        ]
        + shapes((2, 2, 48), BF16, (3, 2, 2, 48))
        + shapes((2, 2, 48), BF16, (16,))
        + shapes((2, 48), BF16, (2, 48))
        + shapes((2, 48), BF16, (48,))
        + shapes((3, 48), BF16, (16,))
        + shapes((2, 24), F32)
        + shapes((24,), F32)
        + [
            pltpu.VMEM((PIECES, 16, 256), BF16),
            pltpu.VMEM((PIECES, 16, 256), BF16),
            pltpu.VMEM((32, 16, 256), BF16),
            pltpu.VMEM((8, 128), F32),
            pltpu.VMEM((32, 8, 128), F32),
            pltpu.VMEM((8, VP), F32),
            pltpu.VMEM((32, 8, VP), F32),
            pltpu.VMEM((4, 24, VP), F32),
            pltpu.SemaphoreType.DMA((4, 32)),
            pltpu.SemaphoreType.DMA((4, 32)),
            pltpu.SemaphoreType.DMA((units, 9)),
            pltpu.SemaphoreType.DMA((units, 9)),
            pltpu.SemaphoreType.DMA((len(SAVED) + count + 3,)),
        ],
        compiler_params=pltpu.CompilerParams(
            collective_id=1, has_side_effects=True, vmem_limit_bytes=63 * 2**20
        ),
    )(contact_head, *weights, in_row, *saved)
    return outs[:count], outs[count:]


UPDATE_RATES = (LEARN_RATE,) * 4 + (VECTOR_RATE,) * 3


def update_kernel(*refs):
    given, far, held, results = refs[:32], refs[32:60], refs[60:92], refs[92:120]
    sems, out_sems = refs[120:122]
    outs, copies = results[:21], results[21:26]
    loss_ref, norm_ref = results[26:]

    def leave(*numbers):
        for n in numbers:
            pltpu.make_async_copy(results[n], far[n], out_sems.at[n]).start()

    moves = [pltpu.make_async_copy(a, b, sems.at[n]) for n, (a, b) in enumerate(zip(given, held))]
    groups = (
        (10, 7, 5, 11, 12, 13),
        (4, 6, 14, 15, 16),
        (2, 3, 17, 18, 19),
        (0, 1, 20, 21, 22),
        (8, 9, *range(23, 32)),
    )
    for group in groups:
        for n in group:
            moves[n].start()

    def arrive(number):
        for n in groups[number]:
            moves[n].wait()

    reduced, g_in, g_emb, g_norm, stats = held[:7], held[7], held[8], held[9], held[10]
    states = [held[11 + 3 * n : 14 + 3 * n] for n in range(7)]
    outs = [outs[3 * n : 3 * n + 3] for n in range(7)]
    order = feature_order()
    arrive(0)
    factor = stats[2:3, 0:1]
    loss_ref[...] = stats[4:5, 0:4]
    norm_ref[...] = stats[3:4, 0:1]

    def natural(values):
        top, rest = split_two(values)
        last = (values - top.astype(F32) - rest.astype(F32)).astype(BF16)
        return nt(top, order) + nt(rest, order) + nt(last, order)

    def update(number, where, grad):
        master, first, second = (ref[where] for ref in states[number])
        new, first, second = adam_update(master, first, second, grad * factor, UPDATE_RATES[number])
        for ref, value in zip(outs[number], (new, first, second)):
            ref[where] = value
        if number < 5:
            copies[number][where] = new.astype(BF16)

    every = slice(None)
    g_out_col, g_in_col, g_out_row = reduced[4:]
    for half in range(2):
        lanes = slice(half * 1152, half * 1152 + 1152)
        update(0, (0, every, lanes), g_in[:, lanes])
        update(0, (1, every, lanes), g_in_col[half])
    leave(0, 1, 2, 21, 26, 27)
    arrive(1)
    for half in range(2):
        lanes = slice(half * 384, half * 384 + 384)
        update(1, (0, every, lanes), natural(g_out_row[half]))
        update(1, (1, every, lanes), natural(g_out_col[half]))
    leave(3, 4, 5, 22)
    for number, first in ((2, 2), (3, 0)):
        arrive(number)
        for half in range(2):
            for part in range(2):
                start = part * 1536 + half * 768
                lanes = slice(start, start + 768)
                update(number, (every, lanes), reduced[first + part][half])
        leave(*((6, 7, 8, 23) if number == 2 else (9, 10, 11, 24)))
    arrive(4)
    update(4, (every, every), g_emb[:, :VOCAB])
    update(5, (every, every), g_norm[...])
    update(6, (every, every), stats[0:1, : HEADS + 1])
    leave(12, 13, 14, 25, 15, 16, 17, 18, 19, 20)
    for n in range(28):
        pltpu.make_async_copy(results[n], far[n], out_sems.at[n]).wait()


def update_call(reduced, g_in, g_emb, g_norm, stats, states):
    anywhere = pl.BlockSpec(memory_space=pl.ANY)
    flat = [item for state in states for item in state]
    shapes = [jax.ShapeDtypeStruct(item.shape, F32) for item in flat]
    shapes += [jax.ShapeDtypeStruct(states[n][0].shape, BF16) for n in range(5)]
    shapes += [jax.ShapeDtypeStruct((1, 4), F32), jax.ShapeDtypeStruct((1, 1), F32)]
    given = (*reduced, g_in, g_emb, g_norm, stats, *flat)
    return pl.pallas_call(
        update_kernel,
        out_shape=shapes,
        in_specs=[anywhere] * len(given),
        out_specs=[anywhere] * len(shapes),
        scratch_shapes=[pltpu.VMEM(item.shape, F32) for item in given]
        + [pltpu.VMEM(item.shape, item.dtype) for item in shapes]
        + [
            pltpu.SemaphoreType.DMA((len(given),)),
            pltpu.SemaphoreType.DMA((len(shapes),)),
            pltpu.VMEM((44, 512, 512), F32),
        ],
        compiler_params=pltpu.CompilerParams(vmem_limit_bytes=62 * 2**20),
    )(*given)


def adam_update(master, first, second, grad_part, rate):
    first = BETA_ONE * first + (1.0 - BETA_ONE) * grad_part
    second = BETA_TWO * second + (1.0 - BETA_TWO) * grad_part * grad_part
    scaled = first * (1.0 / (1.0 - BETA_ONE**STEP))
    moved = scaled / (jnp.sqrt(second * (1.0 / (1.0 - BETA_TWO**STEP))) + ADAM_EPS)
    return (master - rate * (moved + WEIGHT_DECAY * master), first, second)


def shards(
    tokens,
    targets,
    masked,
    contact_pairs,
    labels,
    attention_in_master,
    attention_in_first,
    attention_in_second,
    attention_out_master,
    attention_out_first,
    attention_out_second,
    feed_up_master,
    feed_up_first,
    feed_up_second,
    feed_down_master,
    feed_down_first,
    feed_down_second,
    embedding_master,
    embedding_first,
    embedding_second,
    norm_params_master,
    norm_params_first,
    norm_params_second,
    contact_head_master,
    contact_head_first,
    contact_head_second,
):
    both = ("seq", "col")
    micro, rows_here, cols_here = tokens.shape
    ncol = lax.axis_size("col")
    ndev = lax.axis_size("seq") * ncol
    cols = cols_here * ncol
    me = lax.axis_index("seq") * ncol + lax.axis_index("col")
    per = ndev // micro
    cw = cols // per
    mine = me // per
    base = (me % per) * cw
    shard = D // ndev

    tiled = lax.axis_size("seq") == 16 and ncol == 2
    if tiled:
        raw = (
            tokens,
            targets,
            masked,
            contact_pairs.transpose(0, 2, 1),
            labels,
            embedding_master.T,
            norm_params_master,
            attention_in_master,
            attention_out_master,
            feed_up_master,
            feed_down_master.T,
        )
        weights, saved = forward_call(raw, contact_head_master)
        reduced, (g_in, g_emb, g_norm, stats) = backward_call(
            contact_head_master, [weights[n] for n in (5, 6, 3, 4, 2, 1, 0)], attention_in_master, saved
        )
        states = (
            (attention_in_master, attention_in_first, attention_in_second),
            (attention_out_master, attention_out_first, attention_out_second),
            (feed_up_master, feed_up_first, feed_up_second),
            (feed_down_master.T, feed_down_first.T, feed_down_second.T),
            (embedding_master.T, embedding_first.T, embedding_second.T),
            (norm_params_master, norm_params_first, norm_params_second),
            (contact_head_master[None], contact_head_first[None], contact_head_second[None]),
        )
        outs = update_call(reduced, g_in, g_emb, g_norm, stats, states)
        return (
            *outs[:9],
            *(item.T for item in outs[9:15]),
            *outs[15:18],
            *(item[0] for item in outs[18:21]),
            *outs[21:24],
            *(item.T for item in outs[24:26]),
            outs[26][0],
            outs[27][0, 0],
        )
    inputs = jnp.where(masked > 0, MASK_ID, tokens)
    masters = [
        jnp.concatenate(
            [
                jnp.pad(embedding_master.T, ((0, 0), (0, 128 - VOCAB))),
                jnp.pad(norm_params_master.T, ((0, 0), (0, 120))),
            ],
            1,
        ),
        attention_in_master[0],
        attention_out_master[0],
        attention_in_master[1],
        attention_out_master[1],
        feed_up_master,
        feed_down_master.T,
    ]
    whole = jnp.stack([inputs, targets])
    whole = lax.all_gather(lax.all_gather(whole, "col", axis=3, tiled=True), "seq", axis=2, tiled=True)
    pairs_all = lax.all_gather(
        jnp.concatenate([contact_pairs, labels[:, :, None]], -1), both, axis=1, tiled=True
    )
    gathered = []
    for master in masters:
        full = lax.all_gather(master.astype(BF16), both, axis=0, tiled=True)
        gathered.append(full.reshape(D, 2, -1).transpose(1, 0, 2))
    counts = (
        jnp.sum(whole[0] == MASK_ID).astype(F32),
        jnp.sum(pairs_all[..., 2] >= 0).astype(F32),
    )
    ids_all = lax.dynamic_index_in_dim(whole[0], mine, 0, False)
    ids_local = lax.dynamic_slice_in_dim(ids_all, base, cw, 1)
    targets_local = lax.dynamic_slice_in_dim(
        lax.dynamic_index_in_dim(whole[1], mine, 0, False), base, cw, 1
    )
    pairs = lax.dynamic_index_in_dim(pairs_all, mine, 0, False)

    table = gathered[0][0][:, :VP].T
    norms = gathered[0][1][:, :8].T.astype(F32)
    in_row, out_row, in_col, out_col, up_w, down_t = (
        jnp.concatenate([g[0], g[1]], 1) for g in gathered[1:]
    )
    big = (in_row, in_col, out_row, out_col, up_w, down_t)

    grads, tables, contact_total, mlm_total, bce_total, kept = step(
        big,
        table,
        norms,
        contact_head_master,
        ids_all,
        ids_local.reshape(-1),
        ids_local.T.reshape(-1),
        targets_local.T.reshape(-1),
        pairs[:, 0] - base,
        pairs[:, 1],
        pairs[:, 2],
        counts,
        cw,
    )
    table_pair, value_grad, table_grad, vectors = tables
    extras = jnp.zeros((2, D), F32).at[0, : HEADS + 3].set(
        jnp.concatenate([contact_total, mlm_total[None], bce_total[None]])
    )
    sums = jnp.concatenate([table_pair[:40], value_grad[:40], table_grad[:40], vectors, extras])
    flat_grad = jnp.concatenate([g.astype(BF16) for g in grads], 1)
    reduced = lax.psum_scatter(flat_grad, both, scatter_dimension=0, tiled=True).astype(F32)
    g_in_col, g_out_row, g_out_col, g_up, g_down = jnp.split(
        reduced, [3 * D, 4 * D, 5 * D, 5 * D + FF], 1
    )
    sums = lax.psum(sums, both)
    unit_t, rstd_t, normed_t, query_t, key_t = kept
    rows_all = ids_all.shape[0]
    spare = ((0, VP - 40), (0, 0))
    table_pair, value_grad, table_grad = (
        jnp.pad(sums[a : a + 40], spare) for a in (0, 40, 80)
    )
    vectors = sums[120:126]
    contact_grad, mlm_total, bce_total = (
        sums[126, : HEADS + 1], sums[126, HEADS + 1], sums[126, HEADS + 2]
    )
    row_scale = (HD * rows_all) ** (-0.5)
    query_grad = []
    key_grad = []
    for h in range(HEADS):
        pair = heads_of(table_pair, h)
        query_grad.append(jnp.dot(pair, heads_of(key_t, h).astype(F32), precision=PRECISE))
        key_grad.append(jnp.dot(pair.T, heads_of(query_t, h).astype(F32), precision=PRECISE))
    proj_grad = jnp.concatenate(
        [
            jnp.concatenate(query_grad, 1) * row_scale,
            jnp.concatenate(key_grad, 1) * row_scale,
            value_grad,
        ],
        1,
    )
    proj_hi, proj_lo = split_two(proj_grad)
    normed_grad = nt(proj_hi, in_row) + nt(proj_lo, in_row)
    back_t, scale_0, shift_0 = norm_back(unit_t, rstd_t, norms[0], normed_grad)
    table_grad = table_grad + back_t
    low = me * shard
    normed_mine = lax.dynamic_slice_in_dim(normed_t, low, shard, 1)
    grad_in_row = tn(normed_mine, proj_hi) + tn(normed_mine, proj_lo)
    norm_grad = jnp.concatenate([scale_0[None], vectors[:3], shift_0[None], vectors[3:]])
    table_mine = lax.dynamic_slice_in_dim(table_grad[:VOCAB], low, shard, 1)
    norm_mine = lax.dynamic_slice_in_dim(norm_grad, low, shard, 1)
    reduced_all = (g_in_col, g_out_row, g_out_col, g_up, g_down)

    local_square = (
        sum(jnp.sum(g * g) for g in reduced_all)
        + jnp.sum(grad_in_row * grad_in_row)
        + jnp.sum(table_mine * table_mine)
        + jnp.sum(norm_mine * norm_mine)
    )
    square = lax.psum(local_square, both) + jnp.sum(contact_grad * contact_grad)
    grad_norm = jnp.sqrt(square)
    factor = jnp.minimum(1.0, MAX_NORM / grad_norm)
    in_new, in_moment, in_square = adam_update(
        attention_in_master, attention_in_first, attention_in_second, jnp.stack([grad_in_row, g_in_col]) * factor, LEARN_RATE
    )
    out_new, out_moment, out_square = adam_update(
        attention_out_master, attention_out_first, attention_out_second, jnp.stack([g_out_row, g_out_col]) * factor, LEARN_RATE
    )
    up_new, up_moment, up_square = adam_update(
        feed_up_master, feed_up_first, feed_up_second, g_up * factor, LEARN_RATE
    )
    down_new, down_moment, down_square = adam_update(
        feed_down_master, feed_down_first, feed_down_second, g_down.T * factor, LEARN_RATE
    )
    table_new, table_moment, table_square = adam_update(
        embedding_master, embedding_first, embedding_second, table_mine * factor, VECTOR_RATE
    )
    norm_new, norm_moment, norm_square = adam_update(
        norm_params_master, norm_params_first, norm_params_second, norm_mine * factor, VECTOR_RATE
    )
    head_new, head_moment, head_square = adam_update(
        contact_head_master, contact_head_first, contact_head_second, contact_grad * factor, VECTOR_RATE
    )
    loss_parts = jnp.stack([mlm_total, counts[0], bce_total, counts[1]])
    return (
        in_new, in_moment, in_square,
        out_new, out_moment, out_square,
        up_new, up_moment, up_square,
        down_new, down_moment, down_square,
        table_new, table_moment, table_square,
        norm_new, norm_moment, norm_square,
        head_new, head_moment, head_square,
        in_new.astype(BF16), out_new.astype(BF16), up_new.astype(BF16), down_new.astype(BF16), table_new.astype(BF16),
        loss_parts, grad_norm,
    )


def solution(mesh):
    both = ("seq", "col")
    cells = P(None, "seq", "col")
    stack = P(None, both, None)
    row_split = P(both, None)
    col_split = P(None, both)
    weights = [stack] * 6 + [row_split] * 3 + [col_split] * 9 + [P()] * 3
    return jax.shard_map(
        shards,
        mesh=mesh,
        in_specs=(cells, cells, cells, stack, col_split, *weights),
        out_specs=(*weights, stack, stack, row_split, col_split, col_split, P(), P()),
        check_vma=False,
    )
```

```python
import typing

import jax
import jax.numpy as jnp
from jax import lax
from jax.experimental import pallas as pl
from jax.experimental.pallas import tpu as pltpu
from jax.sharding import PartitionSpec as P

D = 768
HEADS = 12
HD = 64
FF = 3072
VOCAB = 33
VP = 64
STEP = 10

NORM_EPS = 1e-05
MASK_ID = 32
MAX_NORM = 0.001
LEARN_RATE = 0.05
VECTOR_RATE = 0.5
BETA_ONE = 0.9
BETA_TWO = 0.95
ADAM_EPS = 1e-08
WEIGHT_DECAY = 0.01
PRECISE = lax.Precision.HIGHEST
F32 = jnp.float32
BF16 = jnp.bfloat16


def nn(left, right):
    return lax.dot_general(left, right, (((1,), (0,)), ((), ())), preferred_element_type=F32)


def tn(left, right):
    return lax.dot_general(left, right, (((0,), (0,)), ((), ())), preferred_element_type=F32)


def nt(left, right):
    return lax.dot_general(left, right, (((1,), (1,)), ((), ())), preferred_element_type=F32)


def split_two(values):
    high = values.astype(BF16)
    return high, (values - high.astype(F32)).astype(BF16)


def norm_stats(values):
    centre = values - jnp.mean(values, -1, keepdims=True)
    rstd = lax.rsqrt(jnp.mean(centre * centre, -1, keepdims=True) + NORM_EPS)
    return centre * rstd, rstd


def norm_back(unit, rstd, scale_vec, upstream):
    inner = upstream * scale_vec
    grad = rstd * (
        inner - jnp.mean(inner, -1, keepdims=True) - unit * jnp.mean(inner * unit, -1, keepdims=True)
    )
    return grad, jnp.sum(upstream * unit, 0), jnp.sum(upstream, 0)


GELU_K = 0.7978845608028654
GELU_C = 0.044715


def gelu_parts(up):
    square = up * up
    bent = jnp.tanh(GELU_K * up * (1.0 + GELU_C * square))
    half = 0.5 * (1.0 + bent)
    slope = half + 0.5 * up * (1.0 - bent * bent) * GELU_K * (1.0 + 3.0 * GELU_C * square)
    return up * half, slope


def heads_of(block, head):
    return block[:, head * HD : (head + 1) * HD]


def step(big, table, norms, contact_head, ids_all, ids_ri, ids_ir, targets_ir, pair_first, pair_second, labels, counts, cw):
    in_row, in_col, out_row, out_col, up_w, down_t = big
    rows, cols = ids_all.shape
    here = rows * cw
    row_scale = (HD * rows) ** (-0.5)
    vocab = jnp.arange(VP)[:, None]
    hot_all = (ids_all[:, None, :] == vocab[None]).astype(BF16).reshape(rows * VP, cols)
    hot_ri = (ids_ri[None, :] == vocab).astype(BF16)
    hot_ir = (ids_ir[None, :] == vocab).astype(BF16)
    spot = jnp.arange(here)
    perm = (
        ((spot // rows)[:, None] == (spot % cw)[None, :])
        & ((spot % rows)[:, None] == (spot // cw)[None, :])
    ).astype(BF16)

    def to_heads(block):
        return block.reshape(rows, cw, HEADS, VP).transpose(2, 1, 0, 3).reshape(HEADS * cw, rows * VP)

    def to_tokens(block):
        return block.reshape(HEADS, cw, rows, VP).transpose(2, 1, 0, 3).reshape(here, HEADS * VP)

    def per_head(block, other, how):
        return jnp.concatenate(
            [how(heads_of(block, h), heads_of(other, h)) for h in range(HEADS)], -1
        )

    table_f = table.astype(F32)
    unit_t, rstd_t = norm_stats(table_f)
    normed_t = (unit_t * norms[0] + norms[4]).astype(BF16)
    proj_t = nn(normed_t, in_row).astype(BF16)
    query_t, key_t, value_t = proj_t[:, :D], proj_t[:, D : 2 * D], proj_t[:, 2 * D :]

    pair_t = per_head(query_t, key_t, nt)
    pair_hi, pair_lo = split_two(pair_t)
    left_hi = to_heads(tn(hot_ri, pair_hi).astype(BF16))
    left_lo = to_heads(tn(hot_ri, pair_lo).astype(BF16))
    score = (nn(left_hi, hot_all) + nn(left_lo, hot_all)) * row_scale
    prob = jax.nn.softmax(score, axis=-1)
    prob_low = prob.astype(BF16)
    weight_t = to_tokens(nt(prob_low, hot_all))
    weight_hi, weight_lo = split_two(weight_t)
    row_mixed_ri = (
        per_head(weight_hi, value_t, nn) + per_head(weight_lo, value_t, nn)
    ).astype(BF16)
    row_mixed = nn(perm, row_mixed_ri).astype(BF16)
    embedded = tn(hot_ir, table)
    after_row = embedded + nn(row_mixed, out_row)

    prob_cube = prob_low.astype(F32).reshape(HEADS, cw, cols)
    head_sum = jnp.sum(prob_cube * contact_head[:HEADS, None, None], 0)
    first_hot = (pair_first[None, :] == jnp.arange(cw)[:, None]).astype(F32)
    second_hot = (pair_second[None, :] == jnp.arange(cols)[:, None]).astype(BF16)
    sum_hi, sum_lo = split_two(head_sum)
    sum_last = (head_sum - sum_hi.astype(F32) - sum_lo.astype(F32)).astype(BF16)
    picked = nn(sum_hi, second_hot) + nn(sum_lo, second_hot) + nn(sum_last, second_hot)
    contact_logit = jnp.sum(picked * first_hot, 0) * cols + contact_head[HEADS]
    owned = jnp.sum(first_hot, 0) > 0
    valid = (labels >= 0) & owned
    positive = (labels == 1).astype(F32)
    bce_sum = jnp.sum(
        jnp.where(valid, jax.nn.softplus(contact_logit) - positive * contact_logit, 0.0)
    )
    coef = jnp.where(valid, jax.nn.sigmoid(contact_logit) - positive, 0.0) / counts[1]
    coef_hi, coef_lo = split_two(coef)
    first_low = first_hot.astype(BF16)
    touch = nt(first_low * coef_hi[None], second_hot) + nt(first_low * coef_lo[None], second_hot)
    grad_contact = jnp.concatenate(
        [jnp.sum(prob_cube * touch[None], (1, 2)) * cols, jnp.sum(coef)[None]]
    )

    unit_1, rstd_1 = norm_stats(after_row)
    col_normed = (unit_1 * norms[1] + norms[5]).astype(BF16)
    col_proj = nn(col_normed, in_col).astype(BF16)
    group = 128 if here % 128 == 0 and 128 % rows == 0 else here
    groups = here // group
    lane = jnp.arange(group)
    same = (lane[:, None] // rows) == (lane[None, :] // rows)

    def cut(block):
        return block.reshape(groups, group, HEADS, HD)

    col_query, col_key, col_value = (cut(col_proj[:, k * D : (k + 1) * D]) for k in range(3))
    col_score = jnp.einsum("gqhe,gkhe->ghqk", col_query, col_key, preferred_element_type=F32) * HD ** (-0.5)
    col_prob = jax.nn.softmax(jnp.where(same, col_score, -1e30), axis=-1)
    col_prob_low = col_prob.astype(BF16)
    col_mixed = (
        jnp.einsum("ghqk,gkhe->gqhe", col_prob_low, col_value, preferred_element_type=F32)
        .astype(BF16)
        .reshape(here, D)
    )
    after_col = after_row + nn(col_mixed, out_col)

    unit_2, rstd_2 = norm_stats(after_col)
    feed_normed = (unit_2 * norms[2] + norms[6]).astype(BF16)
    hidden_up = nn(feed_normed, up_w)
    active, slope = gelu_parts(hidden_up)
    active = active.astype(BF16)
    after_feed = after_col + nt(active, down_t)
    unit_3, rstd_3 = norm_stats(after_feed)
    head_normed = (unit_3 * norms[3] + norms[7]).astype(BF16)
    logits = nt(table, head_normed) * D ** (-0.5)
    logits = jnp.where(vocab < VOCAB, logits, -1e30)
    top = jnp.max(logits, 0, keepdims=True)
    shifted = logits - top
    log_probs = shifted - jnp.log(jnp.sum(jnp.exp(shifted), 0, keepdims=True))
    target_hot = (targets_ir[None, :] == vocab).astype(F32)
    keep = ids_ir[None, :] == MASK_ID
    mlm_sum = -jnp.sum(jnp.where(keep & (target_hot > 0), log_probs, 0.0))
    logit_grad = jnp.where(keep, jnp.exp(log_probs) - target_hot, 0.0) / counts[0]
    logit_low = (logit_grad * D ** (-0.5)).astype(BF16)

    grad_head = nn(logit_low, head_normed)
    stream, scale_3, shift_3 = norm_back(unit_3, rstd_3, norms[3], tn(logit_low, table))
    branch = stream.astype(BF16)
    grad_down = tn(branch, active)
    up_low = (nn(branch, down_t) * slope).astype(BF16)
    grad_up = tn(feed_normed, up_low)
    inner, scale_2, shift_2 = norm_back(unit_2, rstd_2, norms[2], nt(up_low, up_w))
    stream = stream + inner
    branch = stream.astype(BF16)
    grad_out_col = tn(col_mixed, branch)
    mixed_low = nt(branch, out_col).astype(BF16)
    mixed_cut = cut(mixed_low)
    prob_grad = jnp.einsum("gqhe,gkhe->ghqk", mixed_cut, col_value, preferred_element_type=F32)
    score_grad = col_prob * (prob_grad - jnp.sum(col_prob * prob_grad, -1, keepdims=True))
    score_low = score_grad.astype(BF16)
    grad_q = jnp.einsum("ghqk,gkhe->gqhe", score_low, col_key, preferred_element_type=F32)
    grad_k = jnp.einsum("ghqk,gqhe->gkhe", score_low, col_query, preferred_element_type=F32)
    grad_v = jnp.einsum("ghqk,gqhe->gkhe", col_prob_low, mixed_cut, preferred_element_type=F32)
    proj_low = jnp.concatenate(
        [
            (grad_q * HD ** (-0.5)).reshape(here, D),
            (grad_k * HD ** (-0.5)).reshape(here, D),
            grad_v.reshape(here, D),
        ],
        -1,
    ).astype(BF16)
    grad_in_col = tn(col_normed, proj_low)
    inner, scale_1, shift_1 = norm_back(unit_1, rstd_1, norms[1], nt(proj_low, in_col))
    stream = stream + inner
    branch = stream.astype(BF16)
    grad_out_row = tn(row_mixed, branch)
    mixed_low = nt(branch, out_row).astype(BF16)
    mixed_ri = tn(perm, mixed_low).astype(BF16)
    drive_hi, drive_lo = split_two(per_head(mixed_ri, value_t, nt))
    prob_grad = nn(to_heads(drive_hi), hot_all) + nn(to_heads(drive_lo), hot_all)
    prob_grad = prob_grad + (
        touch[None] * (contact_head[:HEADS, None, None] * cols)
    ).reshape(HEADS * cw, cols)
    score_grad = prob * (prob_grad - jnp.sum(prob * prob_grad, -1, keepdims=True))
    score_low = score_grad.astype(BF16)
    spread = to_tokens(nt(score_low, hot_all)).astype(BF16)
    table_pair = nn(hot_ri, spread)
    value_grad = per_head(weight_hi, mixed_ri, tn)
    stream_hi, stream_lo = split_two(stream)
    lookup_grad = nn(hot_ir, stream_hi) + nn(hot_ir, stream_lo)
    vectors = jnp.stack([scale_1, scale_2, scale_3, shift_1, shift_2, shift_3])
    return (
        (grad_in_col, grad_out_row, grad_out_col, grad_up, grad_down),
        (table_pair, value_grad, grad_head + lookup_grad, vectors),
        grad_contact,
        mlm_sum,
        bce_sum,
        (unit_t, rstd_t, normed_t, query_t, key_t),
    )


MESH = pl.DeviceIdType.MESH
NZ, NY = 4, 2


def place():
    s, c = lax.axis_index("seq"), lax.axis_index("col")
    z, y, k = s // 4, lax.rem(s // 2, 2), lax.rem(s, 2)
    return z, y, k, c


def device(z, y, k, c):
    return (z * 4 + y * 2 + k, c)


def greet_all():
    z, y, k, c = place()
    me = (z * 4 + y * 2 + k) * 2 + c
    barrier = pltpu.get_barrier_semaphore()

    def signal(step, carry):
        other = lax.rem(me + step, 32)
        pl.semaphore_signal(
            barrier, inc=1, device_id=(other // 2, lax.rem(other, 2)), device_id_type=MESH
        )
        return carry

    lax.fori_loop(1, 32, signal, 0)
    return barrier


def remote(src, dst, send, recv, target):
    return pltpu.make_async_remote_copy(
        src_ref=src, dst_ref=dst, send_sem=send, recv_sem=recv, device_id=target, device_id_type=MESH
    )


ROWS, COLS, WIDE, HERE = 16, 512, 32, 512
PAIRS = 6
SLOTS = 1024
UP_TILE = 384


def iota(shape, dim):
    return lax.broadcasted_iota(jnp.int32, shape, dim)


def one_zero(test):
    return jnp.where(test, 1.0, 0.0)


def total_of(values):
    return jnp.sum(jnp.sum(values, 0, keepdims=True), 1, keepdims=True)


def half_lanes(values, side):
    lane = iota(values.shape, len(values.shape) - 1)
    keep = (lane < 64) if side == 0 else (lane >= 64)
    return jnp.where(keep, values.astype(F32), 0.0).astype(BF16)


def stacked(values):
    return jnp.concatenate([half_lanes(values, 0), half_lanes(values, 1)], 0)


def unstacked(values, count):
    lane = iota((count, 128), 1)
    return jnp.where(lane < 64, values[:count], values[count:])


def swap_blocks(first, second):
    lane = iota(first.shape, 1)
    low = jnp.where(lane < 64, first, pltpu.roll(second, 64, 1))
    high = jnp.where(lane < 64, pltpu.roll(first, 64, 1), second)
    return low, high


def split_heads_to(source, high_ref, low_ref):
    for rp in range(ROWS // 2):
        for hp in range(PAIRS):
            lanes = slice(hp * 128, hp * 128 + 128)
            first = source[rp * 64 : rp * 64 + 32, lanes]
            second = source[rp * 64 + 32 : rp * 64 + 64, lanes]
            for side, block in enumerate(swap_blocks(first, second)):
                top, rest = split_two(block)
                rows = slice((2 * hp + side) * 32, (2 * hp + side) * 32 + 32)
                high_ref[rows, rp * 128 : rp * 128 + 128] = top
                low_ref[rows, rp * 128 : rp * 128 + 128] = rest


def merge_heads(probs, hot_all, high_ref, low_ref):
    for rp in range(ROWS // 2):
        if rp % 2 == 0:
            blocks = nt(probs, hot_all[rp * 128 : rp * 128 + 256, :])
        block = blocks[:, (rp % 2) * 128 : (rp % 2) * 128 + 128]
        for hp in range(PAIRS):
            first = block[hp * 64 : hp * 64 + 32]
            second = block[hp * 64 + 32 : hp * 64 + 64]
            for side, part in enumerate(swap_blocks(first, second)):
                top, rest = split_two(part)
                rows = slice(rp * 64 + side * 32, rp * 64 + side * 32 + 32)
                high_ref[rows, hp * 128 : hp * 128 + 128] = top
                if low_ref is not None:
                    low_ref[rows, hp * 128 : hp * 128 + 128] = rest


def norm_rows(source, gain, bias, unit_ref, rstd_ref, normed_ref):
    def body(at, carry):
        rows = pl.ds(pl.multiple_of(at * 64, 64), 64)
        values = source[rows, :]
        centre = values - jnp.sum(values, -1, keepdims=True) * (1.0 / D)
        rstd = lax.rsqrt(jnp.sum(centre * centre, -1, keepdims=True) * (1.0 / D) + NORM_EPS)
        unit = centre * rstd
        unit_ref[rows, :] = unit
        rstd_ref[rows, :] = jnp.broadcast_to(rstd, (64, 128))
        normed_ref[rows, :] = (unit * gain + bias).astype(BF16)
        return carry

    lax.fori_loop(0, HERE // 64, body, 0, unroll=2)


def transpose_into(source, target):
    def body(at, carry):
        rows = pl.ds(pl.multiple_of(at * 128, 128), 128)
        target[:, rows] = source[rows, :].astype(F32).T.astype(BF16)
        return carry

    lax.fori_loop(0, HERE // 128, body, 0)


def over_tiles(width, tile, body):
    for half in range(2):

        def step(at, carry, half=half):
            body(half, pl.multiple_of(at * tile, tile))
            return carry

        lax.fori_loop(0, width // tile, step, 0)


def column_mask():
    rows, lanes = iota((256, 128), 0), iota((256, 128), 1)
    return ((rows & 127) >> 4) == (lanes >> 4)


class Saved(typing.NamedTuple):
    stream: typing.Any
    branch: typing.Any
    unit_1: typing.Any
    unit_2: typing.Any
    rstd_1: typing.Any
    rstd_2: typing.Any
    row_mixed_t: typing.Any
    col_normed_t: typing.Any
    col_mixed_t: typing.Any
    feed_normed_t: typing.Any
    col_proj: typing.Any
    col_prob: typing.Any
    active: typing.Any
    slope: typing.Any
    grad_head: typing.Any
    hot_all: typing.Any
    hot_ri: typing.Any
    hot_ir: typing.Any
    prob: typing.Any
    weight_hi: typing.Any
    value_two: typing.Any
    touch: typing.Any
    table: typing.Any
    norms: typing.Any
    proj_t: typing.Any
    extras: typing.Any
    moved: typing.Any


AT = Saved(*range(len(Saved._fields)))
SAVED = Saved(
    stream=((HERE, D), F32),
    branch=((HERE, D), BF16),
    unit_1=((HERE, D), F32),
    unit_2=((HERE, D), F32),
    rstd_1=((HERE, 128), F32),
    rstd_2=((HERE, 128), F32),
    row_mixed_t=((D, HERE), BF16),
    col_normed_t=((D, HERE), BF16),
    col_mixed_t=((D, HERE), BF16),
    feed_normed_t=((D, HERE), BF16),
    col_proj=((HERE, 3 * D), BF16),
    col_prob=((4 * PAIRS, 256, 128), F32),
    active=((HERE, FF), BF16),
    slope=((HERE, FF), BF16),
    grad_head=((VP, D), F32),
    hot_all=((ROWS * VP, COLS), BF16),
    hot_ri=((VP, HERE), BF16),
    hot_ir=((VP, HERE), BF16),
    prob=((HEADS * WIDE, COLS), F32),
    weight_hi=((HERE, D), BF16),
    value_two=((PAIRS, 128, 128), BF16),
    touch=((WIDE, COLS), F32),
    table=((VP, D), F32),
    norms=((8, D), F32),
    proj_t=((VP, 3 * D), BF16),
    extras=((8, 128), F32),
    moved=((8, D), F32),
)


class Forward(typing.NamedTuple):
    ids: typing.Any
    targets: typing.Any
    slots: typing.Any
    normed: typing.Any
    mixed: typing.Any
    normed_2: typing.Any
    mixed_2: typing.Any
    second_hot: typing.Any
    weight_lo: typing.Any
    left_hi: typing.Any
    left_lo: typing.Any
    lookup: typing.Any
    prob_low: typing.Any
    unit: typing.Any
    rstd: typing.Any


FORWARD = Forward(
    ids=((ROWS, COLS), jnp.int32),
    targets=((ROWS, 128), jnp.int32),
    slots=((8, SLOTS), jnp.int32),
    normed=((HERE, D), BF16),
    mixed=((HERE, D), BF16),
    normed_2=((HERE, D), BF16),
    mixed_2=((HERE, D), BF16),
    second_hot=((COLS, SLOTS), BF16),
    weight_lo=((HERE, D), BF16),
    left_hi=((HEADS * WIDE, ROWS * VP), BF16),
    left_lo=((HEADS * WIDE, ROWS * VP), BF16),
    lookup=((HERE, D), F32),
    prob_low=((HEADS * WIDE, COLS), BF16),
    unit=((HERE, D), F32),
    rstd=((HERE, 128), F32),
)


def position():
    z, y, k, c = place()
    me = (z * 4 + y * 2 + k) * 2 + c
    return z // 2, lax.rem(me, 16)


def read_tokens(small, f):
    alignment, block = position()
    side, part = block // 8, lax.rem(block // 4, 2)
    for r in range(ROWS):
        for cc in range(2):
            for q in range(2):
                lanes = slice(cc * 256 + q * 128, cc * 256 + q * 128 + 128)
                f.ids[r : r + 1, lanes] = small[r * 2 + cc, pl.ds(2 * alignment + q, 1), :]
        f.targets[r : r + 1, :] = small[r * 2 + side, pl.ds(4 + 2 * alignment + part, 1), :]
    lane = iota((1, 128), 1)
    for number in range(SLOTS // 128):
        for which in range(3):
            row = pl.ds(8 + 3 * alignment + which, 1)
            first = small[number * 4 + side, row, :]
            second = pltpu.roll(small[number * 4 + 2 + side, row, :], 64, 1)
            f.slots[which : which + 1, number * 128 : number * 128 + 128] = jnp.where(
                lane < 64, first, second
            )


def local_hot(values, shift):
    values = pltpu.roll(values, shift, 1)
    turned = [values] + [pltpu.roll(values, 32 * n, 1) for n in (1, 2, 3)]
    lane = iota((1, 128), 1)
    tiles = []
    for tile in range(4):
        row = turned[3][4 * tile + 3 : 4 * tile + 4]
        for n in (2, 1, 0):
            row = jnp.where(lane < 32 * n + 32, turned[n][4 * tile + n : 4 * tile + n + 1], row)
        tiles.append(row)
    row = jnp.concatenate(tiles, 1)
    return one_zero(row == iota((VP, HERE), 0)).astype(BF16)


def contact_part(contact_head, f, s, pair_count):
    _, block = position()
    base = block * WIDE
    head_sum = jnp.zeros((WIDE, COLS), F32)
    for h in range(HEADS):
        head_sum = head_sum + contact_head[h] * f.prob_low[h * 32 : h * 32 + 32, :].astype(F32)
    top, rest = split_two(head_sum)
    last = (head_sum - top.astype(F32) - rest.astype(F32)).astype(BF16)
    parts = jnp.concatenate([top, rest, last], 0)
    touch = jnp.zeros((WIDE, COLS), F32)
    bce = jnp.zeros((1, 1), F32)
    coef_sum = jnp.zeros((1, 1), F32)
    for number in range(SLOTS // 512):
        lanes = slice(number * 512, number * 512 + 512)
        first, label = (f.slots[n : n + 1, lanes] for n in (0, 2))
        second_hot = f.second_hot[:, lanes]
        picked = nn(parts, second_hot)
        picked = picked[:32] + picked[32:64] + picked[64:]
        first_hot = one_zero((first - base) == iota((WIDE, 512), 0))
        logit = jnp.sum(picked * first_hot, 0, keepdims=True) * COLS + contact_head[HEADS]
        owned = jnp.sum(first_hot, 0, keepdims=True) > 0.5
        valid = (label >= 0) & owned
        positive = one_zero(label == 1)
        small = jnp.exp(-jnp.abs(logit))
        soft = jnp.maximum(logit, 0.0) + jnp.log(1.0 + small)
        bce = bce + total_of(jnp.where(valid, soft - positive * logit, 0.0))
        sigmoid = jnp.where(logit >= 0.0, 1.0, small) / (1.0 + small)
        coef = jnp.where(valid, sigmoid - positive, 0.0) / pair_count
        coef_sum = coef_sum + total_of(coef)
        coef_top, coef_rest = split_two(first_hot * coef)
        touch = touch + nt(coef_top, second_hot) + nt(coef_rest, second_hot)
    s.touch[...] = touch
    column = iota((1, 128), 1)
    row = jnp.where(column == HEADS, coef_sum, 0.0)
    for h in range(HEADS):
        part = total_of(touch * f.prob_low[h * 32 : h * 32 + 32, :].astype(F32)) * COLS
        row = row + jnp.where(column == h, part, 0.0)
    return row, bce


def feature_order():
    shape = (384, 384)
    spot = iota(shape, 0)
    block = (spot * 2731) >> 16
    swapped = (block & 28) | ((block & 1) << 1) | ((block >> 1) & 1)
    return one_zero(spot + (swapped - block) * 24 == iota(shape, 1)).astype(BF16)


def forward_body(small, contact_head, weights, s, f, cells, projected, hook, emit):
    out_row, in_col, out_col = weights[:3]
    up_parts, down_parts = weights[3:5], weights[5:7]
    hook()
    features = cells()
    ahead = (
        ((iota((HERE, HERE), 0) >> 4) == (iota((HERE, HERE), 1) & 31))
        & ((iota((HERE, HERE), 0) & 15) == (iota((HERE, HERE), 1) >> 5))
    )
    ahead = one_zero(ahead).astype(BF16)
    read_tokens(small, f)
    _, block = position()
    shift = lax.rem(128 - lax.rem(block, 4) * 32, 128)
    window = pl.ds(pl.multiple_of((block // 4) * 128, 128), 128)
    hot_ri = local_hot(f.ids[:, window], shift)
    goal_ri = local_hot(f.targets[...], shift)
    s.hot_ri[...] = hot_ri
    for number in range(SLOTS // 512):
        lanes = slice(number * 512, number * 512 + 512)
        f.second_hot[:, lanes] = one_zero(f.slots[1:2, lanes] == iota((COLS, 512), 0)).astype(BF16)
    for r in range(ROWS):
        row = f.ids[r : r + 1, :]
        s.hot_all[r * VP : r * VP + VP, :] = one_zero(row == iota((VP, COLS), 0)).astype(BF16)
    shape = (HERE, HERE)
    back = (
        ((iota(shape, 1) >> 4) == (iota(shape, 0) & 31))
        & ((iota(shape, 1) & 15) == (iota(shape, 0) >> 5))
    )
    back = one_zero(back).astype(BF16)
    hot_ir = nn(hot_ri, back).astype(BF16)
    s.hot_ir[...] = hot_ir
    goal = nn(goal_ri, back)
    entries = jnp.zeros((4, 128), F32)
    labelled = jnp.zeros((1, 128), F32)
    for d in range(32):
        entries = entries + one_zero(small[d, 0:4, :] == MASK_ID)
        labelled = labelled + one_zero(small[d, 10:11, :] >= 0) + one_zero(small[d, 13:14, :] >= 0)
    entries, labelled = total_of(entries), total_of(labelled)

    hook()
    features = features[...].T
    table = features[:VP]
    norms = features[VP : VP + 8]
    s.table[...] = table
    s.norms[...] = norms
    table_low = table.astype(BF16)

    def vector(number):
        return norms[number : number + 1, :]

    hook()
    projected(s.proj_t)
    pair_parts = []
    for hp in range(PAIRS):
        lanes = slice(hp * 128, hp * 128 + 128)
        key = s.proj_t[:, D + hp * 128 : D + hp * 128 + 128]
        value = s.proj_t[:, 2 * D + hp * 128 : 2 * D + hp * 128 + 128]
        s.value_two[hp] = stacked(value)
        pair_parts.append(nt(s.proj_t[:, lanes], stacked(key)))
    pair_hi, pair_lo = split_two(jnp.concatenate(pair_parts, 1))
    hook()
    f.lookup[...] = tn(hot_ri, pair_hi) + tn(hot_ri, pair_lo)
    split_heads_to(f.lookup, f.left_hi, f.left_lo)
    hook()
    hot_all = s.hot_all[...]
    score = (nn(f.left_hi[...], hot_all) + nn(f.left_lo[...], hot_all)) * (HD * ROWS) ** (-0.5)
    score = jnp.exp(score - jnp.max(score, -1, keepdims=True))
    prob = score / jnp.sum(score, -1, keepdims=True)
    s.prob[...] = prob
    f.prob_low[...] = prob.astype(BF16)
    hook()
    merge_heads(f.prob_low[...], s.hot_all, s.weight_hi, f.weight_lo)
    hook()
    for hp in range(PAIRS):
        lanes = slice(hp * 128, hp * 128 + 128)
        value = s.value_two[hp]
        both = jnp.concatenate([s.weight_hi[:, lanes], f.weight_lo[:, lanes]], 1)
        f.mixed[:, lanes] = nn(both, jnp.concatenate([value, value], 0)).astype(BF16)
    f.mixed[...] = nn(ahead, f.mixed[...]).astype(BF16)
    s.stream[...] = tn(hot_ir, table_low)
    emit(AT.hot_all, AT.hot_ri, AT.hot_ir, AT.table, AT.norms, AT.proj_t, AT.value_two, AT.prob, AT.weight_hi)
    hook()
    for half in range(2):
        lanes = slice(half * 384, half * 384 + 384)
        s.stream[:, lanes] += nn(f.mixed[...], out_row[half])
    norm_rows(s.stream, vector(1), vector(5), s.unit_1, s.rstd_1, f.normed)
    emit(AT.unit_1, AT.rstd_1)

    def project(half, at):
        s.col_proj[:, half * 1152 + at : half * 1152 + at + 384] = nn(
            f.normed[...], in_col[half, :, at : at + 384]
        ).astype(BF16)

    for third in range(3):
        hook()
        for half in range(2):
            project(half, third * 384)
    emit(AT.col_proj)

    def attend(at, carry):
        rows = pl.ds(pl.multiple_of((at // PAIRS) * 128, 128), 128)
        lane = lax.rem(at, PAIRS) * 128

        def lanes(part):
            return pl.ds(pl.multiple_of(part * D + lane, 128), 128)

        query = stacked(s.col_proj[rows, lanes(0)])
        score = nt(query, s.col_proj[rows, lanes(1)]) * HD ** (-0.5)
        score = jnp.where(column_mask(), score, -1e30)
        score = jnp.exp(score - jnp.max(score, -1, keepdims=True))
        prob = score / jnp.sum(score, -1, keepdims=True)
        s.col_prob[at] = prob
        mixed = nn(prob.astype(BF16), s.col_proj[rows, lanes(2)])
        f.mixed_2[rows, lanes(0)] = unstacked(mixed, 128).astype(BF16)
        return carry

    for part in range(4):
        hook()
        lax.fori_loop(part * PAIRS, part * PAIRS + PAIRS, attend, 0, unroll=3)
    hook()
    emit(AT.col_prob)
    for half in range(2):
        lanes = slice(half * 384, half * 384 + 384)
        s.stream[:, lanes] += nn(f.mixed_2[...], out_col[half])
    norm_rows(s.stream, vector(2), vector(6), s.unit_2, s.rstd_2, f.normed_2)
    emit(AT.unit_2, AT.rstd_2)
    hook()
    contact_row, bce = contact_part(contact_head, f, s, labelled)
    emit(AT.touch)
    for part in range(2):

        def widen(half, at, part=part):
            lanes = slice(part * 1536 + half * 768 + at, part * 1536 + half * 768 + at + UP_TILE)
            up = nn(f.normed_2[...], up_parts[part][half, :, at : at + UP_TILE])
            active, slope = gelu_parts(up)
            s.active[:, lanes] = active.astype(BF16)
            s.slope[:, lanes] = slope.astype(BF16)

        for half in range(2):
            hook()
            for at in range(0, 768, UP_TILE):
                widen(half, at)
        hook()
        if part == 0:
            transpose_into(f.mixed, s.row_mixed_t)
            transpose_into(f.normed, s.col_normed_t)
            emit(AT.row_mixed_t, AT.col_normed_t)
        else:
            transpose_into(f.mixed_2, s.col_mixed_t)
            emit(AT.col_mixed_t)

    emit(AT.active, AT.slope)
    for part, at, size in ((0, 0, 768), (1, 0, 384), (1, 384, 384)):
        hook()
        added = []
        for half in range(2):
            start = part * 1536 + half * 768 + at
            matrix = down_parts[part][half, :, at : at + size]
            added.append(nt(s.active[:, start : start + size], matrix))
        s.stream[...] += added[0] + added[1]
        if part == 0:
            hook()
            transpose_into(f.normed_2, s.feed_normed_t)
            emit(AT.feed_normed_t)
    hook()
    norm_rows(s.stream, vector(3), vector(7), f.unit, f.rstd, f.normed)
    logits = nt(table_low, f.normed[...]) * D ** (-0.5)
    vocab = iota((VP, HERE), 0)
    logits = jnp.where(vocab < VOCAB, logits, -1e30)
    shifted = logits - jnp.max(logits, 0, keepdims=True)
    log_probs = shifted - jnp.log(jnp.sum(jnp.exp(shifted), 0, keepdims=True))
    keep = hot_ir[MASK_ID : MASK_ID + 1].astype(F32) > 0.5
    mlm = -total_of(jnp.where(keep & (goal > 0.5), log_probs, 0.0))
    logit_grad = jnp.where(keep, jnp.exp(log_probs) - goal, 0.0) / entries
    logit_low = (logit_grad * D ** (-0.5)).astype(BF16)
    s.grad_head[...] = nn(logit_low, f.normed[...])
    hook()
    f.lookup[...] = tn(logit_low, table_low)
    scale_3, shift_3 = back_rows(f.unit, f.rstd, vector(3), f.lookup, s.stream, s.branch, True)
    emit(AT.stream, AT.branch)
    line = iota((8, D), 0)
    s.moved[...] = jnp.where(line == 0, scale_3, jnp.where(line == 1, shift_3, 0.0))
    column = iota((1, 128), 1)
    row = contact_row + jnp.where(column == HEADS + 1, mlm, 0.0) + jnp.where(column == HEADS + 2, bce, 0.0)
    counted = jnp.where(column == 0, entries, 0.0) + jnp.where(column == 1, labelled, 0.0)
    line = iota((8, 128), 0)
    s.extras[...] = jnp.where(line == 0, row, jnp.where(line == 1, counted, 0.0))
    emit(AT.grad_head, AT.extras, AT.moved)
    hook()


def back_rows(unit_ref, rstd_ref, gain, upstream_ref, stream_ref, low_ref, first):
    def body(at, carry):
        scale, move = carry
        rows = pl.ds(pl.multiple_of(at * 64, 64), 64)
        upstream = upstream_ref[rows, :]
        unit = unit_ref[rows, :]
        inner = upstream * gain
        mean = jnp.sum(inner, -1, keepdims=True) * (1.0 / D)
        along = jnp.sum(inner * unit, -1, keepdims=True) * (1.0 / D)
        grad = rstd_ref[rows, 0:1] * (inner - mean - unit * along)
        if not first:
            grad = grad + stream_ref[rows, :]
        stream_ref[rows, :] = grad
        low_ref[rows, :] = grad.astype(BF16)
        touched = upstream * unit
        for n in range(8):
            scale = scale + touched[n * 8 : n * 8 + 8]
            move = move + upstream[n * 8 : n * 8 + 8]
        return scale, move

    zero = jnp.zeros((8, D), F32)
    scale, move = lax.fori_loop(0, HERE // 64, body, (zero, zero), unroll=2)
    return jnp.sum(scale, 0, keepdims=True), jnp.sum(move, 0, keepdims=True)


MATRICES = (128, 384, 1152, 384, 768, 768, 768, 768)
UNITS = (
    (0, 0, 128, True),
    (1, 0, 384, False),
    (2, 0, 384, True),
    (2, 384, 384, True),
    (2, 768, 384, True),
    (3, 0, 384, False),
    (4, 0, 768, True),
    (5, 0, 768, True),
    (6, 0, 768, True),
    (7, 0, 384, True),
    (7, 384, 384, True),
)
Z_LAST = {9: 1, 10: 2}
FORWARD_ORDER = (
    ((0, 0), (0, 2), (0, 11), (1, 0), (0, 1), (0, 9), (0, 10), (1, 11), (2, 0), (0, 3), (1, 2), (0, 4), (2, 11), (3, 0), (1, 10), (1, 9), (1, 1), (4, 0),),
    ((2, 2), (0, 5), (2, 1),),
    ((3, 11), (1, 3), (0, 6), (3, 2), (4, 11), (1, 4),),
    ((3, 1), (4, 2), (1, 5), (0, 7),),
    ((4, 1), (2, 3), (2, 4),),
    ((1, 6), (0, 8),),
    (),
    ((3, 3),),
    ((3, 4), (2, 5), (4, 3), (2, 9), (1, 7), (4, 4),),
    (),
    (),
    (),
    ((3, 5), (2, 6),),
    (),
    ((4, 5), (2, 7), (2, 10),),
    ((1, 8),),
    ((3, 6),),
    ((3, 9), (3, 7), (4, 6),),
    (),
    ((2, 8), (4, 9),),
    ((4, 7),),
    (),
    (),
    ((3, 8), (3, 10), (4, 8),),
    ((4, 10),),
    (),
    (),
    (),
    (),
    (),
)


def spot(paired, cc, zz, yy, k):
    return (k, zz, yy, cc) if paired else (cc, zz, yy, k)


def forward_kernel(*refs):
    count, parts = len(UNITS), len(MATRICES)
    raw = refs[:11]
    contact_head = refs[11]
    at = 12
    far = (None, *refs[at : at + parts - 1])
    saved_far = refs[at + parts - 1 : at + parts - 1 + len(SAVED)]
    at += parts - 1 + len(SAVED)
    outs = refs[at : at + parts]
    at += parts
    outgoing = refs[at : at + count]
    incoming = refs[at + count : at + 2 * count]
    piece = refs[at + 2 * count : at + 3 * count]
    at += 3 * count
    saved = Saved(*refs[at : at + len(SAVED)])
    at += len(SAVED)
    scratch = Forward(*refs[at : at + len(FORWARD)])
    at += len(FORWARD)
    near = refs[at : at + 11]
    at += 11
    small, small_out, corner, features, stat, stat_got, part, part_got, part_line, proj, room = refs[at : at + 11]
    small_send, small_recv, send, recv, local, out_sem, raw_sem, twin_send, twin_recv = refs[at + 11 :]
    tokens, targets, masked, pairs, labels, table, norms, in_w, out_w, up_w, down_w = near
    z, y, k, c = place()
    me = (z * 4 + y * 2 + k) * 2 + c
    raw_copies = [pltpu.make_async_copy(a, b, raw_sem.at[n]) for n, (a, b) in enumerate(zip(raw, near))]
    for item in raw_copies:
        item.start()
    barrier = greet_all()
    for item in raw_copies[:7]:
        item.wait()
    small[...] = jnp.full(small.shape, -1, jnp.int32)
    for micro in range(2):
        for half in range(2):
            lanes = slice(half * 128, half * 128 + 128)
            row = 2 * micro + half
            small[row : row + 1, :] = jnp.where(
                masked[micro, :, lanes] > 0, MASK_ID, tokens[micro, :, lanes]
            )
            small[4 + row : 5 + row, :] = targets[micro, :, lanes]
        row = 8 + 3 * micro
        for which in range(2):
            small[row + which : row + which + 1, 0:64] = pairs[micro, which : which + 1, :]
        small[row + 2 : row + 3, 0:64] = labels[micro : micro + 1, :]
    corner[...] = jnp.zeros(corner.shape, F32)
    corner[0:8, 0:24] = norms[...]
    vectors = pltpu.roll(corner[...].T[:24], 64, 1)
    corner[0:8, 0:24] = jnp.zeros((8, 24), F32)
    corner[0:24, 0:VOCAB] = table[...]
    mine_rows = (corner[0:24, :] + vectors).astype(BF16).astype(F32)
    table_rows = jnp.where(iota((24, 128), 1) < VP, mine_rows, 0.0)
    gain, bias = mine_rows[:, 64:65], mine_rows[:, 68:69]
    piece[0][0:16, :] = small[...].astype(F32)
    piece[0][16:40, :] = mine_rows
    mean = jnp.sum(table_rows, 0, keepdims=True) * (1.0 / 24)
    centre = table_rows - mean
    spread = jnp.sum(centre * centre, 0, keepdims=True)
    line = iota((8, 128), 0)
    stat[...] = jnp.where(line == 0, mean, jnp.where(line == 1, spread, 0.0))
    def master(u, side):
        matrix, start, n, _ = UNITS[u]
        width = MATRICES[matrix]
        if matrix == 2:
            return in_w[1, :, side * 1152 + start : side * 1152 + start + n]
        if matrix in (1, 3):
            rows = out_w[matrix // 2, :, side * 384 : side * 384 + 384].astype(BF16)
            return nn(rows, order)
        begin = (matrix % 2) * 1536 + side * width + start
        return (up_w if matrix < 6 else down_w)[:, begin : begin + n]

    def mine(u):
        return k if UNITS[u][3] else c

    def set_out(u):
        other = jnp.where(mine(u) == 0, master(u, 1), master(u, 0))
        other = jnp.concatenate([other, jnp.zeros((8, UNITS[u][2]), F32)], 0)
        outgoing[u][...] = other.astype(BF16)

    pl.semaphore_wait(barrier, 31)

    def stat_copy(step):
        other = lax.rem(me + step, 32)
        return remote(
            stat, stat_got.at[me], small_send.at[0, step], small_recv.at[0, step], (other // 2, lax.rem(other, 2))
        )

    chip = (z * 2 + y) * 2 + c

    def chip_copy(phase, step):
        other = lax.rem(chip + step, 16)
        target = device(other // 4, lax.rem(other // 2, 2), k, lax.rem(other, 2))
        if phase == 1:
            src, dst = part.at[k, other], part_line.at[chip]
        else:
            src, dst = proj.at[k, chip], proj.at[k, chip]
        return remote(src, dst, small_send.at[phase, step], small_recv.at[phase, step], target)

    def each(last, action):
        def body(step, carry):
            action(step)
            return carry

        lax.fori_loop(1, last, body, 0)

    each(32, lambda step: stat_copy(step).start())

    across, beside, twin = device(z, y, k, 1 - c), device(z, 1 - y, k, c), device(z, y, 1 - k, c)

    def block(u, cc, zz, yy):
        matrix, start, n, paired = UNITS[u]
        where = spot(paired, cc, zz, yy, k)
        if n == MATRICES[matrix]:
            return outs[matrix].at[where]
        return outs[matrix].at[(*where, slice(None), pl.ds(start, n))]

    def copy(u, at, src, dst, target):
        return remote(src, dst, send.at[u, at], recv.at[u, at], target)

    def pair_copy(u):
        return copy(u, 0, outgoing[u], incoming[u], twin if UNITS[u][3] else across)

    def own_copy(u):
        return pltpu.make_async_copy(piece[u], block(u, c, z, y), local.at[u])

    def line_copy(u, step):
        return copy(u, step, piece[u], block(u, c, z, y), device(lax.rem(z + step, 4), y, k, c))

    def same(u, at, cc, zz, yy, target):
        view = block(u, cc, zz, yy)
        return copy(u, at, view, view, target)

    low, high, every = pl.ds(0, 2), pl.ds(2, 2), slice(None)

    def second(u):
        return [same(u, 4, c, low, y, across), same(u, 5, c, high, y, beside)]

    def third_own(u):
        return [same(u, 6, c, low, y, beside), same(u, 7, c, high, y, across)]

    def third_far(u):
        return [same(u, 8, 1 - c, low, y, beside), same(u, 9, c, high, 1 - y, across)]

    def twin_own(u):
        return [same(u, 10, c, every, y, twin)]

    def twin_second(u):
        return [same(u, 11, 1 - c, low, y, twin), same(u, 12, c, high, 1 - y, twin)]

    def twin_third(u):
        return [
            same(u, 13, c, low, 1 - y, twin),
            same(u, 14, 1 - c, high, y, twin),
            same(u, 15, 1 - c, low, 1 - y, twin),
            same(u, 16, 1 - c, high, 1 - y, twin),
        ]

    own_copy(0).start()
    for item in raw_copies[7:]:
        item.wait()
    order = feature_order()
    for u in range(1, count):
        set_out(u)
        pair_copy(u).start()

    def part_twin():
        return remote(part.at[1 - k], part_got, twin_send.at[0], twin_recv.at[0], twin)

    def proj_twin():
        return remote(proj.at[k], proj.at[k], twin_send.at[1], twin_recv.at[1], twin)

    def project_part():
        stat_got[me] = stat[...]
        each(32, lambda step: stat_copy(step).wait())
        means = jnp.zeros((1, 128), F32)
        spreads = jnp.zeros((1, 128), F32)
        for d in range(32):
            means = means + stat_got[d, 0:1, :]
            spreads = spreads + stat_got[d, 1:2, :]
        means = means * (1.0 / 32)
        for d in range(32):
            away = stat_got[d, 0:1, :] - means
            spreads = spreads + 24.0 * away * away
        rstd = lax.rsqrt(spreads * (1.0 / D) + NORM_EPS)
        normed = (table_rows - means) * rstd * gain + bias
        normed = jnp.concatenate([normed, jnp.zeros((8, 128), F32)], 0).astype(BF16)
        for block_at in range(6):
            lanes = slice(block_at * 384, block_at * 384 + 384)
            rows = jnp.concatenate([in_w[0, :, lanes], jnp.zeros((8, 384), F32)], 0).astype(BF16)
            product = tn(normed, rows)
            for group in range(5):
                number = group * 6 + block_at
                part[number // 16, number % 16] = product[group * 8 : group * 8 + 8]
        for number in (30, 31):
            part[number // 16, number % 16] = jnp.zeros((8, 384), F32)
        part_twin().start()

    def project_chip():
        part_twin().wait_recv()
        part[k] = part[k] + part_got[...]
        each(16, lambda step: chip_copy(1, step).start())

    def project_line():
        part_line[chip] = part[k, chip]
        each(16, lambda step: chip_copy(1, step).wait_recv())
        proj[k, chip] = lax.fori_loop(1, 16, lambda at, held: held + part_line[at], part_line[0])
        each(16, lambda step: chip_copy(2, step).start())

    def project_twin():
        each(16, lambda step: chip_copy(2, step).wait_recv())
        proj_twin().start()

    def project_end():
        proj_twin().wait_recv()

    projecting = (project_part, project_chip, project_line, project_twin, project_end)

    def cells():
        for d in range(32):
            at = ((d // 2) % 2, d // 8, (d // 4) % 2, d % 2)
            small_out[d] = outs[0][(*at, slice(0, 16))].astype(jnp.int32)
            start = (((at[1] * 2 + at[2]) * 2 + at[3]) * 2 + at[0]) * 24
            features[start : start + 24, :] = outs[0][(*at, slice(16, 40))]
        return features

    def projected(target):
        room[40:64, :] = jnp.zeros((24, 3 * D), F32)
        for number in range(30):
            rows, lanes = (number // 6) * 8, (number % 6) * 384
            room[rows : rows + 8, lanes : lanes + 384] = proj[number // 16, number % 16]
        target[...] = room[...].astype(BF16)

    def to_across(u):
        return copy(u, 4, piece[u], block(u, c, z, y), across)

    def to_beside(u):
        return copy(u, 5, piece[u], block(u, c, z, y), beside)

    def to_corner(u):
        if Z_LAST[u] == 1:
            return same(u, 6, 1 - c, z, y, beside)
        return same(u, 6, c, z, 1 - y, across)

    def to_line(u):
        return [
            same(u, step, every, z, every, device(lax.rem(z + step, 4), y, k, c)) for step in (1, 3, 2)
        ]

    def to_twin(u):
        return [same(u, 7, every, z, every, twin)]

    def rest_to_twin(u):
        return [same(u, 7 + step, every, lax.rem(z + 4 - step, 4), every, twin) for step in (1, 3, 2)]

    def stage_line(u):
        if u == 0:
            for step in (1, 3, 2):
                line_copy(u, step).start()
            return
        pair_copy(u).wait_recv()
        side = mine(u)
        own = jnp.where(side == 0, master(u, 0), master(u, 1))
        theirs = incoming[u][...].astype(F32)[:24]
        top = jnp.where(side == 0, own, theirs)
        bottom = jnp.where(side == 0, theirs, own)
        piece[u][...] = jnp.concatenate([top, bottom], 0).astype(BF16)
        own_copy(u).start()
        if u in Z_LAST:
            to_across(u).start()
            to_beside(u).start()
            return
        for step in (1, 3, 2):
            line_copy(u, step).start()

    def stage_second(u):
        own_copy(u).wait()
        if u in Z_LAST:
            to_across(u).wait_recv()
            to_beside(u).wait_recv()
            to_corner(u).start()
            return
        for step in (1, 3, 2):
            line_copy(u, step).wait_recv()
        for item in second(u) + third_own(u) + twin_own(u):
            item.start()

    def stage_third(u):
        if u in Z_LAST:
            to_corner(u).wait_recv()
            for item in to_line(u) + to_twin(u):
                item.start()
            return
        for item in second(u):
            item.wait_recv()
        for item in third_far(u) + twin_second(u):
            item.start()

    def stage_twin(u):
        if u in Z_LAST:
            for item in to_line(u):
                item.wait_recv()
            for item in rest_to_twin(u):
                item.start()
            return
        for item in third_own(u) + third_far(u):
            item.wait_recv()
        for item in twin_third(u):
            item.start()

    def far_copy(matrix):
        return pltpu.make_async_copy(outs[matrix], far[matrix], local.at[count + matrix])

    def stage_end(u):
        if u in Z_LAST:
            for item in to_twin(u) + rest_to_twin(u):
                item.wait_recv()
            sent = [to_across(u), to_beside(u), to_corner(u)] + to_line(u) + to_twin(u)
        else:
            for item in twin_own(u) + twin_second(u) + twin_third(u):
                item.wait_recv()
            sent = [line_copy(u, step) for step in (1, 2, 3)]
            sent += second(u) + third_own(u) + third_far(u) + twin_own(u) + twin_second(u)
        for item in sent if u == 0 else [pair_copy(u)] + sent:
            item.wait_send()
        if u == 0:
            return
        if u + 1 == count or UNITS[u + 1][0] != UNITS[u][0]:
            far_copy(UNITS[u][0]).start()

    stages = (stage_line, stage_second, stage_third, stage_twin, stage_end)
    pending = list(FORWARD_ORDER)

    def hook():
        for stage, u in pending.pop(0):
            if u == count:
                projecting[stage]()
            else:
                stages[stage](u)

    def out_copy(at):
        return pltpu.make_async_copy(saved[at], saved_far[at], out_sem.at[at])

    def emit(*numbers):
        for number in numbers:
            out_copy(number).start()

    views = [w.reshape(2, D, n) for w, n in zip(outs[1:], MATRICES[1:])]
    forward_body(small_out, contact_head, views, saved, scratch, cells, projected, hook, emit)
    part_twin().wait_send()
    proj_twin().wait_send()
    for phase in (1, 2):
        each(16, lambda step, phase=phase: chip_copy(phase, step).wait_send())
    assert not pending
    for u in range(count):
        for item in rest_to_twin(u) if u in Z_LAST else twin_third(u):
            item.wait_send()
    for matrix in range(1, parts):
        far_copy(matrix).wait()
    for at in range(len(SAVED)):
        out_copy(at).wait()


def forward_call(raw, contact_head):
    count, parts = len(UNITS), len(MATRICES)
    anywhere = pl.BlockSpec(memory_space=pl.ANY)
    shapes = [(2, NZ, NY, 2, 48, n) for n in MATRICES[1:]]
    widths = [n for _, _, n, _ in UNITS]
    outs = pl.pallas_call(
        forward_kernel,
        out_shape=[jax.ShapeDtypeStruct(shape, BF16) for shape in shapes]
        + [jax.ShapeDtypeStruct(*item) for item in SAVED],
        in_specs=[anywhere] * 11 + [pl.BlockSpec(memory_space=pltpu.SMEM)],
        out_specs=[anywhere] * (parts - 1 + len(SAVED)),
        scratch_shapes=[pltpu.VMEM((2, NZ, NY, 2, 40, 128), F32)]
        + [pltpu.VMEM(shape, BF16) for shape in shapes]
        + [pltpu.VMEM((32, n), BF16) for n in widths] * 2
        + [pltpu.VMEM((40, 128), F32)]
        + [pltpu.VMEM((48, n), BF16) for n in widths[1:]]
        + [pltpu.VMEM(*item) for item in SAVED]
        + [pltpu.VMEM(*item) for item in FORWARD]
        + [pltpu.VMEM(item.shape, item.dtype) for item in raw]
        + [
            pltpu.VMEM((16, 128), jnp.int32),
            pltpu.VMEM((32, 16, 128), jnp.int32),
            pltpu.VMEM((128, 128), F32),
            pltpu.VMEM((D, 128), F32),
            pltpu.VMEM((8, 128), F32),
            pltpu.VMEM((32, 8, 128), F32),
            pltpu.VMEM((2, 16, 8, 384), F32),
            pltpu.VMEM((16, 8, 384), F32),
            pltpu.VMEM((16, 8, 384), F32),
            pltpu.VMEM((2, 16, 8, 384), F32),
            pltpu.VMEM((VP, 3 * D), F32),
            pltpu.SemaphoreType.DMA((3, 32)),
            pltpu.SemaphoreType.DMA((3, 32)),
            pltpu.SemaphoreType.DMA((count, 17)),
            pltpu.SemaphoreType.DMA((count, 17)),
            pltpu.SemaphoreType.DMA((count + parts,)),
            pltpu.SemaphoreType.DMA((len(SAVED),)),
            pltpu.SemaphoreType.DMA((len(raw),)),
            pltpu.SemaphoreType.DMA((2,)),
            pltpu.SemaphoreType.DMA((2,)),
        ],
        compiler_params=pltpu.CompilerParams(
            collective_id=0, has_side_effects=True, vmem_limit_bytes=62 * 2**20
        ),
    )(*raw, contact_head)
    return outs[: parts - 1], Saved(*outs[parts - 1 :])


def summed_rows(sums, group):
    return jnp.concatenate([sums[3 * group + third] for third in range(3)], 1).astype(F32)


def table_finish(sums, room, table_ref, norms_ref, proj_t, in_row, g_in, g_norm, send_stat):
    z, y, k, c = place()
    me = ((z * 2 + y) * 2 + c) * 2 + k
    room[0:128, :] = jnp.zeros((128, D), F32)
    for number in range(2):
        room[4 + 16 * number : 20 + 16 * number, :] = summed_rows(sums, number)
        room[68 + 16 * number : 84 + 16 * number, :] = summed_rows(sums, 2 + number)
    pair = room[0:64, :]
    value_grad = room[64:128, :]
    vectors = summed_rows(sums, 6)
    vectors = vectors[:8] + vectors[8:]
    line = iota((8, D), 0)
    table_grad = jnp.concatenate(
        [
            summed_rows(sums, 4),
            summed_rows(sums, 5),
            jnp.where(line == 0, vectors[7:8], 0.0),
            jnp.zeros((24, D), F32),
        ],
        0,
    )
    pair_hi, pair_lo = split_two(pair)
    scale = (HD * ROWS) ** (-0.5)
    query_grad, key_grad = [], []
    for hp in range(PAIRS):
        lanes = slice(hp * 128, hp * 128 + 128)
        query = proj_t[:, lanes]
        key = stacked(proj_t[:, D + hp * 128 : D + hp * 128 + 128])
        high, low = pair_hi[:, lanes], pair_lo[:, lanes]
        query_grad.append((nn(high, key) + nn(low, key)) * scale)
        key_grad.append(unstacked(tn(high, query) + tn(low, query), VP) * scale)
    proj_hi, proj_lo = split_two(jnp.concatenate(query_grad + key_grad + [value_grad], 1))
    shard = D // 32
    pick = one_zero(iota((shard, D), 1) == iota((shard, D), 0) + me * shard).astype(BF16)
    weight = in_row[...].astype(BF16)
    back_t = nt(weight, proj_hi) + nt(weight, proj_lo)
    back = nt(proj_hi, weight) + nt(proj_lo, weight)
    table = table_ref[...]
    table_low = table.astype(BF16)
    unit, rstd = norm_stats(table)
    mean = jnp.sum(table, -1, keepdims=True) * (1.0 / D)
    same = iota((VP, VP), 0) == iota((VP, VP), 1)

    def as_row(column):
        return jnp.sum(jnp.where(same, column, 0.0), 0, keepdims=True)

    rstd_row = as_row(rstd)
    unit_t = (nt(pick, table_low) - as_row(mean)) * rstd_row
    unit_mine = (nt(table_low, pick) - mean) * rstd
    norms = jnp.concatenate([norms_ref[...], jnp.zeros((8, D), F32)], 0).astype(BF16)
    inner = back_t * nt(pick, norms)[:, 0:1]

    def three(values):
        top, rest = split_two(values)
        return top, rest, (values - top.astype(F32) - rest.astype(F32)).astype(BF16)

    emb_grad = sum(nt(pick, part) for part in three(table_grad))
    before = emb_grad + rstd_row * inner
    parts = (inner, inner * unit_t, before, before * unit_t, unit_t, unit_t * unit_t, before * before)
    send_stat([jnp.sum(part, 0, keepdims=True) for part in parts])
    scale_0 = jnp.sum(back * unit_mine, 0, keepdims=True)
    shift_0 = jnp.sum(back, 0, keepdims=True)
    line = iota((16, D), 0)
    norm_grad = jnp.zeros((16, D), F32)
    for number, source in ((1, 0), (2, 1), (3, 2), (5, 3), (6, 4), (7, 5)):
        norm_grad = jnp.where(line == number, vectors[source : source + 1], norm_grad)
    normed = (unit * norms_ref[0:1, :] + norms_ref[4:5, :]).astype(BF16)
    mine = nt(pick, normed).astype(BF16)
    in_grad = nn(mine, proj_hi) + nn(mine, proj_lo)
    g_in[...] = in_grad
    own_norm = sum(nt(part, pick) for part in three(norm_grad))[:8]
    line = iota((8, shard), 0)
    own_norm = jnp.where(line == 0, scale_0, jnp.where(line == 4, shift_0, own_norm))
    g_norm[...] = own_norm
    found = total_of(in_grad * in_grad) + total_of(own_norm * own_norm)
    return inner, unit_t, rstd_row, emb_grad, found


PIECES = 21
GRAD_WIDTHS = (768, 768, 768, 768, 384, 1152, 384)
GRAD_UNITS = (
    (0, 0, 384, True),
    (0, 384, 384, True),
    (1, 0, 384, True),
    (1, 384, 384, True),
    (2, 0, 384, True),
    (2, 384, 384, True),
    (3, 0, 384, True),
    (3, 384, 384, True),
    (4, 0, 384, False),
    (5, 0, 384, True),
    (5, 384, 384, True),
    (5, 768, 384, True),
    (6, 0, 384, False),
)
Z_FIRST = {0: 1, 3: 2}
BACKWARD_ORDER = (
    (),
    (),
    (),
    (),
    (),
    (),
    ((0, 0),),
    (),
    ((0, 1),),
    (),
    (),
    ((0, 2),),
    ((0, 3),),
    ((1, 1),),
    ((0, 4),),
    (),
    ((1, 2), (0, 5),),
    ((2, 1), (0, 6),),
    ((1, 0), (1, 4), (0, 7),),
    ((2, 2),),
    (),
    ((1, 5), (0, 8),),
    (),
    ((1, 6),),
    ((2, 0),),
    ((1, 3), (2, 4),),
    (),
    ((1, 7),),
    ((2, 5),),
    (),
    (),
    ((1, 8), (0, 9), (2, 6),),
    ((2, 3), (0, 10),),
    ((2, 7), (0, 11),),
    ((2, 8),),
    ((0, 12),),
    ((1, 9),),
    ((1, 10),),
    ((1, 11),),
    ((3, 0), (3, 1), (3, 2), (3, 3), (3, 4), (3, 5), (3, 6), (1, 12), (3, 7), (3, 8), (4, 0), (2, 9), (4, 1), (4, 2), (2, 10), (4, 3), (4, 4), (5, 0), (2, 11), (3, 9), (4, 5), (2, 12), (4, 6), (4, 7), (3, 10), (4, 8), (4, 9), (4, 10), (6, 0), (3, 11), (3, 12), (4, 11), (4, 12),),
)


class Kept(typing.NamedTuple):
    stream: typing.Any
    norms: typing.Any
    table: typing.Any
    proj_t: typing.Any
    extras: typing.Any
    moved: typing.Any
    grad_head: typing.Any
    touch: typing.Any
    value_two: typing.Any


class Early(typing.NamedTuple):
    slope: typing.Any
    active: typing.Any
    feed_normed_t: typing.Any
    unit_2: typing.Any
    rstd_2: typing.Any
    col_mixed_t: typing.Any
    col_proj: typing.Any
    col_prob: typing.Any
    col_normed_t: typing.Any
    unit_1: typing.Any
    rstd_1: typing.Any


class Late(typing.NamedTuple):
    row_mixed_t: typing.Any
    hot_all: typing.Any
    weight_hi: typing.Any
    prob: typing.Any
    hot_ri: typing.Any
    hot_ir: typing.Any


def pick_items(group, source):
    return [getattr(source, name) for name in group._fields]


def backward_kernel(*refs):
    widths = GRAD_WIDTHS
    count = len(widths)
    contact_head = refs[0]
    far = refs[1 : 1 + count]
    in_row_far = refs[1 + count]
    saved = Saved(*refs[2 + count : 2 + count + len(SAVED)])
    at = 2 + count + len(SAVED)
    outs = refs[at : at + count]
    g_in, g_emb, g_norm, stats = refs[at + count : at + count + 4]
    at += count + 4
    grads = refs[at : at + count]
    kept = Kept(*refs[at + count : at + count + len(Kept._fields)])
    at += count + len(Kept._fields)
    upstream, branch, branch_t, mixed = refs[at : at + 4]
    scratch = refs[at + 4 :]
    units = len(GRAD_UNITS)
    got_0, got_1a, got_1b, got_2a, got_2b, got_3, total, got_4 = (
        scratch[i * units : (i + 1) * units] for i in range(8)
    )
    table, table_out, table_got, square, square_got, stat, stat_got, late_rows = scratch[8 * units : 8 * units + 8]
    table_send, table_recv, send, recv, local = scratch[8 * units + 8 :]
    z, y, k, c = place()
    me = (z * 4 + y * 2 + k) * 2 + c
    across, beside, twin = device(z, y, k, 1 - c), device(z, 1 - y, k, c), device(z, y, 1 - k, c)
    stream = kept.stream
    square[...] = jnp.zeros(square.shape, F32)

    copies = {}

    def load(number, source, target):
        copies[number] = pltpu.make_async_copy(source, target, local.at[number])
        copies[number].start()

    def need(*numbers):
        for number in numbers:
            copies[number].wait()

    def weight(m):
        return len(SAVED) + m

    load(AT.branch, saved.branch, branch)
    load(weight(0), far[0], grads[0])
    barrier = greet_all()

    def copy(m, at, src, dst, target):
        return remote(src, dst, send.at[m, at], recv.at[m, at], target)

    low, high = pl.ds(0, 2), pl.ds(2, 2)
    every = slice(None)

    def where(u, cc, zz, yy):
        matrix, start, n, paired = GRAD_UNITS[u]
        index = spot(paired, cc, zz, yy, k)
        return index if n == widths[matrix] else (*index, every, pl.ds(start, n))

    def block(u, cc, zz, yy):
        return grads[GRAD_UNITS[u][0]].at[where(u, cc, zz, yy)]

    def ordered(u, cc, rest):
        return (*rest, cc) if GRAD_UNITS[u][3] else (cc, *rest)

    def twin_copy(u):
        matrix, start, n, paired = GRAD_UNITS[u]
        index = (1 - k,) if paired else (every, every, every, 1 - k)
        if n != widths[matrix]:
            index = (*index, *(every,) * (5 - len(index)), pl.ds(start, n))
        return copy(u, 0, grads[matrix].at[index], got_0[u], twin)

    def first(u):
        return [
            copy(u, 1, block(u, every, low, 1 - y), got_1a[u], beside),
            copy(u, 2, block(u, 1 - c, high, every), got_1b[u], across),
        ]

    def second(u):
        return [
            copy(u, 3, block(u, 1 - c, low, y), got_2a[u], across),
            copy(u, 4, block(u, c, high, 1 - y), got_2b[u], beside),
        ]

    def along(u):
        return [
            copy(
                u,
                4 + step,
                block(u, c, lax.rem(z + step, 4), y),
                got_3[u].at[step - 1],
                device(lax.rem(z + step, 4), y, k, c),
            )
            for step in (1, 3, 2)
        ]

    def z_first(u):
        return [
            copy(
                u,
                step,
                block(u, every, lax.rem(z + step, 4), every),
                got_1a[u].at[step - 1],
                device(lax.rem(z + step, 4), y, k, c),
            )
            for step in (1, 3, 2)
        ]

    def plane_first(u):
        if Z_FIRST[u] == 1:
            return [copy(u, 4, block(u, every, z, 1 - y), got_2a[u], beside)]
        return [copy(u, 4, block(u, 1 - c, z, every), got_2a[u], across)]

    def plane_second(u):
        if Z_FIRST[u] == 1:
            return [copy(u, 5, block(u, 1 - c, z, y), got_2b[u], across)]
        return [copy(u, 5, block(u, c, z, 1 - y), got_2b[u], beside)]

    def mine(u):
        return k if GRAD_UNITS[u][3] else c

    def pair(u):
        return [copy(u, 8, total[u].at[1 - mine(u)], got_4[u], twin if GRAD_UNITS[u][3] else across)]

    def peer(step):
        return lax.rem(me + step, 32)

    def source(step):
        return lax.rem(me + 32 - step, 32)

    def table_copy(step, back, index):
        target = (peer(step) // 2, lax.rem(peer(step), 2))
        if back:
            return remote(
                table_out.at[index], table_out.at[index], table_send.at[1, step], table_recv.at[1, step], target
            )
        return remote(
            table.at[index], table_got.at[me], table_send.at[0, step], table_recv.at[0, step], target
        )

    def table_start(step):
        @pl.when(peer(step) < PIECES)
        def _():
            table_copy(step, False, peer(step)).start()

    def table_wait_send(step):
        @pl.when(peer(step) < PIECES)
        def _():
            table_copy(step, False, 0).wait_send()

        @pl.when(me < PIECES)
        def _():
            table_copy(step, True, 0).wait_send()

    def table_wait_back(step):
        @pl.when(source(step) < PIECES)
        def _():
            table_copy(step, True, 0).wait_recv()

    def each(action):
        def body(step, carry):
            action(step)
            return carry

        lax.fori_loop(1, 32, body, 0)

    def gather_into(u, cc, zz, yy, *others):
        matrix = GRAD_UNITS[u][0]
        index = where(u, cc, zz, yy)
        if not others:
            grads[matrix][index] = grads[matrix][index] + got_0[u][ordered(u, cc, (zz, yy))]
            return
        value = grads[matrix][index].astype(F32) + got_0[u][ordered(u, cc, (zz, yy))].astype(F32)
        for other in others:
            value = value + other.astype(F32)
        grads[matrix][index] = value.astype(BF16)

    def from_line(u, cc, yy):
        index = (yy, cc) if GRAD_UNITS[u][3] else (cc, yy)
        return [got_1a[u][(step, *index)] for step in range(3)]

    def stage_first(u):
        twin_copy(u).wait_recv()
        if u in Z_FIRST:
            for step in (1, 3, 2):
                for cc in range(2):
                    for yy in range(2):
                        gather_into(u, cc, lax.rem(z + step, 4), yy)
            for item in z_first(u):
                item.start()
            return
        for a in range(2):
            for b in range(2):
                gather_into(u, a, b, 1 - y)
                gather_into(u, 1 - c, 2 + a, b)
        for item in first(u):
            item.start()

    def from_beside(u, cc, a):
        return got_1a[u][ordered(u, cc, (a,))]

    def stage_second(u):
        if u in Z_FIRST:
            for item in z_first(u):
                item.wait_recv()
            for a in range(2):
                cc, yy = (a, 1 - y) if Z_FIRST[u] == 1 else (1 - c, a)
                gather_into(u, cc, z, yy, *from_line(u, cc, yy))
            for item in plane_first(u):
                item.start()
            return
        for item in first(u):
            item.wait_recv()
        for a in range(2):
            gather_into(u, 1 - c, a, y, from_beside(u, 1 - c, a))
            gather_into(u, c, 2 + a, 1 - y, got_1b[u][a, 1 - y])
        for item in second(u):
            item.start()

    def stage_along(u):
        if u in Z_FIRST:
            for item in plane_first(u):
                item.wait_recv()
            cc, yy = (1 - c, y) if Z_FIRST[u] == 1 else (c, 1 - y)
            gather_into(u, cc, z, yy, *from_line(u, cc, yy), got_2a[u][cc if Z_FIRST[u] == 1 else yy])
            for item in plane_second(u):
                item.start()
            return
        for item in second(u):
            item.wait_recv()
        for a in range(2):
            gather_into(u, c, a, y, from_beside(u, c, a), got_2a[u][a])
            gather_into(u, c, 2 + a, y, got_1b[u][a, y], got_2b[u][a])
        for item in along(u):
            item.start()

    def stage_pair(u):
        full = grads[GRAD_UNITS[u][0]][where(u, c, z, y)].astype(F32)
        if u in Z_FIRST:
            for item in plane_second(u):
                item.wait_recv()
            others = [got_0[u][ordered(u, c, (z, y))], *from_line(u, c, y)]
            others += [got_2a[u][c if Z_FIRST[u] == 1 else y], got_2b[u][...]]
        else:
            for item in along(u):
                item.wait_recv()
            others = [got_3[u][step] for step in range(3)]
        for other in others:
            full = full + other.astype(F32)
        total[u][0] = full[:24]
        total[u][1] = full[24:]
        for item in pair(u):
            item.start()

    def stage_end(u):
        matrix, start, n, _ = GRAD_UNITS[u]
        lanes = slice(start, start + n)
        side = mine(u)
        outs[matrix][side, :, lanes] = total[u][side]
        for item in pair(u):
            item.wait_recv()
        outs[matrix][1 - side, :, lanes] = got_4[u][...]
        own, other = total[u][side], got_4[u][...]
        square[...] += jnp.broadcast_to(total_of(own * own + other * other), (8, 128))
        if u in Z_FIRST:
            sent = z_first(u) + plane_first(u) + plane_second(u)
        else:
            sent = first(u) + second(u) + along(u)
        for item in [twin_copy(u)] + sent:
            item.wait_send()

    def table_sum(u):
        @pl.when(me < PIECES)
        def _():
            each(lambda step: table_copy(step, False, 0).wait_recv())
            table_got[me] = table[me]

            def add(at, held):
                return held + table_got[at].astype(F32)

            total_rows = lax.fori_loop(1, 32, add, table_got[0].astype(F32))
            top, rest = split_two(total_rows[:8] + total_rows[8:])
            exact = jnp.concatenate([top.astype(F32), rest.astype(F32)], 0)
            table_out[me] = jnp.where(me >= 18, exact, total_rows).astype(BF16)
            each(lambda step: table_copy(step, True, me).start())

    late_parts = []

    def table_end(u):
        each(table_wait_back)
        need(weight(count))
        late_parts.append(
            table_finish(
                table_out, upstream, kept.table, kept.norms, kept.proj_t, late_parts[0], g_in, g_norm, send_stat
            )
        )
        for at, value in enumerate(late_parts[1][:4]):
            late_rows[at] = jnp.broadcast_to(value, (24, VP))
        square[...] += jnp.broadcast_to(late_parts[1][-1], (8, 128))

    def stat_copy(step):
        target = (peer(step) // 2, lax.rem(peer(step), 2))
        return remote(stat, stat_got.at[me], table_send.at[3, step], table_recv.at[3, step], target)

    def send_stat(rows):
        line = iota((8, VP), 0)
        result = jnp.zeros((8, VP), F32)
        for at, row in enumerate(rows):
            result = jnp.where(line == at, row, result)
        stat[...] = result
        each(lambda step: stat_copy(step).start())
        stat_got[me] = stat[...]

    def table_last():
        each(lambda step: stat_copy(step).wait())
        totals = lax.fori_loop(1, 32, lambda at, held: held + stat_got[at], stat_got[0])
        mean_1, mean_2 = totals[0:1] * (1.0 / D), totals[1:2] * (1.0 / D)
        inner, unit, rstd, emb_grad = (late_rows[at] for at in range(4))
        g_emb[...] = emb_grad + rstd * (inner - mean_1 - unit * mean_2)
        first, second = rstd[0:1] * mean_1, rstd[0:1] * mean_2
        whole = totals[6:7] - 2.0 * (first * totals[2:3] + second * totals[3:4])
        whole = whole + first * first * D + 2.0 * first * second * totals[4:5] + second * second * totals[5:6]
        return total_of(whole)

    stages = (stage_first, stage_second, stage_along, stage_pair, stage_end, table_sum, table_end)
    pending = list(BACKWARD_ORDER)

    def hook():
        for stage, u in pending.pop(0):
            stages[stage](u)

    def done(u):
        if u == 0:
            pl.semaphore_wait(barrier, 31)
        twin_copy(u).start()
        hook()

    names = Kept._fields

    def phase_one(*early_refs):
        e = Early(*early_refs)
        left, right = slice(0, 1536), slice(1536, 3072)
        spare = len(SAVED) + count + 1
        load(AT.slope, saved.slope.at[:, left], e.slope.at[:, left])
        load(AT.active, saved.active.at[:, left], e.active.at[:, left])
        load(spare, saved.slope.at[:, right], e.slope.at[:, right])
        load(spare + 1, saved.active.at[:, right], e.active.at[:, right])
        load(weight(1), far[1], grads[1])
        for name in names:
            load(getattr(AT, name), getattr(saved, name), getattr(kept, name))
        for m in (2, 3):
            load(weight(m), far[m], grads[m])
        for name in Early._fields[2:6]:
            load(getattr(AT, name), getattr(saved, name), getattr(e, name))
        load(weight(4), far[4], grads[4])
        for name in Early._fields[6:8]:
            load(getattr(AT, name), getattr(saved, name), getattr(e, name))
        load(weight(5), far[5], grads[5])
        for name in Early._fields[8:]:
            load(getattr(AT, name), getattr(saved, name), getattr(e, name))
        load(weight(6), far[6], grads[6])
        view = [g.reshape(2, D, n) for g, n in zip(grads, widths)]
        need(AT.branch)
        transpose_into(branch, branch_t)
        hook()

        def grad_tile(m, start, left_t, right, half, at):
            lanes = slice(start + half * widths[m] + at, start + half * widths[m] + at + 384)
            view[m][half, :, at : at + 384] = nn(left_t[...], right[:, lanes]).astype(BF16)

        def grad_half(m, start, left_t, right, half):
            for at in range(0, widths[m], 384):
                grad_tile(m, start, left_t, right, half, at)

        for part in range(2):
            need(weight(part))
            need(*((AT.slope,) if part == 0 else (spare, spare + 1)))

            def down_back(half, at, part=part):
                lanes = slice(part * 1536 + half * 768 + at, part * 1536 + half * 768 + at + 384)
                back = nn(branch[...], view[part][half, :, at : at + 384])
                e.slope[:, lanes] = (back * e.slope[:, lanes].astype(F32)).astype(BF16)

            if part == 0:
                for at in (0, 384):
                    for half in range(2):
                        down_back(half, at)
                    hook()
                    if at == 0:
                        need(AT.active)
                    for half in range(2):
                        grad_tile(part, 0, branch_t, e.active, half, at)
                    done(at // 384)
            else:
                for half in range(2):
                    for at in (0, 384):
                        down_back(half, at)
                    hook()
                for at in (0, 384):
                    for half in range(2):
                        grad_tile(part, part * 1536, branch_t, e.active, half, at)
                    done(2 + at // 384)
        for part in range(2):
            need(weight(2 + part))
            for half in range(2):
                start = part * 1536 + half * 768
                back = nt(e.slope[:, start : start + 768], view[2 + part][half])
                upstream[...] = back if start == 0 else upstream[...] + back
                hook()
            if part == 0:
                need(AT.feed_normed_t)
            for at in (0, 384):
                for half in range(2):
                    grad_tile(2 + part, part * 1536, e.feed_normed_t, e.slope, half, at)
                done(4 + 2 * part + at // 384)
        need(*(getattr(AT, name) for name in names))
        norms = kept.norms[...]

        def gain(number):
            return norms[number : number + 1, :]

        need(AT.unit_2, AT.rstd_2)
        scale_2, shift_2 = back_rows(e.unit_2, e.rstd_2, gain(2), upstream, stream, branch, False)
        hook()
        need(weight(4), AT.col_mixed_t)
        mixed[...] = (nt(branch[:, :384], view[4][0]) + nt(branch[:, 384:], view[4][1])).astype(BF16)
        hook()
        for half in range(2):
            grad_half(4, 0, e.col_mixed_t, branch, half)
        done(8)
        need(AT.col_proj, AT.col_prob)
        proj = e.active

        def attend(at, carry):
            rows = pl.ds(pl.multiple_of((at // PAIRS) * 128, 128), 128)
            lane = lax.rem(at, PAIRS) * 128

            def lanes(part):
                return pl.ds(pl.multiple_of(part * D + lane, 128), 128)

            query = stacked(e.col_proj[rows, lanes(0)])
            key = e.col_proj[rows, lanes(1)]
            value = e.col_proj[rows, lanes(2)]
            above = stacked(mixed[rows, lanes(0)])
            prob = e.col_prob[at]
            grad = nt(above, value)
            grad = prob * (grad - jnp.sum(prob * grad, -1, keepdims=True))
            small = grad.astype(BF16)
            scale = HD ** (-0.5)
            proj[rows, lanes(0)] = (unstacked(nn(small, key), 128) * scale).astype(BF16)
            proj[rows, lanes(1)] = (tn(small, query) * scale).astype(BF16)
            proj[rows, lanes(2)] = tn(prob.astype(BF16), above).astype(BF16)
            return carry

        for part in range(6):
            lax.fori_loop(4 * part, 4 * part + 4, attend, 0, unroll=4)
            hook()
        need(weight(5))
        for half in range(2):
            back = nt(proj[:, half * 1152 : half * 1152 + 1152], view[5][half])
            upstream[...] = back if half == 0 else upstream[...] + back
            hook()
        need(AT.col_normed_t)
        for third in range(3):
            for half in range(2):
                grad_tile(5, 0, e.col_normed_t, proj, half, third * 384)
            done(9 + third)
        need(AT.unit_1, AT.rstd_1)
        scale_1, shift_1 = back_rows(e.unit_1, e.rstd_1, gain(1), upstream, stream, branch, False)
        hook()
        need(weight(6))
        mixed[...] = (nt(branch[:, :384], view[6][0]) + nt(branch[:, 384:], view[6][1])).astype(BF16)
        line = iota((8, D), 0)
        vectors = jnp.zeros((8, D), F32)
        moved = kept.moved[...]
        rows = (scale_1, scale_2, moved[0:1], shift_1, shift_2, moved[1:2])
        for number, row in enumerate(rows):
            vectors = jnp.where(line == number, row, vectors)
        extras = jnp.concatenate([kept.extras[0:1, :], jnp.zeros((1, D - 128), F32)], 1)
        kept.moved[...] = jnp.where(line == 6, extras, vectors)
        hook()

    pl.run_scoped(phase_one, *(pltpu.VMEM(*item) for item in pick_items(Early, SAVED)))

    def phase_two(*late_refs):
        e = Late(*late_refs[:-3])
        in_row, left_hi, left_lo = late_refs[-3:]
        for name in Late._fields:
            load(getattr(AT, name), getattr(saved, name), getattr(e, name))
        load(weight(count), in_row_far.at[0], in_row)
        view = grads[6].reshape(2, D, widths[6])
        late_parts.append(in_row)
        need(AT.row_mixed_t)
        for half in range(2):
            lanes = slice(half * 384, half * 384 + 384)
            view[half] = nn(e.row_mixed_t[...], branch[:, lanes]).astype(BF16)
        done(12)
        need(AT.hot_all, AT.weight_hi, AT.prob, AT.hot_ri, AT.hot_ir)
        shape = (HERE, HERE)
        back = (
            ((iota(shape, 1) >> 4) == (iota(shape, 0) & 31))
            & ((iota(shape, 1) & 15) == (iota(shape, 0) >> 5))
        )
        mixed[...] = nn(one_zero(back).astype(BF16), mixed[...]).astype(BF16)
        value_rows = []
        for hp in range(PAIRS):
            lanes = slice(hp * 128, hp * 128 + 128)
            part = mixed[:, lanes]
            upstream[:, lanes] = nt(part, kept.value_two[hp])
            value_rows.append(unstacked(tn(e.weight_hi[:, lanes], part), 64))
        hook()
        split_heads_to(upstream, left_hi, left_lo)
        hook()
        hot_all = e.hot_all[...]
        grad = nn(left_hi[...], hot_all) + nn(left_lo[...], hot_all)
        extra = jnp.concatenate(
            [kept.touch[...] * (contact_head[h] * COLS) for h in range(HEADS)], 0
        )
        grad = grad + extra
        prob = e.prob[...]
        grad = prob * (grad - jnp.sum(prob * grad, -1, keepdims=True))
        low_grad = grad.astype(BF16)
        hook()
        merge_heads(low_grad, e.hot_all, branch, None)
        hook()
        table_pair = nn(e.hot_ri[...], branch[...])
        stream_hi, stream_lo = split_two(stream[...])
        hot_ir = e.hot_ir[...]
        table_grad = kept.grad_head[...] + nn(hot_ir, stream_hi) + nn(hot_ir, stream_lo)
        value_grad = jnp.concatenate(value_rows, 1)
        last = jnp.where(iota((8, D), 0) == 7, table_grad[32:33], kept.moved[...])
        top, rest = split_two(last)
        groups = [table_pair[4:20], table_pair[20:36], value_grad[4:20], value_grad[20:36]]
        groups += [table_grad[0:16], table_grad[16:32]]
        groups += [jnp.concatenate([top.astype(F32), rest.astype(F32)], 0)]
        for number, group in enumerate(groups):
            for third in range(3):
                table[3 * number + third] = group[:, third * 256 : third * 256 + 256].astype(BF16)
        each(table_start)
        hook()
        hook()

    pl.run_scoped(
        phase_two,
        *(pltpu.VMEM(*item) for item in pick_items(Late, SAVED)),
        pltpu.VMEM((24, 3 * D), F32),
        pltpu.VMEM((HEADS * WIDE, ROWS * VP), BF16),
        pltpu.VMEM((HEADS * WIDE, ROWS * VP), BF16),
    )
    assert not pending

    def square_copy(step):
        other = lax.rem(me + step, 32)
        return remote(
            square, square_got.at[me], table_send.at[2, step], table_recv.at[2, step], (other // 2, lax.rem(other, 2))
        )

    each(lambda step: square_copy(step).start())
    square_got[me] = square[...]
    each(lambda step: table_wait_send(step))
    for u in range(units):
        for item in pair(u):
            item.wait_send()
    emb_square = table_last()
    each(lambda step: square_copy(step).wait())
    total_square = lax.fori_loop(1, 32, lambda at, held: held + square_got[at], square_got[0])[0:1]
    vector = table_out[18].astype(F32)
    vector = vector[6:7, :128] + vector[14:15, :128]
    counted = kept.extras[1:2, :]
    column = iota((1, 128), 1)
    contact = jnp.where(column <= HEADS, vector, 0.0)
    total_square = total_square + total_of(contact * contact) + emb_square
    grad_norm = jnp.sqrt(total_square)
    factor = jnp.minimum(1.0, MAX_NORM / grad_norm)
    losses = (
        (0, vector[:, HEADS + 1 : HEADS + 2]),
        (1, counted[:, 0:1]),
        (2, vector[:, HEADS + 2 : HEADS + 3]),
        (3, counted[:, 1:2]),
    )
    loss_row = jnp.zeros((1, 128), F32)
    for at, value in losses:
        loss_row = jnp.where(column == at, value, loss_row)
    number = iota((8, 128), 0)
    result = jnp.zeros((8, 128), F32)
    for at, row in enumerate((contact, counted, factor, grad_norm, loss_row)):
        result = jnp.where(number == at, row, result)
    stats[...] = result


def backward_call(contact_head, weights, in_row, saved):
    widths = GRAD_WIDTHS
    count = len(widths)
    inside = pl.BlockSpec(memory_space=pltpu.VMEM)
    anywhere = pl.BlockSpec(memory_space=pl.ANY)

    units = len(GRAD_UNITS)

    def shapes(lead, dtype, other=None):
        leads = [other if other and u in Z_FIRST else lead for u in range(units)]
        return [pltpu.VMEM((*at, n), dtype) for at, (_, _, n, _) in zip(leads, GRAD_UNITS)]

    outs = pl.pallas_call(
        backward_kernel,
        out_shape=[jax.ShapeDtypeStruct((2, 24, n), F32) for n in widths]
        + [
            jax.ShapeDtypeStruct((24, 3 * D), F32),
            jax.ShapeDtypeStruct((24, VP), F32),
            jax.ShapeDtypeStruct((8, 24), F32),
            jax.ShapeDtypeStruct((8, 128), F32),
        ],
        in_specs=[pl.BlockSpec(memory_space=pltpu.SMEM)] + [anywhere] * (1 + count + len(SAVED)),
        out_specs=[inside] * (4 + count),
        scratch_shapes=[pltpu.VMEM((2, NZ, NY, 2, 48, n), BF16) for n in widths]
        + [pltpu.VMEM(*item) for item in pick_items(Kept, SAVED)]
        + [
            pltpu.VMEM((HERE, D), F32),
            pltpu.VMEM((HERE, D), BF16),
            pltpu.VMEM((D, HERE), BF16),
            pltpu.VMEM((HERE, D), BF16),
        ]
        + [
            pltpu.VMEM((NZ, NY, 2, 48, n) if paired else (2, NZ, NY, 48, n), BF16)
            for _, _, n, paired in GRAD_UNITS
        ]
        + shapes((2, 2, 48), BF16, (3, 2, 2, 48))
        + shapes((2, 2, 48), BF16, (16,))
        + shapes((2, 48), BF16, (2, 48))
        + shapes((2, 48), BF16, (48,))
        + shapes((3, 48), BF16, (16,))
        + shapes((2, 24), F32)
        + shapes((24,), F32)
        + [
            pltpu.VMEM((PIECES, 16, 256), BF16),
            pltpu.VMEM((PIECES, 16, 256), BF16),
            pltpu.VMEM((32, 16, 256), BF16),
            pltpu.VMEM((8, 128), F32),
            pltpu.VMEM((32, 8, 128), F32),
            pltpu.VMEM((8, VP), F32),
            pltpu.VMEM((32, 8, VP), F32),
            pltpu.VMEM((4, 24, VP), F32),
            pltpu.SemaphoreType.DMA((4, 32)),
            pltpu.SemaphoreType.DMA((4, 32)),
            pltpu.SemaphoreType.DMA((units, 9)),
            pltpu.SemaphoreType.DMA((units, 9)),
            pltpu.SemaphoreType.DMA((len(SAVED) + count + 3,)),
        ],
        compiler_params=pltpu.CompilerParams(
            collective_id=1, has_side_effects=True, vmem_limit_bytes=63 * 2**20
        ),
    )(contact_head, *weights, in_row, *saved)
    return outs[:count], outs[count:]


UPDATE_RATES = (LEARN_RATE,) * 4 + (VECTOR_RATE,) * 3


def update_kernel(*refs):
    given, far, held, results = refs[:32], refs[32:60], refs[60:92], refs[92:120]
    sems, out_sems = refs[120:122]
    outs, copies = results[:21], results[21:26]
    loss_ref, norm_ref = results[26:]

    def leave(*numbers):
        for n in numbers:
            pltpu.make_async_copy(results[n], far[n], out_sems.at[n]).start()

    moves = [pltpu.make_async_copy(a, b, sems.at[n]) for n, (a, b) in enumerate(zip(given, held))]
    groups = (
        (10, 7, 5, 11, 12, 13),
        (4, 6, 14, 15, 16),
        (2, 3, 17, 18, 19),
        (0, 1, 20, 21, 22),
        (8, 9, *range(23, 32)),
    )
    for group in groups:
        for n in group:
            moves[n].start()

    def arrive(number):
        for n in groups[number]:
            moves[n].wait()

    reduced, g_in, g_emb, g_norm, stats = held[:7], held[7], held[8], held[9], held[10]
    states = [held[11 + 3 * n : 14 + 3 * n] for n in range(7)]
    outs = [outs[3 * n : 3 * n + 3] for n in range(7)]
    order = feature_order()
    arrive(0)
    factor = stats[2:3, 0:1]
    loss_ref[...] = stats[4:5, 0:4]
    norm_ref[...] = stats[3:4, 0:1]

    def natural(values):
        top, rest = split_two(values)
        last = (values - top.astype(F32) - rest.astype(F32)).astype(BF16)
        return nt(top, order) + nt(rest, order) + nt(last, order)

    def update(number, where, grad):
        master, first, second = (ref[where] for ref in states[number])
        new, first, second = adam_update(master, first, second, grad * factor, UPDATE_RATES[number])
        for ref, value in zip(outs[number], (new, first, second)):
            ref[where] = value
        if number < 5:
            copies[number][where] = new.astype(BF16)

    every = slice(None)
    g_out_col, g_in_col, g_out_row = reduced[4:]
    for half in range(2):
        lanes = slice(half * 1152, half * 1152 + 1152)
        update(0, (0, every, lanes), g_in[:, lanes])
        update(0, (1, every, lanes), g_in_col[half])
    leave(0, 1, 2, 21, 26, 27)
    arrive(1)
    for half in range(2):
        lanes = slice(half * 384, half * 384 + 384)
        update(1, (0, every, lanes), natural(g_out_row[half]))
        update(1, (1, every, lanes), natural(g_out_col[half]))
    leave(3, 4, 5, 22)
    for number, first in ((2, 2), (3, 0)):
        arrive(number)
        for half in range(2):
            for part in range(2):
                start = part * 1536 + half * 768
                lanes = slice(start, start + 768)
                update(number, (every, lanes), reduced[first + part][half])
        leave(*((6, 7, 8, 23) if number == 2 else (9, 10, 11, 24)))
    arrive(4)
    update(4, (every, every), g_emb[:, :VOCAB])
    update(5, (every, every), g_norm[...])
    update(6, (every, every), stats[0:1, : HEADS + 1])
    leave(12, 13, 14, 25, 15, 16, 17, 18, 19, 20)
    for n in range(28):
        pltpu.make_async_copy(results[n], far[n], out_sems.at[n]).wait()


def update_call(reduced, g_in, g_emb, g_norm, stats, states):
    anywhere = pl.BlockSpec(memory_space=pl.ANY)
    flat = [item for state in states for item in state]
    shapes = [jax.ShapeDtypeStruct(item.shape, F32) for item in flat]
    shapes += [jax.ShapeDtypeStruct(states[n][0].shape, BF16) for n in range(5)]
    shapes += [jax.ShapeDtypeStruct((1, 4), F32), jax.ShapeDtypeStruct((1, 1), F32)]
    given = (*reduced, g_in, g_emb, g_norm, stats, *flat)
    return pl.pallas_call(
        update_kernel,
        out_shape=shapes,
        in_specs=[anywhere] * len(given),
        out_specs=[anywhere] * len(shapes),
        scratch_shapes=[pltpu.VMEM(item.shape, F32) for item in given]
        + [pltpu.VMEM(item.shape, item.dtype) for item in shapes]
        + [
            pltpu.SemaphoreType.DMA((len(given),)),
            pltpu.SemaphoreType.DMA((len(shapes),)),
            pltpu.VMEM((44, 512, 512), F32),
        ],
        compiler_params=pltpu.CompilerParams(vmem_limit_bytes=62 * 2**20),
    )(*given)


def adam_update(master, first, second, grad_part, rate):
    first = BETA_ONE * first + (1.0 - BETA_ONE) * grad_part
    second = BETA_TWO * second + (1.0 - BETA_TWO) * grad_part * grad_part
    scaled = first * (1.0 / (1.0 - BETA_ONE**STEP))
    moved = scaled / (jnp.sqrt(second * (1.0 / (1.0 - BETA_TWO**STEP))) + ADAM_EPS)
    return (master - rate * (moved + WEIGHT_DECAY * master), first, second)


def shards(
    tokens,
    targets,
    masked,
    contact_pairs,
    labels,
    attention_in_master,
    attention_in_first,
    attention_in_second,
    attention_out_master,
    attention_out_first,
    attention_out_second,
    feed_up_master,
    feed_up_first,
    feed_up_second,
    feed_down_master,
    feed_down_first,
    feed_down_second,
    embedding_master,
    embedding_first,
    embedding_second,
    norm_params_master,
    norm_params_first,
    norm_params_second,
    contact_head_master,
    contact_head_first,
    contact_head_second,
):
    both = ("seq", "col")
    micro, rows_here, cols_here = tokens.shape
    ncol = lax.axis_size("col")
    ndev = lax.axis_size("seq") * ncol
    cols = cols_here * ncol
    me = lax.axis_index("seq") * ncol + lax.axis_index("col")
    per = ndev // micro
    cw = cols // per
    mine = me // per
    base = (me % per) * cw
    shard = D // ndev

    tiled = lax.axis_size("seq") == 16 and ncol == 2
    if tiled:
        raw = (
            tokens,
            targets,
            masked,
            contact_pairs.transpose(0, 2, 1),
            labels,
            embedding_master.T,
            norm_params_master,
            attention_in_master,
            attention_out_master,
            feed_up_master,
            feed_down_master.T,
        )
        weights, saved = forward_call(raw, contact_head_master)
        reduced, (g_in, g_emb, g_norm, stats) = backward_call(
            contact_head_master, [weights[n] for n in (5, 6, 3, 4, 2, 1, 0)], attention_in_master, saved
        )
        states = (
            (attention_in_master, attention_in_first, attention_in_second),
            (attention_out_master, attention_out_first, attention_out_second),
            (feed_up_master, feed_up_first, feed_up_second),
            (feed_down_master.T, feed_down_first.T, feed_down_second.T),
            (embedding_master.T, embedding_first.T, embedding_second.T),
            (norm_params_master, norm_params_first, norm_params_second),
            (contact_head_master[None], contact_head_first[None], contact_head_second[None]),
        )
        outs = update_call(reduced, g_in, g_emb, g_norm, stats, states)
        return (
            *outs[:9],
            *(item.T for item in outs[9:15]),
            *outs[15:18],
            *(item[0] for item in outs[18:21]),
            *outs[21:24],
            *(item.T for item in outs[24:26]),
            outs[26][0],
            outs[27][0, 0],
        )
    inputs = jnp.where(masked > 0, MASK_ID, tokens)
    masters = [
        jnp.concatenate(
            [
                jnp.pad(embedding_master.T, ((0, 0), (0, 128 - VOCAB))),
                jnp.pad(norm_params_master.T, ((0, 0), (0, 120))),
            ],
            1,
        ),
        attention_in_master[0],
        attention_out_master[0],
        attention_in_master[1],
        attention_out_master[1],
        feed_up_master,
        feed_down_master.T,
    ]
    whole = jnp.stack([inputs, targets])
    whole = lax.all_gather(lax.all_gather(whole, "col", axis=3, tiled=True), "seq", axis=2, tiled=True)
    pairs_all = lax.all_gather(
        jnp.concatenate([contact_pairs, labels[:, :, None]], -1), both, axis=1, tiled=True
    )
    gathered = []
    for master in masters:
        full = lax.all_gather(master.astype(BF16), both, axis=0, tiled=True)
        gathered.append(full.reshape(D, 2, -1).transpose(1, 0, 2))
    counts = (
        jnp.sum(whole[0] == MASK_ID).astype(F32),
        jnp.sum(pairs_all[..., 2] >= 0).astype(F32),
    )
    ids_all = lax.dynamic_index_in_dim(whole[0], mine, 0, False)
    ids_local = lax.dynamic_slice_in_dim(ids_all, base, cw, 1)
    targets_local = lax.dynamic_slice_in_dim(
        lax.dynamic_index_in_dim(whole[1], mine, 0, False), base, cw, 1
    )
    pairs = lax.dynamic_index_in_dim(pairs_all, mine, 0, False)

    table = gathered[0][0][:, :VP].T
    norms = gathered[0][1][:, :8].T.astype(F32)
    in_row, out_row, in_col, out_col, up_w, down_t = (
        jnp.concatenate([g[0], g[1]], 1) for g in gathered[1:]
    )
    big = (in_row, in_col, out_row, out_col, up_w, down_t)

    grads, tables, contact_total, mlm_total, bce_total, kept = step(
        big,
        table,
        norms,
        contact_head_master,
        ids_all,
        ids_local.reshape(-1),
        ids_local.T.reshape(-1),
        targets_local.T.reshape(-1),
        pairs[:, 0] - base,
        pairs[:, 1],
        pairs[:, 2],
        counts,
        cw,
    )
    table_pair, value_grad, table_grad, vectors = tables
    extras = jnp.zeros((2, D), F32).at[0, : HEADS + 3].set(
        jnp.concatenate([contact_total, mlm_total[None], bce_total[None]])
    )
    sums = jnp.concatenate([table_pair[:40], value_grad[:40], table_grad[:40], vectors, extras])
    flat_grad = jnp.concatenate([g.astype(BF16) for g in grads], 1)
    reduced = lax.psum_scatter(flat_grad, both, scatter_dimension=0, tiled=True).astype(F32)
    g_in_col, g_out_row, g_out_col, g_up, g_down = jnp.split(
        reduced, [3 * D, 4 * D, 5 * D, 5 * D + FF], 1
    )
    sums = lax.psum(sums, both)
    unit_t, rstd_t, normed_t, query_t, key_t = kept
    rows_all = ids_all.shape[0]
    spare = ((0, VP - 40), (0, 0))
    table_pair, value_grad, table_grad = (
        jnp.pad(sums[a : a + 40], spare) for a in (0, 40, 80)
    )
    vectors = sums[120:126]
    contact_grad, mlm_total, bce_total = (
        sums[126, : HEADS + 1], sums[126, HEADS + 1], sums[126, HEADS + 2]
    )
    row_scale = (HD * rows_all) ** (-0.5)
    query_grad = []
    key_grad = []
    for h in range(HEADS):
        pair = heads_of(table_pair, h)
        query_grad.append(jnp.dot(pair, heads_of(key_t, h).astype(F32), precision=PRECISE))
        key_grad.append(jnp.dot(pair.T, heads_of(query_t, h).astype(F32), precision=PRECISE))
    proj_grad = jnp.concatenate(
        [
            jnp.concatenate(query_grad, 1) * row_scale,
            jnp.concatenate(key_grad, 1) * row_scale,
            value_grad,
        ],
        1,
    )
    proj_hi, proj_lo = split_two(proj_grad)
    normed_grad = nt(proj_hi, in_row) + nt(proj_lo, in_row)
    back_t, scale_0, shift_0 = norm_back(unit_t, rstd_t, norms[0], normed_grad)
    table_grad = table_grad + back_t
    low = me * shard
    normed_mine = lax.dynamic_slice_in_dim(normed_t, low, shard, 1)
    grad_in_row = tn(normed_mine, proj_hi) + tn(normed_mine, proj_lo)
    norm_grad = jnp.concatenate([scale_0[None], vectors[:3], shift_0[None], vectors[3:]])
    table_mine = lax.dynamic_slice_in_dim(table_grad[:VOCAB], low, shard, 1)
    norm_mine = lax.dynamic_slice_in_dim(norm_grad, low, shard, 1)
    reduced_all = (g_in_col, g_out_row, g_out_col, g_up, g_down)

    local_square = (
        sum(jnp.sum(g * g) for g in reduced_all)
        + jnp.sum(grad_in_row * grad_in_row)
        + jnp.sum(table_mine * table_mine)
        + jnp.sum(norm_mine * norm_mine)
    )
    square = lax.psum(local_square, both) + jnp.sum(contact_grad * contact_grad)
    grad_norm = jnp.sqrt(square)
    factor = jnp.minimum(1.0, MAX_NORM / grad_norm)
    in_new, in_moment, in_square = adam_update(
        attention_in_master, attention_in_first, attention_in_second, jnp.stack([grad_in_row, g_in_col]) * factor, LEARN_RATE
    )
    out_new, out_moment, out_square = adam_update(
        attention_out_master, attention_out_first, attention_out_second, jnp.stack([g_out_row, g_out_col]) * factor, LEARN_RATE
    )
    up_new, up_moment, up_square = adam_update(
        feed_up_master, feed_up_first, feed_up_second, g_up * factor, LEARN_RATE
    )
    down_new, down_moment, down_square = adam_update(
        feed_down_master, feed_down_first, feed_down_second, g_down.T * factor, LEARN_RATE
    )
    table_new, table_moment, table_square = adam_update(
        embedding_master, embedding_first, embedding_second, table_mine * factor, VECTOR_RATE
    )
    norm_new, norm_moment, norm_square = adam_update(
        norm_params_master, norm_params_first, norm_params_second, norm_mine * factor, VECTOR_RATE
    )
    head_new, head_moment, head_square = adam_update(
        contact_head_master, contact_head_first, contact_head_second, contact_grad * factor, VECTOR_RATE
    )
    loss_parts = jnp.stack([mlm_total, counts[0], bce_total, counts[1]])
    return (
        in_new, in_moment, in_square,
        out_new, out_moment, out_square,
        up_new, up_moment, up_square,
        down_new, down_moment, down_square,
        table_new, table_moment, table_square,
        norm_new, norm_moment, norm_square,
        head_new, head_moment, head_square,
        in_new.astype(BF16), out_new.astype(BF16), up_new.astype(BF16), down_new.astype(BF16), table_new.astype(BF16),
        loss_parts, grad_norm,
    )


def solution(mesh):
    both = ("seq", "col")
    cells = P(None, "seq", "col")
    stack = P(None, both, None)
    row_split = P(both, None)
    col_split = P(None, both)
    weights = [stack] * 6 + [row_split] * 3 + [col_split] * 9 + [P()] * 3
    return jax.shard_map(
        shards,
        mesh=mesh,
        in_specs=(cells, cells, cells, stack, col_split, *weights),
        out_specs=(*weights, stack, stack, row_split, col_split, col_split, P(), P()),
        check_vma=False,
    )
```
